32 devices in a mesh: fsdp: 16 (over z, x, core), rep: 2 (over y).
Axes of the slice: x: 2, y: 2, z: 4, core: 2. Of those that a mesh axis runs over, the one named last changes fastest.
Arguments:
- layer_input: bfloat16 [4096, 1536], P(('fsdp', 'rep')), may hold values from -6 to 6
- lengths: int32 [32], P(('fsdp', 'rep')), may hold values from 16 to 128, as said below
- cotangent: bfloat16 [4096, 1536], P(('fsdp', 'rep')), may hold values from -6 to 6
- w_query: bfloat16 [1536, 1536], P('fsdp'), may hold values from -0.15625 to 0.15625
- w_key: bfloat16 [1536, 1536], P('fsdp'), may hold values from -0.15625 to 0.15625
- w_value: bfloat16 [1536, 1536], P('fsdp'), may hold values from -0.15625 to 0.15625
- w_out: bfloat16 [1536, 1536], P('fsdp'), may hold values from -0.15625 to 0.15625
- w_gate: bfloat16 [1536, 4096], P('fsdp'), may hold values from -0.15625 to 0.15625
- w_up: bfloat16 [1536, 4096], P('fsdp'), may hold values from -0.15625 to 0.15625
- w_down: bfloat16 [4096, 1536], P('fsdp'), may hold values from -0.09375 to 0.09375
- vec_copy: bfloat16 [5696], P('fsdp')
- owners: int32 [108], replicated, may hold values from 0 to 127, as said below
- basis_left: float32 [128, 512, 512], P(('fsdp', 'rep')), may hold values from -0.25 to 0.25
- basis_right: float32 [128, 512, 512], P(('fsdp', 'rep')), may hold values from -0.25 to 0.25
- block_master: float32 [128, 512, 512], P(('fsdp', 'rep')), may hold values from -0.15625 to 0.15625
- block_first: float32 [128, 512, 512], P(('fsdp', 'rep'))
- block_second: float32 [128, 512, 512], P(('fsdp', 'rep'))
- vec_master: float32 [5696], P('fsdp')
- vec_first: float32 [5696], P('fsdp')
- vec_second: float32 [5696], P('fsdp')
Outputs:
- layer_output: bfloat16 [4096, 1536], P(('fsdp', 'rep'))
- input_grad: float32 [4096, 1536], P(('fsdp', 'rep'))
- block_first_new: float32 [128, 512, 512], P(('fsdp', 'rep'))
- block_second_new: float32 [128, 512, 512], P(('fsdp', 'rep'))
- block_master_new: float32 [128, 512, 512], P(('fsdp', 'rep'))
- block_copy_new: bfloat16 [128, 512, 512], P(('fsdp', 'rep'))
- vec_first_new: float32 [5696], P('fsdp')
- vec_second_new: float32 [5696], P('fsdp')
- vec_master_new: float32 [5696], P('fsdp')
- vec_copy_new: bfloat16 [5696], P('fsdp')
The draws below stay inside these ranges and needn't reach their ends.
Inputs may be any that keep to these rules, and one draw needn't show every extreme that they name: `lengths`: valid tokens of each sequence come first; the rest of its 128 rows are padding. `owners`: distinct slots, one for each tile.
All inputs are finite; a program needn't handle non-finite values.
Results may differ from the reference program's by a relative error of at most 0.02.
Values may be sent and summed in bfloat16 or wider, within the bound.
A program may use at most 512 MiB of HBM per device.

```python
import math
import jax
import jax.numpy as jnp
import numpy as np
from jax import lax

H = 16
DH = 96
D = 1536
FF = 4096
CQ = 6
CK = 11
BLK = 512
SEQ_LEN = 128
QB = 128
SEQS = 32
TOKENS = 4096
NBLK = 108
SLOTS = 128
NVEC = 5696


def owner_table(key):
    inner = jax.random.permutation(jax.random.fold_in(key, 11), SLOTS - 2) + 1
    chosen = jnp.concatenate([jnp.array([0, SLOTS - 1], jnp.int32), inner[:NBLK - 2].astype(jnp.int32)])
    return jax.random.permutation(jax.random.fold_in(key, 12), chosen).astype(jnp.int32)


def draw_owners(key, part):
    return owner_table(key)


def draw_lengths(key, part):
    drawn = jax.random.randint(jax.random.fold_in(key, 21), (SEQS,), SEQ_LEN // 8, SEQ_LEN + 1).astype(jnp.int32)
    picked = jax.random.permutation(jax.random.fold_in(key, 22), SEQS)
    drawn = drawn.at[picked[0]].set(SEQ_LEN)
    drawn = drawn.at[picked[1]].set(SEQ_LEN // 8)
    return drawn.astype(jnp.int32)


def tile_scales():
    across = H * DH // BLK
    wide = FF // BLK
    listed = [0.75] * (3 * across * across) + [0.56] * (across * across) + [0.22] * (2 * across * wide) + [0.34] * (wide * across)
    return np.array(listed, np.float32)


def slot_scale(key):
    owner_list = owner_table(key)
    matches = (owner_list[None, :] == jnp.arange(SLOTS)[:, None]).astype(jnp.float32)
    per_slot = jnp.sum(matches * jnp.asarray(tile_scales())[None, :], axis=1) + 0.5 * (1.0 - jnp.sum(matches, axis=1))
    return per_slot * math.sqrt(TOKENS)


def draw_block_first(key, part):
    scale_slot = slot_scale(key)[:, None, None]
    stream = jax.random.fold_in(key, 31)
    drawn = jnp.clip(jax.random.normal(stream, (SLOTS, BLK, BLK), jnp.float32), -5.0, 5.0)
    return scale_slot * drawn


def draw_block_second(key, part):
    scale_slot = slot_scale(key)[:, None, None]
    stream = jax.random.fold_in(key, 41)
    factor = jnp.exp(jax.random.uniform(stream, (SLOTS, BLK, BLK), jnp.float32, math.log(0.7), math.log(5.0)))
    return scale_slot * scale_slot * factor


def vector_law(key, stream_id):
    model_width = H * DH
    position = jnp.arange(NVEC)
    normal_part = jnp.clip(jax.random.normal(jax.random.fold_in(key, stream_id), (NVEC,), jnp.float32), -4.0, 4.0)
    flat_part = jax.random.uniform(jax.random.fold_in(key, stream_id + 1), (NVEC,), jnp.float32)
    gain_part = 1.0 + 0.1 * normal_part
    conv_part = 0.25 * normal_part
    mix_part = 0.2 + flat_part
    conv_end = 3 * model_width + H * CQ * CK
    return jnp.where(position < 3 * model_width, gain_part, jnp.where(position < conv_end, conv_part, mix_part))


def draw_vec_copy(key, part):
    return vector_law(key, 51).astype(jnp.bfloat16)


def draw_vec_master(key, part):
    return vector_law(key, 61)


def vector_scale():
    model_width = H * DH
    position = jnp.arange(NVEC)
    return jnp.where(position < 3 * model_width, 1.5, 3.0) * math.sqrt(TOKENS)


def draw_vec_first(key, part):
    stream = jax.random.fold_in(key, 71)
    drawn = jnp.clip(jax.random.normal(stream, (NVEC,), jnp.float32), -5.0, 5.0)
    return vector_scale() * drawn


def draw_vec_second(key, part):
    stream = jax.random.fold_in(key, 81)
    scale_vec = vector_scale()
    factor = jnp.exp(jax.random.uniform(stream, (NVEC,), jnp.float32, math.log(0.7), math.log(5.0)))
    return scale_vec * scale_vec * factor


def block_scale(own_key, extent, shards, smallest, top_value):
    loudness, own = 1.0, jax.random.fold_in(own_key, 6)
    for axis_at, parts in shards:
        heights = jnp.exp(jax.random.uniform(jax.random.fold_in(own, axis_at), (parts,), jnp.float32, smallest / len(shards), top_value / len(shards)))
        loudness = loudness * jnp.repeat(heights, extent[axis_at] // parts).reshape([-1 if axis == axis_at else 1 for axis in range(len(extent))])
    return loudness


def bell_draw(key, dims, scale, bound, pieces=(), kind=jnp.bfloat16):
    values = jax.random.normal(key, dims, jnp.float32) * scale
    if len(pieces) > 0:
        values = block_scale(key, dims, pieces, -0.22, 0.18) * values
    return jnp.clip(values, min=-bound, max=bound).astype(kind)


def setup_inputs(seed: int = 0) -> dict:
    keys = jax.random.split(jax.random.key(seed), 21)
    layer_input = bell_draw(keys[0], (TOKENS, D), 1.0, 6.0, ((0, 32),))
    lengths = draw_lengths(jax.random.fold_in(keys[20], 71), 0)
    cotangent = bell_draw(keys[2], (TOKENS, D), 1.0, 6.0, ((0, 32),))
    w_query = bell_draw(keys[3], (D, D), D ** -0.5, 0.15625, ((0, 16),))
    w_key = bell_draw(keys[4], (D, D), D ** -0.5, 0.15625, ((0, 16),))
    w_value = bell_draw(keys[5], (D, D), D ** -0.5, 0.15625, ((0, 16),))
    w_out = bell_draw(keys[6], (D, D), D ** -0.5, 0.15625, ((0, 16),))
    w_gate = bell_draw(keys[7], (D, FF), D ** -0.5, 0.15625, ((0, 16),))
    w_up = bell_draw(keys[8], (D, FF), D ** -0.5, 0.15625, ((0, 16),))
    w_down = bell_draw(keys[9], (FF, D), FF ** -0.5, 0.09375, ((0, 16),))
    vec_copy = draw_vec_copy(jax.random.fold_in(keys[20], 71), 0)
    owners = draw_owners(jax.random.fold_in(keys[20], 71), 0)
    basis_left = bell_draw(keys[12], (SLOTS, BLK, BLK), BLK ** -0.5, 0.25, ((0, 32),), jnp.float32)
    basis_right = bell_draw(keys[13], (SLOTS, BLK, BLK), BLK ** -0.5, 0.25, ((0, 32),), jnp.float32)
    block_master = bell_draw(keys[14], (SLOTS, BLK, BLK), D ** -0.5, 0.15625, ((0, 32),), jnp.float32)
    block_first = draw_block_first(jax.random.fold_in(keys[20], 71), 0)
    block_second = draw_block_second(jax.random.fold_in(keys[20], 71), 0)
    vec_master = draw_vec_master(jax.random.fold_in(keys[20], 71), 0)
    vec_first = draw_vec_first(jax.random.fold_in(keys[20], 71), 0)
    vec_second = draw_vec_second(jax.random.fold_in(keys[20], 71), 0)
    return {"layer_input": layer_input, "lengths": lengths, "cotangent": cotangent, "w_query": w_query, "w_key": w_key, "w_value": w_value, "w_out": w_out, "w_gate": w_gate, "w_up": w_up, "w_down": w_down, "vec_copy": vec_copy, "owners": owners, "basis_left": basis_left, "basis_right": basis_right, "block_master": block_master, "block_first": block_first, "block_second": block_second, "vec_master": vec_master, "vec_first": vec_first, "vec_second": vec_second}


@jax.custom_vjp
def low(v):
    return lax.optimization_barrier(v.astype(jnp.bfloat16)).astype(jnp.float32)

@jax.custom_vjp
def low_back(v):
    return v

def low_keep(v):
    return (low(v), None)

def low_pass(kept, grad):
    return (grad,)

def back_keep(v):
    return (v, None)

def back_low(kept, grad):
    return (low(grad),)
low.defvjp(low_keep, low_pass)
low_back.defvjp(back_keep, back_low)
eps_norm = 1e-05
eps_adam = 1e-08
rate_block = 0.02
rate_vector = 0.3
decay_block = 0.1
beta_first = 0.5
beta_second = 0.5
highest = lax.Precision.HIGHEST

def product(left, right):
    return jnp.dot(left, right, precision=highest, preferred_element_type=jnp.float32)

def rms_norm(values, gain):
    return values * lax.rsqrt(lax.optimization_barrier(jnp.mean(values * values, axis=-1, keepdims=True)) + eps_norm) * gain

def head_norm(values, gain):
    normed = values * lax.rsqrt(lax.optimization_barrier(jnp.mean(values * values, axis=-1, keepdims=True)) + eps_norm)
    return normed.reshape(values.shape[0], -1) * gain

def split_vectors(vector):
    model_width = H * DH
    gain_attn = vector[0:model_width]
    gain_head = vector[model_width:2 * model_width]
    gain_ffn = vector[2 * model_width:3 * model_width]
    conv_end = 3 * model_width + H * CQ * CK
    theta = vector[3 * model_width:conv_end].reshape(H, CQ, CK)
    mixer = vector[conv_end:conv_end + 2 * H].reshape(H, 2)
    return (gain_attn, gain_head, gain_ffn, theta, mixer)

def mixed_weights(scores, theta, mixer, first_row, length):
    head_count = scores.shape[0]
    row_count = scores.shape[1] - (CQ - 1)
    key_count = scores.shape[2]
    key_index = jnp.arange(key_count)
    ext_rows = first_row - (CQ - 1) + jnp.arange(row_count + CQ - 1)
    keep_ext = (key_index[None, :] <= ext_rows[:, None]) & (key_index[None, :] < length) & (ext_rows[:, None] >= 0)
    masked = jnp.where(keep_ext[None], scores, 0.0)
    half_width = CK // 2
    padded = jnp.pad(masked, ((0, 0), (0, 0), (half_width, half_width)))
    convolved = jnp.zeros((head_count, row_count, key_count), jnp.float32)
    for query_lag in range(CQ):
        for key_tap in range(CK):
            window = padded[:, CQ - 1 - query_lag:CQ - 1 - query_lag + row_count, key_tap:key_tap + key_count]
            convolved = convolved + theta[:, query_lag, key_tap][:, None, None] * window
    positions = first_row + jnp.arange(row_count)
    keep = (key_index[None, :] <= positions[:, None]) & (key_index[None, :] < length)
    logits = jnp.where(keep[None], convolved, -1e+30)
    row_max = lax.optimization_barrier(jnp.max(logits, axis=-1, keepdims=True))
    exponent = jnp.exp(logits - row_max)
    softmax_w = exponent / lax.optimization_barrier(jnp.sum(exponent, axis=-1, keepdims=True))
    grouped = softmax_w.reshape(head_count // 2, 2, row_count, key_count)
    mixing = mixer.reshape(head_count // 2, 2, 2)
    return jnp.einsum('goe,gerl->gorl', mixing, grouped, precision=highest).reshape(head_count, row_count, key_count)

def attention(query_seq, key_seq, value_seq, length, theta, mixer):
    query_padded = jnp.pad(query_seq, ((CQ - 1, 0), (0, 0), (0, 0)))
    score_scale = 1.0 / math.sqrt(DH)

    def one_block(first_row):
        query_ext = lax.dynamic_slice_in_dim(query_padded, first_row, QB + CQ - 1, 0)
        scores = low_back(jnp.einsum('rhd,lhd->hrl', query_ext, key_seq, precision=highest) * score_scale)
        mixed = low(mixed_weights(scores, theta, mixer, first_row, length))
        return jnp.einsum('hrl,lhd->rhd', mixed, value_seq, precision=highest)
    starts = jnp.arange(SEQ_LEN // QB, dtype=jnp.int32) * QB
    blocks = lax.map(jax.checkpoint(one_block), starts)
    return blocks.reshape(SEQ_LEN, H, DH)

def layer(input_rows, lengths, weight_set, vector):
    w_query, w_key, w_value, w_out, w_gate, w_up, w_down = weight_set
    gain_attn, gain_head, gain_ffn, theta, mixer = split_vectors(vector)
    row_count = input_rows.shape[0]
    seq_count = row_count // SEQ_LEN
    xn_low = low(rms_norm(input_rows, gain_attn))
    query_low = low(low_back(product(xn_low, w_query)))
    key_low = low(low_back(product(xn_low, w_key)))
    value_low = low(low_back(product(xn_low, w_value)))

    def to_heads(values):
        return values.reshape(seq_count, SEQ_LEN, H, DH)

    def one_sequence(members):
        query_seq, key_seq, value_seq, length = members
        return attention(query_seq, key_seq, value_seq, length, theta, mixer)
    attn_heads = lax.map(one_sequence, (to_heads(query_low), to_heads(key_low), to_heads(value_low), lengths))
    attn_heads = low_back(attn_heads.reshape(row_count, H, DH))
    head_low = low(head_norm(attn_heads, gain_head))
    attn_out = low_back(product(head_low, w_out))
    hidden_in = input_rows + attn_out
    hn_low = low(rms_norm(hidden_in, gain_ffn))
    gate_act = low_back(product(hn_low, w_gate))
    up_act = low_back(product(hn_low, w_up))
    inner_low = low(jax.nn.silu(gate_act) * up_act)
    ffn_out = low_back(product(inner_low, w_down))
    return hidden_in + ffn_out

def add_pair(left, right):
    return left + right

def reference(layer_input, lengths, cotangent, w_query, w_key, w_value, w_out, w_gate, w_up, w_down, vec_copy, owners, basis_left, basis_right, block_master, block_first, block_second, vec_master, vec_first, vec_second):
    weight_set = tuple((matrix.astype(jnp.float32) for matrix in (w_query, w_key, w_value, w_out, w_gate, w_up, w_down)))
    vector = vec_copy.astype(jnp.float32)
    group_size = math.gcd(SEQS, max(1, 4096 // SEQ_LEN))
    group_count = SEQS // group_size
    input_groups = layer_input.reshape(group_count, group_size * SEQ_LEN, D)
    cot_groups = cotangent.reshape(group_count, group_size * SEQ_LEN, D)
    len_groups = lengths.reshape(group_count, group_size)

    def scan_step(totals, members):
        input_group, cot_group, len_group = members
        input_float = input_group.astype(jnp.float32)
        positions = jnp.arange(SEQ_LEN, dtype=jnp.int32)
        valid_rows = (positions[None, :] < len_group[:, None]).astype(jnp.float32).reshape(-1)

        def forward(input_in, weights_in, vector_in):
            return layer(input_in, len_group, weights_in, vector_in)
        result, pullback = jax.vjp(forward, input_float, weight_set, vector)
        grad_input, grad_weights, grad_vector = pullback(cot_group.astype(jnp.float32) * valid_rows[:, None])
        totals = jax.tree.map(add_pair, totals, (grad_weights, grad_vector))
        return (totals, (result.astype(jnp.bfloat16), grad_input))
    zero_totals = (tuple((jnp.zeros(matrix.shape, jnp.float32) for matrix in weight_set)), jnp.zeros((NVEC,), jnp.float32))
    (grad_weights, grad_vector), (out_groups, grad_groups) = lax.scan(scan_step, zero_totals, (input_groups, cot_groups, len_groups))
    layer_output = out_groups.reshape(TOKENS, D)
    input_grad = grad_groups.reshape(TOKENS, D)
    tiles = []
    for grad_matrix in grad_weights:
        for row_tile in range(grad_matrix.shape[0] // BLK):
            for col_tile in range(grad_matrix.shape[1] // BLK):
                tiles.append(grad_matrix[row_tile * BLK:(row_tile + 1) * BLK, col_tile * BLK:(col_tile + 1) * BLK])
    slot_grad = jnp.zeros((SLOTS, BLK, BLK), jnp.float32).at[owners].set(jnp.stack(tiles))
    rotated = jnp.einsum('sia,sij->saj', basis_left, slot_grad, precision=highest)
    rotated = jnp.einsum('saj,sjb->sab', rotated, basis_right, precision=highest)
    first_new = beta_first * block_first + (1.0 - beta_first) * rotated
    second_new = beta_second * block_second + (1.0 - beta_second) * rotated * rotated
    direction = first_new / (jnp.sqrt(second_new) + eps_adam)
    turned = jnp.einsum('sia,sab->sib', basis_left, direction, precision=highest)
    turned = jnp.einsum('sib,sjb->sij', turned, basis_right, precision=highest)
    master_new = block_master - rate_block * (turned + decay_block * block_master)
    vec_first_new = beta_first * vec_first + (1.0 - beta_first) * grad_vector
    vec_second_new = beta_second * vec_second + (1.0 - beta_second) * grad_vector * grad_vector
    vec_master_new = vec_master - rate_vector * vec_first_new / (jnp.sqrt(vec_second_new) + eps_adam)
    return (layer_output, input_grad, first_new, second_new, master_new, master_new.astype(jnp.bfloat16), vec_first_new, vec_second_new, vec_master_new, vec_master_new.astype(jnp.bfloat16))
```

```python
import math

import jax
import jax.numpy as jnp
import numpy as np
from jax import lax
from jax.experimental import pallas as pl
from jax.experimental.pallas import tpu as pltpu
from jax.sharding import Mesh
from jax.sharding import PartitionSpec as P

H = 16
DH = 96
HP = 128
D = H * DH
FF = 4096
CQ = 6
CK = 11
BLK = 512
CHIPS = 8
ROW_TILES = D // BLK
FF_TILES = FF // BLK

eps_norm = 1e-05
eps_adam = 1e-08
rate_block = 0.02
rate_vector = 0.3
decay_block = 0.1
beta_first = 0.5
beta_second = 0.5

FS = ("g", "a", "b", "c")
CHIP = ("y", "a", "b")
ALL = ("g", "a", "b", "c", "y")
bf16 = jnp.bfloat16
f32 = jnp.float32


def dot(left, right):
    return jnp.dot(left, right, preferred_element_type=f32)


def dot_nt(left, right):
    return lax.dot_general(left, right, (((1,), (1,)), ((), ())), preferred_element_type=f32)


def dot_tn(left, right):
    return lax.dot_general(left, right, (((0,), (0,)), ((), ())), preferred_element_type=f32)


def rms(values):
    return lax.rsqrt(jnp.mean(values * values, axis=-1, keepdims=True) + eps_norm)


def norm_backward(values, scale, gain, grad):
    unit = values * scale
    inner = grad * gain
    grad_values = scale * (inner - unit * jnp.mean(inner * unit, axis=-1, keepdims=True))
    return grad_values, jnp.sum(grad * unit, axis=0)


def shifted_down(pad_ref, values):
    rows = values.shape[0]
    pad_ref[8 : 8 + rows, :] = values
    return jnp.concatenate(
        [values] + [pad_ref[8 - lag : 8 - lag + rows, :] for lag in range(1, CQ)], axis=1
    )


def shifted_up(pad_ref, values):
    rows = values.shape[0]
    pad_ref[0:rows, :] = values
    return jnp.concatenate(
        [values] + [pad_ref[lag : lag + rows, :] for lag in range(1, CQ)], axis=1
    )


def attention_forward(len_ref, mix_ref, qkv_ref, toep_ref, gain_ref, heads_ref, s_ref, p_ref, o_ref, pad_ref):
    rows = qkv_ref.shape[1]
    length = len_ref[pl.program_id(0)]
    query_at = lax.broadcasted_iota(jnp.int32, (rows, rows), 0)
    key_at = lax.broadcasted_iota(jnp.int32, (rows, rows), 1)
    keep = (key_at <= query_at) & (key_at < length)
    pad_ref[0:8, :] = jnp.zeros((8, rows), f32)
    weights = []
    for head in range(2):
        query = qkv_ref[0, :, head * HP : (head + 1) * HP]
        key = qkv_ref[0, :, (2 + head) * HP : (3 + head) * HP]
        scores = jnp.where(keep, dot_nt(query, key) * (1.0 / math.sqrt(DH)), 0.0)
        s_ref[0, head] = scores.astype(bf16)
        wide = shifted_down(pad_ref, scores)
        high = wide.astype(bf16)
        low = (wide - high.astype(f32)).astype(bf16)
        conv = dot(high, toep_ref[head]) + dot(low, toep_ref[head])
        logits = jnp.where(keep, conv, -1e30)
        weight = jnp.exp(logits - jnp.max(logits, axis=-1, keepdims=True))
        weight = weight / jnp.sum(weight, axis=-1, keepdims=True)
        p_ref[0, head] = weight
        weights.append(weight)
    for head in range(2):
        mixed = mix_ref[2 * head] * weights[0] + mix_ref[2 * head + 1] * weights[1]
        value = qkv_ref[0, :, (4 + head) * HP : (5 + head) * HP]
        out = dot(mixed.astype(bf16), value)
        o_ref[0, :, head * HP : (head + 1) * HP] = out
        scale = lax.rsqrt(jnp.sum(out * out, axis=-1, keepdims=True) * (1.0 / DH) + eps_norm)
        heads_ref[0, :, head * HP : (head + 1) * HP] = (
            out * scale * gain_ref[:, head * HP : (head + 1) * HP]
        ).astype(bf16)


def attention_backward(
    len_ref, mix_ref, qkv_ref, toep_ref, gain_ref, s_ref, p_ref, o_ref, grad_ref,
    dqkv_ref, theta_ref, mixer_ref, gain_grad_ref, pad_ref,
):
    rows = qkv_ref.shape[1]
    length = len_ref[pl.program_id(0)]
    query_at = lax.broadcasted_iota(jnp.int32, (rows, rows), 0)
    key_at = lax.broadcasted_iota(jnp.int32, (rows, rows), 1)
    keep = (key_at <= query_at) & (key_at < length)
    pad_ref[rows : rows + 8, :] = jnp.zeros((8, rows), f32)

    @pl.when(pl.program_id(0) == 0)
    def _():
        theta_ref[...] = jnp.zeros_like(theta_ref)
        mixer_ref[...] = jnp.zeros_like(mixer_ref)
        gain_grad_ref[...] = jnp.zeros_like(gain_grad_ref)

    weights = [p_ref[0, 0], p_ref[0, 1]]
    grad_mixed = []
    for head in range(2):
        cols = slice(head * HP, (head + 1) * HP)
        out = o_ref[0, :, cols]
        grad = grad_ref[0, :, cols].astype(f32)
        scale = lax.rsqrt(jnp.sum(out * out, axis=-1, keepdims=True) * (1.0 / DH) + eps_norm)
        unit = out * scale
        gain_grad_ref[:, cols] += jnp.sum(grad * unit, axis=0, keepdims=True)
        inner = grad * gain_ref[:, cols]
        grad_out = scale * (inner - unit * (jnp.sum(inner * unit, axis=-1, keepdims=True) * (1.0 / DH)))
        grad_out = grad_out.astype(bf16)
        value = qkv_ref[0, :, (4 + head) * HP : (5 + head) * HP]
        mixed = (mix_ref[2 * head] * weights[0] + mix_ref[2 * head + 1] * weights[1]).astype(bf16)
        dqkv_ref[0, :, (4 + head) * HP : (5 + head) * HP] = dot_tn(mixed, grad_out).astype(bf16)
        back = dot_nt(grad_out, value)
        grad_mixed.append(back)
        for source in range(2):
            mixer_ref[2 * head + source : 2 * head + source + 1, :] += jnp.sum(
                back * weights[source], axis=0, keepdims=True
            )
    for head in range(2):
        grad_weight = mix_ref[head] * grad_mixed[0] + mix_ref[2 + head] * grad_mixed[1]
        weight = weights[head]
        grad_conv = weight * (grad_weight - jnp.sum(weight * grad_weight, axis=-1, keepdims=True))
        wide = shifted_up(pad_ref, grad_conv).astype(bf16)
        theta_ref[head] += dot_tn(s_ref[0, head], wide)
        grad_scores = jnp.zeros((rows, rows), f32)
        for lag in range(CQ):
            grad_scores += dot_nt(
                wide[:, lag * rows : (lag + 1) * rows], toep_ref[head, lag * rows : (lag + 1) * rows, :]
            )
        grad_scores = jnp.where(keep, grad_scores * (1.0 / math.sqrt(DH)), 0.0).astype(bf16)
        query = qkv_ref[0, :, head * HP : (head + 1) * HP]
        key = qkv_ref[0, :, (2 + head) * HP : (3 + head) * HP]
        dqkv_ref[0, :, head * HP : (head + 1) * HP] = dot(grad_scores, key).astype(bf16)
        dqkv_ref[0, :, (2 + head) * HP : (3 + head) * HP] = dot_tn(grad_scores, query).astype(bf16)


SMEM = pl.BlockSpec(memory_space=pltpu.SMEM)


def seq_spec(*dims):
    return pl.BlockSpec((1,) + dims, lambda s: (s,) + (0,) * len(dims))


def whole_spec(*dims):
    return pl.BlockSpec(dims, lambda s: (0,) * len(dims))


def run_forward(lengths, mix, qkv, toep, gain):
    seqs, rows, _ = qkv.shape
    return pl.pallas_call(
        attention_forward,
        grid=(seqs,),
        in_specs=[SMEM, SMEM, seq_spec(rows, 6 * HP), whole_spec(2, CQ * rows, rows), whole_spec(1, 2 * HP)],
        out_specs=[seq_spec(rows, 2 * HP), seq_spec(2, rows, rows), seq_spec(2, rows, rows), seq_spec(rows, 2 * HP)],
        out_shape=[
            jax.ShapeDtypeStruct((seqs, rows, 2 * HP), bf16),
            jax.ShapeDtypeStruct((seqs, 2, rows, rows), bf16),
            jax.ShapeDtypeStruct((seqs, 2, rows, rows), f32),
            jax.ShapeDtypeStruct((seqs, rows, 2 * HP), f32),
        ],
        scratch_shapes=[pltpu.VMEM((rows + 8, rows), f32)],
        name="attention_forward",
        compiler_params=pltpu.CompilerParams(vmem_limit_bytes=24 * 2**20),
        cost_estimate=pl.CostEstimate(flops=2 * 10**9, bytes_accessed=8 * 2**20, transcendentals=10**5),
    )(lengths, mix, qkv, toep, gain)


def run_backward(lengths, mix, qkv, toep, gain, scores, weights, outs, grads):
    seqs, rows, _ = qkv.shape
    return pl.pallas_call(
        attention_backward,
        grid=(seqs,),
        in_specs=[
            SMEM, SMEM, seq_spec(rows, 6 * HP), whole_spec(2, CQ * rows, rows), whole_spec(1, 2 * HP),
            seq_spec(2, rows, rows), seq_spec(2, rows, rows), seq_spec(rows, 2 * HP), seq_spec(rows, 2 * HP),
        ],
        out_specs=[seq_spec(rows, 6 * HP), whole_spec(2, rows, CQ * rows), whole_spec(8, rows), whole_spec(1, 2 * HP)],
        out_shape=[
            jax.ShapeDtypeStruct((seqs, rows, 6 * HP), bf16),
            jax.ShapeDtypeStruct((2, rows, CQ * rows), f32),
            jax.ShapeDtypeStruct((8, rows), f32),
            jax.ShapeDtypeStruct((1, 2 * HP), f32),
        ],
        scratch_shapes=[pltpu.VMEM((rows + 8, rows), f32)],
        name="attention_backward",
        compiler_params=pltpu.CompilerParams(vmem_limit_bytes=24 * 2**20),
        cost_estimate=pl.CostEstimate(flops=4 * 10**9, bytes_accessed=12 * 2**20, transcendentals=10**5),
    )(lengths, mix, qkv, toep, gain, scores, weights, outs, grads)


def gather_chips(rows):
    return lax.all_to_all(
        jnp.broadcast_to(rows[None], (CHIPS,) + rows.shape), CHIP, split_axis=0, concat_axis=0, tiled=True
    )


def exchange_chips(parts):
    return lax.all_to_all(parts, CHIP, split_axis=0, concat_axis=0, tiled=True)


def scatter_chips(parts):
    return jnp.sum(exchange_chips(parts.astype(bf16)).astype(f32), axis=0)


def swap(values, axis):
    return lax.ppermute(values, axis, [(0, 1), (1, 0)])


def both_cores(own, axis):
    other = swap(own, "c")
    first = lax.axis_index("c") == 0
    return jnp.stack([jnp.where(first, own, other), jnp.where(first, other, own)], axis=axis)


def half_for_core(values, axis):
    core = lax.axis_index("c")
    own = lax.dynamic_index_in_dim(values, core, axis, keepdims=False)
    sent = lax.dynamic_index_in_dim(values, 1 - core, axis, keepdims=False)
    return own + swap(sent.astype(bf16), "c").astype(f32)


def spread_columns(weight, width):
    rows = weight.shape[0]
    blocks = weight.reshape(rows, 2, CHIPS // 2, width)
    mine = lax.dynamic_index_in_dim(blocks, lax.axis_index("y"), 1, keepdims=False)
    return jnp.transpose(mine, (1, 0, 2))


def to_columns(blocks):
    groups = lax.axis_size("g")
    sent = jnp.broadcast_to(blocks[None], (groups,) + blocks.shape).reshape((-1,) + blocks.shape[1:])
    got = lax.all_to_all(sent, ("g", "a", "b"), split_axis=0, concat_axis=0, tiled=True)
    return both_cores(got, 1).reshape(-1, blocks.shape[-1])


def down_rows(w_down, chip):
    if lax.axis_size("g") == 2:
        other = swap(w_down, "g")
        mine = jnp.where(lax.axis_index("g") == lax.axis_index("y"), w_down, other)
        return both_cores(mine, 0).reshape(BLK, D)
    return lax.dynamic_slice_in_dim(lax.all_gather(w_down, FS, axis=0, tiled=True), chip * BLK, BLK, 0)


def band():
    tap = np.arange(CK)[:, None, None]
    source = np.arange(128)[None, :, None]
    target = np.arange(128)[None, None, :]
    return source - target + CK // 2 == tap


def body(
    layer_input, lengths, cotangent, w_query, w_key, w_value, w_out, w_gate, w_up, w_down, vec_copy, owners,
    basis_left, basis_right, block_master, block_first, block_second, vec_master, vec_first, vec_second,
):
    chip = (lax.axis_index("y") * 2 + lax.axis_index("a")) * 2 + lax.axis_index("b")
    fs_index = ((lax.axis_index("g") * 2 + lax.axis_index("a")) * 2 + lax.axis_index("b")) * 2 + lax.axis_index("c")
    seq_len = layer_input.shape[0]
    length = lengths[0]

    vector = lax.all_gather(vec_copy, FS, axis=0, tiled=True).astype(f32)
    gain_attn, gain_head, gain_ffn = vector[:D], vector[D : 2 * D], vector[2 * D : 3 * D]
    conv_end = 3 * D + H * CQ * CK
    theta = lax.dynamic_slice_in_dim(vector[3 * D : conv_end].reshape(H, CQ, CK), chip * 2, 2, 0)
    mixer = lax.dynamic_slice_in_dim(vector[conv_end : conv_end + 2 * H].reshape(H, 2), chip * 2, 2, 0)
    mix = mixer.reshape(4)
    gain_pair = jnp.pad(
        lax.dynamic_slice_in_dim(gain_head.reshape(H, DH), chip * 2, 2, 0), ((0, 0), (0, HP - DH))
    ).reshape(1, 2 * HP)
    toep = jnp.zeros((2, CQ, seq_len, seq_len), f32)
    offset = (
        jnp.arange(seq_len, dtype=jnp.int32)[:, None] - jnp.arange(seq_len, dtype=jnp.int32)[None, :] + CK // 2
    )
    for tap in range(CK):
        toep = jnp.where(offset[None, None] == tap, theta[:, :, tap][:, :, None, None], toep)
    toep = toep.astype(bf16).reshape(2, CQ * seq_len, seq_len)

    qkv_rows = to_columns(
        jnp.concatenate([spread_columns(w, 2 * DH) for w in (w_query, w_key, w_value)], axis=2)
    )
    w_qkv = jnp.pad(qkv_rows.reshape(D, 6, DH), ((0, 0), (0, 0), (0, HP - DH))).reshape(D, 6 * HP)
    w_in = to_columns(jnp.concatenate([spread_columns(w, BLK) for w in (w_gate, w_up)], axis=2))
    w_dn = down_rows(w_down, chip)
    w_o = lax.all_gather(w_out, FS, axis=0, tiled=True)

    group_lengths = lax.all_gather(lengths, CHIP, axis=0, tiled=True)
    input_float = layer_input.astype(f32)
    input_scale = rms(input_float)
    xn = gather_chips((input_float * input_scale * gain_attn).astype(bf16))
    xn_rows = xn.reshape(CHIPS * seq_len, D)
    qkv = dot(xn_rows, w_qkv).astype(bf16).reshape(CHIPS, seq_len, 6 * HP)
    heads_pad, scores, weights, outs = run_forward(group_lengths, mix, qkv, toep, gain_pair)
    heads_sent = heads_pad.reshape(CHIPS, seq_len, 2, HP)[..., :DH].reshape(CHIPS, seq_len, 2 * DH)
    heads = jnp.transpose(exchange_chips(heads_sent), (1, 0, 2)).reshape(seq_len, D)
    hmid = input_float + dot(heads, w_o)
    hmid_scale = rms(hmid)
    hn_rows = gather_chips((hmid * hmid_scale * gain_ffn).astype(bf16)).reshape(CHIPS * seq_len, D)
    both = dot(hn_rows, w_in)
    gate, up = both[:, :BLK], both[:, BLK:]
    sig = jax.nn.sigmoid(gate)
    silu = gate * sig
    inner = (silu * up).astype(bf16)
    ffn = scatter_chips(dot(inner, w_dn).reshape(CHIPS, seq_len, D))
    layer_output = (hmid + ffn).astype(bf16)

    valid = (jnp.arange(seq_len) < length).astype(f32)
    dy = cotangent.astype(f32) * valid[:, None]
    dy_rows = gather_chips(dy.astype(bf16)).reshape(CHIPS * seq_len, D)
    dinner = dot_nt(dy_rows, w_dn)
    dgate = (dinner * up * (sig * (1.0 + gate * (1.0 - sig)))).astype(bf16)
    dup = (dinner * silu).astype(bf16)
    dboth = jnp.concatenate([dgate, dup], axis=1)
    dhn = scatter_chips(dot_nt(dboth, w_in).reshape(CHIPS, seq_len, D))
    dhmid, grad_gain_ffn = norm_backward(hmid, hmid_scale, gain_ffn, dhn)
    dhmid = dhmid + dy
    dattn = dhmid.astype(bf16)
    dheads = dot_nt(dattn, w_o).astype(bf16).reshape(seq_len, CHIPS, 2 * DH)
    dheads = exchange_chips(jnp.transpose(dheads, (1, 0, 2)))
    dheads = jnp.pad(dheads.reshape(CHIPS, seq_len, 2, DH), ((0, 0), (0, 0), (0, 0), (0, HP - DH)))
    dqkv, theta_sums, mixer_sums, gain_sums = run_backward(
        group_lengths, mix, qkv, toep, gain_pair, scores, weights, outs, dheads.reshape(CHIPS, seq_len, 2 * HP)
    )
    dqkv_rows = dqkv.reshape(CHIPS * seq_len, 6 * HP)
    dxn = scatter_chips(dot_nt(dqkv_rows, w_qkv).reshape(CHIPS, seq_len, D))
    dinput, grad_gain_attn = norm_backward(input_float, input_scale, gain_attn, dxn)
    input_grad = dinput + dhmid

    taps = jnp.asarray(band())
    theta_sums = theta_sums.reshape(2, seq_len, CQ, seq_len)
    grad_theta = jnp.stack(
        [jnp.sum(jnp.where(taps[tap][None, :, None, :], theta_sums, 0.0), axis=(1, 3)) for tap in range(CK)], axis=2
    )
    grad_mixer = jnp.sum(mixer_sums[:4], axis=1)
    vector_grad = jnp.concatenate(
        [
            grad_gain_attn,
            lax.dynamic_update_slice_in_dim(
                jnp.zeros((D,), f32), gain_sums.reshape(2, HP)[:, :DH].reshape(-1), chip * 2 * DH, 0
            ),
            grad_gain_ffn,
            lax.dynamic_update_slice_in_dim(
                jnp.zeros((H * CQ * CK,), f32), grad_theta.reshape(-1), chip * 2 * CQ * CK, 0
            ),
            lax.dynamic_update_slice_in_dim(jnp.zeros((2 * H,), f32), grad_mixer, chip * 4, 0),
        ]
    )
    own_vec = vec_master.shape[0]
    vector_total = lax.dynamic_slice_in_dim(lax.psum(vector_grad, ALL), fs_index * own_vec, own_vec, 0)

    strip = BLK // (2 * CHIPS)
    grad_in = dot_tn(hn_rows, dboth).reshape(ROW_TILES, 2, CHIPS, strip, 2, BLK)
    grad_down = dot_tn(inner, dy_rows).reshape(2, CHIPS, strip, ROW_TILES, BLK)
    grad_in = jnp.transpose(half_for_core(grad_in, 1), (1, 3, 0, 2, 4)).reshape(CHIPS, 2 * ROW_TILES, strip, BLK)
    grad_down = jnp.transpose(half_for_core(grad_down, 0), (0, 2, 1, 3))
    ffn_tiles = exchange_chips(jnp.concatenate([grad_in, grad_down], axis=1).astype(bf16))
    gate_tiles = jnp.transpose(ffn_tiles[:, : 2 * ROW_TILES], (1, 0, 2, 3)).reshape(-1, strip, BLK)
    down_tiles = ffn_tiles[:, 2 * ROW_TILES :].reshape(-1, strip, BLK)
    grad_qkv = dot_tn(xn_rows, dqkv_rows).reshape(ROW_TILES, 2, CHIPS, strip, 6, HP)[..., :DH]
    grad_qkv = jnp.transpose(half_for_core(grad_qkv, 1), (1, 0, 2, 3, 4))
    grad_qkv = exchange_chips(grad_qkv.astype(bf16).reshape(CHIPS, ROW_TILES, strip, 6 * DH))
    grad_qkv = jnp.transpose(
        grad_qkv.reshape(CHIPS, ROW_TILES, strip, 3, 2 * DH), (3, 1, 2, 0, 4)
    ).reshape(3, ROW_TILES, strip, ROW_TILES, BLK)
    qkv_tiles = jnp.transpose(grad_qkv, (0, 1, 3, 2, 4)).reshape(-1, strip, BLK)
    heads_strips = jnp.transpose(heads.reshape(seq_len, 2 * ROW_TILES, CHIPS, strip), (2, 0, 1, 3))
    heads_strips = exchange_chips(heads_strips.reshape(CHIPS, seq_len, 2 * ROW_TILES * strip))
    dattn_rows = gather_chips(dattn).reshape(CHIPS * seq_len, D)
    grad_out = dot_tn(heads_strips.reshape(CHIPS * seq_len, -1), dattn_rows)
    grad_out = half_for_core(grad_out.reshape(ROW_TILES, 2, strip, ROW_TILES, BLK), 1)
    out_tiles = jnp.transpose(grad_out.astype(bf16), (0, 2, 1, 3)).reshape(-1, strip, BLK)
    tiles = jnp.concatenate([qkv_tiles, out_tiles, gate_tiles, down_tiles], axis=0)

    groups = lax.axis_size("g")
    part = strip // groups
    own_slots = basis_left.shape[0]
    devices = groups * 2 * CHIPS
    slot_total = own_slots * devices
    sums = lax.psum_scatter(tiles.astype(f32), "g", scatter_dimension=1, tiled=True).astype(bf16)
    matches = (jnp.arange(slot_total)[:, None] == owners[None, :]).astype(bf16)
    slots = dot(matches, sums.reshape(sums.shape[0], -1)).astype(bf16)
    slots = lax.all_to_all(
        slots.reshape(devices, own_slots, part, BLK), ALL, split_axis=0, concat_axis=0, tiled=True
    )
    slots = slots.reshape(groups, 2, 2, 2, 2, own_slots, part, BLK)
    own_grad = jnp.transpose(slots, (5, 3, 4, 1, 2, 0, 6, 7)).reshape(own_slots, BLK, BLK)

    left_low, right_low = basis_left.astype(bf16), basis_right.astype(bf16)
    rotated = jnp.einsum("sia,sij->saj", left_low, own_grad, preferred_element_type=f32)
    rotated = jnp.einsum("saj,sjb->sab", rotated.astype(bf16), right_low, preferred_element_type=f32)
    first_new = beta_first * block_first + (1.0 - beta_first) * rotated
    second_new = beta_second * block_second + (1.0 - beta_second) * rotated * rotated
    direction = (first_new / (jnp.sqrt(second_new) + eps_adam)).astype(bf16)
    turned = jnp.einsum("sia,sab->sib", left_low, direction, preferred_element_type=f32)
    turned = jnp.einsum("sib,sjb->sij", turned.astype(bf16), right_low, preferred_element_type=f32)
    master_new = block_master - rate_block * (turned + decay_block * block_master)
    vec_first_new = beta_first * vec_first + (1.0 - beta_first) * vector_total
    vec_second_new = beta_second * vec_second + (1.0 - beta_second) * vector_total * vector_total
    vec_master_new = vec_master - rate_vector * vec_first_new / (jnp.sqrt(vec_second_new) + eps_adam)
    return (
        layer_output, input_grad, first_new, second_new, master_new, master_new.astype(bf16),
        vec_first_new, vec_second_new, vec_master_new, vec_master_new.astype(bf16),
    )


def solution(mesh):
    fsdp, rep = mesh.shape["fsdp"], mesh.shape["rep"]
    fine = Mesh(mesh.devices.reshape(fsdp // 8, 2, 2, 2, rep), ALL)
    rows, both = P(ALL, None), P(ALL, None, None)
    weight, vec = P(FS, None), P(FS)
    return jax.shard_map(
        body,
        mesh=fine,
        in_specs=(rows, P(ALL), rows) + (weight,) * 7 + (vec, P()) + (both,) * 5 + (vec,) * 3,
        out_specs=(rows, rows) + (both,) * 4 + (vec,) * 4,
        check_vma=False,
    )
```

```python
import math

import jax
import jax.numpy as jnp
import numpy as np
from jax import lax
from jax.experimental import pallas as pl
from jax.experimental.pallas import tpu as pltpu
from jax.sharding import Mesh
from jax.sharding import PartitionSpec as P

H = 16
DH = 96
HP = 128
D = H * DH
FF = 4096
CQ = 6
CK = 11
BLK = 512
CHIPS = 8
ROW_TILES = D // BLK
FF_TILES = FF // BLK

eps_norm = 1e-05
eps_adam = 1e-08
rate_block = 0.02
rate_vector = 0.3
decay_block = 0.1
beta_first = 0.5
beta_second = 0.5

FS = ("g", "a", "b", "c")
CHIP = ("y", "a", "b")
ALL = ("g", "a", "b", "c", "y")
bf16 = jnp.bfloat16
f32 = jnp.float32


def dot(left, right):
    return jnp.dot(left, right, preferred_element_type=f32)


def dot_nt(left, right):
    return lax.dot_general(left, right, (((1,), (1,)), ((), ())), preferred_element_type=f32)


def dot_tn(left, right):
    return lax.dot_general(left, right, (((0,), (0,)), ((), ())), preferred_element_type=f32)


def rms(values):
    return lax.rsqrt(jnp.mean(values * values, axis=-1, keepdims=True) + eps_norm)


def norm_backward(values, scale, gain, grad):
    unit = values * scale
    inner = grad * gain
    grad_values = scale * (inner - unit * jnp.mean(inner * unit, axis=-1, keepdims=True))
    return grad_values, jnp.sum(grad * unit, axis=0)


def shifted_down(pad_ref, values):
    rows = values.shape[0]
    pad_ref[8 : 8 + rows, :] = values
    return jnp.concatenate(
        [values] + [pad_ref[8 - lag : 8 - lag + rows, :] for lag in range(1, CQ)], axis=1
    )


def shifted_up(pad_ref, values):
    rows = values.shape[0]
    pad_ref[0:rows, :] = values
    return jnp.concatenate(
        [values] + [pad_ref[lag : lag + rows, :] for lag in range(1, CQ)], axis=1
    )


def attention_forward(len_ref, mix_ref, qkv_ref, toep_ref, gain_ref, heads_ref, s_ref, p_ref, o_ref, pad_ref):
    rows = qkv_ref.shape[1]
    length = len_ref[pl.program_id(0)]
    query_at = lax.broadcasted_iota(jnp.int32, (rows, rows), 0)
    key_at = lax.broadcasted_iota(jnp.int32, (rows, rows), 1)
    keep = (key_at <= query_at) & (key_at < length)
    pad_ref[0:8, :] = jnp.zeros((8, rows), f32)
    weights = []
    for head in range(2):
        query = qkv_ref[0, :, head * HP : (head + 1) * HP]
        key = qkv_ref[0, :, (2 + head) * HP : (3 + head) * HP]
        scores = jnp.where(keep, dot_nt(query, key) * (1.0 / math.sqrt(DH)), 0.0)
        s_ref[0, head] = scores.astype(bf16)
        wide = shifted_down(pad_ref, scores)
        high = wide.astype(bf16)
        low = (wide - high.astype(f32)).astype(bf16)
        conv = dot(high, toep_ref[head]) + dot(low, toep_ref[head])
        logits = jnp.where(keep, conv, -1e30)
        weight = jnp.exp(logits - jnp.max(logits, axis=-1, keepdims=True))
        weight = weight / jnp.sum(weight, axis=-1, keepdims=True)
        p_ref[0, head] = weight
        weights.append(weight)
    for head in range(2):
        mixed = mix_ref[2 * head] * weights[0] + mix_ref[2 * head + 1] * weights[1]
        value = qkv_ref[0, :, (4 + head) * HP : (5 + head) * HP]
        out = dot(mixed.astype(bf16), value)
        o_ref[0, :, head * HP : (head + 1) * HP] = out
        scale = lax.rsqrt(jnp.sum(out * out, axis=-1, keepdims=True) * (1.0 / DH) + eps_norm)
        heads_ref[0, :, head * HP : (head + 1) * HP] = (
            out * scale * gain_ref[:, head * HP : (head + 1) * HP]
        ).astype(bf16)


def attention_backward(
    len_ref, mix_ref, qkv_ref, toep_ref, gain_ref, s_ref, p_ref, o_ref, grad_ref,
    dqkv_ref, theta_ref, mixer_ref, gain_grad_ref, pad_ref,
):
    rows = qkv_ref.shape[1]
    length = len_ref[pl.program_id(0)]
    query_at = lax.broadcasted_iota(jnp.int32, (rows, rows), 0)
    key_at = lax.broadcasted_iota(jnp.int32, (rows, rows), 1)
    keep = (key_at <= query_at) & (key_at < length)
    pad_ref[rows : rows + 8, :] = jnp.zeros((8, rows), f32)

    @pl.when(pl.program_id(0) == 0)
    def _():
        theta_ref[...] = jnp.zeros_like(theta_ref)
        mixer_ref[...] = jnp.zeros_like(mixer_ref)
        gain_grad_ref[...] = jnp.zeros_like(gain_grad_ref)

    weights = [p_ref[0, 0], p_ref[0, 1]]
    grad_mixed = []
    for head in range(2):
        cols = slice(head * HP, (head + 1) * HP)
        out = o_ref[0, :, cols]
        grad = grad_ref[0, :, cols].astype(f32)
        scale = lax.rsqrt(jnp.sum(out * out, axis=-1, keepdims=True) * (1.0 / DH) + eps_norm)
        unit = out * scale
        gain_grad_ref[:, cols] += jnp.sum(grad * unit, axis=0, keepdims=True)
        inner = grad * gain_ref[:, cols]
        grad_out = scale * (inner - unit * (jnp.sum(inner * unit, axis=-1, keepdims=True) * (1.0 / DH)))
        grad_out = grad_out.astype(bf16)
        value = qkv_ref[0, :, (4 + head) * HP : (5 + head) * HP]
        mixed = (mix_ref[2 * head] * weights[0] + mix_ref[2 * head + 1] * weights[1]).astype(bf16)
        dqkv_ref[0, :, (4 + head) * HP : (5 + head) * HP] = dot_tn(mixed, grad_out).astype(bf16)
        back = dot_nt(grad_out, value)
        grad_mixed.append(back)
        for source in range(2):
            mixer_ref[2 * head + source : 2 * head + source + 1, :] += jnp.sum(
                back * weights[source], axis=0, keepdims=True
            )
    for head in range(2):
        grad_weight = mix_ref[head] * grad_mixed[0] + mix_ref[2 + head] * grad_mixed[1]
        weight = weights[head]
        grad_conv = weight * (grad_weight - jnp.sum(weight * grad_weight, axis=-1, keepdims=True))
        wide = shifted_up(pad_ref, grad_conv).astype(bf16)
        theta_ref[head] += dot_tn(s_ref[0, head], wide)
        grad_scores = jnp.zeros((rows, rows), f32)
        for lag in range(CQ):
            grad_scores += dot_nt(
                wide[:, lag * rows : (lag + 1) * rows], toep_ref[head, lag * rows : (lag + 1) * rows, :]
            )
        grad_scores = jnp.where(keep, grad_scores * (1.0 / math.sqrt(DH)), 0.0).astype(bf16)
        query = qkv_ref[0, :, head * HP : (head + 1) * HP]
        key = qkv_ref[0, :, (2 + head) * HP : (3 + head) * HP]
        dqkv_ref[0, :, head * HP : (head + 1) * HP] = dot(grad_scores, key).astype(bf16)
        dqkv_ref[0, :, (2 + head) * HP : (3 + head) * HP] = dot_tn(grad_scores, query).astype(bf16)


SMEM = pl.BlockSpec(memory_space=pltpu.SMEM)


def seq_spec(*dims):
    return pl.BlockSpec((1,) + dims, lambda s: (s,) + (0,) * len(dims))


def whole_spec(*dims):
    return pl.BlockSpec(dims, lambda s: (0,) * len(dims))


def run_forward(lengths, mix, qkv, toep, gain):
    seqs, rows, _ = qkv.shape
    return pl.pallas_call(
        attention_forward,
        grid=(seqs,),
        in_specs=[SMEM, SMEM, seq_spec(rows, 6 * HP), whole_spec(2, CQ * rows, rows), whole_spec(1, 2 * HP)],
        out_specs=[seq_spec(rows, 2 * HP), seq_spec(2, rows, rows), seq_spec(2, rows, rows), seq_spec(rows, 2 * HP)],
        out_shape=[
            jax.ShapeDtypeStruct((seqs, rows, 2 * HP), bf16),
            jax.ShapeDtypeStruct((seqs, 2, rows, rows), bf16),
            jax.ShapeDtypeStruct((seqs, 2, rows, rows), f32),
            jax.ShapeDtypeStruct((seqs, rows, 2 * HP), f32),
        ],
        scratch_shapes=[pltpu.VMEM((rows + 8, rows), f32)],
        name="attention_forward",
        compiler_params=pltpu.CompilerParams(vmem_limit_bytes=24 * 2**20),
        cost_estimate=pl.CostEstimate(flops=2 * 10**9, bytes_accessed=8 * 2**20, transcendentals=10**5),
    )(lengths, mix, qkv, toep, gain)


def run_backward(lengths, mix, qkv, toep, gain, scores, weights, outs, grads):
    seqs, rows, _ = qkv.shape
    return pl.pallas_call(
        attention_backward,
        grid=(seqs,),
        in_specs=[
            SMEM, SMEM, seq_spec(rows, 6 * HP), whole_spec(2, CQ * rows, rows), whole_spec(1, 2 * HP),
            seq_spec(2, rows, rows), seq_spec(2, rows, rows), seq_spec(rows, 2 * HP), seq_spec(rows, 2 * HP),
        ],
        out_specs=[seq_spec(rows, 6 * HP), whole_spec(2, rows, CQ * rows), whole_spec(8, rows), whole_spec(1, 2 * HP)],
        out_shape=[
            jax.ShapeDtypeStruct((seqs, rows, 6 * HP), bf16),
            jax.ShapeDtypeStruct((2, rows, CQ * rows), f32),
            jax.ShapeDtypeStruct((8, rows), f32),
            jax.ShapeDtypeStruct((1, 2 * HP), f32),
        ],
        scratch_shapes=[pltpu.VMEM((rows + 8, rows), f32)],
        name="attention_backward",
        compiler_params=pltpu.CompilerParams(vmem_limit_bytes=24 * 2**20),
        cost_estimate=pl.CostEstimate(flops=4 * 10**9, bytes_accessed=12 * 2**20, transcendentals=10**5),
    )(lengths, mix, qkv, toep, gain, scores, weights, outs, grads)


BITS = {"y": 4, "a": 2, "b": 1}
HOPS = (("y", "b", "a"), ("a", "y", "b"), ("b", "a", "y"))
THIRDS = ((0, 48), (48, 48), (96, 32))
ANYS = pl.BlockSpec(memory_space=pl.ANY)


def chip_index():
    return (lax.axis_index("y") * 2 + lax.axis_index("a")) * 2 + lax.axis_index("b")


def flipped(chip, axes):
    for axis in axes:
        chip = chip + BITS[axis] * (1 - 2 * lax.axis_index(axis))
    return chip


def across(axis):
    return {axis: 1 - lax.axis_index(axis)}


def device_index():
    index = lax.axis_index("g")
    for axis in ("a", "b", "c", "y"):
        index = index * lax.axis_size(axis) + lax.axis_index(axis)
    return index


def device_at(index):
    at = {}
    for axis in ("y", "c", "b", "a", "g"):
        at[axis] = lax.rem(index, lax.axis_size(axis))
        index = lax.div(index, lax.axis_size(axis))
    return at


def greet_all():
    devices = lax.axis_size(ALL)
    me = device_index()
    barrier = pltpu.get_barrier_semaphore()

    def greet(step, carry):
        pl.semaphore_signal(barrier, inc=1, device_id=device_at(lax.rem(me + step, devices)))
        return carry

    lax.fori_loop(1, devices, greet, 0)
    pl.semaphore_wait(barrier, devices - 1)


def greet_neighbours():
    barrier = pltpu.get_barrier_semaphore()
    for axis in BITS:
        pl.semaphore_signal(barrier, inc=1, device_id=across(axis))
    pl.semaphore_wait(barrier, 3)


def remote(src, dst, send, recv, axis):
    return pltpu.make_async_remote_copy(src_ref=src, dst_ref=dst, send_sem=send, recv_sem=recv, device_id=across(axis))


def gather_body(x_ref, out_ref, *sems):
    greet_neighbours()
    gather_hops(x_ref, out_ref, *sems)


def gather_first_body(x_ref, vec_ref, out_ref, vecs_ref, vec_send, vec_recv, vec_local, *sems):
    devices = lax.axis_size(ALL)
    me = device_index()
    local = pltpu.make_async_copy(vec_ref, vecs_ref.at[me], vec_local)
    local.start()
    greet_all()

    def push(step, carry):
        pltpu.make_async_remote_copy(
            src_ref=vec_ref, dst_ref=vecs_ref.at[me], send_sem=vec_send, recv_sem=vec_recv,
            device_id=device_at(lax.rem(me + step, devices)),
        ).start()
        return carry

    lax.fori_loop(1, devices, push, 0)
    gather_hops(x_ref, out_ref, *sems)
    others = vecs_ref.at[pl.ds(0, devices - 1)]
    pltpu.make_async_copy(others, others, vec_recv).wait()
    pltpu.make_async_copy(others, others, vec_send).wait()
    local.wait()


def gather_hops(x_ref, out_ref, local_sem, send1, recv1, send2, recv2, send3, recv3):
    me = chip_index()
    rows = x_ref.shape[0]
    half = rows // 2
    local = pltpu.make_async_copy(x_ref, out_ref.at[me], local_sem)
    local.start()
    first = []
    for part in range(2):
        here = pl.ds(part * half, half)
        for at, (axis, _, _) in enumerate(HOPS):
            copy = remote(x_ref.at[here], out_ref.at[me, here], send1.at[at, part], recv1.at[at, part], axis)
            copy.start()
            first.append(copy)
    second = []
    for part in range(2):
        here = pl.ds(part * half, half)
        for at, (axis, onward, _) in enumerate(HOPS):
            first[part * 3 + at].wait_recv()
            block = out_ref.at[flipped(me, (axis,)), here]
            copy = remote(block, block, send2.at[at, part], recv2.at[at, part], onward)
            copy.start()
            second.append(copy)
    third = []
    for at, (axis, onward, last) in enumerate(HOPS):
        begin, count = THIRDS[at]
        block = flipped(me, (axis, onward))
        for part in range(2):
            if part * half < begin + count and begin < (part + 1) * half:
                second[part * 3 + at].wait_recv()
        piece = out_ref.at[block, pl.ds(begin, count)]
        copy = remote(piece, piece, send3.at[at], recv3.at[at], last)
        copy.start()
        third.append(copy)
    for at in range(3):
        begin, count = THIRDS[at]
        for part in range(2):
            if not (part * half < begin + count and begin < (part + 1) * half):
                second[part * 3 + at].wait_recv()
    for copy in third:
        copy.wait_recv()
    for copy in first + second + third:
        copy.wait_send()
    local.wait()


def hop_sems():
    dma = pltpu.SemaphoreType.DMA
    return [dma] + [dma((3, 2))] * 4 + [dma((3,))] * 2


def gather_first(rows, vec, collective_id):
    count, width = rows.shape
    return pl.pallas_call(
        gather_first_body,
        in_specs=[ANYS, ANYS],
        out_specs=[ANYS, ANYS],
        out_shape=[
            jax.ShapeDtypeStruct((CHIPS, count, width), rows.dtype),
            jax.ShapeDtypeStruct((lax.axis_size(ALL),) + vec.shape, vec.dtype),
        ],
        scratch_shapes=[pltpu.SemaphoreType.DMA] * 3 + hop_sems(),
        name="gather_first",
        compiler_params=pltpu.CompilerParams(collective_id=collective_id, has_side_effects=True),
    )(rows, vec)


def gather_chips(rows, collective_id):
    count, width = rows.shape
    return pl.pallas_call(
        gather_body,
        in_specs=[ANYS],
        out_specs=ANYS,
        out_shape=jax.ShapeDtypeStruct((CHIPS, count, width), rows.dtype),
        scratch_shapes=hop_sems(),
        name="gather_chips",
        compiler_params=pltpu.CompilerParams(collective_id=collective_id, has_side_effects=True),
    )(rows)


def scatter_body(
    parts_ref, out_ref, near_ref, in2_ref, in3_ref, acc2_ref, acc3_ref, send1, recv1, send2, recv2, send3, recv3
):
    me = chip_index()
    greet_neighbours()
    opposite = flipped(me, ("y", "a", "b"))
    first = []
    for at, (axis, onward, last) in enumerate(HOPS):
        begin, count = THIRDS[at]
        copy = remote(parts_ref.at[opposite, pl.ds(begin, count)], in2_ref.at[pl.ds(begin, count)], send1.at[at], recv1.at[at], last)
        copy.start()
        first.append(copy)
    second = []
    rows = parts_ref.shape[1]
    half = rows // 2
    for part in range(2):
        here = pl.ds(part * half, half)
        for at, (axis, onward, last) in enumerate(HOPS):
            dest = flipped(me, (axis, onward))
            begin, count = THIRDS[at]
            if part == 0:
                first[at].wait_recv()
                acc2_ref[at] = parts_ref[dest]
                piece = pl.ds(begin, count)
                acc2_ref[at, piece] = (parts_ref[dest, piece].astype(f32) + in2_ref[piece].astype(f32)).astype(bf16)
            copy = remote(acc2_ref.at[at, here], in3_ref.at[at, here], send2.at[at, part], recv2.at[at, part], onward)
            copy.start()
            second.append(copy)
    third = []
    for part in range(2):
        here = pl.ds(part * half, half)
        for at, (axis, onward, last) in enumerate(HOPS):
            dest = flipped(me, (axis,))
            second[part * 3 + at].wait_recv()
            acc3_ref[at, here] = (parts_ref[dest, here].astype(f32) + in3_ref[at, here].astype(f32)).astype(bf16)
            copy = remote(acc3_ref.at[at, here], near_ref.at[at, here], send3.at[at, part], recv3.at[at, part], axis)
            copy.start()
            third.append(copy)
    for part in range(2):
        here = pl.ds(part * half, half)
        for at in range(3):
            third[part * 3 + at].wait_recv()
        out_ref[here] = (
            (parts_ref[me, here].astype(f32) + near_ref[0, here].astype(f32))
            + (near_ref[1, here].astype(f32) + near_ref[2, here].astype(f32))
        )
    for copy in first + second + third:
        copy.wait_send()


def scatter_chips(parts, collective_id):
    _, rows, width = parts.shape
    vmem = pl.BlockSpec(memory_space=pltpu.VMEM)
    dma = pltpu.SemaphoreType.DMA
    return pl.pallas_call(
        scatter_body,
        in_specs=[vmem],
        out_specs=vmem,
        out_shape=jax.ShapeDtypeStruct((rows, width), f32),
        scratch_shapes=[pltpu.VMEM((3, rows, width), bf16), pltpu.VMEM((rows, width), bf16)] + [pltpu.VMEM((3, rows, width), bf16)] * 3
        + [dma((3,))] * 2 + [dma((3, 2))] * 4,
        name="scatter_chips",
        compiler_params=pltpu.CompilerParams(collective_id=collective_id, has_side_effects=True, vmem_limit_bytes=32*2**20),
    )(parts)


def gather_slow(rows):
    return lax.all_to_all(
        jnp.broadcast_to(rows[None], (CHIPS,) + rows.shape), CHIP, split_axis=0, concat_axis=0, tiled=True
    )


def exchange_chips(parts):
    return lax.all_to_all(parts, CHIP, split_axis=0, concat_axis=0, tiled=True)


def scatter_slow(parts):
    return jnp.sum(exchange_chips(parts.astype(bf16)).astype(f32), axis=0)


def swap(values, axis):
    return lax.ppermute(values, axis, [(0, 1), (1, 0)])


def both_cores(own, axis):
    other = swap(own, "c")
    first = lax.axis_index("c") == 0
    return jnp.stack([jnp.where(first, own, other), jnp.where(first, other, own)], axis=axis)


def half_for_core(values, axis):
    core = lax.axis_index("c")
    own = lax.dynamic_index_in_dim(values, core, axis, keepdims=False)
    sent = lax.dynamic_index_in_dim(values, 1 - core, axis, keepdims=False)
    return own + swap(sent.astype(bf16), "c").astype(f32)


def sum_groups(tiles):
    groups = lax.axis_size("g")
    if groups != 2:
        return lax.psum_scatter(tiles.astype(f32), "g", scatter_dimension=1, tiled=True).astype(bf16)
    part = tiles.shape[1] // 2
    group = lax.axis_index("g")
    own = lax.dynamic_slice_in_dim(tiles, group * part, part, 1)
    sent = lax.dynamic_slice_in_dim(tiles, (1 - group) * part, part, 1)
    return (own.astype(f32) + swap(sent, "g").astype(f32)).astype(bf16)


def spread_columns(weight, width):
    rows = weight.shape[0]
    blocks = weight.reshape(rows, 2, CHIPS // 2, width)
    mine = lax.dynamic_index_in_dim(blocks, lax.axis_index("y"), 1, keepdims=False)
    return jnp.transpose(mine, (1, 0, 2))


def to_columns(blocks):
    groups = lax.axis_size("g")
    sent = jnp.broadcast_to(blocks[None], (groups,) + blocks.shape).reshape((-1,) + blocks.shape[1:])
    got = lax.all_to_all(sent, ("g", "a", "b"), split_axis=0, concat_axis=0, tiled=True)
    return both_cores(got, 1).reshape(-1, blocks.shape[-1])


def down_rows(w_down, chip):
    if lax.axis_size("g") == 2:
        other = swap(w_down, "g")
        mine = jnp.where(lax.axis_index("g") == lax.axis_index("y"), w_down, other)
        return both_cores(mine, 0).reshape(BLK, D)
    return lax.dynamic_slice_in_dim(lax.all_gather(w_down, FS, axis=0, tiled=True), chip * BLK, BLK, 0)


def band():
    tap = np.arange(CK)[:, None, None]
    source = np.arange(128)[None, :, None]
    target = np.arange(128)[None, None, :]
    return source - target + CK // 2 == tap


def body(
    layer_input, lengths, cotangent, w_query, w_key, w_value, w_out, w_gate, w_up, w_down, vec_copy, owners,
    basis_left, basis_right, block_master, block_first, block_second, vec_master, vec_first, vec_second,
):
    chip = (lax.axis_index("y") * 2 + lax.axis_index("a")) * 2 + lax.axis_index("b")
    fs_index = ((lax.axis_index("g") * 2 + lax.axis_index("a")) * 2 + lax.axis_index("b")) * 2 + lax.axis_index("c")
    seq_len = layer_input.shape[0]
    length = lengths[0]
    reps = lax.axis_size("y")
    fs_size = lax.axis_size(FS)

    own_vec = vec_copy.shape[0]
    small = jnp.concatenate(
        [vec_copy.astype(f32), jnp.zeros((1023 - own_vec,), f32), length.astype(f32).reshape(1)]
    ).reshape(8, 128)
    x_all, small_all = gather_first(layer_input, small, 1)
    small_all = small_all.reshape(fs_size, reps, 1024)
    vector = small_all[:, 0, :own_vec].reshape(-1)
    group_lengths = small_all[:, :, 1023].reshape(-1, 2, 2, 2, reps)
    group_lengths = lax.dynamic_index_in_dim(group_lengths, lax.axis_index("g"), 0, keepdims=False)
    group_lengths = lax.dynamic_index_in_dim(group_lengths, lax.axis_index("c"), 2, keepdims=False)
    group_lengths = jnp.transpose(group_lengths, (2, 0, 1)).reshape(CHIPS).astype(jnp.int32)
    gain_attn, gain_head, gain_ffn = vector[:D], vector[D : 2 * D], vector[2 * D : 3 * D]
    conv_end = 3 * D + H * CQ * CK
    theta = lax.dynamic_slice_in_dim(vector[3 * D : conv_end].reshape(H, CQ, CK), chip * 2, 2, 0)
    mixer = lax.dynamic_slice_in_dim(vector[conv_end : conv_end + 2 * H].reshape(H, 2), chip * 2, 2, 0)
    mix = mixer.reshape(4)
    gain_pair = jnp.pad(
        lax.dynamic_slice_in_dim(gain_head.reshape(H, DH), chip * 2, 2, 0), ((0, 0), (0, HP - DH))
    ).reshape(1, 2 * HP)
    toep = jnp.zeros((2, CQ, seq_len, seq_len), f32)
    offset = (
        jnp.arange(seq_len, dtype=jnp.int32)[:, None] - jnp.arange(seq_len, dtype=jnp.int32)[None, :] + CK // 2
    )
    for tap in range(CK):
        toep = jnp.where(offset[None, None] == tap, theta[:, :, tap][:, :, None, None], toep)
    toep = toep.astype(bf16).reshape(2, CQ * seq_len, seq_len)

    qkv_rows = to_columns(
        jnp.concatenate([spread_columns(w, 2 * DH) for w in (w_query, w_key, w_value)], axis=2)
    )
    w_qkv = jnp.pad(qkv_rows.reshape(D, 6, DH), ((0, 0), (0, 0), (0, HP - DH))).reshape(D, 6 * HP)
    w_in = to_columns(jnp.concatenate([spread_columns(w, BLK) for w in (w_gate, w_up)], axis=2))
    w_dn = down_rows(w_down, chip)
    w_o = lax.all_gather(w_out, FS, axis=0, tiled=True)

    input_float = layer_input.astype(f32)
    input_scale = rms(input_float)
    x_rows = x_all.reshape(CHIPS * seq_len, D).astype(f32)
    xn_rows = (x_rows * rms(x_rows) * gain_attn).astype(bf16)
    qkv = dot(xn_rows, w_qkv).astype(bf16).reshape(CHIPS, seq_len, 6 * HP)
    heads_pad, scores, weights, outs = run_forward(group_lengths, mix, qkv, toep, gain_pair)
    heads_sent = heads_pad.reshape(CHIPS, seq_len, 2, HP)[..., :DH].reshape(CHIPS, seq_len, 2 * DH)
    heads = jnp.transpose(exchange_chips(heads_sent), (1, 0, 2)).reshape(seq_len, D)
    hmid = input_float + dot(heads, w_o)
    hmid_scale = rms(hmid)
    hn_rows = gather_chips((hmid * hmid_scale * gain_ffn).astype(bf16), 2).reshape(CHIPS * seq_len, D)
    both = dot(hn_rows, w_in)
    gate, up = both[:, :BLK], both[:, BLK:]
    sig = jax.nn.sigmoid(gate)
    silu = gate * sig
    inner = (silu * up).astype(bf16)
    ffn = scatter_slow(dot(inner, w_dn).reshape(CHIPS, seq_len, D))
    layer_output = (hmid + ffn).astype(bf16)

    valid = (jnp.arange(seq_len) < length).astype(f32)
    dy = cotangent.astype(f32) * valid[:, None]
    dy_rows = gather_slow(dy.astype(bf16)).reshape(CHIPS * seq_len, D)
    dinner = dot_nt(dy_rows, w_dn)
    dgate = (dinner * up * (sig * (1.0 + gate * (1.0 - sig)))).astype(bf16)
    dup = (dinner * silu).astype(bf16)
    dboth = jnp.concatenate([dgate, dup], axis=1)
    dhn = scatter_chips(dot_nt(dboth, w_in).astype(bf16).reshape(CHIPS, seq_len, D), 3)
    dhmid, grad_gain_ffn = norm_backward(hmid, hmid_scale, gain_ffn, dhn)
    dhmid = dhmid + dy
    dattn = dhmid.astype(bf16)
    dheads = dot_nt(dattn, w_o).astype(bf16).reshape(seq_len, CHIPS, 2 * DH)
    dheads = exchange_chips(jnp.transpose(dheads, (1, 0, 2)))
    dheads = jnp.pad(dheads.reshape(CHIPS, seq_len, 2, DH), ((0, 0), (0, 0), (0, 0), (0, HP - DH)))
    dqkv, theta_sums, mixer_sums, gain_sums = run_backward(
        group_lengths, mix, qkv, toep, gain_pair, scores, weights, outs, dheads.reshape(CHIPS, seq_len, 2 * HP)
    )
    dqkv_rows = dqkv.reshape(CHIPS * seq_len, 6 * HP)
    dxn = scatter_slow(dot_nt(dqkv_rows, w_qkv).reshape(CHIPS, seq_len, D))
    dinput, grad_gain_attn = norm_backward(input_float, input_scale, gain_attn, dxn)
    input_grad = dinput + dhmid

    taps = jnp.asarray(band())
    theta_sums = theta_sums.reshape(2, seq_len, CQ, seq_len)
    grad_theta = jnp.stack(
        [jnp.sum(jnp.where(taps[tap][None, :, None, :], theta_sums, 0.0), axis=(1, 3)) for tap in range(CK)], axis=2
    )
    grad_mixer = jnp.sum(mixer_sums[:4], axis=1)
    vector_grad = jnp.concatenate(
        [
            grad_gain_attn,
            lax.dynamic_update_slice_in_dim(
                jnp.zeros((D,), f32), gain_sums.reshape(2, HP)[:, :DH].reshape(-1), chip * 2 * DH, 0
            ),
            grad_gain_ffn,
            lax.dynamic_update_slice_in_dim(
                jnp.zeros((H * CQ * CK,), f32), grad_theta.reshape(-1), chip * 2 * CQ * CK, 0
            ),
            lax.dynamic_update_slice_in_dim(jnp.zeros((2 * H,), f32), grad_mixer, chip * 4, 0),
        ]
    )
    pieces = jnp.pad(vector_grad.reshape(fs_size, 1, own_vec), ((0, 0), (0, 0), (0, 512 - own_vec)))
    pieces = jnp.broadcast_to(pieces, (fs_size, reps, 512)).reshape(-1, 4, 128)
    vector_total = jnp.sum(
        lax.all_to_all(pieces, ALL, split_axis=0, concat_axis=0, tiled=True), axis=0
    ).reshape(512)[:own_vec]

    strip = BLK // (2 * CHIPS)
    grad_in = dot_tn(hn_rows, dboth).reshape(ROW_TILES, 2, CHIPS, strip, 2, BLK)
    grad_down = dot_tn(inner, dy_rows).reshape(2, CHIPS, strip, ROW_TILES, BLK)
    grad_in = jnp.transpose(half_for_core(grad_in, 1), (1, 3, 0, 2, 4)).reshape(CHIPS, 2 * ROW_TILES, strip, BLK)
    grad_down = jnp.transpose(half_for_core(grad_down, 0), (0, 2, 1, 3))
    ffn_tiles = exchange_chips(jnp.concatenate([grad_in, grad_down], axis=1).astype(bf16))
    gate_tiles = jnp.transpose(ffn_tiles[:, : 2 * ROW_TILES], (1, 0, 2, 3)).reshape(-1, strip, BLK)
    down_tiles = ffn_tiles[:, 2 * ROW_TILES :].reshape(-1, strip, BLK)
    grad_qkv = dot_tn(xn_rows, dqkv_rows).reshape(ROW_TILES, 2, CHIPS, strip, 6, HP)[..., :DH]
    grad_qkv = jnp.transpose(half_for_core(grad_qkv, 1), (1, 0, 2, 3, 4))
    grad_qkv = exchange_chips(grad_qkv.astype(bf16).reshape(CHIPS, ROW_TILES, strip, 6 * DH))
    grad_qkv = jnp.transpose(
        grad_qkv.reshape(CHIPS, ROW_TILES, strip, 3, 2 * DH), (3, 1, 2, 0, 4)
    ).reshape(3, ROW_TILES, strip, ROW_TILES, BLK)
    qkv_tiles = jnp.transpose(grad_qkv, (0, 1, 3, 2, 4)).reshape(-1, strip, BLK)
    heads_strips = jnp.transpose(heads.reshape(seq_len, 2 * ROW_TILES, CHIPS, strip), (2, 0, 1, 3))
    heads_strips = exchange_chips(heads_strips.reshape(CHIPS, seq_len, 2 * ROW_TILES * strip))
    dattn_rows = gather_slow(dattn).reshape(CHIPS * seq_len, D)
    grad_out = dot_tn(heads_strips.reshape(CHIPS * seq_len, -1), dattn_rows)
    grad_out = half_for_core(grad_out.reshape(ROW_TILES, 2, strip, ROW_TILES, BLK), 1)
    out_tiles = jnp.transpose(grad_out.astype(bf16), (0, 2, 1, 3)).reshape(-1, strip, BLK)

    groups = lax.axis_size("g")
    part = strip // groups
    own_slots = basis_left.shape[0]
    devices = groups * 2 * CHIPS
    slot_total = own_slots * devices
    sums = jnp.concatenate(
        [sum_groups(jnp.concatenate([qkv_tiles, out_tiles], axis=0)), sum_groups(jnp.concatenate([gate_tiles, down_tiles], axis=0))],
        axis=0,
    )
    matches = (jnp.arange(slot_total)[:, None] == owners[None, :]).astype(bf16)
    slots = dot(matches, sums.reshape(sums.shape[0], -1)).astype(bf16)
    slots = lax.all_to_all(
        slots.reshape(devices, own_slots, part, BLK), ALL, split_axis=0, concat_axis=0, tiled=True
    )
    slots = slots.reshape(groups, 2, 2, 2, 2, own_slots, part, BLK)
    own_grad = jnp.transpose(slots, (5, 3, 4, 1, 2, 0, 6, 7)).reshape(own_slots, BLK, BLK)

    left_low, right_low = basis_left.astype(bf16), basis_right.astype(bf16)
    rotated = jnp.einsum("sia,sij->saj", left_low, own_grad, preferred_element_type=f32)
    rotated = jnp.einsum("saj,sjb->sab", rotated.astype(bf16), right_low, preferred_element_type=f32)
    first_new = beta_first * block_first + (1.0 - beta_first) * rotated
    second_new = beta_second * block_second + (1.0 - beta_second) * rotated * rotated
    direction = (first_new / (jnp.sqrt(second_new) + eps_adam)).astype(bf16)
    turned = jnp.einsum("sia,sab->sib", left_low, direction, preferred_element_type=f32)
    turned = jnp.einsum("sib,sjb->sij", turned.astype(bf16), right_low, preferred_element_type=f32)
    master_new = block_master - rate_block * (turned + decay_block * block_master)
    vec_first_new = beta_first * vec_first + (1.0 - beta_first) * vector_total
    vec_second_new = beta_second * vec_second + (1.0 - beta_second) * vector_total * vector_total
    vec_master_new = vec_master - rate_vector * vec_first_new / (jnp.sqrt(vec_second_new) + eps_adam)
    return (
        layer_output, input_grad, first_new, second_new, master_new, master_new.astype(bf16),
        vec_first_new, vec_second_new, vec_master_new, vec_master_new.astype(bf16),
    )


def solution(mesh):
    fsdp, rep = mesh.shape["fsdp"], mesh.shape["rep"]
    fine = Mesh(mesh.devices.reshape(fsdp // 8, 2, 2, 2, rep), ALL)
    rows, both = P(ALL, None), P(ALL, None, None)
    weight, vec = P(FS, None), P(FS)
    return jax.shard_map(
        body,
        mesh=fine,
        in_specs=(rows, P(ALL), rows) + (weight,) * 7 + (vec, P()) + (both,) * 5 + (vec,) * 3,
        out_specs=(rows, rows) + (both,) * 4 + (vec,) * 4,
        check_vma=False,
    )
```

```python
import math

import jax
import jax.numpy as jnp
import numpy as np
from jax import lax
from jax.experimental import pallas as pl
from jax.experimental.pallas import tpu as pltpu
from jax.sharding import Mesh
from jax.sharding import PartitionSpec as P

H = 16
DH = 96
HP = 128
D = H * DH
FF = 4096
CQ = 6
CK = 11
BLK = 512
CHIPS = 8
ROW_TILES = D // BLK
FF_TILES = FF // BLK

eps_norm = 1e-05
eps_adam = 1e-08
rate_block = 0.02
rate_vector = 0.3
decay_block = 0.1
beta_first = 0.5
beta_second = 0.5

FS = ("g", "a", "b", "c")
CHIP = ("y", "a", "b")
ALL = ("g", "a", "b", "c", "y")
bf16 = jnp.bfloat16
f32 = jnp.float32


def dot(left, right):
    return jnp.dot(left, right, preferred_element_type=f32)


def dot_nt(left, right):
    return lax.dot_general(left, right, (((1,), (1,)), ((), ())), preferred_element_type=f32)


def dot_tn(left, right):
    return lax.dot_general(left, right, (((0,), (0,)), ((), ())), preferred_element_type=f32)


def rms(values):
    return lax.rsqrt(jnp.mean(values * values, axis=-1, keepdims=True) + eps_norm)


def norm_backward(values, scale, gain, grad):
    unit = values * scale
    inner = grad * gain
    grad_values = scale * (inner - unit * jnp.mean(inner * unit, axis=-1, keepdims=True))
    return grad_values, jnp.sum(grad * unit, axis=0)


def shifted_down(pad_ref, values):
    rows = values.shape[0]
    pad_ref[8 : 8 + rows, :] = values
    return jnp.concatenate(
        [values] + [pad_ref[8 - lag : 8 - lag + rows, :] for lag in range(1, CQ)], axis=1
    )


def shifted_up(pad_ref, values):
    rows = values.shape[0]
    pad_ref[0:rows, :] = values
    return jnp.concatenate(
        [values] + [pad_ref[lag : lag + rows, :] for lag in range(1, CQ)], axis=1
    )


def attention_forward(len_ref, mix_ref, qkv_ref, toep_ref, gain_ref, heads_ref, s_ref, p_ref, o_ref, pad_ref):
    rows = qkv_ref.shape[1]
    length = len_ref[pl.program_id(0)]
    query_at = lax.broadcasted_iota(jnp.int32, (rows, rows), 0)
    key_at = lax.broadcasted_iota(jnp.int32, (rows, rows), 1)
    keep = (key_at <= query_at) & (key_at < length)
    pad_ref[0:8, :] = jnp.zeros((8, rows), f32)
    weights = []
    for head in range(2):
        query = qkv_ref[0, :, head * HP : (head + 1) * HP]
        key = qkv_ref[0, :, (2 + head) * HP : (3 + head) * HP]
        scores = jnp.where(keep, dot_nt(query, key) * (1.0 / math.sqrt(DH)), 0.0)
        s_ref[0, head] = scores.astype(bf16)
        wide = shifted_down(pad_ref, scores)
        high = wide.astype(bf16)
        low = (wide - high.astype(f32)).astype(bf16)
        conv = dot(high, toep_ref[head]) + dot(low, toep_ref[head])
        logits = jnp.where(keep, conv, -1e30)
        weight = jnp.exp(logits - jnp.max(logits, axis=-1, keepdims=True))
        weight = weight / jnp.sum(weight, axis=-1, keepdims=True)
        p_ref[0, head] = weight
        weights.append(weight)
    for head in range(2):
        mixed = mix_ref[2 * head] * weights[0] + mix_ref[2 * head + 1] * weights[1]
        value = qkv_ref[0, :, (4 + head) * HP : (5 + head) * HP]
        out = dot(mixed.astype(bf16), value)
        o_ref[0, :, head * HP : (head + 1) * HP] = out
        scale = lax.rsqrt(jnp.sum(out * out, axis=-1, keepdims=True) * (1.0 / DH) + eps_norm)
        heads_ref[0, :, head * HP : (head + 1) * HP] = (
            out * scale * gain_ref[:, head * HP : (head + 1) * HP]
        ).astype(bf16)


def attention_backward(
    len_ref, mix_ref, qkv_ref, toep_ref, gain_ref, s_ref, p_ref, o_ref, grad_ref,
    dqkv_ref, theta_ref, mixer_ref, gain_grad_ref, pad_ref,
):
    rows = qkv_ref.shape[1]
    length = len_ref[pl.program_id(0)]
    query_at = lax.broadcasted_iota(jnp.int32, (rows, rows), 0)
    key_at = lax.broadcasted_iota(jnp.int32, (rows, rows), 1)
    keep = (key_at <= query_at) & (key_at < length)
    pad_ref[rows : rows + 8, :] = jnp.zeros((8, rows), f32)

    @pl.when(pl.program_id(0) == 0)
    def _():
        theta_ref[...] = jnp.zeros_like(theta_ref)
        mixer_ref[...] = jnp.zeros_like(mixer_ref)
        gain_grad_ref[...] = jnp.zeros_like(gain_grad_ref)

    weights = [p_ref[0, 0], p_ref[0, 1]]
    grad_mixed = []
    for head in range(2):
        cols = slice(head * HP, (head + 1) * HP)
        out = o_ref[0, :, cols]
        grad = grad_ref[0, :, cols].astype(f32)
        scale = lax.rsqrt(jnp.sum(out * out, axis=-1, keepdims=True) * (1.0 / DH) + eps_norm)
        unit = out * scale
        gain_grad_ref[:, cols] += jnp.sum(grad * unit, axis=0, keepdims=True)
        inner = grad * gain_ref[:, cols]
        grad_out = scale * (inner - unit * (jnp.sum(inner * unit, axis=-1, keepdims=True) * (1.0 / DH)))
        grad_out = grad_out.astype(bf16)
        value = qkv_ref[0, :, (4 + head) * HP : (5 + head) * HP]
        mixed = (mix_ref[2 * head] * weights[0] + mix_ref[2 * head + 1] * weights[1]).astype(bf16)
        dqkv_ref[0, :, (4 + head) * HP : (5 + head) * HP] = dot_tn(mixed, grad_out).astype(bf16)
        back = dot_nt(grad_out, value)
        grad_mixed.append(back)
        for source in range(2):
            mixer_ref[2 * head + source : 2 * head + source + 1, :] += jnp.sum(
                back * weights[source], axis=0, keepdims=True
            )
    for head in range(2):
        grad_weight = mix_ref[head] * grad_mixed[0] + mix_ref[2 + head] * grad_mixed[1]
        weight = weights[head]
        grad_conv = weight * (grad_weight - jnp.sum(weight * grad_weight, axis=-1, keepdims=True))
        wide = shifted_up(pad_ref, grad_conv).astype(bf16)
        theta_ref[head] += dot_tn(s_ref[0, head], wide)
        grad_scores = jnp.zeros((rows, rows), f32)
        for lag in range(CQ):
            grad_scores += dot_nt(
                wide[:, lag * rows : (lag + 1) * rows], toep_ref[head, lag * rows : (lag + 1) * rows, :]
            )
        grad_scores = jnp.where(keep, grad_scores * (1.0 / math.sqrt(DH)), 0.0).astype(bf16)
        query = qkv_ref[0, :, head * HP : (head + 1) * HP]
        key = qkv_ref[0, :, (2 + head) * HP : (3 + head) * HP]
        dqkv_ref[0, :, head * HP : (head + 1) * HP] = dot(grad_scores, key).astype(bf16)
        dqkv_ref[0, :, (2 + head) * HP : (3 + head) * HP] = dot_tn(grad_scores, query).astype(bf16)


SMEM = pl.BlockSpec(memory_space=pltpu.SMEM)


def seq_spec(*dims):
    return pl.BlockSpec((1,) + dims, lambda s: (s,) + (0,) * len(dims))


def whole_spec(*dims):
    return pl.BlockSpec(dims, lambda s: (0,) * len(dims))


def run_forward(lengths, mix, qkv, toep, gain):
    seqs, rows, _ = qkv.shape
    return pl.pallas_call(
        attention_forward,
        grid=(seqs,),
        in_specs=[SMEM, SMEM, seq_spec(rows, 6 * HP), whole_spec(2, CQ * rows, rows), whole_spec(1, 2 * HP)],
        out_specs=[seq_spec(rows, 2 * HP), seq_spec(2, rows, rows), seq_spec(2, rows, rows), seq_spec(rows, 2 * HP)],
        out_shape=[
            jax.ShapeDtypeStruct((seqs, rows, 2 * HP), bf16),
            jax.ShapeDtypeStruct((seqs, 2, rows, rows), bf16),
            jax.ShapeDtypeStruct((seqs, 2, rows, rows), f32),
            jax.ShapeDtypeStruct((seqs, rows, 2 * HP), f32),
        ],
        scratch_shapes=[pltpu.VMEM((rows + 8, rows), f32)],
        name="attention_forward",
        compiler_params=pltpu.CompilerParams(vmem_limit_bytes=24 * 2**20),
        cost_estimate=pl.CostEstimate(flops=2 * 10**9, bytes_accessed=8 * 2**20, transcendentals=10**5),
    )(lengths, mix, qkv, toep, gain)


def run_backward(lengths, mix, qkv, toep, gain, scores, weights, outs, grads):
    seqs, rows, _ = qkv.shape
    return pl.pallas_call(
        attention_backward,
        grid=(seqs,),
        in_specs=[
            SMEM, SMEM, seq_spec(rows, 6 * HP), whole_spec(2, CQ * rows, rows), whole_spec(1, 2 * HP),
            seq_spec(2, rows, rows), seq_spec(2, rows, rows), seq_spec(rows, 2 * HP), seq_spec(rows, 2 * HP),
        ],
        out_specs=[seq_spec(rows, 6 * HP), whole_spec(2, rows, CQ * rows), whole_spec(8, rows), whole_spec(1, 2 * HP)],
        out_shape=[
            jax.ShapeDtypeStruct((seqs, rows, 6 * HP), bf16),
            jax.ShapeDtypeStruct((2, rows, CQ * rows), f32),
            jax.ShapeDtypeStruct((8, rows), f32),
            jax.ShapeDtypeStruct((1, 2 * HP), f32),
        ],
        scratch_shapes=[pltpu.VMEM((rows + 8, rows), f32)],
        name="attention_backward",
        compiler_params=pltpu.CompilerParams(vmem_limit_bytes=24 * 2**20),
        cost_estimate=pl.CostEstimate(flops=4 * 10**9, bytes_accessed=12 * 2**20, transcendentals=10**5),
    )(lengths, mix, qkv, toep, gain, scores, weights, outs, grads)


BITS = {"y": 4, "a": 2, "b": 1}
HOPS = (("y", "b", "a"), ("a", "y", "b"), ("b", "a", "y"))
THIRDS = ((0, 48), (48, 48), (96, 32))
ANYS = pl.BlockSpec(memory_space=pl.ANY)


def chip_index():
    return (lax.axis_index("y") * 2 + lax.axis_index("a")) * 2 + lax.axis_index("b")


def flipped(chip, axes):
    for axis in axes:
        chip = chip + BITS[axis] * (1 - 2 * lax.axis_index(axis))
    return chip


def across(axis):
    return {axis: 1 - lax.axis_index(axis)}


def device_index():
    index = lax.axis_index("g")
    for axis in ("a", "b", "c", "y"):
        index = index * lax.axis_size(axis) + lax.axis_index(axis)
    return index


def device_at(index):
    at = {}
    for axis in ("y", "c", "b", "a", "g"):
        at[axis] = lax.rem(index, lax.axis_size(axis))
        index = lax.div(index, lax.axis_size(axis))
    return at


def greet_all():
    devices = lax.axis_size(ALL)
    me = device_index()
    barrier = pltpu.get_barrier_semaphore()

    def greet(step, carry):
        pl.semaphore_signal(barrier, inc=1, device_id=device_at(lax.rem(me + step, devices)))
        return carry

    lax.fori_loop(1, devices, greet, 0)
    pl.semaphore_wait(barrier, devices - 1)


def greet_neighbours():
    barrier = pltpu.get_barrier_semaphore()
    for axis in BITS:
        pl.semaphore_signal(barrier, inc=1, device_id=across(axis))
    pl.semaphore_wait(barrier, 3)


def remote(src, dst, send, recv, axis):
    return pltpu.make_async_remote_copy(src_ref=src, dst_ref=dst, send_sem=send, recv_sem=recv, device_id=across(axis))


def gather_body(x_ref, out_ref, *sems):
    greet_neighbours()
    gather_hops(x_ref, out_ref, *sems)


def gather_first_body(x_ref, vec_ref, out_ref, vecs_ref, vec_send, vec_recv, vec_local, *sems):
    devices = lax.axis_size(ALL)
    me = device_index()
    local = pltpu.make_async_copy(vec_ref, vecs_ref.at[me], vec_local)
    local.start()
    greet_all()

    def push(step, carry):
        pltpu.make_async_remote_copy(
            src_ref=vec_ref, dst_ref=vecs_ref.at[me], send_sem=vec_send, recv_sem=vec_recv,
            device_id=device_at(lax.rem(me + step, devices)),
        ).start()
        return carry

    lax.fori_loop(1, devices, push, 0)
    gather_hops(x_ref, out_ref, *sems)
    others = vecs_ref.at[pl.ds(0, devices - 1)]
    pltpu.make_async_copy(others, others, vec_recv).wait()
    pltpu.make_async_copy(others, others, vec_send).wait()
    local.wait()


def gather_hops(x_ref, out_ref, local_sem, send1, recv1, send2, recv2, send3, recv3):
    me = chip_index()
    rows = x_ref.shape[0]
    half = rows // 2
    local = pltpu.make_async_copy(x_ref, out_ref.at[me], local_sem)
    local.start()
    first = []
    for part in range(2):
        here = pl.ds(part * half, half)
        for at, (axis, _, _) in enumerate(HOPS):
            copy = remote(x_ref.at[here], out_ref.at[me, here], send1.at[at, part], recv1.at[at, part], axis)
            copy.start()
            first.append(copy)
    second = []
    for part in range(2):
        here = pl.ds(part * half, half)
        for at, (axis, onward, _) in enumerate(HOPS):
            first[part * 3 + at].wait_recv()
            block = out_ref.at[flipped(me, (axis,)), here]
            copy = remote(block, block, send2.at[at, part], recv2.at[at, part], onward)
            copy.start()
            second.append(copy)
    third = []
    for at, (axis, onward, last) in enumerate(HOPS):
        begin, count = THIRDS[at]
        block = flipped(me, (axis, onward))
        for part in range(2):
            if part * half < begin + count and begin < (part + 1) * half:
                second[part * 3 + at].wait_recv()
        piece = out_ref.at[block, pl.ds(begin, count)]
        copy = remote(piece, piece, send3.at[at], recv3.at[at], last)
        copy.start()
        third.append(copy)
    for at in range(3):
        begin, count = THIRDS[at]
        for part in range(2):
            if not (part * half < begin + count and begin < (part + 1) * half):
                second[part * 3 + at].wait_recv()
    for copy in third:
        copy.wait_recv()
    for copy in first + second + third:
        copy.wait_send()
    local.wait()


def hop_sems():
    dma = pltpu.SemaphoreType.DMA
    return [dma] + [dma((3, 2))] * 4 + [dma((3,))] * 2


def gather_first(rows, vec, collective_id):
    count, width = rows.shape
    return pl.pallas_call(
        gather_first_body,
        in_specs=[ANYS, ANYS],
        out_specs=[ANYS, ANYS],
        out_shape=[
            jax.ShapeDtypeStruct((CHIPS, count, width), rows.dtype),
            jax.ShapeDtypeStruct((lax.axis_size(ALL),) + vec.shape, vec.dtype),
        ],
        scratch_shapes=[pltpu.SemaphoreType.DMA] * 3 + hop_sems(),
        name="gather_first",
        compiler_params=pltpu.CompilerParams(collective_id=collective_id, has_side_effects=True),
    )(rows, vec)


def gather_chips(rows, collective_id):
    count, width = rows.shape
    return pl.pallas_call(
        gather_body,
        in_specs=[ANYS],
        out_specs=ANYS,
        out_shape=jax.ShapeDtypeStruct((CHIPS, count, width), rows.dtype),
        scratch_shapes=hop_sems(),
        name="gather_chips",
        compiler_params=pltpu.CompilerParams(collective_id=collective_id, has_side_effects=True),
    )(rows)


def scatter_body(
    parts_ref, out_ref, near_ref, in2_ref, in3_ref, acc2_ref, acc3_ref, send1, recv1, send2, recv2, send3, recv3
):
    me = chip_index()
    greet_neighbours()
    opposite = flipped(me, ("y", "a", "b"))
    first = []
    for at, (axis, onward, last) in enumerate(HOPS):
        begin, count = THIRDS[at]
        copy = remote(parts_ref.at[opposite, pl.ds(begin, count)], in2_ref.at[pl.ds(begin, count)], send1.at[at], recv1.at[at], last)
        copy.start()
        first.append(copy)
    second = []
    rows = parts_ref.shape[1]
    half = rows // 2
    for part in range(2):
        here = pl.ds(part * half, half)
        for at, (axis, onward, last) in enumerate(HOPS):
            dest = flipped(me, (axis, onward))
            begin, count = THIRDS[at]
            if part == 0:
                first[at].wait_recv()
                acc2_ref[at] = parts_ref[dest]
                piece = pl.ds(begin, count)
                acc2_ref[at, piece] = (parts_ref[dest, piece].astype(f32) + in2_ref[piece].astype(f32)).astype(bf16)
            copy = remote(acc2_ref.at[at, here], in3_ref.at[at, here], send2.at[at, part], recv2.at[at, part], onward)
            copy.start()
            second.append(copy)
    third = []
    for part in range(2):
        here = pl.ds(part * half, half)
        for at, (axis, onward, last) in enumerate(HOPS):
            dest = flipped(me, (axis,))
            second[part * 3 + at].wait_recv()
            acc3_ref[at, here] = (parts_ref[dest, here].astype(f32) + in3_ref[at, here].astype(f32)).astype(bf16)
            copy = remote(acc3_ref.at[at, here], near_ref.at[at, here], send3.at[at, part], recv3.at[at, part], axis)
            copy.start()
            third.append(copy)
    for part in range(2):
        here = pl.ds(part * half, half)
        for at in range(3):
            third[part * 3 + at].wait_recv()
        out_ref[here] = (
            (parts_ref[me, here].astype(f32) + near_ref[0, here].astype(f32))
            + (near_ref[1, here].astype(f32) + near_ref[2, here].astype(f32))
        )
    for copy in first + second + third:
        copy.wait_send()


def scatter_chips(parts, collective_id):
    _, rows, width = parts.shape
    vmem = pl.BlockSpec(memory_space=pltpu.VMEM)
    dma = pltpu.SemaphoreType.DMA
    return pl.pallas_call(
        scatter_body,
        in_specs=[vmem],
        out_specs=vmem,
        out_shape=jax.ShapeDtypeStruct((rows, width), f32),
        scratch_shapes=[pltpu.VMEM((3, rows, width), bf16), pltpu.VMEM((rows, width), bf16)] + [pltpu.VMEM((3, rows, width), bf16)] * 3
        + [dma((3,))] * 2 + [dma((3, 2))] * 4,
        name="scatter_chips",
        compiler_params=pltpu.CompilerParams(collective_id=collective_id, has_side_effects=True, vmem_limit_bytes=32*2**20),
    )(parts)


def gather_slow(rows):
    return lax.all_to_all(
        jnp.broadcast_to(rows[None], (CHIPS,) + rows.shape), CHIP, split_axis=0, concat_axis=0, tiled=True
    )


def exchange_chips(parts):
    return lax.all_to_all(parts, CHIP, split_axis=0, concat_axis=0, tiled=True)


def scatter_slow(parts):
    return jnp.sum(exchange_chips(parts.astype(bf16)).astype(f32), axis=0)


def swap(values, axis):
    return lax.ppermute(values, axis, [(0, 1), (1, 0)])


def both_cores(own, axis):
    other = swap(own, "c")
    first = lax.axis_index("c") == 0
    return jnp.stack([jnp.where(first, own, other), jnp.where(first, other, own)], axis=axis)


def half_for_core(values, axis):
    core = lax.axis_index("c")
    own = lax.dynamic_index_in_dim(values, core, axis, keepdims=False)
    sent = lax.dynamic_index_in_dim(values, 1 - core, axis, keepdims=False)
    return own + swap(sent.astype(bf16), "c").astype(f32)


def sum_groups(tiles):
    groups = lax.axis_size("g")
    if groups != 2:
        return lax.psum_scatter(tiles.astype(f32), "g", scatter_dimension=1, tiled=True).astype(bf16)
    part = tiles.shape[1] // 2
    group = lax.axis_index("g")
    own = lax.dynamic_slice_in_dim(tiles, group * part, part, 1)
    sent = lax.dynamic_slice_in_dim(tiles, (1 - group) * part, part, 1)
    return (own.astype(f32) + swap(sent, "g").astype(f32)).astype(bf16)


def spread_columns(weight, width):
    rows = weight.shape[0]
    blocks = weight.reshape(rows, 2, CHIPS // 2, width)
    mine = lax.dynamic_index_in_dim(blocks, lax.axis_index("y"), 1, keepdims=False)
    return jnp.transpose(mine, (1, 0, 2))


def to_columns(blocks):
    groups = lax.axis_size("g")
    sent = jnp.broadcast_to(blocks[None], (groups,) + blocks.shape).reshape((-1,) + blocks.shape[1:])
    got = lax.all_to_all(sent, ("g", "a", "b"), split_axis=0, concat_axis=0, tiled=True)
    return both_cores(got, 1).reshape(-1, blocks.shape[-1])


def down_rows(w_down, chip):
    if lax.axis_size("g") == 2:
        other = swap(w_down, "g")
        mine = jnp.where(lax.axis_index("g") == lax.axis_index("y"), w_down, other)
        return both_cores(mine, 0).reshape(BLK, D)
    return lax.dynamic_slice_in_dim(lax.all_gather(w_down, FS, axis=0, tiled=True), chip * BLK, BLK, 0)


def band():
    tap = np.arange(CK)[:, None, None]
    source = np.arange(128)[None, :, None]
    target = np.arange(128)[None, None, :]
    return source - target + CK // 2 == tap


def body_any(
    layer_input, lengths, cotangent, w_query, w_key, w_value, w_out, w_gate, w_up, w_down, vec_copy, owners,
    basis_left, basis_right, block_master, block_first, block_second, vec_master, vec_first, vec_second,
):
    chip = (lax.axis_index("y") * 2 + lax.axis_index("a")) * 2 + lax.axis_index("b")
    fs_index = ((lax.axis_index("g") * 2 + lax.axis_index("a")) * 2 + lax.axis_index("b")) * 2 + lax.axis_index("c")
    seq_len = layer_input.shape[0]
    length = lengths[0]
    reps = lax.axis_size("y")
    fs_size = lax.axis_size(FS)

    own_vec = vec_copy.shape[0]
    small = jnp.concatenate(
        [vec_copy.astype(f32), jnp.zeros((1023 - own_vec,), f32), length.astype(f32).reshape(1)]
    ).reshape(8, 128)
    x_all, small_all = gather_first(layer_input, small, 1)
    small_all = small_all.reshape(fs_size, reps, 1024)
    vector = small_all[:, 0, :own_vec].reshape(-1)
    group_lengths = small_all[:, :, 1023].reshape(-1, 2, 2, 2, reps)
    group_lengths = lax.dynamic_index_in_dim(group_lengths, lax.axis_index("g"), 0, keepdims=False)
    group_lengths = lax.dynamic_index_in_dim(group_lengths, lax.axis_index("c"), 2, keepdims=False)
    group_lengths = jnp.transpose(group_lengths, (2, 0, 1)).reshape(CHIPS).astype(jnp.int32)
    gain_attn, gain_head, gain_ffn = vector[:D], vector[D : 2 * D], vector[2 * D : 3 * D]
    conv_end = 3 * D + H * CQ * CK
    theta = lax.dynamic_slice_in_dim(vector[3 * D : conv_end].reshape(H, CQ, CK), chip * 2, 2, 0)
    mixer = lax.dynamic_slice_in_dim(vector[conv_end : conv_end + 2 * H].reshape(H, 2), chip * 2, 2, 0)
    mix = mixer.reshape(4)
    gain_pair = jnp.pad(
        lax.dynamic_slice_in_dim(gain_head.reshape(H, DH), chip * 2, 2, 0), ((0, 0), (0, HP - DH))
    ).reshape(1, 2 * HP)
    toep = jnp.zeros((2, CQ, seq_len, seq_len), f32)
    offset = (
        jnp.arange(seq_len, dtype=jnp.int32)[:, None] - jnp.arange(seq_len, dtype=jnp.int32)[None, :] + CK // 2
    )
    for tap in range(CK):
        toep = jnp.where(offset[None, None] == tap, theta[:, :, tap][:, :, None, None], toep)
    toep = toep.astype(bf16).reshape(2, CQ * seq_len, seq_len)

    qkv_rows = to_columns(
        jnp.concatenate([spread_columns(w, 2 * DH) for w in (w_query, w_key, w_value)], axis=2)
    )
    w_qkv = jnp.pad(qkv_rows.reshape(D, 6, DH), ((0, 0), (0, 0), (0, HP - DH))).reshape(D, 6 * HP)
    w_in = to_columns(jnp.concatenate([spread_columns(w, BLK) for w in (w_gate, w_up)], axis=2))
    w_dn = down_rows(w_down, chip)
    w_o = lax.all_gather(w_out, FS, axis=0, tiled=True)

    input_float = layer_input.astype(f32)
    input_scale = rms(input_float)
    x_rows = x_all.reshape(CHIPS * seq_len, D).astype(f32)
    xn_rows = (x_rows * rms(x_rows) * gain_attn).astype(bf16)
    qkv = dot(xn_rows, w_qkv).astype(bf16).reshape(CHIPS, seq_len, 6 * HP)
    heads_pad, scores, weights, outs = run_forward(group_lengths, mix, qkv, toep, gain_pair)
    heads_sent = heads_pad.reshape(CHIPS, seq_len, 2, HP)[..., :DH].reshape(CHIPS, seq_len, 2 * DH)
    heads = jnp.transpose(exchange_chips(heads_sent), (1, 0, 2)).reshape(seq_len, D)
    hmid = input_float + dot(heads, w_o)
    hmid_scale = rms(hmid)
    hn_rows = gather_chips((hmid * hmid_scale * gain_ffn).astype(bf16), 2).reshape(CHIPS * seq_len, D)
    both = dot(hn_rows, w_in)
    gate, up = both[:, :BLK], both[:, BLK:]
    sig = jax.nn.sigmoid(gate)
    silu = gate * sig
    inner = (silu * up).astype(bf16)
    ffn = scatter_slow(dot(inner, w_dn).reshape(CHIPS, seq_len, D))
    layer_output = (hmid + ffn).astype(bf16)

    valid = (jnp.arange(seq_len) < length).astype(f32)
    dy = cotangent.astype(f32) * valid[:, None]
    dy_rows = gather_slow(dy.astype(bf16)).reshape(CHIPS * seq_len, D)
    dinner = dot_nt(dy_rows, w_dn)
    dgate = (dinner * up * (sig * (1.0 + gate * (1.0 - sig)))).astype(bf16)
    dup = (dinner * silu).astype(bf16)
    dboth = jnp.concatenate([dgate, dup], axis=1)
    dhn = scatter_chips(dot_nt(dboth, w_in).astype(bf16).reshape(CHIPS, seq_len, D), 3)
    dhmid, grad_gain_ffn = norm_backward(hmid, hmid_scale, gain_ffn, dhn)
    dhmid = dhmid + dy
    dattn = dhmid.astype(bf16)
    dheads = dot_nt(dattn, w_o).astype(bf16).reshape(seq_len, CHIPS, 2 * DH)
    dheads = exchange_chips(jnp.transpose(dheads, (1, 0, 2)))
    dheads = jnp.pad(dheads.reshape(CHIPS, seq_len, 2, DH), ((0, 0), (0, 0), (0, 0), (0, HP - DH)))
    dqkv, theta_sums, mixer_sums, gain_sums = run_backward(
        group_lengths, mix, qkv, toep, gain_pair, scores, weights, outs, dheads.reshape(CHIPS, seq_len, 2 * HP)
    )
    dqkv_rows = dqkv.reshape(CHIPS * seq_len, 6 * HP)
    dxn = scatter_slow(dot_nt(dqkv_rows, w_qkv).reshape(CHIPS, seq_len, D))
    dinput, grad_gain_attn = norm_backward(input_float, input_scale, gain_attn, dxn)
    input_grad = dinput + dhmid

    taps = jnp.asarray(band())
    theta_sums = theta_sums.reshape(2, seq_len, CQ, seq_len)
    grad_theta = jnp.stack(
        [jnp.sum(jnp.where(taps[tap][None, :, None, :], theta_sums, 0.0), axis=(1, 3)) for tap in range(CK)], axis=2
    )
    grad_mixer = jnp.sum(mixer_sums[:4], axis=1)
    vector_grad = jnp.concatenate(
        [
            grad_gain_attn,
            lax.dynamic_update_slice_in_dim(
                jnp.zeros((D,), f32), gain_sums.reshape(2, HP)[:, :DH].reshape(-1), chip * 2 * DH, 0
            ),
            grad_gain_ffn,
            lax.dynamic_update_slice_in_dim(
                jnp.zeros((H * CQ * CK,), f32), grad_theta.reshape(-1), chip * 2 * CQ * CK, 0
            ),
            lax.dynamic_update_slice_in_dim(jnp.zeros((2 * H,), f32), grad_mixer, chip * 4, 0),
        ]
    )
    pieces = jnp.pad(vector_grad.reshape(fs_size, 1, own_vec), ((0, 0), (0, 0), (0, 512 - own_vec)))
    pieces = jnp.broadcast_to(pieces, (fs_size, reps, 512)).reshape(-1, 4, 128)
    vector_total = jnp.sum(
        lax.all_to_all(pieces, ALL, split_axis=0, concat_axis=0, tiled=True), axis=0
    ).reshape(512)[:own_vec]

    strip = BLK // (2 * CHIPS)
    grad_in = dot_tn(hn_rows, dboth).reshape(ROW_TILES, 2, CHIPS, strip, 2, BLK)
    grad_down = dot_tn(inner, dy_rows).reshape(2, CHIPS, strip, ROW_TILES, BLK)
    grad_in = jnp.transpose(half_for_core(grad_in, 1), (1, 3, 0, 2, 4)).reshape(CHIPS, 2 * ROW_TILES, strip, BLK)
    grad_down = jnp.transpose(half_for_core(grad_down, 0), (0, 2, 1, 3))
    ffn_tiles = exchange_chips(jnp.concatenate([grad_in, grad_down], axis=1).astype(bf16))
    gate_tiles = jnp.transpose(ffn_tiles[:, : 2 * ROW_TILES], (1, 0, 2, 3)).reshape(-1, strip, BLK)
    down_tiles = ffn_tiles[:, 2 * ROW_TILES :].reshape(-1, strip, BLK)
    grad_qkv = dot_tn(xn_rows, dqkv_rows).reshape(ROW_TILES, 2, CHIPS, strip, 6, HP)[..., :DH]
    grad_qkv = jnp.transpose(half_for_core(grad_qkv, 1), (1, 0, 2, 3, 4))
    grad_qkv = exchange_chips(grad_qkv.astype(bf16).reshape(CHIPS, ROW_TILES, strip, 6 * DH))
    grad_qkv = jnp.transpose(
        grad_qkv.reshape(CHIPS, ROW_TILES, strip, 3, 2 * DH), (3, 1, 2, 0, 4)
    ).reshape(3, ROW_TILES, strip, ROW_TILES, BLK)
    qkv_tiles = jnp.transpose(grad_qkv, (0, 1, 3, 2, 4)).reshape(-1, strip, BLK)
    heads_strips = jnp.transpose(heads.reshape(seq_len, 2 * ROW_TILES, CHIPS, strip), (2, 0, 1, 3))
    heads_strips = exchange_chips(heads_strips.reshape(CHIPS, seq_len, 2 * ROW_TILES * strip))
    dattn_rows = gather_slow(dattn).reshape(CHIPS * seq_len, D)
    grad_out = dot_tn(heads_strips.reshape(CHIPS * seq_len, -1), dattn_rows)
    grad_out = half_for_core(grad_out.reshape(ROW_TILES, 2, strip, ROW_TILES, BLK), 1)
    out_tiles = jnp.transpose(grad_out.astype(bf16), (0, 2, 1, 3)).reshape(-1, strip, BLK)

    groups = lax.axis_size("g")
    part = strip // groups
    own_slots = basis_left.shape[0]
    devices = groups * 2 * CHIPS
    slot_total = own_slots * devices
    sums = jnp.concatenate(
        [sum_groups(jnp.concatenate([qkv_tiles, out_tiles], axis=0)), sum_groups(jnp.concatenate([gate_tiles, down_tiles], axis=0))],
        axis=0,
    )
    matches = (jnp.arange(slot_total)[:, None] == owners[None, :]).astype(bf16)
    slots = dot(matches, sums.reshape(sums.shape[0], -1)).astype(bf16)
    slots = lax.all_to_all(
        slots.reshape(devices, own_slots, part, BLK), ALL, split_axis=0, concat_axis=0, tiled=True
    )
    slots = slots.reshape(groups, 2, 2, 2, 2, own_slots, part, BLK)
    own_grad = jnp.transpose(slots, (5, 3, 4, 1, 2, 0, 6, 7)).reshape(own_slots, BLK, BLK)

    left_low, right_low = basis_left.astype(bf16), basis_right.astype(bf16)
    rotated = jnp.einsum("sia,sij->saj", left_low, own_grad, preferred_element_type=f32)
    rotated = jnp.einsum("saj,sjb->sab", rotated.astype(bf16), right_low, preferred_element_type=f32)
    first_new = beta_first * block_first + (1.0 - beta_first) * rotated
    second_new = beta_second * block_second + (1.0 - beta_second) * rotated * rotated
    direction = (first_new / (jnp.sqrt(second_new) + eps_adam)).astype(bf16)
    turned = jnp.einsum("sia,sab->sib", left_low, direction, preferred_element_type=f32)
    turned = jnp.einsum("sib,sjb->sij", turned.astype(bf16), right_low, preferred_element_type=f32)
    master_new = block_master - rate_block * (turned + decay_block * block_master)
    vec_first_new = beta_first * vec_first + (1.0 - beta_first) * vector_total
    vec_second_new = beta_second * vec_second + (1.0 - beta_second) * vector_total * vector_total
    vec_master_new = vec_master - rate_vector * vec_first_new / (jnp.sqrt(vec_second_new) + eps_adam)
    return (
        layer_output, input_grad, first_new, second_new, master_new, master_new.astype(bf16),
        vec_first_new, vec_second_new, vec_master_new, vec_master_new.astype(bf16),
    )


def group_at(mask):
    return {axis: 1 - lax.axis_index(axis) for axis, bit in (("g", 4), ("a", 2), ("b", 1)) if mask & bit}


def other_bit(axis, changed):
    at = lax.axis_index(axis)
    return 1 - at if changed else at


def push(src, dst, send, recv, device):
    copy = pltpu.make_async_remote_copy(src_ref=src, dst_ref=dst, send_sem=send, recv_sem=recv, device_id=device)
    copy.start()
    return copy


class Gather:
    def __init__(self, x_ref, out_ref, local_sem, send1, recv1, send2, recv2, send3, recv3):
        self.x, self.out, self.local_sem = x_ref, out_ref, local_sem
        self.sems = ((send1, recv1), (send2, recv2), (send3, recv3))
        self.me = chip_index()
        self.half = x_ref.shape[0] // 2
        self.sent, self.second = [], []

    def here(self, part):
        return pl.ds(part * self.half, self.half)

    def start(self):
        self.local = pltpu.make_async_copy(self.x, self.out.at[self.me], self.local_sem)
        self.local.start()
        send, recv = self.sems[0]
        for part in range(2):
            for at, (axis, _, _) in enumerate(HOPS):
                self.sent.append(
                    push(
                        self.x.at[self.here(part)], self.out.at[self.me, self.here(part)],
                        send.at[at, part], recv.at[at, part], across(axis),
                    )
                )

    def onward(self):
        send, recv = self.sems[1]
        for part in range(2):
            for at, (axis, onward, _) in enumerate(HOPS):
                self.sent[part * 3 + at].wait_recv()
                block = self.out.at[flipped(self.me, (axis,)), self.here(part)]
                self.second.append(push(block, block, send.at[at, part], recv.at[at, part], across(onward)))

    def last(self):
        send, recv = self.sems[2]
        self.third = []
        for copy in self.second:
            copy.wait_recv()
        for at, (axis, onward, last) in enumerate(HOPS):
            begin, count = THIRDS[at]
            piece = self.out.at[flipped(self.me, (axis, onward)), pl.ds(begin, count)]
            self.third.append(push(piece, piece, send.at[at], recv.at[at], across(last)))

    def finish(self):
        for copy in self.third:
            copy.wait_recv()
        self.local.wait()

    def drain(self):
        for copy in self.sent + self.second + self.third:
            copy.wait_send()


class Scatter:
    def __init__(self, parts, near, in2, in3, acc2, acc3, send1, recv1, send2, recv2, send3, recv3):
        self.parts, self.near, self.in2, self.in3, self.acc2, self.acc3 = parts, near, in2, in3, acc2, acc3
        self.sems = ((send1, recv1), (send2, recv2), (send3, recv3))
        self.me = chip_index()
        self.half = parts.shape[1] // 2

    def here(self, part):
        return pl.ds(part * self.half, self.half)

    def start(self):
        send, recv = self.sems[0]
        opposite = flipped(self.me, ("y", "a", "b"))
        self.first = []
        for at, (_, _, last) in enumerate(HOPS):
            rows = pl.ds(*THIRDS[at])
            self.first.append(push(self.parts.at[opposite, rows], self.in2.at[rows], send.at[at], recv.at[at], across(last)))

    def onward(self):
        send, recv = self.sems[1]
        self.second = []
        for part in range(2):
            for at, (axis, onward, _) in enumerate(HOPS):
                dest = flipped(self.me, (axis, onward))
                if part == 0:
                    self.first[at].wait_recv()
                    rows = pl.ds(*THIRDS[at])
                    self.acc2[at] = self.parts[dest]
                    self.acc2[at, rows] = (
                        self.parts[dest, rows].astype(f32) + self.in2[rows].astype(f32)
                    ).astype(bf16)
                here = self.here(part)
                self.second.append(
                    push(self.acc2.at[at, here], self.in3.at[at, here], send.at[at, part], recv.at[at, part], across(onward))
                )

    def last(self):
        send, recv = self.sems[2]
        self.third = []
        for part in range(2):
            here = self.here(part)
            for at, (axis, _, _) in enumerate(HOPS):
                dest = flipped(self.me, (axis,))
                self.second[part * 3 + at].wait_recv()
                self.acc3[at, here] = (
                    self.parts[dest, here].astype(f32) + self.in3[at, here].astype(f32)
                ).astype(bf16)
                self.third.append(
                    push(self.acc3.at[at, here], self.near.at[at, here], send.at[at, part], recv.at[at, part], across(axis))
                )

    def finish(self, part):
        here = self.here(part)
        for at in range(3):
            self.third[part * 3 + at].wait_recv()
        return (self.parts[self.me, here].astype(f32) + self.near[0, here].astype(f32)) + (
            self.near[1, here].astype(f32) + self.near[2, here].astype(f32)
        )

    def drain(self):
        for copy in self.first + self.second + self.third:
            copy.wait_send()


def scatter_scratch(rows, width):
    dma = pltpu.SemaphoreType.DMA
    three = pltpu.VMEM((3, rows, width), bf16)
    return [three, pltpu.VMEM((rows, width), bf16), three, three, three] + [dma((3,))] * 2 + [dma((3, 2))] * 4


VMEM = pl.BlockSpec(memory_space=pltpu.VMEM)


def dispatch_body(
    x_ref, vec_ref, blocks_ref, out_ref, vecs_ref, wq_ref,
    vec_send, vec_recv, vec_local, w_local, w_send, w_recv, core_send, core_recv, *hops,
):
    devices = lax.axis_size(ALL)
    me = device_index()
    g, a, b, c, y = (lax.axis_index(axis) for axis in ALL)
    mine = ((g * 2 + a) * 2 + b) * 2 + c
    local = pltpu.make_async_copy(vec_ref, vecs_ref.at[me], vec_local)
    local.start()
    own = pltpu.make_async_copy(blocks_ref.at[chip_index()], wq_ref.at[mine], w_local)
    own.start()
    greet_all()
    gather = Gather(x_ref, out_ref, *hops)
    gather.start()

    def push_vec(step, carry):
        pltpu.make_async_remote_copy(
            src_ref=vec_ref, dst_ref=vecs_ref.at[me], send_sem=vec_send, recv_sem=vec_recv,
            device_id=device_at(lax.rem(me + step, devices)),
        ).start()
        return carry

    lax.fori_loop(1, devices, push_vec, 0)
    sent, relayed = [], []
    for mask in (4, 6, 5, 7, 2, 1, 3):
        block = (y * 2 + other_bit("a", mask & 2)) * 2 + other_bit("b", mask & 1)
        sent.append(push(blocks_ref.at[block], wq_ref.at[mine], w_send.at[mask], w_recv.at[mask], group_at(mask)))
    own.wait()
    relayed.append(push(wq_ref.at[mine], wq_ref.at[mine], core_send.at[0], core_recv.at[0], across("c")))
    gather.onward()
    for at, mask in enumerate((4, 6, 5, 7, 2, 1, 3)):
        sent[at].wait_recv()
        source = ((other_bit("g", mask & 4) * 2 + other_bit("a", mask & 2)) * 2 + other_bit("b", mask & 1)) * 2 + c
        relayed.append(push(wq_ref.at[source], wq_ref.at[source], core_send.at[mask], core_recv.at[mask], across("c")))
        if at == 1:
            gather.last()
    gather.finish()
    for copy in relayed:
        copy.wait_recv()
    others = vecs_ref.at[pl.ds(0, devices - 1)]
    pltpu.make_async_copy(others, others, vec_recv).wait()
    pltpu.make_async_copy(others, others, vec_send).wait()
    local.wait()
    gather.drain()
    for copy in sent + relayed:
        copy.wait_send()


def dispatch(rows, vec, blocks):
    count, width = rows.shape
    dma = pltpu.SemaphoreType.DMA
    return pl.pallas_call(
        dispatch_body,
        in_specs=[ANYS] * 3,
        out_specs=[ANYS] * 3,
        out_shape=[
            jax.ShapeDtypeStruct((CHIPS, count, width), rows.dtype),
            jax.ShapeDtypeStruct((lax.axis_size(ALL),) + vec.shape, vec.dtype),
            jax.ShapeDtypeStruct((16,) + blocks.shape[1:], blocks.dtype),
        ],
        scratch_shapes=[dma] * 4 + [dma((8,))] * 4 + hop_sems(),
        name="dispatch",
        compiler_params=pltpu.CompilerParams(collective_id=1, has_side_effects=True),
    )(rows, vec, blocks)


def back_body(
    len_ref, mix_ref, qkv_ref, toep_ref, gain_ref, s_ref, p_ref, o_ref, sent_ref, dattn_ref, strips_ref,
    dqkv_ref, theta_ref, mixer_ref, gain_grad_ref, go_ref,
    pad_ref, grads_ref, all_ref, own_sem, send, recv, *hops,
):
    seqs, rows = qkv_ref.shape[:2]
    me = chip_index()
    own = pltpu.make_async_copy(sent_ref.at[me], grads_ref.at[me], own_sem)
    own.start()
    barrier = pltpu.get_barrier_semaphore()
    for mask in range(1, 8):
        pl.semaphore_signal(barrier, inc=1, device_id=chip_at(mask))
    pl.semaphore_wait(barrier, 7)
    sent = []
    for mask in (7, 6, 5, 3, 4, 2, 1):
        to = flipped(me, [axis for axis in BITS if mask & BITS[axis]])
        sent.append(push(sent_ref.at[to], grads_ref.at[me], send.at[mask], recv.at[mask], chip_at(mask)))
    gather = Gather(dattn_ref, all_ref, *hops)
    gather.start()
    pad_ref[rows : rows + 8, :] = jnp.zeros((8, rows), f32)
    theta_ref[...] = jnp.zeros_like(theta_ref)
    mixer_ref[...] = jnp.zeros_like(mixer_ref)
    gain_grad_ref[...] = jnp.zeros_like(gain_grad_ref)
    own.wait()
    for copy in sent:
        copy.wait_recv()
    query_at = lax.broadcasted_iota(jnp.int32, (rows, rows), 0)
    key_at = lax.broadcasted_iota(jnp.int32, (rows, rows), 1)
    blank = jnp.zeros((rows, HP - DH), f32)

    def one(seq, carry):
        keep = (key_at <= query_at) & (key_at < len_ref[seq])
        weights = [p_ref[seq, 0], p_ref[seq, 1]]
        grad_mixed = []
        grads = grads_ref[seq].astype(f32)
        for head in range(2):
            cols = slice(head * HP, (head + 1) * HP)
            out = o_ref[seq, :, cols]
            grad = jnp.concatenate([grads[:, head * DH : (head + 1) * DH], blank], axis=1)
            scale = lax.rsqrt(jnp.sum(out * out, axis=-1, keepdims=True) * (1.0 / DH) + eps_norm)
            unit = out * scale
            gain_grad_ref[:, cols] += jnp.sum(grad * unit, axis=0, keepdims=True)
            inner = grad * gain_ref[:, cols]
            grad_out = scale * (inner - unit * (jnp.sum(inner * unit, axis=-1, keepdims=True) * (1.0 / DH)))
            grad_out = grad_out.astype(bf16)
            value = qkv_ref[seq, :, (4 + head) * HP : (5 + head) * HP]
            mixed = (mix_ref[2 * head] * weights[0] + mix_ref[2 * head + 1] * weights[1]).astype(bf16)
            dqkv_ref[seq, :, (4 + head) * HP : (5 + head) * HP] = dot_tn(mixed, grad_out).astype(bf16)
            back = dot_nt(grad_out, value)
            grad_mixed.append(back)
            for source in range(2):
                mixer_ref[2 * head + source : 2 * head + source + 1, :] += jnp.sum(
                    back * weights[source], axis=0, keepdims=True
                )
        for head in range(2):
            grad_weight = mix_ref[head] * grad_mixed[0] + mix_ref[2 + head] * grad_mixed[1]
            weight = weights[head]
            grad_conv = weight * (grad_weight - jnp.sum(weight * grad_weight, axis=-1, keepdims=True))
            wide = shifted_up(pad_ref, grad_conv).astype(bf16)
            theta_ref[head] += dot_tn(s_ref[seq, head], wide)
            grad_scores = jnp.zeros((rows, rows), f32)
            for lag in range(CQ):
                grad_scores += dot_nt(
                    wide[:, lag * rows : (lag + 1) * rows], toep_ref[head, lag * rows : (lag + 1) * rows, :]
                )
            grad_scores = jnp.where(keep, grad_scores * (1.0 / math.sqrt(DH)), 0.0).astype(bf16)
            query = qkv_ref[seq, :, head * HP : (head + 1) * HP]
            key = qkv_ref[seq, :, (2 + head) * HP : (3 + head) * HP]
            dqkv_ref[seq, :, head * HP : (head + 1) * HP] = dot(grad_scores, key).astype(bf16)
            dqkv_ref[seq, :, (2 + head) * HP : (3 + head) * HP] = dot_tn(grad_scores, query).astype(bf16)
        return carry

    lax.fori_loop(0, 4, one, 0)
    gather.onward()
    lax.fori_loop(4, seqs, one, 0)
    gather.last()
    gather.finish()
    strips = strips_ref[...]
    for col in range(ROW_TILES):
        at = slice(col * BLK, (col + 1) * BLK)
        go_ref[:, at] = dot_tn(strips, all_ref[:, :, at].reshape(seqs * rows, BLK)).astype(bf16)
    gather.drain()
    for copy in sent:
        copy.wait_send()


def chip_at(mask):
    return {axis: 1 - lax.axis_index(axis) for axis in BITS if mask & BITS[axis]}


def run_back(lengths, mix, qkv, toep, gain, scores, weights, outs, sent, dattn, strips):
    seqs, rows, _ = qkv.shape
    dma = pltpu.SemaphoreType.DMA
    return pl.pallas_call(
        back_body,
        in_specs=[SMEM, SMEM] + [VMEM] * 9,
        out_specs=[VMEM] * 5,
        out_shape=[
            jax.ShapeDtypeStruct((seqs, rows, 6 * HP), bf16),
            jax.ShapeDtypeStruct((2, rows, CQ * rows), f32),
            jax.ShapeDtypeStruct((8, rows), f32),
            jax.ShapeDtypeStruct((1, 2 * HP), f32),
            jax.ShapeDtypeStruct((2 * DH, D), bf16),
        ],
        scratch_shapes=[
            pltpu.VMEM((rows + 8, rows), f32), pltpu.VMEM((seqs, rows, 2 * DH), bf16),
            pltpu.VMEM((CHIPS, rows, D), bf16), dma, dma((8,)), dma((8,)),
        ] + hop_sems(),
        name="attention_back",
        compiler_params=pltpu.CompilerParams(collective_id=4, has_side_effects=True, vmem_limit_bytes=32 * 2**20),
    )(lengths, mix, qkv, toep, gain, scores, weights, outs, sent, dattn, strips)


def share_body(
    parts_ref, gq_ref, go_ref, dxn_ref, qkv_ref, out_ref,
    core_q, core_o, in_q, in_o, core_send, core_recv, send, recv, go_send, go_recv, *scatter_args,
):
    g, a, b, c, y = (lax.axis_index(axis) for axis in ALL)
    me = chip_index()
    barrier = pltpu.get_barrier_semaphore()
    pl.semaphore_signal(barrier, inc=1, device_id=across("c"))
    for mask in range(1, 16):
        pl.semaphore_signal(barrier, inc=1, device_id=wide_at(mask))
    pl.semaphore_wait(barrier, 16)
    to_core = [
        push(gq_ref.at[:, 1 - c], core_q, core_send.at[0], core_recv.at[0], across("c")),
        push(go_ref.at[:, 1 - c], core_o, core_send.at[1], core_recv.at[1], across("c")),
    ]
    scatter = Scatter(parts_ref, *scatter_args)
    scatter.start()
    to_core[0].wait_recv()
    for row in range(ROW_TILES):
        core_q[row] = (core_q[row].astype(f32) + gq_ref[row, c].astype(f32)).astype(bf16)
    slot = g * CHIPS + me
    sent = []
    for mask in (15, 14, 13, 11, 12, 10, 9, 8, 7, 6, 5, 3, 4, 2, 1):
        to = flipped(me, [axis for axis in BITS if mask & BITS[axis]])
        sent.append(
            push(
                core_q.at[:, to, other_bit("g", mask & 8)], in_q.at[slot], send.at[mask], recv.at[mask], wide_at(mask)
            )
        )
    to_core[1].wait_recv()
    core_o[...] = (core_o[...].astype(f32) + go_ref[:, c].astype(f32)).astype(bf16)
    to_group = push(core_o.at[:, 1 - g], in_o, go_send, go_recv, across("g"))
    in_q[slot] = core_q[:, me, g]
    scatter.onward()
    scatter.last()
    dxn_ref[0 : dxn_ref.shape[0] // 2] = scatter.finish(0)
    dxn_ref[dxn_ref.shape[0] // 2 :] = scatter.finish(1)
    to_group.wait_recv()
    out_ref[...] = (in_o[...].astype(f32) + core_o[:, g].astype(f32)).astype(bf16)
    for copy in sent:
        copy.wait_recv()
    for row in range(ROW_TILES):
        sums = [in_q[chip, row].astype(f32) + in_q[CHIPS + chip, row].astype(f32) for chip in range(CHIPS)]
        for which in range(3):
            qkv_ref[which, row] = jnp.concatenate(
                [part[:, which * 2 * DH : (which + 1) * 2 * DH] for part in sums], axis=1
            ).astype(bf16)
    scatter.drain()
    for copy in to_core + sent + [to_group]:
        copy.wait_send()


def wide_at(mask):
    at = chip_at(mask & 7)
    if mask & 8:
        at["g"] = 1 - lax.axis_index("g")
    return at


def share(parts, gq, go):
    _, rows, width = parts.shape
    dma = pltpu.SemaphoreType.DMA
    part = gq.shape[-2]
    return pl.pallas_call(
        share_body,
        in_specs=[VMEM] * 3,
        out_specs=[VMEM] * 3,
        out_shape=[
            jax.ShapeDtypeStruct((rows, width), f32),
            jax.ShapeDtypeStruct((3, ROW_TILES, part, D), bf16),
            jax.ShapeDtypeStruct((ROW_TILES, part, D), bf16),
        ],
        scratch_shapes=[
            pltpu.VMEM((ROW_TILES, CHIPS, 2, part, 6 * DH), bf16), pltpu.VMEM((ROW_TILES, 2, part, D), bf16),
            pltpu.VMEM((2 * CHIPS, ROW_TILES, part, 6 * DH), bf16), pltpu.VMEM((ROW_TILES, part, D), bf16),
            dma((2,)), dma((2,)), dma((16,)), dma((16,)), dma, dma,
        ] + scatter_scratch(rows, width),
        name="share_gradients",
        compiler_params=pltpu.CompilerParams(collective_id=5, has_side_effects=True, vmem_limit_bytes=40 * 2**20),
    )(parts, gq, go)


def to_slots_body(slots_ref, vec_ref, out_ref, vecs_ref, local_sems, send, recv, vec_send, vec_recv):
    devices = lax.axis_size(ALL)
    me = device_index()
    local = [
        pltpu.make_async_copy(slots_ref.at[me], out_ref.at[me], local_sems.at[0]),
        pltpu.make_async_copy(vec_ref.at[me], vecs_ref.at[me], local_sems.at[1]),
    ]
    for copy in local:
        copy.start()
    greet_all()

    def push_all(step, carry):
        to = lax.rem(me + step, devices)
        pltpu.make_async_remote_copy(
            src_ref=vec_ref.at[to], dst_ref=vecs_ref.at[me], send_sem=vec_send, recv_sem=vec_recv, device_id=device_at(to)
        ).start()
        pltpu.make_async_remote_copy(
            src_ref=slots_ref.at[to], dst_ref=out_ref.at[me], send_sem=send, recv_sem=recv, device_id=device_at(to)
        ).start()
        return carry

    lax.fori_loop(1, devices, push_all, 0)
    for ref, one, two in ((vecs_ref, vec_send, vec_recv), (out_ref, send, recv)):
        others = ref.at[pl.ds(0, devices - 1)]
        pltpu.make_async_copy(others, others, two).wait()
        pltpu.make_async_copy(others, others, one).wait()
    for copy in local:
        copy.wait()


def to_slots(slots, vecs):
    dma = pltpu.SemaphoreType.DMA
    return pl.pallas_call(
        to_slots_body,
        in_specs=[ANYS] * 2,
        out_specs=[ANYS] * 2,
        out_shape=[jax.ShapeDtypeStruct(slots.shape, slots.dtype), jax.ShapeDtypeStruct(vecs.shape, vecs.dtype)],
        scratch_shapes=[dma((2,))] + [dma] * 4,
        name="to_slots",
        compiler_params=pltpu.CompilerParams(collective_id=6, has_side_effects=True),
    )(slots, vecs)


def body_fast(
    layer_input, lengths, cotangent, w_query, w_key, w_value, w_out, w_gate, w_up, w_down, vec_copy, owners,
    basis_left, basis_right, block_master, block_first, block_second, vec_master, vec_first, vec_second,
):
    chip = chip_index()
    seq_len = layer_input.shape[0]
    length = lengths[0]
    own_vec = vec_copy.shape[0]
    devices, fs_size, reps = lax.axis_size(ALL), lax.axis_size(FS), lax.axis_size("y")

    small = jnp.concatenate(
        [vec_copy.astype(f32), jnp.zeros((1023 - own_vec,), f32), length.astype(f32).reshape(1)]
    ).reshape(8, 128)
    blocks = jnp.concatenate([w.reshape(-1, CHIPS, 2 * DH) for w in (w_query, w_key, w_value)], axis=2)
    x_all, small_all, w_qkv = dispatch(layer_input, small, jnp.transpose(blocks, (1, 0, 2)))
    w_gate, w_up, w_down, cotangent, x_all, small_all, w_qkv = lax.optimization_barrier(
        (w_gate, w_up, w_down, cotangent, x_all, small_all, w_qkv)
    )
    small_all = small_all.reshape(fs_size, reps, 1024)
    vector = small_all[:, 0, :own_vec].reshape(-1)
    group_lengths = small_all[:, :, 1023].reshape(-1, 2, 2, 2, reps)
    group_lengths = lax.dynamic_index_in_dim(group_lengths, lax.axis_index("g"), 0, keepdims=False)
    group_lengths = lax.dynamic_index_in_dim(group_lengths, lax.axis_index("c"), 2, keepdims=False)
    group_lengths = jnp.transpose(group_lengths, (2, 0, 1)).reshape(CHIPS).astype(jnp.int32)
    gain_attn, gain_head, gain_ffn = vector[:D], vector[D : 2 * D], vector[2 * D : 3 * D]
    conv_end = 3 * D + H * CQ * CK
    theta = lax.dynamic_slice_in_dim(vector[3 * D : conv_end].reshape(H, CQ, CK), chip * 2, 2, 0)
    mixer = lax.dynamic_slice_in_dim(vector[conv_end : conv_end + 2 * H].reshape(H, 2), chip * 2, 2, 0)
    mix = mixer.reshape(4)
    gain_pair = jnp.pad(
        lax.dynamic_slice_in_dim(gain_head.reshape(H, DH), chip * 2, 2, 0), ((0, 0), (0, HP - DH))
    ).reshape(1, 2 * HP)
    toep = jnp.zeros((2, CQ, seq_len, seq_len), f32)
    offset = (
        jnp.arange(seq_len, dtype=jnp.int32)[:, None] - jnp.arange(seq_len, dtype=jnp.int32)[None, :] + CK // 2
    )
    for tap in range(CK):
        toep = jnp.where(offset[None, None] == tap, theta[:, :, tap][:, :, None, None], toep)
    toep = toep.astype(bf16).reshape(2, CQ * seq_len, seq_len)
    w_qkv = jnp.pad(w_qkv.reshape(D, 6, DH), ((0, 0), (0, 0), (0, HP - DH))).reshape(D, 6 * HP)
    w_o = lax.all_gather(w_out, FS, axis=0, tiled=True)
    w_in = to_columns(jnp.concatenate([spread_columns(w, BLK) for w in (w_gate, w_up)], axis=2))
    w_dn = down_rows(w_down, chip)
    valid = (jnp.arange(seq_len) < length).astype(f32)
    dy = cotangent.astype(f32) * valid[:, None]
    dy_rows = gather_slow(dy.astype(bf16)).reshape(CHIPS * seq_len, D)

    input_float = layer_input.astype(f32)
    input_scale = rms(input_float)
    x_rows = x_all.reshape(CHIPS * seq_len, D).astype(f32)
    xn_rows = (x_rows * rms(x_rows) * gain_attn).astype(bf16)
    qkv = dot(xn_rows, w_qkv).astype(bf16).reshape(CHIPS, seq_len, 6 * HP)
    heads_pad, scores, weights, outs = run_forward(group_lengths, mix, qkv, toep, gain_pair)
    heads_sent = heads_pad.reshape(CHIPS, seq_len, 2, HP)[..., :DH].reshape(CHIPS, seq_len, 2 * DH)
    heads = jnp.transpose(exchange_chips(heads_sent), (1, 0, 2)).reshape(seq_len, D)
    hmid = input_float + dot(heads, w_o)
    hmid_scale = rms(hmid)
    hn_rows = gather_chips((hmid * hmid_scale * gain_ffn).astype(bf16), 2).reshape(CHIPS * seq_len, D)
    both = dot(hn_rows, w_in)
    gate, up = both[:, :BLK], both[:, BLK:]
    sig = jax.nn.sigmoid(gate)
    silu = gate * sig
    inner = (silu * up).astype(bf16)

    strip = BLK // (2 * CHIPS)
    part = strip // 2
    dinner = dot_nt(dy_rows, w_dn)
    dgate = (dinner * up * (sig * (1.0 + gate * (1.0 - sig)))).astype(bf16)
    dup = (dinner * silu).astype(bf16)
    dboth = jnp.concatenate([dgate, dup], axis=1)
    dhn = scatter_chips(dot_nt(dboth, w_in).astype(bf16).reshape(CHIPS, seq_len, D), 3)
    ffn = scatter_slow(dot(inner, w_dn).reshape(CHIPS, seq_len, D))
    layer_output = (hmid + ffn).astype(bf16)
    dhmid, grad_gain_ffn = norm_backward(hmid, hmid_scale, gain_ffn, dhn)
    dhmid = dhmid + dy
    dattn = dhmid.astype(bf16)
    dheads = dot_nt(dattn, w_o).astype(bf16).reshape(seq_len, CHIPS, 2 * DH)
    strips = jnp.transpose(heads.reshape(seq_len, 2 * ROW_TILES, CHIPS, strip), (2, 0, 1, 3))
    strips = exchange_chips(strips.reshape(CHIPS, seq_len, 2 * ROW_TILES * strip)).reshape(CHIPS * seq_len, -1)
    dqkv, theta_sums, mixer_sums, gain_sums, grad_out = run_back(
        group_lengths, mix, qkv, toep, gain_pair, scores, weights, outs, jnp.transpose(dheads, (1, 0, 2)), dattn, strips
    )
    dqkv_rows = dqkv.reshape(CHIPS * seq_len, 6 * HP)
    dxn_parts = dot_nt(dqkv_rows, w_qkv).astype(bf16).reshape(CHIPS, seq_len, D)
    grad_qkv = dot_tn(xn_rows, dqkv_rows).astype(bf16).reshape(D, 6, HP)[..., :DH]
    dxn, qkv_sums, out_sums = share(
        dxn_parts,
        grad_qkv.reshape(ROW_TILES, 2, CHIPS, 2, part, 6 * DH),
        grad_out.reshape(ROW_TILES, 2, 2, part, D),
    )
    dinput, grad_gain_attn = norm_backward(input_float, input_scale, gain_attn, dxn)
    input_grad = dinput + dhmid

    taps = jnp.asarray(band())
    theta_sums = theta_sums.reshape(2, seq_len, CQ, seq_len)
    grad_theta = jnp.stack(
        [jnp.sum(jnp.where(taps[tap][None, :, None, :], theta_sums, 0.0), axis=(1, 3)) for tap in range(CK)], axis=2
    )
    grad_mixer = jnp.sum(mixer_sums[:4], axis=1)
    vector_grad = jnp.concatenate(
        [
            grad_gain_attn,
            lax.dynamic_update_slice_in_dim(
                jnp.zeros((D,), f32), gain_sums.reshape(2, HP)[:, :DH].reshape(-1), chip * 2 * DH, 0
            ),
            grad_gain_ffn,
            lax.dynamic_update_slice_in_dim(
                jnp.zeros((H * CQ * CK,), f32), grad_theta.reshape(-1), chip * 2 * CQ * CK, 0
            ),
            lax.dynamic_update_slice_in_dim(jnp.zeros((2 * H,), f32), grad_mixer, chip * 4, 0),
        ]
    )
    pieces = jnp.pad(vector_grad.reshape(fs_size, 1, own_vec), ((0, 0), (0, 0), (0, 1024 - own_vec)))
    pieces = jnp.broadcast_to(pieces, (fs_size, reps, 1024)).reshape(devices, 8, 128)

    grad_in = dot_tn(hn_rows, dboth).reshape(ROW_TILES, 2, CHIPS, strip, 2, BLK)
    grad_down = dot_tn(inner, dy_rows).reshape(2, CHIPS, strip, ROW_TILES, BLK)
    grad_in = jnp.transpose(half_for_core(grad_in, 1), (1, 3, 0, 2, 4)).reshape(CHIPS, 2 * ROW_TILES, strip, BLK)
    grad_down = jnp.transpose(half_for_core(grad_down, 0), (0, 2, 1, 3))
    ffn_tiles = exchange_chips(jnp.concatenate([grad_in, grad_down], axis=1).astype(bf16))
    gate_tiles = jnp.transpose(ffn_tiles[:, : 2 * ROW_TILES], (1, 0, 2, 3)).reshape(-1, strip, BLK)
    down_tiles = ffn_tiles[:, 2 * ROW_TILES :].reshape(-1, strip, BLK)
    ffn_sums = sum_groups(jnp.concatenate([gate_tiles, down_tiles], axis=0))

    own_slots = basis_left.shape[0]
    slot_total = own_slots * devices
    sums = jnp.concatenate(
        [
            jnp.transpose(qkv_sums.reshape(3, ROW_TILES, part, ROW_TILES, BLK), (0, 1, 3, 2, 4)).reshape(-1, part, BLK),
            jnp.transpose(out_sums.reshape(ROW_TILES, part, ROW_TILES, BLK), (0, 2, 1, 3)).reshape(-1, part, BLK),
            ffn_sums,
        ],
        axis=0,
    )
    matches = (jnp.arange(slot_total)[:, None] == owners[None, :]).astype(bf16)
    slots = dot(matches, sums.reshape(sums.shape[0], -1)).astype(bf16)
    slots, pieces = to_slots(slots.reshape(devices, own_slots * part, BLK), pieces)
    vector_total = jnp.sum(pieces, axis=0).reshape(1024)[:own_vec]
    slots = slots.reshape(2, 2, 2, 2, 2, own_slots, part, BLK)
    own_grad = jnp.transpose(slots, (5, 3, 4, 1, 2, 0, 6, 7)).reshape(own_slots, BLK, BLK)

    left_low, right_low = basis_left.astype(bf16), basis_right.astype(bf16)
    rotated = jnp.einsum("sia,sij->saj", left_low, own_grad, preferred_element_type=f32)
    rotated = jnp.einsum("saj,sjb->sab", rotated.astype(bf16), right_low, preferred_element_type=f32)
    first_new = beta_first * block_first + (1.0 - beta_first) * rotated
    second_new = beta_second * block_second + (1.0 - beta_second) * rotated * rotated
    direction = (first_new / (jnp.sqrt(second_new) + eps_adam)).astype(bf16)
    turned = jnp.einsum("sia,sab->sib", left_low, direction, preferred_element_type=f32)
    turned = jnp.einsum("sib,sjb->sij", turned.astype(bf16), right_low, preferred_element_type=f32)
    master_new = block_master - rate_block * (turned + decay_block * block_master)
    vec_first_new = beta_first * vec_first + (1.0 - beta_first) * vector_total
    vec_second_new = beta_second * vec_second + (1.0 - beta_second) * vector_total * vector_total
    vec_master_new = vec_master - rate_vector * vec_first_new / (jnp.sqrt(vec_second_new) + eps_adam)
    return (
        layer_output, input_grad, first_new, second_new, master_new, master_new.astype(bf16),
        vec_first_new, vec_second_new, vec_master_new, vec_master_new.astype(bf16),
    )


def solution(mesh):
    fsdp, rep = mesh.shape["fsdp"], mesh.shape["rep"]
    fine = Mesh(mesh.devices.reshape(fsdp // 8, 2, 2, 2, rep), ALL)
    rows, both = P(ALL, None), P(ALL, None, None)
    weight, vec = P(FS, None), P(FS)
    return jax.shard_map(
        body_fast if (fsdp, rep) == (16, 2) else body_any,
        mesh=fine,
        in_specs=(rows, P(ALL), rows) + (weight,) * 7 + (vec, P()) + (both,) * 5 + (vec,) * 3,
        out_specs=(rows, rows) + (both,) * 4 + (vec,) * 4,
        check_vma=False,
    )
```

```python
import math

import jax
import jax.numpy as jnp
import numpy as np
from jax import lax
from jax.experimental import pallas as pl
from jax.experimental.pallas import tpu as pltpu
from jax.sharding import Mesh
from jax.sharding import PartitionSpec as P

H = 16
DH = 96
HP = 128
D = H * DH
FF = 4096
CQ = 6
CK = 11
BLK = 512
CHIPS = 8
ROW_TILES = D // BLK
FF_TILES = FF // BLK

eps_norm = 1e-05
eps_adam = 1e-08
rate_block = 0.02
rate_vector = 0.3
decay_block = 0.1
beta_first = 0.5
beta_second = 0.5

FS = ("g", "a", "b", "c")
CHIP = ("y", "a", "b")
ALL = ("g", "a", "b", "c", "y")
bf16 = jnp.bfloat16
f32 = jnp.float32


def dot(left, right):
    return jnp.dot(left, right, preferred_element_type=f32)


def dot_nt(left, right):
    return lax.dot_general(left, right, (((1,), (1,)), ((), ())), preferred_element_type=f32)


def dot_tn(left, right):
    return lax.dot_general(left, right, (((0,), (0,)), ((), ())), preferred_element_type=f32)


def rms(values):
    return lax.rsqrt(jnp.mean(values * values, axis=-1, keepdims=True) + eps_norm)


def norm_backward(values, scale, gain, grad):
    unit = values * scale
    inner = grad * gain
    grad_values = scale * (inner - unit * jnp.mean(inner * unit, axis=-1, keepdims=True))
    return grad_values, jnp.sum(grad * unit, axis=0)


def shifted_down(pad_ref, values):
    rows = values.shape[0]
    pad_ref[8 : 8 + rows, :] = values
    return jnp.concatenate(
        [values] + [pad_ref[8 - lag : 8 - lag + rows, :] for lag in range(1, CQ)], axis=1
    )


def shifted_up(pad_ref, values):
    rows = values.shape[0]
    pad_ref[0:rows, :] = values
    return jnp.concatenate(
        [values] + [pad_ref[lag : lag + rows, :] for lag in range(1, CQ)], axis=1
    )


def attention_forward(len_ref, mix_ref, qkv_ref, toep_ref, gain_ref, heads_ref, s_ref, p_ref, o_ref, pad_ref):
    rows = qkv_ref.shape[1]
    length = len_ref[pl.program_id(0)]
    query_at = lax.broadcasted_iota(jnp.int32, (rows, rows), 0)
    key_at = lax.broadcasted_iota(jnp.int32, (rows, rows), 1)
    keep = (key_at <= query_at) & (key_at < length)
    pad_ref[0:8, :] = jnp.zeros((8, rows), f32)
    weights = []
    for head in range(2):
        query = qkv_ref[0, :, head * HP : (head + 1) * HP]
        key = qkv_ref[0, :, (2 + head) * HP : (3 + head) * HP]
        scores = jnp.where(keep, dot_nt(query, key) * (1.0 / math.sqrt(DH)), 0.0)
        s_ref[0, head] = scores.astype(bf16)
        wide = shifted_down(pad_ref, scores)
        high = wide.astype(bf16)
        low = (wide - high.astype(f32)).astype(bf16)
        conv = dot(high, toep_ref[head]) + dot(low, toep_ref[head])
        logits = jnp.where(keep, conv, -1e30)
        weight = jnp.exp(logits - jnp.max(logits, axis=-1, keepdims=True))
        weight = weight / jnp.sum(weight, axis=-1, keepdims=True)
        p_ref[0, head] = weight
        weights.append(weight)
    for head in range(2):
        mixed = mix_ref[2 * head] * weights[0] + mix_ref[2 * head + 1] * weights[1]
        value = qkv_ref[0, :, (4 + head) * HP : (5 + head) * HP]
        out = dot(mixed.astype(bf16), value)
        o_ref[0, :, head * HP : (head + 1) * HP] = out
        scale = lax.rsqrt(jnp.sum(out * out, axis=-1, keepdims=True) * (1.0 / DH) + eps_norm)
        heads_ref[0, :, head * HP : (head + 1) * HP] = (
            out * scale * gain_ref[:, head * HP : (head + 1) * HP]
        ).astype(bf16)


def attention_backward(
    len_ref, mix_ref, qkv_ref, toep_ref, gain_ref, s_ref, p_ref, o_ref, grad_ref,
    dqkv_ref, theta_ref, mixer_ref, gain_grad_ref, pad_ref,
):
    rows = qkv_ref.shape[1]
    length = len_ref[pl.program_id(0)]
    query_at = lax.broadcasted_iota(jnp.int32, (rows, rows), 0)
    key_at = lax.broadcasted_iota(jnp.int32, (rows, rows), 1)
    keep = (key_at <= query_at) & (key_at < length)
    pad_ref[rows : rows + 8, :] = jnp.zeros((8, rows), f32)

    @pl.when(pl.program_id(0) == 0)
    def _():
        theta_ref[...] = jnp.zeros_like(theta_ref)
        mixer_ref[...] = jnp.zeros_like(mixer_ref)
        gain_grad_ref[...] = jnp.zeros_like(gain_grad_ref)

    weights = [p_ref[0, 0], p_ref[0, 1]]
    grad_mixed = []
    for head in range(2):
        cols = slice(head * HP, (head + 1) * HP)
        out = o_ref[0, :, cols]
        grad = grad_ref[0, :, cols].astype(f32)
        scale = lax.rsqrt(jnp.sum(out * out, axis=-1, keepdims=True) * (1.0 / DH) + eps_norm)
        unit = out * scale
        gain_grad_ref[:, cols] += jnp.sum(grad * unit, axis=0, keepdims=True)
        inner = grad * gain_ref[:, cols]
        grad_out = scale * (inner - unit * (jnp.sum(inner * unit, axis=-1, keepdims=True) * (1.0 / DH)))
        grad_out = grad_out.astype(bf16)
        value = qkv_ref[0, :, (4 + head) * HP : (5 + head) * HP]
        mixed = (mix_ref[2 * head] * weights[0] + mix_ref[2 * head + 1] * weights[1]).astype(bf16)
        dqkv_ref[0, :, (4 + head) * HP : (5 + head) * HP] = dot_tn(mixed, grad_out).astype(bf16)
        back = dot_nt(grad_out, value)
        grad_mixed.append(back)
        for source in range(2):
            mixer_ref[2 * head + source : 2 * head + source + 1, :] += jnp.sum(
                back * weights[source], axis=0, keepdims=True
            )
    for head in range(2):
        grad_weight = mix_ref[head] * grad_mixed[0] + mix_ref[2 + head] * grad_mixed[1]
        weight = weights[head]
        grad_conv = weight * (grad_weight - jnp.sum(weight * grad_weight, axis=-1, keepdims=True))
        wide = shifted_up(pad_ref, grad_conv).astype(bf16)
        theta_ref[head] += dot_tn(s_ref[0, head], wide)
        grad_scores = jnp.zeros((rows, rows), f32)
        for lag in range(CQ):
            grad_scores += dot_nt(
                wide[:, lag * rows : (lag + 1) * rows], toep_ref[head, lag * rows : (lag + 1) * rows, :]
            )
        grad_scores = jnp.where(keep, grad_scores * (1.0 / math.sqrt(DH)), 0.0).astype(bf16)
        query = qkv_ref[0, :, head * HP : (head + 1) * HP]
        key = qkv_ref[0, :, (2 + head) * HP : (3 + head) * HP]
        dqkv_ref[0, :, head * HP : (head + 1) * HP] = dot(grad_scores, key).astype(bf16)
        dqkv_ref[0, :, (2 + head) * HP : (3 + head) * HP] = dot_tn(grad_scores, query).astype(bf16)


SMEM = pl.BlockSpec(memory_space=pltpu.SMEM)


def seq_spec(*dims):
    return pl.BlockSpec((1,) + dims, lambda s: (s,) + (0,) * len(dims))


def whole_spec(*dims):
    return pl.BlockSpec(dims, lambda s: (0,) * len(dims))


def run_forward(lengths, mix, qkv, toep, gain):
    seqs, rows, _ = qkv.shape
    return pl.pallas_call(
        attention_forward,
        grid=(seqs,),
        in_specs=[SMEM, SMEM, seq_spec(rows, 6 * HP), whole_spec(2, CQ * rows, rows), whole_spec(1, 2 * HP)],
        out_specs=[seq_spec(rows, 2 * HP), seq_spec(2, rows, rows), seq_spec(2, rows, rows), seq_spec(rows, 2 * HP)],
        out_shape=[
            jax.ShapeDtypeStruct((seqs, rows, 2 * HP), bf16),
            jax.ShapeDtypeStruct((seqs, 2, rows, rows), bf16),
            jax.ShapeDtypeStruct((seqs, 2, rows, rows), f32),
            jax.ShapeDtypeStruct((seqs, rows, 2 * HP), f32),
        ],
        scratch_shapes=[pltpu.VMEM((rows + 8, rows), f32)],
        name="attention_forward",
        compiler_params=pltpu.CompilerParams(vmem_limit_bytes=24 * 2**20),
        cost_estimate=pl.CostEstimate(flops=2 * 10**9, bytes_accessed=8 * 2**20, transcendentals=10**5),
    )(lengths, mix, qkv, toep, gain)


def run_backward(lengths, mix, qkv, toep, gain, scores, weights, outs, grads):
    seqs, rows, _ = qkv.shape
    return pl.pallas_call(
        attention_backward,
        grid=(seqs,),
        in_specs=[
            SMEM, SMEM, seq_spec(rows, 6 * HP), whole_spec(2, CQ * rows, rows), whole_spec(1, 2 * HP),
            seq_spec(2, rows, rows), seq_spec(2, rows, rows), seq_spec(rows, 2 * HP), seq_spec(rows, 2 * HP),
        ],
        out_specs=[seq_spec(rows, 6 * HP), whole_spec(2, rows, CQ * rows), whole_spec(8, rows), whole_spec(1, 2 * HP)],
        out_shape=[
            jax.ShapeDtypeStruct((seqs, rows, 6 * HP), bf16),
            jax.ShapeDtypeStruct((2, rows, CQ * rows), f32),
            jax.ShapeDtypeStruct((8, rows), f32),
            jax.ShapeDtypeStruct((1, 2 * HP), f32),
        ],
        scratch_shapes=[pltpu.VMEM((rows + 8, rows), f32)],
        name="attention_backward",
        compiler_params=pltpu.CompilerParams(vmem_limit_bytes=24 * 2**20),
        cost_estimate=pl.CostEstimate(flops=4 * 10**9, bytes_accessed=12 * 2**20, transcendentals=10**5),
    )(lengths, mix, qkv, toep, gain, scores, weights, outs, grads)


BITS = {"y": 4, "a": 2, "b": 1}
HOPS = (("y", "b", "a"), ("a", "y", "b"), ("b", "a", "y"))
THIRDS = ((0, 48), (48, 48), (96, 32))
ANYS = pl.BlockSpec(memory_space=pl.ANY)


def chip_index():
    return (lax.axis_index("y") * 2 + lax.axis_index("a")) * 2 + lax.axis_index("b")


def flipped(chip, axes):
    for axis in axes:
        chip = chip + BITS[axis] * (1 - 2 * lax.axis_index(axis))
    return chip


def across(axis):
    return {axis: 1 - lax.axis_index(axis)}


def device_index():
    index = lax.axis_index("g")
    for axis in ("a", "b", "c", "y"):
        index = index * lax.axis_size(axis) + lax.axis_index(axis)
    return index


def device_at(index):
    at = {}
    for axis in ("y", "c", "b", "a", "g"):
        at[axis] = lax.rem(index, lax.axis_size(axis))
        index = lax.div(index, lax.axis_size(axis))
    return at


def greet_all():
    devices = lax.axis_size(ALL)
    me = device_index()
    barrier = pltpu.get_barrier_semaphore()

    def greet(step, carry):
        pl.semaphore_signal(barrier, inc=1, device_id=device_at(lax.rem(me + step, devices)))
        return carry

    lax.fori_loop(1, devices, greet, 0)
    pl.semaphore_wait(barrier, devices - 1)


def greet_neighbours():
    barrier = pltpu.get_barrier_semaphore()
    for axis in BITS:
        pl.semaphore_signal(barrier, inc=1, device_id=across(axis))
    pl.semaphore_wait(barrier, 3)


def remote(src, dst, send, recv, axis):
    return pltpu.make_async_remote_copy(src_ref=src, dst_ref=dst, send_sem=send, recv_sem=recv, device_id=across(axis))


def gather_body(x_ref, out_ref, *sems):
    greet_neighbours()
    gather_hops(x_ref, out_ref, *sems)


def gather_first_body(x_ref, vec_ref, out_ref, vecs_ref, vec_send, vec_recv, vec_local, *sems):
    devices = lax.axis_size(ALL)
    me = device_index()
    local = pltpu.make_async_copy(vec_ref, vecs_ref.at[me], vec_local)
    local.start()
    greet_all()

    def push(step, carry):
        pltpu.make_async_remote_copy(
            src_ref=vec_ref, dst_ref=vecs_ref.at[me], send_sem=vec_send, recv_sem=vec_recv,
            device_id=device_at(lax.rem(me + step, devices)),
        ).start()
        return carry

    lax.fori_loop(1, devices, push, 0)
    gather_hops(x_ref, out_ref, *sems)
    others = vecs_ref.at[pl.ds(0, devices - 1)]
    pltpu.make_async_copy(others, others, vec_recv).wait()
    pltpu.make_async_copy(others, others, vec_send).wait()
    local.wait()


def gather_hops(x_ref, out_ref, local_sem, send1, recv1, send2, recv2, send3, recv3):
    me = chip_index()
    rows = x_ref.shape[0]
    half = rows // 2
    local = pltpu.make_async_copy(x_ref, out_ref.at[me], local_sem)
    local.start()
    first = []
    for part in range(2):
        here = pl.ds(part * half, half)
        for at, (axis, _, _) in enumerate(HOPS):
            copy = remote(x_ref.at[here], out_ref.at[me, here], send1.at[at, part], recv1.at[at, part], axis)
            copy.start()
            first.append(copy)
    second = []
    for part in range(2):
        here = pl.ds(part * half, half)
        for at, (axis, onward, _) in enumerate(HOPS):
            first[part * 3 + at].wait_recv()
            block = out_ref.at[flipped(me, (axis,)), here]
            copy = remote(block, block, send2.at[at, part], recv2.at[at, part], onward)
            copy.start()
            second.append(copy)
    third = []
    for at, (axis, onward, last) in enumerate(HOPS):
        begin, count = THIRDS[at]
        block = flipped(me, (axis, onward))
        for part in range(2):
            if part * half < begin + count and begin < (part + 1) * half:
                second[part * 3 + at].wait_recv()
        piece = out_ref.at[block, pl.ds(begin, count)]
        copy = remote(piece, piece, send3.at[at], recv3.at[at], last)
        copy.start()
        third.append(copy)
    for at in range(3):
        begin, count = THIRDS[at]
        for part in range(2):
            if not (part * half < begin + count and begin < (part + 1) * half):
                second[part * 3 + at].wait_recv()
    for copy in third:
        copy.wait_recv()
    for copy in first + second + third:
        copy.wait_send()
    local.wait()


def hop_sems():
    dma = pltpu.SemaphoreType.DMA
    return [dma] + [dma((3, 2))] * 4 + [dma((3,))] * 2


def gather_first(rows, vec, collective_id):
    count, width = rows.shape
    return pl.pallas_call(
        gather_first_body,
        in_specs=[ANYS, ANYS],
        out_specs=[ANYS, ANYS],
        out_shape=[
            jax.ShapeDtypeStruct((CHIPS, count, width), rows.dtype),
            jax.ShapeDtypeStruct((lax.axis_size(ALL),) + vec.shape, vec.dtype),
        ],
        scratch_shapes=[pltpu.SemaphoreType.DMA] * 3 + hop_sems(),
        name="gather_first",
        compiler_params=pltpu.CompilerParams(collective_id=collective_id, has_side_effects=True),
    )(rows, vec)


def gather_chips(rows, collective_id):
    count, width = rows.shape
    return pl.pallas_call(
        gather_body,
        in_specs=[ANYS],
        out_specs=ANYS,
        out_shape=jax.ShapeDtypeStruct((CHIPS, count, width), rows.dtype),
        scratch_shapes=hop_sems(),
        name="gather_chips",
        compiler_params=pltpu.CompilerParams(collective_id=collective_id, has_side_effects=True),
    )(rows)


def scatter_body(
    parts_ref, out_ref, near_ref, in2_ref, in3_ref, acc2_ref, acc3_ref, send1, recv1, send2, recv2, send3, recv3
):
    me = chip_index()
    greet_neighbours()
    opposite = flipped(me, ("y", "a", "b"))
    first = []
    for at, (axis, onward, last) in enumerate(HOPS):
        begin, count = THIRDS[at]
        copy = remote(parts_ref.at[opposite, pl.ds(begin, count)], in2_ref.at[pl.ds(begin, count)], send1.at[at], recv1.at[at], last)
        copy.start()
        first.append(copy)
    second = []
    rows = parts_ref.shape[1]
    half = rows // 2
    for part in range(2):
        here = pl.ds(part * half, half)
        for at, (axis, onward, last) in enumerate(HOPS):
            dest = flipped(me, (axis, onward))
            begin, count = THIRDS[at]
            if part == 0:
                first[at].wait_recv()
                acc2_ref[at] = parts_ref[dest]
                piece = pl.ds(begin, count)
                acc2_ref[at, piece] = (parts_ref[dest, piece].astype(f32) + in2_ref[piece].astype(f32)).astype(bf16)
            copy = remote(acc2_ref.at[at, here], in3_ref.at[at, here], send2.at[at, part], recv2.at[at, part], onward)
            copy.start()
            second.append(copy)
    third = []
    for part in range(2):
        here = pl.ds(part * half, half)
        for at, (axis, onward, last) in enumerate(HOPS):
            dest = flipped(me, (axis,))
            second[part * 3 + at].wait_recv()
            acc3_ref[at, here] = (parts_ref[dest, here].astype(f32) + in3_ref[at, here].astype(f32)).astype(bf16)
            copy = remote(acc3_ref.at[at, here], near_ref.at[at, here], send3.at[at, part], recv3.at[at, part], axis)
            copy.start()
            third.append(copy)
    for part in range(2):
        here = pl.ds(part * half, half)
        for at in range(3):
            third[part * 3 + at].wait_recv()
        out_ref[here] = (
            (parts_ref[me, here].astype(f32) + near_ref[0, here].astype(f32))
            + (near_ref[1, here].astype(f32) + near_ref[2, here].astype(f32))
        )
    for copy in first + second + third:
        copy.wait_send()


def scatter_chips(parts, collective_id):
    _, rows, width = parts.shape
    vmem = pl.BlockSpec(memory_space=pltpu.VMEM)
    dma = pltpu.SemaphoreType.DMA
    return pl.pallas_call(
        scatter_body,
        in_specs=[vmem],
        out_specs=vmem,
        out_shape=jax.ShapeDtypeStruct((rows, width), f32),
        scratch_shapes=[pltpu.VMEM((3, rows, width), bf16), pltpu.VMEM((rows, width), bf16)] + [pltpu.VMEM((3, rows, width), bf16)] * 3
        + [dma((3,))] * 2 + [dma((3, 2))] * 4,
        name="scatter_chips",
        compiler_params=pltpu.CompilerParams(collective_id=collective_id, has_side_effects=True, vmem_limit_bytes=32*2**20),
    )(parts)


def gather_slow(rows):
    return lax.all_to_all(
        jnp.broadcast_to(rows[None], (CHIPS,) + rows.shape), CHIP, split_axis=0, concat_axis=0, tiled=True
    )


def exchange_chips(parts):
    return lax.all_to_all(parts, CHIP, split_axis=0, concat_axis=0, tiled=True)


def scatter_slow(parts):
    return jnp.sum(exchange_chips(parts.astype(bf16)).astype(f32), axis=0)


def swap(values, axis):
    return lax.ppermute(values, axis, [(0, 1), (1, 0)])


def both_cores(own, axis):
    other = swap(own, "c")
    first = lax.axis_index("c") == 0
    return jnp.stack([jnp.where(first, own, other), jnp.where(first, other, own)], axis=axis)


def half_for_core(values, axis):
    core = lax.axis_index("c")
    own = lax.dynamic_index_in_dim(values, core, axis, keepdims=False)
    sent = lax.dynamic_index_in_dim(values, 1 - core, axis, keepdims=False)
    return own + swap(sent.astype(bf16), "c").astype(f32)


def sum_groups(tiles):
    groups = lax.axis_size("g")
    if groups != 2:
        return lax.psum_scatter(tiles.astype(f32), "g", scatter_dimension=1, tiled=True).astype(bf16)
    part = tiles.shape[1] // 2
    group = lax.axis_index("g")
    own = lax.dynamic_slice_in_dim(tiles, group * part, part, 1)
    sent = lax.dynamic_slice_in_dim(tiles, (1 - group) * part, part, 1)
    return (own.astype(f32) + swap(sent, "g").astype(f32)).astype(bf16)


def spread_columns(weight, width):
    rows = weight.shape[0]
    blocks = weight.reshape(rows, 2, CHIPS // 2, width)
    mine = lax.dynamic_index_in_dim(blocks, lax.axis_index("y"), 1, keepdims=False)
    return jnp.transpose(mine, (1, 0, 2))


def to_columns(blocks):
    groups = lax.axis_size("g")
    sent = jnp.broadcast_to(blocks[None], (groups,) + blocks.shape).reshape((-1,) + blocks.shape[1:])
    got = lax.all_to_all(sent, ("g", "a", "b"), split_axis=0, concat_axis=0, tiled=True)
    return both_cores(got, 1).reshape(-1, blocks.shape[-1])


def down_rows(w_down, chip):
    if lax.axis_size("g") == 2:
        other = swap(w_down, "g")
        mine = jnp.where(lax.axis_index("g") == lax.axis_index("y"), w_down, other)
        return both_cores(mine, 0).reshape(BLK, D)
    return lax.dynamic_slice_in_dim(lax.all_gather(w_down, FS, axis=0, tiled=True), chip * BLK, BLK, 0)


def band():
    tap = np.arange(CK)[:, None, None]
    source = np.arange(128)[None, :, None]
    target = np.arange(128)[None, None, :]
    return source - target + CK // 2 == tap


def body_any(
    layer_input, lengths, cotangent, w_query, w_key, w_value, w_out, w_gate, w_up, w_down, vec_copy, owners,
    basis_left, basis_right, block_master, block_first, block_second, vec_master, vec_first, vec_second,
):
    chip = (lax.axis_index("y") * 2 + lax.axis_index("a")) * 2 + lax.axis_index("b")
    fs_index = ((lax.axis_index("g") * 2 + lax.axis_index("a")) * 2 + lax.axis_index("b")) * 2 + lax.axis_index("c")
    seq_len = layer_input.shape[0]
    length = lengths[0]
    reps = lax.axis_size("y")
    fs_size = lax.axis_size(FS)

    own_vec = vec_copy.shape[0]
    small = jnp.concatenate(
        [vec_copy.astype(f32), jnp.zeros((1023 - own_vec,), f32), length.astype(f32).reshape(1)]
    ).reshape(8, 128)
    x_all, small_all = gather_first(layer_input, small, 1)
    small_all = small_all.reshape(fs_size, reps, 1024)
    vector = small_all[:, 0, :own_vec].reshape(-1)
    group_lengths = small_all[:, :, 1023].reshape(-1, 2, 2, 2, reps)
    group_lengths = lax.dynamic_index_in_dim(group_lengths, lax.axis_index("g"), 0, keepdims=False)
    group_lengths = lax.dynamic_index_in_dim(group_lengths, lax.axis_index("c"), 2, keepdims=False)
    group_lengths = jnp.transpose(group_lengths, (2, 0, 1)).reshape(CHIPS).astype(jnp.int32)
    gain_attn, gain_head, gain_ffn = vector[:D], vector[D : 2 * D], vector[2 * D : 3 * D]
    conv_end = 3 * D + H * CQ * CK
    theta = lax.dynamic_slice_in_dim(vector[3 * D : conv_end].reshape(H, CQ, CK), chip * 2, 2, 0)
    mixer = lax.dynamic_slice_in_dim(vector[conv_end : conv_end + 2 * H].reshape(H, 2), chip * 2, 2, 0)
    mix = mixer.reshape(4)
    gain_pair = jnp.pad(
        lax.dynamic_slice_in_dim(gain_head.reshape(H, DH), chip * 2, 2, 0), ((0, 0), (0, HP - DH))
    ).reshape(1, 2 * HP)
    toep = jnp.zeros((2, CQ, seq_len, seq_len), f32)
    offset = (
        jnp.arange(seq_len, dtype=jnp.int32)[:, None] - jnp.arange(seq_len, dtype=jnp.int32)[None, :] + CK // 2
    )
    for tap in range(CK):
        toep = jnp.where(offset[None, None] == tap, theta[:, :, tap][:, :, None, None], toep)
    toep = toep.astype(bf16).reshape(2, CQ * seq_len, seq_len)

    qkv_rows = to_columns(
        jnp.concatenate([spread_columns(w, 2 * DH) for w in (w_query, w_key, w_value)], axis=2)
    )
    w_qkv = jnp.pad(qkv_rows.reshape(D, 6, DH), ((0, 0), (0, 0), (0, HP - DH))).reshape(D, 6 * HP)
    w_in = to_columns(jnp.concatenate([spread_columns(w, BLK) for w in (w_gate, w_up)], axis=2))
    w_dn = down_rows(w_down, chip)
    w_o = lax.all_gather(w_out, FS, axis=0, tiled=True)

    input_float = layer_input.astype(f32)
    input_scale = rms(input_float)
    x_rows = x_all.reshape(CHIPS * seq_len, D).astype(f32)
    xn_rows = (x_rows * rms(x_rows) * gain_attn).astype(bf16)
    qkv = dot(xn_rows, w_qkv).astype(bf16).reshape(CHIPS, seq_len, 6 * HP)
    heads_pad, scores, weights, outs = run_forward(group_lengths, mix, qkv, toep, gain_pair)
    heads_sent = heads_pad.reshape(CHIPS, seq_len, 2, HP)[..., :DH].reshape(CHIPS, seq_len, 2 * DH)
    heads = jnp.transpose(exchange_chips(heads_sent), (1, 0, 2)).reshape(seq_len, D)
    hmid = input_float + dot(heads, w_o)
    hmid_scale = rms(hmid)
    hn_rows = gather_chips((hmid * hmid_scale * gain_ffn).astype(bf16), 2).reshape(CHIPS * seq_len, D)
    both = dot(hn_rows, w_in)
    gate, up = both[:, :BLK], both[:, BLK:]
    sig = jax.nn.sigmoid(gate)
    silu = gate * sig
    inner = (silu * up).astype(bf16)
    ffn = scatter_slow(dot(inner, w_dn).reshape(CHIPS, seq_len, D))
    layer_output = (hmid + ffn).astype(bf16)

    valid = (jnp.arange(seq_len) < length).astype(f32)
    dy = cotangent.astype(f32) * valid[:, None]
    dy_rows = gather_slow(dy.astype(bf16)).reshape(CHIPS * seq_len, D)
    dinner = dot_nt(dy_rows, w_dn)
    dgate = (dinner * up * (sig * (1.0 + gate * (1.0 - sig)))).astype(bf16)
    dup = (dinner * silu).astype(bf16)
    dboth = jnp.concatenate([dgate, dup], axis=1)
    dhn = scatter_chips(dot_nt(dboth, w_in).astype(bf16).reshape(CHIPS, seq_len, D), 3)
    dhmid, grad_gain_ffn = norm_backward(hmid, hmid_scale, gain_ffn, dhn)
    dhmid = dhmid + dy
    dattn = dhmid.astype(bf16)
    dheads = dot_nt(dattn, w_o).astype(bf16).reshape(seq_len, CHIPS, 2 * DH)
    dheads = exchange_chips(jnp.transpose(dheads, (1, 0, 2)))
    dheads = jnp.pad(dheads.reshape(CHIPS, seq_len, 2, DH), ((0, 0), (0, 0), (0, 0), (0, HP - DH)))
    dqkv, theta_sums, mixer_sums, gain_sums = run_backward(
        group_lengths, mix, qkv, toep, gain_pair, scores, weights, outs, dheads.reshape(CHIPS, seq_len, 2 * HP)
    )
    dqkv_rows = dqkv.reshape(CHIPS * seq_len, 6 * HP)
    dxn = scatter_slow(dot_nt(dqkv_rows, w_qkv).reshape(CHIPS, seq_len, D))
    dinput, grad_gain_attn = norm_backward(input_float, input_scale, gain_attn, dxn)
    input_grad = dinput + dhmid

    taps = jnp.asarray(band())
    theta_sums = theta_sums.reshape(2, seq_len, CQ, seq_len)
    grad_theta = jnp.stack(
        [jnp.sum(jnp.where(taps[tap][None, :, None, :], theta_sums, 0.0), axis=(1, 3)) for tap in range(CK)], axis=2
    )
    grad_mixer = jnp.sum(mixer_sums[:4], axis=1)
    vector_grad = jnp.concatenate(
        [
            grad_gain_attn,
            lax.dynamic_update_slice_in_dim(
                jnp.zeros((D,), f32), gain_sums.reshape(2, HP)[:, :DH].reshape(-1), chip * 2 * DH, 0
            ),
            grad_gain_ffn,
            lax.dynamic_update_slice_in_dim(
                jnp.zeros((H * CQ * CK,), f32), grad_theta.reshape(-1), chip * 2 * CQ * CK, 0
            ),
            lax.dynamic_update_slice_in_dim(jnp.zeros((2 * H,), f32), grad_mixer, chip * 4, 0),
        ]
    )
    pieces = jnp.pad(vector_grad.reshape(fs_size, 1, own_vec), ((0, 0), (0, 0), (0, 512 - own_vec)))
    pieces = jnp.broadcast_to(pieces, (fs_size, reps, 512)).reshape(-1, 4, 128)
    vector_total = jnp.sum(
        lax.all_to_all(pieces, ALL, split_axis=0, concat_axis=0, tiled=True), axis=0
    ).reshape(512)[:own_vec]

    strip = BLK // (2 * CHIPS)
    grad_in = dot_tn(hn_rows, dboth).reshape(ROW_TILES, 2, CHIPS, strip, 2, BLK)
    grad_down = dot_tn(inner, dy_rows).reshape(2, CHIPS, strip, ROW_TILES, BLK)
    grad_in = jnp.transpose(half_for_core(grad_in, 1), (1, 3, 0, 2, 4)).reshape(CHIPS, 2 * ROW_TILES, strip, BLK)
    grad_down = jnp.transpose(half_for_core(grad_down, 0), (0, 2, 1, 3))
    ffn_tiles = exchange_chips(jnp.concatenate([grad_in, grad_down], axis=1).astype(bf16))
    gate_tiles = jnp.transpose(ffn_tiles[:, : 2 * ROW_TILES], (1, 0, 2, 3)).reshape(-1, strip, BLK)
    down_tiles = ffn_tiles[:, 2 * ROW_TILES :].reshape(-1, strip, BLK)
    grad_qkv = dot_tn(xn_rows, dqkv_rows).reshape(ROW_TILES, 2, CHIPS, strip, 6, HP)[..., :DH]
    grad_qkv = jnp.transpose(half_for_core(grad_qkv, 1), (1, 0, 2, 3, 4))
    grad_qkv = exchange_chips(grad_qkv.astype(bf16).reshape(CHIPS, ROW_TILES, strip, 6 * DH))
    grad_qkv = jnp.transpose(
        grad_qkv.reshape(CHIPS, ROW_TILES, strip, 3, 2 * DH), (3, 1, 2, 0, 4)
    ).reshape(3, ROW_TILES, strip, ROW_TILES, BLK)
    qkv_tiles = jnp.transpose(grad_qkv, (0, 1, 3, 2, 4)).reshape(-1, strip, BLK)
    heads_strips = jnp.transpose(heads.reshape(seq_len, 2 * ROW_TILES, CHIPS, strip), (2, 0, 1, 3))
    heads_strips = exchange_chips(heads_strips.reshape(CHIPS, seq_len, 2 * ROW_TILES * strip))
    dattn_rows = gather_slow(dattn).reshape(CHIPS * seq_len, D)
    grad_out = dot_tn(heads_strips.reshape(CHIPS * seq_len, -1), dattn_rows)
    grad_out = half_for_core(grad_out.reshape(ROW_TILES, 2, strip, ROW_TILES, BLK), 1)
    out_tiles = jnp.transpose(grad_out.astype(bf16), (0, 2, 1, 3)).reshape(-1, strip, BLK)

    groups = lax.axis_size("g")
    part = strip // groups
    own_slots = basis_left.shape[0]
    devices = groups * 2 * CHIPS
    slot_total = own_slots * devices
    sums = jnp.concatenate(
        [sum_groups(jnp.concatenate([qkv_tiles, out_tiles], axis=0)), sum_groups(jnp.concatenate([gate_tiles, down_tiles], axis=0))],
        axis=0,
    )
    matches = (jnp.arange(slot_total)[:, None] == owners[None, :]).astype(bf16)
    slots = dot(matches, sums.reshape(sums.shape[0], -1)).astype(bf16)
    slots = lax.all_to_all(
        slots.reshape(devices, own_slots, part, BLK), ALL, split_axis=0, concat_axis=0, tiled=True
    )
    slots = slots.reshape(groups, 2, 2, 2, 2, own_slots, part, BLK)
    own_grad = jnp.transpose(slots, (5, 3, 4, 1, 2, 0, 6, 7)).reshape(own_slots, BLK, BLK)

    left_low, right_low = basis_left.astype(bf16), basis_right.astype(bf16)
    rotated = jnp.einsum("sia,sij->saj", left_low, own_grad, preferred_element_type=f32)
    rotated = jnp.einsum("saj,sjb->sab", rotated.astype(bf16), right_low, preferred_element_type=f32)
    first_new = beta_first * block_first + (1.0 - beta_first) * rotated
    second_new = beta_second * block_second + (1.0 - beta_second) * rotated * rotated
    direction = (first_new / (jnp.sqrt(second_new) + eps_adam)).astype(bf16)
    turned = jnp.einsum("sia,sab->sib", left_low, direction, preferred_element_type=f32)
    turned = jnp.einsum("sib,sjb->sij", turned.astype(bf16), right_low, preferred_element_type=f32)
    master_new = block_master - rate_block * (turned + decay_block * block_master)
    vec_first_new = beta_first * vec_first + (1.0 - beta_first) * vector_total
    vec_second_new = beta_second * vec_second + (1.0 - beta_second) * vector_total * vector_total
    vec_master_new = vec_master - rate_vector * vec_first_new / (jnp.sqrt(vec_second_new) + eps_adam)
    return (
        layer_output, input_grad, first_new, second_new, master_new, master_new.astype(bf16),
        vec_first_new, vec_second_new, vec_master_new, vec_master_new.astype(bf16),
    )


def group_at(mask):
    return {axis: 1 - lax.axis_index(axis) for axis, bit in (("g", 4), ("a", 2), ("b", 1)) if mask & bit}


def other_bit(axis, changed):
    at = lax.axis_index(axis)
    return 1 - at if changed else at


def push(src, dst, send, recv, device):
    copy = pltpu.make_async_remote_copy(src_ref=src, dst_ref=dst, send_sem=send, recv_sem=recv, device_id=device)
    copy.start()
    return copy


class Gather:
    def __init__(self, x_ref, out_ref, local_sem, send1, recv1, send2, recv2, send3, recv3):
        self.x, self.out, self.local_sem = x_ref, out_ref, local_sem
        self.sems = ((send1, recv1), (send2, recv2), (send3, recv3))
        self.me = chip_index()
        self.half = x_ref.shape[0] // 2
        self.sent, self.second = [], []

    def here(self, part):
        return pl.ds(part * self.half, self.half)

    def start(self):
        self.local = pltpu.make_async_copy(self.x, self.out.at[self.me], self.local_sem)
        self.local.start()
        send, recv = self.sems[0]
        for part in range(2):
            for at, (axis, _, _) in enumerate(HOPS):
                self.sent.append(
                    push(
                        self.x.at[self.here(part)], self.out.at[self.me, self.here(part)],
                        send.at[at, part], recv.at[at, part], across(axis),
                    )
                )

    def onward(self):
        send, recv = self.sems[1]
        for part in range(2):
            for at, (axis, onward, _) in enumerate(HOPS):
                self.sent[part * 3 + at].wait_recv()
                block = self.out.at[flipped(self.me, (axis,)), self.here(part)]
                self.second.append(push(block, block, send.at[at, part], recv.at[at, part], across(onward)))

    def last(self):
        send, recv = self.sems[2]
        self.third = []
        for copy in self.second:
            copy.wait_recv()
        for at, (axis, onward, last) in enumerate(HOPS):
            begin, count = THIRDS[at]
            piece = self.out.at[flipped(self.me, (axis, onward)), pl.ds(begin, count)]
            self.third.append(push(piece, piece, send.at[at], recv.at[at], across(last)))

    def finish(self):
        for copy in self.third:
            copy.wait_recv()
        self.local.wait()

    def drain(self):
        for copy in self.sent + self.second + self.third:
            copy.wait_send()


class SideGather:
    def __init__(self, x_ref, out_ref, local_sem, send1, recv1, send2, recv2, send3, recv3):
        self.x, self.out, self.local_sem = x_ref, out_ref, local_sem
        self.sems = ((send1, recv1), (send2, recv2), (send3, recv3))
        self.me = chip_index()
        half = x_ref.shape[0] // 2
        self.low, self.high = pl.ds(0, half), pl.ds(half, half)

    def start(self):
        self.local = pltpu.make_async_copy(self.x, self.out.at[self.me], self.local_sem)
        self.local.start()
        send, recv = self.sems[0]
        self.first = [
            push(self.x, self.out.at[self.me], send.at[at], recv.at[at], across(axis)) for at, axis in enumerate("aby")
        ]

    def onward(self):
        send, recv = self.sems[1]
        blocks = [self.out.at[flipped(self.me, (axis,))] for axis in "aby"]
        self.first[0].wait_recv()
        self.second = [
            push(blocks[0], blocks[0], send.at[0], recv.at[0], across("b")),
            push(blocks[0], blocks[0], send.at[1], recv.at[1], across("y")),
        ]
        self.first[1].wait_recv()
        piece = blocks[1].at[self.high]
        self.second.append(push(piece, piece, send.at[2], recv.at[2], across("y")))
        self.first[2].wait_recv()
        piece = blocks[2].at[self.low]
        self.second.append(push(piece, piece, send.at[3], recv.at[3], across("b")))

    def last(self):
        send, recv = self.sems[2]
        self.second[0].wait_recv()
        piece = self.out.at[flipped(self.me, ("a", "b")), self.high]
        self.third = [push(piece, piece, send.at[0], recv.at[0], across("y"))]
        self.second[1].wait_recv()
        piece = self.out.at[flipped(self.me, ("a", "y")), self.low]
        self.third.append(push(piece, piece, send.at[1], recv.at[1], across("b")))

    def finish(self):
        for copy in self.second[2:] + self.third:
            copy.wait_recv()
        self.local.wait()

    def drain(self):
        for copy in self.first + self.second + self.third:
            copy.wait_send()


def side_sems():
    dma = pltpu.SemaphoreType.DMA
    return [dma] + [dma((3,))] * 2 + [dma((4,))] * 2 + [dma((2,))] * 2


class Scatter:
    def __init__(self, parts, near, in2, in3, acc2, acc3, send1, recv1, send2, recv2, send3, recv3):
        self.parts, self.near, self.in2, self.in3, self.acc2, self.acc3 = parts, near, in2, in3, acc2, acc3
        self.sems = ((send1, recv1), (send2, recv2), (send3, recv3))
        self.me = chip_index()
        self.half = parts.shape[1] // 2

    def here(self, part):
        return pl.ds(part * self.half, self.half)

    def start(self):
        send, recv = self.sems[0]
        opposite = flipped(self.me, ("y", "a", "b"))
        self.first = []
        for at, (_, _, last) in enumerate(HOPS):
            rows = pl.ds(*THIRDS[at])
            self.first.append(push(self.parts.at[opposite, rows], self.in2.at[rows], send.at[at], recv.at[at], across(last)))

    def onward(self):
        send, recv = self.sems[1]
        self.second = []
        for part in range(2):
            for at, (axis, onward, _) in enumerate(HOPS):
                dest = flipped(self.me, (axis, onward))
                if part == 0:
                    self.first[at].wait_recv()
                    rows = pl.ds(*THIRDS[at])
                    self.acc2[at] = self.parts[dest]
                    self.acc2[at, rows] = (
                        self.parts[dest, rows].astype(f32) + self.in2[rows].astype(f32)
                    ).astype(bf16)
                here = self.here(part)
                self.second.append(
                    push(self.acc2.at[at, here], self.in3.at[at, here], send.at[at, part], recv.at[at, part], across(onward))
                )

    def last(self):
        send, recv = self.sems[2]
        self.third = []
        for part in range(2):
            here = self.here(part)
            for at, (axis, _, _) in enumerate(HOPS):
                dest = flipped(self.me, (axis,))
                self.second[part * 3 + at].wait_recv()
                self.acc3[at, here] = (
                    self.parts[dest, here].astype(f32) + self.in3[at, here].astype(f32)
                ).astype(bf16)
                self.third.append(
                    push(self.acc3.at[at, here], self.near.at[at, here], send.at[at, part], recv.at[at, part], across(axis))
                )

    def finish(self, part):
        here = self.here(part)
        for at in range(3):
            self.third[part * 3 + at].wait_recv()
        return (self.parts[self.me, here].astype(f32) + self.near[0, here].astype(f32)) + (
            self.near[1, here].astype(f32) + self.near[2, here].astype(f32)
        )

    def drain(self):
        for copy in self.first + self.second + self.third:
            copy.wait_send()


def scatter_scratch(rows, width):
    dma = pltpu.SemaphoreType.DMA
    three = pltpu.VMEM((3, rows, width), bf16)
    return [three, pltpu.VMEM((rows, width), bf16), three, three, three] + [dma((3,))] * 2 + [dma((3, 2))] * 4


VMEM = pl.BlockSpec(memory_space=pltpu.VMEM)


def dispatch_body(
    x_ref, vec_ref, blocks_ref, w_out_ref, out_ref, vecs_ref, wq_ref, wo_ref,
    vec_send, vec_recv, vec_local, w_local, o_local, w_send, w_recv, core_send, core_recv,
    o_send, o_recv, o_side_send, o_side_recv, o_core_send, o_core_recv, *hops,
):
    devices = lax.axis_size(ALL)
    me = device_index()
    g, a, b, c, y = (lax.axis_index(axis) for axis in ALL)
    mine = ((g * 2 + a) * 2 + b) * 2 + c
    local = pltpu.make_async_copy(vec_ref, vecs_ref.at[me], vec_local)
    local.start()
    own = pltpu.make_async_copy(blocks_ref.at[chip_index()], wq_ref.at[mine], w_local)
    own.start()
    own_out = pltpu.make_async_copy(w_out_ref, wo_ref.at[mine], o_local)
    own_out.start()
    greet_all()
    gather = Gather(x_ref, out_ref, *hops)
    gather.start()

    def push_vec(step, carry):
        pltpu.make_async_remote_copy(
            src_ref=vec_ref, dst_ref=vecs_ref.at[me], send_sem=vec_send, recv_sem=vec_recv,
            device_id=device_at(lax.rem(me + step, devices)),
        ).start()
        return carry

    lax.fori_loop(1, devices, push_vec, 0)
    sent, relayed = [], []
    for mask in (4, 6, 5, 7, 2, 1, 3):
        block = (y * 2 + other_bit("a", mask & 2)) * 2 + other_bit("b", mask & 1)
        sent.append(push(blocks_ref.at[block], wq_ref.at[mine], w_send.at[mask], w_recv.at[mask], group_at(mask)))
    half = pl.ds(pl.multiple_of(y * 48, 16), 48)
    shard = {mask: source_at(mask) for mask in range(8)}
    lines = {
        mask: push(w_out_ref.at[half], wo_ref.at[mine, half], o_send.at[mask], o_recv.at[mask], group_at(mask))
        for mask in (2, 4, 6)
    }
    lines[1] = push(w_out_ref.at[half], wo_ref.at[mine, half], o_send.at[1], o_recv.at[1], across("b"))
    o_core = [push(w_out_ref, wo_ref.at[mine], o_core_send.at[0], o_core_recv.at[0], across("c"))]
    own.wait()
    relayed.append(push(wq_ref.at[mine], wq_ref.at[mine], core_send.at[0], core_recv.at[0], across("c")))
    gather.onward()
    o_side = {}

    def to_side(mask):
        lines[mask].wait_recv()
        piece = wo_ref.at[shard[mask], half]
        o_side[mask] = push(piece, piece, o_side_send.at[mask], o_side_recv.at[mask], across("y"))

    def relay(mask):
        sent[(4, 6, 5, 7, 2, 1, 3).index(mask)].wait_recv()
        block = wq_ref.at[shard[mask]]
        relayed.append(push(block, block, core_send.at[mask], core_recv.at[mask], across("c")))

    for mask in (2, 4, 6):
        lines[mask].wait_recv()
        piece = wo_ref.at[shard[mask], half]
        lines[mask + 1] = push(piece, piece, o_send.at[mask + 1], o_recv.at[mask + 1], across("b"))
        o_side[mask] = push(piece, piece, o_side_send.at[mask], o_side_recv.at[mask], across("y"))
    to_side(1)
    relay(4)
    relay(6)
    gather.last()
    for mask in (3, 5, 7):
        to_side(mask)
    for mask in (5, 7, 2, 1, 3):
        relay(mask)
    for mask in (2, 4, 6, 1, 3, 5, 7):
        o_side[mask].wait_recv()
        block = wo_ref.at[shard[mask]]
        o_core.append(push(block, block, o_core_send.at[mask], o_core_recv.at[mask], across("c")))
    gather.finish()
    for copy in relayed + o_core:
        copy.wait_recv()
    others = vecs_ref.at[pl.ds(0, devices - 1)]
    pltpu.make_async_copy(others, others, vec_recv).wait()
    pltpu.make_async_copy(others, others, vec_send).wait()
    local.wait()
    own_out.wait()
    gather.drain()
    for copy in sent + relayed + list(lines.values()) + list(o_side.values()) + o_core:
        copy.wait_send()


def source_at(mask):
    return ((other_bit("g", mask & 4) * 2 + other_bit("a", mask & 2)) * 2 + other_bit("b", mask & 1)) * 2 + lax.axis_index("c")


def dispatch(rows, vec, blocks, w_out):
    count, width = rows.shape
    dma = pltpu.SemaphoreType.DMA
    return pl.pallas_call(
        dispatch_body,
        in_specs=[ANYS] * 4,
        out_specs=[ANYS] * 4,
        out_shape=[
            jax.ShapeDtypeStruct((CHIPS, count, width), rows.dtype),
            jax.ShapeDtypeStruct((lax.axis_size(ALL),) + vec.shape, vec.dtype),
            jax.ShapeDtypeStruct((16,) + blocks.shape[1:], blocks.dtype),
            jax.ShapeDtypeStruct((16,) + w_out.shape, w_out.dtype),
        ],
        scratch_shapes=[dma] * 5 + [dma((8,))] * 10 + hop_sems(),
        name="dispatch",
        compiler_params=pltpu.CompilerParams(collective_id=1, has_side_effects=True),
    )(rows, vec, blocks, w_out)


def forward_body(
    len_ref, mix_ref, x_all_ref, x_ref, gains_ref, wq_ref, toep_ref, gain_ref, wo_ref, w_gate_ref, w_up_ref, w_down_ref, dy_ref,
    xn_ref, qkv_ref, s_ref, p_ref, o_ref, heads_ref, hmid_ref, hn_all_ref, w_in_ref, w_dn_ref, dy_all_ref,
    pad_ref, out_heads, hn_ref, local_sems, w_send, w_recv, u_send, u_recv, core_send, core_recv,
    d_send, d_recv, head_send, head_recv, *hops,
):
    seqs, rows, _ = x_all_ref.shape
    g, a, b, c, y = (lax.axis_index(axis) for axis in ALL)
    me = chip_index()
    mine = source_at(0)
    low, high = pl.ds(0, BLK), pl.ds(BLK, BLK)

    def columns(chip):
        return pl.ds(pl.multiple_of(chip * BLK, BLK), BLK)

    greet_all()
    local = [
        pltpu.make_async_copy(w_gate_ref.at[:, columns(me)], w_in_ref.at[mine, :, low], local_sems.at[0]),
        pltpu.make_async_copy(w_up_ref.at[:, columns(me)], w_in_ref.at[mine, :, high], local_sems.at[1]),
    ]
    for copy in local:
        copy.start()
    gate, up, relayed = {}, {}, []
    order = (4, 6, 5, 7, 2, 1, 3)
    for mask in order:
        to = (y * 2 + other_bit("a", mask & 2)) * 2 + other_bit("b", mask & 1)
        gate[mask] = push(
            w_gate_ref.at[:, columns(to)], w_in_ref.at[mine, :, low], w_send.at[mask], w_recv.at[mask], group_at(mask)
        )
        up[mask] = push(
            w_up_ref.at[:, columns(to)], w_in_ref.at[mine, :, high], u_send.at[mask], u_recv.at[mask], group_at(mask)
        )

    def down_to_group():
        return pltpu.make_async_remote_copy(
            src_ref=w_down_ref, dst_ref=w_dn_ref.at[c], send_sem=d_send.at[0], recv_sem=d_recv.at[0], device_id=across("g")
        )

    def down_to_core():
        return pltpu.make_async_remote_copy(
            src_ref=w_dn_ref.at[c], dst_ref=w_dn_ref.at[c], send_sem=d_send.at[1], recv_sem=d_recv.at[1], device_id=across("c")
        )

    down_local = pltpu.make_async_copy(w_down_ref, w_dn_ref.at[c], local_sems.at[2])

    @pl.when(g == y)
    def _():
        down_local.start()
        down_to_group().start()

    side = SideGather(dy_ref, dy_all_ref, *hops[:7])
    side.start()

    def relay(mask):
        gate[mask].wait_recv()
        up[mask].wait_recv()
        block = w_in_ref.at[source_at(mask)]
        relayed.append(push(block, block, core_send.at[mask], core_recv.at[mask], across("c")))

    pad_ref[0:8, :] = jnp.zeros((8, rows), f32)
    blank = jnp.zeros((rows, HP - DH), bf16)
    batch = 4

    def project(at, carry):
        values = x_all_ref[pl.ds(at * batch, batch)].astype(f32).reshape(batch * rows, D)
        normed = (values * rms(values) * gains_ref[0:1, :]).astype(bf16)
        xn_ref[pl.ds(at * batch, batch)] = normed.reshape(batch, rows, D)
        made = dot(normed, wq_ref[...]).astype(bf16)
        for seq in range(batch):
            for piece in range(6):
                qkv_ref[at * batch + seq, :, piece * HP : (piece + 1) * HP] = jnp.concatenate(
                    [made[seq * rows : (seq + 1) * rows, piece * DH : (piece + 1) * DH], blank], axis=1
                )
        return carry

    lax.fori_loop(0, seqs // batch, project, 0)
    for copy in local:
        copy.wait()
    relayed.append(push(w_in_ref.at[mine], w_in_ref.at[mine], core_send.at[0], core_recv.at[0], across("c")))
    query_at = lax.broadcasted_iota(jnp.int32, (rows, rows), 0)
    key_at = lax.broadcasted_iota(jnp.int32, (rows, rows), 1)

    def head_copy(seq):
        return pltpu.make_async_remote_copy(
            src_ref=out_heads.at[seq], dst_ref=heads_ref.at[me], send_sem=head_send.at[seq], recv_sem=head_recv.at[me],
            device_id={"y": lax.div(seq, 4), "a": lax.rem(lax.div(seq, 2), 2), "b": lax.rem(seq, 2)},
        )

    def attend(step, carry):
        seq = lax.rem(me + step, seqs)
        keep = (key_at <= query_at) & (key_at < len_ref[seq])
        weights, made = [], []
        for head in range(2):
            query = qkv_ref[seq, :, head * HP : (head + 1) * HP]
            key = qkv_ref[seq, :, (2 + head) * HP : (3 + head) * HP]
            scores = jnp.where(keep, dot_nt(query, key) * (1.0 / math.sqrt(DH)), 0.0)
            s_ref[seq, head] = scores.astype(bf16)
            wide = shifted_down(pad_ref, scores)
            near = wide.astype(bf16)
            rest = (wide - near.astype(f32)).astype(bf16)
            conv = dot(near, toep_ref[head]) + dot(rest, toep_ref[head])
            logits = jnp.where(keep, conv, -1e30)
            weight = jnp.exp(logits - jnp.max(logits, axis=-1, keepdims=True))
            weight = weight / jnp.sum(weight, axis=-1, keepdims=True)
            p_ref[seq, head] = weight
            weights.append(weight)
        for head in range(2):
            mixed = mix_ref[2 * head] * weights[0] + mix_ref[2 * head + 1] * weights[1]
            value = qkv_ref[seq, :, (4 + head) * HP : (5 + head) * HP]
            out = dot(mixed.astype(bf16), value)
            o_ref[seq, :, head * HP : (head + 1) * HP] = out
            scale = lax.rsqrt(jnp.sum(out * out, axis=-1, keepdims=True) * (1.0 / DH) + eps_norm)
            made.append((out * scale * gain_ref[:, head * HP : (head + 1) * HP])[:, :DH])
        out_heads[seq] = jnp.concatenate(made, axis=1).astype(bf16)

        @pl.when(step > 0)
        def _():
            head_copy(seq).start()

        return carry

    lax.fori_loop(0, 4, attend, 0)
    side.onward()
    lax.fori_loop(4, seqs, attend, 0)
    heads_ref[me] = out_heads[me]
    side.last()

    def head_arrived(step, carry):
        source = lax.rem(me + step, seqs)
        pltpu.make_async_copy(out_heads.at[source], heads_ref.at[source], head_recv.at[source]).wait()
        return carry

    lax.fori_loop(1, seqs, head_arrived, 0)

    def project_out(at, carry):
        cols = pl.ds(pl.multiple_of(at * BLK, BLK), BLK)
        total = x_ref[:, cols].astype(f32)
        for chip in range(CHIPS):
            weight = wo_ref[2 * chip : 2 * chip + 2, :, cols].reshape(2 * DH, BLK)
            total += dot(heads_ref[chip], weight)
        hmid_ref[:, cols] = total
        return carry

    lax.fori_loop(0, ROW_TILES, project_out, 0)
    hmid = hmid_ref[...]
    hn_ref[...] = (hmid * rms(hmid) * gains_ref[1:2, :]).astype(bf16)
    gather = Gather(hn_ref, hn_all_ref, *hops[7:])
    gather.start()
    for mask in (2, 1, 3):
        relay(mask)
    gather.onward()
    for mask in (4, 6):
        relay(mask)
    gather.last()
    for mask in (5, 7):
        relay(mask)

    @pl.when(g == y)
    def _():
        down_local.wait()
        down_to_core().start()
        down_to_group().wait_send()

    @pl.when(g != y)
    def _():
        down_to_group().wait_recv()
        down_to_core().start()

    down_to_core().wait()
    side.finish()
    gather.finish()
    for copy in relayed:
        copy.wait_recv()

    def head_left(step, carry):
        head_copy(lax.rem(me + step, seqs)).wait_send()
        return carry

    lax.fori_loop(1, seqs, head_left, 0)
    side.drain()
    gather.drain()
    for copy in relayed + list(gate.values()) + list(up.values()):
        copy.wait_send()


def run_front(lengths, mix, x_all, x, gains, w_qkv, toep, gain, w_o, w_gate, w_up, w_down, dy):
    seqs, rows, _ = x_all.shape
    dma = pltpu.SemaphoreType.DMA
    shapes = [
        ((seqs, rows, D), bf16), ((seqs, rows, 6 * HP), bf16), ((seqs, 2, rows, rows), bf16), ((seqs, 2, rows, rows), f32),
        ((seqs, rows, 2 * HP), f32), ((CHIPS, rows, 2 * DH), bf16), ((rows, D), f32), ((CHIPS, rows, D), bf16),
        ((16, w_gate.shape[0], 2 * BLK), bf16), ((2,) + w_down.shape, bf16), ((CHIPS, rows, D), bf16),
    ]
    return pl.pallas_call(
        forward_body,
        in_specs=[SMEM, SMEM] + [VMEM] * 7 + [ANYS] * 4,
        out_specs=[VMEM] * 7 + [ANYS] * 4,
        out_shape=[jax.ShapeDtypeStruct(*shape) for shape in shapes],
        scratch_shapes=[
            pltpu.VMEM((rows + 8, rows), f32), pltpu.VMEM((seqs, rows, 2 * DH), bf16), pltpu.VMEM((rows, D), bf16),
            dma((3,)),
        ] + [dma((8,))] * 6 + [dma((2,))] * 2 + [dma((8,))] * 2 + side_sems() + hop_sems(),
        name="front",
        compiler_params=pltpu.CompilerParams(collective_id=2, has_side_effects=True, vmem_limit_bytes=56 * 2**20),
    )(lengths, mix, x_all, x, gains, w_qkv, toep, gain, w_o, w_gate, w_up, w_down, dy)


def back_body(
    len_ref, mix_ref, qkv_ref, toep_ref, gain_ref, s_ref, p_ref, o_ref, sent_ref, dattn_ref, strips_ref,
    dqkv_ref, theta_ref, mixer_ref, gain_grad_ref, go_ref,
    pad_ref, grads_ref, all_ref, own_sem, send, recv, *hops,
):
    seqs, rows = qkv_ref.shape[:2]
    me = chip_index()
    own = pltpu.make_async_copy(sent_ref.at[me], grads_ref.at[me], own_sem)
    own.start()
    barrier = pltpu.get_barrier_semaphore()
    for mask in range(1, 8):
        pl.semaphore_signal(barrier, inc=1, device_id=chip_at(mask))
    pl.semaphore_wait(barrier, 7)
    sent = []
    for mask in (7, 6, 5, 3, 4, 2, 1):
        to = flipped(me, [axis for axis in BITS if mask & BITS[axis]])
        sent.append(push(sent_ref.at[to], grads_ref.at[me], send.at[mask], recv.at[mask], chip_at(mask)))
    gather = SideGather(dattn_ref, all_ref, *hops)
    gather.start()
    pad_ref[rows : rows + 8, :] = jnp.zeros((8, rows), f32)
    theta_ref[...] = jnp.zeros_like(theta_ref)
    mixer_ref[...] = jnp.zeros_like(mixer_ref)
    gain_grad_ref[...] = jnp.zeros_like(gain_grad_ref)
    own.wait()
    for copy in sent:
        copy.wait_recv()
    query_at = lax.broadcasted_iota(jnp.int32, (rows, rows), 0)
    key_at = lax.broadcasted_iota(jnp.int32, (rows, rows), 1)
    blank = jnp.zeros((rows, HP - DH), f32)

    def one(seq, carry):
        keep = (key_at <= query_at) & (key_at < len_ref[seq])
        weights = [p_ref[seq, 0], p_ref[seq, 1]]
        grad_mixed, made = [], [None] * 6
        grads = grads_ref[seq].astype(f32)
        for head in range(2):
            cols = slice(head * HP, (head + 1) * HP)
            out = o_ref[seq, :, cols]
            grad = jnp.concatenate([grads[:, head * DH : (head + 1) * DH], blank], axis=1)
            scale = lax.rsqrt(jnp.sum(out * out, axis=-1, keepdims=True) * (1.0 / DH) + eps_norm)
            unit = out * scale
            gain_grad_ref[:, cols] += jnp.sum(grad * unit, axis=0, keepdims=True)
            inner = grad * gain_ref[:, cols]
            grad_out = scale * (inner - unit * (jnp.sum(inner * unit, axis=-1, keepdims=True) * (1.0 / DH)))
            grad_out = grad_out.astype(bf16)
            value = qkv_ref[seq, :, (4 + head) * HP : (5 + head) * HP]
            mixed = (mix_ref[2 * head] * weights[0] + mix_ref[2 * head + 1] * weights[1]).astype(bf16)
            made[4 + head] = dot_tn(mixed, grad_out)
            back = dot_nt(grad_out, value)
            grad_mixed.append(back)
            for source in range(2):
                mixer_ref[2 * head + source : 2 * head + source + 1, :] += jnp.sum(
                    back * weights[source], axis=0, keepdims=True
                )
        for head in range(2):
            grad_weight = mix_ref[head] * grad_mixed[0] + mix_ref[2 + head] * grad_mixed[1]
            weight = weights[head]
            grad_conv = weight * (grad_weight - jnp.sum(weight * grad_weight, axis=-1, keepdims=True))
            wide = shifted_up(pad_ref, grad_conv).astype(bf16)
            theta_ref[head] += dot_tn(s_ref[seq, head], wide)
            grad_scores = jnp.zeros((rows, rows), f32)
            for lag in range(CQ):
                grad_scores += dot_nt(
                    wide[:, lag * rows : (lag + 1) * rows], toep_ref[head, lag * rows : (lag + 1) * rows, :]
                )
            grad_scores = jnp.where(keep, grad_scores * (1.0 / math.sqrt(DH)), 0.0).astype(bf16)
            query = qkv_ref[seq, :, head * HP : (head + 1) * HP]
            key = qkv_ref[seq, :, (2 + head) * HP : (3 + head) * HP]
            made[head] = dot(grad_scores, key)
            made[2 + head] = dot_tn(grad_scores, query)
        dqkv_ref[seq] = jnp.concatenate([part[:, :DH] for part in made], axis=1).astype(bf16)
        return carry

    lax.fori_loop(0, 4, one, 0)
    gather.onward()
    lax.fori_loop(4, seqs, one, 0)
    gather.last()
    gather.finish()
    strips = strips_ref[...]
    for col in range(ROW_TILES):
        at = slice(col * BLK, (col + 1) * BLK)
        go_ref[:, at] = dot_tn(strips, all_ref[:, :, at].reshape(seqs * rows, BLK)).astype(bf16)
    gather.drain()
    for copy in sent:
        copy.wait_send()


def chip_at(mask):
    return {axis: 1 - lax.axis_index(axis) for axis in BITS if mask & BITS[axis]}


def run_back(lengths, mix, qkv, toep, gain, scores, weights, outs, sent, dattn, strips):
    seqs, rows, _ = qkv.shape
    dma = pltpu.SemaphoreType.DMA
    return pl.pallas_call(
        back_body,
        in_specs=[SMEM, SMEM] + [VMEM] * 9,
        out_specs=[VMEM] * 5,
        out_shape=[
            jax.ShapeDtypeStruct((seqs, rows, 6 * DH), bf16),
            jax.ShapeDtypeStruct((2, rows, CQ * rows), f32),
            jax.ShapeDtypeStruct((8, rows), f32),
            jax.ShapeDtypeStruct((1, 2 * HP), f32),
            jax.ShapeDtypeStruct((2 * DH, D), bf16),
        ],
        scratch_shapes=[
            pltpu.VMEM((rows + 8, rows), f32), pltpu.VMEM((seqs, rows, 2 * DH), bf16),
            pltpu.VMEM((CHIPS, rows, D), bf16), dma, dma((8,)), dma((8,)),
        ] + side_sems(),
        name="attention_back",
        compiler_params=pltpu.CompilerParams(collective_id=4, has_side_effects=True, vmem_limit_bytes=32 * 2**20),
    )(lengths, mix, qkv, toep, gain, scores, weights, outs, sent, dattn, strips)


def share_body(
    parts_ref, gq_ref, go_ref, dxn_ref, qkv_ref, out_ref,
    core_q, core_o, in_q, in_o, core_send, core_recv, send, recv, go_send, go_recv, *scatter_args,
):
    g, a, b, c, y = (lax.axis_index(axis) for axis in ALL)
    me = chip_index()
    barrier = pltpu.get_barrier_semaphore()
    pl.semaphore_signal(barrier, inc=1, device_id=across("c"))
    for mask in range(1, 16):
        pl.semaphore_signal(barrier, inc=1, device_id=wide_at(mask))
    pl.semaphore_wait(barrier, 16)
    to_core = [
        push(gq_ref.at[:, 1 - c], core_q, core_send.at[0], core_recv.at[0], across("c")),
        push(go_ref.at[:, 1 - c], core_o, core_send.at[1], core_recv.at[1], across("c")),
    ]
    scatter = Scatter(parts_ref, *scatter_args)
    scatter.start()
    to_core[0].wait_recv()
    for row in range(ROW_TILES):
        core_q[row] = (core_q[row].astype(f32) + gq_ref[row, c].astype(f32)).astype(bf16)
    slot = g * CHIPS + me
    sent = []
    for mask in (15, 14, 13, 11, 12, 10, 9, 8, 7, 6, 5, 3, 4, 2, 1):
        to = flipped(me, [axis for axis in BITS if mask & BITS[axis]])
        sent.append(
            push(
                core_q.at[:, to, other_bit("g", mask & 8)], in_q.at[slot], send.at[mask], recv.at[mask], wide_at(mask)
            )
        )
    to_core[1].wait_recv()
    core_o[...] = (core_o[...].astype(f32) + go_ref[:, c].astype(f32)).astype(bf16)
    to_group = push(core_o.at[:, 1 - g], in_o, go_send, go_recv, across("g"))
    in_q[slot] = core_q[:, me, g]
    scatter.onward()
    scatter.last()
    dxn_ref[0 : dxn_ref.shape[0] // 2] = scatter.finish(0)
    dxn_ref[dxn_ref.shape[0] // 2 :] = scatter.finish(1)
    to_group.wait_recv()
    out_ref[...] = (in_o[...].astype(f32) + core_o[:, g].astype(f32)).astype(bf16)
    for copy in sent:
        copy.wait_recv()
    for row in range(ROW_TILES):
        sums = [in_q[chip, row].astype(f32) + in_q[CHIPS + chip, row].astype(f32) for chip in range(CHIPS)]
        for which in range(3):
            qkv_ref[which, row] = jnp.concatenate(
                [part[:, which * 2 * DH : (which + 1) * 2 * DH] for part in sums], axis=1
            ).astype(bf16)
    scatter.drain()
    for copy in to_core + sent + [to_group]:
        copy.wait_send()


def wide_at(mask):
    at = chip_at(mask & 7)
    if mask & 8:
        at["g"] = 1 - lax.axis_index("g")
    return at


def share(parts, gq, go):
    _, rows, width = parts.shape
    dma = pltpu.SemaphoreType.DMA
    part = gq.shape[-2]
    return pl.pallas_call(
        share_body,
        in_specs=[VMEM] * 3,
        out_specs=[VMEM] * 3,
        out_shape=[
            jax.ShapeDtypeStruct((rows, width), f32),
            jax.ShapeDtypeStruct((3, ROW_TILES, part, D), bf16),
            jax.ShapeDtypeStruct((ROW_TILES, part, D), bf16),
        ],
        scratch_shapes=[
            pltpu.VMEM((ROW_TILES, CHIPS, 2, part, 6 * DH), bf16), pltpu.VMEM((ROW_TILES, 2, part, D), bf16),
            pltpu.VMEM((2 * CHIPS, ROW_TILES, part, 6 * DH), bf16), pltpu.VMEM((ROW_TILES, part, D), bf16),
            dma((2,)), dma((2,)), dma((16,)), dma((16,)), dma, dma,
        ] + scatter_scratch(rows, width),
        name="share_gradients",
        compiler_params=pltpu.CompilerParams(collective_id=5, has_side_effects=True, vmem_limit_bytes=40 * 2**20),
    )(parts, gq, go)


def to_slots_body(slots_ref, vec_ref, out_ref, vecs_ref, local_sems, send, recv, vec_send, vec_recv):
    devices = lax.axis_size(ALL)
    me = device_index()
    local = [
        pltpu.make_async_copy(slots_ref.at[me], out_ref.at[me], local_sems.at[0]),
        pltpu.make_async_copy(vec_ref.at[me], vecs_ref.at[me], local_sems.at[1]),
    ]
    for copy in local:
        copy.start()
    greet_all()

    def push_all(step, carry):
        to = lax.rem(me + step, devices)
        pltpu.make_async_remote_copy(
            src_ref=vec_ref.at[to], dst_ref=vecs_ref.at[me], send_sem=vec_send, recv_sem=vec_recv, device_id=device_at(to)
        ).start()
        pltpu.make_async_remote_copy(
            src_ref=slots_ref.at[to], dst_ref=out_ref.at[me], send_sem=send, recv_sem=recv, device_id=device_at(to)
        ).start()
        return carry

    lax.fori_loop(1, devices, push_all, 0)
    for ref, one, two in ((vecs_ref, vec_send, vec_recv), (out_ref, send, recv)):
        others = ref.at[pl.ds(0, devices - 1)]
        pltpu.make_async_copy(others, others, two).wait()
        pltpu.make_async_copy(others, others, one).wait()
    for copy in local:
        copy.wait()


def to_slots(slots, vecs):
    dma = pltpu.SemaphoreType.DMA
    return pl.pallas_call(
        to_slots_body,
        in_specs=[ANYS] * 2,
        out_specs=[ANYS] * 2,
        out_shape=[jax.ShapeDtypeStruct(slots.shape, slots.dtype), jax.ShapeDtypeStruct(vecs.shape, vecs.dtype)],
        scratch_shapes=[dma((2,))] + [dma] * 4,
        name="to_slots",
        compiler_params=pltpu.CompilerParams(collective_id=6, has_side_effects=True),
    )(slots, vecs)


def body_fast(
    layer_input, lengths, cotangent, w_query, w_key, w_value, w_out, w_gate, w_up, w_down, vec_copy, owners,
    basis_left, basis_right, block_master, block_first, block_second, vec_master, vec_first, vec_second,
):
    chip = chip_index()
    seq_len = layer_input.shape[0]
    length = lengths[0]
    own_vec = vec_copy.shape[0]
    devices, fs_size, reps = lax.axis_size(ALL), lax.axis_size(FS), lax.axis_size("y")

    small = jnp.concatenate(
        [vec_copy.astype(f32), jnp.zeros((1023 - own_vec,), f32), length.astype(f32).reshape(1)]
    ).reshape(8, 128)
    blocks = jnp.concatenate([w.reshape(-1, CHIPS, 2 * DH) for w in (w_query, w_key, w_value)], axis=2)
    x_all, small_all, w_qkv, w_out_all = dispatch(layer_input, small, jnp.transpose(blocks, (1, 0, 2)), w_out)
    w_qkv = w_qkv.reshape(D, 6 * DH)
    small_all = small_all.reshape(fs_size, reps, 1024)
    vector = small_all[:, 0, :own_vec].reshape(-1)
    group_lengths = small_all[:, :, 1023].reshape(-1, 2, 2, 2, reps)
    group_lengths = lax.dynamic_index_in_dim(group_lengths, lax.axis_index("g"), 0, keepdims=False)
    group_lengths = lax.dynamic_index_in_dim(group_lengths, lax.axis_index("c"), 2, keepdims=False)
    group_lengths = jnp.transpose(group_lengths, (2, 0, 1)).reshape(CHIPS).astype(jnp.int32)
    gain_attn, gain_head, gain_ffn = vector[:D], vector[D : 2 * D], vector[2 * D : 3 * D]
    conv_end = 3 * D + H * CQ * CK
    theta = lax.dynamic_slice_in_dim(vector[3 * D : conv_end].reshape(H, CQ, CK), chip * 2, 2, 0)
    mixer = lax.dynamic_slice_in_dim(vector[conv_end : conv_end + 2 * H].reshape(H, 2), chip * 2, 2, 0)
    mix = mixer.reshape(4)
    gain_pair = jnp.pad(
        lax.dynamic_slice_in_dim(gain_head.reshape(H, DH), chip * 2, 2, 0), ((0, 0), (0, HP - DH))
    ).reshape(1, 2 * HP)
    toep = jnp.zeros((2, CQ, seq_len, seq_len), f32)
    offset = (
        jnp.arange(seq_len, dtype=jnp.int32)[:, None] - jnp.arange(seq_len, dtype=jnp.int32)[None, :] + CK // 2
    )
    for tap in range(CK):
        toep = jnp.where(offset[None, None] == tap, theta[:, :, tap][:, :, None, None], toep)
    toep = toep.astype(bf16).reshape(2, CQ * seq_len, seq_len)
    valid = (jnp.arange(seq_len) < length).astype(f32)
    dy = cotangent.astype(f32) * valid[:, None]

    gains = jnp.concatenate([gain_attn[None], gain_ffn[None], jnp.zeros((6, D), f32)], axis=0)
    xn, qkv, scores, weights, outs, heads, hmid, hn_rows, w_in, w_dn, dy_rows = run_front(
        group_lengths, mix, x_all, layer_input, gains, w_qkv, toep, gain_pair, w_out_all, w_gate, w_up, w_down, dy.astype(bf16)
    )
    xn_rows, hn_rows, dy_rows = (rows.reshape(CHIPS * seq_len, D) for rows in (xn, hn_rows, dy_rows))
    w_in, w_dn, w_o = w_in.reshape(D, 2 * BLK), w_dn.reshape(BLK, D), w_out_all.reshape(D, D)
    heads = jnp.transpose(heads, (1, 0, 2)).reshape(seq_len, D)
    input_float = layer_input.astype(f32)
    input_scale = rms(input_float)
    hmid_scale = rms(hmid)
    both = dot(hn_rows, w_in)
    gate, up = both[:, :BLK], both[:, BLK:]
    sig = jax.nn.sigmoid(gate)
    silu = gate * sig
    inner = (silu * up).astype(bf16)

    strip = BLK // (2 * CHIPS)
    part = strip // 2
    dinner = dot_nt(dy_rows, w_dn)
    dgate = (dinner * up * (sig * (1.0 + gate * (1.0 - sig)))).astype(bf16)
    dup = (dinner * silu).astype(bf16)
    dboth = jnp.concatenate([dgate, dup], axis=1)
    dhn = scatter_chips(dot_nt(dboth, w_in).astype(bf16).reshape(CHIPS, seq_len, D), 3)
    ffn = scatter_slow(dot(inner, w_dn).reshape(CHIPS, seq_len, D))
    layer_output = (hmid + ffn).astype(bf16)
    dhmid, grad_gain_ffn = norm_backward(hmid, hmid_scale, gain_ffn, dhn)
    dhmid = dhmid + dy
    dattn = dhmid.astype(bf16)
    dheads = dot_nt(dattn, w_o).astype(bf16).reshape(seq_len, CHIPS, 2 * DH)
    strips = jnp.transpose(heads.reshape(seq_len, 2 * ROW_TILES, CHIPS, strip), (2, 0, 1, 3))
    strips = exchange_chips(strips.reshape(CHIPS, seq_len, 2 * ROW_TILES * strip)).reshape(CHIPS * seq_len, -1)
    dqkv, theta_sums, mixer_sums, gain_sums, grad_out = run_back(
        group_lengths, mix, qkv, toep, gain_pair, scores, weights, outs, jnp.transpose(dheads, (1, 0, 2)), dattn, strips
    )
    dqkv_rows = dqkv.reshape(CHIPS * seq_len, 6 * DH)
    dxn_parts = dot_nt(dqkv_rows, w_qkv).astype(bf16).reshape(CHIPS, seq_len, D)
    grad_qkv = dot_tn(xn_rows, dqkv_rows).astype(bf16)
    dxn, qkv_sums, out_sums = share(
        dxn_parts,
        grad_qkv.reshape(ROW_TILES, 2, CHIPS, 2, part, 6 * DH),
        grad_out.reshape(ROW_TILES, 2, 2, part, D),
    )
    dinput, grad_gain_attn = norm_backward(input_float, input_scale, gain_attn, dxn)
    input_grad = dinput + dhmid

    taps = jnp.asarray(band())
    theta_sums = theta_sums.reshape(2, seq_len, CQ, seq_len)
    grad_theta = jnp.stack(
        [jnp.sum(jnp.where(taps[tap][None, :, None, :], theta_sums, 0.0), axis=(1, 3)) for tap in range(CK)], axis=2
    )
    grad_mixer = jnp.sum(mixer_sums[:4], axis=1)
    vector_grad = jnp.concatenate(
        [
            grad_gain_attn,
            lax.dynamic_update_slice_in_dim(
                jnp.zeros((D,), f32), gain_sums.reshape(2, HP)[:, :DH].reshape(-1), chip * 2 * DH, 0
            ),
            grad_gain_ffn,
            lax.dynamic_update_slice_in_dim(
                jnp.zeros((H * CQ * CK,), f32), grad_theta.reshape(-1), chip * 2 * CQ * CK, 0
            ),
            lax.dynamic_update_slice_in_dim(jnp.zeros((2 * H,), f32), grad_mixer, chip * 4, 0),
        ]
    )
    pieces = jnp.pad(vector_grad.reshape(fs_size, 1, own_vec), ((0, 0), (0, 0), (0, 1024 - own_vec)))
    pieces = jnp.broadcast_to(pieces, (fs_size, reps, 1024)).reshape(devices, 8, 128)

    grad_in = dot_tn(hn_rows, dboth).reshape(ROW_TILES, 2, CHIPS, strip, 2, BLK)
    grad_down = dot_tn(inner, dy_rows).reshape(2, CHIPS, strip, ROW_TILES, BLK)
    grad_in = jnp.transpose(half_for_core(grad_in, 1), (1, 3, 0, 2, 4)).reshape(CHIPS, 2 * ROW_TILES, strip, BLK)
    grad_down = jnp.transpose(half_for_core(grad_down, 0), (0, 2, 1, 3))
    ffn_tiles = exchange_chips(jnp.concatenate([grad_in, grad_down], axis=1).astype(bf16))
    gate_tiles = jnp.transpose(ffn_tiles[:, : 2 * ROW_TILES], (1, 0, 2, 3)).reshape(-1, strip, BLK)
    down_tiles = ffn_tiles[:, 2 * ROW_TILES :].reshape(-1, strip, BLK)
    ffn_sums = sum_groups(jnp.concatenate([gate_tiles, down_tiles], axis=0))

    own_slots = basis_left.shape[0]
    slot_total = own_slots * devices
    sums = jnp.concatenate(
        [
            jnp.transpose(qkv_sums.reshape(3, ROW_TILES, part, ROW_TILES, BLK), (0, 1, 3, 2, 4)).reshape(-1, part, BLK),
            jnp.transpose(out_sums.reshape(ROW_TILES, part, ROW_TILES, BLK), (0, 2, 1, 3)).reshape(-1, part, BLK),
            ffn_sums,
        ],
        axis=0,
    )
    matches = (jnp.arange(slot_total)[:, None] == owners[None, :]).astype(bf16)
    slots = dot(matches, sums.reshape(sums.shape[0], -1)).astype(bf16)
    slots, pieces = to_slots(slots.reshape(devices, own_slots * part, BLK), pieces)
    vector_total = jnp.sum(pieces, axis=0).reshape(1024)[:own_vec]
    slots = slots.reshape(2, 2, 2, 2, 2, own_slots, part, BLK)
    own_grad = jnp.transpose(slots, (5, 3, 4, 1, 2, 0, 6, 7)).reshape(own_slots, BLK, BLK)

    left_low, right_low = basis_left.astype(bf16), basis_right.astype(bf16)
    rotated = jnp.einsum("sia,sij->saj", left_low, own_grad, preferred_element_type=f32)
    rotated = jnp.einsum("saj,sjb->sab", rotated.astype(bf16), right_low, preferred_element_type=f32)
    first_new = beta_first * block_first + (1.0 - beta_first) * rotated
    second_new = beta_second * block_second + (1.0 - beta_second) * rotated * rotated
    direction = (first_new / (jnp.sqrt(second_new) + eps_adam)).astype(bf16)
    turned = jnp.einsum("sia,sab->sib", left_low, direction, preferred_element_type=f32)
    turned = jnp.einsum("sib,sjb->sij", turned.astype(bf16), right_low, preferred_element_type=f32)
    master_new = block_master - rate_block * (turned + decay_block * block_master)
    vec_first_new = beta_first * vec_first + (1.0 - beta_first) * vector_total
    vec_second_new = beta_second * vec_second + (1.0 - beta_second) * vector_total * vector_total
    vec_master_new = vec_master - rate_vector * vec_first_new / (jnp.sqrt(vec_second_new) + eps_adam)
    return (
        layer_output, input_grad, first_new, second_new, master_new, master_new.astype(bf16),
        vec_first_new, vec_second_new, vec_master_new, vec_master_new.astype(bf16),
    )


def solution(mesh):
    fsdp, rep = mesh.shape["fsdp"], mesh.shape["rep"]
    fine = Mesh(mesh.devices.reshape(fsdp // 8, 2, 2, 2, rep), ALL)
    rows, both = P(ALL, None), P(ALL, None, None)
    weight, vec = P(FS, None), P(FS)
    return jax.shard_map(
        body_fast if (fsdp, rep) == (16, 2) else body_any,
        mesh=fine,
        in_specs=(rows, P(ALL), rows) + (weight,) * 7 + (vec, P()) + (both,) * 5 + (vec,) * 3,
        out_specs=(rows, rows) + (both,) * 4 + (vec,) * 4,
        check_vma=False,
    )
```

```python
import math

import jax
import jax.numpy as jnp
import numpy as np
from jax import lax
from jax.experimental import pallas as pl
from jax.experimental.pallas import tpu as pltpu
from jax.sharding import Mesh
from jax.sharding import PartitionSpec as P

H = 16
DH = 96
HP = 128
D = H * DH
FF = 4096
CQ = 6
CK = 11
BLK = 512
CHIPS = 8
ROW_TILES = D // BLK
FF_TILES = FF // BLK

eps_norm = 1e-05
eps_adam = 1e-08
rate_block = 0.02
rate_vector = 0.3
decay_block = 0.1
beta_first = 0.5
beta_second = 0.5

FS = ("g", "a", "b", "c")
CHIP = ("y", "a", "b")
ALL = ("g", "a", "b", "c", "y")
bf16 = jnp.bfloat16
f32 = jnp.float32


def dot(left, right):
    return jnp.dot(left, right, preferred_element_type=f32)


def dot_nt(left, right):
    return lax.dot_general(left, right, (((1,), (1,)), ((), ())), preferred_element_type=f32)


def dot_tn(left, right):
    return lax.dot_general(left, right, (((0,), (0,)), ((), ())), preferred_element_type=f32)


def rms(values):
    return lax.rsqrt(jnp.mean(values * values, axis=-1, keepdims=True) + eps_norm)


def norm_backward(values, scale, gain, grad):
    unit = values * scale
    inner = grad * gain
    grad_values = scale * (inner - unit * jnp.mean(inner * unit, axis=-1, keepdims=True))
    return grad_values, jnp.sum(grad * unit, axis=0)


def shifted_down(pad_ref, values):
    rows = values.shape[0]
    pad_ref[8 : 8 + rows, :] = values
    return jnp.concatenate(
        [values] + [pad_ref[8 - lag : 8 - lag + rows, :] for lag in range(1, CQ)], axis=1
    )


def shifted_up(pad_ref, values):
    rows = values.shape[0]
    pad_ref[0:rows, :] = values
    return jnp.concatenate(
        [values] + [pad_ref[lag : lag + rows, :] for lag in range(1, CQ)], axis=1
    )


def attention_forward(len_ref, mix_ref, qkv_ref, toep_ref, gain_ref, heads_ref, s_ref, p_ref, o_ref, pad_ref):
    rows = qkv_ref.shape[1]
    length = len_ref[pl.program_id(0)]
    query_at = lax.broadcasted_iota(jnp.int32, (rows, rows), 0)
    key_at = lax.broadcasted_iota(jnp.int32, (rows, rows), 1)
    keep = (key_at <= query_at) & (key_at < length)
    pad_ref[0:8, :] = jnp.zeros((8, rows), f32)
    weights = []
    for head in range(2):
        query = qkv_ref[0, :, head * HP : (head + 1) * HP]
        key = qkv_ref[0, :, (2 + head) * HP : (3 + head) * HP]
        scores = jnp.where(keep, dot_nt(query, key) * (1.0 / math.sqrt(DH)), 0.0)
        s_ref[0, head] = scores.astype(bf16)
        wide = shifted_down(pad_ref, scores)
        high = wide.astype(bf16)
        low = (wide - high.astype(f32)).astype(bf16)
        conv = dot(high, toep_ref[head]) + dot(low, toep_ref[head])
        logits = jnp.where(keep, conv, -1e30)
        weight = jnp.exp(logits - jnp.max(logits, axis=-1, keepdims=True))
        weight = weight / jnp.sum(weight, axis=-1, keepdims=True)
        p_ref[0, head] = weight
        weights.append(weight)
    for head in range(2):
        mixed = mix_ref[2 * head] * weights[0] + mix_ref[2 * head + 1] * weights[1]
        value = qkv_ref[0, :, (4 + head) * HP : (5 + head) * HP]
        out = dot(mixed.astype(bf16), value)
        o_ref[0, :, head * HP : (head + 1) * HP] = out
        scale = lax.rsqrt(jnp.sum(out * out, axis=-1, keepdims=True) * (1.0 / DH) + eps_norm)
        heads_ref[0, :, head * HP : (head + 1) * HP] = (
            out * scale * gain_ref[:, head * HP : (head + 1) * HP]
        ).astype(bf16)


def attention_backward(
    len_ref, mix_ref, qkv_ref, toep_ref, gain_ref, s_ref, p_ref, o_ref, grad_ref,
    dqkv_ref, theta_ref, mixer_ref, gain_grad_ref, pad_ref,
):
    rows = qkv_ref.shape[1]
    length = len_ref[pl.program_id(0)]
    query_at = lax.broadcasted_iota(jnp.int32, (rows, rows), 0)
    key_at = lax.broadcasted_iota(jnp.int32, (rows, rows), 1)
    keep = (key_at <= query_at) & (key_at < length)
    pad_ref[rows : rows + 8, :] = jnp.zeros((8, rows), f32)

    @pl.when(pl.program_id(0) == 0)
    def _():
        theta_ref[...] = jnp.zeros_like(theta_ref)
        mixer_ref[...] = jnp.zeros_like(mixer_ref)
        gain_grad_ref[...] = jnp.zeros_like(gain_grad_ref)

    weights = [p_ref[0, 0], p_ref[0, 1]]
    grad_mixed = []
    for head in range(2):
        cols = slice(head * HP, (head + 1) * HP)
        out = o_ref[0, :, cols]
        grad = grad_ref[0, :, cols].astype(f32)
        scale = lax.rsqrt(jnp.sum(out * out, axis=-1, keepdims=True) * (1.0 / DH) + eps_norm)
        unit = out * scale
        gain_grad_ref[:, cols] += jnp.sum(grad * unit, axis=0, keepdims=True)
        inner = grad * gain_ref[:, cols]
        grad_out = scale * (inner - unit * (jnp.sum(inner * unit, axis=-1, keepdims=True) * (1.0 / DH)))
        grad_out = grad_out.astype(bf16)
        value = qkv_ref[0, :, (4 + head) * HP : (5 + head) * HP]
        mixed = (mix_ref[2 * head] * weights[0] + mix_ref[2 * head + 1] * weights[1]).astype(bf16)
        dqkv_ref[0, :, (4 + head) * HP : (5 + head) * HP] = dot_tn(mixed, grad_out).astype(bf16)
        back = dot_nt(grad_out, value)
        grad_mixed.append(back)
        for source in range(2):
            mixer_ref[2 * head + source : 2 * head + source + 1, :] += jnp.sum(
                back * weights[source], axis=0, keepdims=True
            )
    for head in range(2):
        grad_weight = mix_ref[head] * grad_mixed[0] + mix_ref[2 + head] * grad_mixed[1]
        weight = weights[head]
        grad_conv = weight * (grad_weight - jnp.sum(weight * grad_weight, axis=-1, keepdims=True))
        wide = shifted_up(pad_ref, grad_conv).astype(bf16)
        theta_ref[head] += dot_tn(s_ref[0, head], wide)
        grad_scores = jnp.zeros((rows, rows), f32)
        for lag in range(CQ):
            grad_scores += dot_nt(
                wide[:, lag * rows : (lag + 1) * rows], toep_ref[head, lag * rows : (lag + 1) * rows, :]
            )
        grad_scores = jnp.where(keep, grad_scores * (1.0 / math.sqrt(DH)), 0.0).astype(bf16)
        query = qkv_ref[0, :, head * HP : (head + 1) * HP]
        key = qkv_ref[0, :, (2 + head) * HP : (3 + head) * HP]
        dqkv_ref[0, :, head * HP : (head + 1) * HP] = dot(grad_scores, key).astype(bf16)
        dqkv_ref[0, :, (2 + head) * HP : (3 + head) * HP] = dot_tn(grad_scores, query).astype(bf16)


SMEM = pl.BlockSpec(memory_space=pltpu.SMEM)


def seq_spec(*dims):
    return pl.BlockSpec((1,) + dims, lambda s: (s,) + (0,) * len(dims))


def whole_spec(*dims):
    return pl.BlockSpec(dims, lambda s: (0,) * len(dims))


def run_forward(lengths, mix, qkv, toep, gain):
    seqs, rows, _ = qkv.shape
    return pl.pallas_call(
        attention_forward,
        grid=(seqs,),
        in_specs=[SMEM, SMEM, seq_spec(rows, 6 * HP), whole_spec(2, CQ * rows, rows), whole_spec(1, 2 * HP)],
        out_specs=[seq_spec(rows, 2 * HP), seq_spec(2, rows, rows), seq_spec(2, rows, rows), seq_spec(rows, 2 * HP)],
        out_shape=[
            jax.ShapeDtypeStruct((seqs, rows, 2 * HP), bf16),
            jax.ShapeDtypeStruct((seqs, 2, rows, rows), bf16),
            jax.ShapeDtypeStruct((seqs, 2, rows, rows), f32),
            jax.ShapeDtypeStruct((seqs, rows, 2 * HP), f32),
        ],
        scratch_shapes=[pltpu.VMEM((rows + 8, rows), f32)],
        name="attention_forward",
        compiler_params=pltpu.CompilerParams(vmem_limit_bytes=24 * 2**20),
        cost_estimate=pl.CostEstimate(flops=2 * 10**9, bytes_accessed=8 * 2**20, transcendentals=10**5),
    )(lengths, mix, qkv, toep, gain)


def run_backward(lengths, mix, qkv, toep, gain, scores, weights, outs, grads):
    seqs, rows, _ = qkv.shape
    return pl.pallas_call(
        attention_backward,
        grid=(seqs,),
        in_specs=[
            SMEM, SMEM, seq_spec(rows, 6 * HP), whole_spec(2, CQ * rows, rows), whole_spec(1, 2 * HP),
            seq_spec(2, rows, rows), seq_spec(2, rows, rows), seq_spec(rows, 2 * HP), seq_spec(rows, 2 * HP),
        ],
        out_specs=[seq_spec(rows, 6 * HP), whole_spec(2, rows, CQ * rows), whole_spec(8, rows), whole_spec(1, 2 * HP)],
        out_shape=[
            jax.ShapeDtypeStruct((seqs, rows, 6 * HP), bf16),
            jax.ShapeDtypeStruct((2, rows, CQ * rows), f32),
            jax.ShapeDtypeStruct((8, rows), f32),
            jax.ShapeDtypeStruct((1, 2 * HP), f32),
        ],
        scratch_shapes=[pltpu.VMEM((rows + 8, rows), f32)],
        name="attention_backward",
        compiler_params=pltpu.CompilerParams(vmem_limit_bytes=24 * 2**20),
        cost_estimate=pl.CostEstimate(flops=4 * 10**9, bytes_accessed=12 * 2**20, transcendentals=10**5),
    )(lengths, mix, qkv, toep, gain, scores, weights, outs, grads)


BITS = {"y": 4, "a": 2, "b": 1}
HOPS = (("y", "b", "a"), ("a", "y", "b"), ("b", "a", "y"))
THIRDS = ((0, 48), (48, 48), (96, 32))
ANYS = pl.BlockSpec(memory_space=pl.ANY)


def chip_index():
    return (lax.axis_index("y") * 2 + lax.axis_index("a")) * 2 + lax.axis_index("b")


def flipped(chip, axes):
    for axis in axes:
        chip = chip + BITS[axis] * (1 - 2 * lax.axis_index(axis))
    return chip


def across(axis):
    return {axis: 1 - lax.axis_index(axis)}


def device_index():
    index = lax.axis_index("g")
    for axis in ("a", "b", "c", "y"):
        index = index * lax.axis_size(axis) + lax.axis_index(axis)
    return index


def device_at(index):
    at = {}
    for axis in ("y", "c", "b", "a", "g"):
        at[axis] = lax.rem(index, lax.axis_size(axis))
        index = lax.div(index, lax.axis_size(axis))
    return at


def greet_all():
    devices = lax.axis_size(ALL)
    me = device_index()
    barrier = pltpu.get_barrier_semaphore()

    def greet(step, carry):
        pl.semaphore_signal(barrier, inc=1, device_id=device_at(lax.rem(me + step, devices)))
        return carry

    lax.fori_loop(1, devices, greet, 0)
    pl.semaphore_wait(barrier, devices - 1)


def greet_neighbours():
    barrier = pltpu.get_barrier_semaphore()
    for axis in BITS:
        pl.semaphore_signal(barrier, inc=1, device_id=across(axis))
    pl.semaphore_wait(barrier, 3)


def remote(src, dst, send, recv, axis):
    return pltpu.make_async_remote_copy(src_ref=src, dst_ref=dst, send_sem=send, recv_sem=recv, device_id=across(axis))


def gather_body(x_ref, out_ref, *sems):
    greet_neighbours()
    gather_hops(x_ref, out_ref, *sems)


def gather_first_body(x_ref, vec_ref, out_ref, vecs_ref, vec_send, vec_recv, vec_local, *sems):
    devices = lax.axis_size(ALL)
    me = device_index()
    local = pltpu.make_async_copy(vec_ref, vecs_ref.at[me], vec_local)
    local.start()
    greet_all()

    def push(step, carry):
        pltpu.make_async_remote_copy(
            src_ref=vec_ref, dst_ref=vecs_ref.at[me], send_sem=vec_send, recv_sem=vec_recv,
            device_id=device_at(lax.rem(me + step, devices)),
        ).start()
        return carry

    lax.fori_loop(1, devices, push, 0)
    gather_hops(x_ref, out_ref, *sems)
    others = vecs_ref.at[pl.ds(0, devices - 1)]
    pltpu.make_async_copy(others, others, vec_recv).wait()
    pltpu.make_async_copy(others, others, vec_send).wait()
    local.wait()


def gather_hops(x_ref, out_ref, local_sem, send1, recv1, send2, recv2, send3, recv3):
    me = chip_index()
    rows = x_ref.shape[0]
    half = rows // 2
    local = pltpu.make_async_copy(x_ref, out_ref.at[me], local_sem)
    local.start()
    first = []
    for part in range(2):
        here = pl.ds(part * half, half)
        for at, (axis, _, _) in enumerate(HOPS):
            copy = remote(x_ref.at[here], out_ref.at[me, here], send1.at[at, part], recv1.at[at, part], axis)
            copy.start()
            first.append(copy)
    second = []
    for part in range(2):
        here = pl.ds(part * half, half)
        for at, (axis, onward, _) in enumerate(HOPS):
            first[part * 3 + at].wait_recv()
            block = out_ref.at[flipped(me, (axis,)), here]
            copy = remote(block, block, send2.at[at, part], recv2.at[at, part], onward)
            copy.start()
            second.append(copy)
    third = []
    for at, (axis, onward, last) in enumerate(HOPS):
        begin, count = THIRDS[at]
        block = flipped(me, (axis, onward))
        for part in range(2):
            if part * half < begin + count and begin < (part + 1) * half:
                second[part * 3 + at].wait_recv()
        piece = out_ref.at[block, pl.ds(begin, count)]
        copy = remote(piece, piece, send3.at[at], recv3.at[at], last)
        copy.start()
        third.append(copy)
    for at in range(3):
        begin, count = THIRDS[at]
        for part in range(2):
            if not (part * half < begin + count and begin < (part + 1) * half):
                second[part * 3 + at].wait_recv()
    for copy in third:
        copy.wait_recv()
    for copy in first + second + third:
        copy.wait_send()
    local.wait()


def hop_sems():
    dma = pltpu.SemaphoreType.DMA
    return [dma] + [dma((3, 2))] * 4 + [dma((3,))] * 2


def gather_first(rows, vec, collective_id):
    count, width = rows.shape
    return pl.pallas_call(
        gather_first_body,
        in_specs=[ANYS, ANYS],
        out_specs=[ANYS, ANYS],
        out_shape=[
            jax.ShapeDtypeStruct((CHIPS, count, width), rows.dtype),
            jax.ShapeDtypeStruct((lax.axis_size(ALL),) + vec.shape, vec.dtype),
        ],
        scratch_shapes=[pltpu.SemaphoreType.DMA] * 3 + hop_sems(),
        name="gather_first",
        compiler_params=pltpu.CompilerParams(collective_id=collective_id, has_side_effects=True),
    )(rows, vec)


def gather_chips(rows, collective_id):
    count, width = rows.shape
    return pl.pallas_call(
        gather_body,
        in_specs=[ANYS],
        out_specs=ANYS,
        out_shape=jax.ShapeDtypeStruct((CHIPS, count, width), rows.dtype),
        scratch_shapes=hop_sems(),
        name="gather_chips",
        compiler_params=pltpu.CompilerParams(collective_id=collective_id, has_side_effects=True),
    )(rows)


def scatter_body(
    parts_ref, out_ref, near_ref, in2_ref, in3_ref, acc2_ref, acc3_ref, send1, recv1, send2, recv2, send3, recv3
):
    me = chip_index()
    greet_neighbours()
    opposite = flipped(me, ("y", "a", "b"))
    first = []
    for at, (axis, onward, last) in enumerate(HOPS):
        begin, count = THIRDS[at]
        copy = remote(parts_ref.at[opposite, pl.ds(begin, count)], in2_ref.at[pl.ds(begin, count)], send1.at[at], recv1.at[at], last)
        copy.start()
        first.append(copy)
    second = []
    rows = parts_ref.shape[1]
    half = rows // 2
    for part in range(2):
        here = pl.ds(part * half, half)
        for at, (axis, onward, last) in enumerate(HOPS):
            dest = flipped(me, (axis, onward))
            begin, count = THIRDS[at]
            if part == 0:
                first[at].wait_recv()
                acc2_ref[at] = parts_ref[dest]
                piece = pl.ds(begin, count)
                acc2_ref[at, piece] = (parts_ref[dest, piece].astype(f32) + in2_ref[piece].astype(f32)).astype(bf16)
            copy = remote(acc2_ref.at[at, here], in3_ref.at[at, here], send2.at[at, part], recv2.at[at, part], onward)
            copy.start()
            second.append(copy)
    third = []
    for part in range(2):
        here = pl.ds(part * half, half)
        for at, (axis, onward, last) in enumerate(HOPS):
            dest = flipped(me, (axis,))
            second[part * 3 + at].wait_recv()
            acc3_ref[at, here] = (parts_ref[dest, here].astype(f32) + in3_ref[at, here].astype(f32)).astype(bf16)
            copy = remote(acc3_ref.at[at, here], near_ref.at[at, here], send3.at[at, part], recv3.at[at, part], axis)
            copy.start()
            third.append(copy)
    for part in range(2):
        here = pl.ds(part * half, half)
        for at in range(3):
            third[part * 3 + at].wait_recv()
        out_ref[here] = (
            (parts_ref[me, here].astype(f32) + near_ref[0, here].astype(f32))
            + (near_ref[1, here].astype(f32) + near_ref[2, here].astype(f32))
        )
    for copy in first + second + third:
        copy.wait_send()


def scatter_chips(parts, collective_id):
    _, rows, width = parts.shape
    vmem = pl.BlockSpec(memory_space=pltpu.VMEM)
    dma = pltpu.SemaphoreType.DMA
    return pl.pallas_call(
        scatter_body,
        in_specs=[vmem],
        out_specs=vmem,
        out_shape=jax.ShapeDtypeStruct((rows, width), f32),
        scratch_shapes=[pltpu.VMEM((3, rows, width), bf16), pltpu.VMEM((rows, width), bf16)] + [pltpu.VMEM((3, rows, width), bf16)] * 3
        + [dma((3,))] * 2 + [dma((3, 2))] * 4,
        name="scatter_chips",
        compiler_params=pltpu.CompilerParams(collective_id=collective_id, has_side_effects=True, vmem_limit_bytes=32*2**20),
    )(parts)


def gather_slow(rows):
    return lax.all_to_all(
        jnp.broadcast_to(rows[None], (CHIPS,) + rows.shape), CHIP, split_axis=0, concat_axis=0, tiled=True
    )


def exchange_chips(parts):
    return lax.all_to_all(parts, CHIP, split_axis=0, concat_axis=0, tiled=True)


def scatter_slow(parts):
    return jnp.sum(exchange_chips(parts.astype(bf16)).astype(f32), axis=0)


def swap(values, axis):
    return lax.ppermute(values, axis, [(0, 1), (1, 0)])


def both_cores(own, axis):
    other = swap(own, "c")
    first = lax.axis_index("c") == 0
    return jnp.stack([jnp.where(first, own, other), jnp.where(first, other, own)], axis=axis)


def half_for_core(values, axis):
    core = lax.axis_index("c")
    own = lax.dynamic_index_in_dim(values, core, axis, keepdims=False)
    sent = lax.dynamic_index_in_dim(values, 1 - core, axis, keepdims=False)
    return own + swap(sent.astype(bf16), "c").astype(f32)


def sum_groups(tiles):
    groups = lax.axis_size("g")
    if groups != 2:
        return lax.psum_scatter(tiles.astype(f32), "g", scatter_dimension=1, tiled=True).astype(bf16)
    part = tiles.shape[1] // 2
    group = lax.axis_index("g")
    own = lax.dynamic_slice_in_dim(tiles, group * part, part, 1)
    sent = lax.dynamic_slice_in_dim(tiles, (1 - group) * part, part, 1)
    return (own.astype(f32) + swap(sent, "g").astype(f32)).astype(bf16)


def spread_columns(weight, width):
    rows = weight.shape[0]
    blocks = weight.reshape(rows, 2, CHIPS // 2, width)
    mine = lax.dynamic_index_in_dim(blocks, lax.axis_index("y"), 1, keepdims=False)
    return jnp.transpose(mine, (1, 0, 2))


def to_columns(blocks):
    groups = lax.axis_size("g")
    sent = jnp.broadcast_to(blocks[None], (groups,) + blocks.shape).reshape((-1,) + blocks.shape[1:])
    got = lax.all_to_all(sent, ("g", "a", "b"), split_axis=0, concat_axis=0, tiled=True)
    return both_cores(got, 1).reshape(-1, blocks.shape[-1])


def down_rows(w_down, chip):
    if lax.axis_size("g") == 2:
        other = swap(w_down, "g")
        mine = jnp.where(lax.axis_index("g") == lax.axis_index("y"), w_down, other)
        return both_cores(mine, 0).reshape(BLK, D)
    return lax.dynamic_slice_in_dim(lax.all_gather(w_down, FS, axis=0, tiled=True), chip * BLK, BLK, 0)


def band():
    tap = np.arange(CK)[:, None, None]
    source = np.arange(128)[None, :, None]
    target = np.arange(128)[None, None, :]
    return source - target + CK // 2 == tap


def body_any(
    layer_input, lengths, cotangent, w_query, w_key, w_value, w_out, w_gate, w_up, w_down, vec_copy, owners,
    basis_left, basis_right, block_master, block_first, block_second, vec_master, vec_first, vec_second,
):
    chip = (lax.axis_index("y") * 2 + lax.axis_index("a")) * 2 + lax.axis_index("b")
    fs_index = ((lax.axis_index("g") * 2 + lax.axis_index("a")) * 2 + lax.axis_index("b")) * 2 + lax.axis_index("c")
    seq_len = layer_input.shape[0]
    length = lengths[0]
    reps = lax.axis_size("y")
    fs_size = lax.axis_size(FS)

    own_vec = vec_copy.shape[0]
    small = jnp.concatenate(
        [vec_copy.astype(f32), jnp.zeros((1023 - own_vec,), f32), length.astype(f32).reshape(1)]
    ).reshape(8, 128)
    x_all, small_all = gather_first(layer_input, small, 1)
    small_all = small_all.reshape(fs_size, reps, 1024)
    vector = small_all[:, 0, :own_vec].reshape(-1)
    group_lengths = small_all[:, :, 1023].reshape(-1, 2, 2, 2, reps)
    group_lengths = lax.dynamic_index_in_dim(group_lengths, lax.axis_index("g"), 0, keepdims=False)
    group_lengths = lax.dynamic_index_in_dim(group_lengths, lax.axis_index("c"), 2, keepdims=False)
    group_lengths = jnp.transpose(group_lengths, (2, 0, 1)).reshape(CHIPS).astype(jnp.int32)
    gain_attn, gain_head, gain_ffn = vector[:D], vector[D : 2 * D], vector[2 * D : 3 * D]
    conv_end = 3 * D + H * CQ * CK
    theta = lax.dynamic_slice_in_dim(vector[3 * D : conv_end].reshape(H, CQ, CK), chip * 2, 2, 0)
    mixer = lax.dynamic_slice_in_dim(vector[conv_end : conv_end + 2 * H].reshape(H, 2), chip * 2, 2, 0)
    mix = mixer.reshape(4)
    gain_pair = jnp.pad(
        lax.dynamic_slice_in_dim(gain_head.reshape(H, DH), chip * 2, 2, 0), ((0, 0), (0, HP - DH))
    ).reshape(1, 2 * HP)
    toep = jnp.zeros((2, CQ, seq_len, seq_len), f32)
    offset = (
        jnp.arange(seq_len, dtype=jnp.int32)[:, None] - jnp.arange(seq_len, dtype=jnp.int32)[None, :] + CK // 2
    )
    for tap in range(CK):
        toep = jnp.where(offset[None, None] == tap, theta[:, :, tap][:, :, None, None], toep)
    toep = toep.astype(bf16).reshape(2, CQ * seq_len, seq_len)

    qkv_rows = to_columns(
        jnp.concatenate([spread_columns(w, 2 * DH) for w in (w_query, w_key, w_value)], axis=2)
    )
    w_qkv = jnp.pad(qkv_rows.reshape(D, 6, DH), ((0, 0), (0, 0), (0, HP - DH))).reshape(D, 6 * HP)
    w_in = to_columns(jnp.concatenate([spread_columns(w, BLK) for w in (w_gate, w_up)], axis=2))
    w_dn = down_rows(w_down, chip)
    w_o = lax.all_gather(w_out, FS, axis=0, tiled=True)

    input_float = layer_input.astype(f32)
    input_scale = rms(input_float)
    x_rows = x_all.reshape(CHIPS * seq_len, D).astype(f32)
    xn_rows = (x_rows * rms(x_rows) * gain_attn).astype(bf16)
    qkv = dot(xn_rows, w_qkv).astype(bf16).reshape(CHIPS, seq_len, 6 * HP)
    heads_pad, scores, weights, outs = run_forward(group_lengths, mix, qkv, toep, gain_pair)
    heads_sent = heads_pad.reshape(CHIPS, seq_len, 2, HP)[..., :DH].reshape(CHIPS, seq_len, 2 * DH)
    heads = jnp.transpose(exchange_chips(heads_sent), (1, 0, 2)).reshape(seq_len, D)
    hmid = input_float + dot(heads, w_o)
    hmid_scale = rms(hmid)
    hn_rows = gather_chips((hmid * hmid_scale * gain_ffn).astype(bf16), 2).reshape(CHIPS * seq_len, D)
    both = dot(hn_rows, w_in)
    gate, up = both[:, :BLK], both[:, BLK:]
    sig = jax.nn.sigmoid(gate)
    silu = gate * sig
    inner = (silu * up).astype(bf16)
    ffn = scatter_slow(dot(inner, w_dn).reshape(CHIPS, seq_len, D))
    layer_output = (hmid + ffn).astype(bf16)

    valid = (jnp.arange(seq_len) < length).astype(f32)
    dy = cotangent.astype(f32) * valid[:, None]
    dy_rows = gather_slow(dy.astype(bf16)).reshape(CHIPS * seq_len, D)
    dinner = dot_nt(dy_rows, w_dn)
    dgate = (dinner * up * (sig * (1.0 + gate * (1.0 - sig)))).astype(bf16)
    dup = (dinner * silu).astype(bf16)
    dboth = jnp.concatenate([dgate, dup], axis=1)
    dhn = scatter_chips(dot_nt(dboth, w_in).astype(bf16).reshape(CHIPS, seq_len, D), 3)
    dhmid, grad_gain_ffn = norm_backward(hmid, hmid_scale, gain_ffn, dhn)
    dhmid = dhmid + dy
    dattn = dhmid.astype(bf16)
    dheads = dot_nt(dattn, w_o).astype(bf16).reshape(seq_len, CHIPS, 2 * DH)
    dheads = exchange_chips(jnp.transpose(dheads, (1, 0, 2)))
    dheads = jnp.pad(dheads.reshape(CHIPS, seq_len, 2, DH), ((0, 0), (0, 0), (0, 0), (0, HP - DH)))
    dqkv, theta_sums, mixer_sums, gain_sums = run_backward(
        group_lengths, mix, qkv, toep, gain_pair, scores, weights, outs, dheads.reshape(CHIPS, seq_len, 2 * HP)
    )
    dqkv_rows = dqkv.reshape(CHIPS * seq_len, 6 * HP)
    dxn = scatter_slow(dot_nt(dqkv_rows, w_qkv).reshape(CHIPS, seq_len, D))
    dinput, grad_gain_attn = norm_backward(input_float, input_scale, gain_attn, dxn)
    input_grad = dinput + dhmid

    taps = jnp.asarray(band())
    theta_sums = theta_sums.reshape(2, seq_len, CQ, seq_len)
    grad_theta = jnp.stack(
        [jnp.sum(jnp.where(taps[tap][None, :, None, :], theta_sums, 0.0), axis=(1, 3)) for tap in range(CK)], axis=2
    )
    grad_mixer = jnp.sum(mixer_sums[:4], axis=1)
    vector_grad = jnp.concatenate(
        [
            grad_gain_attn,
            lax.dynamic_update_slice_in_dim(
                jnp.zeros((D,), f32), gain_sums.reshape(2, HP)[:, :DH].reshape(-1), chip * 2 * DH, 0
            ),
            grad_gain_ffn,
            lax.dynamic_update_slice_in_dim(
                jnp.zeros((H * CQ * CK,), f32), grad_theta.reshape(-1), chip * 2 * CQ * CK, 0
            ),
            lax.dynamic_update_slice_in_dim(jnp.zeros((2 * H,), f32), grad_mixer, chip * 4, 0),
        ]
    )
    pieces = jnp.pad(vector_grad.reshape(fs_size, 1, own_vec), ((0, 0), (0, 0), (0, 512 - own_vec)))
    pieces = jnp.broadcast_to(pieces, (fs_size, reps, 512)).reshape(-1, 4, 128)
    vector_total = jnp.sum(
        lax.all_to_all(pieces, ALL, split_axis=0, concat_axis=0, tiled=True), axis=0
    ).reshape(512)[:own_vec]

    strip = BLK // (2 * CHIPS)
    grad_in = dot_tn(hn_rows, dboth).reshape(ROW_TILES, 2, CHIPS, strip, 2, BLK)
    grad_down = dot_tn(inner, dy_rows).reshape(2, CHIPS, strip, ROW_TILES, BLK)
    grad_in = jnp.transpose(half_for_core(grad_in, 1), (1, 3, 0, 2, 4)).reshape(CHIPS, 2 * ROW_TILES, strip, BLK)
    grad_down = jnp.transpose(half_for_core(grad_down, 0), (0, 2, 1, 3))
    ffn_tiles = exchange_chips(jnp.concatenate([grad_in, grad_down], axis=1).astype(bf16))
    gate_tiles = jnp.transpose(ffn_tiles[:, : 2 * ROW_TILES], (1, 0, 2, 3)).reshape(-1, strip, BLK)
    down_tiles = ffn_tiles[:, 2 * ROW_TILES :].reshape(-1, strip, BLK)
    grad_qkv = dot_tn(xn_rows, dqkv_rows).reshape(ROW_TILES, 2, CHIPS, strip, 6, HP)[..., :DH]
    grad_qkv = jnp.transpose(half_for_core(grad_qkv, 1), (1, 0, 2, 3, 4))
    grad_qkv = exchange_chips(grad_qkv.astype(bf16).reshape(CHIPS, ROW_TILES, strip, 6 * DH))
    grad_qkv = jnp.transpose(
        grad_qkv.reshape(CHIPS, ROW_TILES, strip, 3, 2 * DH), (3, 1, 2, 0, 4)
    ).reshape(3, ROW_TILES, strip, ROW_TILES, BLK)
    qkv_tiles = jnp.transpose(grad_qkv, (0, 1, 3, 2, 4)).reshape(-1, strip, BLK)
    heads_strips = jnp.transpose(heads.reshape(seq_len, 2 * ROW_TILES, CHIPS, strip), (2, 0, 1, 3))
    heads_strips = exchange_chips(heads_strips.reshape(CHIPS, seq_len, 2 * ROW_TILES * strip))
    dattn_rows = gather_slow(dattn).reshape(CHIPS * seq_len, D)
    grad_out = dot_tn(heads_strips.reshape(CHIPS * seq_len, -1), dattn_rows)
    grad_out = half_for_core(grad_out.reshape(ROW_TILES, 2, strip, ROW_TILES, BLK), 1)
    out_tiles = jnp.transpose(grad_out.astype(bf16), (0, 2, 1, 3)).reshape(-1, strip, BLK)

    groups = lax.axis_size("g")
    part = strip // groups
    own_slots = basis_left.shape[0]
    devices = groups * 2 * CHIPS
    slot_total = own_slots * devices
    sums = jnp.concatenate(
        [sum_groups(jnp.concatenate([qkv_tiles, out_tiles], axis=0)), sum_groups(jnp.concatenate([gate_tiles, down_tiles], axis=0))],
        axis=0,
    )
    matches = (jnp.arange(slot_total)[:, None] == owners[None, :]).astype(bf16)
    slots = dot(matches, sums.reshape(sums.shape[0], -1)).astype(bf16)
    slots = lax.all_to_all(
        slots.reshape(devices, own_slots, part, BLK), ALL, split_axis=0, concat_axis=0, tiled=True
    )
    slots = slots.reshape(groups, 2, 2, 2, 2, own_slots, part, BLK)
    own_grad = jnp.transpose(slots, (5, 3, 4, 1, 2, 0, 6, 7)).reshape(own_slots, BLK, BLK)

    left_low, right_low = basis_left.astype(bf16), basis_right.astype(bf16)
    rotated = jnp.einsum("sia,sij->saj", left_low, own_grad, preferred_element_type=f32)
    rotated = jnp.einsum("saj,sjb->sab", rotated.astype(bf16), right_low, preferred_element_type=f32)
    first_new = beta_first * block_first + (1.0 - beta_first) * rotated
    second_new = beta_second * block_second + (1.0 - beta_second) * rotated * rotated
    direction = (first_new / (jnp.sqrt(second_new) + eps_adam)).astype(bf16)
    turned = jnp.einsum("sia,sab->sib", left_low, direction, preferred_element_type=f32)
    turned = jnp.einsum("sib,sjb->sij", turned.astype(bf16), right_low, preferred_element_type=f32)
    master_new = block_master - rate_block * (turned + decay_block * block_master)
    vec_first_new = beta_first * vec_first + (1.0 - beta_first) * vector_total
    vec_second_new = beta_second * vec_second + (1.0 - beta_second) * vector_total * vector_total
    vec_master_new = vec_master - rate_vector * vec_first_new / (jnp.sqrt(vec_second_new) + eps_adam)
    return (
        layer_output, input_grad, first_new, second_new, master_new, master_new.astype(bf16),
        vec_first_new, vec_second_new, vec_master_new, vec_master_new.astype(bf16),
    )


def group_at(mask):
    return {axis: 1 - lax.axis_index(axis) for axis, bit in (("g", 4), ("a", 2), ("b", 1)) if mask & bit}


def other_bit(axis, changed):
    at = lax.axis_index(axis)
    return 1 - at if changed else at


def push(src, dst, send, recv, device):
    copy = pltpu.make_async_remote_copy(src_ref=src, dst_ref=dst, send_sem=send, recv_sem=recv, device_id=device)
    copy.start()
    return copy


class Gather:
    def __init__(self, x_ref, out_ref, local_sem, send1, recv1, send2, recv2, send3, recv3):
        self.x, self.out, self.local_sem = x_ref, out_ref, local_sem
        self.sems = ((send1, recv1), (send2, recv2), (send3, recv3))
        self.me = chip_index()
        self.half = x_ref.shape[0] // 2
        self.sent, self.second = [], []

    def here(self, part):
        return pl.ds(part * self.half, self.half)

    def start(self):
        self.local = pltpu.make_async_copy(self.x, self.out.at[self.me], self.local_sem)
        self.local.start()
        send, recv = self.sems[0]
        for part in range(2):
            for at, (axis, _, _) in enumerate(HOPS):
                self.sent.append(
                    push(
                        self.x.at[self.here(part)], self.out.at[self.me, self.here(part)],
                        send.at[at, part], recv.at[at, part], across(axis),
                    )
                )

    def onward(self):
        send, recv = self.sems[1]
        for part in range(2):
            for at, (axis, onward, _) in enumerate(HOPS):
                self.sent[part * 3 + at].wait_recv()
                block = self.out.at[flipped(self.me, (axis,)), self.here(part)]
                self.second.append(push(block, block, send.at[at, part], recv.at[at, part], across(onward)))

    def last(self):
        send, recv = self.sems[2]
        self.third = []
        for copy in self.second:
            copy.wait_recv()
        for at, (axis, onward, last) in enumerate(HOPS):
            begin, count = THIRDS[at]
            piece = self.out.at[flipped(self.me, (axis, onward)), pl.ds(begin, count)]
            self.third.append(push(piece, piece, send.at[at], recv.at[at], across(last)))

    def finish(self):
        for copy in self.third:
            copy.wait_recv()
        self.local.wait()

    def drain(self):
        for copy in self.sent + self.second + self.third:
            copy.wait_send()


class SideGather:
    def __init__(self, x_ref, out_ref, local_sem, send1, recv1, send2, recv2, send3, recv3):
        self.x, self.out, self.local_sem = x_ref, out_ref, local_sem
        self.sems = ((send1, recv1), (send2, recv2), (send3, recv3))
        self.me = chip_index()
        half = x_ref.shape[0] // 2
        self.low, self.high = pl.ds(0, half), pl.ds(half, half)

    def start(self):
        self.local = pltpu.make_async_copy(self.x, self.out.at[self.me], self.local_sem)
        self.local.start()
        send, recv = self.sems[0]
        self.first = [
            push(self.x, self.out.at[self.me], send.at[at], recv.at[at], across(axis)) for at, axis in enumerate("aby")
        ]

    def onward(self):
        send, recv = self.sems[1]
        blocks = [self.out.at[flipped(self.me, (axis,))] for axis in "aby"]
        self.first[0].wait_recv()
        self.second = [
            push(blocks[0], blocks[0], send.at[0], recv.at[0], across("b")),
            push(blocks[0], blocks[0], send.at[1], recv.at[1], across("y")),
        ]
        self.first[1].wait_recv()
        piece = blocks[1].at[self.high]
        self.second.append(push(piece, piece, send.at[2], recv.at[2], across("y")))
        self.first[2].wait_recv()
        piece = blocks[2].at[self.low]
        self.second.append(push(piece, piece, send.at[3], recv.at[3], across("b")))

    def last(self):
        send, recv = self.sems[2]
        self.second[0].wait_recv()
        piece = self.out.at[flipped(self.me, ("a", "b")), self.high]
        self.third = [push(piece, piece, send.at[0], recv.at[0], across("y"))]
        self.second[1].wait_recv()
        piece = self.out.at[flipped(self.me, ("a", "y")), self.low]
        self.third.append(push(piece, piece, send.at[1], recv.at[1], across("b")))

    def finish(self):
        for copy in self.second[2:] + self.third:
            copy.wait_recv()
        self.local.wait()

    def drain(self):
        for copy in self.first + self.second + self.third:
            copy.wait_send()


def side_sems():
    dma = pltpu.SemaphoreType.DMA
    return [dma] + [dma((3,))] * 2 + [dma((4,))] * 2 + [dma((2,))] * 2


class Scatter:
    def __init__(self, parts, near, in2, in3, acc2, acc3, send1, recv1, send2, recv2, send3, recv3):
        self.parts, self.near, self.in2, self.in3, self.acc2, self.acc3 = parts, near, in2, in3, acc2, acc3
        self.sems = ((send1, recv1), (send2, recv2), (send3, recv3))
        self.me = chip_index()
        self.half = parts.shape[1] // 2

    def here(self, part):
        return pl.ds(part * self.half, self.half)

    def start(self):
        send, recv = self.sems[0]
        opposite = flipped(self.me, ("y", "a", "b"))
        self.first = []
        for at, (_, _, last) in enumerate(HOPS):
            rows = pl.ds(*THIRDS[at])
            self.first.append(push(self.parts.at[opposite, rows], self.in2.at[rows], send.at[at], recv.at[at], across(last)))

    def onward(self):
        send, recv = self.sems[1]
        self.second = []
        for part in range(2):
            for at, (axis, onward, _) in enumerate(HOPS):
                dest = flipped(self.me, (axis, onward))
                if part == 0:
                    self.first[at].wait_recv()
                    rows = pl.ds(*THIRDS[at])
                    self.acc2[at] = self.parts[dest]
                    self.acc2[at, rows] = (
                        self.parts[dest, rows].astype(f32) + self.in2[rows].astype(f32)
                    ).astype(bf16)
                here = self.here(part)
                self.second.append(
                    push(self.acc2.at[at, here], self.in3.at[at, here], send.at[at, part], recv.at[at, part], across(onward))
                )

    def last(self):
        send, recv = self.sems[2]
        self.third = []
        for part in range(2):
            here = self.here(part)
            for at, (axis, _, _) in enumerate(HOPS):
                dest = flipped(self.me, (axis,))
                self.second[part * 3 + at].wait_recv()
                self.acc3[at, here] = (
                    self.parts[dest, here].astype(f32) + self.in3[at, here].astype(f32)
                ).astype(bf16)
                self.third.append(
                    push(self.acc3.at[at, here], self.near.at[at, here], send.at[at, part], recv.at[at, part], across(axis))
                )

    def finish(self, part):
        here = self.here(part)
        for at in range(3):
            self.third[part * 3 + at].wait_recv()
        return (self.parts[self.me, here].astype(f32) + self.near[0, here].astype(f32)) + (
            self.near[1, here].astype(f32) + self.near[2, here].astype(f32)
        )

    def drain(self):
        for copy in self.first + self.second + self.third:
            copy.wait_send()


def scatter_scratch(rows, width):
    dma = pltpu.SemaphoreType.DMA
    three = pltpu.VMEM((3, rows, width), bf16)
    return [three, pltpu.VMEM((rows, width), bf16), three, three, three] + [dma((3,))] * 2 + [dma((3, 2))] * 4


VMEM = pl.BlockSpec(memory_space=pltpu.VMEM)


def dispatch_body(
    x_ref, vec_ref, blocks_ref, w_out_ref, out_ref, vecs_ref, wq_ref, wo_ref,
    vec_send, vec_recv, vec_local, w_local, o_local, w_send, w_recv, core_send, core_recv,
    o_send, o_recv, o_side_send, o_side_recv, o_core_send, o_core_recv, *hops,
):
    devices = lax.axis_size(ALL)
    me = device_index()
    g, a, b, c, y = (lax.axis_index(axis) for axis in ALL)
    mine = ((g * 2 + a) * 2 + b) * 2 + c
    local = pltpu.make_async_copy(vec_ref, vecs_ref.at[me], vec_local)
    local.start()
    own = pltpu.make_async_copy(blocks_ref.at[chip_index()], wq_ref.at[mine], w_local)
    own.start()
    own_out = pltpu.make_async_copy(w_out_ref, wo_ref.at[mine], o_local)
    own_out.start()
    greet_all()
    gather = Gather(x_ref, out_ref, *hops)
    gather.start()

    def push_vec(step, carry):
        pltpu.make_async_remote_copy(
            src_ref=vec_ref, dst_ref=vecs_ref.at[me], send_sem=vec_send, recv_sem=vec_recv,
            device_id=device_at(lax.rem(me + step, devices)),
        ).start()
        return carry

    lax.fori_loop(1, devices, push_vec, 0)
    sent, relayed = [], []
    for mask in (4, 6, 5, 7, 2, 1, 3):
        block = (y * 2 + other_bit("a", mask & 2)) * 2 + other_bit("b", mask & 1)
        sent.append(push(blocks_ref.at[block], wq_ref.at[mine], w_send.at[mask], w_recv.at[mask], group_at(mask)))
    half = pl.ds(pl.multiple_of(y * 48, 16), 48)
    shard = {mask: source_at(mask) for mask in range(8)}
    lines = {
        mask: push(w_out_ref.at[half], wo_ref.at[mine, half], o_send.at[mask], o_recv.at[mask], group_at(mask))
        for mask in (2, 4, 6)
    }
    lines[1] = push(w_out_ref.at[half], wo_ref.at[mine, half], o_send.at[1], o_recv.at[1], across("b"))
    o_core = [push(w_out_ref, wo_ref.at[mine], o_core_send.at[0], o_core_recv.at[0], across("c"))]
    own.wait()
    relayed.append(push(wq_ref.at[mine], wq_ref.at[mine], core_send.at[0], core_recv.at[0], across("c")))
    gather.onward()
    o_side = {}

    def to_side(mask):
        lines[mask].wait_recv()
        piece = wo_ref.at[shard[mask], half]
        o_side[mask] = push(piece, piece, o_side_send.at[mask], o_side_recv.at[mask], across("y"))

    def relay(mask):
        sent[(4, 6, 5, 7, 2, 1, 3).index(mask)].wait_recv()
        block = wq_ref.at[shard[mask]]
        relayed.append(push(block, block, core_send.at[mask], core_recv.at[mask], across("c")))

    for mask in (2, 4, 6):
        lines[mask].wait_recv()
        piece = wo_ref.at[shard[mask], half]
        lines[mask + 1] = push(piece, piece, o_send.at[mask + 1], o_recv.at[mask + 1], across("b"))
        o_side[mask] = push(piece, piece, o_side_send.at[mask], o_side_recv.at[mask], across("y"))
    to_side(1)
    relay(4)
    relay(6)
    gather.last()
    for mask in (3, 5, 7):
        to_side(mask)
    for mask in (5, 7, 2, 1, 3):
        relay(mask)
    for mask in (2, 4, 6, 1, 3, 5, 7):
        o_side[mask].wait_recv()
        block = wo_ref.at[shard[mask]]
        o_core.append(push(block, block, o_core_send.at[mask], o_core_recv.at[mask], across("c")))
    gather.finish()
    for copy in relayed + o_core:
        copy.wait_recv()
    others = vecs_ref.at[pl.ds(0, devices - 1)]
    pltpu.make_async_copy(others, others, vec_recv).wait()
    pltpu.make_async_copy(others, others, vec_send).wait()
    local.wait()
    own_out.wait()
    gather.drain()
    for copy in sent + relayed + list(lines.values()) + list(o_side.values()) + o_core:
        copy.wait_send()


def source_at(mask):
    return ((other_bit("g", mask & 4) * 2 + other_bit("a", mask & 2)) * 2 + other_bit("b", mask & 1)) * 2 + lax.axis_index("c")


def dispatch(rows, vec, blocks, w_out):
    count, width = rows.shape
    dma = pltpu.SemaphoreType.DMA
    return pl.pallas_call(
        dispatch_body,
        in_specs=[ANYS] * 4,
        out_specs=[ANYS] * 4,
        out_shape=[
            jax.ShapeDtypeStruct((CHIPS, count, width), rows.dtype),
            jax.ShapeDtypeStruct((lax.axis_size(ALL),) + vec.shape, vec.dtype),
            jax.ShapeDtypeStruct((16,) + blocks.shape[1:], blocks.dtype),
            jax.ShapeDtypeStruct((16,) + w_out.shape, w_out.dtype),
        ],
        scratch_shapes=[dma] * 5 + [dma((8,))] * 10 + hop_sems(),
        name="dispatch",
        compiler_params=pltpu.CompilerParams(collective_id=1, has_side_effects=True),
    )(rows, vec, blocks, w_out)


def forward_body(
    len_ref, mix_ref, x_all_ref, x_ref, gains_ref, wq_ref, toep_ref, gain_ref, wo_ref, w_gate_ref, w_up_ref, w_down_ref, dy_ref,
    xn_ref, qkv_ref, s_ref, p_ref, o_ref, heads_ref, hmid_ref, hn_all_ref, w_in_ref, w_dn_ref, dy_all_ref,
    pad_ref, out_heads, hn_ref, local_sems, w_send, w_recv, u_send, u_recv, core_send, core_recv,
    d_send, d_recv, head_send, head_recv, *hops,
):
    seqs, rows, _ = x_all_ref.shape
    g, a, b, c, y = (lax.axis_index(axis) for axis in ALL)
    me = chip_index()
    mine = source_at(0)
    low, high = pl.ds(0, BLK), pl.ds(BLK, BLK)

    def columns(chip):
        return pl.ds(pl.multiple_of(chip * BLK, BLK), BLK)

    greet_all()
    local = [
        pltpu.make_async_copy(w_gate_ref.at[:, columns(me)], w_in_ref.at[mine, :, low], local_sems.at[0]),
        pltpu.make_async_copy(w_up_ref.at[:, columns(me)], w_in_ref.at[mine, :, high], local_sems.at[1]),
    ]
    for copy in local:
        copy.start()
    gate, up, relayed = {}, {}, []
    order = (4, 6, 5, 7, 2, 1, 3)
    for mask in order:
        to = (y * 2 + other_bit("a", mask & 2)) * 2 + other_bit("b", mask & 1)
        gate[mask] = push(
            w_gate_ref.at[:, columns(to)], w_in_ref.at[mine, :, low], w_send.at[mask], w_recv.at[mask], group_at(mask)
        )
        up[mask] = push(
            w_up_ref.at[:, columns(to)], w_in_ref.at[mine, :, high], u_send.at[mask], u_recv.at[mask], group_at(mask)
        )

    def down_to_group():
        return pltpu.make_async_remote_copy(
            src_ref=w_down_ref, dst_ref=w_dn_ref.at[c], send_sem=d_send.at[0], recv_sem=d_recv.at[0], device_id=across("g")
        )

    def down_to_core():
        return pltpu.make_async_remote_copy(
            src_ref=w_dn_ref.at[c], dst_ref=w_dn_ref.at[c], send_sem=d_send.at[1], recv_sem=d_recv.at[1], device_id=across("c")
        )

    down_local = pltpu.make_async_copy(w_down_ref, w_dn_ref.at[c], local_sems.at[2])

    @pl.when(g == y)
    def _():
        down_local.start()
        down_to_group().start()

    side = SideGather(dy_ref, dy_all_ref, *hops[:7])
    side.start()

    def relay(mask):
        gate[mask].wait_recv()
        up[mask].wait_recv()
        block = w_in_ref.at[source_at(mask)]
        relayed.append(push(block, block, core_send.at[mask], core_recv.at[mask], across("c")))

    pad_ref[0:8, :] = jnp.zeros((8, rows), f32)
    blank = jnp.zeros((rows, HP - DH), bf16)
    batch = 4

    def project(at, carry):
        values = x_all_ref[pl.ds(at * batch, batch)].astype(f32).reshape(batch * rows, D)
        normed = (values * rms(values) * gains_ref[0:1, :]).astype(bf16)
        xn_ref[pl.ds(at * batch, batch)] = normed.reshape(batch, rows, D)
        made = dot(normed, wq_ref[...]).astype(bf16)
        for seq in range(batch):
            for piece in range(6):
                qkv_ref[at * batch + seq, :, piece * HP : (piece + 1) * HP] = jnp.concatenate(
                    [made[seq * rows : (seq + 1) * rows, piece * DH : (piece + 1) * DH], blank], axis=1
                )
        return carry

    lax.fori_loop(0, seqs // batch, project, 0)
    for copy in local:
        copy.wait()
    relayed.append(push(w_in_ref.at[mine], w_in_ref.at[mine], core_send.at[0], core_recv.at[0], across("c")))
    query_at = lax.broadcasted_iota(jnp.int32, (rows, rows), 0)
    key_at = lax.broadcasted_iota(jnp.int32, (rows, rows), 1)

    def head_copy(seq):
        return pltpu.make_async_remote_copy(
            src_ref=out_heads.at[seq], dst_ref=heads_ref.at[me], send_sem=head_send.at[seq], recv_sem=head_recv.at[me],
            device_id={"y": lax.div(seq, 4), "a": lax.rem(lax.div(seq, 2), 2), "b": lax.rem(seq, 2)},
        )

    def attend(step, carry):
        seq = lax.rem(me + step, seqs)
        keep = (key_at <= query_at) & (key_at < len_ref[seq])
        weights, made = [], []
        for head in range(2):
            query = qkv_ref[seq, :, head * HP : (head + 1) * HP]
            key = qkv_ref[seq, :, (2 + head) * HP : (3 + head) * HP]
            scores = jnp.where(keep, dot_nt(query, key) * (1.0 / math.sqrt(DH)), 0.0)
            s_ref[seq, head] = scores.astype(bf16)
            wide = shifted_down(pad_ref, scores)
            near = wide.astype(bf16)
            rest = (wide - near.astype(f32)).astype(bf16)
            conv = dot(near, toep_ref[head]) + dot(rest, toep_ref[head])
            logits = jnp.where(keep, conv, -1e30)
            weight = jnp.exp(logits - jnp.max(logits, axis=-1, keepdims=True))
            weight = weight / jnp.sum(weight, axis=-1, keepdims=True)
            p_ref[seq, head] = weight
            weights.append(weight)
        for head in range(2):
            mixed = mix_ref[2 * head] * weights[0] + mix_ref[2 * head + 1] * weights[1]
            value = qkv_ref[seq, :, (4 + head) * HP : (5 + head) * HP]
            out = dot(mixed.astype(bf16), value)
            o_ref[seq, :, head * HP : (head + 1) * HP] = out
            scale = lax.rsqrt(jnp.sum(out * out, axis=-1, keepdims=True) * (1.0 / DH) + eps_norm)
            made.append((out * scale * gain_ref[:, head * HP : (head + 1) * HP])[:, :DH])
        out_heads[seq] = jnp.concatenate(made, axis=1).astype(bf16)

        @pl.when(step > 0)
        def _():
            head_copy(seq).start()

        return carry

    lax.fori_loop(0, 4, attend, 0)
    side.onward()
    lax.fori_loop(4, seqs, attend, 0)
    heads_ref[me] = out_heads[me]
    side.last()

    def head_arrived(step, carry):
        source = lax.rem(me + step, seqs)
        pltpu.make_async_copy(out_heads.at[source], heads_ref.at[source], head_recv.at[source]).wait()
        return carry

    lax.fori_loop(1, seqs, head_arrived, 0)

    def project_out(at, carry):
        cols = pl.ds(pl.multiple_of(at * BLK, BLK), BLK)
        total = x_ref[:, cols].astype(f32)
        for chip in range(CHIPS):
            weight = wo_ref[2 * chip : 2 * chip + 2, :, cols].reshape(2 * DH, BLK)
            total += dot(heads_ref[chip], weight)
        hmid_ref[:, cols] = total
        return carry

    lax.fori_loop(0, ROW_TILES, project_out, 0)
    hmid = hmid_ref[...]
    hn_ref[...] = (hmid * rms(hmid) * gains_ref[1:2, :]).astype(bf16)
    gather = Gather(hn_ref, hn_all_ref, *hops[7:])
    gather.start()
    for mask in (2, 1, 3):
        relay(mask)
    gather.onward()
    for mask in (4, 6):
        relay(mask)
    gather.last()
    for mask in (5, 7):
        relay(mask)

    @pl.when(g == y)
    def _():
        down_local.wait()
        down_to_core().start()
        down_to_group().wait_send()

    @pl.when(g != y)
    def _():
        down_to_group().wait_recv()
        down_to_core().start()

    down_to_core().wait()
    side.finish()
    gather.finish()
    for copy in relayed:
        copy.wait_recv()

    def head_left(step, carry):
        head_copy(lax.rem(me + step, seqs)).wait_send()
        return carry

    lax.fori_loop(1, seqs, head_left, 0)
    side.drain()
    gather.drain()
    for copy in relayed + list(gate.values()) + list(up.values()):
        copy.wait_send()


def run_front(lengths, mix, x_all, x, gains, w_qkv, toep, gain, w_o, w_gate, w_up, w_down, dy):
    seqs, rows, _ = x_all.shape
    dma = pltpu.SemaphoreType.DMA
    shapes = [
        ((seqs, rows, D), bf16), ((seqs, rows, 6 * HP), bf16), ((seqs, 2, rows, rows), bf16), ((seqs, 2, rows, rows), f32),
        ((seqs, rows, 2 * HP), f32), ((CHIPS, rows, 2 * DH), bf16), ((rows, D), f32), ((CHIPS, rows, D), bf16),
        ((16, w_gate.shape[0], 2 * BLK), bf16), ((2,) + w_down.shape, bf16), ((CHIPS, rows, D), bf16),
    ]
    return pl.pallas_call(
        forward_body,
        in_specs=[SMEM, SMEM] + [VMEM] * 7 + [ANYS] * 4,
        out_specs=[VMEM] * 7 + [ANYS] * 4,
        out_shape=[jax.ShapeDtypeStruct(*shape) for shape in shapes],
        scratch_shapes=[
            pltpu.VMEM((rows + 8, rows), f32), pltpu.VMEM((seqs, rows, 2 * DH), bf16), pltpu.VMEM((rows, D), bf16),
            dma((3,)),
        ] + [dma((8,))] * 6 + [dma((2,))] * 2 + [dma((8,))] * 2 + side_sems() + hop_sems(),
        name="front",
        compiler_params=pltpu.CompilerParams(collective_id=2, has_side_effects=True, vmem_limit_bytes=56 * 2**20),
    )(lengths, mix, x_all, x, gains, w_qkv, toep, gain, w_o, w_gate, w_up, w_down, dy)


def middle_body(
    len_ref, mix_ref, hn_ref, w_in_ref, w_dn_ref, dy_ref, dy_own_ref, hmid_ref, gain_ffn_ref, wo_ref,
    qkv_ref, toep_ref, gain_ref, s_ref, p_ref, o_ref, strips_ref,
    layer_ref, dhmid_ref, gain_ffn_grad_ref, dqkv_ref, theta_ref, mixer_ref, gain_grad_ref, go_ref, tiles_ref,
    pad_ref, inner_ref, dboth_ref, parts_ref, dattn_ref, all_ref, grads_ref, sent_ref, strips_in, gin_ref, gd_ref,
    half_in, half_d, in_gu, in_d, near2, in22, in32, local_sems, strip_send, strip_recv, head_send, head_recv,
    core_send, core_recv, gu_send, gu_recv, d_send, d_recv, *rest,
):
    scatter_args, scatter2_sems, side = rest[:11], rest[11:17], rest[17:]
    seqs, rows, _ = hn_ref.shape
    g, a, b, c, y = (lax.axis_index(axis) for axis in ALL)
    me = chip_index()
    strip_local = pltpu.make_async_copy(strips_ref.at[me], strips_in.at[me], local_sems.at[0])
    strip_local.start()
    greet_all()
    strips_sent = []
    for mask in (7, 6, 5, 3, 4, 2, 1):
        to = flipped(me, [axis for axis in BITS if mask & BITS[axis]])
        strips_sent.append(push(strips_ref.at[to], strips_in.at[me], strip_send.at[mask], strip_recv.at[mask], chip_at(mask)))

    def hidden(at, carry):
        two = pl.ds(at * 2, 2)
        both = dot(hn_ref[two].reshape(2 * rows, D), w_in_ref[...])
        gate, up = both[:, :BLK], both[:, BLK:]
        dinner = dot_nt(dy_ref[two].reshape(2 * rows, D), w_dn_ref[...])
        sig = jax.nn.sigmoid(gate)
        silu = gate * sig
        inner_ref[two] = (silu * up).astype(bf16).reshape(2, rows, BLK)
        dgate = (dinner * up * (sig * (1.0 + gate * (1.0 - sig)))).astype(bf16)
        dup = (dinner * silu).astype(bf16)
        dboth_ref[two, :, 0:BLK] = dgate.reshape(2, rows, BLK)
        dboth_ref[two, :, BLK:] = dup.reshape(2, rows, BLK)
        back = dot_nt(dgate, w_in_ref[:, 0:BLK]) + dot_nt(dup, w_in_ref[:, BLK:])
        parts_ref[two] = back.astype(bf16).reshape(2, rows, D)
        return carry

    lax.fori_loop(0, seqs // 2, hidden, 0)
    scatter = Scatter(parts_ref, *scatter_args)
    scatter.start()

    def down_grad(col, carry):
        cols = pl.ds(pl.multiple_of(col * BLK, BLK), BLK)
        made = dot_tn(inner_ref[...].reshape(seqs * rows, BLK), dy_ref[:, :, cols].reshape(seqs * rows, BLK))
        gd_ref[:, :, :, :, cols] = made.astype(bf16).reshape(2, CHIPS, 2, BLK // 32, BLK)
        return carry

    lax.fori_loop(0, ROW_TILES, down_grad, 0)
    to_core = [push(gd_ref.at[1 - c], half_d, core_send.at[0], core_recv.at[0], across("c"))]
    scatter.onward()

    def in_grad(row, carry):
        values = hn_ref[:, :, pl.ds(pl.multiple_of(row * BLK, BLK), BLK)].reshape(seqs * rows, BLK)
        for which in range(2):
            cols = slice(which * BLK, (which + 1) * BLK)
            made = dot_tn(values, dboth_ref[:, :, cols].reshape(seqs * rows, BLK))
            gin_ref[row, :, :, :, :, cols] = made.astype(bf16).reshape(2, CHIPS, 2, BLK // 32, BLK)
        return carry

    lax.fori_loop(0, ROW_TILES, in_grad, 0)
    to_core.append(push(gin_ref.at[:, 1 - c], half_in, core_send.at[1], core_recv.at[1], across("c")))
    scatter.last()
    half = rows // 2
    gain_sum = jnp.zeros((1, D), f32)
    for part in range(2):
        here = pl.ds(part * half, half)
        grad = scatter.finish(part)
        values = hmid_ref[here]
        scale = rms(values)
        unit = values * scale
        inside = grad * gain_ffn_ref[...]
        gain_sum += jnp.sum(grad * unit, axis=0, keepdims=True)
        dhmid = scale * (inside - unit * jnp.mean(inside * unit, axis=-1, keepdims=True)) + dy_own_ref[here].astype(f32)
        dhmid_ref[here] = dhmid
        dattn_ref[here] = dhmid.astype(bf16)
    gain_ffn_grad_ref[...] = gain_sum

    def grad_copy(to):
        return pltpu.make_async_remote_copy(
            src_ref=sent_ref.at[to], dst_ref=grads_ref.at[me], send_sem=head_send.at[to], recv_sem=head_recv.at[me],
            device_id={"y": lax.div(to, 4), "a": lax.rem(lax.div(to, 2), 2), "b": lax.rem(to, 2)},
        )

    def send_grad(step, carry):
        to = lax.rem(me + step, seqs)
        sent_ref[to] = dot_nt(dattn_ref[...], wo_ref[to]).astype(bf16)

        @pl.when(step > 0)
        def _():
            grad_copy(to).start()

        return carry

    lax.fori_loop(0, seqs, send_grad, 0)
    grads_ref[me] = sent_ref[me]
    gather = SideGather(dattn_ref, all_ref, *side)
    gather.start()

    slot = g * CHIPS + me
    to_core[0].wait_recv()
    half_d[...] = (half_d[...].astype(f32) + gd_ref[c].astype(f32)).astype(bf16)
    tiles_sent = []
    order = (15, 14, 13, 11, 12, 10, 9, 8, 7, 6, 5, 3, 4, 2, 1)
    for mask in order:
        to = flipped(me, [axis for axis in BITS if mask & BITS[axis]])
        tiles_sent.append(
            push(half_d.at[to, other_bit("g", mask & 8)], in_d.at[slot], d_send.at[mask], d_recv.at[mask], wide_at(mask))
        )
    in_d[slot] = half_d[me, g]
    to_core[1].wait_recv()
    for row in range(ROW_TILES):
        half_in[row] = (half_in[row].astype(f32) + gin_ref[row, c].astype(f32)).astype(bf16)
    for mask in order:
        to = flipped(me, [axis for axis in BITS if mask & BITS[axis]])
        tiles_sent.append(
            push(half_in.at[:, to, other_bit("g", mask & 8)], in_gu.at[slot], gu_send.at[mask], gu_recv.at[mask], wide_at(mask))
        )
    in_gu[slot] = half_in[:, me, g]

    pad_ref[rows : rows + 8, :] = jnp.zeros((8, rows), f32)
    theta_ref[...] = jnp.zeros_like(theta_ref)
    mixer_ref[...] = jnp.zeros_like(mixer_ref)
    gain_grad_ref[...] = jnp.zeros_like(gain_grad_ref)
    query_at = lax.broadcasted_iota(jnp.int32, (rows, rows), 0)
    key_at = lax.broadcasted_iota(jnp.int32, (rows, rows), 1)
    blank = jnp.zeros((rows, HP - DH), f32)

    def grad_arrived(step, carry):
        source = lax.rem(me + step, seqs)
        pltpu.make_async_copy(sent_ref.at[source], grads_ref.at[source], head_recv.at[source]).wait()
        return carry

    lax.fori_loop(1, seqs, grad_arrived, 0)

    def one(seq, carry):
        keep = (key_at <= query_at) & (key_at < len_ref[seq])
        weights = [p_ref[seq, 0], p_ref[seq, 1]]
        grad_mixed, made = [], [None] * 6
        grads = grads_ref[seq].astype(f32)
        for head in range(2):
            cols = slice(head * HP, (head + 1) * HP)
            out = o_ref[seq, :, cols]
            grad = jnp.concatenate([grads[:, head * DH : (head + 1) * DH], blank], axis=1)
            scale = lax.rsqrt(jnp.sum(out * out, axis=-1, keepdims=True) * (1.0 / DH) + eps_norm)
            unit = out * scale
            gain_grad_ref[:, cols] += jnp.sum(grad * unit, axis=0, keepdims=True)
            inner = grad * gain_ref[:, cols]
            grad_out = scale * (inner - unit * (jnp.sum(inner * unit, axis=-1, keepdims=True) * (1.0 / DH)))
            grad_out = grad_out.astype(bf16)
            value = qkv_ref[seq, :, (4 + head) * HP : (5 + head) * HP]
            mixed = (mix_ref[2 * head] * weights[0] + mix_ref[2 * head + 1] * weights[1]).astype(bf16)
            made[4 + head] = dot_tn(mixed, grad_out)
            back = dot_nt(grad_out, value)
            grad_mixed.append(back)
            for source in range(2):
                mixer_ref[2 * head + source : 2 * head + source + 1, :] += jnp.sum(
                    back * weights[source], axis=0, keepdims=True
                )
        for head in range(2):
            grad_weight = mix_ref[head] * grad_mixed[0] + mix_ref[2 + head] * grad_mixed[1]
            weight = weights[head]
            grad_conv = weight * (grad_weight - jnp.sum(weight * grad_weight, axis=-1, keepdims=True))
            wide = shifted_up(pad_ref, grad_conv).astype(bf16)
            theta_ref[head] += dot_tn(s_ref[seq, head], wide)
            grad_scores = jnp.zeros((rows, rows), f32)
            for lag in range(CQ):
                grad_scores += dot_nt(
                    wide[:, lag * rows : (lag + 1) * rows], toep_ref[head, lag * rows : (lag + 1) * rows, :]
                )
            grad_scores = jnp.where(keep, grad_scores * (1.0 / math.sqrt(DH)), 0.0).astype(bf16)
            query = qkv_ref[seq, :, head * HP : (head + 1) * HP]
            key = qkv_ref[seq, :, (2 + head) * HP : (3 + head) * HP]
            made[head] = dot(grad_scores, key)
            made[2 + head] = dot_tn(grad_scores, query)
        dqkv_ref[seq] = jnp.concatenate([part[:, :DH] for part in made], axis=1).astype(bf16)
        return carry

    lax.fori_loop(0, 4, one, 0)
    gather.onward()
    scatter.drain()

    def outputs(at, carry):
        two = pl.ds(at * 2, 2)
        made = dot(inner_ref[two].reshape(2 * rows, BLK), w_dn_ref[...])
        parts_ref[two] = made.astype(bf16).reshape(2, rows, D)
        return carry

    lax.fori_loop(0, seqs // 2, outputs, 0)
    scatter2 = Scatter(parts_ref, near2, in22, in32, *scatter_args[3:5], *scatter2_sems)
    scatter2.start()
    lax.fori_loop(4, seqs, one, 0)
    scatter2.onward()
    gather.last()
    gather.finish()
    strip_local.wait()
    for copy in strips_sent:
        copy.wait_recv()
    strips = strips_in[...].reshape(seqs * rows, 2 * DH)

    def out_grad(col, carry):
        cols = pl.ds(pl.multiple_of(col * BLK, BLK), BLK)
        go_ref[:, cols] = dot_tn(strips, all_ref[:, :, cols].reshape(seqs * rows, BLK)).astype(bf16)
        return carry

    lax.fori_loop(0, ROW_TILES, out_grad, 0)
    scatter2.last()
    for part in range(2):
        here = pl.ds(part * half, half)
        layer_ref[here] = (hmid_ref[here] + scatter2.finish(part)).astype(bf16)
    for copy in tiles_sent:
        copy.wait_recv()

    def sum_tiles(chip, carry):
        for row in range(ROW_TILES):
            made = (in_gu[chip, row].astype(f32) + in_gu[CHIPS + chip, row].astype(f32)).astype(bf16)
            tiles_ref[row * FF_TILES + chip] = made[:, :BLK]
            tiles_ref[(ROW_TILES + row) * FF_TILES + chip] = made[:, BLK:]
        made = (in_d[chip].astype(f32) + in_d[CHIPS + chip].astype(f32)).astype(bf16)
        for col in range(ROW_TILES):
            tiles_ref[2 * ROW_TILES * FF_TILES + chip * ROW_TILES + col] = made[:, col * BLK : (col + 1) * BLK]
        return carry

    lax.fori_loop(0, CHIPS, sum_tiles, 0)

    def grad_left(step, carry):
        grad_copy(lax.rem(me + step, seqs)).wait_send()
        return carry

    lax.fori_loop(1, seqs, grad_left, 0)
    gather.drain()
    scatter2.drain()
    for copy in strips_sent + to_core + tiles_sent:
        copy.wait_send()


def chip_at(mask):
    return {axis: 1 - lax.axis_index(axis) for axis in BITS if mask & BITS[axis]}


def run_middle(
    lengths, mix, hn, w_in, w_dn, dy, dy_own, hmid, gain_ffn, w_o, qkv, toep, gain, scores, weights, outs, strips
):
    seqs, rows, _ = hn.shape
    dma = pltpu.SemaphoreType.DMA
    part = BLK // 32
    shapes = [
        ((rows, D), bf16), ((rows, D), f32), ((1, D), f32), ((seqs, rows, 6 * DH), bf16), ((2, rows, CQ * rows), f32),
        ((8, rows), f32), ((1, 2 * HP), f32), ((2 * DH, D), bf16), ((9 * CHIPS, part, BLK), bf16),
    ]
    three = pltpu.VMEM((3, rows, D), bf16)
    one = pltpu.VMEM((rows, D), bf16)
    every = pltpu.VMEM((CHIPS, rows, D), bf16)
    heads = pltpu.VMEM((CHIPS, rows, 2 * DH), bf16)
    return pl.pallas_call(
        middle_body,
        in_specs=[SMEM, SMEM] + [VMEM] * 15,
        out_specs=[VMEM] * len(shapes),
        out_shape=[jax.ShapeDtypeStruct(*shape) for shape in shapes],
        scratch_shapes=[
            pltpu.VMEM((rows + 8, rows), f32), pltpu.VMEM((seqs, rows, BLK), bf16), pltpu.VMEM((seqs, rows, 2 * BLK), bf16),
            every, one, every, heads, heads, heads,
            pltpu.VMEM((ROW_TILES, 2, CHIPS, 2, part, 2 * BLK), bf16), pltpu.VMEM((2, CHIPS, 2, part, D), bf16),
            pltpu.VMEM((ROW_TILES, CHIPS, 2, part, 2 * BLK), bf16), pltpu.VMEM((CHIPS, 2, part, D), bf16),
            pltpu.VMEM((2 * CHIPS, ROW_TILES, part, 2 * BLK), bf16), pltpu.VMEM((2 * CHIPS, part, D), bf16),
            three, one, three, dma((1,)),
        ] + [dma((8,))] * 4 + [dma((2,))] * 2 + [dma((16,))] * 4
        + scatter_scratch(rows, D) + [dma((3,))] * 2 + [dma((3, 2))] * 4 + side_sems(),
        name="middle",
        compiler_params=pltpu.CompilerParams(collective_id=3, has_side_effects=True, vmem_limit_bytes=61 * 2**20),
    )(lengths, mix, hn, w_in, w_dn, dy, dy_own, hmid, gain_ffn, w_o, qkv, toep, gain, scores, weights, outs, strips)


def share_body(
    parts_ref, gq_ref, go_ref, dxn_ref, qkv_ref, out_ref,
    core_q, core_o, in_q, in_o, core_send, core_recv, send, recv, go_send, go_recv, *scatter_args,
):
    g, a, b, c, y = (lax.axis_index(axis) for axis in ALL)
    me = chip_index()
    barrier = pltpu.get_barrier_semaphore()
    pl.semaphore_signal(barrier, inc=1, device_id=across("c"))
    for mask in range(1, 16):
        pl.semaphore_signal(barrier, inc=1, device_id=wide_at(mask))
    pl.semaphore_wait(barrier, 16)
    to_core = [
        push(gq_ref.at[:, 1 - c], core_q, core_send.at[0], core_recv.at[0], across("c")),
        push(go_ref.at[:, 1 - c], core_o, core_send.at[1], core_recv.at[1], across("c")),
    ]
    scatter = Scatter(parts_ref, *scatter_args)
    scatter.start()
    to_core[0].wait_recv()
    for row in range(ROW_TILES):
        core_q[row] = (core_q[row].astype(f32) + gq_ref[row, c].astype(f32)).astype(bf16)
    slot = g * CHIPS + me
    sent = []
    for mask in (15, 14, 13, 11, 12, 10, 9, 8, 7, 6, 5, 3, 4, 2, 1):
        to = flipped(me, [axis for axis in BITS if mask & BITS[axis]])
        sent.append(
            push(
                core_q.at[:, to, other_bit("g", mask & 8)], in_q.at[slot], send.at[mask], recv.at[mask], wide_at(mask)
            )
        )
    to_core[1].wait_recv()
    core_o[...] = (core_o[...].astype(f32) + go_ref[:, c].astype(f32)).astype(bf16)
    to_group = push(core_o.at[:, 1 - g], in_o, go_send, go_recv, across("g"))
    in_q[slot] = core_q[:, me, g]
    scatter.onward()
    scatter.last()
    dxn_ref[0 : dxn_ref.shape[0] // 2] = scatter.finish(0)
    dxn_ref[dxn_ref.shape[0] // 2 :] = scatter.finish(1)
    to_group.wait_recv()
    out_ref[...] = (in_o[...].astype(f32) + core_o[:, g].astype(f32)).astype(bf16)
    for copy in sent:
        copy.wait_recv()
    for row in range(ROW_TILES):
        sums = [in_q[chip, row].astype(f32) + in_q[CHIPS + chip, row].astype(f32) for chip in range(CHIPS)]
        for which in range(3):
            qkv_ref[which, row] = jnp.concatenate(
                [part[:, which * 2 * DH : (which + 1) * 2 * DH] for part in sums], axis=1
            ).astype(bf16)
    scatter.drain()
    for copy in to_core + sent + [to_group]:
        copy.wait_send()


def wide_at(mask):
    at = chip_at(mask & 7)
    if mask & 8:
        at["g"] = 1 - lax.axis_index("g")
    return at


def share(parts, gq, go):
    _, rows, width = parts.shape
    dma = pltpu.SemaphoreType.DMA
    part = gq.shape[-2]
    return pl.pallas_call(
        share_body,
        in_specs=[VMEM] * 3,
        out_specs=[VMEM] * 3,
        out_shape=[
            jax.ShapeDtypeStruct((rows, width), f32),
            jax.ShapeDtypeStruct((3, ROW_TILES, part, D), bf16),
            jax.ShapeDtypeStruct((ROW_TILES, part, D), bf16),
        ],
        scratch_shapes=[
            pltpu.VMEM((ROW_TILES, CHIPS, 2, part, 6 * DH), bf16), pltpu.VMEM((ROW_TILES, 2, part, D), bf16),
            pltpu.VMEM((2 * CHIPS, ROW_TILES, part, 6 * DH), bf16), pltpu.VMEM((ROW_TILES, part, D), bf16),
            dma((2,)), dma((2,)), dma((16,)), dma((16,)), dma, dma,
        ] + scatter_scratch(rows, width),
        name="share_gradients",
        compiler_params=pltpu.CompilerParams(collective_id=5, has_side_effects=True, vmem_limit_bytes=40 * 2**20),
    )(parts, gq, go)


def to_slots_body(slots_ref, vec_ref, out_ref, vecs_ref, local_sems, send, recv, vec_send, vec_recv):
    devices = lax.axis_size(ALL)
    me = device_index()
    local = [
        pltpu.make_async_copy(slots_ref.at[me], out_ref.at[me], local_sems.at[0]),
        pltpu.make_async_copy(vec_ref.at[me], vecs_ref.at[me], local_sems.at[1]),
    ]
    for copy in local:
        copy.start()
    greet_all()

    def push_all(step, carry):
        to = lax.rem(me + step, devices)
        pltpu.make_async_remote_copy(
            src_ref=vec_ref.at[to], dst_ref=vecs_ref.at[me], send_sem=vec_send, recv_sem=vec_recv, device_id=device_at(to)
        ).start()
        pltpu.make_async_remote_copy(
            src_ref=slots_ref.at[to], dst_ref=out_ref.at[me], send_sem=send, recv_sem=recv, device_id=device_at(to)
        ).start()
        return carry

    lax.fori_loop(1, devices, push_all, 0)
    for ref, one, two in ((vecs_ref, vec_send, vec_recv), (out_ref, send, recv)):
        others = ref.at[pl.ds(0, devices - 1)]
        pltpu.make_async_copy(others, others, two).wait()
        pltpu.make_async_copy(others, others, one).wait()
    for copy in local:
        copy.wait()


def to_slots(slots, vecs):
    dma = pltpu.SemaphoreType.DMA
    return pl.pallas_call(
        to_slots_body,
        in_specs=[ANYS] * 2,
        out_specs=[ANYS] * 2,
        out_shape=[jax.ShapeDtypeStruct(slots.shape, slots.dtype), jax.ShapeDtypeStruct(vecs.shape, vecs.dtype)],
        scratch_shapes=[dma((2,))] + [dma] * 4,
        name="to_slots",
        compiler_params=pltpu.CompilerParams(collective_id=6, has_side_effects=True),
    )(slots, vecs)


def body_fast(
    layer_input, lengths, cotangent, w_query, w_key, w_value, w_out, w_gate, w_up, w_down, vec_copy, owners,
    basis_left, basis_right, block_master, block_first, block_second, vec_master, vec_first, vec_second,
):
    chip = chip_index()
    seq_len = layer_input.shape[0]
    length = lengths[0]
    own_vec = vec_copy.shape[0]
    devices, fs_size, reps = lax.axis_size(ALL), lax.axis_size(FS), lax.axis_size("y")

    small = jnp.concatenate(
        [vec_copy.astype(f32), jnp.zeros((1023 - own_vec,), f32), length.astype(f32).reshape(1)]
    ).reshape(8, 128)
    blocks = jnp.concatenate([w.reshape(-1, CHIPS, 2 * DH) for w in (w_query, w_key, w_value)], axis=2)
    x_all, small_all, w_qkv, w_out_all = dispatch(layer_input, small, jnp.transpose(blocks, (1, 0, 2)), w_out)
    w_qkv = w_qkv.reshape(D, 6 * DH)
    small_all = small_all.reshape(fs_size, reps, 1024)
    vector = small_all[:, 0, :own_vec].reshape(-1)
    group_lengths = small_all[:, :, 1023].reshape(-1, 2, 2, 2, reps)
    group_lengths = lax.dynamic_index_in_dim(group_lengths, lax.axis_index("g"), 0, keepdims=False)
    group_lengths = lax.dynamic_index_in_dim(group_lengths, lax.axis_index("c"), 2, keepdims=False)
    group_lengths = jnp.transpose(group_lengths, (2, 0, 1)).reshape(CHIPS).astype(jnp.int32)
    gain_attn, gain_head, gain_ffn = vector[:D], vector[D : 2 * D], vector[2 * D : 3 * D]
    conv_end = 3 * D + H * CQ * CK
    theta = lax.dynamic_slice_in_dim(vector[3 * D : conv_end].reshape(H, CQ, CK), chip * 2, 2, 0)
    mixer = lax.dynamic_slice_in_dim(vector[conv_end : conv_end + 2 * H].reshape(H, 2), chip * 2, 2, 0)
    mix = mixer.reshape(4)
    gain_pair = jnp.pad(
        lax.dynamic_slice_in_dim(gain_head.reshape(H, DH), chip * 2, 2, 0), ((0, 0), (0, HP - DH))
    ).reshape(1, 2 * HP)
    toep = jnp.zeros((2, CQ, seq_len, seq_len), f32)
    offset = (
        jnp.arange(seq_len, dtype=jnp.int32)[:, None] - jnp.arange(seq_len, dtype=jnp.int32)[None, :] + CK // 2
    )
    for tap in range(CK):
        toep = jnp.where(offset[None, None] == tap, theta[:, :, tap][:, :, None, None], toep)
    toep = toep.astype(bf16).reshape(2, CQ * seq_len, seq_len)
    valid = (jnp.arange(seq_len) < length).astype(f32)
    dy = cotangent.astype(f32) * valid[:, None]

    gains = jnp.concatenate([gain_attn[None], gain_ffn[None], jnp.zeros((6, D), f32)], axis=0)
    xn, qkv, scores, weights, outs, heads, hmid, hn_rows, w_in, w_dn, dy_rows = run_front(
        group_lengths, mix, x_all, layer_input, gains, w_qkv, toep, gain_pair, w_out_all, w_gate, w_up, w_down, dy.astype(bf16)
    )
    xn_rows = xn.reshape(CHIPS * seq_len, D)
    w_in, w_dn = w_in.reshape(D, 2 * BLK), w_dn.reshape(BLK, D)
    strip = BLK // (2 * CHIPS)
    part = strip // 2
    heads = jnp.transpose(heads, (1, 0, 2)).reshape(seq_len, 2 * ROW_TILES, CHIPS, strip)
    strips = jnp.transpose(heads, (2, 0, 1, 3)).reshape(CHIPS, seq_len, 2 * ROW_TILES * strip)
    input_float = layer_input.astype(f32)
    input_scale = rms(input_float)

    layer_output, dhmid, grad_gain_ffn, dqkv, theta_sums, mixer_sums, gain_sums, grad_out, ffn_sums = run_middle(
        group_lengths, mix, hn_rows, w_in, w_dn, dy_rows, dy.astype(bf16), hmid, gain_ffn.reshape(1, D),
        w_out_all.reshape(CHIPS, 2 * DH, D), qkv, toep, gain_pair, scores, weights, outs, strips,
    )
    dqkv_rows = dqkv.reshape(CHIPS * seq_len, 6 * DH)
    dxn_parts = dot_nt(dqkv_rows, w_qkv).astype(bf16).reshape(CHIPS, seq_len, D)
    grad_qkv = dot_tn(xn_rows, dqkv_rows).astype(bf16)
    dxn, qkv_sums, out_sums = share(
        dxn_parts,
        grad_qkv.reshape(ROW_TILES, 2, CHIPS, 2, part, 6 * DH),
        grad_out.reshape(ROW_TILES, 2, 2, part, D),
    )
    dinput, grad_gain_attn = norm_backward(input_float, input_scale, gain_attn, dxn)
    input_grad = dinput + dhmid

    taps = jnp.asarray(band())
    theta_sums = theta_sums.reshape(2, seq_len, CQ, seq_len)
    grad_theta = jnp.stack(
        [jnp.sum(jnp.where(taps[tap][None, :, None, :], theta_sums, 0.0), axis=(1, 3)) for tap in range(CK)], axis=2
    )
    grad_mixer = jnp.sum(mixer_sums[:4], axis=1)
    vector_grad = jnp.concatenate(
        [
            grad_gain_attn,
            lax.dynamic_update_slice_in_dim(
                jnp.zeros((D,), f32), gain_sums.reshape(2, HP)[:, :DH].reshape(-1), chip * 2 * DH, 0
            ),
            grad_gain_ffn.reshape(-1),
            lax.dynamic_update_slice_in_dim(
                jnp.zeros((H * CQ * CK,), f32), grad_theta.reshape(-1), chip * 2 * CQ * CK, 0
            ),
            lax.dynamic_update_slice_in_dim(jnp.zeros((2 * H,), f32), grad_mixer, chip * 4, 0),
        ]
    )
    pieces = jnp.pad(vector_grad.reshape(fs_size, 1, own_vec), ((0, 0), (0, 0), (0, 1024 - own_vec)))
    pieces = jnp.broadcast_to(pieces, (fs_size, reps, 1024)).reshape(devices, 8, 128)

    own_slots = basis_left.shape[0]
    slot_total = own_slots * devices
    sums = jnp.concatenate(
        [
            jnp.transpose(qkv_sums.reshape(3, ROW_TILES, part, ROW_TILES, BLK), (0, 1, 3, 2, 4)).reshape(-1, part, BLK),
            jnp.transpose(out_sums.reshape(ROW_TILES, part, ROW_TILES, BLK), (0, 2, 1, 3)).reshape(-1, part, BLK),
            ffn_sums,
        ],
        axis=0,
    )
    matches = (jnp.arange(slot_total)[:, None] == owners[None, :]).astype(bf16)
    slots = dot(matches, sums.reshape(sums.shape[0], -1)).astype(bf16)
    slots, pieces = to_slots(slots.reshape(devices, own_slots * part, BLK), pieces)
    vector_total = jnp.sum(pieces, axis=0).reshape(1024)[:own_vec]
    slots = slots.reshape(2, 2, 2, 2, 2, own_slots, part, BLK)
    own_grad = jnp.transpose(slots, (5, 3, 4, 1, 2, 0, 6, 7)).reshape(own_slots, BLK, BLK)

    left_low, right_low = basis_left.astype(bf16), basis_right.astype(bf16)
    rotated = jnp.einsum("sia,sij->saj", left_low, own_grad, preferred_element_type=f32)
    rotated = jnp.einsum("saj,sjb->sab", rotated.astype(bf16), right_low, preferred_element_type=f32)
    first_new = beta_first * block_first + (1.0 - beta_first) * rotated
    second_new = beta_second * block_second + (1.0 - beta_second) * rotated * rotated
    direction = (first_new / (jnp.sqrt(second_new) + eps_adam)).astype(bf16)
    turned = jnp.einsum("sia,sab->sib", left_low, direction, preferred_element_type=f32)
    turned = jnp.einsum("sib,sjb->sij", turned.astype(bf16), right_low, preferred_element_type=f32)
    master_new = block_master - rate_block * (turned + decay_block * block_master)
    vec_first_new = beta_first * vec_first + (1.0 - beta_first) * vector_total
    vec_second_new = beta_second * vec_second + (1.0 - beta_second) * vector_total * vector_total
    vec_master_new = vec_master - rate_vector * vec_first_new / (jnp.sqrt(vec_second_new) + eps_adam)
    return (
        layer_output, input_grad, first_new, second_new, master_new, master_new.astype(bf16),
        vec_first_new, vec_second_new, vec_master_new, vec_master_new.astype(bf16),
    )


def solution(mesh):
    fsdp, rep = mesh.shape["fsdp"], mesh.shape["rep"]
    fine = Mesh(mesh.devices.reshape(fsdp // 8, 2, 2, 2, rep), ALL)
    rows, both = P(ALL, None), P(ALL, None, None)
    weight, vec = P(FS, None), P(FS)
    return jax.shard_map(
        body_fast if (fsdp, rep) == (16, 2) else body_any,
        mesh=fine,
        in_specs=(rows, P(ALL), rows) + (weight,) * 7 + (vec, P()) + (both,) * 5 + (vec,) * 3,
        out_specs=(rows, rows) + (both,) * 4 + (vec,) * 4,
        check_vma=False,
    )
```

```python
import math

import jax
import jax.numpy as jnp
import numpy as np
from jax import lax
from jax.experimental import pallas as pl
from jax.experimental.pallas import tpu as pltpu
from jax.sharding import Mesh
from jax.sharding import PartitionSpec as P

H = 16
DH = 96
HP = 128
D = H * DH
FF = 4096
CQ = 6
CK = 11
BLK = 512
CHIPS = 8
ROW_TILES = D // BLK
FF_TILES = FF // BLK

eps_norm = 1e-05
eps_adam = 1e-08
rate_block = 0.02
rate_vector = 0.3
decay_block = 0.1
beta_first = 0.5
beta_second = 0.5

FS = ("g", "a", "b", "c")
CHIP = ("y", "a", "b")
ALL = ("g", "a", "b", "c", "y")
bf16 = jnp.bfloat16
f32 = jnp.float32


def dot(left, right):
    return jnp.dot(left, right, preferred_element_type=f32)


def dot_nt(left, right):
    return lax.dot_general(left, right, (((1,), (1,)), ((), ())), preferred_element_type=f32)


def dot_tn(left, right):
    return lax.dot_general(left, right, (((0,), (0,)), ((), ())), preferred_element_type=f32)


def rms(values):
    return lax.rsqrt(jnp.mean(values * values, axis=-1, keepdims=True) + eps_norm)


def norm_backward(values, scale, gain, grad):
    unit = values * scale
    inner = grad * gain
    grad_values = scale * (inner - unit * jnp.mean(inner * unit, axis=-1, keepdims=True))
    return grad_values, jnp.sum(grad * unit, axis=0)


def shifted_down(pad_ref, values):
    rows = values.shape[0]
    pad_ref[8 : 8 + rows, :] = values
    return jnp.concatenate(
        [values] + [pad_ref[8 - lag : 8 - lag + rows, :] for lag in range(1, CQ)], axis=1
    )


def shifted_up(pad_ref, values):
    rows = values.shape[0]
    pad_ref[0:rows, :] = values
    return jnp.concatenate(
        [values] + [pad_ref[lag : lag + rows, :] for lag in range(1, CQ)], axis=1
    )


def attention_forward(len_ref, mix_ref, qkv_ref, toep_ref, gain_ref, heads_ref, s_ref, p_ref, o_ref, pad_ref):
    rows = qkv_ref.shape[1]
    length = len_ref[pl.program_id(0)]
    query_at = lax.broadcasted_iota(jnp.int32, (rows, rows), 0)
    key_at = lax.broadcasted_iota(jnp.int32, (rows, rows), 1)
    keep = (key_at <= query_at) & (key_at < length)
    pad_ref[0:8, :] = jnp.zeros((8, rows), f32)
    weights = []
    for head in range(2):
        query = qkv_ref[0, :, head * HP : (head + 1) * HP]
        key = qkv_ref[0, :, (2 + head) * HP : (3 + head) * HP]
        scores = jnp.where(keep, dot_nt(query, key) * (1.0 / math.sqrt(DH)), 0.0)
        s_ref[0, head] = scores.astype(bf16)
        wide = shifted_down(pad_ref, scores)
        high = wide.astype(bf16)
        low = (wide - high.astype(f32)).astype(bf16)
        conv = dot(high, toep_ref[head]) + dot(low, toep_ref[head])
        logits = jnp.where(keep, conv, -1e30)
        weight = jnp.exp(logits - jnp.max(logits, axis=-1, keepdims=True))
        weight = weight / jnp.sum(weight, axis=-1, keepdims=True)
        p_ref[0, head] = weight
        weights.append(weight)
    for head in range(2):
        mixed = mix_ref[2 * head] * weights[0] + mix_ref[2 * head + 1] * weights[1]
        value = qkv_ref[0, :, (4 + head) * HP : (5 + head) * HP]
        out = dot(mixed.astype(bf16), value)
        o_ref[0, :, head * HP : (head + 1) * HP] = out
        scale = lax.rsqrt(jnp.sum(out * out, axis=-1, keepdims=True) * (1.0 / DH) + eps_norm)
        heads_ref[0, :, head * HP : (head + 1) * HP] = (
            out * scale * gain_ref[:, head * HP : (head + 1) * HP]
        ).astype(bf16)


def attention_backward(
    len_ref, mix_ref, qkv_ref, toep_ref, gain_ref, s_ref, p_ref, o_ref, grad_ref,
    dqkv_ref, theta_ref, mixer_ref, gain_grad_ref, pad_ref,
):
    rows = qkv_ref.shape[1]
    length = len_ref[pl.program_id(0)]
    query_at = lax.broadcasted_iota(jnp.int32, (rows, rows), 0)
    key_at = lax.broadcasted_iota(jnp.int32, (rows, rows), 1)
    keep = (key_at <= query_at) & (key_at < length)
    pad_ref[rows : rows + 8, :] = jnp.zeros((8, rows), f32)

    @pl.when(pl.program_id(0) == 0)
    def _():
        theta_ref[...] = jnp.zeros_like(theta_ref)
        mixer_ref[...] = jnp.zeros_like(mixer_ref)
        gain_grad_ref[...] = jnp.zeros_like(gain_grad_ref)

    weights = [p_ref[0, 0], p_ref[0, 1]]
    grad_mixed = []
    for head in range(2):
        cols = slice(head * HP, (head + 1) * HP)
        out = o_ref[0, :, cols]
        grad = grad_ref[0, :, cols].astype(f32)
        scale = lax.rsqrt(jnp.sum(out * out, axis=-1, keepdims=True) * (1.0 / DH) + eps_norm)
        unit = out * scale
        gain_grad_ref[:, cols] += jnp.sum(grad * unit, axis=0, keepdims=True)
        inner = grad * gain_ref[:, cols]
        grad_out = scale * (inner - unit * (jnp.sum(inner * unit, axis=-1, keepdims=True) * (1.0 / DH)))
        grad_out = grad_out.astype(bf16)
        value = qkv_ref[0, :, (4 + head) * HP : (5 + head) * HP]
        mixed = (mix_ref[2 * head] * weights[0] + mix_ref[2 * head + 1] * weights[1]).astype(bf16)
        dqkv_ref[0, :, (4 + head) * HP : (5 + head) * HP] = dot_tn(mixed, grad_out).astype(bf16)
        back = dot_nt(grad_out, value)
        grad_mixed.append(back)
        for source in range(2):
            mixer_ref[2 * head + source : 2 * head + source + 1, :] += jnp.sum(
                back * weights[source], axis=0, keepdims=True
            )
    for head in range(2):
        grad_weight = mix_ref[head] * grad_mixed[0] + mix_ref[2 + head] * grad_mixed[1]
        weight = weights[head]
        grad_conv = weight * (grad_weight - jnp.sum(weight * grad_weight, axis=-1, keepdims=True))
        wide = shifted_up(pad_ref, grad_conv).astype(bf16)
        theta_ref[head] += dot_tn(s_ref[0, head], wide)
        grad_scores = jnp.zeros((rows, rows), f32)
        for lag in range(CQ):
            grad_scores += dot_nt(
                wide[:, lag * rows : (lag + 1) * rows], toep_ref[head, lag * rows : (lag + 1) * rows, :]
            )
        grad_scores = jnp.where(keep, grad_scores * (1.0 / math.sqrt(DH)), 0.0).astype(bf16)
        query = qkv_ref[0, :, head * HP : (head + 1) * HP]
        key = qkv_ref[0, :, (2 + head) * HP : (3 + head) * HP]
        dqkv_ref[0, :, head * HP : (head + 1) * HP] = dot(grad_scores, key).astype(bf16)
        dqkv_ref[0, :, (2 + head) * HP : (3 + head) * HP] = dot_tn(grad_scores, query).astype(bf16)


SMEM = pl.BlockSpec(memory_space=pltpu.SMEM)


def seq_spec(*dims):
    return pl.BlockSpec((1,) + dims, lambda s: (s,) + (0,) * len(dims))


def whole_spec(*dims):
    return pl.BlockSpec(dims, lambda s: (0,) * len(dims))


def run_forward(lengths, mix, qkv, toep, gain):
    seqs, rows, _ = qkv.shape
    return pl.pallas_call(
        attention_forward,
        grid=(seqs,),
        in_specs=[SMEM, SMEM, seq_spec(rows, 6 * HP), whole_spec(2, CQ * rows, rows), whole_spec(1, 2 * HP)],
        out_specs=[seq_spec(rows, 2 * HP), seq_spec(2, rows, rows), seq_spec(2, rows, rows), seq_spec(rows, 2 * HP)],
        out_shape=[
            jax.ShapeDtypeStruct((seqs, rows, 2 * HP), bf16),
            jax.ShapeDtypeStruct((seqs, 2, rows, rows), bf16),
            jax.ShapeDtypeStruct((seqs, 2, rows, rows), f32),
            jax.ShapeDtypeStruct((seqs, rows, 2 * HP), f32),
        ],
        scratch_shapes=[pltpu.VMEM((rows + 8, rows), f32)],
        name="attention_forward",
        compiler_params=pltpu.CompilerParams(vmem_limit_bytes=24 * 2**20),
        cost_estimate=pl.CostEstimate(flops=2 * 10**9, bytes_accessed=8 * 2**20, transcendentals=10**5),
    )(lengths, mix, qkv, toep, gain)


def run_backward(lengths, mix, qkv, toep, gain, scores, weights, outs, grads):
    seqs, rows, _ = qkv.shape
    return pl.pallas_call(
        attention_backward,
        grid=(seqs,),
        in_specs=[
            SMEM, SMEM, seq_spec(rows, 6 * HP), whole_spec(2, CQ * rows, rows), whole_spec(1, 2 * HP),
            seq_spec(2, rows, rows), seq_spec(2, rows, rows), seq_spec(rows, 2 * HP), seq_spec(rows, 2 * HP),
        ],
        out_specs=[seq_spec(rows, 6 * HP), whole_spec(2, rows, CQ * rows), whole_spec(8, rows), whole_spec(1, 2 * HP)],
        out_shape=[
            jax.ShapeDtypeStruct((seqs, rows, 6 * HP), bf16),
            jax.ShapeDtypeStruct((2, rows, CQ * rows), f32),
            jax.ShapeDtypeStruct((8, rows), f32),
            jax.ShapeDtypeStruct((1, 2 * HP), f32),
        ],
        scratch_shapes=[pltpu.VMEM((rows + 8, rows), f32)],
        name="attention_backward",
        compiler_params=pltpu.CompilerParams(vmem_limit_bytes=24 * 2**20),
        cost_estimate=pl.CostEstimate(flops=4 * 10**9, bytes_accessed=12 * 2**20, transcendentals=10**5),
    )(lengths, mix, qkv, toep, gain, scores, weights, outs, grads)


BITS = {"y": 4, "a": 2, "b": 1}
HOPS = (("y", "b", "a"), ("a", "y", "b"), ("b", "a", "y"))
THIRDS = ((0, 48), (48, 48), (96, 32))
ANYS = pl.BlockSpec(memory_space=pl.ANY)


def chip_index():
    return (lax.axis_index("y") * 2 + lax.axis_index("a")) * 2 + lax.axis_index("b")


def flipped(chip, axes):
    for axis in axes:
        chip = chip + BITS[axis] * (1 - 2 * lax.axis_index(axis))
    return chip


def across(axis):
    return {axis: 1 - lax.axis_index(axis)}


def device_index():
    index = lax.axis_index("g")
    for axis in ("a", "b", "c", "y"):
        index = index * lax.axis_size(axis) + lax.axis_index(axis)
    return index


def device_at(index):
    at = {}
    for axis in ("y", "c", "b", "a", "g"):
        at[axis] = lax.rem(index, lax.axis_size(axis))
        index = lax.div(index, lax.axis_size(axis))
    return at


def greet_all():
    devices = lax.axis_size(ALL)
    me = device_index()
    barrier = pltpu.get_barrier_semaphore()

    def greet(step, carry):
        pl.semaphore_signal(barrier, inc=1, device_id=device_at(lax.rem(me + step, devices)))
        return carry

    lax.fori_loop(1, devices, greet, 0)
    pl.semaphore_wait(barrier, devices - 1)


def greet_neighbours():
    barrier = pltpu.get_barrier_semaphore()
    for axis in BITS:
        pl.semaphore_signal(barrier, inc=1, device_id=across(axis))
    pl.semaphore_wait(barrier, 3)


def remote(src, dst, send, recv, axis):
    return pltpu.make_async_remote_copy(src_ref=src, dst_ref=dst, send_sem=send, recv_sem=recv, device_id=across(axis))


def gather_body(x_ref, out_ref, *sems):
    greet_neighbours()
    gather_hops(x_ref, out_ref, *sems)


def gather_first_body(x_ref, vec_ref, out_ref, vecs_ref, vec_send, vec_recv, vec_local, *sems):
    devices = lax.axis_size(ALL)
    me = device_index()
    local = pltpu.make_async_copy(vec_ref, vecs_ref.at[me], vec_local)
    local.start()
    greet_all()

    def push(step, carry):
        pltpu.make_async_remote_copy(
            src_ref=vec_ref, dst_ref=vecs_ref.at[me], send_sem=vec_send, recv_sem=vec_recv,
            device_id=device_at(lax.rem(me + step, devices)),
        ).start()
        return carry

    lax.fori_loop(1, devices, push, 0)
    gather_hops(x_ref, out_ref, *sems)
    others = vecs_ref.at[pl.ds(0, devices - 1)]
    pltpu.make_async_copy(others, others, vec_recv).wait()
    pltpu.make_async_copy(others, others, vec_send).wait()
    local.wait()


def gather_hops(x_ref, out_ref, local_sem, send1, recv1, send2, recv2, send3, recv3):
    me = chip_index()
    rows = x_ref.shape[0]
    half = rows // 2
    local = pltpu.make_async_copy(x_ref, out_ref.at[me], local_sem)
    local.start()
    first = []
    for part in range(2):
        here = pl.ds(part * half, half)
        for at, (axis, _, _) in enumerate(HOPS):
            copy = remote(x_ref.at[here], out_ref.at[me, here], send1.at[at, part], recv1.at[at, part], axis)
            copy.start()
            first.append(copy)
    second = []
    for part in range(2):
        here = pl.ds(part * half, half)
        for at, (axis, onward, _) in enumerate(HOPS):
            first[part * 3 + at].wait_recv()
            block = out_ref.at[flipped(me, (axis,)), here]
            copy = remote(block, block, send2.at[at, part], recv2.at[at, part], onward)
            copy.start()
            second.append(copy)
    third = []
    for at, (axis, onward, last) in enumerate(HOPS):
        begin, count = THIRDS[at]
        block = flipped(me, (axis, onward))
        for part in range(2):
            if part * half < begin + count and begin < (part + 1) * half:
                second[part * 3 + at].wait_recv()
        piece = out_ref.at[block, pl.ds(begin, count)]
        copy = remote(piece, piece, send3.at[at], recv3.at[at], last)
        copy.start()
        third.append(copy)
    for at in range(3):
        begin, count = THIRDS[at]
        for part in range(2):
            if not (part * half < begin + count and begin < (part + 1) * half):
                second[part * 3 + at].wait_recv()
    for copy in third:
        copy.wait_recv()
    for copy in first + second + third:
        copy.wait_send()
    local.wait()


def hop_sems():
    dma = pltpu.SemaphoreType.DMA
    return [dma] + [dma((3, 2))] * 4 + [dma((3,))] * 2


def gather_first(rows, vec, collective_id):
    count, width = rows.shape
    return pl.pallas_call(
        gather_first_body,
        in_specs=[ANYS, ANYS],
        out_specs=[ANYS, ANYS],
        out_shape=[
            jax.ShapeDtypeStruct((CHIPS, count, width), rows.dtype),
            jax.ShapeDtypeStruct((lax.axis_size(ALL),) + vec.shape, vec.dtype),
        ],
        scratch_shapes=[pltpu.SemaphoreType.DMA] * 3 + hop_sems(),
        name="gather_first",
        compiler_params=pltpu.CompilerParams(collective_id=collective_id, has_side_effects=True),
    )(rows, vec)


def gather_chips(rows, collective_id):
    count, width = rows.shape
    return pl.pallas_call(
        gather_body,
        in_specs=[ANYS],
        out_specs=ANYS,
        out_shape=jax.ShapeDtypeStruct((CHIPS, count, width), rows.dtype),
        scratch_shapes=hop_sems(),
        name="gather_chips",
        compiler_params=pltpu.CompilerParams(collective_id=collective_id, has_side_effects=True),
    )(rows)


def scatter_body(
    parts_ref, out_ref, near_ref, in2_ref, in3_ref, acc2_ref, acc3_ref, send1, recv1, send2, recv2, send3, recv3
):
    me = chip_index()
    greet_neighbours()
    opposite = flipped(me, ("y", "a", "b"))
    first = []
    for at, (axis, onward, last) in enumerate(HOPS):
        begin, count = THIRDS[at]
        copy = remote(parts_ref.at[opposite, pl.ds(begin, count)], in2_ref.at[pl.ds(begin, count)], send1.at[at], recv1.at[at], last)
        copy.start()
        first.append(copy)
    second = []
    rows = parts_ref.shape[1]
    half = rows // 2
    for part in range(2):
        here = pl.ds(part * half, half)
        for at, (axis, onward, last) in enumerate(HOPS):
            dest = flipped(me, (axis, onward))
            begin, count = THIRDS[at]
            if part == 0:
                first[at].wait_recv()
                acc2_ref[at] = parts_ref[dest]
                piece = pl.ds(begin, count)
                acc2_ref[at, piece] = (parts_ref[dest, piece].astype(f32) + in2_ref[piece].astype(f32)).astype(bf16)
            copy = remote(acc2_ref.at[at, here], in3_ref.at[at, here], send2.at[at, part], recv2.at[at, part], onward)
            copy.start()
            second.append(copy)
    third = []
    for part in range(2):
        here = pl.ds(part * half, half)
        for at, (axis, onward, last) in enumerate(HOPS):
            dest = flipped(me, (axis,))
            second[part * 3 + at].wait_recv()
            acc3_ref[at, here] = (parts_ref[dest, here].astype(f32) + in3_ref[at, here].astype(f32)).astype(bf16)
            copy = remote(acc3_ref.at[at, here], near_ref.at[at, here], send3.at[at, part], recv3.at[at, part], axis)
            copy.start()
            third.append(copy)
    for part in range(2):
        here = pl.ds(part * half, half)
        for at in range(3):
            third[part * 3 + at].wait_recv()
        out_ref[here] = (
            (parts_ref[me, here].astype(f32) + near_ref[0, here].astype(f32))
            + (near_ref[1, here].astype(f32) + near_ref[2, here].astype(f32))
        )
    for copy in first + second + third:
        copy.wait_send()


def scatter_chips(parts, collective_id):
    _, rows, width = parts.shape
    vmem = pl.BlockSpec(memory_space=pltpu.VMEM)
    dma = pltpu.SemaphoreType.DMA
    return pl.pallas_call(
        scatter_body,
        in_specs=[vmem],
        out_specs=vmem,
        out_shape=jax.ShapeDtypeStruct((rows, width), f32),
        scratch_shapes=[pltpu.VMEM((3, rows, width), bf16), pltpu.VMEM((rows, width), bf16)] + [pltpu.VMEM((3, rows, width), bf16)] * 3
        + [dma((3,))] * 2 + [dma((3, 2))] * 4,
        name="scatter_chips",
        compiler_params=pltpu.CompilerParams(collective_id=collective_id, has_side_effects=True, vmem_limit_bytes=32*2**20),
    )(parts)


def gather_slow(rows):
    return lax.all_to_all(
        jnp.broadcast_to(rows[None], (CHIPS,) + rows.shape), CHIP, split_axis=0, concat_axis=0, tiled=True
    )


def exchange_chips(parts):
    return lax.all_to_all(parts, CHIP, split_axis=0, concat_axis=0, tiled=True)


def scatter_slow(parts):
    return jnp.sum(exchange_chips(parts.astype(bf16)).astype(f32), axis=0)


def swap(values, axis):
    return lax.ppermute(values, axis, [(0, 1), (1, 0)])


def both_cores(own, axis):
    other = swap(own, "c")
    first = lax.axis_index("c") == 0
    return jnp.stack([jnp.where(first, own, other), jnp.where(first, other, own)], axis=axis)


def half_for_core(values, axis):
    core = lax.axis_index("c")
    own = lax.dynamic_index_in_dim(values, core, axis, keepdims=False)
    sent = lax.dynamic_index_in_dim(values, 1 - core, axis, keepdims=False)
    return own + swap(sent.astype(bf16), "c").astype(f32)


def sum_groups(tiles):
    groups = lax.axis_size("g")
    if groups != 2:
        return lax.psum_scatter(tiles.astype(f32), "g", scatter_dimension=1, tiled=True).astype(bf16)
    part = tiles.shape[1] // 2
    group = lax.axis_index("g")
    own = lax.dynamic_slice_in_dim(tiles, group * part, part, 1)
    sent = lax.dynamic_slice_in_dim(tiles, (1 - group) * part, part, 1)
    return (own.astype(f32) + swap(sent, "g").astype(f32)).astype(bf16)


def spread_columns(weight, width):
    rows = weight.shape[0]
    blocks = weight.reshape(rows, 2, CHIPS // 2, width)
    mine = lax.dynamic_index_in_dim(blocks, lax.axis_index("y"), 1, keepdims=False)
    return jnp.transpose(mine, (1, 0, 2))


def to_columns(blocks):
    groups = lax.axis_size("g")
    sent = jnp.broadcast_to(blocks[None], (groups,) + blocks.shape).reshape((-1,) + blocks.shape[1:])
    got = lax.all_to_all(sent, ("g", "a", "b"), split_axis=0, concat_axis=0, tiled=True)
    return both_cores(got, 1).reshape(-1, blocks.shape[-1])


def down_rows(w_down, chip):
    if lax.axis_size("g") == 2:
        other = swap(w_down, "g")
        mine = jnp.where(lax.axis_index("g") == lax.axis_index("y"), w_down, other)
        return both_cores(mine, 0).reshape(BLK, D)
    return lax.dynamic_slice_in_dim(lax.all_gather(w_down, FS, axis=0, tiled=True), chip * BLK, BLK, 0)


def band():
    tap = np.arange(CK)[:, None, None]
    source = np.arange(128)[None, :, None]
    target = np.arange(128)[None, None, :]
    return source - target + CK // 2 == tap


def body_any(
    layer_input, lengths, cotangent, w_query, w_key, w_value, w_out, w_gate, w_up, w_down, vec_copy, owners,
    basis_left, basis_right, block_master, block_first, block_second, vec_master, vec_first, vec_second,
):
    chip = (lax.axis_index("y") * 2 + lax.axis_index("a")) * 2 + lax.axis_index("b")
    fs_index = ((lax.axis_index("g") * 2 + lax.axis_index("a")) * 2 + lax.axis_index("b")) * 2 + lax.axis_index("c")
    seq_len = layer_input.shape[0]
    length = lengths[0]
    reps = lax.axis_size("y")
    fs_size = lax.axis_size(FS)

    own_vec = vec_copy.shape[0]
    small = jnp.concatenate(
        [vec_copy.astype(f32), jnp.zeros((1023 - own_vec,), f32), length.astype(f32).reshape(1)]
    ).reshape(8, 128)
    x_all, small_all = gather_first(layer_input, small, 1)
    small_all = small_all.reshape(fs_size, reps, 1024)
    vector = small_all[:, 0, :own_vec].reshape(-1)
    group_lengths = small_all[:, :, 1023].reshape(-1, 2, 2, 2, reps)
    group_lengths = lax.dynamic_index_in_dim(group_lengths, lax.axis_index("g"), 0, keepdims=False)
    group_lengths = lax.dynamic_index_in_dim(group_lengths, lax.axis_index("c"), 2, keepdims=False)
    group_lengths = jnp.transpose(group_lengths, (2, 0, 1)).reshape(CHIPS).astype(jnp.int32)
    gain_attn, gain_head, gain_ffn = vector[:D], vector[D : 2 * D], vector[2 * D : 3 * D]
    conv_end = 3 * D + H * CQ * CK
    theta = lax.dynamic_slice_in_dim(vector[3 * D : conv_end].reshape(H, CQ, CK), chip * 2, 2, 0)
    mixer = lax.dynamic_slice_in_dim(vector[conv_end : conv_end + 2 * H].reshape(H, 2), chip * 2, 2, 0)
    mix = mixer.reshape(4)
    gain_pair = jnp.pad(
        lax.dynamic_slice_in_dim(gain_head.reshape(H, DH), chip * 2, 2, 0), ((0, 0), (0, HP - DH))
    ).reshape(1, 2 * HP)
    toep = jnp.zeros((2, CQ, seq_len, seq_len), f32)
    offset = (
        jnp.arange(seq_len, dtype=jnp.int32)[:, None] - jnp.arange(seq_len, dtype=jnp.int32)[None, :] + CK // 2
    )
    for tap in range(CK):
        toep = jnp.where(offset[None, None] == tap, theta[:, :, tap][:, :, None, None], toep)
    toep = toep.astype(bf16).reshape(2, CQ * seq_len, seq_len)

    qkv_rows = to_columns(
        jnp.concatenate([spread_columns(w, 2 * DH) for w in (w_query, w_key, w_value)], axis=2)
    )
    w_qkv = jnp.pad(qkv_rows.reshape(D, 6, DH), ((0, 0), (0, 0), (0, HP - DH))).reshape(D, 6 * HP)
    w_in = to_columns(jnp.concatenate([spread_columns(w, BLK) for w in (w_gate, w_up)], axis=2))
    w_dn = down_rows(w_down, chip)
    w_o = lax.all_gather(w_out, FS, axis=0, tiled=True)

    input_float = layer_input.astype(f32)
    input_scale = rms(input_float)
    x_rows = x_all.reshape(CHIPS * seq_len, D).astype(f32)
    xn_rows = (x_rows * rms(x_rows) * gain_attn).astype(bf16)
    qkv = dot(xn_rows, w_qkv).astype(bf16).reshape(CHIPS, seq_len, 6 * HP)
    heads_pad, scores, weights, outs = run_forward(group_lengths, mix, qkv, toep, gain_pair)
    heads_sent = heads_pad.reshape(CHIPS, seq_len, 2, HP)[..., :DH].reshape(CHIPS, seq_len, 2 * DH)
    heads = jnp.transpose(exchange_chips(heads_sent), (1, 0, 2)).reshape(seq_len, D)
    hmid = input_float + dot(heads, w_o)
    hmid_scale = rms(hmid)
    hn_rows = gather_chips((hmid * hmid_scale * gain_ffn).astype(bf16), 2).reshape(CHIPS * seq_len, D)
    both = dot(hn_rows, w_in)
    gate, up = both[:, :BLK], both[:, BLK:]
    sig = jax.nn.sigmoid(gate)
    silu = gate * sig
    inner = (silu * up).astype(bf16)
    ffn = scatter_slow(dot(inner, w_dn).reshape(CHIPS, seq_len, D))
    layer_output = (hmid + ffn).astype(bf16)

    valid = (jnp.arange(seq_len) < length).astype(f32)
    dy = cotangent.astype(f32) * valid[:, None]
    dy_rows = gather_slow(dy.astype(bf16)).reshape(CHIPS * seq_len, D)
    dinner = dot_nt(dy_rows, w_dn)
    dgate = (dinner * up * (sig * (1.0 + gate * (1.0 - sig)))).astype(bf16)
    dup = (dinner * silu).astype(bf16)
    dboth = jnp.concatenate([dgate, dup], axis=1)
    dhn = scatter_chips(dot_nt(dboth, w_in).astype(bf16).reshape(CHIPS, seq_len, D), 3)
    dhmid, grad_gain_ffn = norm_backward(hmid, hmid_scale, gain_ffn, dhn)
    dhmid = dhmid + dy
    dattn = dhmid.astype(bf16)
    dheads = dot_nt(dattn, w_o).astype(bf16).reshape(seq_len, CHIPS, 2 * DH)
    dheads = exchange_chips(jnp.transpose(dheads, (1, 0, 2)))
    dheads = jnp.pad(dheads.reshape(CHIPS, seq_len, 2, DH), ((0, 0), (0, 0), (0, 0), (0, HP - DH)))
    dqkv, theta_sums, mixer_sums, gain_sums = run_backward(
        group_lengths, mix, qkv, toep, gain_pair, scores, weights, outs, dheads.reshape(CHIPS, seq_len, 2 * HP)
    )
    dqkv_rows = dqkv.reshape(CHIPS * seq_len, 6 * HP)
    dxn = scatter_slow(dot_nt(dqkv_rows, w_qkv).reshape(CHIPS, seq_len, D))
    dinput, grad_gain_attn = norm_backward(input_float, input_scale, gain_attn, dxn)
    input_grad = dinput + dhmid

    taps = jnp.asarray(band())
    theta_sums = theta_sums.reshape(2, seq_len, CQ, seq_len)
    grad_theta = jnp.stack(
        [jnp.sum(jnp.where(taps[tap][None, :, None, :], theta_sums, 0.0), axis=(1, 3)) for tap in range(CK)], axis=2
    )
    grad_mixer = jnp.sum(mixer_sums[:4], axis=1)
    vector_grad = jnp.concatenate(
        [
            grad_gain_attn,
            lax.dynamic_update_slice_in_dim(
                jnp.zeros((D,), f32), gain_sums.reshape(2, HP)[:, :DH].reshape(-1), chip * 2 * DH, 0
            ),
            grad_gain_ffn,
            lax.dynamic_update_slice_in_dim(
                jnp.zeros((H * CQ * CK,), f32), grad_theta.reshape(-1), chip * 2 * CQ * CK, 0
            ),
            lax.dynamic_update_slice_in_dim(jnp.zeros((2 * H,), f32), grad_mixer, chip * 4, 0),
        ]
    )
    pieces = jnp.pad(vector_grad.reshape(fs_size, 1, own_vec), ((0, 0), (0, 0), (0, 512 - own_vec)))
    pieces = jnp.broadcast_to(pieces, (fs_size, reps, 512)).reshape(-1, 4, 128)
    vector_total = jnp.sum(
        lax.all_to_all(pieces, ALL, split_axis=0, concat_axis=0, tiled=True), axis=0
    ).reshape(512)[:own_vec]

    strip = BLK // (2 * CHIPS)
    grad_in = dot_tn(hn_rows, dboth).reshape(ROW_TILES, 2, CHIPS, strip, 2, BLK)
    grad_down = dot_tn(inner, dy_rows).reshape(2, CHIPS, strip, ROW_TILES, BLK)
    grad_in = jnp.transpose(half_for_core(grad_in, 1), (1, 3, 0, 2, 4)).reshape(CHIPS, 2 * ROW_TILES, strip, BLK)
    grad_down = jnp.transpose(half_for_core(grad_down, 0), (0, 2, 1, 3))
    ffn_tiles = exchange_chips(jnp.concatenate([grad_in, grad_down], axis=1).astype(bf16))
    gate_tiles = jnp.transpose(ffn_tiles[:, : 2 * ROW_TILES], (1, 0, 2, 3)).reshape(-1, strip, BLK)
    down_tiles = ffn_tiles[:, 2 * ROW_TILES :].reshape(-1, strip, BLK)
    grad_qkv = dot_tn(xn_rows, dqkv_rows).reshape(ROW_TILES, 2, CHIPS, strip, 6, HP)[..., :DH]
    grad_qkv = jnp.transpose(half_for_core(grad_qkv, 1), (1, 0, 2, 3, 4))
    grad_qkv = exchange_chips(grad_qkv.astype(bf16).reshape(CHIPS, ROW_TILES, strip, 6 * DH))
    grad_qkv = jnp.transpose(
        grad_qkv.reshape(CHIPS, ROW_TILES, strip, 3, 2 * DH), (3, 1, 2, 0, 4)
    ).reshape(3, ROW_TILES, strip, ROW_TILES, BLK)
    qkv_tiles = jnp.transpose(grad_qkv, (0, 1, 3, 2, 4)).reshape(-1, strip, BLK)
    heads_strips = jnp.transpose(heads.reshape(seq_len, 2 * ROW_TILES, CHIPS, strip), (2, 0, 1, 3))
    heads_strips = exchange_chips(heads_strips.reshape(CHIPS, seq_len, 2 * ROW_TILES * strip))
    dattn_rows = gather_slow(dattn).reshape(CHIPS * seq_len, D)
    grad_out = dot_tn(heads_strips.reshape(CHIPS * seq_len, -1), dattn_rows)
    grad_out = half_for_core(grad_out.reshape(ROW_TILES, 2, strip, ROW_TILES, BLK), 1)
    out_tiles = jnp.transpose(grad_out.astype(bf16), (0, 2, 1, 3)).reshape(-1, strip, BLK)

    groups = lax.axis_size("g")
    part = strip // groups
    own_slots = basis_left.shape[0]
    devices = groups * 2 * CHIPS
    slot_total = own_slots * devices
    sums = jnp.concatenate(
        [sum_groups(jnp.concatenate([qkv_tiles, out_tiles], axis=0)), sum_groups(jnp.concatenate([gate_tiles, down_tiles], axis=0))],
        axis=0,
    )
    matches = (jnp.arange(slot_total)[:, None] == owners[None, :]).astype(bf16)
    slots = dot(matches, sums.reshape(sums.shape[0], -1)).astype(bf16)
    slots = lax.all_to_all(
        slots.reshape(devices, own_slots, part, BLK), ALL, split_axis=0, concat_axis=0, tiled=True
    )
    slots = slots.reshape(groups, 2, 2, 2, 2, own_slots, part, BLK)
    own_grad = jnp.transpose(slots, (5, 3, 4, 1, 2, 0, 6, 7)).reshape(own_slots, BLK, BLK)

    left_low, right_low = basis_left.astype(bf16), basis_right.astype(bf16)
    rotated = jnp.einsum("sia,sij->saj", left_low, own_grad, preferred_element_type=f32)
    rotated = jnp.einsum("saj,sjb->sab", rotated.astype(bf16), right_low, preferred_element_type=f32)
    first_new = beta_first * block_first + (1.0 - beta_first) * rotated
    second_new = beta_second * block_second + (1.0 - beta_second) * rotated * rotated
    direction = (first_new / (jnp.sqrt(second_new) + eps_adam)).astype(bf16)
    turned = jnp.einsum("sia,sab->sib", left_low, direction, preferred_element_type=f32)
    turned = jnp.einsum("sib,sjb->sij", turned.astype(bf16), right_low, preferred_element_type=f32)
    master_new = block_master - rate_block * (turned + decay_block * block_master)
    vec_first_new = beta_first * vec_first + (1.0 - beta_first) * vector_total
    vec_second_new = beta_second * vec_second + (1.0 - beta_second) * vector_total * vector_total
    vec_master_new = vec_master - rate_vector * vec_first_new / (jnp.sqrt(vec_second_new) + eps_adam)
    return (
        layer_output, input_grad, first_new, second_new, master_new, master_new.astype(bf16),
        vec_first_new, vec_second_new, vec_master_new, vec_master_new.astype(bf16),
    )


def group_at(mask):
    return {axis: 1 - lax.axis_index(axis) for axis, bit in (("g", 4), ("a", 2), ("b", 1)) if mask & bit}


def other_bit(axis, changed):
    at = lax.axis_index(axis)
    return 1 - at if changed else at


def push(src, dst, send, recv, device):
    copy = pltpu.make_async_remote_copy(src_ref=src, dst_ref=dst, send_sem=send, recv_sem=recv, device_id=device)
    copy.start()
    return copy


class Gather:
    def __init__(self, x_ref, out_ref, local_sem, send1, recv1, send2, recv2, send3, recv3):
        self.x, self.out, self.local_sem = x_ref, out_ref, local_sem
        self.sems = ((send1, recv1), (send2, recv2), (send3, recv3))
        self.me = chip_index()
        self.half = x_ref.shape[0] // 2
        self.sent, self.second = [], []

    def here(self, part):
        return pl.ds(part * self.half, self.half)

    def start(self):
        self.local = pltpu.make_async_copy(self.x, self.out.at[self.me], self.local_sem)
        self.local.start()
        send, recv = self.sems[0]
        for part in range(2):
            for at, (axis, _, _) in enumerate(HOPS):
                self.sent.append(
                    push(
                        self.x.at[self.here(part)], self.out.at[self.me, self.here(part)],
                        send.at[at, part], recv.at[at, part], across(axis),
                    )
                )

    def onward(self):
        send, recv = self.sems[1]
        for part in range(2):
            for at, (axis, onward, _) in enumerate(HOPS):
                self.sent[part * 3 + at].wait_recv()
                block = self.out.at[flipped(self.me, (axis,)), self.here(part)]
                self.second.append(push(block, block, send.at[at, part], recv.at[at, part], across(onward)))

    def last(self):
        send, recv = self.sems[2]
        self.third = []
        for copy in self.second:
            copy.wait_recv()
        for at, (axis, onward, last) in enumerate(HOPS):
            begin, count = THIRDS[at]
            piece = self.out.at[flipped(self.me, (axis, onward)), pl.ds(begin, count)]
            self.third.append(push(piece, piece, send.at[at], recv.at[at], across(last)))

    def finish(self):
        for copy in self.third:
            copy.wait_recv()
        self.local.wait()

    def drain(self):
        for copy in self.sent + self.second + self.third:
            copy.wait_send()


class SideGather:
    def __init__(self, x_ref, out_ref, local_sem, send1, recv1, send2, recv2, send3, recv3):
        self.x, self.out, self.local_sem = x_ref, out_ref, local_sem
        self.sems = ((send1, recv1), (send2, recv2), (send3, recv3))
        self.me = chip_index()
        half = x_ref.shape[0] // 2
        self.low, self.high = pl.ds(0, half), pl.ds(half, half)

    def start(self):
        self.local = pltpu.make_async_copy(self.x, self.out.at[self.me], self.local_sem)
        self.local.start()
        send, recv = self.sems[0]
        self.first = [
            push(self.x, self.out.at[self.me], send.at[at], recv.at[at], across(axis)) for at, axis in enumerate("aby")
        ]

    def onward(self):
        send, recv = self.sems[1]
        blocks = [self.out.at[flipped(self.me, (axis,))] for axis in "aby"]
        self.first[0].wait_recv()
        self.second = [
            push(blocks[0], blocks[0], send.at[0], recv.at[0], across("b")),
            push(blocks[0], blocks[0], send.at[1], recv.at[1], across("y")),
        ]
        self.first[1].wait_recv()
        piece = blocks[1].at[self.high]
        self.second.append(push(piece, piece, send.at[2], recv.at[2], across("y")))
        self.first[2].wait_recv()
        piece = blocks[2].at[self.low]
        self.second.append(push(piece, piece, send.at[3], recv.at[3], across("b")))

    def last(self):
        send, recv = self.sems[2]
        self.second[0].wait_recv()
        piece = self.out.at[flipped(self.me, ("a", "b")), self.high]
        self.third = [push(piece, piece, send.at[0], recv.at[0], across("y"))]
        self.second[1].wait_recv()
        piece = self.out.at[flipped(self.me, ("a", "y")), self.low]
        self.third.append(push(piece, piece, send.at[1], recv.at[1], across("b")))

    def finish(self):
        for copy in self.second[2:] + self.third:
            copy.wait_recv()
        self.local.wait()

    def drain(self):
        for copy in self.first + self.second + self.third:
            copy.wait_send()


def side_sems():
    dma = pltpu.SemaphoreType.DMA
    return [dma] + [dma((3,))] * 2 + [dma((4,))] * 2 + [dma((2,))] * 2


class Scatter:
    def __init__(self, parts, near, in2, in3, acc2, acc3, send1, recv1, send2, recv2, send3, recv3):
        self.parts, self.near, self.in2, self.in3, self.acc2, self.acc3 = parts, near, in2, in3, acc2, acc3
        self.sems = ((send1, recv1), (send2, recv2), (send3, recv3))
        self.me = chip_index()
        self.half = parts.shape[1] // 2

    def here(self, part):
        return pl.ds(part * self.half, self.half)

    def start(self):
        send, recv = self.sems[0]
        opposite = flipped(self.me, ("y", "a", "b"))
        self.first = []
        for at, (_, _, last) in enumerate(HOPS):
            rows = pl.ds(*THIRDS[at])
            self.first.append(push(self.parts.at[opposite, rows], self.in2.at[rows], send.at[at], recv.at[at], across(last)))

    def onward(self):
        send, recv = self.sems[1]
        self.second = []
        for part in range(2):
            for at, (axis, onward, _) in enumerate(HOPS):
                dest = flipped(self.me, (axis, onward))
                if part == 0:
                    self.first[at].wait_recv()
                    rows = pl.ds(*THIRDS[at])
                    self.acc2[at] = self.parts[dest]
                    self.acc2[at, rows] = (
                        self.parts[dest, rows].astype(f32) + self.in2[rows].astype(f32)
                    ).astype(bf16)
                here = self.here(part)
                self.second.append(
                    push(self.acc2.at[at, here], self.in3.at[at, here], send.at[at, part], recv.at[at, part], across(onward))
                )

    def last(self):
        send, recv = self.sems[2]
        self.third = []
        for part in range(2):
            here = self.here(part)
            for at, (axis, _, _) in enumerate(HOPS):
                dest = flipped(self.me, (axis,))
                self.second[part * 3 + at].wait_recv()
                self.acc3[at, here] = (
                    self.parts[dest, here].astype(f32) + self.in3[at, here].astype(f32)
                ).astype(bf16)
                self.third.append(
                    push(self.acc3.at[at, here], self.near.at[at, here], send.at[at, part], recv.at[at, part], across(axis))
                )

    def finish(self, part):
        here = self.here(part)
        for at in range(3):
            self.third[part * 3 + at].wait_recv()
        return (self.parts[self.me, here].astype(f32) + self.near[0, here].astype(f32)) + (
            self.near[1, here].astype(f32) + self.near[2, here].astype(f32)
        )

    def drain(self):
        for copy in self.first + self.second + self.third:
            copy.wait_send()


class SideScatter:
    def __init__(self, parts, near, in1, in2, acc2, acc3, send1, recv1, send2, recv2, send3, recv3):
        self.parts, self.near, self.in1, self.in2, self.acc2, self.acc3 = parts, near, in1, in2, acc2, acc3
        self.sems = ((send1, recv1), (send2, recv2), (send3, recv3))
        self.me = chip_index()
        half = parts.shape[1] // 2
        self.low, self.high = pl.ds(0, half), pl.ds(half, half)

    def start(self):
        send, recv = self.sems[0]
        far, side = flipped(self.me, ("a", "b", "y")), flipped(self.me, ("b", "y"))
        self.first = [
            push(self.parts.at[block, rows], self.in1.at[at], send.at[at], recv.at[at], across(axis))
            for at, (block, rows, axis) in enumerate(
                ((far, self.high, "y"), (far, self.low, "b"), (side, self.low, "b"), (side, self.high, "y"))
            )
        ]

    def add(self, at, axes, rows, acc):
        self.first[at].wait_recv()
        block = flipped(self.me, axes)
        acc[...] = self.parts[block]
        acc[rows] = (self.parts[block, rows].astype(f32) + self.in1[at].astype(f32)).astype(bf16)
        return acc

    def onward(self):
        send, recv = self.sems[1]
        third_send, third_recv = self.sems[2]
        self.second = [
            push(self.add(0, ("a", "b"), self.high, self.acc2.at[0]), self.in2.at[0], send.at[0], recv.at[0], across("b")),
            push(self.add(1, ("a", "y"), self.low, self.acc2.at[1]), self.in2.at[1], send.at[1], recv.at[1], across("y")),
        ]
        self.third = [
            push(self.add(at, (axis,), rows, self.acc3.at[to]), self.near.at[to], third_send.at[to], third_recv.at[to], across(axis))
            for at, axis, rows, to in ((3, "b", self.high, 1), (2, "y", self.low, 2))
        ]

    def last(self):
        send, recv = self.sems[2]
        for copy in self.second:
            copy.wait_recv()
        self.acc3[0] = (
            self.parts[flipped(self.me, ("a",))].astype(f32) + (self.in2[0].astype(f32) + self.in2[1].astype(f32))
        ).astype(bf16)
        self.third.append(push(self.acc3.at[0], self.near.at[0], send.at[0], recv.at[0], across("a")))

    def finish(self):
        for copy in self.third:
            copy.wait_recv()
        return (self.parts[self.me].astype(f32) + self.near[0].astype(f32)) + (
            self.near[1].astype(f32) + self.near[2].astype(f32)
        )

    def drain(self):
        for copy in self.first + self.second + self.third:
            copy.wait_send()


def side_scatter_scratch(rows, width):
    dma = pltpu.SemaphoreType.DMA
    return [
        pltpu.VMEM(dims + (width,), bf16) for dims in ((3, rows), (4, rows // 2), (2, rows), (2, rows), (3, rows))
    ] + [dma((4,))] * 2 + [dma((2,))] * 2 + [dma((3,))] * 2


def scatter_scratch(rows, width):
    dma = pltpu.SemaphoreType.DMA
    three = pltpu.VMEM((3, rows, width), bf16)
    return [three, pltpu.VMEM((rows, width), bf16), three, three, three] + [dma((3,))] * 2 + [dma((3, 2))] * 4


VMEM = pl.BlockSpec(memory_space=pltpu.VMEM)


def vectors_body(vec_ref, vecs_ref, send, recv, local_sem):
    devices = lax.axis_size(ALL)
    me = device_index()
    local = pltpu.make_async_copy(vec_ref, vecs_ref.at[me], local_sem)
    local.start()
    greet_all()

    def push_vec(step, carry):
        pltpu.make_async_remote_copy(
            src_ref=vec_ref, dst_ref=vecs_ref.at[me], send_sem=send, recv_sem=recv,
            device_id=device_at(lax.rem(me + step, devices)),
        ).start()
        return carry

    lax.fori_loop(1, devices, push_vec, 0)
    others = vecs_ref.at[pl.ds(0, devices - 1)]
    pltpu.make_async_copy(others, others, recv).wait()
    pltpu.make_async_copy(others, others, send).wait()
    local.wait()


def gather_vectors(vec):
    return pl.pallas_call(
        vectors_body,
        in_specs=[VMEM],
        out_specs=VMEM,
        out_shape=jax.ShapeDtypeStruct((lax.axis_size(ALL),) + vec.shape, vec.dtype),
        scratch_shapes=[pltpu.SemaphoreType.DMA] * 3,
        name="gather_vectors",
        compiler_params=pltpu.CompilerParams(collective_id=1, has_side_effects=True),
    )(vec)


def source_at(mask):
    return ((other_bit("g", mask & 4) * 2 + other_bit("a", mask & 2)) * 2 + other_bit("b", mask & 1)) * 2 + lax.axis_index("c")


def front_body(
    len_ref, mix_ref, x_ref, gains_ref, toep_ref, gain_ref, blocks_ref, w_out_ref, w_gate_ref, w_up_ref, w_down_ref, dy_ref,
    xn_ref, qkv_ref, s_ref, p_ref, o_ref, heads_ref, hmid_ref, wq_ref, wo_ref, hn_all_ref, w_in_ref, w_dn_ref, dy_all_ref,
    x_all_ref, pad_ref, out_heads, hn_ref, passing, local_sems, q_send, q_recv, q_core_send, q_core_recv,
    o_send, o_recv, o_side_send, o_side_recv, o_core_send, o_core_recv, d_send, d_recv,
    w_send, w_recv, u_send, u_recv, core_send, core_recv, head_send, head_recv, *hops,
):
    seqs, rows, _ = x_all_ref.shape
    g, a, b, c, y = (lax.axis_index(axis) for axis in ALL)
    me = chip_index()
    mine = source_at(0)
    shard = {mask: source_at(mask) for mask in range(8)}
    low, high = pl.ds(0, BLK), pl.ds(BLK, BLK)
    order = (4, 6, 5, 7, 2, 1, 3)

    def columns(chip):
        return pl.ds(pl.multiple_of(chip * BLK, BLK), BLK)

    def block_to(mask):
        return (y * 2 + other_bit("a", mask & 2)) * 2 + other_bit("b", mask & 1)

    local = [
        pltpu.make_async_copy(blocks_ref.at[me], wq_ref.at[mine], local_sems.at[0]),
        pltpu.make_async_copy(w_out_ref, wo_ref.at[mine], local_sems.at[1]),
        pltpu.make_async_copy(w_gate_ref.at[:, columns(me)], w_in_ref.at[mine, :, low], local_sems.at[2]),
        pltpu.make_async_copy(w_up_ref.at[:, columns(me)], w_in_ref.at[mine, :, high], local_sems.at[3]),
    ]
    down_local = pltpu.make_async_copy(w_down_ref, w_dn_ref.at[c], local_sems.at[4])
    for copy in local:
        copy.start()

    @pl.when(g == y)
    def _():
        down_local.start()

    greet_all()
    sent, relayed = {}, []
    first = Gather(x_ref, x_all_ref, *hops[:7])
    side = SideGather(dy_ref, dy_all_ref, *hops[7:14])
    gather = Gather(hn_ref, hn_all_ref, *hops[14:])

    first.start()
    for mask in order:
        sent[mask] = push(blocks_ref.at[block_to(mask)], wq_ref.at[mine], q_send.at[mask], q_recv.at[mask], group_at(mask))

    def relay_qkv(mask):
        sent[mask].wait_recv()
        block = wq_ref.at[shard[mask]]
        relayed.append(push(block, block, q_core_send.at[mask], q_core_recv.at[mask], across("c")))

    half = pl.ds(pl.multiple_of(y * 48, 16), 48)
    lines, o_side, o_core = {}, {}, []

    def start_lines():
        for mask in (2, 4, 6):
            lines[mask] = push(w_out_ref.at[half], wo_ref.at[mine, half], o_send.at[mask], o_recv.at[mask], group_at(mask))
        lines[1] = push(w_out_ref.at[half], wo_ref.at[mine, half], o_send.at[1], o_recv.at[1], across("b"))
        o_core.append(push(w_out_ref, wo_ref.at[mine], o_core_send.at[0], o_core_recv.at[0], across("c")))

    def to_side(mask):
        lines[mask].wait_recv()
        piece = wo_ref.at[shard[mask], half]
        o_side[mask] = push(piece, piece, o_side_send.at[mask], o_side_recv.at[mask], across("y"))
        if mask in (2, 4, 6):
            lines[mask + 1] = push(piece, piece, o_send.at[mask + 1], o_recv.at[mask + 1], across("b"))

    def out_to_core():
        for mask in (2, 4, 6, 1, 3, 5, 7):
            o_side[mask].wait_recv()
            block = wo_ref.at[shard[mask]]
            o_core.append(push(block, block, o_core_send.at[mask], o_core_recv.at[mask], across("c")))

    count = w_down_ref.shape[0] // 2
    upper, lower = pl.ds(0, count), pl.ds(count, count)

    def down_copy(src, dst, at, axis):
        return pltpu.make_async_remote_copy(
            src_ref=src, dst_ref=dst, send_sem=d_send.at[at], recv_sem=d_recv.at[at], device_id=across(axis)
        )

    def down_direct():
        return down_copy(w_down_ref.at[upper], w_dn_ref.at[c, upper], 0, "g")

    def down_around():
        return down_copy(w_down_ref.at[lower], passing, 1, "g")

    def down_over():
        return down_copy(passing, w_dn_ref.at[c, lower], 2, "y")

    def down_to_core():
        return down_copy(w_dn_ref.at[c], w_dn_ref.at[c], 3, "c")

    def down_start():
        @pl.when(g == y)
        def _():
            down_direct().start()

        @pl.when(g != y)
        def _():
            down_around().start()

    def down_pass():
        @pl.when(g == y)
        def _():
            down_around().wait_recv()
            down_over().start()

    def down_last():
        @pl.when(g == y)
        def _():
            down_local.wait()
            down_to_core().start()
            down_direct().wait_send()
            down_over().wait_send()

        @pl.when(g != y)
        def _():
            down_direct().wait_recv()
            down_over().wait_recv()
            down_to_core().start()
            down_around().wait_send()

    gate, up = {}, {}

    def send_columns(masks):
        for mask in masks:
            to = columns(block_to(mask))
            gate[mask] = push(w_gate_ref.at[:, to], w_in_ref.at[mine, :, low], w_send.at[mask], w_recv.at[mask], group_at(mask))
            up[mask] = push(w_up_ref.at[:, to], w_in_ref.at[mine, :, high], u_send.at[mask], u_recv.at[mask], group_at(mask))

    def relay(mask):
        gate[mask].wait_recv()
        up[mask].wait_recv()
        block = w_in_ref.at[shard[mask]]
        relayed.append(push(block, block, core_send.at[mask], core_recv.at[mask], across("c")))

    start_lines()
    local[0].wait()
    relayed.append(push(wq_ref.at[mine], wq_ref.at[mine], q_core_send.at[0], q_core_recv.at[0], across("c")))
    first.onward()
    down_start()
    for mask in (2, 4, 6):
        to_side(mask)
    to_side(1)
    relay_qkv(4)
    relay_qkv(6)
    first.last()
    send_columns((4, 6, 5, 7))
    for mask in (5, 7, 2, 1, 3):
        relay_qkv(mask)
    side.start()
    first.finish()
    for copy in relayed:
        copy.wait_recv()
    send_columns((2, 1, 3))
    qkv_relayed = relayed[:]
    del relayed[:]

    pad_ref[0:8, :] = jnp.zeros((8, rows), f32)
    blank = jnp.zeros((rows, HP - DH), bf16)
    batch = 4

    def project(at, carry):
        values = x_all_ref[pl.ds(at * batch, batch)].astype(f32).reshape(batch * rows, D)
        normed = (values * rms(values) * gains_ref[0:1, :]).astype(bf16)
        xn_ref[pl.ds(at * batch, batch)] = normed.reshape(batch, rows, D)
        made = dot(normed, wq_ref[...].reshape(D, 6 * DH)).astype(bf16)
        for seq in range(batch):
            for piece in range(6):
                qkv_ref[at * batch + seq, :, piece * HP : (piece + 1) * HP] = jnp.concatenate(
                    [made[seq * rows : (seq + 1) * rows, piece * DH : (piece + 1) * DH], blank], axis=1
                )
        return carry

    project(0, 0)
    for mask in (3, 5, 7):
        to_side(mask)
    down_pass()
    project(1, 0)
    side.onward()
    for copy in local[1:]:
        copy.wait()
    relayed.append(push(w_in_ref.at[mine], w_in_ref.at[mine], core_send.at[0], core_recv.at[0], across("c")))
    query_at = lax.broadcasted_iota(jnp.int32, (rows, rows), 0)
    key_at = lax.broadcasted_iota(jnp.int32, (rows, rows), 1)

    def head_copy(seq):
        return pltpu.make_async_remote_copy(
            src_ref=out_heads.at[seq], dst_ref=heads_ref.at[me], send_sem=head_send.at[seq], recv_sem=head_recv.at[me],
            device_id={"y": lax.div(seq, 4), "a": lax.rem(lax.div(seq, 2), 2), "b": lax.rem(seq, 2)},
        )

    def attend(step, carry):
        seq = lax.rem(me + step, seqs)
        keep = (key_at <= query_at) & (key_at < len_ref[seq])
        weights, made = [], []
        for head in range(2):
            query = qkv_ref[seq, :, head * HP : (head + 1) * HP]
            key = qkv_ref[seq, :, (2 + head) * HP : (3 + head) * HP]
            scores = jnp.where(keep, dot_nt(query, key) * (1.0 / math.sqrt(DH)), 0.0)
            s_ref[seq, head] = scores.astype(bf16)
            wide = shifted_down(pad_ref, scores)
            near = wide.astype(bf16)
            rest = (wide - near.astype(f32)).astype(bf16)
            conv = dot(near, toep_ref[head]) + dot(rest, toep_ref[head])
            logits = jnp.where(keep, conv, -1e30)
            weight = jnp.exp(logits - jnp.max(logits, axis=-1, keepdims=True))
            weight = weight / jnp.sum(weight, axis=-1, keepdims=True)
            p_ref[seq, head] = weight
            weights.append(weight)
        for head in range(2):
            mixed = mix_ref[2 * head] * weights[0] + mix_ref[2 * head + 1] * weights[1]
            value = qkv_ref[seq, :, (4 + head) * HP : (5 + head) * HP]
            out = dot(mixed.astype(bf16), value)
            o_ref[seq, :, head * HP : (head + 1) * HP] = out
            scale = lax.rsqrt(jnp.sum(out * out, axis=-1, keepdims=True) * (1.0 / DH) + eps_norm)
            made.append((out * scale * gain_ref[:, head * HP : (head + 1) * HP])[:, :DH])
        out_heads[seq] = jnp.concatenate(made, axis=1).astype(bf16)

        @pl.when(step > 0)
        def _():
            head_copy(seq).start()

        return carry

    lax.fori_loop(0, 4, attend, 0)
    out_to_core()
    lax.fori_loop(4, seqs, attend, 0)
    heads_ref[me] = out_heads[me]
    for copy in o_core:
        copy.wait_recv()

    def head_arrived(step, carry):
        source = lax.rem(me + step, seqs)
        pltpu.make_async_copy(out_heads.at[source], heads_ref.at[source], head_recv.at[source]).wait()
        return carry

    lax.fori_loop(1, seqs, head_arrived, 0)

    def project_out(at, carry):
        cols = pl.ds(pl.multiple_of(at * BLK, BLK), BLK)
        total = x_ref[:, cols].astype(f32)
        for chip in range(CHIPS):
            weight = wo_ref[2 * chip : 2 * chip + 2, :, cols].reshape(2 * DH, BLK)
            total += dot(heads_ref[chip], weight)
        hmid_ref[:, cols] = total
        return carry

    lax.fori_loop(0, ROW_TILES, project_out, 0)
    hmid = hmid_ref[...]
    hn_ref[...] = (hmid * rms(hmid) * gains_ref[1:2, :]).astype(bf16)
    gather.start()
    side.last()
    for mask in (4, 6):
        relay(mask)
    gather.onward()
    for mask in (5, 7, 2):
        relay(mask)
    gather.last()
    for mask in (1, 3):
        relay(mask)
    down_last()
    down_to_core().wait()
    side.finish()
    gather.finish()
    for copy in relayed:
        copy.wait_recv()

    def head_left(step, carry):
        head_copy(lax.rem(me + step, seqs)).wait_send()
        return carry

    lax.fori_loop(1, seqs, head_left, 0)
    first.drain()
    side.drain()
    gather.drain()
    for copies in (sent, lines, o_side, gate, up):
        for copy in copies.values():
            copy.wait_send()
    for copy in qkv_relayed + relayed + o_core:
        copy.wait_send()


def run_front(lengths, mix, x, gains, toep, gain, blocks, w_out, w_gate, w_up, w_down, dy):
    rows = x.shape[0]
    dma = pltpu.SemaphoreType.DMA
    shapes = [
        ((CHIPS, rows, D), bf16), ((CHIPS, rows, 6 * HP), bf16), ((CHIPS, 2, rows, rows), bf16), ((CHIPS, 2, rows, rows), f32),
        ((CHIPS, rows, 2 * HP), f32), ((CHIPS, rows, 2 * DH), bf16), ((rows, D), f32),
        ((16,) + blocks.shape[1:], bf16), ((16,) + w_out.shape, bf16), ((CHIPS, rows, D), bf16),
        ((16, w_gate.shape[0], 2 * BLK), bf16), ((2,) + w_down.shape, bf16), ((CHIPS, rows, D), bf16),
    ]
    return pl.pallas_call(
        front_body,
        in_specs=[SMEM, SMEM] + [VMEM] * 4 + [ANYS] * 6,
        out_specs=[VMEM] * 9 + [ANYS] * 4,
        out_shape=[jax.ShapeDtypeStruct(*shape) for shape in shapes],
        scratch_shapes=[
            pltpu.VMEM((CHIPS, rows, D), bf16), pltpu.VMEM((rows + 8, rows), f32), pltpu.VMEM((CHIPS, rows, 2 * DH), bf16),
            pltpu.VMEM((rows, D), bf16), pltpu.VMEM((w_down.shape[0] // 2, D), bf16), dma((5,)),
        ] + [dma((8,))] * 10 + [dma((4,))] * 2 + [dma((8,))] * 8 + hop_sems() + side_sems() + hop_sems(),
        name="front",
        compiler_params=pltpu.CompilerParams(collective_id=2, has_side_effects=True, vmem_limit_bytes=56 * 2**20),
    )(lengths, mix, x, gains, toep, gain, blocks, w_out, w_gate, w_up, w_down, dy)


def middle_body(
    len_ref, mix_ref, hn_ref, dy_ref, xn_ref, w_in_ref, w_dn_ref, wq_ref, dy_own_ref, hmid_ref, gain_ffn_ref, wo_ref,
    qkv_ref, toep_ref, gain_ref, s_ref, p_ref, o_ref, strips_ref,
    inner_ref, dhmid_ref, dxn_ref, gain_ffn_grad_ref, theta_ref, mixer_ref, gain_grad_ref, tiles_ref,
    theta_sums, pad_ref, first_ref, second_ref, dboth_ref, parts_ref, dattn_ref, grads_ref, sent_ref, strips_in, gin_ref, gd_ref,
    half_in, half_d, near_in, near_d, dqkv_ref, gq_ref, go_ref, core_q, core_o, in_q, in_o,
    near3, in23, in33, local_sems, load_sems, strip_send, strip_recv, head_send, head_recv,
    core_send, core_recv, near_send, near_recv, gu_send, gu_recv, q_send, q_recv, *rest,
):
    scatter_args, scatter3_sems, side = rest[:11], rest[11:17], rest[17:]
    seqs, rows, _ = hn_ref.shape
    g, a, b, c, y = (lax.axis_index(axis) for axis in ALL)
    me = chip_index()
    pairs = [(1 - y) * 2 + 1 - a, (1 - y) * 2 + a, y * 2 + 1 - a, y * 2 + a]
    loads = []
    for at, pair in enumerate(pairs):
        two = pl.ds(pair * 2, 2)
        loads.append(
            [
                pltpu.make_async_copy(hn_ref.at[two], first_ref.at[two], load_sems.at[at]),
                pltpu.make_async_copy(dy_ref.at[two], second_ref.at[two], load_sems.at[4 + at]),
            ]
        )
    for copies in loads:
        for copy in copies:
            copy.start()
    strip_local = pltpu.make_async_copy(strips_ref.at[me], strips_in.at[me], local_sems.at[0])
    strip_local.start()
    greet_all()
    chips = (7, 6, 5, 3, 4, 2, 1)
    to_chip = {mask: flipped(me, [axis for axis in BITS if mask & BITS[axis]]) for mask in chips}
    strips_sent = [
        push(strips_ref.at[to_chip[mask]], strips_in.at[me], strip_send.at[mask], strip_recv.at[mask], chip_at(mask))
        for mask in chips
    ]

    def hidden(pair):
        two = pl.ds(pair * 2, 2)
        both = dot(first_ref[two].reshape(2 * rows, D), w_in_ref[...])
        gate, up = both[:, :BLK], both[:, BLK:]
        dinner = dot_nt(second_ref[two].reshape(2 * rows, D), w_dn_ref[...])
        sig = jax.nn.sigmoid(gate)
        silu = gate * sig
        inner_ref[two] = (silu * up).astype(bf16).reshape(2, rows, BLK)
        dgate = (dinner * up * (sig * (1.0 + gate * (1.0 - sig)))).astype(bf16)
        dup = (dinner * silu).astype(bf16)
        dboth_ref[two, :, 0:BLK] = dgate.reshape(2, rows, BLK)
        dboth_ref[two, :, BLK:] = dup.reshape(2, rows, BLK)
        back = dot_nt(dgate, w_in_ref[:, 0:BLK]) + dot_nt(dup, w_in_ref[:, BLK:])
        parts_ref[two] = back.astype(bf16).reshape(2, rows, D)

    def wait_load(at):
        for copy in loads[at]:
            copy.wait()

    wait_load(0)
    hidden(pairs[0])
    scatter = Scatter(parts_ref, *scatter_args)
    scatter.start()
    wait_load(1)
    wait_load(2)

    def two_more(step, carry):
        hidden((1 - y) * 2 + a + step * ((2 * y - 1) * 2 + 1 - a - a))
        return carry

    lax.fori_loop(0, 2, two_more, 0)
    scatter.onward()
    wait_load(3)
    hidden(pairs[3])

    def down_grad(col, carry):
        cols = pl.ds(pl.multiple_of(col * BLK, BLK), BLK)
        made = dot_tn(inner_ref[...].reshape(seqs * rows, BLK), second_ref[:, :, cols].reshape(seqs * rows, BLK))
        gd_ref[:, :, :, :, cols] = made.astype(bf16).reshape(2, CHIPS, 2, BLK // 32, BLK)
        return carry

    lax.fori_loop(0, ROW_TILES, down_grad, 0)
    to_core = [push(gd_ref.at[1 - c], half_d, core_send.at[0], core_recv.at[0], across("c"))]

    def in_grad(row, carry):
        values = first_ref[:, :, pl.ds(pl.multiple_of(row * BLK, BLK), BLK)].reshape(seqs * rows, BLK)
        for which in range(2):
            cols = slice(which * BLK, (which + 1) * BLK)
            made = dot_tn(values, dboth_ref[:, :, cols].reshape(seqs * rows, BLK))
            gin_ref[row, :, :, :, :, cols] = made.astype(bf16).reshape(2, CHIPS, 2, BLK // 32, BLK)
        return carry

    def in_to_core(row):
        to_core.append(push(gin_ref.at[row, 1 - c], half_in.at[row], core_send.at[1 + row], core_recv.at[1 + row], across("c")))

    in_grad(0, 0)
    in_to_core(0)
    to_core[0].wait_recv()

    def core_down(chip, carry):
        half_d[chip] = (half_d[chip].astype(f32) + gd_ref[c, chip].astype(f32)).astype(bf16)
        return carry

    lax.fori_loop(0, CHIPS, core_down, 0)
    to_near = [push(half_d.at[:, 1 - g], near_d, near_send.at[0], near_recv.at[0], across("g"))]
    scatter.last()
    lax.fori_loop(1, ROW_TILES, in_grad, 0)
    in_to_core(1)
    in_to_core(2)
    xn_load = pltpu.make_async_copy(xn_ref, first_ref, load_sems.at[8])
    xn_load.start()

    def core_rows(row):
        to_core[1 + row].wait_recv()

        def core_chip(chip, carry):
            half_in[row, chip] = (half_in[row, chip].astype(f32) + gin_ref[row, c, chip].astype(f32)).astype(bf16)
            return carry

        lax.fori_loop(0, CHIPS, core_chip, 0)
        to_near.append(push(half_in.at[row, :, 1 - g], near_in.at[row], near_send.at[1 + row], near_recv.at[1 + row], across("g")))

    core_rows(0)
    core_rows(1)
    core_rows(2)
    half = rows // 2
    gain_sum = jnp.zeros((1, D), f32)
    for part in range(2):
        here = pl.ds(part * half, half)
        grad = scatter.finish(part)
        values = hmid_ref[here]
        scale = rms(values)
        unit = values * scale
        inside = grad * gain_ffn_ref[...]
        gain_sum += jnp.sum(grad * unit, axis=0, keepdims=True)
        dhmid = scale * (inside - unit * jnp.mean(inside * unit, axis=-1, keepdims=True)) + dy_own_ref[here].astype(f32)
        dhmid_ref[here] = dhmid
        dattn_ref[here] = dhmid.astype(bf16)
    gain_ffn_grad_ref[...] = gain_sum

    def grad_copy(to):
        return pltpu.make_async_remote_copy(
            src_ref=sent_ref.at[to], dst_ref=grads_ref.at[me], send_sem=head_send.at[to], recv_sem=head_recv.at[me],
            device_id={"y": lax.div(to, 4), "a": lax.rem(lax.div(to, 2), 2), "b": lax.rem(to, 2)},
        )

    def send_grad(step, carry):
        to = lax.rem(me + step, seqs)
        sent_ref[to] = dot_nt(dattn_ref[...], wo_ref[to]).astype(bf16)

        @pl.when(step > 0)
        def _():
            grad_copy(to).start()

        return carry

    lax.fori_loop(0, seqs, send_grad, 0)
    grads_ref[me] = sent_ref[me]
    gather = SideGather(dattn_ref, second_ref, *side)
    gather.start()

    pad_ref[rows : rows + 8, :] = jnp.zeros((8, rows), f32)
    theta_sums[...] = jnp.zeros_like(theta_sums)
    mixer_ref[...] = jnp.zeros_like(mixer_ref)
    gain_grad_ref[...] = jnp.zeros_like(gain_grad_ref)
    query_at = lax.broadcasted_iota(jnp.int32, (rows, rows), 0)
    key_at = lax.broadcasted_iota(jnp.int32, (rows, rows), 1)
    blank = jnp.zeros((rows, HP - DH), f32)

    def grad_arrived(step, carry):
        source = lax.rem(me + step, seqs)
        pltpu.make_async_copy(sent_ref.at[source], grads_ref.at[source], head_recv.at[source]).wait()
        return carry

    lax.fori_loop(1, seqs, grad_arrived, 0)

    def one(seq, carry):
        keep = (key_at <= query_at) & (key_at < len_ref[seq])
        weights = [p_ref[seq, 0], p_ref[seq, 1]]
        grad_mixed, made = [], [None] * 6
        grads = grads_ref[seq].astype(f32)
        for head in range(2):
            cols = slice(head * HP, (head + 1) * HP)
            out = o_ref[seq, :, cols]
            grad = jnp.concatenate([grads[:, head * DH : (head + 1) * DH], blank], axis=1)
            scale = lax.rsqrt(jnp.sum(out * out, axis=-1, keepdims=True) * (1.0 / DH) + eps_norm)
            unit = out * scale
            gain_grad_ref[:, cols] += jnp.sum(grad * unit, axis=0, keepdims=True)
            inner = grad * gain_ref[:, cols]
            grad_out = scale * (inner - unit * (jnp.sum(inner * unit, axis=-1, keepdims=True) * (1.0 / DH)))
            grad_out = grad_out.astype(bf16)
            value = qkv_ref[seq, :, (4 + head) * HP : (5 + head) * HP]
            mixed = (mix_ref[2 * head] * weights[0] + mix_ref[2 * head + 1] * weights[1]).astype(bf16)
            made[4 + head] = dot_tn(mixed, grad_out)
            back = dot_nt(grad_out, value)
            grad_mixed.append(back)
            for source in range(2):
                mixer_ref[2 * head + source : 2 * head + source + 1, :] += jnp.sum(
                    back * weights[source], axis=0, keepdims=True
                )
        for head in range(2):
            grad_weight = mix_ref[head] * grad_mixed[0] + mix_ref[2 + head] * grad_mixed[1]
            weight = weights[head]
            grad_conv = weight * (grad_weight - jnp.sum(weight * grad_weight, axis=-1, keepdims=True))
            wide = shifted_up(pad_ref, grad_conv).astype(bf16)
            theta_sums[head] += dot_tn(s_ref[seq, head], wide)
            grad_scores = jnp.zeros((rows, rows), f32)
            for lag in range(CQ):
                grad_scores += dot_nt(
                    wide[:, lag * rows : (lag + 1) * rows], toep_ref[head, lag * rows : (lag + 1) * rows, :]
                )
            grad_scores = jnp.where(keep, grad_scores * (1.0 / math.sqrt(DH)), 0.0).astype(bf16)
            query = qkv_ref[seq, :, head * HP : (head + 1) * HP]
            key = qkv_ref[seq, :, (2 + head) * HP : (3 + head) * HP]
            made[head] = dot(grad_scores, key)
            made[2 + head] = dot_tn(grad_scores, query)
        dqkv_ref[seq] = jnp.concatenate([part[:, :DH] for part in made], axis=1).astype(bf16)
        return carry

    lax.fori_loop(0, seqs, one, 0)
    gather.onward()
    scatter.drain()
    tiles_sent = []

    tap_at = query_at - key_at + CK // 2

    def taps(at, carry):
        lag = lax.rem(at, CQ)
        values = theta_sums[lax.div(at, CQ), :, pl.ds(pl.multiple_of(lag * rows, rows), rows)]
        for tap in range(CK):
            theta_ref[pl.ds(at * CK + tap, 1), :] = jnp.sum(
                jnp.where(tap_at == tap, values, 0.0), axis=0, keepdims=True
            )
        return carry

    xn_load.wait()
    all_rows = seqs * rows

    def qkv_grad(row, carry):
        cols = pl.ds(pl.multiple_of(row * BLK, BLK), BLK)
        made = dot_tn(first_ref[:, :, cols].reshape(all_rows, BLK), dqkv_ref[...].reshape(all_rows, 6 * DH))
        gq_ref[row] = made.astype(bf16).reshape(2, CHIPS, 2, BLK // 32, 6 * DH)
        return carry

    lax.fori_loop(0, ROW_TILES, qkv_grad, 0)
    to_core.append(push(gq_ref.at[:, 1 - c], core_q, core_send.at[4], core_recv.at[4], across("c")))

    def input_part(at, carry):
        two = pl.ds(at * 2, 2)
        made = dot_nt(dqkv_ref[two].reshape(2 * rows, 6 * DH), wq_ref[...])
        parts_ref[two] = made.astype(bf16).reshape(2, rows, D)
        return carry

    lax.fori_loop(0, seqs // 2, input_part, 0)
    scatter3 = Scatter(parts_ref, near3, in23, in33, *scatter_args[3:5], *scatter3_sems)
    scatter3.start()
    lax.fori_loop(0, 2 * CQ, taps, 0)
    to_core[4].wait_recv()

    def core_chip_q(chip, carry):
        for row in range(ROW_TILES):
            core_q[row, chip] = (core_q[row, chip].astype(f32) + gq_ref[row, c, chip].astype(f32)).astype(bf16)
        return carry

    lax.fori_loop(0, CHIPS, core_chip_q, 0)
    slot = g * CHIPS + me
    order = (15, 14, 13, 11, 12, 10, 9, 8, 7, 6, 5, 3, 4, 2, 1)
    for mask in order:
        to = flipped(me, [axis for axis in BITS if mask & BITS[axis]])
        tiles_sent.append(
            push(core_q.at[:, to, other_bit("g", mask & 8)], in_q.at[slot], q_send.at[mask], q_recv.at[mask], wide_at(mask))
        )
    in_q[slot] = core_q[:, me, g]
    gather.last()
    to_near[0].wait_recv()

    def near_down(chip, carry):
        half_d[chip, g] = (half_d[chip, g].astype(f32) + near_d[chip].astype(f32)).astype(bf16)
        return carry

    lax.fori_loop(0, CHIPS, near_down, 0)
    base = 4 * ROW_TILES**2

    def spread(ref, cols, tile, which):
        for mask in chips:
            at = which * CHIPS + mask
            tiles_sent.append(
                push(ref.at[to_chip[mask], g, :, cols], tiles_ref.at[tile], gu_send.at[at], gu_recv.at[at], chip_at(mask))
            )
        tiles_ref[tile] = ref[me, g, :, cols]

    for col in range(ROW_TILES):
        spread(half_d, pl.ds(col * BLK, BLK), base + 2 * ROW_TILES * FF_TILES + me * ROW_TILES + col, 6 + col)
    scatter3.onward()
    gather.finish()
    strip_local.wait()
    for copy in strips_sent:
        copy.wait_recv()

    def out_grad(col, carry):
        cols = pl.ds(pl.multiple_of(col * BLK, BLK), BLK)
        made = dot_tn(strips_in[...].reshape(all_rows, 2 * DH), second_ref[:, :, cols].reshape(all_rows, BLK))
        go_ref[:, :, :, :, cols] = made.astype(bf16).reshape(ROW_TILES, 2, 2, BLK // 32, BLK)
        return carry

    lax.fori_loop(0, ROW_TILES, out_grad, 0)
    to_core.append(push(go_ref.at[:, 1 - c], core_o, core_send.at[5], core_recv.at[5], across("c")))

    def near_rows(row):
        to_near[1 + row].wait_recv()

        def near_chip(chip, carry):
            half_in[row, chip, g] = (half_in[row, chip, g].astype(f32) + near_in[row, chip].astype(f32)).astype(bf16)
            return carry

        lax.fori_loop(0, CHIPS, near_chip, 0)
        for which in range(2):
            spread(
                half_in.at[row], pl.ds(which * BLK, BLK), base + (which * ROW_TILES + row) * FF_TILES + me, 2 * row + which
            )

    near_rows(0)
    to_core[5].wait_recv()
    core_o[...] = (core_o[...].astype(f32) + go_ref[:, c].astype(f32)).astype(bf16)
    to_near.append(push(core_o.at[:, 1 - g], in_o, near_send.at[4], near_recv.at[4], across("g")))
    scatter3.last()
    near_rows(1)
    near_rows(2)
    dxn_ref[0:half] = scatter3.finish(0)
    dxn_ref[half:] = scatter3.finish(1)

    def three_tiles(at, values):
        for col in range(ROW_TILES):
            tiles_ref[at + col] = values[:, col * BLK : (col + 1) * BLK].astype(bf16)

    to_near[4].wait_recv()
    for row in range(ROW_TILES):
        three_tiles(3 * ROW_TILES**2 + row * ROW_TILES, in_o[row].astype(f32) + core_o[row, g].astype(f32))
    for copy in tiles_sent:
        copy.wait_recv()
    for row in range(ROW_TILES):
        sums = [in_q[chip, row].astype(f32) + in_q[CHIPS + chip, row].astype(f32) for chip in range(CHIPS)]
        for which in range(3):
            three_tiles(
                which * ROW_TILES**2 + row * ROW_TILES,
                jnp.concatenate([part[:, which * 2 * DH : (which + 1) * 2 * DH] for part in sums], axis=1),
            )
    tiles_ref[tiles_ref.shape[0] - 1] = jnp.zeros(tiles_ref.shape[1:], bf16)

    def grad_left(step, carry):
        grad_copy(lax.rem(me + step, seqs)).wait_send()
        return carry

    lax.fori_loop(1, seqs, grad_left, 0)
    gather.drain()
    scatter3.drain()
    for copy in strips_sent + to_core + to_near + tiles_sent:
        copy.wait_send()


def chip_at(mask):
    return {axis: 1 - lax.axis_index(axis) for axis in BITS if mask & BITS[axis]}


def wide_at(mask):
    at = chip_at(mask & 7)
    if mask & 8:
        at["g"] = 1 - lax.axis_index("g")
    return at


def run_middle(
    lengths, mix, hn, dy, xn, w_in, w_dn, w_qkv, dy_own, hmid, gain_ffn, w_o, qkv, toep, gain, scores, weights, outs, strips
):
    seqs, rows, _ = hn.shape
    dma = pltpu.SemaphoreType.DMA
    part = BLK // 32
    tiles = 4 * ROW_TILES**2 + 3 * ROW_TILES * FF_TILES
    shapes = [
        ((seqs, rows, BLK), bf16), ((rows, D), f32), ((rows, D), f32), ((1, D), f32), ((2 * CQ * CK, rows), f32),
        ((8, rows), f32), ((1, 2 * HP), f32), ((tiles + 1, part, BLK), bf16),
    ]

    def low(*dims):
        return pltpu.VMEM(dims, bf16)

    every, heads = low(CHIPS, rows, D), low(CHIPS, rows, 2 * DH)
    return pl.pallas_call(
        middle_body,
        in_specs=[SMEM] * 2 + [ANYS] * 3 + [VMEM] * 14,
        out_specs=[VMEM] * len(shapes),
        out_shape=[jax.ShapeDtypeStruct(*shape) for shape in shapes],
        scratch_shapes=[
            pltpu.VMEM((2, rows, CQ * rows), f32), pltpu.VMEM((rows + 8, rows), f32), every, every, low(seqs, rows, 2 * BLK), every, low(rows, D), heads, heads, heads,
            low(ROW_TILES, 2, CHIPS, 2, part, 2 * BLK), low(2, CHIPS, 2, part, D),
            low(ROW_TILES, CHIPS, 2, part, 2 * BLK), low(CHIPS, 2, part, D),
            low(ROW_TILES, CHIPS, part, 2 * BLK), low(CHIPS, part, D),
            low(seqs, rows, 6 * DH), low(ROW_TILES, 2, CHIPS, 2, part, 6 * DH), low(ROW_TILES, 2, 2, part, D),
            low(ROW_TILES, CHIPS, 2, part, 6 * DH), low(ROW_TILES, 2, part, D),
            low(2 * CHIPS, ROW_TILES, part, 6 * DH), low(ROW_TILES, part, D),
            low(3, rows, D), low(rows, D), low(3, rows, D), dma((1,)), dma((9,)),
        ] + [dma((8,))] * 4 + [dma((6,))] * 2 + [dma((5,))] * 2 + [dma((9 * CHIPS,))] * 2 + [dma((16,))] * 2
        + scatter_scratch(rows, D) + [dma((3,))] * 2 + [dma((3, 2))] * 4 + side_sems(),
        name="middle",
        compiler_params=pltpu.CompilerParams(collective_id=3, has_side_effects=True, vmem_limit_bytes=63 * 2**20),
    )(
        lengths, mix, hn, dy, xn, w_in, w_dn, w_qkv, dy_own, hmid, gain_ffn, w_o,
        qkv, toep, gain, scores, weights, outs, strips,
    )


def to_slots_body(
    pick_ref, tiles_ref, vec_ref, inner_ref, w_dn_ref, hmid_ref, out_ref, vecs_ref, layer_ref,
    slots_ref, parts_ref, local_sems, send, recv, vec_send, vec_recv, *scatter_args,
):
    devices = lax.axis_size(ALL)
    own_slots, side = out_ref.shape[:2]
    part = slots_ref.shape[1]

    def fill(at, carry):
        slots_ref[at] = tiles_ref[pick_ref[at]]
        return carry

    lax.fori_loop(0, slots_ref.shape[0], fill, 0)
    me = device_index()
    place = (lax.axis_index("c") * CHIPS + chip_index()) * 2 + lax.axis_index("g")
    rows = pl.ds(pl.multiple_of(place * part, part), part)
    local = [pltpu.make_async_copy(vec_ref.at[me], vecs_ref.at[me], local_sems.at[0])]
    for slot in range(own_slots):
        local.append(
            pltpu.make_async_copy(
                slots_ref.at[me * own_slots + slot], out_ref.at[slot, rows], local_sems.at[1 + slot]
            )
        )
    for copy in local:
        copy.start()
    greet_all()

    def push_all(step, carry):
        to = lax.rem(me + step, devices)
        pltpu.make_async_remote_copy(
            src_ref=vec_ref.at[to], dst_ref=vecs_ref.at[me], send_sem=vec_send, recv_sem=vec_recv, device_id=device_at(to)
        ).start()
        for slot in range(own_slots):
            pltpu.make_async_remote_copy(
                src_ref=slots_ref.at[to * own_slots + slot], dst_ref=out_ref.at[slot, rows],
                send_sem=send, recv_sem=recv, device_id=device_at(to),
            ).start()
        return carry

    lax.fori_loop(1, devices, push_all, 0)

    seqs, length = inner_ref.shape[:2]

    def outputs(at, carry):
        two = pl.ds(at * 2, 2)
        made = dot(inner_ref[two].reshape(2 * length, BLK), w_dn_ref[...])
        parts_ref[two] = made.astype(bf16).reshape(2, length, D)
        return carry

    lax.fori_loop(0, seqs // 2, outputs, 0)
    scatter = SideScatter(parts_ref, *scatter_args)
    scatter.start()
    scatter.onward()
    scatter.last()
    layer_ref[...] = (hmid_ref[...] + scatter.finish()).astype(bf16)
    scatter.drain()
    others = vecs_ref.at[pl.ds(0, devices - 1)]
    pltpu.make_async_copy(others, others, vec_recv).wait()
    pltpu.make_async_copy(others, others, vec_send).wait()
    others = out_ref.at[:, pl.ds(0, side - part)]
    pltpu.make_async_copy(others, others, recv).wait()
    pltpu.make_async_copy(others, others, send).wait()
    for copy in local:
        copy.wait()


def to_slots(pick, tiles, vecs, inner, w_dn, hmid, own_slots):
    rows = hmid.shape[0]
    dma = pltpu.SemaphoreType.DMA
    return pl.pallas_call(
        to_slots_body,
        in_specs=[SMEM, VMEM, ANYS] + [VMEM] * 3,
        out_specs=[ANYS] * 2 + [VMEM],
        out_shape=[
            jax.ShapeDtypeStruct((own_slots, BLK, BLK), bf16), jax.ShapeDtypeStruct(vecs.shape, vecs.dtype),
            jax.ShapeDtypeStruct(hmid.shape, bf16),
        ],
        scratch_shapes=[
            pltpu.VMEM((pick.shape[0],) + tiles.shape[1:], bf16), pltpu.VMEM((CHIPS, rows, D), bf16), dma((1 + own_slots,)),
        ] + [dma] * 4 + side_scatter_scratch(rows, D),
        name="to_slots",
        compiler_params=pltpu.CompilerParams(collective_id=6, has_side_effects=True, vmem_limit_bytes=32 * 2**20),
    )(pick, tiles, vecs, inner, w_dn, hmid)


def update_body(grad_ref, left_ref, right_ref, master_ref, first_ref, second_ref, first_out, second_out, master_out, copy_out):
    left, right = left_ref[0].astype(bf16), right_ref[0].astype(bf16)
    rotated = dot(dot_tn(left, grad_ref[0]).astype(bf16), right)
    first = beta_first * first_ref[0] + (1.0 - beta_first) * rotated
    second = beta_second * second_ref[0] + (1.0 - beta_second) * rotated * rotated
    first_out[0] = first
    second_out[0] = second
    direction = (first / (jnp.sqrt(second) + eps_adam)).astype(bf16)
    turned = dot_nt(dot(left, direction).astype(bf16), right)
    master = master_ref[0]
    master = master - rate_block * (turned + decay_block * master)
    master_out[0] = master
    copy_out[0] = master.astype(bf16)


def update(grad, left, right, master, first, second):
    spec = pl.BlockSpec((1, BLK, BLK), lambda slot: (slot, 0, 0))
    return pl.pallas_call(
        update_body,
        grid=(grad.shape[0],),
        in_specs=[spec] * 6,
        out_specs=[spec] * 4,
        out_shape=[jax.ShapeDtypeStruct(grad.shape, kind) for kind in (f32, f32, f32, bf16)],
        name="update",
        compiler_params=pltpu.CompilerParams(vmem_limit_bytes=40 * 2**20),
        cost_estimate=pl.CostEstimate(flops=43 * 10**8, bytes_accessed=36 * 2**20, transcendentals=10**6),
    )(grad, left, right, master, first, second)


def body_fast(
    layer_input, lengths, cotangent, w_query, w_key, w_value, w_out, w_gate, w_up, w_down, vec_copy, owners,
    basis_left, basis_right, block_master, block_first, block_second, vec_master, vec_first, vec_second,
):
    chip = chip_index()
    seq_len = layer_input.shape[0]
    length = lengths[0]
    own_vec = vec_copy.shape[0]
    devices, fs_size, reps = lax.axis_size(ALL), lax.axis_size(FS), lax.axis_size("y")

    small = jnp.concatenate(
        [vec_copy.astype(f32), jnp.zeros((1023 - own_vec,), f32), length.astype(f32).reshape(1)]
    ).reshape(8, 128)
    blocks = jnp.concatenate([w.reshape(-1, CHIPS, 2 * DH) for w in (w_query, w_key, w_value)], axis=2)
    small_all = gather_vectors(small)
    small_all = small_all.reshape(fs_size, reps, 1024)
    vector = small_all[:, 0, :own_vec].reshape(-1)
    group_lengths = small_all[:, :, 1023].reshape(-1, 2, 2, 2, reps)
    group_lengths = lax.dynamic_index_in_dim(group_lengths, lax.axis_index("g"), 0, keepdims=False)
    group_lengths = lax.dynamic_index_in_dim(group_lengths, lax.axis_index("c"), 2, keepdims=False)
    group_lengths = jnp.transpose(group_lengths, (2, 0, 1)).reshape(CHIPS).astype(jnp.int32)
    gain_attn, gain_head, gain_ffn = vector[:D], vector[D : 2 * D], vector[2 * D : 3 * D]
    conv_end = 3 * D + H * CQ * CK
    theta = lax.dynamic_slice_in_dim(vector[3 * D : conv_end].reshape(H, CQ, CK), chip * 2, 2, 0)
    mixer = lax.dynamic_slice_in_dim(vector[conv_end : conv_end + 2 * H].reshape(H, 2), chip * 2, 2, 0)
    mix = mixer.reshape(4)
    gain_pair = jnp.pad(
        lax.dynamic_slice_in_dim(gain_head.reshape(H, DH), chip * 2, 2, 0), ((0, 0), (0, HP - DH))
    ).reshape(1, 2 * HP)
    toep = jnp.zeros((2, CQ, seq_len, seq_len), f32)
    offset = (
        jnp.arange(seq_len, dtype=jnp.int32)[:, None] - jnp.arange(seq_len, dtype=jnp.int32)[None, :] + CK // 2
    )
    for tap in range(CK):
        toep = jnp.where(offset[None, None] == tap, theta[:, :, tap][:, :, None, None], toep)
    toep = toep.astype(bf16).reshape(2, CQ * seq_len, seq_len)
    valid = (jnp.arange(seq_len) < length).astype(f32)
    dy = cotangent.astype(f32) * valid[:, None]

    gains = jnp.concatenate([gain_attn[None], gain_ffn[None], jnp.zeros((6, D), f32)], axis=0)
    xn, qkv, scores, weights, outs, heads, hmid, w_qkv, w_out_all, hn_rows, w_in, w_dn, dy_rows = run_front(
        group_lengths, mix, layer_input, gains, toep, gain_pair, jnp.transpose(blocks, (1, 0, 2)),
        w_out, w_gate, w_up, w_down, dy.astype(bf16),
    )
    w_qkv = w_qkv.reshape(D, 6 * DH)
    w_in, w_dn = w_in.reshape(D, 2 * BLK), w_dn.reshape(BLK, D)
    strip = BLK // (2 * CHIPS)
    part = strip // 2
    heads = jnp.transpose(heads, (1, 0, 2)).reshape(seq_len, 2 * ROW_TILES, CHIPS, strip)
    strips = jnp.transpose(heads, (2, 0, 1, 3)).reshape(CHIPS, seq_len, 2 * ROW_TILES * strip)
    input_float = layer_input.astype(f32)
    input_scale = rms(input_float)

    own_slots = basis_left.shape[0]
    matches = jnp.arange(own_slots * devices)[:, None] == owners[None, :]
    tile_count = owners.shape[0]
    pick = jnp.min(jnp.where(matches, jnp.arange(tile_count, dtype=jnp.int32)[None, :], tile_count), axis=1)
    inner, dhmid, dxn, grad_gain_ffn, theta_sums, mixer_sums, gain_sums, tiles = run_middle(
        group_lengths, mix, hn_rows, dy_rows, xn, w_in, w_dn, w_qkv, dy.astype(bf16), hmid, gain_ffn.reshape(1, D),
        w_out_all.reshape(CHIPS, 2 * DH, D), qkv, toep, gain_pair, scores, weights, outs, strips,
    )
    dinput, grad_gain_attn = norm_backward(input_float, input_scale, gain_attn, dxn)
    input_grad = dinput + dhmid

    grad_theta = jnp.sum(theta_sums, axis=1)
    grad_mixer = jnp.sum(mixer_sums[:4], axis=1)
    vector_grad = jnp.concatenate(
        [
            grad_gain_attn,
            lax.dynamic_update_slice_in_dim(
                jnp.zeros((D,), f32), gain_sums.reshape(2, HP)[:, :DH].reshape(-1), chip * 2 * DH, 0
            ),
            grad_gain_ffn.reshape(-1),
            lax.dynamic_update_slice_in_dim(
                jnp.zeros((H * CQ * CK,), f32), grad_theta.reshape(-1), chip * 2 * CQ * CK, 0
            ),
            lax.dynamic_update_slice_in_dim(jnp.zeros((2 * H,), f32), grad_mixer, chip * 4, 0),
        ]
    )
    pieces = jnp.pad(vector_grad.reshape(fs_size, 1, own_vec), ((0, 0), (0, 0), (0, 1024 - own_vec)))
    pieces = jnp.broadcast_to(pieces, (fs_size, reps, 1024)).reshape(devices, 8, 128)

    own_grad, pieces, layer_output = to_slots(
        pick, tiles, pieces, inner, w_dn, hmid, own_slots
    )
    vector_total = jnp.sum(pieces, axis=0).reshape(1024)[:own_vec]
    first_new, second_new, master_new, copy_new = update(
        own_grad, basis_left, basis_right, block_master, block_first, block_second
    )
    vec_first_new = beta_first * vec_first + (1.0 - beta_first) * vector_total
    vec_second_new = beta_second * vec_second + (1.0 - beta_second) * vector_total * vector_total
    vec_master_new = vec_master - rate_vector * vec_first_new / (jnp.sqrt(vec_second_new) + eps_adam)
    return (
        layer_output, input_grad, first_new, second_new, master_new, copy_new,
        vec_first_new, vec_second_new, vec_master_new, vec_master_new.astype(bf16),
    )


def solution(mesh):
    fsdp, rep = mesh.shape["fsdp"], mesh.shape["rep"]
    fine = Mesh(mesh.devices.reshape(fsdp // 8, 2, 2, 2, rep), ALL)
    rows, both = P(ALL, None), P(ALL, None, None)
    weight, vec = P(FS, None), P(FS)
    return jax.shard_map(
        body_fast if (fsdp, rep) == (16, 2) else body_any,
        mesh=fine,
        in_specs=(rows, P(ALL), rows) + (weight,) * 7 + (vec, P()) + (both,) * 5 + (vec,) * 3,
        out_specs=(rows, rows) + (both,) * 4 + (vec,) * 4,
        check_vma=False,
    )
```

```python
import functools
import math

import jax
import jax.numpy as jnp
import numpy as np
from jax import lax
from jax.experimental import pallas as pl
from jax.experimental.pallas import tpu as pltpu
from jax.sharding import Mesh
from jax.sharding import PartitionSpec as P

H = 16
DH = 96
HP = 128
D = H * DH
FF = 4096
CQ = 6
CK = 11
BLK = 512
CHIPS = 8
ROW_TILES = D // BLK
FF_TILES = FF // BLK

eps_norm = 1e-05
eps_adam = 1e-08
rate_block = 0.02
rate_vector = 0.3
decay_block = 0.1
beta_first = 0.5
beta_second = 0.5

FS = ("g", "a", "b", "c")
CHIP = ("y", "a", "b")
ALL = ("g", "a", "b", "c", "y")
bf16 = jnp.bfloat16
f32 = jnp.float32


def dot(left, right):
    return jnp.dot(left, right, preferred_element_type=f32)


def dot_nt(left, right):
    return lax.dot_general(left, right, (((1,), (1,)), ((), ())), preferred_element_type=f32)


def dot_tn(left, right):
    return lax.dot_general(left, right, (((0,), (0,)), ((), ())), preferred_element_type=f32)


def rms(values):
    return lax.rsqrt(jnp.mean(values * values, axis=-1, keepdims=True) + eps_norm)


def norm_backward(values, scale, gain, grad):
    unit = values * scale
    inner = grad * gain
    grad_values = scale * (inner - unit * jnp.mean(inner * unit, axis=-1, keepdims=True))
    return grad_values, jnp.sum(grad * unit, axis=0)


def shifted_down(pad_ref, values):
    rows = values.shape[0]
    pad_ref[8 : 8 + rows, :] = values
    return jnp.concatenate(
        [values] + [pad_ref[8 - lag : 8 - lag + rows, :] for lag in range(1, CQ)], axis=1
    )


def shifted_up(pad_ref, values):
    rows = values.shape[0]
    pad_ref[0:rows, :] = values
    return jnp.concatenate(
        [values] + [pad_ref[lag : lag + rows, :] for lag in range(1, CQ)], axis=1
    )


def attention_forward(len_ref, mix_ref, qkv_ref, toep_ref, gain_ref, heads_ref, s_ref, p_ref, o_ref, pad_ref):
    rows = qkv_ref.shape[1]
    length = len_ref[pl.program_id(0)]
    query_at = lax.broadcasted_iota(jnp.int32, (rows, rows), 0)
    key_at = lax.broadcasted_iota(jnp.int32, (rows, rows), 1)
    keep = (key_at <= query_at) & (key_at < length)
    pad_ref[0:8, :] = jnp.zeros((8, rows), f32)
    weights = []
    for head in range(2):
        query = qkv_ref[0, :, head * HP : (head + 1) * HP]
        key = qkv_ref[0, :, (2 + head) * HP : (3 + head) * HP]
        scores = jnp.where(keep, dot_nt(query, key) * (1.0 / math.sqrt(DH)), 0.0)
        s_ref[0, head] = scores.astype(bf16)
        wide = shifted_down(pad_ref, scores)
        high = wide.astype(bf16)
        low = (wide - high.astype(f32)).astype(bf16)
        conv = dot(high, toep_ref[head]) + dot(low, toep_ref[head])
        logits = jnp.where(keep, conv, -1e30)
        weight = jnp.exp(logits - jnp.max(logits, axis=-1, keepdims=True))
        weight = weight / jnp.sum(weight, axis=-1, keepdims=True)
        p_ref[0, head] = weight
        weights.append(weight)
    for head in range(2):
        mixed = mix_ref[2 * head] * weights[0] + mix_ref[2 * head + 1] * weights[1]
        value = qkv_ref[0, :, (4 + head) * HP : (5 + head) * HP]
        out = dot(mixed.astype(bf16), value)
        o_ref[0, :, head * HP : (head + 1) * HP] = out
        scale = lax.rsqrt(jnp.sum(out * out, axis=-1, keepdims=True) * (1.0 / DH) + eps_norm)
        heads_ref[0, :, head * HP : (head + 1) * HP] = (
            out * scale * gain_ref[:, head * HP : (head + 1) * HP]
        ).astype(bf16)


def attention_backward(
    len_ref, mix_ref, qkv_ref, toep_ref, gain_ref, s_ref, p_ref, o_ref, grad_ref,
    dqkv_ref, theta_ref, mixer_ref, gain_grad_ref, pad_ref,
):
    rows = qkv_ref.shape[1]
    length = len_ref[pl.program_id(0)]
    query_at = lax.broadcasted_iota(jnp.int32, (rows, rows), 0)
    key_at = lax.broadcasted_iota(jnp.int32, (rows, rows), 1)
    keep = (key_at <= query_at) & (key_at < length)
    pad_ref[rows : rows + 8, :] = jnp.zeros((8, rows), f32)

    @pl.when(pl.program_id(0) == 0)
    def _():
        theta_ref[...] = jnp.zeros_like(theta_ref)
        mixer_ref[...] = jnp.zeros_like(mixer_ref)
        gain_grad_ref[...] = jnp.zeros_like(gain_grad_ref)

    weights = [p_ref[0, 0], p_ref[0, 1]]
    grad_mixed = []
    for head in range(2):
        cols = slice(head * HP, (head + 1) * HP)
        out = o_ref[0, :, cols]
        grad = grad_ref[0, :, cols].astype(f32)
        scale = lax.rsqrt(jnp.sum(out * out, axis=-1, keepdims=True) * (1.0 / DH) + eps_norm)
        unit = out * scale
        gain_grad_ref[:, cols] += jnp.sum(grad * unit, axis=0, keepdims=True)
        inner = grad * gain_ref[:, cols]
        grad_out = scale * (inner - unit * (jnp.sum(inner * unit, axis=-1, keepdims=True) * (1.0 / DH)))
        grad_out = grad_out.astype(bf16)
        value = qkv_ref[0, :, (4 + head) * HP : (5 + head) * HP]
        mixed = (mix_ref[2 * head] * weights[0] + mix_ref[2 * head + 1] * weights[1]).astype(bf16)
        dqkv_ref[0, :, (4 + head) * HP : (5 + head) * HP] = dot_tn(mixed, grad_out).astype(bf16)
        back = dot_nt(grad_out, value)
        grad_mixed.append(back)
        for source in range(2):
            mixer_ref[2 * head + source : 2 * head + source + 1, :] += jnp.sum(
                back * weights[source], axis=0, keepdims=True
            )
    for head in range(2):
        grad_weight = mix_ref[head] * grad_mixed[0] + mix_ref[2 + head] * grad_mixed[1]
        weight = weights[head]
        grad_conv = weight * (grad_weight - jnp.sum(weight * grad_weight, axis=-1, keepdims=True))
        wide = shifted_up(pad_ref, grad_conv).astype(bf16)
        theta_ref[head] += dot_tn(s_ref[0, head], wide)
        grad_scores = jnp.zeros((rows, rows), f32)
        for lag in range(CQ):
            grad_scores += dot_nt(
                wide[:, lag * rows : (lag + 1) * rows], toep_ref[head, lag * rows : (lag + 1) * rows, :]
            )
        grad_scores = jnp.where(keep, grad_scores * (1.0 / math.sqrt(DH)), 0.0).astype(bf16)
        query = qkv_ref[0, :, head * HP : (head + 1) * HP]
        key = qkv_ref[0, :, (2 + head) * HP : (3 + head) * HP]
        dqkv_ref[0, :, head * HP : (head + 1) * HP] = dot(grad_scores, key).astype(bf16)
        dqkv_ref[0, :, (2 + head) * HP : (3 + head) * HP] = dot_tn(grad_scores, query).astype(bf16)


SMEM = pl.BlockSpec(memory_space=pltpu.SMEM)


def seq_spec(*dims):
    return pl.BlockSpec((1,) + dims, lambda s: (s,) + (0,) * len(dims))


def whole_spec(*dims):
    return pl.BlockSpec(dims, lambda s: (0,) * len(dims))


def run_forward(lengths, mix, qkv, toep, gain):
    seqs, rows, _ = qkv.shape
    return pl.pallas_call(
        attention_forward,
        grid=(seqs,),
        in_specs=[SMEM, SMEM, seq_spec(rows, 6 * HP), whole_spec(2, CQ * rows, rows), whole_spec(1, 2 * HP)],
        out_specs=[seq_spec(rows, 2 * HP), seq_spec(2, rows, rows), seq_spec(2, rows, rows), seq_spec(rows, 2 * HP)],
        out_shape=[
            jax.ShapeDtypeStruct((seqs, rows, 2 * HP), bf16),
            jax.ShapeDtypeStruct((seqs, 2, rows, rows), bf16),
            jax.ShapeDtypeStruct((seqs, 2, rows, rows), f32),
            jax.ShapeDtypeStruct((seqs, rows, 2 * HP), f32),
        ],
        scratch_shapes=[pltpu.VMEM((rows + 8, rows), f32)],
        name="attention_forward",
        compiler_params=pltpu.CompilerParams(vmem_limit_bytes=24 * 2**20),
        cost_estimate=pl.CostEstimate(flops=2 * 10**9, bytes_accessed=8 * 2**20, transcendentals=10**5),
    )(lengths, mix, qkv, toep, gain)


def run_backward(lengths, mix, qkv, toep, gain, scores, weights, outs, grads):
    seqs, rows, _ = qkv.shape
    return pl.pallas_call(
        attention_backward,
        grid=(seqs,),
        in_specs=[
            SMEM, SMEM, seq_spec(rows, 6 * HP), whole_spec(2, CQ * rows, rows), whole_spec(1, 2 * HP),
            seq_spec(2, rows, rows), seq_spec(2, rows, rows), seq_spec(rows, 2 * HP), seq_spec(rows, 2 * HP),
        ],
        out_specs=[seq_spec(rows, 6 * HP), whole_spec(2, rows, CQ * rows), whole_spec(8, rows), whole_spec(1, 2 * HP)],
        out_shape=[
            jax.ShapeDtypeStruct((seqs, rows, 6 * HP), bf16),
            jax.ShapeDtypeStruct((2, rows, CQ * rows), f32),
            jax.ShapeDtypeStruct((8, rows), f32),
            jax.ShapeDtypeStruct((1, 2 * HP), f32),
        ],
        scratch_shapes=[pltpu.VMEM((rows + 8, rows), f32)],
        name="attention_backward",
        compiler_params=pltpu.CompilerParams(vmem_limit_bytes=24 * 2**20),
        cost_estimate=pl.CostEstimate(flops=4 * 10**9, bytes_accessed=12 * 2**20, transcendentals=10**5),
    )(lengths, mix, qkv, toep, gain, scores, weights, outs, grads)


BITS = {"y": 4, "a": 2, "b": 1}
HOPS = (("y", "b", "a"), ("a", "y", "b"), ("b", "a", "y"))
THIRDS = ((0, 48), (48, 48), (96, 32))
ANYS = pl.BlockSpec(memory_space=pl.ANY)


def chip_index():
    return (lax.axis_index("y") * 2 + lax.axis_index("a")) * 2 + lax.axis_index("b")


def flipped(chip, axes):
    for axis in axes:
        chip = chip + BITS[axis] * (1 - 2 * lax.axis_index(axis))
    return chip


def across(axis):
    return {axis: 1 - lax.axis_index(axis)}


def device_index():
    index = lax.axis_index("g")
    for axis in ("a", "b", "c", "y"):
        index = index * lax.axis_size(axis) + lax.axis_index(axis)
    return index


def device_at(index):
    at = {}
    for axis in ("y", "c", "b", "a", "g"):
        at[axis] = lax.rem(index, lax.axis_size(axis))
        index = lax.div(index, lax.axis_size(axis))
    return at


def greet_all():
    devices = lax.axis_size(ALL)
    me = device_index()
    barrier = pltpu.get_barrier_semaphore()

    def greet(step, carry):
        pl.semaphore_signal(barrier, inc=1, device_id=device_at(lax.rem(me + step, devices)))
        return carry

    lax.fori_loop(1, devices, greet, 0)
    pl.semaphore_wait(barrier, devices - 1)


def greet_neighbours():
    barrier = pltpu.get_barrier_semaphore()
    for axis in BITS:
        pl.semaphore_signal(barrier, inc=1, device_id=across(axis))
    pl.semaphore_wait(barrier, 3)


def remote(src, dst, send, recv, axis):
    return pltpu.make_async_remote_copy(src_ref=src, dst_ref=dst, send_sem=send, recv_sem=recv, device_id=across(axis))


def gather_body(x_ref, out_ref, *sems):
    greet_neighbours()
    gather_hops(x_ref, out_ref, *sems)


def gather_first_body(x_ref, vec_ref, out_ref, vecs_ref, vec_send, vec_recv, vec_local, *sems):
    devices = lax.axis_size(ALL)
    me = device_index()
    local = pltpu.make_async_copy(vec_ref, vecs_ref.at[me], vec_local)
    local.start()
    greet_all()

    def push(step, carry):
        pltpu.make_async_remote_copy(
            src_ref=vec_ref, dst_ref=vecs_ref.at[me], send_sem=vec_send, recv_sem=vec_recv,
            device_id=device_at(lax.rem(me + step, devices)),
        ).start()
        return carry

    lax.fori_loop(1, devices, push, 0)
    gather_hops(x_ref, out_ref, *sems)
    others = vecs_ref.at[pl.ds(0, devices - 1)]
    pltpu.make_async_copy(others, others, vec_recv).wait()
    pltpu.make_async_copy(others, others, vec_send).wait()
    local.wait()


def gather_hops(x_ref, out_ref, local_sem, send1, recv1, send2, recv2, send3, recv3):
    me = chip_index()
    rows = x_ref.shape[0]
    half = rows // 2
    local = pltpu.make_async_copy(x_ref, out_ref.at[me], local_sem)
    local.start()
    first = []
    for part in range(2):
        here = pl.ds(part * half, half)
        for at, (axis, _, _) in enumerate(HOPS):
            copy = remote(x_ref.at[here], out_ref.at[me, here], send1.at[at, part], recv1.at[at, part], axis)
            copy.start()
            first.append(copy)
    second = []
    for part in range(2):
        here = pl.ds(part * half, half)
        for at, (axis, onward, _) in enumerate(HOPS):
            first[part * 3 + at].wait_recv()
            block = out_ref.at[flipped(me, (axis,)), here]
            copy = remote(block, block, send2.at[at, part], recv2.at[at, part], onward)
            copy.start()
            second.append(copy)
    third = []
    for at, (axis, onward, last) in enumerate(HOPS):
        begin, count = THIRDS[at]
        block = flipped(me, (axis, onward))
        for part in range(2):
            if part * half < begin + count and begin < (part + 1) * half:
                second[part * 3 + at].wait_recv()
        piece = out_ref.at[block, pl.ds(begin, count)]
        copy = remote(piece, piece, send3.at[at], recv3.at[at], last)
        copy.start()
        third.append(copy)
    for at in range(3):
        begin, count = THIRDS[at]
        for part in range(2):
            if not (part * half < begin + count and begin < (part + 1) * half):
                second[part * 3 + at].wait_recv()
    for copy in third:
        copy.wait_recv()
    for copy in first + second + third:
        copy.wait_send()
    local.wait()


def hop_sems():
    dma = pltpu.SemaphoreType.DMA
    return [dma] + [dma((3, 2))] * 4 + [dma((3,))] * 2


def gather_first(rows, vec, collective_id):
    count, width = rows.shape
    return pl.pallas_call(
        gather_first_body,
        in_specs=[ANYS, ANYS],
        out_specs=[ANYS, ANYS],
        out_shape=[
            jax.ShapeDtypeStruct((CHIPS, count, width), rows.dtype),
            jax.ShapeDtypeStruct((lax.axis_size(ALL),) + vec.shape, vec.dtype),
        ],
        scratch_shapes=[pltpu.SemaphoreType.DMA] * 3 + hop_sems(),
        name="gather_first",
        compiler_params=pltpu.CompilerParams(collective_id=collective_id, has_side_effects=True),
    )(rows, vec)


def gather_chips(rows, collective_id):
    count, width = rows.shape
    return pl.pallas_call(
        gather_body,
        in_specs=[ANYS],
        out_specs=ANYS,
        out_shape=jax.ShapeDtypeStruct((CHIPS, count, width), rows.dtype),
        scratch_shapes=hop_sems(),
        name="gather_chips",
        compiler_params=pltpu.CompilerParams(collective_id=collective_id, has_side_effects=True),
    )(rows)


def scatter_body(
    parts_ref, out_ref, near_ref, in2_ref, in3_ref, acc2_ref, acc3_ref, send1, recv1, send2, recv2, send3, recv3
):
    me = chip_index()
    greet_neighbours()
    opposite = flipped(me, ("y", "a", "b"))
    first = []
    for at, (axis, onward, last) in enumerate(HOPS):
        begin, count = THIRDS[at]
        copy = remote(parts_ref.at[opposite, pl.ds(begin, count)], in2_ref.at[pl.ds(begin, count)], send1.at[at], recv1.at[at], last)
        copy.start()
        first.append(copy)
    second = []
    rows = parts_ref.shape[1]
    half = rows // 2
    for part in range(2):
        here = pl.ds(part * half, half)
        for at, (axis, onward, last) in enumerate(HOPS):
            dest = flipped(me, (axis, onward))
            begin, count = THIRDS[at]
            if part == 0:
                first[at].wait_recv()
                acc2_ref[at] = parts_ref[dest]
                piece = pl.ds(begin, count)
                acc2_ref[at, piece] = (parts_ref[dest, piece].astype(f32) + in2_ref[piece].astype(f32)).astype(bf16)
            copy = remote(acc2_ref.at[at, here], in3_ref.at[at, here], send2.at[at, part], recv2.at[at, part], onward)
            copy.start()
            second.append(copy)
    third = []
    for part in range(2):
        here = pl.ds(part * half, half)
        for at, (axis, onward, last) in enumerate(HOPS):
            dest = flipped(me, (axis,))
            second[part * 3 + at].wait_recv()
            acc3_ref[at, here] = (parts_ref[dest, here].astype(f32) + in3_ref[at, here].astype(f32)).astype(bf16)
            copy = remote(acc3_ref.at[at, here], near_ref.at[at, here], send3.at[at, part], recv3.at[at, part], axis)
            copy.start()
            third.append(copy)
    for part in range(2):
        here = pl.ds(part * half, half)
        for at in range(3):
            third[part * 3 + at].wait_recv()
        out_ref[here] = (
            (parts_ref[me, here].astype(f32) + near_ref[0, here].astype(f32))
            + (near_ref[1, here].astype(f32) + near_ref[2, here].astype(f32))
        )
    for copy in first + second + third:
        copy.wait_send()


def scatter_chips(parts, collective_id):
    _, rows, width = parts.shape
    vmem = pl.BlockSpec(memory_space=pltpu.VMEM)
    dma = pltpu.SemaphoreType.DMA
    return pl.pallas_call(
        scatter_body,
        in_specs=[vmem],
        out_specs=vmem,
        out_shape=jax.ShapeDtypeStruct((rows, width), f32),
        scratch_shapes=[pltpu.VMEM((3, rows, width), bf16), pltpu.VMEM((rows, width), bf16)] + [pltpu.VMEM((3, rows, width), bf16)] * 3
        + [dma((3,))] * 2 + [dma((3, 2))] * 4,
        name="scatter_chips",
        compiler_params=pltpu.CompilerParams(collective_id=collective_id, has_side_effects=True, vmem_limit_bytes=32*2**20),
    )(parts)


def gather_slow(rows):
    return lax.all_to_all(
        jnp.broadcast_to(rows[None], (CHIPS,) + rows.shape), CHIP, split_axis=0, concat_axis=0, tiled=True
    )


def exchange_chips(parts):
    return lax.all_to_all(parts, CHIP, split_axis=0, concat_axis=0, tiled=True)


def scatter_slow(parts):
    return jnp.sum(exchange_chips(parts.astype(bf16)).astype(f32), axis=0)


def swap(values, axis):
    return lax.ppermute(values, axis, [(0, 1), (1, 0)])


def both_cores(own, axis):
    other = swap(own, "c")
    first = lax.axis_index("c") == 0
    return jnp.stack([jnp.where(first, own, other), jnp.where(first, other, own)], axis=axis)


def half_for_core(values, axis):
    core = lax.axis_index("c")
    own = lax.dynamic_index_in_dim(values, core, axis, keepdims=False)
    sent = lax.dynamic_index_in_dim(values, 1 - core, axis, keepdims=False)
    return own + swap(sent.astype(bf16), "c").astype(f32)


def sum_groups(tiles):
    groups = lax.axis_size("g")
    if groups != 2:
        return lax.psum_scatter(tiles.astype(f32), "g", scatter_dimension=1, tiled=True).astype(bf16)
    part = tiles.shape[1] // 2
    group = lax.axis_index("g")
    own = lax.dynamic_slice_in_dim(tiles, group * part, part, 1)
    sent = lax.dynamic_slice_in_dim(tiles, (1 - group) * part, part, 1)
    return (own.astype(f32) + swap(sent, "g").astype(f32)).astype(bf16)


def spread_columns(weight, width):
    rows = weight.shape[0]
    blocks = weight.reshape(rows, 2, CHIPS // 2, width)
    mine = lax.dynamic_index_in_dim(blocks, lax.axis_index("y"), 1, keepdims=False)
    return jnp.transpose(mine, (1, 0, 2))


def to_columns(blocks):
    groups = lax.axis_size("g")
    sent = jnp.broadcast_to(blocks[None], (groups,) + blocks.shape).reshape((-1,) + blocks.shape[1:])
    got = lax.all_to_all(sent, ("g", "a", "b"), split_axis=0, concat_axis=0, tiled=True)
    return both_cores(got, 1).reshape(-1, blocks.shape[-1])


def down_rows(w_down, chip):
    if lax.axis_size("g") == 2:
        other = swap(w_down, "g")
        mine = jnp.where(lax.axis_index("g") == lax.axis_index("y"), w_down, other)
        return both_cores(mine, 0).reshape(BLK, D)
    return lax.dynamic_slice_in_dim(lax.all_gather(w_down, FS, axis=0, tiled=True), chip * BLK, BLK, 0)


def band():
    tap = np.arange(CK)[:, None, None]
    source = np.arange(128)[None, :, None]
    target = np.arange(128)[None, None, :]
    return source - target + CK // 2 == tap


def body_any(
    layer_input, lengths, cotangent, w_query, w_key, w_value, w_out, w_gate, w_up, w_down, vec_copy, owners,
    basis_left, basis_right, block_master, block_first, block_second, vec_master, vec_first, vec_second,
):
    chip = (lax.axis_index("y") * 2 + lax.axis_index("a")) * 2 + lax.axis_index("b")
    fs_index = ((lax.axis_index("g") * 2 + lax.axis_index("a")) * 2 + lax.axis_index("b")) * 2 + lax.axis_index("c")
    seq_len = layer_input.shape[0]
    length = lengths[0]
    reps = lax.axis_size("y")
    fs_size = lax.axis_size(FS)

    own_vec = vec_copy.shape[0]
    small = jnp.concatenate(
        [vec_copy.astype(f32), jnp.zeros((1023 - own_vec,), f32), length.astype(f32).reshape(1)]
    ).reshape(8, 128)
    x_all, small_all = gather_first(layer_input, small, 1)
    small_all = small_all.reshape(fs_size, reps, 1024)
    vector = small_all[:, 0, :own_vec].reshape(-1)
    group_lengths = small_all[:, :, 1023].reshape(-1, 2, 2, 2, reps)
    group_lengths = lax.dynamic_index_in_dim(group_lengths, lax.axis_index("g"), 0, keepdims=False)
    group_lengths = lax.dynamic_index_in_dim(group_lengths, lax.axis_index("c"), 2, keepdims=False)
    group_lengths = jnp.transpose(group_lengths, (2, 0, 1)).reshape(CHIPS).astype(jnp.int32)
    gain_attn, gain_head, gain_ffn = vector[:D], vector[D : 2 * D], vector[2 * D : 3 * D]
    conv_end = 3 * D + H * CQ * CK
    theta = lax.dynamic_slice_in_dim(vector[3 * D : conv_end].reshape(H, CQ, CK), chip * 2, 2, 0)
    mixer = lax.dynamic_slice_in_dim(vector[conv_end : conv_end + 2 * H].reshape(H, 2), chip * 2, 2, 0)
    mix = mixer.reshape(4)
    gain_pair = jnp.pad(
        lax.dynamic_slice_in_dim(gain_head.reshape(H, DH), chip * 2, 2, 0), ((0, 0), (0, HP - DH))
    ).reshape(1, 2 * HP)
    toep = jnp.zeros((2, CQ, seq_len, seq_len), f32)
    offset = (
        jnp.arange(seq_len, dtype=jnp.int32)[:, None] - jnp.arange(seq_len, dtype=jnp.int32)[None, :] + CK // 2
    )
    for tap in range(CK):
        toep = jnp.where(offset[None, None] == tap, theta[:, :, tap][:, :, None, None], toep)
    toep = toep.astype(bf16).reshape(2, CQ * seq_len, seq_len)

    qkv_rows = to_columns(
        jnp.concatenate([spread_columns(w, 2 * DH) for w in (w_query, w_key, w_value)], axis=2)
    )
    w_qkv = jnp.pad(qkv_rows.reshape(D, 6, DH), ((0, 0), (0, 0), (0, HP - DH))).reshape(D, 6 * HP)
    w_in = to_columns(jnp.concatenate([spread_columns(w, BLK) for w in (w_gate, w_up)], axis=2))
    w_dn = down_rows(w_down, chip)
    w_o = lax.all_gather(w_out, FS, axis=0, tiled=True)

    input_float = layer_input.astype(f32)
    input_scale = rms(input_float)
    x_rows = x_all.reshape(CHIPS * seq_len, D).astype(f32)
    xn_rows = (x_rows * rms(x_rows) * gain_attn).astype(bf16)
    qkv = dot(xn_rows, w_qkv).astype(bf16).reshape(CHIPS, seq_len, 6 * HP)
    heads_pad, scores, weights, outs = run_forward(group_lengths, mix, qkv, toep, gain_pair)
    heads_sent = heads_pad.reshape(CHIPS, seq_len, 2, HP)[..., :DH].reshape(CHIPS, seq_len, 2 * DH)
    heads = jnp.transpose(exchange_chips(heads_sent), (1, 0, 2)).reshape(seq_len, D)
    hmid = input_float + dot(heads, w_o)
    hmid_scale = rms(hmid)
    hn_rows = gather_chips((hmid * hmid_scale * gain_ffn).astype(bf16), 2).reshape(CHIPS * seq_len, D)
    both = dot(hn_rows, w_in)
    gate, up = both[:, :BLK], both[:, BLK:]
    sig = jax.nn.sigmoid(gate)
    silu = gate * sig
    inner = (silu * up).astype(bf16)
    ffn = scatter_slow(dot(inner, w_dn).reshape(CHIPS, seq_len, D))
    layer_output = (hmid + ffn).astype(bf16)

    valid = (jnp.arange(seq_len) < length).astype(f32)
    dy = cotangent.astype(f32) * valid[:, None]
    dy_rows = gather_slow(dy.astype(bf16)).reshape(CHIPS * seq_len, D)
    dinner = dot_nt(dy_rows, w_dn)
    dgate = (dinner * up * (sig * (1.0 + gate * (1.0 - sig)))).astype(bf16)
    dup = (dinner * silu).astype(bf16)
    dboth = jnp.concatenate([dgate, dup], axis=1)
    dhn = scatter_chips(dot_nt(dboth, w_in).astype(bf16).reshape(CHIPS, seq_len, D), 3)
    dhmid, grad_gain_ffn = norm_backward(hmid, hmid_scale, gain_ffn, dhn)
    dhmid = dhmid + dy
    dattn = dhmid.astype(bf16)
    dheads = dot_nt(dattn, w_o).astype(bf16).reshape(seq_len, CHIPS, 2 * DH)
    dheads = exchange_chips(jnp.transpose(dheads, (1, 0, 2)))
    dheads = jnp.pad(dheads.reshape(CHIPS, seq_len, 2, DH), ((0, 0), (0, 0), (0, 0), (0, HP - DH)))
    dqkv, theta_sums, mixer_sums, gain_sums = run_backward(
        group_lengths, mix, qkv, toep, gain_pair, scores, weights, outs, dheads.reshape(CHIPS, seq_len, 2 * HP)
    )
    dqkv_rows = dqkv.reshape(CHIPS * seq_len, 6 * HP)
    dxn = scatter_slow(dot_nt(dqkv_rows, w_qkv).reshape(CHIPS, seq_len, D))
    dinput, grad_gain_attn = norm_backward(input_float, input_scale, gain_attn, dxn)
    input_grad = dinput + dhmid

    taps = jnp.asarray(band())
    theta_sums = theta_sums.reshape(2, seq_len, CQ, seq_len)
    grad_theta = jnp.stack(
        [jnp.sum(jnp.where(taps[tap][None, :, None, :], theta_sums, 0.0), axis=(1, 3)) for tap in range(CK)], axis=2
    )
    grad_mixer = jnp.sum(mixer_sums[:4], axis=1)
    vector_grad = jnp.concatenate(
        [
            grad_gain_attn,
            lax.dynamic_update_slice_in_dim(
                jnp.zeros((D,), f32), gain_sums.reshape(2, HP)[:, :DH].reshape(-1), chip * 2 * DH, 0
            ),
            grad_gain_ffn,
            lax.dynamic_update_slice_in_dim(
                jnp.zeros((H * CQ * CK,), f32), grad_theta.reshape(-1), chip * 2 * CQ * CK, 0
            ),
            lax.dynamic_update_slice_in_dim(jnp.zeros((2 * H,), f32), grad_mixer, chip * 4, 0),
        ]
    )
    pieces = jnp.pad(vector_grad.reshape(fs_size, 1, own_vec), ((0, 0), (0, 0), (0, 512 - own_vec)))
    pieces = jnp.broadcast_to(pieces, (fs_size, reps, 512)).reshape(-1, 4, 128)
    vector_total = jnp.sum(
        lax.all_to_all(pieces, ALL, split_axis=0, concat_axis=0, tiled=True), axis=0
    ).reshape(512)[:own_vec]

    strip = BLK // (2 * CHIPS)
    grad_in = dot_tn(hn_rows, dboth).reshape(ROW_TILES, 2, CHIPS, strip, 2, BLK)
    grad_down = dot_tn(inner, dy_rows).reshape(2, CHIPS, strip, ROW_TILES, BLK)
    grad_in = jnp.transpose(half_for_core(grad_in, 1), (1, 3, 0, 2, 4)).reshape(CHIPS, 2 * ROW_TILES, strip, BLK)
    grad_down = jnp.transpose(half_for_core(grad_down, 0), (0, 2, 1, 3))
    ffn_tiles = exchange_chips(jnp.concatenate([grad_in, grad_down], axis=1).astype(bf16))
    gate_tiles = jnp.transpose(ffn_tiles[:, : 2 * ROW_TILES], (1, 0, 2, 3)).reshape(-1, strip, BLK)
    down_tiles = ffn_tiles[:, 2 * ROW_TILES :].reshape(-1, strip, BLK)
    grad_qkv = dot_tn(xn_rows, dqkv_rows).reshape(ROW_TILES, 2, CHIPS, strip, 6, HP)[..., :DH]
    grad_qkv = jnp.transpose(half_for_core(grad_qkv, 1), (1, 0, 2, 3, 4))
    grad_qkv = exchange_chips(grad_qkv.astype(bf16).reshape(CHIPS, ROW_TILES, strip, 6 * DH))
    grad_qkv = jnp.transpose(
        grad_qkv.reshape(CHIPS, ROW_TILES, strip, 3, 2 * DH), (3, 1, 2, 0, 4)
    ).reshape(3, ROW_TILES, strip, ROW_TILES, BLK)
    qkv_tiles = jnp.transpose(grad_qkv, (0, 1, 3, 2, 4)).reshape(-1, strip, BLK)
    heads_strips = jnp.transpose(heads.reshape(seq_len, 2 * ROW_TILES, CHIPS, strip), (2, 0, 1, 3))
    heads_strips = exchange_chips(heads_strips.reshape(CHIPS, seq_len, 2 * ROW_TILES * strip))
    dattn_rows = gather_slow(dattn).reshape(CHIPS * seq_len, D)
    grad_out = dot_tn(heads_strips.reshape(CHIPS * seq_len, -1), dattn_rows)
    grad_out = half_for_core(grad_out.reshape(ROW_TILES, 2, strip, ROW_TILES, BLK), 1)
    out_tiles = jnp.transpose(grad_out.astype(bf16), (0, 2, 1, 3)).reshape(-1, strip, BLK)

    groups = lax.axis_size("g")
    part = strip // groups
    own_slots = basis_left.shape[0]
    devices = groups * 2 * CHIPS
    slot_total = own_slots * devices
    sums = jnp.concatenate(
        [sum_groups(jnp.concatenate([qkv_tiles, out_tiles], axis=0)), sum_groups(jnp.concatenate([gate_tiles, down_tiles], axis=0))],
        axis=0,
    )
    matches = (jnp.arange(slot_total)[:, None] == owners[None, :]).astype(bf16)
    slots = dot(matches, sums.reshape(sums.shape[0], -1)).astype(bf16)
    slots = lax.all_to_all(
        slots.reshape(devices, own_slots, part, BLK), ALL, split_axis=0, concat_axis=0, tiled=True
    )
    slots = slots.reshape(groups, 2, 2, 2, 2, own_slots, part, BLK)
    own_grad = jnp.transpose(slots, (5, 3, 4, 1, 2, 0, 6, 7)).reshape(own_slots, BLK, BLK)

    left_low, right_low = basis_left.astype(bf16), basis_right.astype(bf16)
    rotated = jnp.einsum("sia,sij->saj", left_low, own_grad, preferred_element_type=f32)
    rotated = jnp.einsum("saj,sjb->sab", rotated.astype(bf16), right_low, preferred_element_type=f32)
    first_new = beta_first * block_first + (1.0 - beta_first) * rotated
    second_new = beta_second * block_second + (1.0 - beta_second) * rotated * rotated
    direction = (first_new / (jnp.sqrt(second_new) + eps_adam)).astype(bf16)
    turned = jnp.einsum("sia,sab->sib", left_low, direction, preferred_element_type=f32)
    turned = jnp.einsum("sib,sjb->sij", turned.astype(bf16), right_low, preferred_element_type=f32)
    master_new = block_master - rate_block * (turned + decay_block * block_master)
    vec_first_new = beta_first * vec_first + (1.0 - beta_first) * vector_total
    vec_second_new = beta_second * vec_second + (1.0 - beta_second) * vector_total * vector_total
    vec_master_new = vec_master - rate_vector * vec_first_new / (jnp.sqrt(vec_second_new) + eps_adam)
    return (
        layer_output, input_grad, first_new, second_new, master_new, master_new.astype(bf16),
        vec_first_new, vec_second_new, vec_master_new, vec_master_new.astype(bf16),
    )


def group_at(mask):
    return {axis: 1 - lax.axis_index(axis) for axis, bit in (("g", 4), ("a", 2), ("b", 1)) if mask & bit}


def other_bit(axis, changed):
    at = lax.axis_index(axis)
    return 1 - at if changed else at


def push(src, dst, send, recv, device):
    copy = pltpu.make_async_remote_copy(src_ref=src, dst_ref=dst, send_sem=send, recv_sem=recv, device_id=device)
    copy.start()
    return copy


class Gather:
    def __init__(self, x_ref, out_ref, local_sem, send1, recv1, send2, recv2, send3, recv3):
        self.x, self.out, self.local_sem = x_ref, out_ref, local_sem
        self.sems = ((send1, recv1), (send2, recv2), (send3, recv3))
        self.me = chip_index()
        self.half = x_ref.shape[0] // 2
        self.sent, self.second = [], []

    def here(self, part):
        return pl.ds(part * self.half, self.half)

    def start(self):
        self.local = pltpu.make_async_copy(self.x, self.out.at[self.me], self.local_sem)
        self.local.start()
        send, recv = self.sems[0]
        for part in range(2):
            for at, (axis, _, _) in enumerate(HOPS):
                self.sent.append(
                    push(
                        self.x.at[self.here(part)], self.out.at[self.me, self.here(part)],
                        send.at[at, part], recv.at[at, part], across(axis),
                    )
                )

    def onward(self):
        send, recv = self.sems[1]
        for part in range(2):
            for at, (axis, onward, _) in enumerate(HOPS):
                self.sent[part * 3 + at].wait_recv()
                block = self.out.at[flipped(self.me, (axis,)), self.here(part)]
                self.second.append(push(block, block, send.at[at, part], recv.at[at, part], across(onward)))

    def last(self):
        send, recv = self.sems[2]
        self.third = []
        for copy in self.second:
            copy.wait_recv()
        for at, (axis, onward, last) in enumerate(HOPS):
            begin, count = THIRDS[at]
            piece = self.out.at[flipped(self.me, (axis, onward)), pl.ds(begin, count)]
            self.third.append(push(piece, piece, send.at[at], recv.at[at], across(last)))

    def finish(self):
        for copy in self.third:
            copy.wait_recv()
        self.local.wait()

    def drain(self):
        for copy in self.sent + self.second + self.third:
            copy.wait_send()


class SideGather:
    def __init__(self, x_ref, out_ref, local_sem, send1, recv1, send2, recv2, send3, recv3):
        self.x, self.out, self.local_sem = x_ref, out_ref, local_sem
        self.sems = ((send1, recv1), (send2, recv2), (send3, recv3))
        self.me = chip_index()
        half = x_ref.shape[0] // 2
        self.low, self.high = pl.ds(0, half), pl.ds(half, half)

    def start(self):
        self.local = pltpu.make_async_copy(self.x, self.out.at[self.me], self.local_sem)
        self.local.start()
        send, recv = self.sems[0]
        self.first = [
            push(self.x, self.out.at[self.me], send.at[at], recv.at[at], across(axis)) for at, axis in enumerate("aby")
        ]

    def onward(self):
        send, recv = self.sems[1]
        blocks = [self.out.at[flipped(self.me, (axis,))] for axis in "aby"]
        self.first[0].wait_recv()
        self.second = [
            push(blocks[0], blocks[0], send.at[0], recv.at[0], across("b")),
            push(blocks[0], blocks[0], send.at[1], recv.at[1], across("y")),
        ]
        self.first[1].wait_recv()
        piece = blocks[1].at[self.high]
        self.second.append(push(piece, piece, send.at[2], recv.at[2], across("y")))
        self.first[2].wait_recv()
        piece = blocks[2].at[self.low]
        self.second.append(push(piece, piece, send.at[3], recv.at[3], across("b")))

    def last(self):
        send, recv = self.sems[2]
        self.second[0].wait_recv()
        piece = self.out.at[flipped(self.me, ("a", "b")), self.high]
        self.third = [push(piece, piece, send.at[0], recv.at[0], across("y"))]
        self.second[1].wait_recv()
        piece = self.out.at[flipped(self.me, ("a", "y")), self.low]
        self.third.append(push(piece, piece, send.at[1], recv.at[1], across("b")))

    def finish(self):
        for copy in self.second[2:] + self.third:
            copy.wait_recv()
        self.local.wait()

    def drain(self):
        for copy in self.first + self.second + self.third:
            copy.wait_send()


def side_sems():
    dma = pltpu.SemaphoreType.DMA
    return [dma] + [dma((3,))] * 2 + [dma((4,))] * 2 + [dma((2,))] * 2


class Scatter:
    def __init__(self, parts, near, in2, in3, acc2, acc3, send1, recv1, send2, recv2, send3, recv3):
        self.parts, self.near, self.in2, self.in3, self.acc2, self.acc3 = parts, near, in2, in3, acc2, acc3
        self.sems = ((send1, recv1), (send2, recv2), (send3, recv3))
        self.me = chip_index()
        self.half = parts.shape[1] // 2

    def here(self, part):
        return pl.ds(part * self.half, self.half)

    def start(self):
        send, recv = self.sems[0]
        opposite = flipped(self.me, ("y", "a", "b"))
        self.first = []
        for at, (_, _, last) in enumerate(HOPS):
            rows = pl.ds(*THIRDS[at])
            self.first.append(push(self.parts.at[opposite, rows], self.in2.at[rows], send.at[at], recv.at[at], across(last)))

    def onward(self):
        send, recv = self.sems[1]
        self.second = []
        for part in range(2):
            for at, (axis, onward, _) in enumerate(HOPS):
                dest = flipped(self.me, (axis, onward))
                if part == 0:
                    self.first[at].wait_recv()
                    rows = pl.ds(*THIRDS[at])
                    self.acc2[at] = self.parts[dest]
                    self.acc2[at, rows] = (
                        self.parts[dest, rows].astype(f32) + self.in2[rows].astype(f32)
                    ).astype(bf16)
                here = self.here(part)
                self.second.append(
                    push(self.acc2.at[at, here], self.in3.at[at, here], send.at[at, part], recv.at[at, part], across(onward))
                )

    def last(self):
        send, recv = self.sems[2]
        self.third = []
        for part in range(2):
            here = self.here(part)
            for at, (axis, _, _) in enumerate(HOPS):
                dest = flipped(self.me, (axis,))
                self.second[part * 3 + at].wait_recv()
                self.acc3[at, here] = (
                    self.parts[dest, here].astype(f32) + self.in3[at, here].astype(f32)
                ).astype(bf16)
                self.third.append(
                    push(self.acc3.at[at, here], self.near.at[at, here], send.at[at, part], recv.at[at, part], across(axis))
                )

    def finish(self, part):
        here = self.here(part)
        for at in range(3):
            self.third[part * 3 + at].wait_recv()
        return (self.parts[self.me, here].astype(f32) + self.near[0, here].astype(f32)) + (
            self.near[1, here].astype(f32) + self.near[2, here].astype(f32)
        )

    def drain(self):
        for copy in self.first + self.second + self.third:
            copy.wait_send()


class SideScatter:
    def __init__(self, parts, near, in1, in2, acc2, acc3, send1, recv1, send2, recv2, send3, recv3):
        self.parts, self.near, self.in1, self.in2, self.acc2, self.acc3 = parts, near, in1, in2, acc2, acc3
        self.sems = ((send1, recv1), (send2, recv2), (send3, recv3))
        self.me = chip_index()
        half = parts.shape[1] // 2
        self.low, self.high = pl.ds(0, half), pl.ds(half, half)

    def start(self):
        send, recv = self.sems[0]
        far, side = flipped(self.me, ("a", "b", "y")), flipped(self.me, ("b", "y"))
        self.first = [
            push(self.parts.at[block, rows], self.in1.at[at], send.at[at], recv.at[at], across(axis))
            for at, (block, rows, axis) in enumerate(
                ((far, self.high, "y"), (far, self.low, "b"), (side, self.low, "b"), (side, self.high, "y"))
            )
        ]

    def add(self, at, axes, rows, acc):
        self.first[at].wait_recv()
        block = flipped(self.me, axes)
        acc[...] = self.parts[block]
        acc[rows] = (self.parts[block, rows].astype(f32) + self.in1[at].astype(f32)).astype(bf16)
        return acc

    def onward(self):
        send, recv = self.sems[1]
        third_send, third_recv = self.sems[2]
        self.second = [
            push(self.add(0, ("a", "b"), self.high, self.acc2.at[0]), self.in2.at[0], send.at[0], recv.at[0], across("b")),
            push(self.add(1, ("a", "y"), self.low, self.acc2.at[1]), self.in2.at[1], send.at[1], recv.at[1], across("y")),
        ]
        self.third = [
            push(self.add(at, (axis,), rows, self.acc3.at[to]), self.near.at[to], third_send.at[to], third_recv.at[to], across(axis))
            for at, axis, rows, to in ((3, "b", self.high, 1), (2, "y", self.low, 2))
        ]

    def last(self):
        send, recv = self.sems[2]
        for copy in self.second:
            copy.wait_recv()
        self.acc3[0] = (
            self.parts[flipped(self.me, ("a",))].astype(f32) + (self.in2[0].astype(f32) + self.in2[1].astype(f32))
        ).astype(bf16)
        self.third.append(push(self.acc3.at[0], self.near.at[0], send.at[0], recv.at[0], across("a")))

    def finish(self):
        for copy in self.third:
            copy.wait_recv()
        return (self.parts[self.me].astype(f32) + self.near[0].astype(f32)) + (
            self.near[1].astype(f32) + self.near[2].astype(f32)
        )

    def drain(self):
        for copy in self.first + self.second + self.third:
            copy.wait_send()


def side_scatter_scratch(rows, width):
    dma = pltpu.SemaphoreType.DMA
    return [
        pltpu.VMEM(dims + (width,), bf16) for dims in ((3, rows), (4, rows // 2), (2, rows), (2, rows), (3, rows))
    ] + [dma((4,))] * 2 + [dma((2,))] * 2 + [dma((3,))] * 2


def scatter_scratch(rows, width):
    dma = pltpu.SemaphoreType.DMA
    three = pltpu.VMEM((3, rows, width), bf16)
    return [three, pltpu.VMEM((rows, width), bf16), three, three, three] + [dma((3,))] * 2 + [dma((3, 2))] * 4


VMEM = pl.BlockSpec(memory_space=pltpu.VMEM)


HEAD_ROW, FFN_ROW, THETA_ROW, MIX_ROW, VEC_ROWS = 12, 28, 40, 56, 64
SHARD_ROWS = 16


def vector_row(at):
    for begin, row, width in (
        (3 * D + H * CQ * CK, MIX_ROW, 4), (3 * D, THETA_ROW, CQ * CK), (2 * D, FFN_ROW, 128), (D, HEAD_ROW, DH), (0, 0, 128)
    ):
        if at >= begin:
            return row + (at - begin) // width


def vector_rows(own_vec, shards):
    return [min(vector_row(shard * own_vec), VEC_ROWS - SHARD_ROWS) // 8 * 8 for shard in range(shards)]


def rows_of_vector(flat):
    conv_end = 3 * D + H * CQ * CK
    return jnp.concatenate(
        [
            flat[:D].reshape(-1, 128),
            jnp.pad(flat[D : 2 * D].reshape(H, DH), ((0, 0), (0, 128 - DH))),
            flat[2 * D : 3 * D].reshape(-1, 128),
            jnp.pad(flat[3 * D : conv_end].reshape(H, CQ * CK), ((0, 0), (0, 128 - CQ * CK))),
            jnp.pad(flat[conv_end : conv_end + 2 * H].reshape(CHIPS, 4), ((0, 0), (0, 124))),
        ],
        axis=0,
    )


def source_at(mask):
    return ((other_bit("g", mask & 4) * 2 + other_bit("a", mask & 2)) * 2 + other_bit("b", mask & 1)) * 2 + lax.axis_index("c")


def front_body(
    first_rows, length_ref, vec_ref, x_ref, w_query_ref, w_key_ref, w_value_ref, cot_ref,
    w_out_ref, w_gate_ref, w_up_ref, w_down_ref, dy_ref, len_ref, mix_ref, gains_ref, toep_ref, gain_ref, xn_ref, qkv_ref, s_ref, p_ref, o_ref, heads_ref, hmid_ref, wq_ref, wo_ref, hn_all_ref, w_in_ref, w_dn_ref, dy_all_ref,
    blocks_ref, own_len_ref, vecs_ref, full_ref, x_all_ref, pad_ref, out_heads, hn_ref, passing, vec_send, vec_recv, len_send, len_recv, local_sems, q_send, q_recv, q_core_send, q_core_recv,
    o_send, o_recv, o_side_send, o_side_recv, o_core_send, o_core_recv, d_send, d_recv,
    w_send, w_recv, u_send, u_recv, core_send, core_recv, head_send, head_recv, *hops,
):
    seqs, rows, _ = x_all_ref.shape
    g, a, b, c, y = (lax.axis_index(axis) for axis in ALL)
    me = chip_index()
    mine = source_at(0)
    shard = {mask: source_at(mask) for mask in range(8)}
    low, high = pl.ds(0, BLK), pl.ds(BLK, BLK)
    order = (4, 6, 5, 7, 2, 1, 3)

    def columns(chip):
        return pl.ds(pl.multiple_of(chip * BLK, BLK), BLK)

    def block_to(mask):
        return (y * 2 + other_bit("a", mask & 2)) * 2 + other_bit("b", mask & 1)

    local = [
        pltpu.make_async_copy(w_out_ref, wo_ref.at[mine], local_sems.at[1]),
        pltpu.make_async_copy(w_gate_ref.at[:, columns(me)], w_in_ref.at[mine, :, low], local_sems.at[2]),
        pltpu.make_async_copy(w_up_ref.at[:, columns(me)], w_in_ref.at[mine, :, high], local_sems.at[3]),
    ]
    down_local = pltpu.make_async_copy(w_down_ref, w_dn_ref.at[c], local_sems.at[4])
    own_len_ref[...] = jnp.full(own_len_ref.shape, length_ref[0].astype(f32), f32)
    own_small = [
        pltpu.make_async_copy(vec_ref, vecs_ref.at[mine], local_sems.at[5]),
        pltpu.make_async_copy(own_len_ref, len_ref.at[me], local_sems.at[6]),
    ]
    for copy in local + own_small:
        copy.start()

    @pl.when(g == y)
    def _():
        down_local.start()

    greet_all()
    sent, relayed = {}, []
    first = Gather(x_ref, x_all_ref, *hops[:7])
    side = SideGather(dy_ref, dy_all_ref, *hops[7:14])
    gather = Gather(hn_ref, hn_all_ref, *hops[14:])

    def push_vec(step, carry):
        to = lax.rem(mine + step, 16)
        pltpu.make_async_remote_copy(
            src_ref=vec_ref, dst_ref=vecs_ref.at[mine], send_sem=vec_send, recv_sem=vec_recv,
            device_id={
                "g": lax.div(to, 8), "a": lax.rem(lax.div(to, 4), 2), "b": lax.rem(lax.div(to, 2), 2), "c": lax.rem(to, 2)
            },
        ).start()
        return carry

    lax.fori_loop(1, 16, push_vec, 0)
    lengths_sent = [
        push(own_len_ref, len_ref.at[me], len_send.at[mask], len_recv.at[mask], chip_at(mask)) for mask in range(1, 8)
    ]

    first.start()
    for chip in range(CHIPS):
        cols = slice(chip * 2 * DH, (chip + 1) * 2 * DH)
        blocks_ref[chip] = jnp.concatenate([w_query_ref[:, cols], w_key_ref[:, cols], w_value_ref[:, cols]], axis=1)
    wq_ref[mine] = blocks_ref[me]
    valid = lax.broadcasted_iota(jnp.int32, cot_ref.shape, 0) < length_ref[0]
    dy_ref[...] = jnp.where(valid, cot_ref[...].astype(f32), 0.0).astype(bf16)

    for mask in order:
        sent[mask] = push(blocks_ref.at[block_to(mask)], wq_ref.at[mine], q_send.at[mask], q_recv.at[mask], group_at(mask))

    def relay_qkv(mask):
        sent[mask].wait_recv()
        block = wq_ref.at[shard[mask]]
        relayed.append(push(block, block, q_core_send.at[mask], q_core_recv.at[mask], across("c")))

    half = pl.ds(pl.multiple_of(y * 48, 16), 48)
    lines, o_side, o_core = {}, {}, []

    def start_lines():
        for mask in (2, 4, 6):
            lines[mask] = push(w_out_ref.at[half], wo_ref.at[mine, half], o_send.at[mask], o_recv.at[mask], group_at(mask))
        lines[1] = push(w_out_ref.at[half], wo_ref.at[mine, half], o_send.at[1], o_recv.at[1], across("b"))
        o_core.append(push(w_out_ref, wo_ref.at[mine], o_core_send.at[0], o_core_recv.at[0], across("c")))

    def to_side(mask):
        lines[mask].wait_recv()
        piece = wo_ref.at[shard[mask], half]
        o_side[mask] = push(piece, piece, o_side_send.at[mask], o_side_recv.at[mask], across("y"))
        if mask in (2, 4, 6):
            lines[mask + 1] = push(piece, piece, o_send.at[mask + 1], o_recv.at[mask + 1], across("b"))

    def out_to_core(masks):
        for mask in masks:
            o_side[mask].wait_recv()
            block = wo_ref.at[shard[mask]]
            o_core.append(push(block, block, o_core_send.at[mask], o_core_recv.at[mask], across("c")))

    count = w_down_ref.shape[0] // 2
    upper, lower = pl.ds(0, count), pl.ds(count, count)

    def down_copy(src, dst, at, axis):
        return pltpu.make_async_remote_copy(
            src_ref=src, dst_ref=dst, send_sem=d_send.at[at], recv_sem=d_recv.at[at], device_id=across(axis)
        )

    def down_direct():
        return down_copy(w_down_ref.at[upper], w_dn_ref.at[c, upper], 0, "g")

    def down_around():
        return down_copy(w_down_ref.at[lower], passing, 1, "g")

    def down_over():
        return down_copy(passing, w_dn_ref.at[c, lower], 2, "y")

    def down_to_core():
        return down_copy(w_dn_ref.at[c], w_dn_ref.at[c], 3, "c")

    def down_start():
        @pl.when(g == y)
        def _():
            down_direct().start()

        @pl.when(g != y)
        def _():
            down_around().start()

    def down_pass():
        @pl.when(g == y)
        def _():
            down_around().wait_recv()
            down_over().start()

    def down_last():
        @pl.when(g == y)
        def _():
            down_local.wait()
            down_to_core().start()
            down_direct().wait_send()
            down_over().wait_send()

        @pl.when(g != y)
        def _():
            down_direct().wait_recv()
            down_over().wait_recv()
            down_to_core().start()
            down_around().wait_send()

    gate, up = {}, {}

    def send_columns(masks):
        for mask in masks:
            to = columns(block_to(mask))
            gate[mask] = push(w_gate_ref.at[:, to], w_in_ref.at[mine, :, low], w_send.at[mask], w_recv.at[mask], group_at(mask))
            up[mask] = push(w_up_ref.at[:, to], w_in_ref.at[mine, :, high], u_send.at[mask], u_recv.at[mask], group_at(mask))

    def relay(mask):
        gate[mask].wait_recv()
        up[mask].wait_recv()
        block = w_in_ref.at[shard[mask]]
        relayed.append(push(block, block, core_send.at[mask], core_recv.at[mask], across("c")))

    side.start()
    relayed.append(push(wq_ref.at[mine], wq_ref.at[mine], q_core_send.at[0], q_core_recv.at[0], across("c")))
    first.onward()
    start_lines()

    for copy in own_small:
        copy.wait()
    others = vecs_ref.at[pl.ds(0, 15)]
    pltpu.make_async_copy(others, others, vec_recv).wait()
    full_ref[...] = jnp.zeros_like(full_ref)
    for at, row in enumerate(first_rows):
        full_ref[row : row + SHARD_ROWS, :] += vecs_ref[at]
    gains_ref[...] = jnp.zeros_like(gains_ref)
    for row in range(D // 128):
        gains_ref[0:1, row * 128 : (row + 1) * 128] = full_ref[row : row + 1, :]
        gains_ref[1:2, row * 128 : (row + 1) * 128] = full_ref[FFN_ROW + row : FFN_ROW + row + 1, :]
    mix_ref[...] = full_ref[pl.ds(MIX_ROW + me, 1), :]
    query_at = lax.broadcasted_iota(jnp.int32, (rows, rows), 0)
    key_at = lax.broadcasted_iota(jnp.int32, (rows, rows), 1)
    key_float = key_at.astype(f32)
    tap_at = query_at - key_at + CK // 2
    for head in range(2):
        gain_ref[:, head * HP : (head + 1) * HP] = full_ref[pl.ds(HEAD_ROW + 2 * me + head, 1), :]
        theta = full_ref[pl.ds(THETA_ROW + 2 * me + head, 1), :]
        for lag in range(CQ):
            band_values = jnp.zeros((rows, rows), f32)
            for tap in range(CK):
                at = lag * CK + tap
                band_values = jnp.where(tap_at == tap, theta[:, at : at + 1], band_values)
            toep_ref[head, lag * rows : (lag + 1) * rows, :] = band_values.astype(bf16)

    side.onward()
    first.last()
    side.last()
    down_start()
    for mask in order:
        relay_qkv(mask)
    send_columns((2, 1, 3, 4, 6, 5, 7))
    first.finish()
    for copy in relayed + lengths_sent:
        copy.wait_recv()
    qkv_relayed = relayed[:]
    del relayed[:]

    pad_ref[0:8, :] = jnp.zeros((8, rows), f32)
    blank = jnp.zeros((rows, HP - DH), bf16)
    batch = 4

    def project(at, carry):
        values = x_all_ref[pl.ds(at * batch, batch)].astype(f32).reshape(batch * rows, D)
        normed = (values * rms(values) * gains_ref[0:1, :]).astype(bf16)
        xn_ref[pl.ds(at * batch, batch)] = normed.reshape(batch, rows, D)
        made = dot(normed, wq_ref[...].reshape(D, 6 * DH)).astype(bf16)
        for seq in range(batch):
            for piece in range(6):
                qkv_ref[at * batch + seq, :, piece * HP : (piece + 1) * HP] = jnp.concatenate(
                    [made[seq * rows : (seq + 1) * rows, piece * DH : (piece + 1) * DH], blank], axis=1
                )
        return carry

    project(0, 0)
    for mask in (2, 4, 6, 1):
        to_side(mask)
    project(1, 0)
    for copy in local:
        copy.wait()
    relayed.append(push(w_in_ref.at[mine], w_in_ref.at[mine], core_send.at[0], core_recv.at[0], across("c")))

    def head_copy(seq):
        return pltpu.make_async_remote_copy(
            src_ref=out_heads.at[seq], dst_ref=heads_ref.at[me], send_sem=head_send.at[seq], recv_sem=head_recv.at[me],
            device_id={"y": lax.div(seq, 4), "a": lax.rem(lax.div(seq, 2), 2), "b": lax.rem(seq, 2)},
        )

    def attend(step, carry):
        seq = lax.rem(me + step, seqs)
        keep = (key_at <= query_at) & (key_float < len_ref[seq, 0:1, :])
        weights, made = [], []
        for head in range(2):
            query = qkv_ref[seq, :, head * HP : (head + 1) * HP]
            key = qkv_ref[seq, :, (2 + head) * HP : (3 + head) * HP]
            scores = jnp.where(keep, dot_nt(query, key) * (1.0 / math.sqrt(DH)), 0.0)
            s_ref[seq, head] = scores.astype(bf16)
            wide = shifted_down(pad_ref, scores)
            near = wide.astype(bf16)
            rest = (wide - near.astype(f32)).astype(bf16)
            conv = dot(near, toep_ref[head]) + dot(rest, toep_ref[head])
            logits = jnp.where(keep, conv, -1e30)
            weight = jnp.exp(logits - jnp.max(logits, axis=-1, keepdims=True))
            weight = weight / jnp.sum(weight, axis=-1, keepdims=True)
            p_ref[seq, head] = weight
            weights.append(weight)
        for head in range(2):
            mixed = mix_ref[:, 2 * head : 2 * head + 1] * weights[0] + mix_ref[:, 2 * head + 1 : 2 * head + 2] * weights[1]
            value = qkv_ref[seq, :, (4 + head) * HP : (5 + head) * HP]
            out = dot(mixed.astype(bf16), value)
            o_ref[seq, :, head * HP : (head + 1) * HP] = out
            scale = lax.rsqrt(jnp.sum(out * out, axis=-1, keepdims=True) * (1.0 / DH) + eps_norm)
            made.append((out * scale * gain_ref[:, head * HP : (head + 1) * HP])[:, :DH])
        out_heads[seq] = jnp.concatenate(made, axis=1).astype(bf16)

        @pl.when(step > 0)
        def _():
            head_copy(seq).start()

        return carry

    lax.fori_loop(0, 3, attend, 0)
    for mask in (3, 5, 7):
        to_side(mask)
    down_pass()
    lax.fori_loop(3, 6, attend, 0)
    out_to_core((2, 4, 6))
    lax.fori_loop(6, seqs, attend, 0)
    out_to_core((1, 3, 5, 7))
    heads_ref[me] = out_heads[me]
    for copy in o_core:
        copy.wait_recv()

    def head_arrived(step, carry):
        source = lax.rem(me + step, seqs)
        pltpu.make_async_copy(out_heads.at[source], heads_ref.at[source], head_recv.at[source]).wait()
        return carry

    lax.fori_loop(1, seqs, head_arrived, 0)

    def project_out(at, carry):
        cols = pl.ds(pl.multiple_of(at * BLK, BLK), BLK)
        total = x_ref[:, cols].astype(f32)
        for chip in range(CHIPS):
            weight = wo_ref[2 * chip : 2 * chip + 2, :, cols].reshape(2 * DH, BLK)
            total += dot(heads_ref[chip], weight)
        hmid_ref[:, cols] = total
        return carry

    lax.fori_loop(0, ROW_TILES, project_out, 0)
    hmid = hmid_ref[...]
    hn_ref[...] = (hmid * rms(hmid) * gains_ref[1:2, :]).astype(bf16)
    gather.start()
    for mask in (4, 6):
        relay(mask)
    gather.onward()
    for mask in (5, 7, 2):
        relay(mask)
    gather.last()
    for mask in (1, 3):
        relay(mask)
    down_last()
    down_to_core().wait()
    side.finish()
    gather.finish()
    for copy in relayed:
        copy.wait_recv()

    def head_left(step, carry):
        head_copy(lax.rem(me + step, seqs)).wait_send()
        return carry

    lax.fori_loop(1, seqs, head_left, 0)
    first.drain()
    side.drain()
    gather.drain()
    for copies in (sent, lines, o_side, gate, up):
        for copy in copies.values():
            copy.wait_send()
    pltpu.make_async_copy(others, others, vec_send).wait()
    for copy in qkv_relayed + relayed + o_core + lengths_sent:
        copy.wait_send()


def run_front(first_rows, length, vec, x, w_query, w_key, w_value, cotangent, w_out, w_gate, w_up, w_down):
    rows = x.shape[0]
    dma = pltpu.SemaphoreType.DMA
    shapes = [
        (x.shape, bf16), ((CHIPS, 8, 128), f32), ((1, 128), f32), ((8, D), f32), ((2, CQ * rows, rows), bf16), ((1, 2 * HP), f32),
        ((CHIPS, rows, D), bf16), ((CHIPS, rows, 6 * HP), bf16), ((CHIPS, 2, rows, rows), bf16), ((CHIPS, 2, rows, rows), f32),
        ((CHIPS, rows, 2 * HP), f32), ((CHIPS, rows, 2 * DH), bf16), ((rows, D), f32),
        ((16, w_query.shape[0], 6 * DH), bf16), ((16,) + w_out.shape, bf16), ((CHIPS, rows, D), bf16),
        ((16, w_gate.shape[0], 2 * BLK), bf16), ((2,) + w_down.shape, bf16), ((CHIPS, rows, D), bf16),
    ]
    return pl.pallas_call(
        functools.partial(front_body, first_rows),
        in_specs=[SMEM] + [VMEM] * 6 + [ANYS] * 4,
        out_specs=[VMEM] * 15 + [ANYS] * 4,
        out_shape=[jax.ShapeDtypeStruct(*shape) for shape in shapes],
        scratch_shapes=[
            pltpu.VMEM((CHIPS, w_query.shape[0], 6 * DH), bf16), pltpu.VMEM((8, 128), f32), pltpu.VMEM((16,) + vec.shape, f32), pltpu.VMEM((VEC_ROWS, 128), f32), pltpu.VMEM((CHIPS, rows, D), bf16), pltpu.VMEM((rows + 8, rows), f32), pltpu.VMEM((CHIPS, rows, 2 * DH), bf16),
            pltpu.VMEM((rows, D), bf16), pltpu.VMEM((w_down.shape[0] // 2, D), bf16), dma, dma, dma((8,)), dma((8,)), dma((7,)),
        ] + [dma((8,))] * 10 + [dma((4,))] * 2 + [dma((8,))] * 8 + hop_sems() + side_sems() + hop_sems(),
        name="front",
        compiler_params=pltpu.CompilerParams(collective_id=2, has_side_effects=True, vmem_limit_bytes=56 * 2**20),
    )(length, vec, x, w_query, w_key, w_value, cotangent, w_out, w_gate, w_up, w_down)


def middle_body(
    len_ref, mix_ref, hn_ref, dy_ref, xn_ref, w_in_ref, w_dn_ref, wq_ref, dy_own_ref, hmid_ref, gain_ffn_ref, wo_ref,
    qkv_ref, toep_ref, gain_ref, s_ref, p_ref, o_ref, strips_ref,
    inner_ref, dhmid_ref, dxn_ref, gain_ffn_grad_ref, theta_ref, mixer_ref, gain_grad_ref, tiles_ref,
    theta_sums, pad_ref, first_ref, second_ref, dboth_ref, parts_ref, dattn_ref, grads_ref, sent_ref, strips_in, gin_ref, gd_ref,
    half_in, half_d, near_in, near_d, dqkv_ref, gq_ref, go_ref, core_q, core_o, in_q, in_o,
    near3, in23, in33, local_sems, load_sems, strip_send, strip_recv, head_send, head_recv,
    core_send, core_recv, near_send, near_recv, gu_send, gu_recv, q_send, q_recv, *rest,
):
    scatter_args, scatter3_sems, side = rest[:11], rest[11:17], rest[17:]
    seqs, rows, _ = hn_ref.shape
    g, a, b, c, y = (lax.axis_index(axis) for axis in ALL)
    me = chip_index()
    pairs = [(1 - y) * 2 + 1 - a, (1 - y) * 2 + a, y * 2 + 1 - a, y * 2 + a]
    loads = []
    for at, pair in enumerate(pairs):
        two = pl.ds(pair * 2, 2)
        loads.append(
            [
                pltpu.make_async_copy(hn_ref.at[two], first_ref.at[two], load_sems.at[at]),
                pltpu.make_async_copy(dy_ref.at[two], second_ref.at[two], load_sems.at[4 + at]),
            ]
        )
    for copies in loads:
        for copy in copies:
            copy.start()
    strip_local = pltpu.make_async_copy(strips_ref.at[me], strips_in.at[me], local_sems.at[0])
    strip_local.start()
    greet_all()
    chips = (7, 6, 5, 3, 4, 2, 1)
    to_chip = {mask: flipped(me, [axis for axis in BITS if mask & BITS[axis]]) for mask in chips}
    strips_sent = [
        push(strips_ref.at[to_chip[mask]], strips_in.at[me], strip_send.at[mask], strip_recv.at[mask], chip_at(mask))
        for mask in chips
    ]

    def hidden(pair):
        two = pl.ds(pair * 2, 2)
        both = dot(first_ref[two].reshape(2 * rows, D), w_in_ref[...])
        gate, up = both[:, :BLK], both[:, BLK:]
        dinner = dot_nt(second_ref[two].reshape(2 * rows, D), w_dn_ref[...])
        sig = jax.nn.sigmoid(gate)
        silu = gate * sig
        inner_ref[two] = (silu * up).astype(bf16).reshape(2, rows, BLK)
        dgate = (dinner * up * (sig * (1.0 + gate * (1.0 - sig)))).astype(bf16)
        dup = (dinner * silu).astype(bf16)
        dboth_ref[two, :, 0:BLK] = dgate.reshape(2, rows, BLK)
        dboth_ref[two, :, BLK:] = dup.reshape(2, rows, BLK)
        back = dot_nt(dgate, w_in_ref[:, 0:BLK]) + dot_nt(dup, w_in_ref[:, BLK:])
        parts_ref[two] = back.astype(bf16).reshape(2, rows, D)

    def wait_load(at):
        for copy in loads[at]:
            copy.wait()

    wait_load(0)
    hidden(pairs[0])
    scatter = Scatter(parts_ref, *scatter_args)
    scatter.start()
    wait_load(1)
    wait_load(2)

    def two_more(step, carry):
        hidden((1 - y) * 2 + a + step * ((2 * y - 1) * 2 + 1 - a - a))
        return carry

    lax.fori_loop(0, 2, two_more, 0)
    scatter.onward()
    wait_load(3)
    hidden(pairs[3])

    def down_grad(col, carry):
        cols = pl.ds(pl.multiple_of(col * BLK, BLK), BLK)
        made = dot_tn(inner_ref[...].reshape(seqs * rows, BLK), second_ref[:, :, cols].reshape(seqs * rows, BLK))
        gd_ref[:, :, :, :, cols] = made.astype(bf16).reshape(2, CHIPS, 2, BLK // 32, BLK)
        return carry

    lax.fori_loop(0, ROW_TILES, down_grad, 0)
    to_core = [push(gd_ref.at[1 - c], half_d, core_send.at[0], core_recv.at[0], across("c"))]

    def in_grad(row, carry):
        values = first_ref[:, :, pl.ds(pl.multiple_of(row * BLK, BLK), BLK)].reshape(seqs * rows, BLK)
        for which in range(2):
            cols = slice(which * BLK, (which + 1) * BLK)
            made = dot_tn(values, dboth_ref[:, :, cols].reshape(seqs * rows, BLK))
            gin_ref[row, :, :, :, :, cols] = made.astype(bf16).reshape(2, CHIPS, 2, BLK // 32, BLK)
        return carry

    def in_to_core(row):
        to_core.append(push(gin_ref.at[row, 1 - c], half_in.at[row], core_send.at[1 + row], core_recv.at[1 + row], across("c")))

    in_grad(0, 0)
    in_to_core(0)
    to_core[0].wait_recv()

    def core_down(chip, carry):
        half_d[chip] = (half_d[chip].astype(f32) + gd_ref[c, chip].astype(f32)).astype(bf16)
        return carry

    lax.fori_loop(0, CHIPS, core_down, 0)
    to_near = [push(half_d.at[:, 1 - g], near_d, near_send.at[0], near_recv.at[0], across("g"))]
    scatter.last()
    lax.fori_loop(1, ROW_TILES, in_grad, 0)
    in_to_core(1)
    in_to_core(2)
    xn_load = pltpu.make_async_copy(xn_ref, first_ref, load_sems.at[8])
    xn_load.start()

    def core_rows(row):
        to_core[1 + row].wait_recv()

        def core_chip(chip, carry):
            half_in[row, chip] = (half_in[row, chip].astype(f32) + gin_ref[row, c, chip].astype(f32)).astype(bf16)
            return carry

        lax.fori_loop(0, CHIPS, core_chip, 0)
        to_near.append(push(half_in.at[row, :, 1 - g], near_in.at[row], near_send.at[1 + row], near_recv.at[1 + row], across("g")))

    core_rows(0)
    core_rows(1)
    core_rows(2)
    half = rows // 2
    gain_sum = jnp.zeros((1, D), f32)
    for part in range(2):
        here = pl.ds(part * half, half)
        grad = scatter.finish(part)
        values = hmid_ref[here]
        scale = rms(values)
        unit = values * scale
        inside = grad * gain_ffn_ref[...]
        gain_sum += jnp.sum(grad * unit, axis=0, keepdims=True)
        dhmid = scale * (inside - unit * jnp.mean(inside * unit, axis=-1, keepdims=True)) + dy_own_ref[here].astype(f32)
        dhmid_ref[here] = dhmid
        dattn_ref[here] = dhmid.astype(bf16)
    gain_ffn_grad_ref[...] = gain_sum

    def grad_copy(to):
        return pltpu.make_async_remote_copy(
            src_ref=sent_ref.at[to], dst_ref=grads_ref.at[me], send_sem=head_send.at[to], recv_sem=head_recv.at[me],
            device_id={"y": lax.div(to, 4), "a": lax.rem(lax.div(to, 2), 2), "b": lax.rem(to, 2)},
        )

    def send_grad(step, carry):
        to = lax.rem(me + step, seqs)
        sent_ref[to] = dot_nt(dattn_ref[...], wo_ref[to]).astype(bf16)

        @pl.when(step > 0)
        def _():
            grad_copy(to).start()

        return carry

    lax.fori_loop(0, seqs, send_grad, 0)
    grads_ref[me] = sent_ref[me]
    gather = SideGather(dattn_ref, second_ref, *side)
    gather.start()

    pad_ref[rows : rows + 8, :] = jnp.zeros((8, rows), f32)
    theta_sums[...] = jnp.zeros_like(theta_sums)
    mixer_ref[...] = jnp.zeros_like(mixer_ref)
    gain_grad_ref[...] = jnp.zeros_like(gain_grad_ref)
    query_at = lax.broadcasted_iota(jnp.int32, (rows, rows), 0)
    key_at = lax.broadcasted_iota(jnp.int32, (rows, rows), 1)
    blank = jnp.zeros((rows, HP - DH), f32)

    def grad_arrived(step, carry):
        source = lax.rem(me + step, seqs)
        pltpu.make_async_copy(sent_ref.at[source], grads_ref.at[source], head_recv.at[source]).wait()
        return carry

    lax.fori_loop(1, seqs, grad_arrived, 0)

    def one(seq, carry):
        keep = (key_at <= query_at) & (key_at < len_ref[seq])
        weights = [p_ref[seq, 0], p_ref[seq, 1]]
        grad_mixed, made = [], [None] * 6
        grads = grads_ref[seq].astype(f32)
        for head in range(2):
            cols = slice(head * HP, (head + 1) * HP)
            out = o_ref[seq, :, cols]
            grad = jnp.concatenate([grads[:, head * DH : (head + 1) * DH], blank], axis=1)
            scale = lax.rsqrt(jnp.sum(out * out, axis=-1, keepdims=True) * (1.0 / DH) + eps_norm)
            unit = out * scale
            gain_grad_ref[:, cols] += jnp.sum(grad * unit, axis=0, keepdims=True)
            inner = grad * gain_ref[:, cols]
            grad_out = scale * (inner - unit * (jnp.sum(inner * unit, axis=-1, keepdims=True) * (1.0 / DH)))
            grad_out = grad_out.astype(bf16)
            value = qkv_ref[seq, :, (4 + head) * HP : (5 + head) * HP]
            mixed = (mix_ref[2 * head] * weights[0] + mix_ref[2 * head + 1] * weights[1]).astype(bf16)
            made[4 + head] = dot_tn(mixed, grad_out)
            back = dot_nt(grad_out, value)
            grad_mixed.append(back)
            for source in range(2):
                mixer_ref[2 * head + source : 2 * head + source + 1, :] += jnp.sum(
                    back * weights[source], axis=0, keepdims=True
                )
        for head in range(2):
            grad_weight = mix_ref[head] * grad_mixed[0] + mix_ref[2 + head] * grad_mixed[1]
            weight = weights[head]
            grad_conv = weight * (grad_weight - jnp.sum(weight * grad_weight, axis=-1, keepdims=True))
            wide = shifted_up(pad_ref, grad_conv).astype(bf16)
            theta_sums[head] += dot_tn(s_ref[seq, head], wide)
            grad_scores = jnp.zeros((rows, rows), f32)
            for lag in range(CQ):
                grad_scores += dot_nt(
                    wide[:, lag * rows : (lag + 1) * rows], toep_ref[head, lag * rows : (lag + 1) * rows, :]
                )
            grad_scores = jnp.where(keep, grad_scores * (1.0 / math.sqrt(DH)), 0.0).astype(bf16)
            query = qkv_ref[seq, :, head * HP : (head + 1) * HP]
            key = qkv_ref[seq, :, (2 + head) * HP : (3 + head) * HP]
            made[head] = dot(grad_scores, key)
            made[2 + head] = dot_tn(grad_scores, query)
        dqkv_ref[seq] = jnp.concatenate([part[:, :DH] for part in made], axis=1).astype(bf16)
        return carry

    lax.fori_loop(0, seqs, one, 0)
    gather.onward()
    scatter.drain()
    tiles_sent = []

    tap_at = query_at - key_at + CK // 2

    def taps(at, carry):
        lag = lax.rem(at, CQ)
        values = theta_sums[lax.div(at, CQ), :, pl.ds(pl.multiple_of(lag * rows, rows), rows)]
        for tap in range(CK):
            theta_ref[pl.ds(at * CK + tap, 1), :] = jnp.sum(
                jnp.where(tap_at == tap, values, 0.0), axis=0, keepdims=True
            )
        return carry

    xn_load.wait()
    all_rows = seqs * rows

    def qkv_grad(row, carry):
        cols = pl.ds(pl.multiple_of(row * BLK, BLK), BLK)
        made = dot_tn(first_ref[:, :, cols].reshape(all_rows, BLK), dqkv_ref[...].reshape(all_rows, 6 * DH))
        gq_ref[row] = made.astype(bf16).reshape(2, CHIPS, 2, BLK // 32, 6 * DH)
        return carry

    lax.fori_loop(0, ROW_TILES, qkv_grad, 0)
    to_core.append(push(gq_ref.at[:, 1 - c], core_q, core_send.at[4], core_recv.at[4], across("c")))

    def input_part(at, carry):
        two = pl.ds(at * 2, 2)
        made = dot_nt(dqkv_ref[two].reshape(2 * rows, 6 * DH), wq_ref[...])
        parts_ref[two] = made.astype(bf16).reshape(2, rows, D)
        return carry

    lax.fori_loop(0, seqs // 2, input_part, 0)
    scatter3 = Scatter(parts_ref, near3, in23, in33, *scatter_args[3:5], *scatter3_sems)
    scatter3.start()
    lax.fori_loop(0, 2 * CQ, taps, 0)
    to_core[4].wait_recv()

    def core_chip_q(chip, carry):
        for row in range(ROW_TILES):
            core_q[row, chip] = (core_q[row, chip].astype(f32) + gq_ref[row, c, chip].astype(f32)).astype(bf16)
        return carry

    lax.fori_loop(0, CHIPS, core_chip_q, 0)
    slot = g * CHIPS + me
    order = (15, 14, 13, 11, 12, 10, 9, 8, 7, 6, 5, 3, 4, 2, 1)
    for mask in order:
        to = flipped(me, [axis for axis in BITS if mask & BITS[axis]])
        tiles_sent.append(
            push(core_q.at[:, to, other_bit("g", mask & 8)], in_q.at[slot], q_send.at[mask], q_recv.at[mask], wide_at(mask))
        )
    in_q[slot] = core_q[:, me, g]
    gather.last()
    to_near[0].wait_recv()

    def near_down(chip, carry):
        half_d[chip, g] = (half_d[chip, g].astype(f32) + near_d[chip].astype(f32)).astype(bf16)
        return carry

    lax.fori_loop(0, CHIPS, near_down, 0)
    base = 4 * ROW_TILES**2

    def spread(ref, cols, tile, which):
        for mask in chips:
            at = which * CHIPS + mask
            tiles_sent.append(
                push(ref.at[to_chip[mask], g, :, cols], tiles_ref.at[tile], gu_send.at[at], gu_recv.at[at], chip_at(mask))
            )
        tiles_ref[tile] = ref[me, g, :, cols]

    for col in range(ROW_TILES):
        spread(half_d, pl.ds(col * BLK, BLK), base + 2 * ROW_TILES * FF_TILES + me * ROW_TILES + col, 6 + col)
    scatter3.onward()
    gather.finish()
    strip_local.wait()
    for copy in strips_sent:
        copy.wait_recv()

    def out_grad(col, carry):
        cols = pl.ds(pl.multiple_of(col * BLK, BLK), BLK)
        made = dot_tn(strips_in[...].reshape(all_rows, 2 * DH), second_ref[:, :, cols].reshape(all_rows, BLK))
        go_ref[:, :, :, :, cols] = made.astype(bf16).reshape(ROW_TILES, 2, 2, BLK // 32, BLK)
        return carry

    lax.fori_loop(0, ROW_TILES, out_grad, 0)
    to_core.append(push(go_ref.at[:, 1 - c], core_o, core_send.at[5], core_recv.at[5], across("c")))

    def near_rows(row):
        to_near[1 + row].wait_recv()

        def near_chip(chip, carry):
            half_in[row, chip, g] = (half_in[row, chip, g].astype(f32) + near_in[row, chip].astype(f32)).astype(bf16)
            return carry

        lax.fori_loop(0, CHIPS, near_chip, 0)
        for which in range(2):
            spread(
                half_in.at[row], pl.ds(which * BLK, BLK), base + (which * ROW_TILES + row) * FF_TILES + me, 2 * row + which
            )

    near_rows(0)
    to_core[5].wait_recv()
    core_o[...] = (core_o[...].astype(f32) + go_ref[:, c].astype(f32)).astype(bf16)
    to_near.append(push(core_o.at[:, 1 - g], in_o, near_send.at[4], near_recv.at[4], across("g")))
    scatter3.last()
    near_rows(1)
    near_rows(2)
    dxn_ref[0:half] = scatter3.finish(0)
    dxn_ref[half:] = scatter3.finish(1)

    def three_tiles(at, values):
        for col in range(ROW_TILES):
            tiles_ref[at + col] = values[:, col * BLK : (col + 1) * BLK].astype(bf16)

    to_near[4].wait_recv()
    for row in range(ROW_TILES):
        three_tiles(3 * ROW_TILES**2 + row * ROW_TILES, in_o[row].astype(f32) + core_o[row, g].astype(f32))
    for copy in tiles_sent:
        copy.wait_recv()
    for row in range(ROW_TILES):
        sums = [in_q[chip, row].astype(f32) + in_q[CHIPS + chip, row].astype(f32) for chip in range(CHIPS)]
        for which in range(3):
            three_tiles(
                which * ROW_TILES**2 + row * ROW_TILES,
                jnp.concatenate([part[:, which * 2 * DH : (which + 1) * 2 * DH] for part in sums], axis=1),
            )
    tiles_ref[tiles_ref.shape[0] - 1] = jnp.zeros(tiles_ref.shape[1:], bf16)

    def grad_left(step, carry):
        grad_copy(lax.rem(me + step, seqs)).wait_send()
        return carry

    lax.fori_loop(1, seqs, grad_left, 0)
    gather.drain()
    scatter3.drain()
    for copy in strips_sent + to_core + to_near + tiles_sent:
        copy.wait_send()


def chip_at(mask):
    return {axis: 1 - lax.axis_index(axis) for axis in BITS if mask & BITS[axis]}


def wide_at(mask):
    at = chip_at(mask & 7)
    if mask & 8:
        at["g"] = 1 - lax.axis_index("g")
    return at


def run_middle(
    lengths, mix, hn, dy, xn, w_in, w_dn, w_qkv, dy_own, hmid, gain_ffn, w_o, qkv, toep, gain, scores, weights, outs, strips
):
    seqs, rows, _ = hn.shape
    dma = pltpu.SemaphoreType.DMA
    part = BLK // 32
    tiles = 4 * ROW_TILES**2 + 3 * ROW_TILES * FF_TILES
    shapes = [
        ((seqs, rows, BLK), bf16), ((rows, D), f32), ((rows, D), f32), ((1, D), f32), ((2 * CQ * CK, rows), f32),
        ((8, rows), f32), ((1, 2 * HP), f32), ((tiles + 1, part, BLK), bf16),
    ]

    def low(*dims):
        return pltpu.VMEM(dims, bf16)

    every, heads = low(CHIPS, rows, D), low(CHIPS, rows, 2 * DH)
    return pl.pallas_call(
        middle_body,
        in_specs=[SMEM] * 2 + [ANYS] * 3 + [VMEM] * 14,
        out_specs=[VMEM] * len(shapes),
        out_shape=[jax.ShapeDtypeStruct(*shape) for shape in shapes],
        scratch_shapes=[
            pltpu.VMEM((2, rows, CQ * rows), f32), pltpu.VMEM((rows + 8, rows), f32), every, every, low(seqs, rows, 2 * BLK), every, low(rows, D), heads, heads, heads,
            low(ROW_TILES, 2, CHIPS, 2, part, 2 * BLK), low(2, CHIPS, 2, part, D),
            low(ROW_TILES, CHIPS, 2, part, 2 * BLK), low(CHIPS, 2, part, D),
            low(ROW_TILES, CHIPS, part, 2 * BLK), low(CHIPS, part, D),
            low(seqs, rows, 6 * DH), low(ROW_TILES, 2, CHIPS, 2, part, 6 * DH), low(ROW_TILES, 2, 2, part, D),
            low(ROW_TILES, CHIPS, 2, part, 6 * DH), low(ROW_TILES, 2, part, D),
            low(2 * CHIPS, ROW_TILES, part, 6 * DH), low(ROW_TILES, part, D),
            low(3, rows, D), low(rows, D), low(3, rows, D), dma((1,)), dma((9,)),
        ] + [dma((8,))] * 4 + [dma((6,))] * 2 + [dma((5,))] * 2 + [dma((9 * CHIPS,))] * 2 + [dma((16,))] * 2
        + scatter_scratch(rows, D) + [dma((3,))] * 2 + [dma((3, 2))] * 4 + side_sems(),
        name="middle",
        compiler_params=pltpu.CompilerParams(collective_id=3, has_side_effects=True, vmem_limit_bytes=63 * 2**20),
    )(
        lengths, mix, hn, dy, xn, w_in, w_dn, w_qkv, dy_own, hmid, gain_ffn, w_o,
        qkv, toep, gain, scores, weights, outs, strips,
    )


def to_slots_body(
    pick_ref, tiles_ref, vec_ref, inner_ref, w_dn_ref, hmid_ref, out_ref, vecs_ref, layer_ref,
    slots_ref, parts_ref, local_sems, send, recv, vec_send, vec_recv, *scatter_args,
):
    devices = lax.axis_size(ALL)
    own_slots, side = out_ref.shape[:2]
    part = slots_ref.shape[1]

    def fill(at, carry):
        slots_ref[at] = tiles_ref[pick_ref[at]]
        return carry

    lax.fori_loop(0, slots_ref.shape[0], fill, 0)
    me = device_index()
    place = (lax.axis_index("c") * CHIPS + chip_index()) * 2 + lax.axis_index("g")
    rows = pl.ds(pl.multiple_of(place * part, part), part)
    local = [pltpu.make_async_copy(vec_ref.at[me], vecs_ref.at[me], local_sems.at[0])]
    for slot in range(own_slots):
        local.append(
            pltpu.make_async_copy(
                slots_ref.at[me * own_slots + slot], out_ref.at[slot, rows], local_sems.at[1 + slot]
            )
        )
    for copy in local:
        copy.start()
    greet_all()

    def push_all(step, carry):
        to = lax.rem(me + step, devices)
        pltpu.make_async_remote_copy(
            src_ref=vec_ref.at[to], dst_ref=vecs_ref.at[me], send_sem=vec_send, recv_sem=vec_recv, device_id=device_at(to)
        ).start()
        for slot in range(own_slots):
            pltpu.make_async_remote_copy(
                src_ref=slots_ref.at[to * own_slots + slot], dst_ref=out_ref.at[slot, rows],
                send_sem=send, recv_sem=recv, device_id=device_at(to),
            ).start()
        return carry

    lax.fori_loop(1, devices, push_all, 0)

    seqs, length = inner_ref.shape[:2]

    def outputs(at, carry):
        two = pl.ds(at * 2, 2)
        made = dot(inner_ref[two].reshape(2 * length, BLK), w_dn_ref[...])
        parts_ref[two] = made.astype(bf16).reshape(2, length, D)
        return carry

    lax.fori_loop(0, seqs // 2, outputs, 0)
    scatter = SideScatter(parts_ref, *scatter_args)
    scatter.start()
    scatter.onward()
    scatter.last()
    layer_ref[...] = (hmid_ref[...] + scatter.finish()).astype(bf16)
    scatter.drain()
    others = vecs_ref.at[pl.ds(0, devices - 1)]
    pltpu.make_async_copy(others, others, vec_recv).wait()
    pltpu.make_async_copy(others, others, vec_send).wait()
    others = out_ref.at[:, pl.ds(0, side - part)]
    pltpu.make_async_copy(others, others, recv).wait()
    pltpu.make_async_copy(others, others, send).wait()
    for copy in local:
        copy.wait()


def to_slots(pick, tiles, vecs, inner, w_dn, hmid, own_slots):
    rows = hmid.shape[0]
    dma = pltpu.SemaphoreType.DMA
    return pl.pallas_call(
        to_slots_body,
        in_specs=[SMEM, VMEM, ANYS] + [VMEM] * 3,
        out_specs=[ANYS] * 2 + [VMEM],
        out_shape=[
            jax.ShapeDtypeStruct((own_slots, BLK, BLK), bf16), jax.ShapeDtypeStruct(vecs.shape, vecs.dtype),
            jax.ShapeDtypeStruct(hmid.shape, bf16),
        ],
        scratch_shapes=[
            pltpu.VMEM((pick.shape[0],) + tiles.shape[1:], bf16), pltpu.VMEM((CHIPS, rows, D), bf16), dma((1 + own_slots,)),
        ] + [dma] * 4 + side_scatter_scratch(rows, D),
        name="to_slots",
        compiler_params=pltpu.CompilerParams(collective_id=6, has_side_effects=True, vmem_limit_bytes=32 * 2**20),
    )(pick, tiles, vecs, inner, w_dn, hmid)


def update_body(grad_ref, left_ref, right_ref, master_ref, first_ref, second_ref, first_out, second_out, master_out, copy_out):
    left, right = left_ref[0].astype(bf16), right_ref[0].astype(bf16)
    rotated = dot(dot_tn(left, grad_ref[0]).astype(bf16), right)
    first = beta_first * first_ref[0] + (1.0 - beta_first) * rotated
    second = beta_second * second_ref[0] + (1.0 - beta_second) * rotated * rotated
    first_out[0] = first
    second_out[0] = second
    direction = (first / (jnp.sqrt(second) + eps_adam)).astype(bf16)
    turned = dot_nt(dot(left, direction).astype(bf16), right)
    master = master_ref[0]
    master = master - rate_block * (turned + decay_block * master)
    master_out[0] = master
    copy_out[0] = master.astype(bf16)


def update(grad, left, right, master, first, second):
    spec = pl.BlockSpec((1, BLK, BLK), lambda slot: (slot, 0, 0))
    return pl.pallas_call(
        update_body,
        grid=(grad.shape[0],),
        in_specs=[spec] * 6,
        out_specs=[spec] * 4,
        out_shape=[jax.ShapeDtypeStruct(grad.shape, kind) for kind in (f32, f32, f32, bf16)],
        name="update",
        compiler_params=pltpu.CompilerParams(vmem_limit_bytes=40 * 2**20),
        cost_estimate=pl.CostEstimate(flops=43 * 10**8, bytes_accessed=36 * 2**20, transcendentals=10**6),
    )(grad, left, right, master, first, second)


def body_fast(
    layer_input, lengths, cotangent, w_query, w_key, w_value, w_out, w_gate, w_up, w_down, vec_copy, owners,
    basis_left, basis_right, block_master, block_first, block_second, vec_master, vec_first, vec_second,
):
    chip = chip_index()
    seq_len = layer_input.shape[0]
    own_vec = vec_copy.shape[0]
    devices, fs_size, reps = lax.axis_size(ALL), lax.axis_size(FS), lax.axis_size("y")

    fs_index = ((lax.axis_index("g") * 2 + lax.axis_index("a")) * 2 + lax.axis_index("b")) * 2 + lax.axis_index("c")
    first_rows = vector_rows(own_vec, fs_size)
    flat = lax.dynamic_update_slice_in_dim(jnp.zeros((fs_size * own_vec,), f32), vec_copy.astype(f32), fs_index * own_vec, 0)
    first = lax.dynamic_index_in_dim(jnp.array(first_rows, jnp.int32), fs_index, 0, keepdims=False)
    vec = lax.dynamic_slice_in_dim(rows_of_vector(flat), first, SHARD_ROWS, 0)

    (
        dy, group_lengths, mix, gains, toep, gain_pair, xn, qkv, scores, weights, outs, heads, hmid, w_qkv, w_out_all,
        hn_rows, w_in, w_dn, dy_rows,
    ) = run_front(
        first_rows, lengths, vec, layer_input, w_query, w_key, w_value, cotangent, w_out, w_gate, w_up, w_down
    )
    gain_attn = gains[0]
    w_qkv = w_qkv.reshape(D, 6 * DH)
    w_in, w_dn = w_in.reshape(D, 2 * BLK), w_dn.reshape(BLK, D)
    strip = BLK // (2 * CHIPS)
    part = strip // 2
    heads = jnp.transpose(heads, (1, 0, 2)).reshape(seq_len, 2 * ROW_TILES, CHIPS, strip)
    strips = jnp.transpose(heads, (2, 0, 1, 3)).reshape(CHIPS, seq_len, 2 * ROW_TILES * strip)
    input_float = layer_input.astype(f32)
    input_scale = rms(input_float)

    own_slots = basis_left.shape[0]
    matches = jnp.arange(own_slots * devices)[:, None] == owners[None, :]
    tile_count = owners.shape[0]
    pick = jnp.min(jnp.where(matches, jnp.arange(tile_count, dtype=jnp.int32)[None, :], tile_count), axis=1)
    inner, dhmid, dxn, grad_gain_ffn, theta_sums, mixer_sums, gain_sums, tiles = run_middle(
        group_lengths[:, 0, 0].astype(jnp.int32), mix[0, :4], hn_rows, dy_rows, xn, w_in, w_dn, w_qkv, dy, hmid, gains[1:2],
        w_out_all.reshape(CHIPS, 2 * DH, D), qkv, toep, gain_pair, scores, weights, outs, strips,
    )
    dinput, grad_gain_attn = norm_backward(input_float, input_scale, gain_attn, dxn)
    input_grad = dinput + dhmid

    grad_theta = jnp.sum(theta_sums, axis=1)
    grad_mixer = jnp.sum(mixer_sums[:4], axis=1)
    vector_grad = jnp.concatenate(
        [
            grad_gain_attn,
            lax.dynamic_update_slice_in_dim(
                jnp.zeros((D,), f32), gain_sums.reshape(2, HP)[:, :DH].reshape(-1), chip * 2 * DH, 0
            ),
            grad_gain_ffn.reshape(-1),
            lax.dynamic_update_slice_in_dim(
                jnp.zeros((H * CQ * CK,), f32), grad_theta.reshape(-1), chip * 2 * CQ * CK, 0
            ),
            lax.dynamic_update_slice_in_dim(jnp.zeros((2 * H,), f32), grad_mixer, chip * 4, 0),
        ]
    )
    pieces = jnp.pad(vector_grad.reshape(fs_size, 1, own_vec), ((0, 0), (0, 0), (0, 1024 - own_vec)))
    pieces = jnp.broadcast_to(pieces, (fs_size, reps, 1024)).reshape(devices, 8, 128)

    own_grad, pieces, layer_output = to_slots(
        pick, tiles, pieces, inner, w_dn, hmid, own_slots
    )
    vector_total = jnp.sum(pieces, axis=0).reshape(1024)[:own_vec]
    first_new, second_new, master_new, copy_new = update(
        own_grad, basis_left, basis_right, block_master, block_first, block_second
    )
    vec_first_new = beta_first * vec_first + (1.0 - beta_first) * vector_total
    vec_second_new = beta_second * vec_second + (1.0 - beta_second) * vector_total * vector_total
    vec_master_new = vec_master - rate_vector * vec_first_new / (jnp.sqrt(vec_second_new) + eps_adam)
    return (
        layer_output, input_grad, first_new, second_new, master_new, copy_new,
        vec_first_new, vec_second_new, vec_master_new, vec_master_new.astype(bf16),
    )


def solution(mesh):
    fsdp, rep = mesh.shape["fsdp"], mesh.shape["rep"]
    fine = Mesh(mesh.devices.reshape(fsdp // 8, 2, 2, 2, rep), ALL)
    rows, both = P(ALL, None), P(ALL, None, None)
    weight, vec = P(FS, None), P(FS)
    return jax.shard_map(
        body_fast if (fsdp, rep) == (16, 2) else body_any,
        mesh=fine,
        in_specs=(rows, P(ALL), rows) + (weight,) * 7 + (vec, P()) + (both,) * 5 + (vec,) * 3,
        out_specs=(rows, rows) + (both,) * 4 + (vec,) * 4,
        check_vma=False,
    )
```

```python
import functools
import math

import jax
import jax.numpy as jnp
import numpy as np
from jax import lax
from jax.experimental import pallas as pl
from jax.experimental.pallas import tpu as pltpu
from jax.sharding import Mesh
from jax.sharding import PartitionSpec as P

H = 16
DH = 96
HP = 128
D = H * DH
FF = 4096
CQ = 6
CK = 11
BLK = 512
CHIPS = 8
ROW_TILES = D // BLK
FF_TILES = FF // BLK

eps_norm = 1e-05
eps_adam = 1e-08
rate_block = 0.02
rate_vector = 0.3
decay_block = 0.1
beta_first = 0.5
beta_second = 0.5

FS = ("g", "a", "b", "c")
CHIP = ("y", "a", "b")
ALL = ("g", "a", "b", "c", "y")
bf16 = jnp.bfloat16
f32 = jnp.float32


def dot(left, right):
    return jnp.dot(left, right, preferred_element_type=f32)


def dot_nt(left, right):
    return lax.dot_general(left, right, (((1,), (1,)), ((), ())), preferred_element_type=f32)


def dot_tn(left, right):
    return lax.dot_general(left, right, (((0,), (0,)), ((), ())), preferred_element_type=f32)


def rms(values):
    return lax.rsqrt(jnp.mean(values * values, axis=-1, keepdims=True) + eps_norm)


def norm_backward(values, scale, gain, grad):
    unit = values * scale
    inner = grad * gain
    grad_values = scale * (inner - unit * jnp.mean(inner * unit, axis=-1, keepdims=True))
    return grad_values, jnp.sum(grad * unit, axis=0)


def shifted_down(pad_ref, values):
    rows = values.shape[0]
    pad_ref[8 : 8 + rows, :] = values
    return jnp.concatenate(
        [values] + [pad_ref[8 - lag : 8 - lag + rows, :] for lag in range(1, CQ)], axis=1
    )


def shifted_up(pad_ref, values):
    rows = values.shape[0]
    pad_ref[0:rows, :] = values
    return jnp.concatenate(
        [values] + [pad_ref[lag : lag + rows, :] for lag in range(1, CQ)], axis=1
    )


def attention_forward(len_ref, mix_ref, qkv_ref, toep_ref, gain_ref, heads_ref, s_ref, p_ref, o_ref, pad_ref):
    rows = qkv_ref.shape[1]
    length = len_ref[pl.program_id(0)]
    query_at = lax.broadcasted_iota(jnp.int32, (rows, rows), 0)
    key_at = lax.broadcasted_iota(jnp.int32, (rows, rows), 1)
    keep = (key_at <= query_at) & (key_at < length)
    pad_ref[0:8, :] = jnp.zeros((8, rows), f32)
    weights = []
    for head in range(2):
        query = qkv_ref[0, :, head * HP : (head + 1) * HP]
        key = qkv_ref[0, :, (2 + head) * HP : (3 + head) * HP]
        scores = jnp.where(keep, dot_nt(query, key) * (1.0 / math.sqrt(DH)), 0.0)
        s_ref[0, head] = scores.astype(bf16)
        wide = shifted_down(pad_ref, scores)
        high = wide.astype(bf16)
        low = (wide - high.astype(f32)).astype(bf16)
        conv = dot(high, toep_ref[head]) + dot(low, toep_ref[head])
        logits = jnp.where(keep, conv, -1e30)
        weight = jnp.exp(logits - jnp.max(logits, axis=-1, keepdims=True))
        weight = weight / jnp.sum(weight, axis=-1, keepdims=True)
        p_ref[0, head] = weight
        weights.append(weight)
    for head in range(2):
        mixed = mix_ref[2 * head] * weights[0] + mix_ref[2 * head + 1] * weights[1]
        value = qkv_ref[0, :, (4 + head) * HP : (5 + head) * HP]
        out = dot(mixed.astype(bf16), value)
        o_ref[0, :, head * HP : (head + 1) * HP] = out
        scale = lax.rsqrt(jnp.sum(out * out, axis=-1, keepdims=True) * (1.0 / DH) + eps_norm)
        heads_ref[0, :, head * HP : (head + 1) * HP] = (
            out * scale * gain_ref[:, head * HP : (head + 1) * HP]
        ).astype(bf16)


def attention_backward(
    len_ref, mix_ref, qkv_ref, toep_ref, gain_ref, s_ref, p_ref, o_ref, grad_ref,
    dqkv_ref, theta_ref, mixer_ref, gain_grad_ref, pad_ref,
):
    rows = qkv_ref.shape[1]
    length = len_ref[pl.program_id(0)]
    query_at = lax.broadcasted_iota(jnp.int32, (rows, rows), 0)
    key_at = lax.broadcasted_iota(jnp.int32, (rows, rows), 1)
    keep = (key_at <= query_at) & (key_at < length)
    pad_ref[rows : rows + 8, :] = jnp.zeros((8, rows), f32)

    @pl.when(pl.program_id(0) == 0)
    def _():
        theta_ref[...] = jnp.zeros_like(theta_ref)
        mixer_ref[...] = jnp.zeros_like(mixer_ref)
        gain_grad_ref[...] = jnp.zeros_like(gain_grad_ref)

    weights = [p_ref[0, 0], p_ref[0, 1]]
    grad_mixed = []
    for head in range(2):
        cols = slice(head * HP, (head + 1) * HP)
        out = o_ref[0, :, cols]
        grad = grad_ref[0, :, cols].astype(f32)
        scale = lax.rsqrt(jnp.sum(out * out, axis=-1, keepdims=True) * (1.0 / DH) + eps_norm)
        unit = out * scale
        gain_grad_ref[:, cols] += jnp.sum(grad * unit, axis=0, keepdims=True)
        inner = grad * gain_ref[:, cols]
        grad_out = scale * (inner - unit * (jnp.sum(inner * unit, axis=-1, keepdims=True) * (1.0 / DH)))
        grad_out = grad_out.astype(bf16)
        value = qkv_ref[0, :, (4 + head) * HP : (5 + head) * HP]
        mixed = (mix_ref[2 * head] * weights[0] + mix_ref[2 * head + 1] * weights[1]).astype(bf16)
        dqkv_ref[0, :, (4 + head) * HP : (5 + head) * HP] = dot_tn(mixed, grad_out).astype(bf16)
        back = dot_nt(grad_out, value)
        grad_mixed.append(back)
        for source in range(2):
            mixer_ref[2 * head + source : 2 * head + source + 1, :] += jnp.sum(
                back * weights[source], axis=0, keepdims=True
            )
    for head in range(2):
        grad_weight = mix_ref[head] * grad_mixed[0] + mix_ref[2 + head] * grad_mixed[1]
        weight = weights[head]
        grad_conv = weight * (grad_weight - jnp.sum(weight * grad_weight, axis=-1, keepdims=True))
        wide = shifted_up(pad_ref, grad_conv).astype(bf16)
        theta_ref[head] += dot_tn(s_ref[0, head], wide)
        grad_scores = jnp.zeros((rows, rows), f32)
        for lag in range(CQ):
            grad_scores += dot_nt(
                wide[:, lag * rows : (lag + 1) * rows], toep_ref[head, lag * rows : (lag + 1) * rows, :]
            )
        grad_scores = jnp.where(keep, grad_scores * (1.0 / math.sqrt(DH)), 0.0).astype(bf16)
        query = qkv_ref[0, :, head * HP : (head + 1) * HP]
        key = qkv_ref[0, :, (2 + head) * HP : (3 + head) * HP]
        dqkv_ref[0, :, head * HP : (head + 1) * HP] = dot(grad_scores, key).astype(bf16)
        dqkv_ref[0, :, (2 + head) * HP : (3 + head) * HP] = dot_tn(grad_scores, query).astype(bf16)


SMEM = pl.BlockSpec(memory_space=pltpu.SMEM)


def seq_spec(*dims):
    return pl.BlockSpec((1,) + dims, lambda s: (s,) + (0,) * len(dims))


def whole_spec(*dims):
    return pl.BlockSpec(dims, lambda s: (0,) * len(dims))


def run_forward(lengths, mix, qkv, toep, gain):
    seqs, rows, _ = qkv.shape
    return pl.pallas_call(
        attention_forward,
        grid=(seqs,),
        in_specs=[SMEM, SMEM, seq_spec(rows, 6 * HP), whole_spec(2, CQ * rows, rows), whole_spec(1, 2 * HP)],
        out_specs=[seq_spec(rows, 2 * HP), seq_spec(2, rows, rows), seq_spec(2, rows, rows), seq_spec(rows, 2 * HP)],
        out_shape=[
            jax.ShapeDtypeStruct((seqs, rows, 2 * HP), bf16),
            jax.ShapeDtypeStruct((seqs, 2, rows, rows), bf16),
            jax.ShapeDtypeStruct((seqs, 2, rows, rows), f32),
            jax.ShapeDtypeStruct((seqs, rows, 2 * HP), f32),
        ],
        scratch_shapes=[pltpu.VMEM((rows + 8, rows), f32)],
        name="attention_forward",
        compiler_params=pltpu.CompilerParams(vmem_limit_bytes=24 * 2**20),
        cost_estimate=pl.CostEstimate(flops=2 * 10**9, bytes_accessed=8 * 2**20, transcendentals=10**5),
    )(lengths, mix, qkv, toep, gain)


def run_backward(lengths, mix, qkv, toep, gain, scores, weights, outs, grads):
    seqs, rows, _ = qkv.shape
    return pl.pallas_call(
        attention_backward,
        grid=(seqs,),
        in_specs=[
            SMEM, SMEM, seq_spec(rows, 6 * HP), whole_spec(2, CQ * rows, rows), whole_spec(1, 2 * HP),
            seq_spec(2, rows, rows), seq_spec(2, rows, rows), seq_spec(rows, 2 * HP), seq_spec(rows, 2 * HP),
        ],
        out_specs=[seq_spec(rows, 6 * HP), whole_spec(2, rows, CQ * rows), whole_spec(8, rows), whole_spec(1, 2 * HP)],
        out_shape=[
            jax.ShapeDtypeStruct((seqs, rows, 6 * HP), bf16),
            jax.ShapeDtypeStruct((2, rows, CQ * rows), f32),
            jax.ShapeDtypeStruct((8, rows), f32),
            jax.ShapeDtypeStruct((1, 2 * HP), f32),
        ],
        scratch_shapes=[pltpu.VMEM((rows + 8, rows), f32)],
        name="attention_backward",
        compiler_params=pltpu.CompilerParams(vmem_limit_bytes=24 * 2**20),
        cost_estimate=pl.CostEstimate(flops=4 * 10**9, bytes_accessed=12 * 2**20, transcendentals=10**5),
    )(lengths, mix, qkv, toep, gain, scores, weights, outs, grads)


BITS = {"y": 4, "a": 2, "b": 1}
HOPS = (("y", "b", "a"), ("a", "y", "b"), ("b", "a", "y"))
THIRDS = ((0, 48), (48, 48), (96, 32))
ANYS = pl.BlockSpec(memory_space=pl.ANY)


def chip_index():
    return (lax.axis_index("y") * 2 + lax.axis_index("a")) * 2 + lax.axis_index("b")


def flipped(chip, axes):
    for axis in axes:
        chip = chip + BITS[axis] * (1 - 2 * lax.axis_index(axis))
    return chip


def across(axis):
    return {axis: 1 - lax.axis_index(axis)}


def device_index():
    index = lax.axis_index("g")
    for axis in ("a", "b", "c", "y"):
        index = index * lax.axis_size(axis) + lax.axis_index(axis)
    return index


def device_at(index):
    at = {}
    for axis in ("y", "c", "b", "a", "g"):
        at[axis] = lax.rem(index, lax.axis_size(axis))
        index = lax.div(index, lax.axis_size(axis))
    return at


def greet_all():
    devices = lax.axis_size(ALL)
    me = device_index()
    barrier = pltpu.get_barrier_semaphore()

    def greet(step, carry):
        pl.semaphore_signal(barrier, inc=1, device_id=device_at(lax.rem(me + step, devices)))
        return carry

    lax.fori_loop(1, devices, greet, 0)
    pl.semaphore_wait(barrier, devices - 1)


def greet_neighbours():
    barrier = pltpu.get_barrier_semaphore()
    for axis in BITS:
        pl.semaphore_signal(barrier, inc=1, device_id=across(axis))
    pl.semaphore_wait(barrier, 3)


def remote(src, dst, send, recv, axis):
    return pltpu.make_async_remote_copy(src_ref=src, dst_ref=dst, send_sem=send, recv_sem=recv, device_id=across(axis))


def gather_body(x_ref, out_ref, *sems):
    greet_neighbours()
    gather_hops(x_ref, out_ref, *sems)


def gather_first_body(x_ref, vec_ref, out_ref, vecs_ref, vec_send, vec_recv, vec_local, *sems):
    devices = lax.axis_size(ALL)
    me = device_index()
    local = pltpu.make_async_copy(vec_ref, vecs_ref.at[me], vec_local)
    local.start()
    greet_all()

    def push(step, carry):
        pltpu.make_async_remote_copy(
            src_ref=vec_ref, dst_ref=vecs_ref.at[me], send_sem=vec_send, recv_sem=vec_recv,
            device_id=device_at(lax.rem(me + step, devices)),
        ).start()
        return carry

    lax.fori_loop(1, devices, push, 0)
    gather_hops(x_ref, out_ref, *sems)
    others = vecs_ref.at[pl.ds(0, devices - 1)]
    pltpu.make_async_copy(others, others, vec_recv).wait()
    pltpu.make_async_copy(others, others, vec_send).wait()
    local.wait()


def gather_hops(x_ref, out_ref, local_sem, send1, recv1, send2, recv2, send3, recv3):
    me = chip_index()
    rows = x_ref.shape[0]
    half = rows // 2
    local = pltpu.make_async_copy(x_ref, out_ref.at[me], local_sem)
    local.start()
    first = []
    for part in range(2):
        here = pl.ds(part * half, half)
        for at, (axis, _, _) in enumerate(HOPS):
            copy = remote(x_ref.at[here], out_ref.at[me, here], send1.at[at, part], recv1.at[at, part], axis)
            copy.start()
            first.append(copy)
    second = []
    for part in range(2):
        here = pl.ds(part * half, half)
        for at, (axis, onward, _) in enumerate(HOPS):
            first[part * 3 + at].wait_recv()
            block = out_ref.at[flipped(me, (axis,)), here]
            copy = remote(block, block, send2.at[at, part], recv2.at[at, part], onward)
            copy.start()
            second.append(copy)
    third = []
    for at, (axis, onward, last) in enumerate(HOPS):
        begin, count = THIRDS[at]
        block = flipped(me, (axis, onward))
        for part in range(2):
            if part * half < begin + count and begin < (part + 1) * half:
                second[part * 3 + at].wait_recv()
        piece = out_ref.at[block, pl.ds(begin, count)]
        copy = remote(piece, piece, send3.at[at], recv3.at[at], last)
        copy.start()
        third.append(copy)
    for at in range(3):
        begin, count = THIRDS[at]
        for part in range(2):
            if not (part * half < begin + count and begin < (part + 1) * half):
                second[part * 3 + at].wait_recv()
    for copy in third:
        copy.wait_recv()
    for copy in first + second + third:
        copy.wait_send()
    local.wait()


def hop_sems():
    dma = pltpu.SemaphoreType.DMA
    return [dma] + [dma((3, 2))] * 4 + [dma((3,))] * 2


def gather_first(rows, vec, collective_id):
    count, width = rows.shape
    return pl.pallas_call(
        gather_first_body,
        in_specs=[ANYS, ANYS],
        out_specs=[ANYS, ANYS],
        out_shape=[
            jax.ShapeDtypeStruct((CHIPS, count, width), rows.dtype),
            jax.ShapeDtypeStruct((lax.axis_size(ALL),) + vec.shape, vec.dtype),
        ],
        scratch_shapes=[pltpu.SemaphoreType.DMA] * 3 + hop_sems(),
        name="gather_first",
        compiler_params=pltpu.CompilerParams(collective_id=collective_id, has_side_effects=True),
    )(rows, vec)


def gather_chips(rows, collective_id):
    count, width = rows.shape
    return pl.pallas_call(
        gather_body,
        in_specs=[ANYS],
        out_specs=ANYS,
        out_shape=jax.ShapeDtypeStruct((CHIPS, count, width), rows.dtype),
        scratch_shapes=hop_sems(),
        name="gather_chips",
        compiler_params=pltpu.CompilerParams(collective_id=collective_id, has_side_effects=True),
    )(rows)


def scatter_body(
    parts_ref, out_ref, near_ref, in2_ref, in3_ref, acc2_ref, acc3_ref, send1, recv1, send2, recv2, send3, recv3
):
    me = chip_index()
    greet_neighbours()
    opposite = flipped(me, ("y", "a", "b"))
    first = []
    for at, (axis, onward, last) in enumerate(HOPS):
        begin, count = THIRDS[at]
        copy = remote(parts_ref.at[opposite, pl.ds(begin, count)], in2_ref.at[pl.ds(begin, count)], send1.at[at], recv1.at[at], last)
        copy.start()
        first.append(copy)
    second = []
    rows = parts_ref.shape[1]
    half = rows // 2
    for part in range(2):
        here = pl.ds(part * half, half)
        for at, (axis, onward, last) in enumerate(HOPS):
            dest = flipped(me, (axis, onward))
            begin, count = THIRDS[at]
            if part == 0:
                first[at].wait_recv()
                acc2_ref[at] = parts_ref[dest]
                piece = pl.ds(begin, count)
                acc2_ref[at, piece] = (parts_ref[dest, piece].astype(f32) + in2_ref[piece].astype(f32)).astype(bf16)
            copy = remote(acc2_ref.at[at, here], in3_ref.at[at, here], send2.at[at, part], recv2.at[at, part], onward)
            copy.start()
            second.append(copy)
    third = []
    for part in range(2):
        here = pl.ds(part * half, half)
        for at, (axis, onward, last) in enumerate(HOPS):
            dest = flipped(me, (axis,))
            second[part * 3 + at].wait_recv()
            acc3_ref[at, here] = (parts_ref[dest, here].astype(f32) + in3_ref[at, here].astype(f32)).astype(bf16)
            copy = remote(acc3_ref.at[at, here], near_ref.at[at, here], send3.at[at, part], recv3.at[at, part], axis)
            copy.start()
            third.append(copy)
    for part in range(2):
        here = pl.ds(part * half, half)
        for at in range(3):
            third[part * 3 + at].wait_recv()
        out_ref[here] = (
            (parts_ref[me, here].astype(f32) + near_ref[0, here].astype(f32))
            + (near_ref[1, here].astype(f32) + near_ref[2, here].astype(f32))
        )
    for copy in first + second + third:
        copy.wait_send()


def scatter_chips(parts, collective_id):
    _, rows, width = parts.shape
    vmem = pl.BlockSpec(memory_space=pltpu.VMEM)
    dma = pltpu.SemaphoreType.DMA
    return pl.pallas_call(
        scatter_body,
        in_specs=[vmem],
        out_specs=vmem,
        out_shape=jax.ShapeDtypeStruct((rows, width), f32),
        scratch_shapes=[pltpu.VMEM((3, rows, width), bf16), pltpu.VMEM((rows, width), bf16)] + [pltpu.VMEM((3, rows, width), bf16)] * 3
        + [dma((3,))] * 2 + [dma((3, 2))] * 4,
        name="scatter_chips",
        compiler_params=pltpu.CompilerParams(collective_id=collective_id, has_side_effects=True, vmem_limit_bytes=32*2**20),
    )(parts)


def gather_slow(rows):
    return lax.all_to_all(
        jnp.broadcast_to(rows[None], (CHIPS,) + rows.shape), CHIP, split_axis=0, concat_axis=0, tiled=True
    )


def exchange_chips(parts):
    return lax.all_to_all(parts, CHIP, split_axis=0, concat_axis=0, tiled=True)


def scatter_slow(parts):
    return jnp.sum(exchange_chips(parts.astype(bf16)).astype(f32), axis=0)


def swap(values, axis):
    return lax.ppermute(values, axis, [(0, 1), (1, 0)])


def both_cores(own, axis):
    other = swap(own, "c")
    first = lax.axis_index("c") == 0
    return jnp.stack([jnp.where(first, own, other), jnp.where(first, other, own)], axis=axis)


def half_for_core(values, axis):
    core = lax.axis_index("c")
    own = lax.dynamic_index_in_dim(values, core, axis, keepdims=False)
    sent = lax.dynamic_index_in_dim(values, 1 - core, axis, keepdims=False)
    return own + swap(sent.astype(bf16), "c").astype(f32)


def sum_groups(tiles):
    groups = lax.axis_size("g")
    if groups != 2:
        return lax.psum_scatter(tiles.astype(f32), "g", scatter_dimension=1, tiled=True).astype(bf16)
    part = tiles.shape[1] // 2
    group = lax.axis_index("g")
    own = lax.dynamic_slice_in_dim(tiles, group * part, part, 1)
    sent = lax.dynamic_slice_in_dim(tiles, (1 - group) * part, part, 1)
    return (own.astype(f32) + swap(sent, "g").astype(f32)).astype(bf16)


def spread_columns(weight, width):
    rows = weight.shape[0]
    blocks = weight.reshape(rows, 2, CHIPS // 2, width)
    mine = lax.dynamic_index_in_dim(blocks, lax.axis_index("y"), 1, keepdims=False)
    return jnp.transpose(mine, (1, 0, 2))


def to_columns(blocks):
    groups = lax.axis_size("g")
    sent = jnp.broadcast_to(blocks[None], (groups,) + blocks.shape).reshape((-1,) + blocks.shape[1:])
    got = lax.all_to_all(sent, ("g", "a", "b"), split_axis=0, concat_axis=0, tiled=True)
    return both_cores(got, 1).reshape(-1, blocks.shape[-1])


def down_rows(w_down, chip):
    if lax.axis_size("g") == 2:
        other = swap(w_down, "g")
        mine = jnp.where(lax.axis_index("g") == lax.axis_index("y"), w_down, other)
        return both_cores(mine, 0).reshape(BLK, D)
    return lax.dynamic_slice_in_dim(lax.all_gather(w_down, FS, axis=0, tiled=True), chip * BLK, BLK, 0)


def band():
    tap = np.arange(CK)[:, None, None]
    source = np.arange(128)[None, :, None]
    target = np.arange(128)[None, None, :]
    return source - target + CK // 2 == tap


def body_any(
    layer_input, lengths, cotangent, w_query, w_key, w_value, w_out, w_gate, w_up, w_down, vec_copy, owners,
    basis_left, basis_right, block_master, block_first, block_second, vec_master, vec_first, vec_second,
):
    chip = (lax.axis_index("y") * 2 + lax.axis_index("a")) * 2 + lax.axis_index("b")
    fs_index = ((lax.axis_index("g") * 2 + lax.axis_index("a")) * 2 + lax.axis_index("b")) * 2 + lax.axis_index("c")
    seq_len = layer_input.shape[0]
    length = lengths[0]
    reps = lax.axis_size("y")
    fs_size = lax.axis_size(FS)

    own_vec = vec_copy.shape[0]
    small = jnp.concatenate(
        [vec_copy.astype(f32), jnp.zeros((1023 - own_vec,), f32), length.astype(f32).reshape(1)]
    ).reshape(8, 128)
    x_all, small_all = gather_first(layer_input, small, 1)
    small_all = small_all.reshape(fs_size, reps, 1024)
    vector = small_all[:, 0, :own_vec].reshape(-1)
    group_lengths = small_all[:, :, 1023].reshape(-1, 2, 2, 2, reps)
    group_lengths = lax.dynamic_index_in_dim(group_lengths, lax.axis_index("g"), 0, keepdims=False)
    group_lengths = lax.dynamic_index_in_dim(group_lengths, lax.axis_index("c"), 2, keepdims=False)
    group_lengths = jnp.transpose(group_lengths, (2, 0, 1)).reshape(CHIPS).astype(jnp.int32)
    gain_attn, gain_head, gain_ffn = vector[:D], vector[D : 2 * D], vector[2 * D : 3 * D]
    conv_end = 3 * D + H * CQ * CK
    theta = lax.dynamic_slice_in_dim(vector[3 * D : conv_end].reshape(H, CQ, CK), chip * 2, 2, 0)
    mixer = lax.dynamic_slice_in_dim(vector[conv_end : conv_end + 2 * H].reshape(H, 2), chip * 2, 2, 0)
    mix = mixer.reshape(4)
    gain_pair = jnp.pad(
        lax.dynamic_slice_in_dim(gain_head.reshape(H, DH), chip * 2, 2, 0), ((0, 0), (0, HP - DH))
    ).reshape(1, 2 * HP)
    toep = jnp.zeros((2, CQ, seq_len, seq_len), f32)
    offset = (
        jnp.arange(seq_len, dtype=jnp.int32)[:, None] - jnp.arange(seq_len, dtype=jnp.int32)[None, :] + CK // 2
    )
    for tap in range(CK):
        toep = jnp.where(offset[None, None] == tap, theta[:, :, tap][:, :, None, None], toep)
    toep = toep.astype(bf16).reshape(2, CQ * seq_len, seq_len)

    qkv_rows = to_columns(
        jnp.concatenate([spread_columns(w, 2 * DH) for w in (w_query, w_key, w_value)], axis=2)
    )
    w_qkv = jnp.pad(qkv_rows.reshape(D, 6, DH), ((0, 0), (0, 0), (0, HP - DH))).reshape(D, 6 * HP)
    w_in = to_columns(jnp.concatenate([spread_columns(w, BLK) for w in (w_gate, w_up)], axis=2))
    w_dn = down_rows(w_down, chip)
    w_o = lax.all_gather(w_out, FS, axis=0, tiled=True)

    input_float = layer_input.astype(f32)
    input_scale = rms(input_float)
    x_rows = x_all.reshape(CHIPS * seq_len, D).astype(f32)
    xn_rows = (x_rows * rms(x_rows) * gain_attn).astype(bf16)
    qkv = dot(xn_rows, w_qkv).astype(bf16).reshape(CHIPS, seq_len, 6 * HP)
    heads_pad, scores, weights, outs = run_forward(group_lengths, mix, qkv, toep, gain_pair)
    heads_sent = heads_pad.reshape(CHIPS, seq_len, 2, HP)[..., :DH].reshape(CHIPS, seq_len, 2 * DH)
    heads = jnp.transpose(exchange_chips(heads_sent), (1, 0, 2)).reshape(seq_len, D)
    hmid = input_float + dot(heads, w_o)
    hmid_scale = rms(hmid)
    hn_rows = gather_chips((hmid * hmid_scale * gain_ffn).astype(bf16), 2).reshape(CHIPS * seq_len, D)
    both = dot(hn_rows, w_in)
    gate, up = both[:, :BLK], both[:, BLK:]
    sig = jax.nn.sigmoid(gate)
    silu = gate * sig
    inner = (silu * up).astype(bf16)
    ffn = scatter_slow(dot(inner, w_dn).reshape(CHIPS, seq_len, D))
    layer_output = (hmid + ffn).astype(bf16)

    valid = (jnp.arange(seq_len) < length).astype(f32)
    dy = cotangent.astype(f32) * valid[:, None]
    dy_rows = gather_slow(dy.astype(bf16)).reshape(CHIPS * seq_len, D)
    dinner = dot_nt(dy_rows, w_dn)
    dgate = (dinner * up * (sig * (1.0 + gate * (1.0 - sig)))).astype(bf16)
    dup = (dinner * silu).astype(bf16)
    dboth = jnp.concatenate([dgate, dup], axis=1)
    dhn = scatter_chips(dot_nt(dboth, w_in).astype(bf16).reshape(CHIPS, seq_len, D), 3)
    dhmid, grad_gain_ffn = norm_backward(hmid, hmid_scale, gain_ffn, dhn)
    dhmid = dhmid + dy
    dattn = dhmid.astype(bf16)
    dheads = dot_nt(dattn, w_o).astype(bf16).reshape(seq_len, CHIPS, 2 * DH)
    dheads = exchange_chips(jnp.transpose(dheads, (1, 0, 2)))
    dheads = jnp.pad(dheads.reshape(CHIPS, seq_len, 2, DH), ((0, 0), (0, 0), (0, 0), (0, HP - DH)))
    dqkv, theta_sums, mixer_sums, gain_sums = run_backward(
        group_lengths, mix, qkv, toep, gain_pair, scores, weights, outs, dheads.reshape(CHIPS, seq_len, 2 * HP)
    )
    dqkv_rows = dqkv.reshape(CHIPS * seq_len, 6 * HP)
    dxn = scatter_slow(dot_nt(dqkv_rows, w_qkv).reshape(CHIPS, seq_len, D))
    dinput, grad_gain_attn = norm_backward(input_float, input_scale, gain_attn, dxn)
    input_grad = dinput + dhmid

    taps = jnp.asarray(band())
    theta_sums = theta_sums.reshape(2, seq_len, CQ, seq_len)
    grad_theta = jnp.stack(
        [jnp.sum(jnp.where(taps[tap][None, :, None, :], theta_sums, 0.0), axis=(1, 3)) for tap in range(CK)], axis=2
    )
    grad_mixer = jnp.sum(mixer_sums[:4], axis=1)
    vector_grad = jnp.concatenate(
        [
            grad_gain_attn,
            lax.dynamic_update_slice_in_dim(
                jnp.zeros((D,), f32), gain_sums.reshape(2, HP)[:, :DH].reshape(-1), chip * 2 * DH, 0
            ),
            grad_gain_ffn,
            lax.dynamic_update_slice_in_dim(
                jnp.zeros((H * CQ * CK,), f32), grad_theta.reshape(-1), chip * 2 * CQ * CK, 0
            ),
            lax.dynamic_update_slice_in_dim(jnp.zeros((2 * H,), f32), grad_mixer, chip * 4, 0),
        ]
    )
    pieces = jnp.pad(vector_grad.reshape(fs_size, 1, own_vec), ((0, 0), (0, 0), (0, 512 - own_vec)))
    pieces = jnp.broadcast_to(pieces, (fs_size, reps, 512)).reshape(-1, 4, 128)
    vector_total = jnp.sum(
        lax.all_to_all(pieces, ALL, split_axis=0, concat_axis=0, tiled=True), axis=0
    ).reshape(512)[:own_vec]

    strip = BLK // (2 * CHIPS)
    grad_in = dot_tn(hn_rows, dboth).reshape(ROW_TILES, 2, CHIPS, strip, 2, BLK)
    grad_down = dot_tn(inner, dy_rows).reshape(2, CHIPS, strip, ROW_TILES, BLK)
    grad_in = jnp.transpose(half_for_core(grad_in, 1), (1, 3, 0, 2, 4)).reshape(CHIPS, 2 * ROW_TILES, strip, BLK)
    grad_down = jnp.transpose(half_for_core(grad_down, 0), (0, 2, 1, 3))
    ffn_tiles = exchange_chips(jnp.concatenate([grad_in, grad_down], axis=1).astype(bf16))
    gate_tiles = jnp.transpose(ffn_tiles[:, : 2 * ROW_TILES], (1, 0, 2, 3)).reshape(-1, strip, BLK)
    down_tiles = ffn_tiles[:, 2 * ROW_TILES :].reshape(-1, strip, BLK)
    grad_qkv = dot_tn(xn_rows, dqkv_rows).reshape(ROW_TILES, 2, CHIPS, strip, 6, HP)[..., :DH]
    grad_qkv = jnp.transpose(half_for_core(grad_qkv, 1), (1, 0, 2, 3, 4))
    grad_qkv = exchange_chips(grad_qkv.astype(bf16).reshape(CHIPS, ROW_TILES, strip, 6 * DH))
    grad_qkv = jnp.transpose(
        grad_qkv.reshape(CHIPS, ROW_TILES, strip, 3, 2 * DH), (3, 1, 2, 0, 4)
    ).reshape(3, ROW_TILES, strip, ROW_TILES, BLK)
    qkv_tiles = jnp.transpose(grad_qkv, (0, 1, 3, 2, 4)).reshape(-1, strip, BLK)
    heads_strips = jnp.transpose(heads.reshape(seq_len, 2 * ROW_TILES, CHIPS, strip), (2, 0, 1, 3))
    heads_strips = exchange_chips(heads_strips.reshape(CHIPS, seq_len, 2 * ROW_TILES * strip))
    dattn_rows = gather_slow(dattn).reshape(CHIPS * seq_len, D)
    grad_out = dot_tn(heads_strips.reshape(CHIPS * seq_len, -1), dattn_rows)
    grad_out = half_for_core(grad_out.reshape(ROW_TILES, 2, strip, ROW_TILES, BLK), 1)
    out_tiles = jnp.transpose(grad_out.astype(bf16), (0, 2, 1, 3)).reshape(-1, strip, BLK)

    groups = lax.axis_size("g")
    part = strip // groups
    own_slots = basis_left.shape[0]
    devices = groups * 2 * CHIPS
    slot_total = own_slots * devices
    sums = jnp.concatenate(
        [sum_groups(jnp.concatenate([qkv_tiles, out_tiles], axis=0)), sum_groups(jnp.concatenate([gate_tiles, down_tiles], axis=0))],
        axis=0,
    )
    matches = (jnp.arange(slot_total)[:, None] == owners[None, :]).astype(bf16)
    slots = dot(matches, sums.reshape(sums.shape[0], -1)).astype(bf16)
    slots = lax.all_to_all(
        slots.reshape(devices, own_slots, part, BLK), ALL, split_axis=0, concat_axis=0, tiled=True
    )
    slots = slots.reshape(groups, 2, 2, 2, 2, own_slots, part, BLK)
    own_grad = jnp.transpose(slots, (5, 3, 4, 1, 2, 0, 6, 7)).reshape(own_slots, BLK, BLK)

    left_low, right_low = basis_left.astype(bf16), basis_right.astype(bf16)
    rotated = jnp.einsum("sia,sij->saj", left_low, own_grad, preferred_element_type=f32)
    rotated = jnp.einsum("saj,sjb->sab", rotated.astype(bf16), right_low, preferred_element_type=f32)
    first_new = beta_first * block_first + (1.0 - beta_first) * rotated
    second_new = beta_second * block_second + (1.0 - beta_second) * rotated * rotated
    direction = (first_new / (jnp.sqrt(second_new) + eps_adam)).astype(bf16)
    turned = jnp.einsum("sia,sab->sib", left_low, direction, preferred_element_type=f32)
    turned = jnp.einsum("sib,sjb->sij", turned.astype(bf16), right_low, preferred_element_type=f32)
    master_new = block_master - rate_block * (turned + decay_block * block_master)
    vec_first_new = beta_first * vec_first + (1.0 - beta_first) * vector_total
    vec_second_new = beta_second * vec_second + (1.0 - beta_second) * vector_total * vector_total
    vec_master_new = vec_master - rate_vector * vec_first_new / (jnp.sqrt(vec_second_new) + eps_adam)
    return (
        layer_output, input_grad, first_new, second_new, master_new, master_new.astype(bf16),
        vec_first_new, vec_second_new, vec_master_new, vec_master_new.astype(bf16),
    )


def group_at(mask):
    return {axis: 1 - lax.axis_index(axis) for axis, bit in (("g", 4), ("a", 2), ("b", 1)) if mask & bit}


def other_bit(axis, changed):
    at = lax.axis_index(axis)
    return 1 - at if changed else at


def push(src, dst, send, recv, device):
    copy = pltpu.make_async_remote_copy(src_ref=src, dst_ref=dst, send_sem=send, recv_sem=recv, device_id=device)
    copy.start()
    return copy


class Gather:
    def __init__(self, x_ref, out_ref, local_sem, send1, recv1, send2, recv2, send3, recv3):
        self.x, self.out, self.local_sem = x_ref, out_ref, local_sem
        self.sems = ((send1, recv1), (send2, recv2), (send3, recv3))
        self.me = chip_index()
        self.half = x_ref.shape[0] // 2
        self.sent, self.second = [], []

    def here(self, part):
        return pl.ds(part * self.half, self.half)

    def start(self):
        self.local = pltpu.make_async_copy(self.x, self.out.at[self.me], self.local_sem)
        self.local.start()
        send, recv = self.sems[0]
        for part in range(2):
            for at, (axis, _, _) in enumerate(HOPS):
                self.sent.append(
                    push(
                        self.x.at[self.here(part)], self.out.at[self.me, self.here(part)],
                        send.at[at, part], recv.at[at, part], across(axis),
                    )
                )

    def onward(self):
        send, recv = self.sems[1]
        for part in range(2):
            for at, (axis, onward, _) in enumerate(HOPS):
                self.sent[part * 3 + at].wait_recv()
                block = self.out.at[flipped(self.me, (axis,)), self.here(part)]
                self.second.append(push(block, block, send.at[at, part], recv.at[at, part], across(onward)))

    def last(self):
        send, recv = self.sems[2]
        self.third = []
        for copy in self.second:
            copy.wait_recv()
        for at, (axis, onward, last) in enumerate(HOPS):
            begin, count = THIRDS[at]
            piece = self.out.at[flipped(self.me, (axis, onward)), pl.ds(begin, count)]
            self.third.append(push(piece, piece, send.at[at], recv.at[at], across(last)))

    def finish(self):
        for copy in self.third:
            copy.wait_recv()
        self.local.wait()

    def drain(self):
        for copy in self.sent + self.second + self.third:
            copy.wait_send()


class SideGather:
    def __init__(self, x_ref, out_ref, local_sem, send1, recv1, send2, recv2, send3, recv3):
        self.x, self.out, self.local_sem = x_ref, out_ref, local_sem
        self.sems = ((send1, recv1), (send2, recv2), (send3, recv3))
        self.me = chip_index()
        half = x_ref.shape[0] // 2
        self.low, self.high = pl.ds(0, half), pl.ds(half, half)

    def start(self):
        self.local = pltpu.make_async_copy(self.x, self.out.at[self.me], self.local_sem)
        self.local.start()
        send, recv = self.sems[0]
        self.first = [
            push(self.x, self.out.at[self.me], send.at[at], recv.at[at], across(axis)) for at, axis in enumerate("aby")
        ]

    def onward(self):
        send, recv = self.sems[1]
        blocks = [self.out.at[flipped(self.me, (axis,))] for axis in "aby"]
        self.first[0].wait_recv()
        self.second = [
            push(blocks[0], blocks[0], send.at[0], recv.at[0], across("b")),
            push(blocks[0], blocks[0], send.at[1], recv.at[1], across("y")),
        ]
        self.first[1].wait_recv()
        piece = blocks[1].at[self.high]
        self.second.append(push(piece, piece, send.at[2], recv.at[2], across("y")))
        self.first[2].wait_recv()
        piece = blocks[2].at[self.low]
        self.second.append(push(piece, piece, send.at[3], recv.at[3], across("b")))

    def last(self):
        send, recv = self.sems[2]
        self.second[0].wait_recv()
        piece = self.out.at[flipped(self.me, ("a", "b")), self.high]
        self.third = [push(piece, piece, send.at[0], recv.at[0], across("y"))]
        self.second[1].wait_recv()
        piece = self.out.at[flipped(self.me, ("a", "y")), self.low]
        self.third.append(push(piece, piece, send.at[1], recv.at[1], across("b")))

    def finish(self):
        for copy in self.second[2:] + self.third:
            copy.wait_recv()
        self.local.wait()

    def drain(self):
        for copy in self.first + self.second + self.third:
            copy.wait_send()


def side_sems():
    dma = pltpu.SemaphoreType.DMA
    return [dma] + [dma((3,))] * 2 + [dma((4,))] * 2 + [dma((2,))] * 2


class Scatter:
    def __init__(self, parts, near, in2, in3, acc2, acc3, send1, recv1, send2, recv2, send3, recv3):
        self.parts, self.near, self.in2, self.in3, self.acc2, self.acc3 = parts, near, in2, in3, acc2, acc3
        self.sems = ((send1, recv1), (send2, recv2), (send3, recv3))
        self.me = chip_index()
        self.half = parts.shape[1] // 2

    def here(self, part):
        return pl.ds(part * self.half, self.half)

    def start(self):
        send, recv = self.sems[0]
        opposite = flipped(self.me, ("y", "a", "b"))
        self.first = []
        for at, (_, _, last) in enumerate(HOPS):
            rows = pl.ds(*THIRDS[at])
            self.first.append(push(self.parts.at[opposite, rows], self.in2.at[rows], send.at[at], recv.at[at], across(last)))

    def onward(self):
        send, recv = self.sems[1]
        self.second = []
        for part in range(2):
            for at, (axis, onward, _) in enumerate(HOPS):
                dest = flipped(self.me, (axis, onward))
                if part == 0:
                    self.first[at].wait_recv()
                    rows = pl.ds(*THIRDS[at])
                    self.acc2[at] = self.parts[dest]
                    self.acc2[at, rows] = (
                        self.parts[dest, rows].astype(f32) + self.in2[rows].astype(f32)
                    ).astype(bf16)
                here = self.here(part)
                self.second.append(
                    push(self.acc2.at[at, here], self.in3.at[at, here], send.at[at, part], recv.at[at, part], across(onward))
                )

    def last(self):
        send, recv = self.sems[2]
        self.third = []
        for part in range(2):
            here = self.here(part)
            for at, (axis, _, _) in enumerate(HOPS):
                dest = flipped(self.me, (axis,))
                self.second[part * 3 + at].wait_recv()
                self.acc3[at, here] = (
                    self.parts[dest, here].astype(f32) + self.in3[at, here].astype(f32)
                ).astype(bf16)
                self.third.append(
                    push(self.acc3.at[at, here], self.near.at[at, here], send.at[at, part], recv.at[at, part], across(axis))
                )

    def finish(self, part):
        here = self.here(part)
        for at in range(3):
            self.third[part * 3 + at].wait_recv()
        return (self.parts[self.me, here].astype(f32) + self.near[0, here].astype(f32)) + (
            self.near[1, here].astype(f32) + self.near[2, here].astype(f32)
        )

    def drain(self):
        for copy in self.first + self.second + self.third:
            copy.wait_send()


class SideScatter:
    def __init__(self, parts, near, in1, in2, acc2, acc3, send1, recv1, send2, recv2, send3, recv3):
        self.parts, self.near, self.in1, self.in2, self.acc2, self.acc3 = parts, near, in1, in2, acc2, acc3
        self.sems = ((send1, recv1), (send2, recv2), (send3, recv3))
        self.me = chip_index()
        half = parts.shape[1] // 2
        self.low, self.high = pl.ds(0, half), pl.ds(half, half)

    def start(self):
        send, recv = self.sems[0]
        far, side = flipped(self.me, ("a", "b", "y")), flipped(self.me, ("b", "y"))
        self.first = [
            push(self.parts.at[block, rows], self.in1.at[at], send.at[at], recv.at[at], across(axis))
            for at, (block, rows, axis) in enumerate(
                ((far, self.high, "y"), (far, self.low, "b"), (side, self.low, "b"), (side, self.high, "y"))
            )
        ]

    def add(self, at, axes, rows, acc):
        self.first[at].wait_recv()
        block = flipped(self.me, axes)
        acc[...] = self.parts[block]
        acc[rows] = (self.parts[block, rows].astype(f32) + self.in1[at].astype(f32)).astype(bf16)
        return acc

    def onward(self):
        send, recv = self.sems[1]
        third_send, third_recv = self.sems[2]
        self.second = [
            push(self.add(0, ("a", "b"), self.high, self.acc2.at[0]), self.in2.at[0], send.at[0], recv.at[0], across("b")),
            push(self.add(1, ("a", "y"), self.low, self.acc2.at[1]), self.in2.at[1], send.at[1], recv.at[1], across("y")),
        ]
        self.third = [
            push(self.add(at, (axis,), rows, self.acc3.at[to]), self.near.at[to], third_send.at[to], third_recv.at[to], across(axis))
            for at, axis, rows, to in ((3, "b", self.high, 1), (2, "y", self.low, 2))
        ]

    def last(self):
        send, recv = self.sems[2]
        for copy in self.second:
            copy.wait_recv()
        self.acc3[0] = (
            self.parts[flipped(self.me, ("a",))].astype(f32) + (self.in2[0].astype(f32) + self.in2[1].astype(f32))
        ).astype(bf16)
        self.third.append(push(self.acc3.at[0], self.near.at[0], send.at[0], recv.at[0], across("a")))

    def finish(self):
        for copy in self.third:
            copy.wait_recv()
        return (self.parts[self.me].astype(f32) + self.near[0].astype(f32)) + (
            self.near[1].astype(f32) + self.near[2].astype(f32)
        )

    def drain(self):
        for copy in self.first + self.second + self.third:
            copy.wait_send()


def side_scatter_scratch(rows, width):
    dma = pltpu.SemaphoreType.DMA
    return [
        pltpu.VMEM(dims + (width,), bf16) for dims in ((3, rows), (4, rows // 2), (2, rows), (2, rows), (3, rows))
    ] + [dma((4,))] * 2 + [dma((2,))] * 2 + [dma((3,))] * 2


def scatter_scratch(rows, width):
    dma = pltpu.SemaphoreType.DMA
    three = pltpu.VMEM((3, rows, width), bf16)
    return [three, pltpu.VMEM((rows, width), bf16), three, three, three] + [dma((3,))] * 2 + [dma((3, 2))] * 4


VMEM = pl.BlockSpec(memory_space=pltpu.VMEM)


HEAD_ROW, FFN_ROW, THETA_ROW, MIX_ROW, VEC_ROWS = 12, 28, 40, 56, 64
SHARD_ROWS = 16


def vector_row(at):
    for begin, row, width in (
        (3 * D + H * CQ * CK, MIX_ROW, 4), (3 * D, THETA_ROW, CQ * CK), (2 * D, FFN_ROW, 128), (D, HEAD_ROW, DH), (0, 0, 128)
    ):
        if at >= begin:
            return row + (at - begin) // width


def vector_rows(own_vec, shards):
    return [min(vector_row(shard * own_vec), VEC_ROWS - SHARD_ROWS) // 8 * 8 for shard in range(shards)]


def rows_of_vector(flat):
    conv_end = 3 * D + H * CQ * CK
    return jnp.concatenate(
        [
            flat[:D].reshape(-1, 128),
            jnp.pad(flat[D : 2 * D].reshape(H, DH), ((0, 0), (0, 128 - DH))),
            flat[2 * D : 3 * D].reshape(-1, 128),
            jnp.pad(flat[3 * D : conv_end].reshape(H, CQ * CK), ((0, 0), (0, 128 - CQ * CK))),
            jnp.pad(flat[conv_end : conv_end + 2 * H].reshape(CHIPS, 4), ((0, 0), (0, 124))),
        ],
        axis=0,
    )


def source_at(mask):
    return ((other_bit("g", mask & 4) * 2 + other_bit("a", mask & 2)) * 2 + other_bit("b", mask & 1)) * 2 + lax.axis_index("c")


def front_body(
    first_rows, length_ref, vec_ref, x_ref, w_query_ref, w_key_ref, w_value_ref, cot_ref,
    w_out_ref, w_gate_ref, w_up_ref, w_down_ref, dy_ref, len_ref, mix_ref, gains_ref, toep_ref, gain_ref, heads_ref, hmid_ref,
    xn_out, qkv_out, s_out, p_out, o_out, wq_out, wo_out, hn_all_ref, w_in_ref, w_dn_ref, dy_all_ref,
    xn_ref, qkv_ref, s_ref, p_ref, o_ref, wq_ref, wo_ref, leave_sems,
    blocks_ref, own_len_ref, vecs_ref, full_ref, x_all_ref, pad_ref, out_heads, hn_ref, passing, vec_send, vec_recv, len_send, len_recv, local_sems, q_send, q_recv, q_core_send, q_core_recv,
    o_send, o_recv, o_side_send, o_side_recv, o_core_send, o_core_recv, d_send, d_recv,
    w_send, w_recv, u_send, u_recv, core_send, core_recv, head_send, head_recv, *hops,
):
    seqs, rows, _ = x_all_ref.shape
    g, a, b, c, y = (lax.axis_index(axis) for axis in ALL)
    me = chip_index()
    mine = source_at(0)
    shard = {mask: source_at(mask) for mask in range(8)}
    low, high = pl.ds(0, BLK), pl.ds(BLK, BLK)
    order = (4, 6, 5, 7, 2, 1, 3)

    def columns(chip):
        return pl.ds(pl.multiple_of(chip * BLK, BLK), BLK)

    def block_to(mask):
        return (y * 2 + other_bit("a", mask & 2)) * 2 + other_bit("b", mask & 1)

    local = [
        pltpu.make_async_copy(w_out_ref, wo_ref.at[mine], local_sems.at[1]),
        pltpu.make_async_copy(w_gate_ref.at[:, columns(me)], w_in_ref.at[mine, :, low], local_sems.at[2]),
        pltpu.make_async_copy(w_up_ref.at[:, columns(me)], w_in_ref.at[mine, :, high], local_sems.at[3]),
    ]
    down_local = pltpu.make_async_copy(w_down_ref, w_dn_ref.at[c], local_sems.at[4])
    own_len_ref[...] = jnp.full(own_len_ref.shape, length_ref[0].astype(f32), f32)
    own_small = [
        pltpu.make_async_copy(vec_ref, vecs_ref.at[mine], local_sems.at[5]),
        pltpu.make_async_copy(own_len_ref, len_ref.at[me], local_sems.at[6]),
    ]
    for copy in local + own_small:
        copy.start()

    @pl.when(g == y)
    def _():
        down_local.start()

    greet_all()
    leaving = []

    def leave(src, dst):
        copy = pltpu.make_async_copy(src, dst, leave_sems.at[len(leaving)])
        copy.start()
        leaving.append(copy)

    sent, relayed = {}, []
    first = Gather(x_ref, x_all_ref, *hops[:7])
    side = SideGather(dy_ref, dy_all_ref, *hops[7:14])
    gather = Gather(hn_ref, hn_all_ref, *hops[14:])

    def push_vec(step, carry):
        to = lax.rem(mine + step, 16)
        pltpu.make_async_remote_copy(
            src_ref=vec_ref, dst_ref=vecs_ref.at[mine], send_sem=vec_send, recv_sem=vec_recv,
            device_id={
                "g": lax.div(to, 8), "a": lax.rem(lax.div(to, 4), 2), "b": lax.rem(lax.div(to, 2), 2), "c": lax.rem(to, 2)
            },
        ).start()
        return carry

    lax.fori_loop(1, 16, push_vec, 0)
    lengths_sent = [
        push(own_len_ref, len_ref.at[me], len_send.at[mask], len_recv.at[mask], chip_at(mask)) for mask in range(1, 8)
    ]

    first.start()
    for chip in range(CHIPS):
        cols = slice(chip * 2 * DH, (chip + 1) * 2 * DH)
        blocks_ref[chip] = jnp.concatenate([w_query_ref[:, cols], w_key_ref[:, cols], w_value_ref[:, cols]], axis=1)
    wq_ref[mine] = blocks_ref[me]
    valid = lax.broadcasted_iota(jnp.int32, cot_ref.shape, 0) < length_ref[0]
    dy_ref[...] = jnp.where(valid, cot_ref[...].astype(f32), 0.0).astype(bf16)

    for mask in order:
        sent[mask] = push(blocks_ref.at[block_to(mask)], wq_ref.at[mine], q_send.at[mask], q_recv.at[mask], group_at(mask))

    def relay_qkv(mask):
        sent[mask].wait_recv()
        block = wq_ref.at[shard[mask]]
        relayed.append(push(block, block, q_core_send.at[mask], q_core_recv.at[mask], across("c")))

    half = pl.ds(pl.multiple_of(y * 48, 16), 48)
    lines, o_side, o_core = {}, {}, []

    def start_lines():
        for mask in (2, 4, 6):
            lines[mask] = push(w_out_ref.at[half], wo_ref.at[mine, half], o_send.at[mask], o_recv.at[mask], group_at(mask))
        lines[1] = push(w_out_ref.at[half], wo_ref.at[mine, half], o_send.at[1], o_recv.at[1], across("b"))
        o_core.append(push(w_out_ref, wo_ref.at[mine], o_core_send.at[0], o_core_recv.at[0], across("c")))

    def to_side(mask):
        lines[mask].wait_recv()
        piece = wo_ref.at[shard[mask], half]
        o_side[mask] = push(piece, piece, o_side_send.at[mask], o_side_recv.at[mask], across("y"))
        if mask in (2, 4, 6):
            lines[mask + 1] = push(piece, piece, o_send.at[mask + 1], o_recv.at[mask + 1], across("b"))

    def out_to_core(masks):
        for mask in masks:
            o_side[mask].wait_recv()
            block = wo_ref.at[shard[mask]]
            o_core.append(push(block, block, o_core_send.at[mask], o_core_recv.at[mask], across("c")))

    count = w_down_ref.shape[0] // 2
    upper, lower = pl.ds(0, count), pl.ds(count, count)

    def down_copy(src, dst, at, axis):
        return pltpu.make_async_remote_copy(
            src_ref=src, dst_ref=dst, send_sem=d_send.at[at], recv_sem=d_recv.at[at], device_id=across(axis)
        )

    def down_direct():
        return down_copy(w_down_ref.at[upper], w_dn_ref.at[c, upper], 0, "g")

    def down_around():
        return down_copy(w_down_ref.at[lower], passing, 1, "g")

    def down_over():
        return down_copy(passing, w_dn_ref.at[c, lower], 2, "y")

    def down_to_core():
        return down_copy(w_dn_ref.at[c], w_dn_ref.at[c], 3, "c")

    def down_start():
        @pl.when(g == y)
        def _():
            down_direct().start()

        @pl.when(g != y)
        def _():
            down_around().start()

    def down_pass():
        @pl.when(g == y)
        def _():
            down_around().wait_recv()
            down_over().start()

    def down_last():
        @pl.when(g == y)
        def _():
            down_local.wait()
            down_to_core().start()
            down_direct().wait_send()
            down_over().wait_send()

        @pl.when(g != y)
        def _():
            down_direct().wait_recv()
            down_over().wait_recv()
            down_to_core().start()
            down_around().wait_send()

    gate, up = {}, {}

    def send_columns(masks):
        for mask in masks:
            to = columns(block_to(mask))
            gate[mask] = push(w_gate_ref.at[:, to], w_in_ref.at[mine, :, low], w_send.at[mask], w_recv.at[mask], group_at(mask))
            up[mask] = push(w_up_ref.at[:, to], w_in_ref.at[mine, :, high], u_send.at[mask], u_recv.at[mask], group_at(mask))

    def relay(mask):
        gate[mask].wait_recv()
        up[mask].wait_recv()
        block = w_in_ref.at[shard[mask]]
        relayed.append(push(block, block, core_send.at[mask], core_recv.at[mask], across("c")))

    side.start()
    relayed.append(push(wq_ref.at[mine], wq_ref.at[mine], q_core_send.at[0], q_core_recv.at[0], across("c")))
    first.onward()
    start_lines()

    for copy in own_small:
        copy.wait()
    others = vecs_ref.at[pl.ds(0, 15)]
    pltpu.make_async_copy(others, others, vec_recv).wait()
    full_ref[...] = jnp.zeros_like(full_ref)
    for at, row in enumerate(first_rows):
        full_ref[row : row + SHARD_ROWS, :] += vecs_ref[at]
    gains_ref[...] = jnp.zeros_like(gains_ref)
    for row in range(D // 128):
        gains_ref[0:1, row * 128 : (row + 1) * 128] = full_ref[row : row + 1, :]
        gains_ref[1:2, row * 128 : (row + 1) * 128] = full_ref[FFN_ROW + row : FFN_ROW + row + 1, :]
    mix_ref[...] = jnp.zeros_like(mix_ref)
    mix_row = full_ref[pl.ds(MIX_ROW + me, 1), :]
    for at in range(4):
        mix_ref[at : at + 1, :] = jnp.broadcast_to(mix_row[:, at : at + 1], (1, 128))
    query_at = lax.broadcasted_iota(jnp.int32, (rows, rows), 0)
    key_at = lax.broadcasted_iota(jnp.int32, (rows, rows), 1)
    key_float = key_at.astype(f32)
    tap_at = query_at - key_at + CK // 2
    for head in range(2):
        gain_ref[:, head * HP : (head + 1) * HP] = full_ref[pl.ds(HEAD_ROW + 2 * me + head, 1), :]
        theta = full_ref[pl.ds(THETA_ROW + 2 * me + head, 1), :]
        for lag in range(CQ):
            band_values = jnp.zeros((rows, rows), f32)
            for tap in range(CK):
                at = lag * CK + tap
                band_values = jnp.where(tap_at == tap, theta[:, at : at + 1], band_values)
            toep_ref[head, lag * rows : (lag + 1) * rows, :] = band_values.astype(bf16)

    side.onward()
    first.last()
    side.last()
    down_start()
    for mask in order:
        relay_qkv(mask)
    send_columns((2, 1, 3, 4, 6, 5, 7))
    first.finish()
    for copy in relayed + lengths_sent:
        copy.wait_recv()
    qkv_relayed = relayed[:]
    del relayed[:]

    pad_ref[0:8, :] = jnp.zeros((8, rows), f32)
    blank = jnp.zeros((rows, HP - DH), bf16)
    batch = 4

    def project(at, carry):
        values = x_all_ref[pl.ds(at * batch, batch)].astype(f32).reshape(batch * rows, D)
        normed = (values * rms(values) * gains_ref[0:1, :]).astype(bf16)
        xn_ref[pl.ds(at * batch, batch)] = normed.reshape(batch, rows, D)
        made = dot(normed, wq_ref[...].reshape(D, 6 * DH)).astype(bf16)
        for seq in range(batch):
            for piece in range(6):
                qkv_ref[at * batch + seq, :, piece * HP : (piece + 1) * HP] = jnp.concatenate(
                    [made[seq * rows : (seq + 1) * rows, piece * DH : (piece + 1) * DH], blank], axis=1
                )
        return carry

    project(0, 0)
    for mask in (2, 4, 6, 1):
        to_side(mask)
    project(1, 0)
    leave(xn_ref, xn_out)
    leave(qkv_ref, qkv_out)
    leave(wq_ref, wq_out)
    for copy in local:
        copy.wait()
    relayed.append(push(w_in_ref.at[mine], w_in_ref.at[mine], core_send.at[0], core_recv.at[0], across("c")))

    def head_copy(seq):
        return pltpu.make_async_remote_copy(
            src_ref=out_heads.at[seq], dst_ref=heads_ref.at[me], send_sem=head_send.at[seq], recv_sem=head_recv.at[me],
            device_id={"y": lax.div(seq, 4), "a": lax.rem(lax.div(seq, 2), 2), "b": lax.rem(seq, 2)},
        )

    def attend(step, carry):
        seq = lax.rem(me + step, seqs)
        keep = (key_at <= query_at) & (key_float < len_ref[seq, 0:1, :])
        weights, made = [], []
        for head in range(2):
            query = qkv_ref[seq, :, head * HP : (head + 1) * HP]
            key = qkv_ref[seq, :, (2 + head) * HP : (3 + head) * HP]
            scores = jnp.where(keep, dot_nt(query, key) * (1.0 / math.sqrt(DH)), 0.0)
            s_ref[seq, head] = scores.astype(bf16)
            wide = shifted_down(pad_ref, scores)
            near = wide.astype(bf16)
            rest = (wide - near.astype(f32)).astype(bf16)
            conv = dot(near, toep_ref[head]) + dot(rest, toep_ref[head])
            logits = jnp.where(keep, conv, -1e30)
            weight = jnp.exp(logits - jnp.max(logits, axis=-1, keepdims=True))
            weight = weight / jnp.sum(weight, axis=-1, keepdims=True)
            p_ref[seq, head] = weight
            weights.append(weight)
        for head in range(2):
            mixed = mix_ref[2 * head : 2 * head + 1, :] * weights[0] + mix_ref[2 * head + 1 : 2 * head + 2, :] * weights[1]
            value = qkv_ref[seq, :, (4 + head) * HP : (5 + head) * HP]
            out = dot(mixed.astype(bf16), value)
            o_ref[seq, :, head * HP : (head + 1) * HP] = out
            scale = lax.rsqrt(jnp.sum(out * out, axis=-1, keepdims=True) * (1.0 / DH) + eps_norm)
            made.append((out * scale * gain_ref[:, head * HP : (head + 1) * HP])[:, :DH])
        out_heads[seq] = jnp.concatenate(made, axis=1).astype(bf16)

        @pl.when(step > 0)
        def _():
            head_copy(seq).start()

        return carry

    lax.fori_loop(0, 3, attend, 0)
    for mask in (3, 5, 7):
        to_side(mask)
    down_pass()
    lax.fori_loop(3, 6, attend, 0)
    out_to_core((2, 4, 6))
    lax.fori_loop(6, seqs, attend, 0)
    out_to_core((1, 3, 5, 7))
    heads_ref[me] = out_heads[me]
    leave(s_ref, s_out)
    leave(p_ref, p_out)
    leave(o_ref, o_out)
    for copy in o_core:
        copy.wait_recv()
    leave(wo_ref, wo_out)

    def head_arrived(step, carry):
        source = lax.rem(me + step, seqs)
        pltpu.make_async_copy(out_heads.at[source], heads_ref.at[source], head_recv.at[source]).wait()
        return carry

    lax.fori_loop(1, seqs, head_arrived, 0)

    def project_out(at, carry):
        cols = pl.ds(pl.multiple_of(at * BLK, BLK), BLK)
        total = x_ref[:, cols].astype(f32)
        for chip in range(CHIPS):
            weight = wo_ref[2 * chip : 2 * chip + 2, :, cols].reshape(2 * DH, BLK)
            total += dot(heads_ref[chip], weight)
        hmid_ref[:, cols] = total
        return carry

    lax.fori_loop(0, ROW_TILES, project_out, 0)
    hmid = hmid_ref[...]
    hn_ref[...] = (hmid * rms(hmid) * gains_ref[1:2, :]).astype(bf16)
    gather.start()
    for mask in (4, 6):
        relay(mask)
    gather.onward()
    for mask in (5, 7, 2):
        relay(mask)
    gather.last()
    for mask in (1, 3):
        relay(mask)
    down_last()
    down_to_core().wait()
    side.finish()
    gather.finish()
    for copy in relayed:
        copy.wait_recv()
    for copy in leaving:
        copy.wait()

    def head_left(step, carry):
        head_copy(lax.rem(me + step, seqs)).wait_send()
        return carry

    lax.fori_loop(1, seqs, head_left, 0)
    first.drain()
    side.drain()
    gather.drain()
    for copies in (sent, lines, o_side, gate, up):
        for copy in copies.values():
            copy.wait_send()
    pltpu.make_async_copy(others, others, vec_send).wait()
    for copy in qkv_relayed + relayed + o_core + lengths_sent:
        copy.wait_send()


def run_front(first_rows, length, vec, x, w_query, w_key, w_value, cotangent, w_out, w_gate, w_up, w_down):
    rows = x.shape[0]
    dma = pltpu.SemaphoreType.DMA
    small = [
        (x.shape, bf16), ((CHIPS, 8, 128), f32), ((8, 128), f32), ((8, D), f32), ((2, CQ * rows, rows), bf16), ((1, 2 * HP), f32),
        ((CHIPS, rows, 2 * DH), bf16), ((rows, D), f32),
    ]
    large = [
        ((CHIPS, rows, D), bf16), ((CHIPS, rows, 6 * HP), bf16), ((CHIPS, 2, rows, rows), bf16), ((CHIPS, 2, rows, rows), f32),
        ((CHIPS, rows, 2 * HP), f32), ((16, w_query.shape[0], 6 * DH), bf16), ((16,) + w_out.shape, bf16),
    ]
    gathered = [
        ((CHIPS, rows, D), bf16), ((16, w_gate.shape[0], 2 * BLK), bf16), ((2,) + w_down.shape, bf16), ((CHIPS, rows, D), bf16),
    ]
    return pl.pallas_call(
        functools.partial(front_body, first_rows),
        in_specs=[SMEM] + [VMEM] * 6 + [ANYS] * 4,
        out_specs=[VMEM] * len(small) + [ANYS] * (len(large) + len(gathered)),
        out_shape=[jax.ShapeDtypeStruct(*shape) for shape in small + large + gathered],
        scratch_shapes=[pltpu.VMEM(*shape) for shape in large] + [
            dma((len(large),)),
            pltpu.VMEM((CHIPS, w_query.shape[0], 6 * DH), bf16), pltpu.VMEM((8, 128), f32), pltpu.VMEM((16,) + vec.shape, f32), pltpu.VMEM((VEC_ROWS, 128), f32), pltpu.VMEM((CHIPS, rows, D), bf16), pltpu.VMEM((rows + 8, rows), f32), pltpu.VMEM((CHIPS, rows, 2 * DH), bf16),
            pltpu.VMEM((rows, D), bf16), pltpu.VMEM((w_down.shape[0] // 2, D), bf16), dma, dma, dma((8,)), dma((8,)), dma((7,)),
        ] + [dma((8,))] * 10 + [dma((4,))] * 2 + [dma((8,))] * 8 + hop_sems() + side_sems() + hop_sems(),
        name="front",
        compiler_params=pltpu.CompilerParams(collective_id=2, has_side_effects=True, vmem_limit_bytes=56 * 2**20),
    )(length, vec, x, w_query, w_key, w_value, cotangent, w_out, w_gate, w_up, w_down)


def middle_body(
    len_ref, mix_ref, hn_ref, dy_ref, xn_ref, w_in_hbm, w_dn_hbm, wq_hbm, dy_own_ref, hmid_ref, gains_ref, wo_hbm,
    qkv_hbm, toep_ref, gain_ref, s_hbm, p_hbm, o_hbm, strips_ref,
    inner_ref, dhmid_ref, dxn_ref, gain_ffn_grad_ref, theta_ref, mixer_ref, gain_grad_ref, tiles_ref,
    w_in_ref, w_dn_ref, wq_ref, wo_ref, qkv_ref, s_ref, p_ref, o_ref, enter_sems,
    theta_sums, pad_ref, first_ref, second_ref, dboth_ref, parts_ref, dattn_ref, grads_ref, sent_ref, strips_in, gin_ref, gd_ref,
    half_in, half_d, near_in, near_d, dqkv_ref, gq_ref, go_ref, core_q, core_o, in_q, in_o,
    near3, in23, in33, local_sems, load_sems, strip_send, strip_recv, head_send, head_recv,
    core_send, core_recv, near_send, near_recv, gu_send, gu_recv, q_send, q_recv, *rest,
):
    scatter_args, scatter3_sems, side = rest[:11], rest[11:17], rest[17:]
    seqs, rows, _ = hn_ref.shape
    g, a, b, c, y = (lax.axis_index(axis) for axis in ALL)
    me = chip_index()
    pairs = [(1 - y) * 2 + 1 - a, (1 - y) * 2 + a, y * 2 + 1 - a, y * 2 + a]
    loads = []
    for at, pair in enumerate(pairs):
        two = pl.ds(pair * 2, 2)
        loads.append(
            [
                pltpu.make_async_copy(hn_ref.at[two], first_ref.at[two], load_sems.at[at]),
                pltpu.make_async_copy(dy_ref.at[two], second_ref.at[two], load_sems.at[4 + at]),
            ]
        )
    enter = [
        pltpu.make_async_copy(src, dst, enter_sems.at[at])
        for at, (src, dst) in enumerate(
            (
                (w_in_hbm, w_in_ref), (w_dn_hbm, w_dn_ref), (wo_hbm, wo_ref), (qkv_hbm, qkv_ref), (s_hbm, s_ref),
                (p_hbm, p_ref), (o_hbm, o_ref), (wq_hbm, wq_ref),
            )
        )
    ]
    enter[0].start()
    for copies in loads:
        for copy in copies:
            copy.start()
    for copy in enter[1:]:
        copy.start()
    strip_local = pltpu.make_async_copy(strips_ref.at[me], strips_in.at[me], local_sems.at[0])
    strip_local.start()
    greet_all()
    chips = (7, 6, 5, 3, 4, 2, 1)
    to_chip = {mask: flipped(me, [axis for axis in BITS if mask & BITS[axis]]) for mask in chips}
    strips_sent = [
        push(strips_ref.at[to_chip[mask]], strips_in.at[me], strip_send.at[mask], strip_recv.at[mask], chip_at(mask))
        for mask in chips
    ]

    def hidden(pair):
        two = pl.ds(pair * 2, 2)
        both = dot(first_ref[two].reshape(2 * rows, D), w_in_ref[...])
        gate, up = both[:, :BLK], both[:, BLK:]
        dinner = dot_nt(second_ref[two].reshape(2 * rows, D), w_dn_ref[...])
        sig = jax.nn.sigmoid(gate)
        silu = gate * sig
        inner_ref[two] = (silu * up).astype(bf16).reshape(2, rows, BLK)
        dgate = (dinner * up * (sig * (1.0 + gate * (1.0 - sig)))).astype(bf16)
        dup = (dinner * silu).astype(bf16)
        dboth_ref[two, :, 0:BLK] = dgate.reshape(2, rows, BLK)
        dboth_ref[two, :, BLK:] = dup.reshape(2, rows, BLK)
        back = dot_nt(dgate, w_in_ref[:, 0:BLK]) + dot_nt(dup, w_in_ref[:, BLK:])
        parts_ref[two] = back.astype(bf16).reshape(2, rows, D)

    def wait_load(at):
        for copy in loads[at]:
            copy.wait()

    wait_load(0)
    enter[0].wait()
    enter[1].wait()
    hidden(pairs[0])
    scatter = Scatter(parts_ref, *scatter_args)
    scatter.start()
    wait_load(1)
    wait_load(2)

    def two_more(step, carry):
        hidden((1 - y) * 2 + a + step * ((2 * y - 1) * 2 + 1 - a - a))
        return carry

    lax.fori_loop(0, 2, two_more, 0)
    scatter.onward()
    wait_load(3)
    hidden(pairs[3])

    def down_grad(col, carry):
        cols = pl.ds(pl.multiple_of(col * BLK, BLK), BLK)
        made = dot_tn(inner_ref[...].reshape(seqs * rows, BLK), second_ref[:, :, cols].reshape(seqs * rows, BLK))
        gd_ref[:, :, :, :, cols] = made.astype(bf16).reshape(2, CHIPS, 2, BLK // 32, BLK)
        return carry

    lax.fori_loop(0, ROW_TILES, down_grad, 0)
    to_core = [push(gd_ref.at[1 - c], half_d, core_send.at[0], core_recv.at[0], across("c"))]

    def in_grad(row, carry):
        values = first_ref[:, :, pl.ds(pl.multiple_of(row * BLK, BLK), BLK)].reshape(seqs * rows, BLK)
        for which in range(2):
            cols = slice(which * BLK, (which + 1) * BLK)
            made = dot_tn(values, dboth_ref[:, :, cols].reshape(seqs * rows, BLK))
            gin_ref[row, :, :, :, :, cols] = made.astype(bf16).reshape(2, CHIPS, 2, BLK // 32, BLK)
        return carry

    def in_to_core(row):
        to_core.append(push(gin_ref.at[row, 1 - c], half_in.at[row], core_send.at[1 + row], core_recv.at[1 + row], across("c")))

    in_grad(0, 0)
    in_to_core(0)
    to_core[0].wait_recv()

    def core_down(chip, carry):
        half_d[chip] = (half_d[chip].astype(f32) + gd_ref[c, chip].astype(f32)).astype(bf16)
        return carry

    lax.fori_loop(0, CHIPS, core_down, 0)
    to_near = [push(half_d.at[:, 1 - g], near_d, near_send.at[0], near_recv.at[0], across("g"))]
    scatter.last()
    lax.fori_loop(1, ROW_TILES, in_grad, 0)
    in_to_core(1)
    in_to_core(2)
    xn_load = pltpu.make_async_copy(xn_ref, first_ref, load_sems.at[8])
    xn_load.start()

    def core_rows(row):
        to_core[1 + row].wait_recv()

        def core_chip(chip, carry):
            half_in[row, chip] = (half_in[row, chip].astype(f32) + gin_ref[row, c, chip].astype(f32)).astype(bf16)
            return carry

        lax.fori_loop(0, CHIPS, core_chip, 0)
        to_near.append(push(half_in.at[row, :, 1 - g], near_in.at[row], near_send.at[1 + row], near_recv.at[1 + row], across("g")))

    core_rows(0)
    core_rows(1)
    core_rows(2)
    half = rows // 2
    gain_sum = jnp.zeros((1, D), f32)
    for part in range(2):
        here = pl.ds(part * half, half)
        grad = scatter.finish(part)
        values = hmid_ref[here]
        scale = rms(values)
        unit = values * scale
        inside = grad * gains_ref[1:2, :]
        gain_sum += jnp.sum(grad * unit, axis=0, keepdims=True)
        dhmid = scale * (inside - unit * jnp.mean(inside * unit, axis=-1, keepdims=True)) + dy_own_ref[here].astype(f32)
        dhmid_ref[here] = dhmid
        dattn_ref[here] = dhmid.astype(bf16)
    gain_ffn_grad_ref[...] = gain_sum

    for copy in enter[2:]:
        copy.wait()

    def grad_copy(to):
        return pltpu.make_async_remote_copy(
            src_ref=sent_ref.at[to], dst_ref=grads_ref.at[me], send_sem=head_send.at[to], recv_sem=head_recv.at[me],
            device_id={"y": lax.div(to, 4), "a": lax.rem(lax.div(to, 2), 2), "b": lax.rem(to, 2)},
        )

    def send_grad(step, carry):
        to = lax.rem(me + step, seqs)
        sent_ref[to] = dot_nt(dattn_ref[...], wo_ref[to]).astype(bf16)

        @pl.when(step > 0)
        def _():
            grad_copy(to).start()

        return carry

    lax.fori_loop(0, seqs, send_grad, 0)
    grads_ref[me] = sent_ref[me]
    gather = SideGather(dattn_ref, second_ref, *side)
    gather.start()

    pad_ref[rows : rows + 8, :] = jnp.zeros((8, rows), f32)
    theta_sums[...] = jnp.zeros_like(theta_sums)
    mixer_ref[...] = jnp.zeros_like(mixer_ref)
    gain_grad_ref[...] = jnp.zeros_like(gain_grad_ref)
    query_at = lax.broadcasted_iota(jnp.int32, (rows, rows), 0)
    key_at = lax.broadcasted_iota(jnp.int32, (rows, rows), 1)
    key_float = key_at.astype(f32)
    blank = jnp.zeros((rows, HP - DH), f32)

    def grad_arrived(step, carry):
        source = lax.rem(me + step, seqs)
        pltpu.make_async_copy(sent_ref.at[source], grads_ref.at[source], head_recv.at[source]).wait()
        return carry

    lax.fori_loop(1, seqs, grad_arrived, 0)

    def one(seq, carry):
        keep = (key_at <= query_at) & (key_float < len_ref[seq, 0:1, :])
        weights = [p_ref[seq, 0], p_ref[seq, 1]]
        grad_mixed, made = [], [None] * 6
        grads = grads_ref[seq].astype(f32)
        for head in range(2):
            cols = slice(head * HP, (head + 1) * HP)
            out = o_ref[seq, :, cols]
            grad = jnp.concatenate([grads[:, head * DH : (head + 1) * DH], blank], axis=1)
            scale = lax.rsqrt(jnp.sum(out * out, axis=-1, keepdims=True) * (1.0 / DH) + eps_norm)
            unit = out * scale
            gain_grad_ref[:, cols] += jnp.sum(grad * unit, axis=0, keepdims=True)
            inner = grad * gain_ref[:, cols]
            grad_out = scale * (inner - unit * (jnp.sum(inner * unit, axis=-1, keepdims=True) * (1.0 / DH)))
            grad_out = grad_out.astype(bf16)
            value = qkv_ref[seq, :, (4 + head) * HP : (5 + head) * HP]
            mixed = (
                mix_ref[2 * head : 2 * head + 1, :] * weights[0] + mix_ref[2 * head + 1 : 2 * head + 2, :] * weights[1]
            ).astype(bf16)
            made[4 + head] = dot_tn(mixed, grad_out)
            back = dot_nt(grad_out, value)
            grad_mixed.append(back)
            for source in range(2):
                mixer_ref[2 * head + source : 2 * head + source + 1, :] += jnp.sum(
                    back * weights[source], axis=0, keepdims=True
                )
        for head in range(2):
            grad_weight = mix_ref[head : head + 1, :] * grad_mixed[0] + mix_ref[2 + head : 3 + head, :] * grad_mixed[1]
            weight = weights[head]
            grad_conv = weight * (grad_weight - jnp.sum(weight * grad_weight, axis=-1, keepdims=True))
            wide = shifted_up(pad_ref, grad_conv).astype(bf16)
            theta_sums[head] += dot_tn(s_ref[seq, head], wide)
            grad_scores = jnp.zeros((rows, rows), f32)
            for lag in range(CQ):
                grad_scores += dot_nt(
                    wide[:, lag * rows : (lag + 1) * rows], toep_ref[head, lag * rows : (lag + 1) * rows, :]
                )
            grad_scores = jnp.where(keep, grad_scores * (1.0 / math.sqrt(DH)), 0.0).astype(bf16)
            query = qkv_ref[seq, :, head * HP : (head + 1) * HP]
            key = qkv_ref[seq, :, (2 + head) * HP : (3 + head) * HP]
            made[head] = dot(grad_scores, key)
            made[2 + head] = dot_tn(grad_scores, query)
        dqkv_ref[seq] = jnp.concatenate([part[:, :DH] for part in made], axis=1).astype(bf16)
        return carry

    lax.fori_loop(0, 4, one, 0)
    gather.onward()
    lax.fori_loop(4, seqs, one, 0)
    scatter.drain()
    tiles_sent = []

    tap_at = query_at - key_at + CK // 2

    def taps(at, carry):
        lag = lax.rem(at, CQ)
        values = theta_sums[lax.div(at, CQ), :, pl.ds(pl.multiple_of(lag * rows, rows), rows)]
        for tap in range(CK):
            theta_ref[pl.ds(at * CK + tap, 1), :] = jnp.sum(
                jnp.where(tap_at == tap, values, 0.0), axis=0, keepdims=True
            )
        return carry

    xn_load.wait()
    all_rows = seqs * rows

    def qkv_grad(row, carry):
        cols = pl.ds(pl.multiple_of(row * BLK, BLK), BLK)
        made = dot_tn(first_ref[:, :, cols].reshape(all_rows, BLK), dqkv_ref[...].reshape(all_rows, 6 * DH))
        gq_ref[row] = made.astype(bf16).reshape(2, CHIPS, 2, BLK // 32, 6 * DH)
        return carry

    lax.fori_loop(0, ROW_TILES, qkv_grad, 0)
    to_core.append(push(gq_ref.at[:, 1 - c], core_q, core_send.at[4], core_recv.at[4], across("c")))

    def input_part(at, carry):
        two = pl.ds(at * 2, 2)
        made = dot_nt(dqkv_ref[two].reshape(2 * rows, 6 * DH), wq_ref[...])
        parts_ref[two] = made.astype(bf16).reshape(2, rows, D)
        return carry

    lax.fori_loop(0, seqs // 2, input_part, 0)
    scatter3 = Scatter(parts_ref, near3, in23, in33, *scatter_args[3:5], *scatter3_sems)
    scatter3.start()
    lax.fori_loop(0, 2 * CQ, taps, 0)
    to_core[4].wait_recv()

    def core_chip_q(chip, carry):
        for row in range(ROW_TILES):
            core_q[row, chip] = (core_q[row, chip].astype(f32) + gq_ref[row, c, chip].astype(f32)).astype(bf16)
        return carry

    lax.fori_loop(0, CHIPS, core_chip_q, 0)
    slot = g * CHIPS + me
    order = (15, 14, 13, 11, 12, 10, 9, 8, 7, 6, 5, 3, 4, 2, 1)
    for mask in order:
        to = flipped(me, [axis for axis in BITS if mask & BITS[axis]])
        tiles_sent.append(
            push(core_q.at[:, to, other_bit("g", mask & 8)], in_q.at[slot], q_send.at[mask], q_recv.at[mask], wide_at(mask))
        )
    in_q[slot] = core_q[:, me, g]
    gather.last()
    to_near[0].wait_recv()

    def near_down(chip, carry):
        half_d[chip, g] = (half_d[chip, g].astype(f32) + near_d[chip].astype(f32)).astype(bf16)
        return carry

    lax.fori_loop(0, CHIPS, near_down, 0)
    base = 4 * ROW_TILES**2

    def spread(ref, cols, tile, which):
        for mask in chips:
            at = which * CHIPS + mask
            tiles_sent.append(
                push(ref.at[to_chip[mask], g, :, cols], tiles_ref.at[tile], gu_send.at[at], gu_recv.at[at], chip_at(mask))
            )
        tiles_ref[tile] = ref[me, g, :, cols]

    for col in range(ROW_TILES):
        spread(half_d, pl.ds(col * BLK, BLK), base + 2 * ROW_TILES * FF_TILES + me * ROW_TILES + col, 6 + col)
    scatter3.onward()
    gather.finish()
    strip_local.wait()
    for copy in strips_sent:
        copy.wait_recv()

    def out_grad(col, carry):
        cols = pl.ds(pl.multiple_of(col * BLK, BLK), BLK)
        made = dot_tn(strips_in[...].reshape(all_rows, 2 * DH), second_ref[:, :, cols].reshape(all_rows, BLK))
        go_ref[:, :, :, :, cols] = made.astype(bf16).reshape(ROW_TILES, 2, 2, BLK // 32, BLK)
        return carry

    lax.fori_loop(0, ROW_TILES, out_grad, 0)
    to_core.append(push(go_ref.at[:, 1 - c], core_o, core_send.at[5], core_recv.at[5], across("c")))

    def near_rows(row):
        to_near[1 + row].wait_recv()

        def near_chip(chip, carry):
            half_in[row, chip, g] = (half_in[row, chip, g].astype(f32) + near_in[row, chip].astype(f32)).astype(bf16)
            return carry

        lax.fori_loop(0, CHIPS, near_chip, 0)
        for which in range(2):
            spread(
                half_in.at[row], pl.ds(which * BLK, BLK), base + (which * ROW_TILES + row) * FF_TILES + me, 2 * row + which
            )

    near_rows(0)
    to_core[5].wait_recv()
    core_o[...] = (core_o[...].astype(f32) + go_ref[:, c].astype(f32)).astype(bf16)
    to_near.append(push(core_o.at[:, 1 - g], in_o, near_send.at[4], near_recv.at[4], across("g")))
    scatter3.last()
    near_rows(1)
    near_rows(2)
    dxn_ref[0:half] = scatter3.finish(0)
    dxn_ref[half:] = scatter3.finish(1)

    def three_tiles(at, values):
        for col in range(ROW_TILES):
            tiles_ref[at + col] = values[:, col * BLK : (col + 1) * BLK].astype(bf16)

    to_near[4].wait_recv()
    for row in range(ROW_TILES):
        three_tiles(3 * ROW_TILES**2 + row * ROW_TILES, in_o[row].astype(f32) + core_o[row, g].astype(f32))
    for copy in tiles_sent:
        copy.wait_recv()
    for row in range(ROW_TILES):
        sums = [in_q[chip, row].astype(f32) + in_q[CHIPS + chip, row].astype(f32) for chip in range(CHIPS)]
        for which in range(3):
            three_tiles(
                which * ROW_TILES**2 + row * ROW_TILES,
                jnp.concatenate([part[:, which * 2 * DH : (which + 1) * 2 * DH] for part in sums], axis=1),
            )
    tiles_ref[tiles_ref.shape[0] - 1] = jnp.zeros(tiles_ref.shape[1:], bf16)

    def grad_left(step, carry):
        grad_copy(lax.rem(me + step, seqs)).wait_send()
        return carry

    lax.fori_loop(1, seqs, grad_left, 0)
    gather.drain()
    scatter3.drain()
    for copy in strips_sent + to_core + to_near + tiles_sent:
        copy.wait_send()


def chip_at(mask):
    return {axis: 1 - lax.axis_index(axis) for axis in BITS if mask & BITS[axis]}


def wide_at(mask):
    at = chip_at(mask & 7)
    if mask & 8:
        at["g"] = 1 - lax.axis_index("g")
    return at


def run_middle(
    lengths, mix, hn, dy, xn, w_in, w_dn, w_qkv, dy_own, hmid, gain_ffn, w_o, qkv, toep, gain, scores, weights, outs, strips
):
    seqs, rows, _ = hn.shape
    dma = pltpu.SemaphoreType.DMA
    part = BLK // 32
    tiles = 4 * ROW_TILES**2 + 3 * ROW_TILES * FF_TILES
    shapes = [
        ((seqs, rows, BLK), bf16), ((rows, D), f32), ((rows, D), f32), ((1, D), f32), ((2 * CQ * CK, rows), f32),
        ((8, rows), f32), ((1, 2 * HP), f32), ((tiles + 1, part, BLK), bf16),
    ]

    def low(*dims):
        return pltpu.VMEM(dims, bf16)

    every, heads = low(CHIPS, rows, D), low(CHIPS, rows, 2 * DH)
    return pl.pallas_call(
        middle_body,
        in_specs=[VMEM] * 2 + [ANYS] * 6 + [VMEM] * 3 + [ANYS] * 2 + [VMEM] * 2 + [ANYS] * 3 + [VMEM],
        out_specs=[VMEM] * len(shapes),
        out_shape=[jax.ShapeDtypeStruct(*shape) for shape in shapes],
        scratch_shapes=[pltpu.VMEM(a.shape, a.dtype) for a in (w_in, w_dn, w_qkv, w_o, qkv, scores, weights, outs)] + [
            dma((8,)),
            pltpu.VMEM((2, rows, CQ * rows), f32), pltpu.VMEM((rows + 8, rows), f32), every, every, low(seqs, rows, 2 * BLK), every, low(rows, D), heads, heads, heads,
            low(ROW_TILES, 2, CHIPS, 2, part, 2 * BLK), low(2, CHIPS, 2, part, D),
            low(ROW_TILES, CHIPS, 2, part, 2 * BLK), low(CHIPS, 2, part, D),
            low(ROW_TILES, CHIPS, part, 2 * BLK), low(CHIPS, part, D),
            low(seqs, rows, 6 * DH), low(ROW_TILES, 2, CHIPS, 2, part, 6 * DH), low(ROW_TILES, 2, 2, part, D),
            low(ROW_TILES, CHIPS, 2, part, 6 * DH), low(ROW_TILES, 2, part, D),
            low(2 * CHIPS, ROW_TILES, part, 6 * DH), low(ROW_TILES, part, D),
            low(3, rows, D), low(rows, D), low(3, rows, D), dma((1,)), dma((9,)),
        ] + [dma((8,))] * 4 + [dma((6,))] * 2 + [dma((5,))] * 2 + [dma((9 * CHIPS,))] * 2 + [dma((16,))] * 2
        + scatter_scratch(rows, D) + [dma((3,))] * 2 + [dma((3, 2))] * 4 + side_sems(),
        name="middle",
        compiler_params=pltpu.CompilerParams(collective_id=3, has_side_effects=True, vmem_limit_bytes=63 * 2**20),
    )(
        lengths, mix, hn, dy, xn, w_in, w_dn, w_qkv, dy_own, hmid, gain_ffn, w_o,
        qkv, toep, gain, scores, weights, outs, strips,
    )


def to_slots_body(
    pick_ref, tiles_ref, vec_ref, inner_hbm, w_dn_hbm, hmid_hbm, out_ref, vecs_ref, layer_ref,
    inner_ref, w_dn_ref, hmid_ref, enter_sems, slots_ref, parts_ref, local_sems, send, recv, vec_send, vec_recv, *scatter_args,
):
    devices = lax.axis_size(ALL)
    own_slots, side = out_ref.shape[:2]
    part = slots_ref.shape[1]
    enter = [
        pltpu.make_async_copy(src, dst, enter_sems.at[at])
        for at, (src, dst) in enumerate(((inner_hbm, inner_ref), (w_dn_hbm, w_dn_ref), (hmid_hbm, hmid_ref)))
    ]
    for copy in enter:
        copy.start()

    def fill(at, carry):
        slots_ref[at] = tiles_ref[pick_ref[at]]
        return carry

    lax.fori_loop(0, slots_ref.shape[0], fill, 0)
    me = device_index()
    place = (lax.axis_index("c") * CHIPS + chip_index()) * 2 + lax.axis_index("g")
    rows = pl.ds(pl.multiple_of(place * part, part), part)
    local = [pltpu.make_async_copy(vec_ref.at[me], vecs_ref.at[me], local_sems.at[0])]
    for slot in range(own_slots):
        local.append(
            pltpu.make_async_copy(
                slots_ref.at[me * own_slots + slot], out_ref.at[slot, rows], local_sems.at[1 + slot]
            )
        )
    for copy in local:
        copy.start()
    greet_all()

    def push_all(step, carry):
        to = lax.rem(me + step, devices)
        pltpu.make_async_remote_copy(
            src_ref=vec_ref.at[to], dst_ref=vecs_ref.at[me], send_sem=vec_send, recv_sem=vec_recv, device_id=device_at(to)
        ).start()
        pltpu.make_async_remote_copy(
            src_ref=slots_ref.at[pl.ds(to * own_slots, own_slots)], dst_ref=out_ref.at[:, rows],
            send_sem=send, recv_sem=recv, device_id=device_at(to),
        ).start()
        return carry

    lax.fori_loop(1, devices, push_all, 0)

    seqs, length = inner_ref.shape[:2]
    for copy in enter:
        copy.wait()

    def outputs(at, carry):
        two = pl.ds(at * 2, 2)
        made = dot(inner_ref[two].reshape(2 * length, BLK), w_dn_ref[...])
        parts_ref[two] = made.astype(bf16).reshape(2, length, D)
        return carry

    lax.fori_loop(0, seqs // 2, outputs, 0)
    scatter = SideScatter(parts_ref, *scatter_args)
    scatter.start()
    scatter.onward()
    scatter.last()
    layer_ref[...] = (hmid_ref[...] + scatter.finish()).astype(bf16)
    scatter.drain()
    others = vecs_ref.at[pl.ds(0, devices - 1)]
    pltpu.make_async_copy(others, others, vec_recv).wait()
    pltpu.make_async_copy(others, others, vec_send).wait()
    others = out_ref.at[:, pl.ds(0, side - part)]
    pltpu.make_async_copy(others, others, recv).wait()
    pltpu.make_async_copy(others, others, send).wait()
    for copy in local:
        copy.wait()


def to_slots(pick, tiles, vecs, inner, w_dn, hmid, own_slots):
    rows = hmid.shape[0]
    dma = pltpu.SemaphoreType.DMA
    return pl.pallas_call(
        to_slots_body,
        in_specs=[SMEM, VMEM] + [ANYS] * 4,
        out_specs=[ANYS] * 2 + [VMEM],
        out_shape=[
            jax.ShapeDtypeStruct((own_slots, BLK, BLK), bf16), jax.ShapeDtypeStruct(vecs.shape, vecs.dtype),
            jax.ShapeDtypeStruct(hmid.shape, bf16),
        ],
        scratch_shapes=[pltpu.VMEM(a.shape, a.dtype) for a in (inner, w_dn, hmid)] + [
            dma((3,)), pltpu.VMEM((pick.shape[0],) + tiles.shape[1:], bf16), pltpu.VMEM((CHIPS, rows, D), bf16), dma((1 + own_slots,)),
        ] + [dma] * 4 + side_scatter_scratch(rows, D),
        name="to_slots",
        compiler_params=pltpu.CompilerParams(collective_id=6, has_side_effects=True, vmem_limit_bytes=60 * 2**20),
    )(pick, tiles, vecs, inner, w_dn, hmid)


def update_body(grad_ref, left_ref, right_ref, master_ref, first_ref, second_ref, first_out, second_out, master_out, copy_out):
    left, right = left_ref[0].astype(bf16), right_ref[0].astype(bf16)
    rotated = dot(dot_tn(left, grad_ref[0]).astype(bf16), right)
    first = beta_first * first_ref[0] + (1.0 - beta_first) * rotated
    second = beta_second * second_ref[0] + (1.0 - beta_second) * rotated * rotated
    first_out[0] = first
    second_out[0] = second
    direction = (first / (jnp.sqrt(second) + eps_adam)).astype(bf16)
    turned = dot_nt(dot(left, direction).astype(bf16), right)
    master = master_ref[0]
    master = master - rate_block * (turned + decay_block * master)
    master_out[0] = master
    copy_out[0] = master.astype(bf16)


def update(grad, left, right, master, first, second):
    spec = pl.BlockSpec((1, BLK, BLK), lambda slot: (slot, 0, 0))
    return pl.pallas_call(
        update_body,
        grid=(grad.shape[0],),
        in_specs=[spec] * 6,
        out_specs=[spec] * 4,
        out_shape=[jax.ShapeDtypeStruct(grad.shape, kind) for kind in (f32, f32, f32, bf16)],
        name="update",
        compiler_params=pltpu.CompilerParams(vmem_limit_bytes=60 * 2**20),
        cost_estimate=pl.CostEstimate(flops=43 * 10**8, bytes_accessed=36 * 2**20, transcendentals=10**6),
    )(grad, left, right, master, first, second)


def body_fast(
    layer_input, lengths, cotangent, w_query, w_key, w_value, w_out, w_gate, w_up, w_down, vec_copy, owners,
    basis_left, basis_right, block_master, block_first, block_second, vec_master, vec_first, vec_second,
):
    chip = chip_index()
    seq_len = layer_input.shape[0]
    own_vec = vec_copy.shape[0]
    devices, fs_size, reps = lax.axis_size(ALL), lax.axis_size(FS), lax.axis_size("y")

    fs_index = ((lax.axis_index("g") * 2 + lax.axis_index("a")) * 2 + lax.axis_index("b")) * 2 + lax.axis_index("c")
    first_rows = vector_rows(own_vec, fs_size)
    flat = lax.dynamic_update_slice_in_dim(jnp.zeros((fs_size * own_vec,), f32), vec_copy.astype(f32), fs_index * own_vec, 0)
    first = lax.dynamic_index_in_dim(jnp.array(first_rows, jnp.int32), fs_index, 0, keepdims=False)
    vec = lax.dynamic_slice_in_dim(rows_of_vector(flat), first, SHARD_ROWS, 0)

    (
        dy, group_lengths, mix, gains, toep, gain_pair, heads, hmid, xn, qkv, scores, weights, outs, w_qkv, w_out_all,
        hn_rows, w_in, w_dn, dy_rows,
    ) = run_front(
        first_rows, lengths, vec, layer_input, w_query, w_key, w_value, cotangent, w_out, w_gate, w_up, w_down
    )
    gain_attn = gains[0]
    w_qkv = w_qkv.reshape(D, 6 * DH)
    w_in, w_dn = w_in.reshape(D, 2 * BLK), w_dn.reshape(BLK, D)
    strip = BLK // (2 * CHIPS)
    part = strip // 2
    heads = jnp.transpose(heads, (1, 0, 2)).reshape(seq_len, 2 * ROW_TILES, CHIPS, strip)
    strips = jnp.transpose(heads, (2, 0, 1, 3)).reshape(CHIPS, seq_len, 2 * ROW_TILES * strip)
    input_float = layer_input.astype(f32)
    input_scale = rms(input_float)

    own_slots = basis_left.shape[0]
    matches = jnp.arange(own_slots * devices)[:, None] == owners[None, :]
    tile_count = owners.shape[0]
    pick = jnp.min(jnp.where(matches, jnp.arange(tile_count, dtype=jnp.int32)[None, :], tile_count), axis=1)
    inner, dhmid, dxn, grad_gain_ffn, theta_sums, mixer_sums, gain_sums, tiles = run_middle(
        group_lengths, mix, hn_rows, dy_rows, xn, w_in, w_dn, w_qkv, dy, hmid, gains,
        w_out_all.reshape(CHIPS, 2 * DH, D), qkv, toep, gain_pair, scores, weights, outs, strips,
    )
    dinput, grad_gain_attn = norm_backward(input_float, input_scale, gain_attn, dxn)
    input_grad = dinput + dhmid

    grad_theta = jnp.sum(theta_sums, axis=1)
    grad_mixer = jnp.sum(mixer_sums[:4], axis=1)
    vector_grad = jnp.concatenate(
        [
            grad_gain_attn,
            lax.dynamic_update_slice_in_dim(
                jnp.zeros((D,), f32), gain_sums.reshape(2, HP)[:, :DH].reshape(-1), chip * 2 * DH, 0
            ),
            grad_gain_ffn.reshape(-1),
            lax.dynamic_update_slice_in_dim(
                jnp.zeros((H * CQ * CK,), f32), grad_theta.reshape(-1), chip * 2 * CQ * CK, 0
            ),
            lax.dynamic_update_slice_in_dim(jnp.zeros((2 * H,), f32), grad_mixer, chip * 4, 0),
        ]
    )
    pieces = jnp.pad(vector_grad.reshape(fs_size, 1, own_vec), ((0, 0), (0, 0), (0, 1024 - own_vec)))
    pieces = jnp.broadcast_to(pieces, (fs_size, reps, 1024)).reshape(devices, 8, 128)

    own_grad, pieces, layer_output = to_slots(
        pick, tiles, pieces, inner, w_dn, hmid, own_slots
    )
    vector_total = jnp.sum(pieces, axis=0).reshape(1024)[:own_vec]
    first_new, second_new, master_new, copy_new = update(
        own_grad, basis_left, basis_right, block_master, block_first, block_second
    )
    vec_first_new = beta_first * vec_first + (1.0 - beta_first) * vector_total
    vec_second_new = beta_second * vec_second + (1.0 - beta_second) * vector_total * vector_total
    vec_master_new = vec_master - rate_vector * vec_first_new / (jnp.sqrt(vec_second_new) + eps_adam)
    return (
        layer_output, input_grad, first_new, second_new, master_new, copy_new,
        vec_first_new, vec_second_new, vec_master_new, vec_master_new.astype(bf16),
    )


def solution(mesh):
    fsdp, rep = mesh.shape["fsdp"], mesh.shape["rep"]
    fine = Mesh(mesh.devices.reshape(fsdp // 8, 2, 2, 2, rep), ALL)
    rows, both = P(ALL, None), P(ALL, None, None)
    weight, vec = P(FS, None), P(FS)
    return jax.shard_map(
        body_fast if (fsdp, rep) == (16, 2) else body_any,
        mesh=fine,
        in_specs=(rows, P(ALL), rows) + (weight,) * 7 + (vec, P()) + (both,) * 5 + (vec,) * 3,
        out_specs=(rows, rows) + (both,) * 4 + (vec,) * 4,
        check_vma=False,
    )
```

```python
import functools
import math

import jax
import jax.numpy as jnp
import numpy as np
from jax import lax
from jax.experimental import pallas as pl
from jax.experimental.pallas import tpu as pltpu
from jax.sharding import Mesh
from jax.sharding import PartitionSpec as P

H = 16
DH = 96
HP = 128
D = H * DH
FF = 4096
CQ = 6
CK = 11
BLK = 512
CHIPS = 8
ROW_TILES = D // BLK
FF_TILES = FF // BLK

eps_norm = 1e-05
eps_adam = 1e-08
rate_block = 0.02
rate_vector = 0.3
decay_block = 0.1
beta_first = 0.5
beta_second = 0.5

FS = ("g", "a", "b", "c")
CHIP = ("y", "a", "b")
ALL = ("g", "a", "b", "c", "y")
bf16 = jnp.bfloat16
f32 = jnp.float32


def dot(left, right):
    return jnp.dot(left, right, preferred_element_type=f32)


def dot_nt(left, right):
    return lax.dot_general(left, right, (((1,), (1,)), ((), ())), preferred_element_type=f32)


def dot_tn(left, right):
    return lax.dot_general(left, right, (((0,), (0,)), ((), ())), preferred_element_type=f32)


def rms(values):
    return lax.rsqrt(jnp.mean(values * values, axis=-1, keepdims=True) + eps_norm)


def norm_backward(values, scale, gain, grad):
    unit = values * scale
    inner = grad * gain
    grad_values = scale * (inner - unit * jnp.mean(inner * unit, axis=-1, keepdims=True))
    return grad_values, jnp.sum(grad * unit, axis=0)


def shifted_down(pad_ref, values):
    rows = values.shape[0]
    pad_ref[8 : 8 + rows, :] = values
    return jnp.concatenate(
        [values] + [pad_ref[8 - lag : 8 - lag + rows, :] for lag in range(1, CQ)], axis=1
    )


def shifted_up(pad_ref, values):
    rows = values.shape[0]
    pad_ref[0:rows, :] = values
    return jnp.concatenate(
        [values] + [pad_ref[lag : lag + rows, :] for lag in range(1, CQ)], axis=1
    )


def attention_forward(len_ref, mix_ref, qkv_ref, toep_ref, gain_ref, heads_ref, s_ref, p_ref, o_ref, pad_ref):
    rows = qkv_ref.shape[1]
    length = len_ref[pl.program_id(0)]
    query_at = lax.broadcasted_iota(jnp.int32, (rows, rows), 0)
    key_at = lax.broadcasted_iota(jnp.int32, (rows, rows), 1)
    keep = (key_at <= query_at) & (key_at < length)
    pad_ref[0:8, :] = jnp.zeros((8, rows), f32)
    weights = []
    for head in range(2):
        query = qkv_ref[0, :, head * HP : (head + 1) * HP]
        key = qkv_ref[0, :, (2 + head) * HP : (3 + head) * HP]
        scores = jnp.where(keep, dot_nt(query, key) * (1.0 / math.sqrt(DH)), 0.0)
        s_ref[0, head] = scores.astype(bf16)
        wide = shifted_down(pad_ref, scores)
        high = wide.astype(bf16)
        low = (wide - high.astype(f32)).astype(bf16)
        conv = dot(high, toep_ref[head]) + dot(low, toep_ref[head])
        logits = jnp.where(keep, conv, -1e30)
        weight = jnp.exp(logits - jnp.max(logits, axis=-1, keepdims=True))
        weight = weight / jnp.sum(weight, axis=-1, keepdims=True)
        p_ref[0, head] = weight
        weights.append(weight)
    for head in range(2):
        mixed = mix_ref[2 * head] * weights[0] + mix_ref[2 * head + 1] * weights[1]
        value = qkv_ref[0, :, (4 + head) * HP : (5 + head) * HP]
        out = dot(mixed.astype(bf16), value)
        o_ref[0, :, head * HP : (head + 1) * HP] = out
        scale = lax.rsqrt(jnp.sum(out * out, axis=-1, keepdims=True) * (1.0 / DH) + eps_norm)
        heads_ref[0, :, head * HP : (head + 1) * HP] = (
            out * scale * gain_ref[:, head * HP : (head + 1) * HP]
        ).astype(bf16)


def attention_backward(
    len_ref, mix_ref, qkv_ref, toep_ref, gain_ref, s_ref, p_ref, o_ref, grad_ref,
    dqkv_ref, theta_ref, mixer_ref, gain_grad_ref, pad_ref,
):
    rows = qkv_ref.shape[1]
    length = len_ref[pl.program_id(0)]
    query_at = lax.broadcasted_iota(jnp.int32, (rows, rows), 0)
    key_at = lax.broadcasted_iota(jnp.int32, (rows, rows), 1)
    keep = (key_at <= query_at) & (key_at < length)
    pad_ref[rows : rows + 8, :] = jnp.zeros((8, rows), f32)

    @pl.when(pl.program_id(0) == 0)
    def _():
        theta_ref[...] = jnp.zeros_like(theta_ref)
        mixer_ref[...] = jnp.zeros_like(mixer_ref)
        gain_grad_ref[...] = jnp.zeros_like(gain_grad_ref)

    weights = [p_ref[0, 0], p_ref[0, 1]]
    grad_mixed = []
    for head in range(2):
        cols = slice(head * HP, (head + 1) * HP)
        out = o_ref[0, :, cols]
        grad = grad_ref[0, :, cols].astype(f32)
        scale = lax.rsqrt(jnp.sum(out * out, axis=-1, keepdims=True) * (1.0 / DH) + eps_norm)
        unit = out * scale
        gain_grad_ref[:, cols] += jnp.sum(grad * unit, axis=0, keepdims=True)
        inner = grad * gain_ref[:, cols]
        grad_out = scale * (inner - unit * (jnp.sum(inner * unit, axis=-1, keepdims=True) * (1.0 / DH)))
        grad_out = grad_out.astype(bf16)
        value = qkv_ref[0, :, (4 + head) * HP : (5 + head) * HP]
        mixed = (mix_ref[2 * head] * weights[0] + mix_ref[2 * head + 1] * weights[1]).astype(bf16)
        dqkv_ref[0, :, (4 + head) * HP : (5 + head) * HP] = dot_tn(mixed, grad_out).astype(bf16)
        back = dot_nt(grad_out, value)
        grad_mixed.append(back)
        for source in range(2):
            mixer_ref[2 * head + source : 2 * head + source + 1, :] += jnp.sum(
                back * weights[source], axis=0, keepdims=True
            )
    for head in range(2):
        grad_weight = mix_ref[head] * grad_mixed[0] + mix_ref[2 + head] * grad_mixed[1]
        weight = weights[head]
        grad_conv = weight * (grad_weight - jnp.sum(weight * grad_weight, axis=-1, keepdims=True))
        wide = shifted_up(pad_ref, grad_conv).astype(bf16)
        theta_ref[head] += dot_tn(s_ref[0, head], wide)
        grad_scores = jnp.zeros((rows, rows), f32)
        for lag in range(CQ):
            grad_scores += dot_nt(
                wide[:, lag * rows : (lag + 1) * rows], toep_ref[head, lag * rows : (lag + 1) * rows, :]
            )
        grad_scores = jnp.where(keep, grad_scores * (1.0 / math.sqrt(DH)), 0.0).astype(bf16)
        query = qkv_ref[0, :, head * HP : (head + 1) * HP]
        key = qkv_ref[0, :, (2 + head) * HP : (3 + head) * HP]
        dqkv_ref[0, :, head * HP : (head + 1) * HP] = dot(grad_scores, key).astype(bf16)
        dqkv_ref[0, :, (2 + head) * HP : (3 + head) * HP] = dot_tn(grad_scores, query).astype(bf16)


SMEM = pl.BlockSpec(memory_space=pltpu.SMEM)


def seq_spec(*dims):
    return pl.BlockSpec((1,) + dims, lambda s: (s,) + (0,) * len(dims))


def whole_spec(*dims):
    return pl.BlockSpec(dims, lambda s: (0,) * len(dims))


def run_forward(lengths, mix, qkv, toep, gain):
    seqs, rows, _ = qkv.shape
    return pl.pallas_call(
        attention_forward,
        grid=(seqs,),
        in_specs=[SMEM, SMEM, seq_spec(rows, 6 * HP), whole_spec(2, CQ * rows, rows), whole_spec(1, 2 * HP)],
        out_specs=[seq_spec(rows, 2 * HP), seq_spec(2, rows, rows), seq_spec(2, rows, rows), seq_spec(rows, 2 * HP)],
        out_shape=[
            jax.ShapeDtypeStruct((seqs, rows, 2 * HP), bf16),
            jax.ShapeDtypeStruct((seqs, 2, rows, rows), bf16),
            jax.ShapeDtypeStruct((seqs, 2, rows, rows), f32),
            jax.ShapeDtypeStruct((seqs, rows, 2 * HP), f32),
        ],
        scratch_shapes=[pltpu.VMEM((rows + 8, rows), f32)],
        name="attention_forward",
        compiler_params=pltpu.CompilerParams(vmem_limit_bytes=24 * 2**20),
        cost_estimate=pl.CostEstimate(flops=2 * 10**9, bytes_accessed=8 * 2**20, transcendentals=10**5),
    )(lengths, mix, qkv, toep, gain)


def run_backward(lengths, mix, qkv, toep, gain, scores, weights, outs, grads):
    seqs, rows, _ = qkv.shape
    return pl.pallas_call(
        attention_backward,
        grid=(seqs,),
        in_specs=[
            SMEM, SMEM, seq_spec(rows, 6 * HP), whole_spec(2, CQ * rows, rows), whole_spec(1, 2 * HP),
            seq_spec(2, rows, rows), seq_spec(2, rows, rows), seq_spec(rows, 2 * HP), seq_spec(rows, 2 * HP),
        ],
        out_specs=[seq_spec(rows, 6 * HP), whole_spec(2, rows, CQ * rows), whole_spec(8, rows), whole_spec(1, 2 * HP)],
        out_shape=[
            jax.ShapeDtypeStruct((seqs, rows, 6 * HP), bf16),
            jax.ShapeDtypeStruct((2, rows, CQ * rows), f32),
            jax.ShapeDtypeStruct((8, rows), f32),
            jax.ShapeDtypeStruct((1, 2 * HP), f32),
        ],
        scratch_shapes=[pltpu.VMEM((rows + 8, rows), f32)],
        name="attention_backward",
        compiler_params=pltpu.CompilerParams(vmem_limit_bytes=24 * 2**20),
        cost_estimate=pl.CostEstimate(flops=4 * 10**9, bytes_accessed=12 * 2**20, transcendentals=10**5),
    )(lengths, mix, qkv, toep, gain, scores, weights, outs, grads)


BITS = {"y": 4, "a": 2, "b": 1}
HOPS = (("y", "b", "a"), ("a", "y", "b"), ("b", "a", "y"))
THIRDS = ((0, 48), (48, 48), (96, 32))
ANYS = pl.BlockSpec(memory_space=pl.ANY)


def chip_index():
    return (lax.axis_index("y") * 2 + lax.axis_index("a")) * 2 + lax.axis_index("b")


def flipped(chip, axes):
    for axis in axes:
        chip = chip + BITS[axis] * (1 - 2 * lax.axis_index(axis))
    return chip


def across(axis):
    return {axis: 1 - lax.axis_index(axis)}


def device_index():
    index = lax.axis_index("g")
    for axis in ("a", "b", "c", "y"):
        index = index * lax.axis_size(axis) + lax.axis_index(axis)
    return index


def device_at(index):
    at = {}
    for axis in ("y", "c", "b", "a", "g"):
        at[axis] = lax.rem(index, lax.axis_size(axis))
        index = lax.div(index, lax.axis_size(axis))
    return at


def greet_all():
    devices = lax.axis_size(ALL)
    me = device_index()
    barrier = pltpu.get_barrier_semaphore()

    def greet(step, carry):
        pl.semaphore_signal(barrier, inc=1, device_id=device_at(lax.rem(me + step, devices)))
        return carry

    lax.fori_loop(1, devices, greet, 0)
    pl.semaphore_wait(barrier, devices - 1)


def greet_neighbours():
    barrier = pltpu.get_barrier_semaphore()
    for axis in BITS:
        pl.semaphore_signal(barrier, inc=1, device_id=across(axis))
    pl.semaphore_wait(barrier, 3)


def remote(src, dst, send, recv, axis):
    return pltpu.make_async_remote_copy(src_ref=src, dst_ref=dst, send_sem=send, recv_sem=recv, device_id=across(axis))


def gather_body(x_ref, out_ref, *sems):
    greet_neighbours()
    gather_hops(x_ref, out_ref, *sems)


def gather_first_body(x_ref, vec_ref, out_ref, vecs_ref, vec_send, vec_recv, vec_local, *sems):
    devices = lax.axis_size(ALL)
    me = device_index()
    local = pltpu.make_async_copy(vec_ref, vecs_ref.at[me], vec_local)
    local.start()
    greet_all()

    def push(step, carry):
        pltpu.make_async_remote_copy(
            src_ref=vec_ref, dst_ref=vecs_ref.at[me], send_sem=vec_send, recv_sem=vec_recv,
            device_id=device_at(lax.rem(me + step, devices)),
        ).start()
        return carry

    lax.fori_loop(1, devices, push, 0)
    gather_hops(x_ref, out_ref, *sems)
    others = vecs_ref.at[pl.ds(0, devices - 1)]
    pltpu.make_async_copy(others, others, vec_recv).wait()
    pltpu.make_async_copy(others, others, vec_send).wait()
    local.wait()


def gather_hops(x_ref, out_ref, local_sem, send1, recv1, send2, recv2, send3, recv3):
    me = chip_index()
    rows = x_ref.shape[0]
    half = rows // 2
    local = pltpu.make_async_copy(x_ref, out_ref.at[me], local_sem)
    local.start()
    first = []
    for part in range(2):
        here = pl.ds(part * half, half)
        for at, (axis, _, _) in enumerate(HOPS):
            copy = remote(x_ref.at[here], out_ref.at[me, here], send1.at[at, part], recv1.at[at, part], axis)
            copy.start()
            first.append(copy)
    second = []
    for part in range(2):
        here = pl.ds(part * half, half)
        for at, (axis, onward, _) in enumerate(HOPS):
            first[part * 3 + at].wait_recv()
            block = out_ref.at[flipped(me, (axis,)), here]
            copy = remote(block, block, send2.at[at, part], recv2.at[at, part], onward)
            copy.start()
            second.append(copy)
    third = []
    for at, (axis, onward, last) in enumerate(HOPS):
        begin, count = THIRDS[at]
        block = flipped(me, (axis, onward))
        for part in range(2):
            if part * half < begin + count and begin < (part + 1) * half:
                second[part * 3 + at].wait_recv()
        piece = out_ref.at[block, pl.ds(begin, count)]
        copy = remote(piece, piece, send3.at[at], recv3.at[at], last)
        copy.start()
        third.append(copy)
    for at in range(3):
        begin, count = THIRDS[at]
        for part in range(2):
            if not (part * half < begin + count and begin < (part + 1) * half):
                second[part * 3 + at].wait_recv()
    for copy in third:
        copy.wait_recv()
    for copy in first + second + third:
        copy.wait_send()
    local.wait()


def hop_sems():
    dma = pltpu.SemaphoreType.DMA
    return [dma] + [dma((3, 2))] * 4 + [dma((3,))] * 2


def gather_first(rows, vec, collective_id):
    count, width = rows.shape
    return pl.pallas_call(
        gather_first_body,
        in_specs=[ANYS, ANYS],
        out_specs=[ANYS, ANYS],
        out_shape=[
            jax.ShapeDtypeStruct((CHIPS, count, width), rows.dtype),
            jax.ShapeDtypeStruct((lax.axis_size(ALL),) + vec.shape, vec.dtype),
        ],
        scratch_shapes=[pltpu.SemaphoreType.DMA] * 3 + hop_sems(),
        name="gather_first",
        compiler_params=pltpu.CompilerParams(collective_id=collective_id, has_side_effects=True),
    )(rows, vec)


def gather_chips(rows, collective_id):
    count, width = rows.shape
    return pl.pallas_call(
        gather_body,
        in_specs=[ANYS],
        out_specs=ANYS,
        out_shape=jax.ShapeDtypeStruct((CHIPS, count, width), rows.dtype),
        scratch_shapes=hop_sems(),
        name="gather_chips",
        compiler_params=pltpu.CompilerParams(collective_id=collective_id, has_side_effects=True),
    )(rows)


def scatter_body(
    parts_ref, out_ref, near_ref, in2_ref, in3_ref, acc2_ref, acc3_ref, send1, recv1, send2, recv2, send3, recv3
):
    me = chip_index()
    greet_neighbours()
    opposite = flipped(me, ("y", "a", "b"))
    first = []
    for at, (axis, onward, last) in enumerate(HOPS):
        begin, count = THIRDS[at]
        copy = remote(parts_ref.at[opposite, pl.ds(begin, count)], in2_ref.at[pl.ds(begin, count)], send1.at[at], recv1.at[at], last)
        copy.start()
        first.append(copy)
    second = []
    rows = parts_ref.shape[1]
    half = rows // 2
    for part in range(2):
        here = pl.ds(part * half, half)
        for at, (axis, onward, last) in enumerate(HOPS):
            dest = flipped(me, (axis, onward))
            begin, count = THIRDS[at]
            if part == 0:
                first[at].wait_recv()
                acc2_ref[at] = parts_ref[dest]
                piece = pl.ds(begin, count)
                acc2_ref[at, piece] = (parts_ref[dest, piece].astype(f32) + in2_ref[piece].astype(f32)).astype(bf16)
            copy = remote(acc2_ref.at[at, here], in3_ref.at[at, here], send2.at[at, part], recv2.at[at, part], onward)
            copy.start()
            second.append(copy)
    third = []
    for part in range(2):
        here = pl.ds(part * half, half)
        for at, (axis, onward, last) in enumerate(HOPS):
            dest = flipped(me, (axis,))
            second[part * 3 + at].wait_recv()
            acc3_ref[at, here] = (parts_ref[dest, here].astype(f32) + in3_ref[at, here].astype(f32)).astype(bf16)
            copy = remote(acc3_ref.at[at, here], near_ref.at[at, here], send3.at[at, part], recv3.at[at, part], axis)
            copy.start()
            third.append(copy)
    for part in range(2):
        here = pl.ds(part * half, half)
        for at in range(3):
            third[part * 3 + at].wait_recv()
        out_ref[here] = (
            (parts_ref[me, here].astype(f32) + near_ref[0, here].astype(f32))
            + (near_ref[1, here].astype(f32) + near_ref[2, here].astype(f32))
        )
    for copy in first + second + third:
        copy.wait_send()


def scatter_chips(parts, collective_id):
    _, rows, width = parts.shape
    vmem = pl.BlockSpec(memory_space=pltpu.VMEM)
    dma = pltpu.SemaphoreType.DMA
    return pl.pallas_call(
        scatter_body,
        in_specs=[vmem],
        out_specs=vmem,
        out_shape=jax.ShapeDtypeStruct((rows, width), f32),
        scratch_shapes=[pltpu.VMEM((3, rows, width), bf16), pltpu.VMEM((rows, width), bf16)] + [pltpu.VMEM((3, rows, width), bf16)] * 3
        + [dma((3,))] * 2 + [dma((3, 2))] * 4,
        name="scatter_chips",
        compiler_params=pltpu.CompilerParams(collective_id=collective_id, has_side_effects=True, vmem_limit_bytes=32*2**20),
    )(parts)


def gather_slow(rows):
    return lax.all_to_all(
        jnp.broadcast_to(rows[None], (CHIPS,) + rows.shape), CHIP, split_axis=0, concat_axis=0, tiled=True
    )


def exchange_chips(parts):
    return lax.all_to_all(parts, CHIP, split_axis=0, concat_axis=0, tiled=True)


def scatter_slow(parts):
    return jnp.sum(exchange_chips(parts.astype(bf16)).astype(f32), axis=0)


def swap(values, axis):
    return lax.ppermute(values, axis, [(0, 1), (1, 0)])


def both_cores(own, axis):
    other = swap(own, "c")
    first = lax.axis_index("c") == 0
    return jnp.stack([jnp.where(first, own, other), jnp.where(first, other, own)], axis=axis)


def half_for_core(values, axis):
    core = lax.axis_index("c")
    own = lax.dynamic_index_in_dim(values, core, axis, keepdims=False)
    sent = lax.dynamic_index_in_dim(values, 1 - core, axis, keepdims=False)
    return own + swap(sent.astype(bf16), "c").astype(f32)


def sum_groups(tiles):
    groups = lax.axis_size("g")
    if groups != 2:
        return lax.psum_scatter(tiles.astype(f32), "g", scatter_dimension=1, tiled=True).astype(bf16)
    part = tiles.shape[1] // 2
    group = lax.axis_index("g")
    own = lax.dynamic_slice_in_dim(tiles, group * part, part, 1)
    sent = lax.dynamic_slice_in_dim(tiles, (1 - group) * part, part, 1)
    return (own.astype(f32) + swap(sent, "g").astype(f32)).astype(bf16)


def spread_columns(weight, width):
    rows = weight.shape[0]
    blocks = weight.reshape(rows, 2, CHIPS // 2, width)
    mine = lax.dynamic_index_in_dim(blocks, lax.axis_index("y"), 1, keepdims=False)
    return jnp.transpose(mine, (1, 0, 2))


def to_columns(blocks):
    groups = lax.axis_size("g")
    sent = jnp.broadcast_to(blocks[None], (groups,) + blocks.shape).reshape((-1,) + blocks.shape[1:])
    got = lax.all_to_all(sent, ("g", "a", "b"), split_axis=0, concat_axis=0, tiled=True)
    return both_cores(got, 1).reshape(-1, blocks.shape[-1])


def down_rows(w_down, chip):
    if lax.axis_size("g") == 2:
        other = swap(w_down, "g")
        mine = jnp.where(lax.axis_index("g") == lax.axis_index("y"), w_down, other)
        return both_cores(mine, 0).reshape(BLK, D)
    return lax.dynamic_slice_in_dim(lax.all_gather(w_down, FS, axis=0, tiled=True), chip * BLK, BLK, 0)


def band():
    tap = np.arange(CK)[:, None, None]
    source = np.arange(128)[None, :, None]
    target = np.arange(128)[None, None, :]
    return source - target + CK // 2 == tap


def body_any(
    layer_input, lengths, cotangent, w_query, w_key, w_value, w_out, w_gate, w_up, w_down, vec_copy, owners,
    basis_left, basis_right, block_master, block_first, block_second, vec_master, vec_first, vec_second,
):
    chip = (lax.axis_index("y") * 2 + lax.axis_index("a")) * 2 + lax.axis_index("b")
    fs_index = ((lax.axis_index("g") * 2 + lax.axis_index("a")) * 2 + lax.axis_index("b")) * 2 + lax.axis_index("c")
    seq_len = layer_input.shape[0]
    length = lengths[0]
    reps = lax.axis_size("y")
    fs_size = lax.axis_size(FS)

    own_vec = vec_copy.shape[0]
    small = jnp.concatenate(
        [vec_copy.astype(f32), jnp.zeros((1023 - own_vec,), f32), length.astype(f32).reshape(1)]
    ).reshape(8, 128)
    x_all, small_all = gather_first(layer_input, small, 1)
    small_all = small_all.reshape(fs_size, reps, 1024)
    vector = small_all[:, 0, :own_vec].reshape(-1)
    group_lengths = small_all[:, :, 1023].reshape(-1, 2, 2, 2, reps)
    group_lengths = lax.dynamic_index_in_dim(group_lengths, lax.axis_index("g"), 0, keepdims=False)
    group_lengths = lax.dynamic_index_in_dim(group_lengths, lax.axis_index("c"), 2, keepdims=False)
    group_lengths = jnp.transpose(group_lengths, (2, 0, 1)).reshape(CHIPS).astype(jnp.int32)
    gain_attn, gain_head, gain_ffn = vector[:D], vector[D : 2 * D], vector[2 * D : 3 * D]
    conv_end = 3 * D + H * CQ * CK
    theta = lax.dynamic_slice_in_dim(vector[3 * D : conv_end].reshape(H, CQ, CK), chip * 2, 2, 0)
    mixer = lax.dynamic_slice_in_dim(vector[conv_end : conv_end + 2 * H].reshape(H, 2), chip * 2, 2, 0)
    mix = mixer.reshape(4)
    gain_pair = jnp.pad(
        lax.dynamic_slice_in_dim(gain_head.reshape(H, DH), chip * 2, 2, 0), ((0, 0), (0, HP - DH))
    ).reshape(1, 2 * HP)
    toep = jnp.zeros((2, CQ, seq_len, seq_len), f32)
    offset = (
        jnp.arange(seq_len, dtype=jnp.int32)[:, None] - jnp.arange(seq_len, dtype=jnp.int32)[None, :] + CK // 2
    )
    for tap in range(CK):
        toep = jnp.where(offset[None, None] == tap, theta[:, :, tap][:, :, None, None], toep)
    toep = toep.astype(bf16).reshape(2, CQ * seq_len, seq_len)

    qkv_rows = to_columns(
        jnp.concatenate([spread_columns(w, 2 * DH) for w in (w_query, w_key, w_value)], axis=2)
    )
    w_qkv = jnp.pad(qkv_rows.reshape(D, 6, DH), ((0, 0), (0, 0), (0, HP - DH))).reshape(D, 6 * HP)
    w_in = to_columns(jnp.concatenate([spread_columns(w, BLK) for w in (w_gate, w_up)], axis=2))
    w_dn = down_rows(w_down, chip)
    w_o = lax.all_gather(w_out, FS, axis=0, tiled=True)

    input_float = layer_input.astype(f32)
    input_scale = rms(input_float)
    x_rows = x_all.reshape(CHIPS * seq_len, D).astype(f32)
    xn_rows = (x_rows * rms(x_rows) * gain_attn).astype(bf16)
    qkv = dot(xn_rows, w_qkv).astype(bf16).reshape(CHIPS, seq_len, 6 * HP)
    heads_pad, scores, weights, outs = run_forward(group_lengths, mix, qkv, toep, gain_pair)
    heads_sent = heads_pad.reshape(CHIPS, seq_len, 2, HP)[..., :DH].reshape(CHIPS, seq_len, 2 * DH)
    heads = jnp.transpose(exchange_chips(heads_sent), (1, 0, 2)).reshape(seq_len, D)
    hmid = input_float + dot(heads, w_o)
    hmid_scale = rms(hmid)
    hn_rows = gather_chips((hmid * hmid_scale * gain_ffn).astype(bf16), 2).reshape(CHIPS * seq_len, D)
    both = dot(hn_rows, w_in)
    gate, up = both[:, :BLK], both[:, BLK:]
    sig = jax.nn.sigmoid(gate)
    silu = gate * sig
    inner = (silu * up).astype(bf16)
    ffn = scatter_slow(dot(inner, w_dn).reshape(CHIPS, seq_len, D))
    layer_output = (hmid + ffn).astype(bf16)

    valid = (jnp.arange(seq_len) < length).astype(f32)
    dy = cotangent.astype(f32) * valid[:, None]
    dy_rows = gather_slow(dy.astype(bf16)).reshape(CHIPS * seq_len, D)
    dinner = dot_nt(dy_rows, w_dn)
    dgate = (dinner * up * (sig * (1.0 + gate * (1.0 - sig)))).astype(bf16)
    dup = (dinner * silu).astype(bf16)
    dboth = jnp.concatenate([dgate, dup], axis=1)
    dhn = scatter_chips(dot_nt(dboth, w_in).astype(bf16).reshape(CHIPS, seq_len, D), 3)
    dhmid, grad_gain_ffn = norm_backward(hmid, hmid_scale, gain_ffn, dhn)
    dhmid = dhmid + dy
    dattn = dhmid.astype(bf16)
    dheads = dot_nt(dattn, w_o).astype(bf16).reshape(seq_len, CHIPS, 2 * DH)
    dheads = exchange_chips(jnp.transpose(dheads, (1, 0, 2)))
    dheads = jnp.pad(dheads.reshape(CHIPS, seq_len, 2, DH), ((0, 0), (0, 0), (0, 0), (0, HP - DH)))
    dqkv, theta_sums, mixer_sums, gain_sums = run_backward(
        group_lengths, mix, qkv, toep, gain_pair, scores, weights, outs, dheads.reshape(CHIPS, seq_len, 2 * HP)
    )
    dqkv_rows = dqkv.reshape(CHIPS * seq_len, 6 * HP)
    dxn = scatter_slow(dot_nt(dqkv_rows, w_qkv).reshape(CHIPS, seq_len, D))
    dinput, grad_gain_attn = norm_backward(input_float, input_scale, gain_attn, dxn)
    input_grad = dinput + dhmid

    taps = jnp.asarray(band())
    theta_sums = theta_sums.reshape(2, seq_len, CQ, seq_len)
    grad_theta = jnp.stack(
        [jnp.sum(jnp.where(taps[tap][None, :, None, :], theta_sums, 0.0), axis=(1, 3)) for tap in range(CK)], axis=2
    )
    grad_mixer = jnp.sum(mixer_sums[:4], axis=1)
    vector_grad = jnp.concatenate(
        [
            grad_gain_attn,
            lax.dynamic_update_slice_in_dim(
                jnp.zeros((D,), f32), gain_sums.reshape(2, HP)[:, :DH].reshape(-1), chip * 2 * DH, 0
            ),
            grad_gain_ffn,
            lax.dynamic_update_slice_in_dim(
                jnp.zeros((H * CQ * CK,), f32), grad_theta.reshape(-1), chip * 2 * CQ * CK, 0
            ),
            lax.dynamic_update_slice_in_dim(jnp.zeros((2 * H,), f32), grad_mixer, chip * 4, 0),
        ]
    )
    pieces = jnp.pad(vector_grad.reshape(fs_size, 1, own_vec), ((0, 0), (0, 0), (0, 512 - own_vec)))
    pieces = jnp.broadcast_to(pieces, (fs_size, reps, 512)).reshape(-1, 4, 128)
    vector_total = jnp.sum(
        lax.all_to_all(pieces, ALL, split_axis=0, concat_axis=0, tiled=True), axis=0
    ).reshape(512)[:own_vec]

    strip = BLK // (2 * CHIPS)
    grad_in = dot_tn(hn_rows, dboth).reshape(ROW_TILES, 2, CHIPS, strip, 2, BLK)
    grad_down = dot_tn(inner, dy_rows).reshape(2, CHIPS, strip, ROW_TILES, BLK)
    grad_in = jnp.transpose(half_for_core(grad_in, 1), (1, 3, 0, 2, 4)).reshape(CHIPS, 2 * ROW_TILES, strip, BLK)
    grad_down = jnp.transpose(half_for_core(grad_down, 0), (0, 2, 1, 3))
    ffn_tiles = exchange_chips(jnp.concatenate([grad_in, grad_down], axis=1).astype(bf16))
    gate_tiles = jnp.transpose(ffn_tiles[:, : 2 * ROW_TILES], (1, 0, 2, 3)).reshape(-1, strip, BLK)
    down_tiles = ffn_tiles[:, 2 * ROW_TILES :].reshape(-1, strip, BLK)
    grad_qkv = dot_tn(xn_rows, dqkv_rows).reshape(ROW_TILES, 2, CHIPS, strip, 6, HP)[..., :DH]
    grad_qkv = jnp.transpose(half_for_core(grad_qkv, 1), (1, 0, 2, 3, 4))
    grad_qkv = exchange_chips(grad_qkv.astype(bf16).reshape(CHIPS, ROW_TILES, strip, 6 * DH))
    grad_qkv = jnp.transpose(
        grad_qkv.reshape(CHIPS, ROW_TILES, strip, 3, 2 * DH), (3, 1, 2, 0, 4)
    ).reshape(3, ROW_TILES, strip, ROW_TILES, BLK)
    qkv_tiles = jnp.transpose(grad_qkv, (0, 1, 3, 2, 4)).reshape(-1, strip, BLK)
    heads_strips = jnp.transpose(heads.reshape(seq_len, 2 * ROW_TILES, CHIPS, strip), (2, 0, 1, 3))
    heads_strips = exchange_chips(heads_strips.reshape(CHIPS, seq_len, 2 * ROW_TILES * strip))
    dattn_rows = gather_slow(dattn).reshape(CHIPS * seq_len, D)
    grad_out = dot_tn(heads_strips.reshape(CHIPS * seq_len, -1), dattn_rows)
    grad_out = half_for_core(grad_out.reshape(ROW_TILES, 2, strip, ROW_TILES, BLK), 1)
    out_tiles = jnp.transpose(grad_out.astype(bf16), (0, 2, 1, 3)).reshape(-1, strip, BLK)

    groups = lax.axis_size("g")
    part = strip // groups
    own_slots = basis_left.shape[0]
    devices = groups * 2 * CHIPS
    slot_total = own_slots * devices
    sums = jnp.concatenate(
        [sum_groups(jnp.concatenate([qkv_tiles, out_tiles], axis=0)), sum_groups(jnp.concatenate([gate_tiles, down_tiles], axis=0))],
        axis=0,
    )
    matches = (jnp.arange(slot_total)[:, None] == owners[None, :]).astype(bf16)
    slots = dot(matches, sums.reshape(sums.shape[0], -1)).astype(bf16)
    slots = lax.all_to_all(
        slots.reshape(devices, own_slots, part, BLK), ALL, split_axis=0, concat_axis=0, tiled=True
    )
    slots = slots.reshape(groups, 2, 2, 2, 2, own_slots, part, BLK)
    own_grad = jnp.transpose(slots, (5, 3, 4, 1, 2, 0, 6, 7)).reshape(own_slots, BLK, BLK)

    left_low, right_low = basis_left.astype(bf16), basis_right.astype(bf16)
    rotated = jnp.einsum("sia,sij->saj", left_low, own_grad, preferred_element_type=f32)
    rotated = jnp.einsum("saj,sjb->sab", rotated.astype(bf16), right_low, preferred_element_type=f32)
    first_new = beta_first * block_first + (1.0 - beta_first) * rotated
    second_new = beta_second * block_second + (1.0 - beta_second) * rotated * rotated
    direction = (first_new / (jnp.sqrt(second_new) + eps_adam)).astype(bf16)
    turned = jnp.einsum("sia,sab->sib", left_low, direction, preferred_element_type=f32)
    turned = jnp.einsum("sib,sjb->sij", turned.astype(bf16), right_low, preferred_element_type=f32)
    master_new = block_master - rate_block * (turned + decay_block * block_master)
    vec_first_new = beta_first * vec_first + (1.0 - beta_first) * vector_total
    vec_second_new = beta_second * vec_second + (1.0 - beta_second) * vector_total * vector_total
    vec_master_new = vec_master - rate_vector * vec_first_new / (jnp.sqrt(vec_second_new) + eps_adam)
    return (
        layer_output, input_grad, first_new, second_new, master_new, master_new.astype(bf16),
        vec_first_new, vec_second_new, vec_master_new, vec_master_new.astype(bf16),
    )


def group_at(mask):
    return {axis: 1 - lax.axis_index(axis) for axis, bit in (("g", 4), ("a", 2), ("b", 1)) if mask & bit}


def other_bit(axis, changed):
    at = lax.axis_index(axis)
    return 1 - at if changed else at


def push(src, dst, send, recv, device):
    copy = pltpu.make_async_remote_copy(src_ref=src, dst_ref=dst, send_sem=send, recv_sem=recv, device_id=device)
    copy.start()
    return copy


class Gather:
    def __init__(self, x_ref, out_ref, local_sem, send1, recv1, send2, recv2, send3, recv3):
        self.x, self.out, self.local_sem = x_ref, out_ref, local_sem
        self.sems = ((send1, recv1), (send2, recv2), (send3, recv3))
        self.me = chip_index()
        self.half = x_ref.shape[0] // 2
        self.sent, self.second = [], []

    def here(self, part):
        return pl.ds(part * self.half, self.half)

    def start(self):
        self.local = pltpu.make_async_copy(self.x, self.out.at[self.me], self.local_sem)
        self.local.start()
        send, recv = self.sems[0]
        for part in range(2):
            for at, (axis, _, _) in enumerate(HOPS):
                self.sent.append(
                    push(
                        self.x.at[self.here(part)], self.out.at[self.me, self.here(part)],
                        send.at[at, part], recv.at[at, part], across(axis),
                    )
                )

    def onward(self):
        send, recv = self.sems[1]
        for part in range(2):
            for at, (axis, onward, _) in enumerate(HOPS):
                self.sent[part * 3 + at].wait_recv()
                block = self.out.at[flipped(self.me, (axis,)), self.here(part)]
                self.second.append(push(block, block, send.at[at, part], recv.at[at, part], across(onward)))

    def last(self):
        send, recv = self.sems[2]
        self.third = []
        for copy in self.second:
            copy.wait_recv()
        for at, (axis, onward, last) in enumerate(HOPS):
            begin, count = THIRDS[at]
            piece = self.out.at[flipped(self.me, (axis, onward)), pl.ds(begin, count)]
            self.third.append(push(piece, piece, send.at[at], recv.at[at], across(last)))

    def finish(self):
        for copy in self.third:
            copy.wait_recv()
        self.local.wait()

    def drain(self):
        for copy in self.sent + self.second + self.third:
            copy.wait_send()


class SideGather:
    def __init__(self, x_ref, out_ref, local_sem, send1, recv1, send2, recv2, send3, recv3):
        self.x, self.out, self.local_sem = x_ref, out_ref, local_sem
        self.sems = ((send1, recv1), (send2, recv2), (send3, recv3))
        self.me = chip_index()
        half = x_ref.shape[0] // 2
        self.low, self.high = pl.ds(0, half), pl.ds(half, half)

    def start(self):
        self.local = pltpu.make_async_copy(self.x, self.out.at[self.me], self.local_sem)
        self.local.start()
        send, recv = self.sems[0]
        self.first = [
            push(self.x, self.out.at[self.me], send.at[at], recv.at[at], across(axis)) for at, axis in enumerate("aby")
        ]

    def onward(self):
        send, recv = self.sems[1]
        blocks = [self.out.at[flipped(self.me, (axis,))] for axis in "aby"]
        self.first[0].wait_recv()
        self.second = [
            push(blocks[0], blocks[0], send.at[0], recv.at[0], across("b")),
            push(blocks[0], blocks[0], send.at[1], recv.at[1], across("y")),
        ]
        self.first[1].wait_recv()
        piece = blocks[1].at[self.high]
        self.second.append(push(piece, piece, send.at[2], recv.at[2], across("y")))
        self.first[2].wait_recv()
        piece = blocks[2].at[self.low]
        self.second.append(push(piece, piece, send.at[3], recv.at[3], across("b")))

    def last(self):
        send, recv = self.sems[2]
        self.second[0].wait_recv()
        piece = self.out.at[flipped(self.me, ("a", "b")), self.high]
        self.third = [push(piece, piece, send.at[0], recv.at[0], across("y"))]
        self.second[1].wait_recv()
        piece = self.out.at[flipped(self.me, ("a", "y")), self.low]
        self.third.append(push(piece, piece, send.at[1], recv.at[1], across("b")))

    def finish(self):
        for copy in self.second[2:] + self.third:
            copy.wait_recv()
        self.local.wait()

    def drain(self):
        for copy in self.first + self.second + self.third:
            copy.wait_send()


def side_sems():
    dma = pltpu.SemaphoreType.DMA
    return [dma] + [dma((3,))] * 2 + [dma((4,))] * 2 + [dma((2,))] * 2


class Scatter:
    def __init__(self, parts, near, in2, in3, acc2, acc3, send1, recv1, send2, recv2, send3, recv3):
        self.parts, self.near, self.in2, self.in3, self.acc2, self.acc3 = parts, near, in2, in3, acc2, acc3
        self.sems = ((send1, recv1), (send2, recv2), (send3, recv3))
        self.me = chip_index()
        self.half = parts.shape[1] // 2

    def here(self, part):
        return pl.ds(part * self.half, self.half)

    def start(self):
        send, recv = self.sems[0]
        opposite = flipped(self.me, ("y", "a", "b"))
        self.first = []
        for at, (_, _, last) in enumerate(HOPS):
            rows = pl.ds(*THIRDS[at])
            self.first.append(push(self.parts.at[opposite, rows], self.in2.at[rows], send.at[at], recv.at[at], across(last)))

    def onward(self):
        send, recv = self.sems[1]
        self.second = []
        for part in range(2):
            for at, (axis, onward, _) in enumerate(HOPS):
                dest = flipped(self.me, (axis, onward))
                if part == 0:
                    self.first[at].wait_recv()
                    rows = pl.ds(*THIRDS[at])
                    self.acc2[at] = self.parts[dest]
                    self.acc2[at, rows] = (
                        self.parts[dest, rows].astype(f32) + self.in2[rows].astype(f32)
                    ).astype(bf16)
                here = self.here(part)
                self.second.append(
                    push(self.acc2.at[at, here], self.in3.at[at, here], send.at[at, part], recv.at[at, part], across(onward))
                )

    def last(self):
        send, recv = self.sems[2]
        self.third = []
        for part in range(2):
            here = self.here(part)
            for at, (axis, _, _) in enumerate(HOPS):
                dest = flipped(self.me, (axis,))
                self.second[part * 3 + at].wait_recv()
                self.acc3[at, here] = (
                    self.parts[dest, here].astype(f32) + self.in3[at, here].astype(f32)
                ).astype(bf16)
                self.third.append(
                    push(self.acc3.at[at, here], self.near.at[at, here], send.at[at, part], recv.at[at, part], across(axis))
                )

    def finish(self, part):
        here = self.here(part)
        for at in range(3):
            self.third[part * 3 + at].wait_recv()
        return (self.parts[self.me, here].astype(f32) + self.near[0, here].astype(f32)) + (
            self.near[1, here].astype(f32) + self.near[2, here].astype(f32)
        )

    def drain(self):
        for copy in self.first + self.second + self.third:
            copy.wait_send()


class SideScatter:
    def __init__(self, parts, near, in1, in2, acc2, acc3, send1, recv1, send2, recv2, send3, recv3):
        self.parts, self.near, self.in1, self.in2, self.acc2, self.acc3 = parts, near, in1, in2, acc2, acc3
        self.sems = ((send1, recv1), (send2, recv2), (send3, recv3))
        self.me = chip_index()
        half = parts.shape[1] // 2
        self.low, self.high = pl.ds(0, half), pl.ds(half, half)

    def start(self):
        send, recv = self.sems[0]
        far, side = flipped(self.me, ("a", "b", "y")), flipped(self.me, ("b", "y"))
        self.first = [
            push(self.parts.at[block, rows], self.in1.at[at], send.at[at], recv.at[at], across(axis))
            for at, (block, rows, axis) in enumerate(
                ((far, self.high, "y"), (far, self.low, "b"), (side, self.low, "b"), (side, self.high, "y"))
            )
        ]

    def add(self, at, axes, rows, acc):
        self.first[at].wait_recv()
        block = flipped(self.me, axes)
        acc[...] = self.parts[block]
        acc[rows] = (self.parts[block, rows].astype(f32) + self.in1[at].astype(f32)).astype(bf16)
        return acc

    def onward(self):
        send, recv = self.sems[1]
        third_send, third_recv = self.sems[2]
        self.second = [
            push(self.add(0, ("a", "b"), self.high, self.acc2.at[0]), self.in2.at[0], send.at[0], recv.at[0], across("b")),
            push(self.add(1, ("a", "y"), self.low, self.acc2.at[1]), self.in2.at[1], send.at[1], recv.at[1], across("y")),
        ]
        self.third = [
            push(self.add(at, (axis,), rows, self.acc3.at[to]), self.near.at[to], third_send.at[to], third_recv.at[to], across(axis))
            for at, axis, rows, to in ((3, "b", self.high, 1), (2, "y", self.low, 2))
        ]

    def last(self):
        send, recv = self.sems[2]
        for copy in self.second:
            copy.wait_recv()
        self.acc3[0] = (
            self.parts[flipped(self.me, ("a",))].astype(f32) + (self.in2[0].astype(f32) + self.in2[1].astype(f32))
        ).astype(bf16)
        self.third.append(push(self.acc3.at[0], self.near.at[0], send.at[0], recv.at[0], across("a")))

    def finish(self):
        for copy in self.third:
            copy.wait_recv()
        return (self.parts[self.me].astype(f32) + self.near[0].astype(f32)) + (
            self.near[1].astype(f32) + self.near[2].astype(f32)
        )

    def drain(self):
        for copy in self.first + self.second + self.third:
            copy.wait_send()


def side_scatter_scratch(rows, width):
    dma = pltpu.SemaphoreType.DMA
    return [
        pltpu.VMEM(dims + (width,), bf16) for dims in ((3, rows), (4, rows // 2), (2, rows), (2, rows), (3, rows))
    ] + [dma((4,))] * 2 + [dma((2,))] * 2 + [dma((3,))] * 2


def scatter_scratch(rows, width):
    dma = pltpu.SemaphoreType.DMA
    three = pltpu.VMEM((3, rows, width), bf16)
    return [three, pltpu.VMEM((rows, width), bf16), three, three, three] + [dma((3,))] * 2 + [dma((3, 2))] * 4


VMEM = pl.BlockSpec(memory_space=pltpu.VMEM)


HEAD_ROW, FFN_ROW, THETA_ROW, MIX_ROW, VEC_ROWS = 12, 28, 40, 56, 64
SHARD_ROWS = 16


def vector_row(at):
    for begin, row, width in (
        (3 * D + H * CQ * CK, MIX_ROW, 4), (3 * D, THETA_ROW, CQ * CK), (2 * D, FFN_ROW, 128), (D, HEAD_ROW, DH), (0, 0, 128)
    ):
        if at >= begin:
            return row + (at - begin) // width


def vector_rows(own_vec, shards):
    return [min(vector_row(shard * own_vec), VEC_ROWS - SHARD_ROWS) // 8 * 8 for shard in range(shards)]


def rows_of_vector(flat):
    conv_end = 3 * D + H * CQ * CK
    return jnp.concatenate(
        [
            flat[:D].reshape(-1, 128),
            jnp.pad(flat[D : 2 * D].reshape(H, DH), ((0, 0), (0, 128 - DH))),
            flat[2 * D : 3 * D].reshape(-1, 128),
            jnp.pad(flat[3 * D : conv_end].reshape(H, CQ * CK), ((0, 0), (0, 128 - CQ * CK))),
            jnp.pad(flat[conv_end : conv_end + 2 * H].reshape(CHIPS, 4), ((0, 0), (0, 124))),
        ],
        axis=0,
    )


def source_at(mask):
    return ((other_bit("g", mask & 4) * 2 + other_bit("a", mask & 2)) * 2 + other_bit("b", mask & 1)) * 2 + lax.axis_index("c")


def front_body(
    first_rows, length_ref, vec_ref, x_ref, w_query_ref, w_key_ref, w_value_ref, cot_ref,
    w_out_ref, w_gate_ref, w_up_ref, w_down_ref, dy_ref, len_ref, mix_ref, gains_ref, toep_ref, gain_ref, strips_ref, hmid_ref,
    xn_out, qkv_out, s_out, p_out, o_out, wq_out, wo_out, hn_all_ref, w_in_ref, w_dn_ref, dy_all_ref,
    xn_ref, qkv_ref, s_ref, p_ref, o_ref, wq_ref, wo_ref, heads_ref, leave_sems,
    blocks_ref, own_len_ref, vecs_ref, full_ref, x_all_ref, pad_ref, out_heads, hn_ref, passing, vec_send, vec_recv, len_send, len_recv, local_sems, q_send, q_recv, q_core_send, q_core_recv,
    o_send, o_recv, o_side_send, o_side_recv, o_core_send, o_core_recv, d_send, d_recv,
    w_send, w_recv, u_send, u_recv, core_send, core_recv, head_send, head_recv, *hops,
):
    seqs, rows, _ = x_all_ref.shape
    g, a, b, c, y = (lax.axis_index(axis) for axis in ALL)
    me = chip_index()
    mine = source_at(0)
    shard = {mask: source_at(mask) for mask in range(8)}
    low, high = pl.ds(0, BLK), pl.ds(BLK, BLK)
    order = (4, 6, 5, 7, 2, 1, 3)

    def columns(chip):
        return pl.ds(pl.multiple_of(chip * BLK, BLK), BLK)

    def block_to(mask):
        return (y * 2 + other_bit("a", mask & 2)) * 2 + other_bit("b", mask & 1)

    local = [
        pltpu.make_async_copy(w_out_ref, wo_ref.at[mine], local_sems.at[1]),
        pltpu.make_async_copy(w_gate_ref.at[:, columns(me)], w_in_ref.at[mine, :, low], local_sems.at[2]),
        pltpu.make_async_copy(w_up_ref.at[:, columns(me)], w_in_ref.at[mine, :, high], local_sems.at[3]),
    ]
    down_local = pltpu.make_async_copy(w_down_ref, w_dn_ref.at[c], local_sems.at[4])
    own_len_ref[...] = jnp.full(own_len_ref.shape, length_ref[0].astype(f32), f32)
    own_small = [
        pltpu.make_async_copy(vec_ref, vecs_ref.at[mine], local_sems.at[5]),
        pltpu.make_async_copy(own_len_ref, len_ref.at[me], local_sems.at[6]),
    ]
    for copy in local + own_small:
        copy.start()

    @pl.when(g == y)
    def _():
        down_local.start()

    greet_all()
    leaving = []

    def leave(src, dst):
        copy = pltpu.make_async_copy(src, dst, leave_sems.at[len(leaving)])
        copy.start()
        leaving.append(copy)

    sent, relayed = {}, []
    first = Gather(x_ref, x_all_ref, *hops[:7])
    side = SideGather(dy_ref, dy_all_ref, *hops[7:14])
    gather = Gather(hn_ref, hn_all_ref, *hops[14:])

    def push_vec(step, carry):
        to = lax.rem(mine + step, 16)
        pltpu.make_async_remote_copy(
            src_ref=vec_ref, dst_ref=vecs_ref.at[mine], send_sem=vec_send, recv_sem=vec_recv,
            device_id={
                "g": lax.div(to, 8), "a": lax.rem(lax.div(to, 4), 2), "b": lax.rem(lax.div(to, 2), 2), "c": lax.rem(to, 2)
            },
        ).start()
        return carry

    lax.fori_loop(1, 16, push_vec, 0)
    lengths_sent = [
        push(own_len_ref, len_ref.at[me], len_send.at[mask], len_recv.at[mask], chip_at(mask)) for mask in range(1, 8)
    ]

    first.start()
    for chip in range(CHIPS):
        cols = slice(chip * 2 * DH, (chip + 1) * 2 * DH)
        blocks_ref[chip] = jnp.concatenate([w_query_ref[:, cols], w_key_ref[:, cols], w_value_ref[:, cols]], axis=1)
    wq_ref[mine] = blocks_ref[me]
    valid = lax.broadcasted_iota(jnp.int32, cot_ref.shape, 0) < length_ref[0]
    dy_ref[...] = jnp.where(valid, cot_ref[...].astype(f32), 0.0).astype(bf16)

    for mask in order:
        sent[mask] = push(blocks_ref.at[block_to(mask)], wq_ref.at[mine], q_send.at[mask], q_recv.at[mask], group_at(mask))

    def relay_qkv(mask):
        sent[mask].wait_recv()
        block = wq_ref.at[shard[mask]]
        relayed.append(push(block, block, q_core_send.at[mask], q_core_recv.at[mask], across("c")))

    half = pl.ds(pl.multiple_of(y * 48, 16), 48)
    lines, o_side, o_core = {}, {}, []

    def start_lines():
        for mask in (2, 4, 6):
            lines[mask] = push(w_out_ref.at[half], wo_ref.at[mine, half], o_send.at[mask], o_recv.at[mask], group_at(mask))
        lines[1] = push(w_out_ref.at[half], wo_ref.at[mine, half], o_send.at[1], o_recv.at[1], across("b"))
        o_core.append(push(w_out_ref, wo_ref.at[mine], o_core_send.at[0], o_core_recv.at[0], across("c")))

    def to_side(mask):
        lines[mask].wait_recv()
        piece = wo_ref.at[shard[mask], half]
        o_side[mask] = push(piece, piece, o_side_send.at[mask], o_side_recv.at[mask], across("y"))
        if mask in (2, 4, 6):
            lines[mask + 1] = push(piece, piece, o_send.at[mask + 1], o_recv.at[mask + 1], across("b"))

    def out_to_core(masks):
        for mask in masks:
            o_side[mask].wait_recv()
            block = wo_ref.at[shard[mask]]
            o_core.append(push(block, block, o_core_send.at[mask], o_core_recv.at[mask], across("c")))

    count = w_down_ref.shape[0] // 2
    upper, lower = pl.ds(0, count), pl.ds(count, count)

    def down_copy(src, dst, at, axis):
        return pltpu.make_async_remote_copy(
            src_ref=src, dst_ref=dst, send_sem=d_send.at[at], recv_sem=d_recv.at[at], device_id=across(axis)
        )

    def down_direct():
        return down_copy(w_down_ref.at[upper], w_dn_ref.at[c, upper], 0, "g")

    def down_around():
        return down_copy(w_down_ref.at[lower], passing, 1, "g")

    def down_over():
        return down_copy(passing, w_dn_ref.at[c, lower], 2, "y")

    def down_to_core():
        return down_copy(w_dn_ref.at[c], w_dn_ref.at[c], 3, "c")

    def down_start():
        @pl.when(g == y)
        def _():
            down_direct().start()

        @pl.when(g != y)
        def _():
            down_around().start()

    def down_pass():
        @pl.when(g == y)
        def _():
            down_around().wait_recv()
            down_over().start()

    def down_last():
        @pl.when(g == y)
        def _():
            down_local.wait()
            down_to_core().start()
            down_direct().wait_send()
            down_over().wait_send()

        @pl.when(g != y)
        def _():
            down_direct().wait_recv()
            down_over().wait_recv()
            down_to_core().start()
            down_around().wait_send()

    gate, up = {}, {}

    def send_columns(masks):
        for mask in masks:
            to = columns(block_to(mask))
            gate[mask] = push(w_gate_ref.at[:, to], w_in_ref.at[mine, :, low], w_send.at[mask], w_recv.at[mask], group_at(mask))
            up[mask] = push(w_up_ref.at[:, to], w_in_ref.at[mine, :, high], u_send.at[mask], u_recv.at[mask], group_at(mask))

    def relay(mask):
        gate[mask].wait_recv()
        up[mask].wait_recv()
        block = w_in_ref.at[shard[mask]]
        relayed.append(push(block, block, core_send.at[mask], core_recv.at[mask], across("c")))

    side.start()
    relayed.append(push(wq_ref.at[mine], wq_ref.at[mine], q_core_send.at[0], q_core_recv.at[0], across("c")))
    first.onward()
    start_lines()

    for copy in own_small:
        copy.wait()
    others = vecs_ref.at[pl.ds(0, 15)]
    pltpu.make_async_copy(others, others, vec_recv).wait()
    full_ref[...] = jnp.zeros_like(full_ref)
    for at, row in enumerate(first_rows):
        full_ref[row : row + SHARD_ROWS, :] += vecs_ref[at]
    gains_ref[...] = jnp.zeros_like(gains_ref)
    for row in range(D // 128):
        gains_ref[0:1, row * 128 : (row + 1) * 128] = full_ref[row : row + 1, :]
        gains_ref[1:2, row * 128 : (row + 1) * 128] = full_ref[FFN_ROW + row : FFN_ROW + row + 1, :]
    mix_ref[...] = jnp.zeros_like(mix_ref)
    mix_row = full_ref[pl.ds(MIX_ROW + me, 1), :]
    for at in range(4):
        mix_ref[at : at + 1, :] = jnp.broadcast_to(mix_row[:, at : at + 1], (1, 128))
    query_at = lax.broadcasted_iota(jnp.int32, (rows, rows), 0)
    key_at = lax.broadcasted_iota(jnp.int32, (rows, rows), 1)
    key_float = key_at.astype(f32)
    tap_at = query_at - key_at + CK // 2
    for head in range(2):
        gain_ref[:, head * HP : (head + 1) * HP] = full_ref[pl.ds(HEAD_ROW + 2 * me + head, 1), :]
        theta = full_ref[pl.ds(THETA_ROW + 2 * me + head, 1), :]
        for lag in range(CQ):
            band_values = jnp.zeros((rows, rows), f32)
            for tap in range(CK):
                at = lag * CK + tap
                band_values = jnp.where(tap_at == tap, theta[:, at : at + 1], band_values)
            toep_ref[head, lag * rows : (lag + 1) * rows, :] = band_values.astype(bf16)

    side.onward()
    first.last()
    side.last()
    down_start()
    for mask in order:
        relay_qkv(mask)
    send_columns((2, 1, 3, 4, 6, 5, 7))
    first.finish()
    for copy in relayed + lengths_sent:
        copy.wait_recv()
    qkv_relayed = relayed[:]
    del relayed[:]

    pad_ref[0:8, :] = jnp.zeros((8, rows), f32)
    blank = jnp.zeros((rows, HP - DH), bf16)
    batch = 4

    def project(at, carry):
        values = x_all_ref[pl.ds(at * batch, batch)].astype(f32).reshape(batch * rows, D)
        normed = (values * rms(values) * gains_ref[0:1, :]).astype(bf16)
        xn_ref[pl.ds(at * batch, batch)] = normed.reshape(batch, rows, D)
        made = dot(normed, wq_ref[...].reshape(D, 6 * DH)).astype(bf16)
        for seq in range(batch):
            for piece in range(6):
                qkv_ref[at * batch + seq, :, piece * HP : (piece + 1) * HP] = jnp.concatenate(
                    [made[seq * rows : (seq + 1) * rows, piece * DH : (piece + 1) * DH], blank], axis=1
                )
        return carry

    project(0, 0)
    for mask in (2, 4, 6, 1):
        to_side(mask)
    project(1, 0)
    leave(xn_ref, xn_out)
    leave(qkv_ref, qkv_out)
    leave(wq_ref, wq_out)
    for copy in local:
        copy.wait()
    relayed.append(push(w_in_ref.at[mine], w_in_ref.at[mine], core_send.at[0], core_recv.at[0], across("c")))

    def head_copy(seq):
        return pltpu.make_async_remote_copy(
            src_ref=out_heads.at[seq], dst_ref=heads_ref.at[me], send_sem=head_send.at[seq], recv_sem=head_recv.at[me],
            device_id={"y": lax.div(seq, 4), "a": lax.rem(lax.div(seq, 2), 2), "b": lax.rem(seq, 2)},
        )

    def attend(step, carry):
        seq = lax.rem(me + step, seqs)
        keep = (key_at <= query_at) & (key_float < len_ref[seq, 0:1, :])
        weights, made = [], []
        for head in range(2):
            query = qkv_ref[seq, :, head * HP : (head + 1) * HP]
            key = qkv_ref[seq, :, (2 + head) * HP : (3 + head) * HP]
            scores = jnp.where(keep, dot_nt(query, key) * (1.0 / math.sqrt(DH)), 0.0)
            s_ref[seq, head] = scores.astype(bf16)
            wide = shifted_down(pad_ref, scores)
            near = wide.astype(bf16)
            rest = (wide - near.astype(f32)).astype(bf16)
            conv = dot(near, toep_ref[head]) + dot(rest, toep_ref[head])
            logits = jnp.where(keep, conv, -1e30)
            weight = jnp.exp(logits - jnp.max(logits, axis=-1, keepdims=True))
            weight = weight / jnp.sum(weight, axis=-1, keepdims=True)
            p_ref[seq, head] = weight
            weights.append(weight)
        for head in range(2):
            mixed = mix_ref[2 * head : 2 * head + 1, :] * weights[0] + mix_ref[2 * head + 1 : 2 * head + 2, :] * weights[1]
            value = qkv_ref[seq, :, (4 + head) * HP : (5 + head) * HP]
            out = dot(mixed.astype(bf16), value)
            o_ref[seq, :, head * HP : (head + 1) * HP] = out
            scale = lax.rsqrt(jnp.sum(out * out, axis=-1, keepdims=True) * (1.0 / DH) + eps_norm)
            made.append((out * scale * gain_ref[:, head * HP : (head + 1) * HP])[:, :DH])
        out_heads[seq] = jnp.concatenate(made, axis=1).astype(bf16)

        @pl.when(step > 0)
        def _():
            head_copy(seq).start()

        return carry

    lax.fori_loop(0, 3, attend, 0)
    for mask in (3, 5, 7):
        to_side(mask)
    down_pass()
    lax.fori_loop(3, 6, attend, 0)
    out_to_core((2, 4, 6))
    lax.fori_loop(6, seqs, attend, 0)
    out_to_core((1, 3, 5, 7))
    heads_ref[me] = out_heads[me]
    leave(s_ref, s_out)
    leave(p_ref, p_out)
    leave(o_ref, o_out)
    for copy in o_core:
        copy.wait_recv()
    leave(wo_ref, wo_out)

    def head_arrived(step, carry):
        source = lax.rem(me + step, seqs)
        pltpu.make_async_copy(out_heads.at[source], heads_ref.at[source], head_recv.at[source]).wait()
        return carry

    lax.fori_loop(1, seqs, head_arrived, 0)

    def project_out(at, carry):
        cols = pl.ds(pl.multiple_of(at * BLK, BLK), BLK)
        total = x_ref[:, cols].astype(f32)
        for chip in range(CHIPS):
            weight = wo_ref[2 * chip : 2 * chip + 2, :, cols].reshape(2 * DH, BLK)
            total += dot(heads_ref[chip], weight)
        hmid_ref[:, cols] = total
        return carry

    lax.fori_loop(0, ROW_TILES, project_out, 0)
    hmid = hmid_ref[...]
    hn_ref[...] = (hmid * rms(hmid) * gains_ref[1:2, :]).astype(bf16)
    gather.start()
    width = BLK // (2 * CHIPS)
    for chip in range(CHIPS):
        pieces = []
        for at in range(2 * ROW_TILES):
            begin = at * (BLK // 2) + chip * width
            source, begin = begin // (2 * DH), begin % (2 * DH)
            pieces.append(heads_ref[source, :, begin : begin + width])
        strips_ref[chip] = jnp.concatenate(pieces, axis=1)
    for mask in (4, 6):
        relay(mask)
    gather.onward()
    for mask in (5, 7, 2):
        relay(mask)
    gather.last()
    for mask in (1, 3):
        relay(mask)
    down_last()
    down_to_core().wait()
    side.finish()
    gather.finish()
    for copy in relayed:
        copy.wait_recv()
    for copy in leaving:
        copy.wait()

    def head_left(step, carry):
        head_copy(lax.rem(me + step, seqs)).wait_send()
        return carry

    lax.fori_loop(1, seqs, head_left, 0)
    first.drain()
    side.drain()
    gather.drain()
    for copies in (sent, lines, o_side, gate, up):
        for copy in copies.values():
            copy.wait_send()
    pltpu.make_async_copy(others, others, vec_send).wait()
    for copy in qkv_relayed + relayed + o_core + lengths_sent:
        copy.wait_send()


def run_front(first_rows, length, vec, x, w_query, w_key, w_value, cotangent, w_out, w_gate, w_up, w_down):
    rows = x.shape[0]
    dma = pltpu.SemaphoreType.DMA
    small = [
        (x.shape, bf16), ((CHIPS, 8, 128), f32), ((8, 128), f32), ((8, D), f32), ((2, CQ * rows, rows), bf16), ((1, 2 * HP), f32),
        ((CHIPS, rows, 2 * DH), bf16), ((rows, D), f32),
    ]
    large = [
        ((CHIPS, rows, D), bf16), ((CHIPS, rows, 6 * HP), bf16), ((CHIPS, 2, rows, rows), bf16), ((CHIPS, 2, rows, rows), f32),
        ((CHIPS, rows, 2 * HP), f32), ((16, w_query.shape[0], 6 * DH), bf16), ((16,) + w_out.shape, bf16),
    ]
    gathered = [
        ((CHIPS, rows, D), bf16), ((16, w_gate.shape[0], 2 * BLK), bf16), ((2,) + w_down.shape, bf16), ((CHIPS, rows, D), bf16),
    ]
    return pl.pallas_call(
        functools.partial(front_body, first_rows),
        in_specs=[SMEM] + [VMEM] * 6 + [ANYS] * 4,
        out_specs=[VMEM] * len(small) + [ANYS] * (len(large) + len(gathered)),
        out_shape=[jax.ShapeDtypeStruct(*shape) for shape in small + large + gathered],
        scratch_shapes=[pltpu.VMEM(*shape) for shape in large] + [
            pltpu.VMEM((CHIPS, rows, 2 * DH), bf16), dma((len(large),)),
            pltpu.VMEM((CHIPS, w_query.shape[0], 6 * DH), bf16), pltpu.VMEM((8, 128), f32), pltpu.VMEM((16,) + vec.shape, f32), pltpu.VMEM((VEC_ROWS, 128), f32), pltpu.VMEM((CHIPS, rows, D), bf16), pltpu.VMEM((rows + 8, rows), f32), pltpu.VMEM((CHIPS, rows, 2 * DH), bf16),
            pltpu.VMEM((rows, D), bf16), pltpu.VMEM((w_down.shape[0] // 2, D), bf16), dma, dma, dma((8,)), dma((8,)), dma((7,)),
        ] + [dma((8,))] * 10 + [dma((4,))] * 2 + [dma((8,))] * 8 + hop_sems() + side_sems() + hop_sems(),
        name="front",
        compiler_params=pltpu.CompilerParams(collective_id=2, has_side_effects=True, vmem_limit_bytes=56 * 2**20),
    )(length, vec, x, w_query, w_key, w_value, cotangent, w_out, w_gate, w_up, w_down)


def middle_body(
    len_ref, mix_ref, hn_ref, dy_ref, xn_ref, w_in_hbm, w_dn_hbm, wq_hbm, dy_own_ref, hmid_ref, gains_ref, wo_hbm,
    qkv_hbm, toep_ref, gain_ref, s_hbm, p_hbm, o_hbm, strips_ref,
    inner_ref, dhmid_ref, dxn_ref, gain_ffn_grad_ref, theta_ref, mixer_ref, gain_grad_ref, tiles_ref,
    w_in_ref, w_dn_ref, wq_ref, wo_ref, qkv_ref, s_ref, p_ref, o_ref, enter_sems,
    theta_sums, pad_ref, first_ref, second_ref, dboth_ref, parts_ref, dattn_ref, grads_ref, sent_ref, strips_in, gin_ref, gd_ref,
    half_in, half_d, near_in, near_d, dqkv_ref, gq_ref, go_ref, core_q, core_o, in_q, in_o,
    near3, in23, in33, local_sems, load_sems, strip_send, strip_recv, head_send, head_recv,
    core_send, core_recv, near_send, near_recv, gu_send, gu_recv, q_send, q_recv, *rest,
):
    scatter_args, scatter3_sems, side = rest[:11], rest[11:17], rest[17:]
    seqs, rows, _ = hn_ref.shape
    g, a, b, c, y = (lax.axis_index(axis) for axis in ALL)
    me = chip_index()
    pairs = [(1 - y) * 2 + 1 - a, (1 - y) * 2 + a, y * 2 + 1 - a, y * 2 + a]
    loads = []
    for at, pair in enumerate(pairs):
        two = pl.ds(pair * 2, 2)
        loads.append(
            [
                pltpu.make_async_copy(hn_ref.at[two], first_ref.at[two], load_sems.at[at]),
                pltpu.make_async_copy(dy_ref.at[two], second_ref.at[two], load_sems.at[4 + at]),
            ]
        )
    enter = [
        pltpu.make_async_copy(src, dst, enter_sems.at[at])
        for at, (src, dst) in enumerate(
            (
                (w_in_hbm, w_in_ref), (w_dn_hbm, w_dn_ref), (wo_hbm, wo_ref), (qkv_hbm, qkv_ref), (s_hbm, s_ref),
                (p_hbm, p_ref), (o_hbm, o_ref), (wq_hbm, wq_ref),
            )
        )
    ]
    enter[0].start()
    for copies in loads:
        for copy in copies:
            copy.start()
    for copy in enter[1:]:
        copy.start()
    strip_local = pltpu.make_async_copy(strips_ref.at[me], strips_in.at[me], local_sems.at[0])
    strip_local.start()
    greet_all()
    chips = (7, 6, 5, 3, 4, 2, 1)
    to_chip = {mask: flipped(me, [axis for axis in BITS if mask & BITS[axis]]) for mask in chips}
    strips_sent = [
        push(strips_ref.at[to_chip[mask]], strips_in.at[me], strip_send.at[mask], strip_recv.at[mask], chip_at(mask))
        for mask in chips
    ]

    def hidden(pair):
        two = pl.ds(pair * 2, 2)
        both = dot(first_ref[two].reshape(2 * rows, D), w_in_ref[...])
        gate, up = both[:, :BLK], both[:, BLK:]
        dinner = dot_nt(second_ref[two].reshape(2 * rows, D), w_dn_ref[...])
        sig = jax.nn.sigmoid(gate)
        silu = gate * sig
        inner_ref[two] = (silu * up).astype(bf16).reshape(2, rows, BLK)
        dgate = (dinner * up * (sig * (1.0 + gate * (1.0 - sig)))).astype(bf16)
        dup = (dinner * silu).astype(bf16)
        dboth_ref[two, :, 0:BLK] = dgate.reshape(2, rows, BLK)
        dboth_ref[two, :, BLK:] = dup.reshape(2, rows, BLK)
        back = dot_nt(dgate, w_in_ref[:, 0:BLK]) + dot_nt(dup, w_in_ref[:, BLK:])
        parts_ref[two] = back.astype(bf16).reshape(2, rows, D)

    def wait_load(at):
        for copy in loads[at]:
            copy.wait()

    wait_load(0)
    enter[0].wait()
    enter[1].wait()
    hidden(pairs[0])
    scatter = Scatter(parts_ref, *scatter_args)
    scatter.start()
    wait_load(1)
    wait_load(2)

    def two_more(step, carry):
        hidden((1 - y) * 2 + a + step * ((2 * y - 1) * 2 + 1 - a - a))
        return carry

    lax.fori_loop(0, 2, two_more, 0)
    scatter.onward()
    wait_load(3)
    hidden(pairs[3])

    def down_grad(col, carry):
        cols = pl.ds(pl.multiple_of(col * BLK, BLK), BLK)
        made = dot_tn(inner_ref[...].reshape(seqs * rows, BLK), second_ref[:, :, cols].reshape(seqs * rows, BLK))
        gd_ref[:, :, :, :, cols] = made.astype(bf16).reshape(2, CHIPS, 2, BLK // 32, BLK)
        return carry

    lax.fori_loop(0, ROW_TILES, down_grad, 0)
    to_core = [push(gd_ref.at[1 - c], half_d, core_send.at[0], core_recv.at[0], across("c"))]

    def in_grad(row, carry):
        values = first_ref[:, :, pl.ds(pl.multiple_of(row * BLK, BLK), BLK)].reshape(seqs * rows, BLK)
        for which in range(2):
            cols = slice(which * BLK, (which + 1) * BLK)
            made = dot_tn(values, dboth_ref[:, :, cols].reshape(seqs * rows, BLK))
            gin_ref[row, :, :, :, :, cols] = made.astype(bf16).reshape(2, CHIPS, 2, BLK // 32, BLK)
        return carry

    def in_to_core(row):
        to_core.append(push(gin_ref.at[row, 1 - c], half_in.at[row], core_send.at[1 + row], core_recv.at[1 + row], across("c")))

    in_grad(0, 0)
    in_to_core(0)
    to_core[0].wait_recv()

    def core_down(chip, carry):
        half_d[chip] = (half_d[chip].astype(f32) + gd_ref[c, chip].astype(f32)).astype(bf16)
        return carry

    lax.fori_loop(0, CHIPS, core_down, 0)
    to_near = [push(half_d.at[:, 1 - g], near_d, near_send.at[0], near_recv.at[0], across("g"))]
    scatter.last()
    lax.fori_loop(1, ROW_TILES, in_grad, 0)
    in_to_core(1)
    in_to_core(2)
    xn_load = pltpu.make_async_copy(xn_ref, first_ref, load_sems.at[8])
    xn_load.start()

    def core_rows(row):
        to_core[1 + row].wait_recv()

        def core_chip(chip, carry):
            half_in[row, chip] = (half_in[row, chip].astype(f32) + gin_ref[row, c, chip].astype(f32)).astype(bf16)
            return carry

        lax.fori_loop(0, CHIPS, core_chip, 0)
        to_near.append(push(half_in.at[row, :, 1 - g], near_in.at[row], near_send.at[1 + row], near_recv.at[1 + row], across("g")))

    core_rows(0)
    core_rows(1)
    core_rows(2)
    half = rows // 2
    gain_sum = jnp.zeros((1, D), f32)
    for part in range(2):
        here = pl.ds(part * half, half)
        grad = scatter.finish(part)
        values = hmid_ref[here]
        scale = rms(values)
        unit = values * scale
        inside = grad * gains_ref[1:2, :]
        gain_sum += jnp.sum(grad * unit, axis=0, keepdims=True)
        dhmid = scale * (inside - unit * jnp.mean(inside * unit, axis=-1, keepdims=True)) + dy_own_ref[here].astype(f32)
        dhmid_ref[here] = dhmid
        dattn_ref[here] = dhmid.astype(bf16)
    gain_ffn_grad_ref[...] = gain_sum

    for copy in enter[2:]:
        copy.wait()

    def grad_copy(to):
        return pltpu.make_async_remote_copy(
            src_ref=sent_ref.at[to], dst_ref=grads_ref.at[me], send_sem=head_send.at[to], recv_sem=head_recv.at[me],
            device_id={"y": lax.div(to, 4), "a": lax.rem(lax.div(to, 2), 2), "b": lax.rem(to, 2)},
        )

    def send_grad(step, carry):
        to = lax.rem(me + step, seqs)
        sent_ref[to] = dot_nt(dattn_ref[...], wo_ref[to]).astype(bf16)

        @pl.when(step > 0)
        def _():
            grad_copy(to).start()

        return carry

    lax.fori_loop(0, seqs, send_grad, 0)
    grads_ref[me] = sent_ref[me]
    gather = SideGather(dattn_ref, second_ref, *side)
    gather.start()

    pad_ref[rows : rows + 8, :] = jnp.zeros((8, rows), f32)
    theta_sums[...] = jnp.zeros_like(theta_sums)
    mixer_ref[...] = jnp.zeros_like(mixer_ref)
    gain_grad_ref[...] = jnp.zeros_like(gain_grad_ref)
    query_at = lax.broadcasted_iota(jnp.int32, (rows, rows), 0)
    key_at = lax.broadcasted_iota(jnp.int32, (rows, rows), 1)
    key_float = key_at.astype(f32)
    blank = jnp.zeros((rows, HP - DH), f32)

    def grad_arrived(step, carry):
        source = lax.rem(me + step, seqs)
        pltpu.make_async_copy(sent_ref.at[source], grads_ref.at[source], head_recv.at[source]).wait()
        return carry

    lax.fori_loop(1, seqs, grad_arrived, 0)

    def one(seq, carry):
        keep = (key_at <= query_at) & (key_float < len_ref[seq, 0:1, :])
        weights = [p_ref[seq, 0], p_ref[seq, 1]]
        grad_mixed, made = [], [None] * 6
        grads = grads_ref[seq].astype(f32)
        for head in range(2):
            cols = slice(head * HP, (head + 1) * HP)
            out = o_ref[seq, :, cols]
            grad = jnp.concatenate([grads[:, head * DH : (head + 1) * DH], blank], axis=1)
            scale = lax.rsqrt(jnp.sum(out * out, axis=-1, keepdims=True) * (1.0 / DH) + eps_norm)
            unit = out * scale
            gain_grad_ref[:, cols] += jnp.sum(grad * unit, axis=0, keepdims=True)
            inner = grad * gain_ref[:, cols]
            grad_out = scale * (inner - unit * (jnp.sum(inner * unit, axis=-1, keepdims=True) * (1.0 / DH)))
            grad_out = grad_out.astype(bf16)
            value = qkv_ref[seq, :, (4 + head) * HP : (5 + head) * HP]
            mixed = (
                mix_ref[2 * head : 2 * head + 1, :] * weights[0] + mix_ref[2 * head + 1 : 2 * head + 2, :] * weights[1]
            ).astype(bf16)
            made[4 + head] = dot_tn(mixed, grad_out)
            back = dot_nt(grad_out, value)
            grad_mixed.append(back)
            for source in range(2):
                mixer_ref[2 * head + source : 2 * head + source + 1, :] += jnp.sum(
                    back * weights[source], axis=0, keepdims=True
                )
        for head in range(2):
            grad_weight = mix_ref[head : head + 1, :] * grad_mixed[0] + mix_ref[2 + head : 3 + head, :] * grad_mixed[1]
            weight = weights[head]
            grad_conv = weight * (grad_weight - jnp.sum(weight * grad_weight, axis=-1, keepdims=True))
            wide = shifted_up(pad_ref, grad_conv).astype(bf16)
            theta_sums[head] += dot_tn(s_ref[seq, head], wide)
            grad_scores = jnp.zeros((rows, rows), f32)
            for lag in range(CQ):
                grad_scores += dot_nt(
                    wide[:, lag * rows : (lag + 1) * rows], toep_ref[head, lag * rows : (lag + 1) * rows, :]
                )
            grad_scores = jnp.where(keep, grad_scores * (1.0 / math.sqrt(DH)), 0.0).astype(bf16)
            query = qkv_ref[seq, :, head * HP : (head + 1) * HP]
            key = qkv_ref[seq, :, (2 + head) * HP : (3 + head) * HP]
            made[head] = dot(grad_scores, key)
            made[2 + head] = dot_tn(grad_scores, query)
        dqkv_ref[seq] = jnp.concatenate([part[:, :DH] for part in made], axis=1).astype(bf16)
        return carry

    lax.fori_loop(0, 4, one, 0)
    gather.onward()
    lax.fori_loop(4, seqs, one, 0)
    scatter.drain()
    tiles_sent = []

    tap_at = query_at - key_at + CK // 2

    def taps(at, carry):
        lag = lax.rem(at, CQ)
        values = theta_sums[lax.div(at, CQ), :, pl.ds(pl.multiple_of(lag * rows, rows), rows)]
        for tap in range(CK):
            theta_ref[pl.ds(at * CK + tap, 1), :] = jnp.sum(
                jnp.where(tap_at == tap, values, 0.0), axis=0, keepdims=True
            )
        return carry

    xn_load.wait()
    all_rows = seqs * rows

    def qkv_grad(row, carry):
        cols = pl.ds(pl.multiple_of(row * BLK, BLK), BLK)
        made = dot_tn(first_ref[:, :, cols].reshape(all_rows, BLK), dqkv_ref[...].reshape(all_rows, 6 * DH))
        gq_ref[row] = made.astype(bf16).reshape(2, CHIPS, 2, BLK // 32, 6 * DH)
        return carry

    lax.fori_loop(0, ROW_TILES, qkv_grad, 0)
    to_core.append(push(gq_ref.at[:, 1 - c], core_q, core_send.at[4], core_recv.at[4], across("c")))

    def input_part(at, carry):
        two = pl.ds(at * 2, 2)
        made = dot_nt(dqkv_ref[two].reshape(2 * rows, 6 * DH), wq_ref[...])
        parts_ref[two] = made.astype(bf16).reshape(2, rows, D)
        return carry

    lax.fori_loop(0, seqs // 2, input_part, 0)
    scatter3 = Scatter(parts_ref, near3, in23, in33, *scatter_args[3:5], *scatter3_sems)
    scatter3.start()
    lax.fori_loop(0, 2 * CQ, taps, 0)
    to_core[4].wait_recv()

    def core_chip_q(chip, carry):
        for row in range(ROW_TILES):
            core_q[row, chip] = (core_q[row, chip].astype(f32) + gq_ref[row, c, chip].astype(f32)).astype(bf16)
        return carry

    lax.fori_loop(0, CHIPS, core_chip_q, 0)
    slot = g * CHIPS + me
    order = (15, 14, 13, 11, 12, 10, 9, 8, 7, 6, 5, 3, 4, 2, 1)
    for mask in order:
        to = flipped(me, [axis for axis in BITS if mask & BITS[axis]])
        tiles_sent.append(
            push(core_q.at[:, to, other_bit("g", mask & 8)], in_q.at[slot], q_send.at[mask], q_recv.at[mask], wide_at(mask))
        )
    in_q[slot] = core_q[:, me, g]
    gather.last()
    to_near[0].wait_recv()

    def near_down(chip, carry):
        half_d[chip, g] = (half_d[chip, g].astype(f32) + near_d[chip].astype(f32)).astype(bf16)
        return carry

    lax.fori_loop(0, CHIPS, near_down, 0)
    base = 4 * ROW_TILES**2

    def spread(ref, cols, tile, which):
        for mask in chips:
            at = which * CHIPS + mask
            tiles_sent.append(
                push(ref.at[to_chip[mask], g, :, cols], tiles_ref.at[tile], gu_send.at[at], gu_recv.at[at], chip_at(mask))
            )
        tiles_ref[tile] = ref[me, g, :, cols]

    for col in range(ROW_TILES):
        spread(half_d, pl.ds(col * BLK, BLK), base + 2 * ROW_TILES * FF_TILES + me * ROW_TILES + col, 6 + col)
    scatter3.onward()
    gather.finish()
    strip_local.wait()
    for copy in strips_sent:
        copy.wait_recv()

    def out_grad(col, carry):
        cols = pl.ds(pl.multiple_of(col * BLK, BLK), BLK)
        made = dot_tn(strips_in[...].reshape(all_rows, 2 * DH), second_ref[:, :, cols].reshape(all_rows, BLK))
        go_ref[:, :, :, :, cols] = made.astype(bf16).reshape(ROW_TILES, 2, 2, BLK // 32, BLK)
        return carry

    lax.fori_loop(0, ROW_TILES, out_grad, 0)
    to_core.append(push(go_ref.at[:, 1 - c], core_o, core_send.at[5], core_recv.at[5], across("c")))

    def near_rows(row):
        to_near[1 + row].wait_recv()

        def near_chip(chip, carry):
            half_in[row, chip, g] = (half_in[row, chip, g].astype(f32) + near_in[row, chip].astype(f32)).astype(bf16)
            return carry

        lax.fori_loop(0, CHIPS, near_chip, 0)
        for which in range(2):
            spread(
                half_in.at[row], pl.ds(which * BLK, BLK), base + (which * ROW_TILES + row) * FF_TILES + me, 2 * row + which
            )

    near_rows(0)
    to_core[5].wait_recv()
    core_o[...] = (core_o[...].astype(f32) + go_ref[:, c].astype(f32)).astype(bf16)
    to_near.append(push(core_o.at[:, 1 - g], in_o, near_send.at[4], near_recv.at[4], across("g")))
    scatter3.last()
    near_rows(1)
    near_rows(2)
    dxn_ref[0:half] = scatter3.finish(0)
    dxn_ref[half:] = scatter3.finish(1)

    def three_tiles(at, values):
        for col in range(ROW_TILES):
            tiles_ref[at + col] = values[:, col * BLK : (col + 1) * BLK].astype(bf16)

    to_near[4].wait_recv()
    for row in range(ROW_TILES):
        three_tiles(3 * ROW_TILES**2 + row * ROW_TILES, in_o[row].astype(f32) + core_o[row, g].astype(f32))
    for copy in tiles_sent:
        copy.wait_recv()
    for row in range(ROW_TILES):
        sums = [in_q[chip, row].astype(f32) + in_q[CHIPS + chip, row].astype(f32) for chip in range(CHIPS)]
        for which in range(3):
            three_tiles(
                which * ROW_TILES**2 + row * ROW_TILES,
                jnp.concatenate([part[:, which * 2 * DH : (which + 1) * 2 * DH] for part in sums], axis=1),
            )
    tiles_ref[tiles_ref.shape[0] - 1] = jnp.zeros(tiles_ref.shape[1:], bf16)

    def grad_left(step, carry):
        grad_copy(lax.rem(me + step, seqs)).wait_send()
        return carry

    lax.fori_loop(1, seqs, grad_left, 0)
    gather.drain()
    scatter3.drain()
    for copy in strips_sent + to_core + to_near + tiles_sent:
        copy.wait_send()


def chip_at(mask):
    return {axis: 1 - lax.axis_index(axis) for axis in BITS if mask & BITS[axis]}


def wide_at(mask):
    at = chip_at(mask & 7)
    if mask & 8:
        at["g"] = 1 - lax.axis_index("g")
    return at


def run_middle(
    lengths, mix, hn, dy, xn, w_in, w_dn, w_qkv, dy_own, hmid, gain_ffn, w_o, qkv, toep, gain, scores, weights, outs, strips
):
    seqs, rows, _ = hn.shape
    dma = pltpu.SemaphoreType.DMA
    part = BLK // 32
    tiles = 4 * ROW_TILES**2 + 3 * ROW_TILES * FF_TILES
    shapes = [
        ((seqs, rows, BLK), bf16), ((rows, D), f32), ((rows, D), f32), ((1, D), f32), ((2 * CQ * CK, rows), f32),
        ((8, rows), f32), ((1, 2 * HP), f32), ((tiles + 1, part, BLK), bf16),
    ]

    def low(*dims):
        return pltpu.VMEM(dims, bf16)

    every, heads = low(CHIPS, rows, D), low(CHIPS, rows, 2 * DH)
    return pl.pallas_call(
        middle_body,
        in_specs=[VMEM] * 2 + [ANYS] * 6 + [VMEM] * 3 + [ANYS] * 2 + [VMEM] * 2 + [ANYS] * 3 + [VMEM],
        out_specs=[VMEM] * len(shapes),
        out_shape=[jax.ShapeDtypeStruct(*shape) for shape in shapes],
        scratch_shapes=[pltpu.VMEM(a.shape, a.dtype) for a in (w_in, w_dn, w_qkv, w_o, qkv, scores, weights, outs)] + [
            dma((8,)),
            pltpu.VMEM((2, rows, CQ * rows), f32), pltpu.VMEM((rows + 8, rows), f32), every, every, low(seqs, rows, 2 * BLK), every, low(rows, D), heads, heads, heads,
            low(ROW_TILES, 2, CHIPS, 2, part, 2 * BLK), low(2, CHIPS, 2, part, D),
            low(ROW_TILES, CHIPS, 2, part, 2 * BLK), low(CHIPS, 2, part, D),
            low(ROW_TILES, CHIPS, part, 2 * BLK), low(CHIPS, part, D),
            low(seqs, rows, 6 * DH), low(ROW_TILES, 2, CHIPS, 2, part, 6 * DH), low(ROW_TILES, 2, 2, part, D),
            low(ROW_TILES, CHIPS, 2, part, 6 * DH), low(ROW_TILES, 2, part, D),
            low(2 * CHIPS, ROW_TILES, part, 6 * DH), low(ROW_TILES, part, D),
            low(3, rows, D), low(rows, D), low(3, rows, D), dma((1,)), dma((9,)),
        ] + [dma((8,))] * 4 + [dma((6,))] * 2 + [dma((5,))] * 2 + [dma((9 * CHIPS,))] * 2 + [dma((16,))] * 2
        + scatter_scratch(rows, D) + [dma((3,))] * 2 + [dma((3, 2))] * 4 + side_sems(),
        name="middle",
        compiler_params=pltpu.CompilerParams(collective_id=3, has_side_effects=True, vmem_limit_bytes=63 * 2**20),
    )(
        lengths, mix, hn, dy, xn, w_in, w_dn, w_qkv, dy_own, hmid, gain_ffn, w_o,
        qkv, toep, gain, scores, weights, outs, strips,
    )


def to_slots_body(
    pick_ref, tiles_ref, vec_ref, inner_hbm, w_dn_hbm, hmid_hbm, out_ref, vecs_ref, layer_ref,
    inner_ref, w_dn_ref, hmid_ref, enter_sems, slots_ref, parts_ref, local_sems, send, recv, vec_send, vec_recv, *scatter_args,
):
    devices = lax.axis_size(ALL)
    own_slots, side = out_ref.shape[:2]
    part = slots_ref.shape[1]
    enter = [
        pltpu.make_async_copy(src, dst, enter_sems.at[at])
        for at, (src, dst) in enumerate(((inner_hbm, inner_ref), (w_dn_hbm, w_dn_ref), (hmid_hbm, hmid_ref)))
    ]
    for copy in enter:
        copy.start()

    def fill(at, carry):
        slots_ref[at] = tiles_ref[pick_ref[at]]
        return carry

    lax.fori_loop(0, slots_ref.shape[0], fill, 0)
    me = device_index()
    place = (lax.axis_index("c") * CHIPS + chip_index()) * 2 + lax.axis_index("g")
    rows = pl.ds(pl.multiple_of(place * part, part), part)
    local = [pltpu.make_async_copy(vec_ref.at[me], vecs_ref.at[me], local_sems.at[0])]
    for slot in range(own_slots):
        local.append(
            pltpu.make_async_copy(
                slots_ref.at[me * own_slots + slot], out_ref.at[slot, rows], local_sems.at[1 + slot]
            )
        )
    for copy in local:
        copy.start()
    greet_all()

    def push_all(step, carry):
        to = lax.rem(me + step, devices)
        pltpu.make_async_remote_copy(
            src_ref=vec_ref.at[to], dst_ref=vecs_ref.at[me], send_sem=vec_send, recv_sem=vec_recv, device_id=device_at(to)
        ).start()
        pltpu.make_async_remote_copy(
            src_ref=slots_ref.at[pl.ds(to * own_slots, own_slots)], dst_ref=out_ref.at[:, rows],
            send_sem=send, recv_sem=recv, device_id=device_at(to),
        ).start()
        return carry

    lax.fori_loop(1, devices, push_all, 0)

    seqs, length = inner_ref.shape[:2]
    for copy in enter:
        copy.wait()

    def outputs(at, carry):
        two = pl.ds(at * 2, 2)
        made = dot(inner_ref[two].reshape(2 * length, BLK), w_dn_ref[...])
        parts_ref[two] = made.astype(bf16).reshape(2, length, D)
        return carry

    lax.fori_loop(0, seqs // 2, outputs, 0)
    scatter = SideScatter(parts_ref, *scatter_args)
    scatter.start()
    scatter.onward()
    scatter.last()
    layer_ref[...] = (hmid_ref[...] + scatter.finish()).astype(bf16)
    scatter.drain()
    others = vecs_ref.at[pl.ds(0, devices - 1)]
    pltpu.make_async_copy(others, others, vec_recv).wait()
    pltpu.make_async_copy(others, others, vec_send).wait()
    others = out_ref.at[:, pl.ds(0, side - part)]
    pltpu.make_async_copy(others, others, recv).wait()
    pltpu.make_async_copy(others, others, send).wait()
    for copy in local:
        copy.wait()


def to_slots(pick, tiles, vecs, inner, w_dn, hmid, own_slots):
    rows = hmid.shape[0]
    dma = pltpu.SemaphoreType.DMA
    return pl.pallas_call(
        to_slots_body,
        in_specs=[SMEM, VMEM] + [ANYS] * 4,
        out_specs=[ANYS] * 2 + [VMEM],
        out_shape=[
            jax.ShapeDtypeStruct((own_slots, BLK, BLK), bf16), jax.ShapeDtypeStruct(vecs.shape, vecs.dtype),
            jax.ShapeDtypeStruct(hmid.shape, bf16),
        ],
        scratch_shapes=[pltpu.VMEM(a.shape, a.dtype) for a in (inner, w_dn, hmid)] + [
            dma((3,)), pltpu.VMEM((pick.shape[0],) + tiles.shape[1:], bf16), pltpu.VMEM((CHIPS, rows, D), bf16), dma((1 + own_slots,)),
        ] + [dma] * 4 + side_scatter_scratch(rows, D),
        name="to_slots",
        compiler_params=pltpu.CompilerParams(collective_id=6, has_side_effects=True, vmem_limit_bytes=60 * 2**20),
    )(pick, tiles, vecs, inner, w_dn, hmid)


def update_body(grad_ref, left_ref, right_ref, master_ref, first_ref, second_ref, first_out, second_out, master_out, copy_out):
    left, right = left_ref[0].astype(bf16), right_ref[0].astype(bf16)
    rotated = dot(dot_tn(left, grad_ref[0]).astype(bf16), right)
    first = beta_first * first_ref[0] + (1.0 - beta_first) * rotated
    second = beta_second * second_ref[0] + (1.0 - beta_second) * rotated * rotated
    first_out[0] = first
    second_out[0] = second
    direction = (first / (jnp.sqrt(second) + eps_adam)).astype(bf16)
    turned = dot_nt(dot(left, direction).astype(bf16), right)
    master = master_ref[0]
    master = master - rate_block * (turned + decay_block * master)
    master_out[0] = master
    copy_out[0] = master.astype(bf16)


def update(grad, left, right, master, first, second):
    spec = pl.BlockSpec((1, BLK, BLK), lambda slot: (slot, 0, 0))
    return pl.pallas_call(
        update_body,
        grid=(grad.shape[0],),
        in_specs=[spec] * 6,
        out_specs=[spec] * 4,
        out_shape=[jax.ShapeDtypeStruct(grad.shape, kind) for kind in (f32, f32, f32, bf16)],
        name="update",
        compiler_params=pltpu.CompilerParams(vmem_limit_bytes=60 * 2**20),
        cost_estimate=pl.CostEstimate(flops=43 * 10**8, bytes_accessed=36 * 2**20, transcendentals=10**6),
    )(grad, left, right, master, first, second)


def body_fast(
    layer_input, lengths, cotangent, w_query, w_key, w_value, w_out, w_gate, w_up, w_down, vec_copy, owners,
    basis_left, basis_right, block_master, block_first, block_second, vec_master, vec_first, vec_second,
):
    chip = chip_index()
    seq_len = layer_input.shape[0]
    own_vec = vec_copy.shape[0]
    devices, fs_size, reps = lax.axis_size(ALL), lax.axis_size(FS), lax.axis_size("y")

    fs_index = ((lax.axis_index("g") * 2 + lax.axis_index("a")) * 2 + lax.axis_index("b")) * 2 + lax.axis_index("c")
    first_rows = vector_rows(own_vec, fs_size)
    flat = lax.dynamic_update_slice_in_dim(jnp.zeros((fs_size * own_vec,), f32), vec_copy.astype(f32), fs_index * own_vec, 0)
    first = sum(
        (first_rows[at] - first_rows[at - 1]) * (fs_index >= at).astype(jnp.int32)
        for at in range(1, fs_size) if first_rows[at] != first_rows[at - 1]
    )
    vec = lax.dynamic_slice_in_dim(rows_of_vector(flat), first, SHARD_ROWS, 0)

    (
        dy, group_lengths, mix, gains, toep, gain_pair, strips, hmid, xn, qkv, scores, weights, outs, w_qkv, w_out_all,
        hn_rows, w_in, w_dn, dy_rows,
    ) = run_front(
        first_rows, lengths, vec, layer_input, w_query, w_key, w_value, cotangent, w_out, w_gate, w_up, w_down
    )
    gain_attn = gains[0]
    w_qkv = w_qkv.reshape(D, 6 * DH)
    w_in, w_dn = w_in.reshape(D, 2 * BLK), w_dn.reshape(BLK, D)
    input_float = layer_input.astype(f32)
    input_scale = rms(input_float)

    own_slots = basis_left.shape[0]
    matches = jnp.arange(own_slots * devices)[:, None] == owners[None, :]
    tile_count = owners.shape[0]
    pick = jnp.min(jnp.where(matches, jnp.arange(tile_count, dtype=jnp.int32)[None, :], tile_count), axis=1)
    inner, dhmid, dxn, grad_gain_ffn, theta_sums, mixer_sums, gain_sums, tiles = run_middle(
        group_lengths, mix, hn_rows, dy_rows, xn, w_in, w_dn, w_qkv, dy, hmid, gains,
        w_out_all.reshape(CHIPS, 2 * DH, D), qkv, toep, gain_pair, scores, weights, outs, strips,
    )
    dinput, grad_gain_attn = norm_backward(input_float, input_scale, gain_attn, dxn)
    input_grad = dinput + dhmid

    grad_theta = jnp.sum(theta_sums, axis=1)
    grad_mixer = jnp.sum(mixer_sums[:4], axis=1)
    vector_grad = jnp.concatenate(
        [
            grad_gain_attn,
            lax.dynamic_update_slice_in_dim(
                jnp.zeros((D,), f32), gain_sums.reshape(2, HP)[:, :DH].reshape(-1), chip * 2 * DH, 0
            ),
            grad_gain_ffn.reshape(-1),
            lax.dynamic_update_slice_in_dim(
                jnp.zeros((H * CQ * CK,), f32), grad_theta.reshape(-1), chip * 2 * CQ * CK, 0
            ),
            lax.dynamic_update_slice_in_dim(jnp.zeros((2 * H,), f32), grad_mixer, chip * 4, 0),
        ]
    )
    pieces = jnp.pad(vector_grad.reshape(fs_size, 1, own_vec), ((0, 0), (0, 0), (0, 1024 - own_vec)))
    pieces = jnp.broadcast_to(pieces, (fs_size, reps, 1024)).reshape(devices, 8, 128)

    own_grad, pieces, layer_output = to_slots(
        pick, tiles, pieces, inner, w_dn, hmid, own_slots
    )
    vector_total = jnp.sum(pieces, axis=0).reshape(1024)[:own_vec]
    first_new, second_new, master_new, copy_new = update(
        own_grad, basis_left, basis_right, block_master, block_first, block_second
    )
    vec_first_new = beta_first * vec_first + (1.0 - beta_first) * vector_total
    vec_second_new = beta_second * vec_second + (1.0 - beta_second) * vector_total * vector_total
    vec_master_new = vec_master - rate_vector * vec_first_new / (jnp.sqrt(vec_second_new) + eps_adam)
    return (
        layer_output, input_grad, first_new, second_new, master_new, copy_new,
        vec_first_new, vec_second_new, vec_master_new, vec_master_new.astype(bf16),
    )


def solution(mesh):
    fsdp, rep = mesh.shape["fsdp"], mesh.shape["rep"]
    fine = Mesh(mesh.devices.reshape(fsdp // 8, 2, 2, 2, rep), ALL)
    rows, both = P(ALL, None), P(ALL, None, None)
    weight, vec = P(FS, None), P(FS)
    return jax.shard_map(
        body_fast if (fsdp, rep) == (16, 2) else body_any,
        mesh=fine,
        in_specs=(rows, P(ALL), rows) + (weight,) * 7 + (vec, P()) + (both,) * 5 + (vec,) * 3,
        out_specs=(rows, rows) + (both,) * 4 + (vec,) * 4,
        check_vma=False,
    )
```

```python
import functools
import math

import jax
import jax.numpy as jnp
import numpy as np
from jax import lax
from jax.experimental import pallas as pl
from jax.experimental.pallas import tpu as pltpu
from jax.sharding import Mesh
from jax.sharding import PartitionSpec as P

H = 16
DH = 96
HP = 128
D = H * DH
FF = 4096
CQ = 6
CK = 11
BLK = 512
CHIPS = 8
ROW_TILES = D // BLK
FF_TILES = FF // BLK

eps_norm = 1e-05
eps_adam = 1e-08
rate_block = 0.02
rate_vector = 0.3
decay_block = 0.1
beta_first = 0.5
beta_second = 0.5

FS = ("g", "a", "b", "c")
CHIP = ("y", "a", "b")
ALL = ("g", "a", "b", "c", "y")
bf16 = jnp.bfloat16
f32 = jnp.float32


def dot(left, right):
    return jnp.dot(left, right, preferred_element_type=f32)


def dot_nt(left, right):
    return lax.dot_general(left, right, (((1,), (1,)), ((), ())), preferred_element_type=f32)


def dot_tn(left, right):
    return lax.dot_general(left, right, (((0,), (0,)), ((), ())), preferred_element_type=f32)


def rms(values):
    return lax.rsqrt(jnp.mean(values * values, axis=-1, keepdims=True) + eps_norm)


def norm_backward(values, scale, gain, grad):
    unit = values * scale
    inner = grad * gain
    grad_values = scale * (inner - unit * jnp.mean(inner * unit, axis=-1, keepdims=True))
    return grad_values, jnp.sum(grad * unit, axis=0)


def shifted_down(pad_ref, values):
    rows = values.shape[0]
    pad_ref[8 : 8 + rows, :] = values
    return jnp.concatenate(
        [values] + [pad_ref[8 - lag : 8 - lag + rows, :] for lag in range(1, CQ)], axis=1
    )


def shifted_up(pad_ref, values):
    rows = values.shape[0]
    pad_ref[0:rows, :] = values
    return jnp.concatenate(
        [values] + [pad_ref[lag : lag + rows, :] for lag in range(1, CQ)], axis=1
    )


def attention_forward(len_ref, mix_ref, qkv_ref, toep_ref, gain_ref, heads_ref, s_ref, p_ref, o_ref, pad_ref):
    rows = qkv_ref.shape[1]
    length = len_ref[pl.program_id(0)]
    query_at = lax.broadcasted_iota(jnp.int32, (rows, rows), 0)
    key_at = lax.broadcasted_iota(jnp.int32, (rows, rows), 1)
    keep = (key_at <= query_at) & (key_at < length)
    pad_ref[0:8, :] = jnp.zeros((8, rows), f32)
    weights = []
    for head in range(2):
        query = qkv_ref[0, :, head * HP : (head + 1) * HP]
        key = qkv_ref[0, :, (2 + head) * HP : (3 + head) * HP]
        scores = jnp.where(keep, dot_nt(query, key) * (1.0 / math.sqrt(DH)), 0.0)
        s_ref[0, head] = scores.astype(bf16)
        wide = shifted_down(pad_ref, scores)
        high = wide.astype(bf16)
        low = (wide - high.astype(f32)).astype(bf16)
        conv = dot(high, toep_ref[head]) + dot(low, toep_ref[head])
        logits = jnp.where(keep, conv, -1e30)
        weight = jnp.exp(logits - jnp.max(logits, axis=-1, keepdims=True))
        weight = weight / jnp.sum(weight, axis=-1, keepdims=True)
        p_ref[0, head] = weight
        weights.append(weight)
    for head in range(2):
        mixed = mix_ref[2 * head] * weights[0] + mix_ref[2 * head + 1] * weights[1]
        value = qkv_ref[0, :, (4 + head) * HP : (5 + head) * HP]
        out = dot(mixed.astype(bf16), value)
        o_ref[0, :, head * HP : (head + 1) * HP] = out
        scale = lax.rsqrt(jnp.sum(out * out, axis=-1, keepdims=True) * (1.0 / DH) + eps_norm)
        heads_ref[0, :, head * HP : (head + 1) * HP] = (
            out * scale * gain_ref[:, head * HP : (head + 1) * HP]
        ).astype(bf16)


def attention_backward(
    len_ref, mix_ref, qkv_ref, toep_ref, gain_ref, s_ref, p_ref, o_ref, grad_ref,
    dqkv_ref, theta_ref, mixer_ref, gain_grad_ref, pad_ref,
):
    rows = qkv_ref.shape[1]
    length = len_ref[pl.program_id(0)]
    query_at = lax.broadcasted_iota(jnp.int32, (rows, rows), 0)
    key_at = lax.broadcasted_iota(jnp.int32, (rows, rows), 1)
    keep = (key_at <= query_at) & (key_at < length)
    pad_ref[rows : rows + 8, :] = jnp.zeros((8, rows), f32)

    @pl.when(pl.program_id(0) == 0)
    def _():
        theta_ref[...] = jnp.zeros_like(theta_ref)
        mixer_ref[...] = jnp.zeros_like(mixer_ref)
        gain_grad_ref[...] = jnp.zeros_like(gain_grad_ref)

    weights = [p_ref[0, 0], p_ref[0, 1]]
    grad_mixed = []
    for head in range(2):
        cols = slice(head * HP, (head + 1) * HP)
        out = o_ref[0, :, cols]
        grad = grad_ref[0, :, cols].astype(f32)
        scale = lax.rsqrt(jnp.sum(out * out, axis=-1, keepdims=True) * (1.0 / DH) + eps_norm)
        unit = out * scale
        gain_grad_ref[:, cols] += jnp.sum(grad * unit, axis=0, keepdims=True)
        inner = grad * gain_ref[:, cols]
        grad_out = scale * (inner - unit * (jnp.sum(inner * unit, axis=-1, keepdims=True) * (1.0 / DH)))
        grad_out = grad_out.astype(bf16)
        value = qkv_ref[0, :, (4 + head) * HP : (5 + head) * HP]
        mixed = (mix_ref[2 * head] * weights[0] + mix_ref[2 * head + 1] * weights[1]).astype(bf16)
        dqkv_ref[0, :, (4 + head) * HP : (5 + head) * HP] = dot_tn(mixed, grad_out).astype(bf16)
        back = dot_nt(grad_out, value)
        grad_mixed.append(back)
        for source in range(2):
            mixer_ref[2 * head + source : 2 * head + source + 1, :] += jnp.sum(
                back * weights[source], axis=0, keepdims=True
            )
    for head in range(2):
        grad_weight = mix_ref[head] * grad_mixed[0] + mix_ref[2 + head] * grad_mixed[1]
        weight = weights[head]
        grad_conv = weight * (grad_weight - jnp.sum(weight * grad_weight, axis=-1, keepdims=True))
        wide = shifted_up(pad_ref, grad_conv).astype(bf16)
        theta_ref[head] += dot_tn(s_ref[0, head], wide)
        grad_scores = jnp.zeros((rows, rows), f32)
        for lag in range(CQ):
            grad_scores += dot_nt(
                wide[:, lag * rows : (lag + 1) * rows], toep_ref[head, lag * rows : (lag + 1) * rows, :]
            )
        grad_scores = jnp.where(keep, grad_scores * (1.0 / math.sqrt(DH)), 0.0).astype(bf16)
        query = qkv_ref[0, :, head * HP : (head + 1) * HP]
        key = qkv_ref[0, :, (2 + head) * HP : (3 + head) * HP]
        dqkv_ref[0, :, head * HP : (head + 1) * HP] = dot(grad_scores, key).astype(bf16)
        dqkv_ref[0, :, (2 + head) * HP : (3 + head) * HP] = dot_tn(grad_scores, query).astype(bf16)


SMEM = pl.BlockSpec(memory_space=pltpu.SMEM)


def seq_spec(*dims):
    return pl.BlockSpec((1,) + dims, lambda s: (s,) + (0,) * len(dims))


def whole_spec(*dims):
    return pl.BlockSpec(dims, lambda s: (0,) * len(dims))


def run_forward(lengths, mix, qkv, toep, gain):
    seqs, rows, _ = qkv.shape
    return pl.pallas_call(
        attention_forward,
        grid=(seqs,),
        in_specs=[SMEM, SMEM, seq_spec(rows, 6 * HP), whole_spec(2, CQ * rows, rows), whole_spec(1, 2 * HP)],
        out_specs=[seq_spec(rows, 2 * HP), seq_spec(2, rows, rows), seq_spec(2, rows, rows), seq_spec(rows, 2 * HP)],
        out_shape=[
            jax.ShapeDtypeStruct((seqs, rows, 2 * HP), bf16),
            jax.ShapeDtypeStruct((seqs, 2, rows, rows), bf16),
            jax.ShapeDtypeStruct((seqs, 2, rows, rows), f32),
            jax.ShapeDtypeStruct((seqs, rows, 2 * HP), f32),
        ],
        scratch_shapes=[pltpu.VMEM((rows + 8, rows), f32)],
        name="attention_forward",
        compiler_params=pltpu.CompilerParams(vmem_limit_bytes=24 * 2**20),
        cost_estimate=pl.CostEstimate(flops=2 * 10**9, bytes_accessed=8 * 2**20, transcendentals=10**5),
    )(lengths, mix, qkv, toep, gain)


def run_backward(lengths, mix, qkv, toep, gain, scores, weights, outs, grads):
    seqs, rows, _ = qkv.shape
    return pl.pallas_call(
        attention_backward,
        grid=(seqs,),
        in_specs=[
            SMEM, SMEM, seq_spec(rows, 6 * HP), whole_spec(2, CQ * rows, rows), whole_spec(1, 2 * HP),
            seq_spec(2, rows, rows), seq_spec(2, rows, rows), seq_spec(rows, 2 * HP), seq_spec(rows, 2 * HP),
        ],
        out_specs=[seq_spec(rows, 6 * HP), whole_spec(2, rows, CQ * rows), whole_spec(8, rows), whole_spec(1, 2 * HP)],
        out_shape=[
            jax.ShapeDtypeStruct((seqs, rows, 6 * HP), bf16),
            jax.ShapeDtypeStruct((2, rows, CQ * rows), f32),
            jax.ShapeDtypeStruct((8, rows), f32),
            jax.ShapeDtypeStruct((1, 2 * HP), f32),
        ],
        scratch_shapes=[pltpu.VMEM((rows + 8, rows), f32)],
        name="attention_backward",
        compiler_params=pltpu.CompilerParams(vmem_limit_bytes=24 * 2**20),
        cost_estimate=pl.CostEstimate(flops=4 * 10**9, bytes_accessed=12 * 2**20, transcendentals=10**5),
    )(lengths, mix, qkv, toep, gain, scores, weights, outs, grads)


BITS = {"y": 4, "a": 2, "b": 1}
HOPS = (("y", "b", "a"), ("a", "y", "b"), ("b", "a", "y"))
THIRDS = ((0, 48), (48, 48), (96, 32))
ANYS = pl.BlockSpec(memory_space=pl.ANY)


def chip_index():
    return (lax.axis_index("y") * 2 + lax.axis_index("a")) * 2 + lax.axis_index("b")


def flipped(chip, axes):
    for axis in axes:
        chip = chip + BITS[axis] * (1 - 2 * lax.axis_index(axis))
    return chip


def across(axis):
    return {axis: 1 - lax.axis_index(axis)}


def device_index():
    index = lax.axis_index("g")
    for axis in ("a", "b", "c", "y"):
        index = index * lax.axis_size(axis) + lax.axis_index(axis)
    return index


def device_at(index):
    at = {}
    for axis in ("y", "c", "b", "a", "g"):
        at[axis] = lax.rem(index, lax.axis_size(axis))
        index = lax.div(index, lax.axis_size(axis))
    return at


def greet_all():
    devices = lax.axis_size(ALL)
    me = device_index()
    barrier = pltpu.get_barrier_semaphore()

    def greet(step, carry):
        pl.semaphore_signal(barrier, inc=1, device_id=device_at(lax.rem(me + step, devices)))
        return carry

    lax.fori_loop(1, devices, greet, 0)
    pl.semaphore_wait(barrier, devices - 1)


def greet_neighbours():
    barrier = pltpu.get_barrier_semaphore()
    for axis in BITS:
        pl.semaphore_signal(barrier, inc=1, device_id=across(axis))
    pl.semaphore_wait(barrier, 3)


def remote(src, dst, send, recv, axis):
    return pltpu.make_async_remote_copy(src_ref=src, dst_ref=dst, send_sem=send, recv_sem=recv, device_id=across(axis))


def gather_body(x_ref, out_ref, *sems):
    greet_neighbours()
    gather_hops(x_ref, out_ref, *sems)


def gather_first_body(x_ref, vec_ref, out_ref, vecs_ref, vec_send, vec_recv, vec_local, *sems):
    devices = lax.axis_size(ALL)
    me = device_index()
    local = pltpu.make_async_copy(vec_ref, vecs_ref.at[me], vec_local)
    local.start()
    greet_all()

    def push(step, carry):
        pltpu.make_async_remote_copy(
            src_ref=vec_ref, dst_ref=vecs_ref.at[me], send_sem=vec_send, recv_sem=vec_recv,
            device_id=device_at(lax.rem(me + step, devices)),
        ).start()
        return carry

    lax.fori_loop(1, devices, push, 0)
    gather_hops(x_ref, out_ref, *sems)
    others = vecs_ref.at[pl.ds(0, devices - 1)]
    pltpu.make_async_copy(others, others, vec_recv).wait()
    pltpu.make_async_copy(others, others, vec_send).wait()
    local.wait()


def gather_hops(x_ref, out_ref, local_sem, send1, recv1, send2, recv2, send3, recv3):
    me = chip_index()
    rows = x_ref.shape[0]
    half = rows // 2
    local = pltpu.make_async_copy(x_ref, out_ref.at[me], local_sem)
    local.start()
    first = []
    for part in range(2):
        here = pl.ds(part * half, half)
        for at, (axis, _, _) in enumerate(HOPS):
            copy = remote(x_ref.at[here], out_ref.at[me, here], send1.at[at, part], recv1.at[at, part], axis)
            copy.start()
            first.append(copy)
    second = []
    for part in range(2):
        here = pl.ds(part * half, half)
        for at, (axis, onward, _) in enumerate(HOPS):
            first[part * 3 + at].wait_recv()
            block = out_ref.at[flipped(me, (axis,)), here]
            copy = remote(block, block, send2.at[at, part], recv2.at[at, part], onward)
            copy.start()
            second.append(copy)
    third = []
    for at, (axis, onward, last) in enumerate(HOPS):
        begin, count = THIRDS[at]
        block = flipped(me, (axis, onward))
        for part in range(2):
            if part * half < begin + count and begin < (part + 1) * half:
                second[part * 3 + at].wait_recv()
        piece = out_ref.at[block, pl.ds(begin, count)]
        copy = remote(piece, piece, send3.at[at], recv3.at[at], last)
        copy.start()
        third.append(copy)
    for at in range(3):
        begin, count = THIRDS[at]
        for part in range(2):
            if not (part * half < begin + count and begin < (part + 1) * half):
                second[part * 3 + at].wait_recv()
    for copy in third:
        copy.wait_recv()
    for copy in first + second + third:
        copy.wait_send()
    local.wait()


def hop_sems():
    dma = pltpu.SemaphoreType.DMA
    return [dma] + [dma((3, 2))] * 4 + [dma((3,))] * 2


def gather_first(rows, vec, collective_id):
    count, width = rows.shape
    return pl.pallas_call(
        gather_first_body,
        in_specs=[ANYS, ANYS],
        out_specs=[ANYS, ANYS],
        out_shape=[
            jax.ShapeDtypeStruct((CHIPS, count, width), rows.dtype),
            jax.ShapeDtypeStruct((lax.axis_size(ALL),) + vec.shape, vec.dtype),
        ],
        scratch_shapes=[pltpu.SemaphoreType.DMA] * 3 + hop_sems(),
        name="gather_first",
        compiler_params=pltpu.CompilerParams(collective_id=collective_id, has_side_effects=True),
    )(rows, vec)


def gather_chips(rows, collective_id):
    count, width = rows.shape
    return pl.pallas_call(
        gather_body,
        in_specs=[ANYS],
        out_specs=ANYS,
        out_shape=jax.ShapeDtypeStruct((CHIPS, count, width), rows.dtype),
        scratch_shapes=hop_sems(),
        name="gather_chips",
        compiler_params=pltpu.CompilerParams(collective_id=collective_id, has_side_effects=True),
    )(rows)


def scatter_body(
    parts_ref, out_ref, near_ref, in2_ref, in3_ref, acc2_ref, acc3_ref, send1, recv1, send2, recv2, send3, recv3
):
    me = chip_index()
    greet_neighbours()
    opposite = flipped(me, ("y", "a", "b"))
    first = []
    for at, (axis, onward, last) in enumerate(HOPS):
        begin, count = THIRDS[at]
        copy = remote(parts_ref.at[opposite, pl.ds(begin, count)], in2_ref.at[pl.ds(begin, count)], send1.at[at], recv1.at[at], last)
        copy.start()
        first.append(copy)
    second = []
    rows = parts_ref.shape[1]
    half = rows // 2
    for part in range(2):
        here = pl.ds(part * half, half)
        for at, (axis, onward, last) in enumerate(HOPS):
            dest = flipped(me, (axis, onward))
            begin, count = THIRDS[at]
            if part == 0:
                first[at].wait_recv()
                acc2_ref[at] = parts_ref[dest]
                piece = pl.ds(begin, count)
                acc2_ref[at, piece] = (parts_ref[dest, piece].astype(f32) + in2_ref[piece].astype(f32)).astype(bf16)
            copy = remote(acc2_ref.at[at, here], in3_ref.at[at, here], send2.at[at, part], recv2.at[at, part], onward)
            copy.start()
            second.append(copy)
    third = []
    for part in range(2):
        here = pl.ds(part * half, half)
        for at, (axis, onward, last) in enumerate(HOPS):
            dest = flipped(me, (axis,))
            second[part * 3 + at].wait_recv()
            acc3_ref[at, here] = (parts_ref[dest, here].astype(f32) + in3_ref[at, here].astype(f32)).astype(bf16)
            copy = remote(acc3_ref.at[at, here], near_ref.at[at, here], send3.at[at, part], recv3.at[at, part], axis)
            copy.start()
            third.append(copy)
    for part in range(2):
        here = pl.ds(part * half, half)
        for at in range(3):
            third[part * 3 + at].wait_recv()
        out_ref[here] = (
            (parts_ref[me, here].astype(f32) + near_ref[0, here].astype(f32))
            + (near_ref[1, here].astype(f32) + near_ref[2, here].astype(f32))
        )
    for copy in first + second + third:
        copy.wait_send()


def scatter_chips(parts, collective_id):
    _, rows, width = parts.shape
    vmem = pl.BlockSpec(memory_space=pltpu.VMEM)
    dma = pltpu.SemaphoreType.DMA
    return pl.pallas_call(
        scatter_body,
        in_specs=[vmem],
        out_specs=vmem,
        out_shape=jax.ShapeDtypeStruct((rows, width), f32),
        scratch_shapes=[pltpu.VMEM((3, rows, width), bf16), pltpu.VMEM((rows, width), bf16)] + [pltpu.VMEM((3, rows, width), bf16)] * 3
        + [dma((3,))] * 2 + [dma((3, 2))] * 4,
        name="scatter_chips",
        compiler_params=pltpu.CompilerParams(collective_id=collective_id, has_side_effects=True, vmem_limit_bytes=32*2**20),
    )(parts)


def gather_slow(rows):
    return lax.all_to_all(
        jnp.broadcast_to(rows[None], (CHIPS,) + rows.shape), CHIP, split_axis=0, concat_axis=0, tiled=True
    )


def exchange_chips(parts):
    return lax.all_to_all(parts, CHIP, split_axis=0, concat_axis=0, tiled=True)


def scatter_slow(parts):
    return jnp.sum(exchange_chips(parts.astype(bf16)).astype(f32), axis=0)


def swap(values, axis):
    return lax.ppermute(values, axis, [(0, 1), (1, 0)])


def both_cores(own, axis):
    other = swap(own, "c")
    first = lax.axis_index("c") == 0
    return jnp.stack([jnp.where(first, own, other), jnp.where(first, other, own)], axis=axis)


def half_for_core(values, axis):
    core = lax.axis_index("c")
    own = lax.dynamic_index_in_dim(values, core, axis, keepdims=False)
    sent = lax.dynamic_index_in_dim(values, 1 - core, axis, keepdims=False)
    return own + swap(sent.astype(bf16), "c").astype(f32)


def sum_groups(tiles):
    groups = lax.axis_size("g")
    if groups != 2:
        return lax.psum_scatter(tiles.astype(f32), "g", scatter_dimension=1, tiled=True).astype(bf16)
    part = tiles.shape[1] // 2
    group = lax.axis_index("g")
    own = lax.dynamic_slice_in_dim(tiles, group * part, part, 1)
    sent = lax.dynamic_slice_in_dim(tiles, (1 - group) * part, part, 1)
    return (own.astype(f32) + swap(sent, "g").astype(f32)).astype(bf16)


def spread_columns(weight, width):
    rows = weight.shape[0]
    blocks = weight.reshape(rows, 2, CHIPS // 2, width)
    mine = lax.dynamic_index_in_dim(blocks, lax.axis_index("y"), 1, keepdims=False)
    return jnp.transpose(mine, (1, 0, 2))


def to_columns(blocks):
    groups = lax.axis_size("g")
    sent = jnp.broadcast_to(blocks[None], (groups,) + blocks.shape).reshape((-1,) + blocks.shape[1:])
    got = lax.all_to_all(sent, ("g", "a", "b"), split_axis=0, concat_axis=0, tiled=True)
    return both_cores(got, 1).reshape(-1, blocks.shape[-1])


def down_rows(w_down, chip):
    if lax.axis_size("g") == 2:
        other = swap(w_down, "g")
        mine = jnp.where(lax.axis_index("g") == lax.axis_index("y"), w_down, other)
        return both_cores(mine, 0).reshape(BLK, D)
    return lax.dynamic_slice_in_dim(lax.all_gather(w_down, FS, axis=0, tiled=True), chip * BLK, BLK, 0)


def band():
    tap = np.arange(CK)[:, None, None]
    source = np.arange(128)[None, :, None]
    target = np.arange(128)[None, None, :]
    return source - target + CK // 2 == tap


def body_any(
    layer_input, lengths, cotangent, w_query, w_key, w_value, w_out, w_gate, w_up, w_down, vec_copy, owners,
    basis_left, basis_right, block_master, block_first, block_second, vec_master, vec_first, vec_second,
):
    chip = (lax.axis_index("y") * 2 + lax.axis_index("a")) * 2 + lax.axis_index("b")
    fs_index = ((lax.axis_index("g") * 2 + lax.axis_index("a")) * 2 + lax.axis_index("b")) * 2 + lax.axis_index("c")
    seq_len = layer_input.shape[0]
    length = lengths[0]
    reps = lax.axis_size("y")
    fs_size = lax.axis_size(FS)

    own_vec = vec_copy.shape[0]
    small = jnp.concatenate(
        [vec_copy.astype(f32), jnp.zeros((1023 - own_vec,), f32), length.astype(f32).reshape(1)]
    ).reshape(8, 128)
    x_all, small_all = gather_first(layer_input, small, 1)
    small_all = small_all.reshape(fs_size, reps, 1024)
    vector = small_all[:, 0, :own_vec].reshape(-1)
    group_lengths = small_all[:, :, 1023].reshape(-1, 2, 2, 2, reps)
    group_lengths = lax.dynamic_index_in_dim(group_lengths, lax.axis_index("g"), 0, keepdims=False)
    group_lengths = lax.dynamic_index_in_dim(group_lengths, lax.axis_index("c"), 2, keepdims=False)
    group_lengths = jnp.transpose(group_lengths, (2, 0, 1)).reshape(CHIPS).astype(jnp.int32)
    gain_attn, gain_head, gain_ffn = vector[:D], vector[D : 2 * D], vector[2 * D : 3 * D]
    conv_end = 3 * D + H * CQ * CK
    theta = lax.dynamic_slice_in_dim(vector[3 * D : conv_end].reshape(H, CQ, CK), chip * 2, 2, 0)
    mixer = lax.dynamic_slice_in_dim(vector[conv_end : conv_end + 2 * H].reshape(H, 2), chip * 2, 2, 0)
    mix = mixer.reshape(4)
    gain_pair = jnp.pad(
        lax.dynamic_slice_in_dim(gain_head.reshape(H, DH), chip * 2, 2, 0), ((0, 0), (0, HP - DH))
    ).reshape(1, 2 * HP)
    toep = jnp.zeros((2, CQ, seq_len, seq_len), f32)
    offset = (
        jnp.arange(seq_len, dtype=jnp.int32)[:, None] - jnp.arange(seq_len, dtype=jnp.int32)[None, :] + CK // 2
    )
    for tap in range(CK):
        toep = jnp.where(offset[None, None] == tap, theta[:, :, tap][:, :, None, None], toep)
    toep = toep.astype(bf16).reshape(2, CQ * seq_len, seq_len)

    qkv_rows = to_columns(
        jnp.concatenate([spread_columns(w, 2 * DH) for w in (w_query, w_key, w_value)], axis=2)
    )
    w_qkv = jnp.pad(qkv_rows.reshape(D, 6, DH), ((0, 0), (0, 0), (0, HP - DH))).reshape(D, 6 * HP)
    w_in = to_columns(jnp.concatenate([spread_columns(w, BLK) for w in (w_gate, w_up)], axis=2))
    w_dn = down_rows(w_down, chip)
    w_o = lax.all_gather(w_out, FS, axis=0, tiled=True)

    input_float = layer_input.astype(f32)
    input_scale = rms(input_float)
    x_rows = x_all.reshape(CHIPS * seq_len, D).astype(f32)
    xn_rows = (x_rows * rms(x_rows) * gain_attn).astype(bf16)
    qkv = dot(xn_rows, w_qkv).astype(bf16).reshape(CHIPS, seq_len, 6 * HP)
    heads_pad, scores, weights, outs = run_forward(group_lengths, mix, qkv, toep, gain_pair)
    heads_sent = heads_pad.reshape(CHIPS, seq_len, 2, HP)[..., :DH].reshape(CHIPS, seq_len, 2 * DH)
    heads = jnp.transpose(exchange_chips(heads_sent), (1, 0, 2)).reshape(seq_len, D)
    hmid = input_float + dot(heads, w_o)
    hmid_scale = rms(hmid)
    hn_rows = gather_chips((hmid * hmid_scale * gain_ffn).astype(bf16), 2).reshape(CHIPS * seq_len, D)
    both = dot(hn_rows, w_in)
    gate, up = both[:, :BLK], both[:, BLK:]
    sig = jax.nn.sigmoid(gate)
    silu = gate * sig
    inner = (silu * up).astype(bf16)
    ffn = scatter_slow(dot(inner, w_dn).reshape(CHIPS, seq_len, D))
    layer_output = (hmid + ffn).astype(bf16)

    valid = (jnp.arange(seq_len) < length).astype(f32)
    dy = cotangent.astype(f32) * valid[:, None]
    dy_rows = gather_slow(dy.astype(bf16)).reshape(CHIPS * seq_len, D)
    dinner = dot_nt(dy_rows, w_dn)
    dgate = (dinner * up * (sig * (1.0 + gate * (1.0 - sig)))).astype(bf16)
    dup = (dinner * silu).astype(bf16)
    dboth = jnp.concatenate([dgate, dup], axis=1)
    dhn = scatter_chips(dot_nt(dboth, w_in).astype(bf16).reshape(CHIPS, seq_len, D), 3)
    dhmid, grad_gain_ffn = norm_backward(hmid, hmid_scale, gain_ffn, dhn)
    dhmid = dhmid + dy
    dattn = dhmid.astype(bf16)
    dheads = dot_nt(dattn, w_o).astype(bf16).reshape(seq_len, CHIPS, 2 * DH)
    dheads = exchange_chips(jnp.transpose(dheads, (1, 0, 2)))
    dheads = jnp.pad(dheads.reshape(CHIPS, seq_len, 2, DH), ((0, 0), (0, 0), (0, 0), (0, HP - DH)))
    dqkv, theta_sums, mixer_sums, gain_sums = run_backward(
        group_lengths, mix, qkv, toep, gain_pair, scores, weights, outs, dheads.reshape(CHIPS, seq_len, 2 * HP)
    )
    dqkv_rows = dqkv.reshape(CHIPS * seq_len, 6 * HP)
    dxn = scatter_slow(dot_nt(dqkv_rows, w_qkv).reshape(CHIPS, seq_len, D))
    dinput, grad_gain_attn = norm_backward(input_float, input_scale, gain_attn, dxn)
    input_grad = dinput + dhmid

    taps = jnp.asarray(band())
    theta_sums = theta_sums.reshape(2, seq_len, CQ, seq_len)
    grad_theta = jnp.stack(
        [jnp.sum(jnp.where(taps[tap][None, :, None, :], theta_sums, 0.0), axis=(1, 3)) for tap in range(CK)], axis=2
    )
    grad_mixer = jnp.sum(mixer_sums[:4], axis=1)
    vector_grad = jnp.concatenate(
        [
            grad_gain_attn,
            lax.dynamic_update_slice_in_dim(
                jnp.zeros((D,), f32), gain_sums.reshape(2, HP)[:, :DH].reshape(-1), chip * 2 * DH, 0
            ),
            grad_gain_ffn,
            lax.dynamic_update_slice_in_dim(
                jnp.zeros((H * CQ * CK,), f32), grad_theta.reshape(-1), chip * 2 * CQ * CK, 0
            ),
            lax.dynamic_update_slice_in_dim(jnp.zeros((2 * H,), f32), grad_mixer, chip * 4, 0),
        ]
    )
    pieces = jnp.pad(vector_grad.reshape(fs_size, 1, own_vec), ((0, 0), (0, 0), (0, 512 - own_vec)))
    pieces = jnp.broadcast_to(pieces, (fs_size, reps, 512)).reshape(-1, 4, 128)
    vector_total = jnp.sum(
        lax.all_to_all(pieces, ALL, split_axis=0, concat_axis=0, tiled=True), axis=0
    ).reshape(512)[:own_vec]

    strip = BLK // (2 * CHIPS)
    grad_in = dot_tn(hn_rows, dboth).reshape(ROW_TILES, 2, CHIPS, strip, 2, BLK)
    grad_down = dot_tn(inner, dy_rows).reshape(2, CHIPS, strip, ROW_TILES, BLK)
    grad_in = jnp.transpose(half_for_core(grad_in, 1), (1, 3, 0, 2, 4)).reshape(CHIPS, 2 * ROW_TILES, strip, BLK)
    grad_down = jnp.transpose(half_for_core(grad_down, 0), (0, 2, 1, 3))
    ffn_tiles = exchange_chips(jnp.concatenate([grad_in, grad_down], axis=1).astype(bf16))
    gate_tiles = jnp.transpose(ffn_tiles[:, : 2 * ROW_TILES], (1, 0, 2, 3)).reshape(-1, strip, BLK)
    down_tiles = ffn_tiles[:, 2 * ROW_TILES :].reshape(-1, strip, BLK)
    grad_qkv = dot_tn(xn_rows, dqkv_rows).reshape(ROW_TILES, 2, CHIPS, strip, 6, HP)[..., :DH]
    grad_qkv = jnp.transpose(half_for_core(grad_qkv, 1), (1, 0, 2, 3, 4))
    grad_qkv = exchange_chips(grad_qkv.astype(bf16).reshape(CHIPS, ROW_TILES, strip, 6 * DH))
    grad_qkv = jnp.transpose(
        grad_qkv.reshape(CHIPS, ROW_TILES, strip, 3, 2 * DH), (3, 1, 2, 0, 4)
    ).reshape(3, ROW_TILES, strip, ROW_TILES, BLK)
    qkv_tiles = jnp.transpose(grad_qkv, (0, 1, 3, 2, 4)).reshape(-1, strip, BLK)
    heads_strips = jnp.transpose(heads.reshape(seq_len, 2 * ROW_TILES, CHIPS, strip), (2, 0, 1, 3))
    heads_strips = exchange_chips(heads_strips.reshape(CHIPS, seq_len, 2 * ROW_TILES * strip))
    dattn_rows = gather_slow(dattn).reshape(CHIPS * seq_len, D)
    grad_out = dot_tn(heads_strips.reshape(CHIPS * seq_len, -1), dattn_rows)
    grad_out = half_for_core(grad_out.reshape(ROW_TILES, 2, strip, ROW_TILES, BLK), 1)
    out_tiles = jnp.transpose(grad_out.astype(bf16), (0, 2, 1, 3)).reshape(-1, strip, BLK)

    groups = lax.axis_size("g")
    part = strip // groups
    own_slots = basis_left.shape[0]
    devices = groups * 2 * CHIPS
    slot_total = own_slots * devices
    sums = jnp.concatenate(
        [sum_groups(jnp.concatenate([qkv_tiles, out_tiles], axis=0)), sum_groups(jnp.concatenate([gate_tiles, down_tiles], axis=0))],
        axis=0,
    )
    matches = (jnp.arange(slot_total)[:, None] == owners[None, :]).astype(bf16)
    slots = dot(matches, sums.reshape(sums.shape[0], -1)).astype(bf16)
    slots = lax.all_to_all(
        slots.reshape(devices, own_slots, part, BLK), ALL, split_axis=0, concat_axis=0, tiled=True
    )
    slots = slots.reshape(groups, 2, 2, 2, 2, own_slots, part, BLK)
    own_grad = jnp.transpose(slots, (5, 3, 4, 1, 2, 0, 6, 7)).reshape(own_slots, BLK, BLK)

    left_low, right_low = basis_left.astype(bf16), basis_right.astype(bf16)
    rotated = jnp.einsum("sia,sij->saj", left_low, own_grad, preferred_element_type=f32)
    rotated = jnp.einsum("saj,sjb->sab", rotated.astype(bf16), right_low, preferred_element_type=f32)
    first_new = beta_first * block_first + (1.0 - beta_first) * rotated
    second_new = beta_second * block_second + (1.0 - beta_second) * rotated * rotated
    direction = (first_new / (jnp.sqrt(second_new) + eps_adam)).astype(bf16)
    turned = jnp.einsum("sia,sab->sib", left_low, direction, preferred_element_type=f32)
    turned = jnp.einsum("sib,sjb->sij", turned.astype(bf16), right_low, preferred_element_type=f32)
    master_new = block_master - rate_block * (turned + decay_block * block_master)
    vec_first_new = beta_first * vec_first + (1.0 - beta_first) * vector_total
    vec_second_new = beta_second * vec_second + (1.0 - beta_second) * vector_total * vector_total
    vec_master_new = vec_master - rate_vector * vec_first_new / (jnp.sqrt(vec_second_new) + eps_adam)
    return (
        layer_output, input_grad, first_new, second_new, master_new, master_new.astype(bf16),
        vec_first_new, vec_second_new, vec_master_new, vec_master_new.astype(bf16),
    )


def group_at(mask):
    return {axis: 1 - lax.axis_index(axis) for axis, bit in (("g", 4), ("a", 2), ("b", 1)) if mask & bit}


def other_bit(axis, changed):
    at = lax.axis_index(axis)
    return 1 - at if changed else at


def push(src, dst, send, recv, device):
    copy = pltpu.make_async_remote_copy(src_ref=src, dst_ref=dst, send_sem=send, recv_sem=recv, device_id=device)
    copy.start()
    return copy


class Gather:
    def __init__(self, x_ref, out_ref, local_sem, send1, recv1, send2, recv2, send3, recv3):
        self.x, self.out, self.local_sem = x_ref, out_ref, local_sem
        self.sems = ((send1, recv1), (send2, recv2), (send3, recv3))
        self.me = chip_index()
        self.half = x_ref.shape[0] // 2
        self.sent, self.second = [], []

    def here(self, part):
        return pl.ds(part * self.half, self.half)

    def start(self):
        self.local = pltpu.make_async_copy(self.x, self.out.at[self.me], self.local_sem)
        self.local.start()
        send, recv = self.sems[0]
        for part in range(2):
            for at, (axis, _, _) in enumerate(HOPS):
                self.sent.append(
                    push(
                        self.x.at[self.here(part)], self.out.at[self.me, self.here(part)],
                        send.at[at, part], recv.at[at, part], across(axis),
                    )
                )

    def onward(self):
        send, recv = self.sems[1]
        for part in range(2):
            for at, (axis, onward, _) in enumerate(HOPS):
                self.sent[part * 3 + at].wait_recv()
                block = self.out.at[flipped(self.me, (axis,)), self.here(part)]
                self.second.append(push(block, block, send.at[at, part], recv.at[at, part], across(onward)))

    def last(self):
        send, recv = self.sems[2]
        self.third = []
        for copy in self.second:
            copy.wait_recv()
        for at, (axis, onward, last) in enumerate(HOPS):
            begin, count = THIRDS[at]
            piece = self.out.at[flipped(self.me, (axis, onward)), pl.ds(begin, count)]
            self.third.append(push(piece, piece, send.at[at], recv.at[at], across(last)))

    def finish(self):
        for copy in self.third:
            copy.wait_recv()
        self.local.wait()

    def drain(self):
        for copy in self.sent + self.second + self.third:
            copy.wait_send()


class SideGather:
    def __init__(self, x_ref, out_ref, local_sem, send1, recv1, send2, recv2, send3, recv3):
        self.x, self.out, self.local_sem = x_ref, out_ref, local_sem
        self.sems = ((send1, recv1), (send2, recv2), (send3, recv3))
        self.me = chip_index()
        half = x_ref.shape[0] // 2
        self.low, self.high = pl.ds(0, half), pl.ds(half, half)

    def start(self):
        self.local = pltpu.make_async_copy(self.x, self.out.at[self.me], self.local_sem)
        self.local.start()
        send, recv = self.sems[0]
        self.first = [
            push(self.x, self.out.at[self.me], send.at[at], recv.at[at], across(axis)) for at, axis in enumerate("aby")
        ]

    def onward(self):
        send, recv = self.sems[1]
        blocks = [self.out.at[flipped(self.me, (axis,))] for axis in "aby"]
        self.first[0].wait_recv()
        self.second = [
            push(blocks[0], blocks[0], send.at[0], recv.at[0], across("b")),
            push(blocks[0], blocks[0], send.at[1], recv.at[1], across("y")),
        ]
        self.first[1].wait_recv()
        piece = blocks[1].at[self.high]
        self.second.append(push(piece, piece, send.at[2], recv.at[2], across("y")))
        self.first[2].wait_recv()
        piece = blocks[2].at[self.low]
        self.second.append(push(piece, piece, send.at[3], recv.at[3], across("b")))

    def last(self):
        send, recv = self.sems[2]
        self.second[0].wait_recv()
        piece = self.out.at[flipped(self.me, ("a", "b")), self.high]
        self.third = [push(piece, piece, send.at[0], recv.at[0], across("y"))]
        self.second[1].wait_recv()
        piece = self.out.at[flipped(self.me, ("a", "y")), self.low]
        self.third.append(push(piece, piece, send.at[1], recv.at[1], across("b")))

    def finish(self):
        for copy in self.second[2:] + self.third:
            copy.wait_recv()
        self.local.wait()

    def drain(self):
        for copy in self.first + self.second + self.third:
            copy.wait_send()


def side_sems():
    dma = pltpu.SemaphoreType.DMA
    return [dma] + [dma((3,))] * 2 + [dma((4,))] * 2 + [dma((2,))] * 2


class Scatter:
    def __init__(self, parts, near, in2, in3, acc2, acc3, send1, recv1, send2, recv2, send3, recv3):
        self.parts, self.near, self.in2, self.in3, self.acc2, self.acc3 = parts, near, in2, in3, acc2, acc3
        self.sems = ((send1, recv1), (send2, recv2), (send3, recv3))
        self.me = chip_index()
        self.half = parts.shape[1] // 2

    def here(self, part):
        return pl.ds(part * self.half, self.half)

    def start(self):
        send, recv = self.sems[0]
        opposite = flipped(self.me, ("y", "a", "b"))
        self.first = []
        for at, (_, _, last) in enumerate(HOPS):
            rows = pl.ds(*THIRDS[at])
            self.first.append(push(self.parts.at[opposite, rows], self.in2.at[rows], send.at[at], recv.at[at], across(last)))

    def onward(self):
        send, recv = self.sems[1]
        self.second = []
        for part in range(2):
            for at, (axis, onward, _) in enumerate(HOPS):
                dest = flipped(self.me, (axis, onward))
                if part == 0:
                    self.first[at].wait_recv()
                    rows = pl.ds(*THIRDS[at])
                    self.acc2[at] = self.parts[dest]
                    self.acc2[at, rows] = (
                        self.parts[dest, rows].astype(f32) + self.in2[rows].astype(f32)
                    ).astype(bf16)
                here = self.here(part)
                self.second.append(
                    push(self.acc2.at[at, here], self.in3.at[at, here], send.at[at, part], recv.at[at, part], across(onward))
                )

    def last(self):
        send, recv = self.sems[2]
        self.third = []
        for part in range(2):
            here = self.here(part)
            for at, (axis, _, _) in enumerate(HOPS):
                dest = flipped(self.me, (axis,))
                self.second[part * 3 + at].wait_recv()
                self.acc3[at, here] = (
                    self.parts[dest, here].astype(f32) + self.in3[at, here].astype(f32)
                ).astype(bf16)
                self.third.append(
                    push(self.acc3.at[at, here], self.near.at[at, here], send.at[at, part], recv.at[at, part], across(axis))
                )

    def finish(self, part):
        here = self.here(part)
        for at in range(3):
            self.third[part * 3 + at].wait_recv()
        return (self.parts[self.me, here].astype(f32) + self.near[0, here].astype(f32)) + (
            self.near[1, here].astype(f32) + self.near[2, here].astype(f32)
        )

    def drain(self):
        for copy in self.first + self.second + self.third:
            copy.wait_send()


class SideScatter:
    def __init__(self, parts, near, in1, in2, acc2, acc3, send1, recv1, send2, recv2, send3, recv3):
        self.parts, self.near, self.in1, self.in2, self.acc2, self.acc3 = parts, near, in1, in2, acc2, acc3
        self.sems = ((send1, recv1), (send2, recv2), (send3, recv3))
        self.me = chip_index()
        half = parts.shape[1] // 2
        self.low, self.high = pl.ds(0, half), pl.ds(half, half)

    def start(self):
        send, recv = self.sems[0]
        far, side = flipped(self.me, ("a", "b", "y")), flipped(self.me, ("b", "y"))
        self.first = [
            push(self.parts.at[block, rows], self.in1.at[at], send.at[at], recv.at[at], across(axis))
            for at, (block, rows, axis) in enumerate(
                ((far, self.high, "y"), (far, self.low, "b"), (side, self.low, "b"), (side, self.high, "y"))
            )
        ]

    def add(self, at, axes, rows, acc):
        self.first[at].wait_recv()
        block = flipped(self.me, axes)
        acc[...] = self.parts[block]
        acc[rows] = (self.parts[block, rows].astype(f32) + self.in1[at].astype(f32)).astype(bf16)
        return acc

    def onward(self):
        send, recv = self.sems[1]
        third_send, third_recv = self.sems[2]
        self.second = [
            push(self.add(0, ("a", "b"), self.high, self.acc2.at[0]), self.in2.at[0], send.at[0], recv.at[0], across("b")),
            push(self.add(1, ("a", "y"), self.low, self.acc2.at[1]), self.in2.at[1], send.at[1], recv.at[1], across("y")),
        ]
        self.third = [
            push(self.add(at, (axis,), rows, self.acc3.at[to]), self.near.at[to], third_send.at[to], third_recv.at[to], across(axis))
            for at, axis, rows, to in ((3, "b", self.high, 1), (2, "y", self.low, 2))
        ]

    def last(self):
        send, recv = self.sems[2]
        for copy in self.second:
            copy.wait_recv()
        self.acc3[0] = (
            self.parts[flipped(self.me, ("a",))].astype(f32) + (self.in2[0].astype(f32) + self.in2[1].astype(f32))
        ).astype(bf16)
        self.third.append(push(self.acc3.at[0], self.near.at[0], send.at[0], recv.at[0], across("a")))

    def finish(self):
        for copy in self.third:
            copy.wait_recv()
        return (self.parts[self.me].astype(f32) + self.near[0].astype(f32)) + (
            self.near[1].astype(f32) + self.near[2].astype(f32)
        )

    def drain(self):
        for copy in self.first + self.second + self.third:
            copy.wait_send()


def side_scatter_scratch(rows, width):
    dma = pltpu.SemaphoreType.DMA
    return [
        pltpu.VMEM(dims + (width,), bf16) for dims in ((3, rows), (4, rows // 2), (2, rows), (2, rows), (3, rows))
    ] + [dma((4,))] * 2 + [dma((2,))] * 2 + [dma((3,))] * 2


def scatter_scratch(rows, width):
    dma = pltpu.SemaphoreType.DMA
    three = pltpu.VMEM((3, rows, width), bf16)
    return [three, pltpu.VMEM((rows, width), bf16), three, three, three] + [dma((3,))] * 2 + [dma((3, 2))] * 4


VMEM = pl.BlockSpec(memory_space=pltpu.VMEM)


HEAD_ROW, FFN_ROW, THETA_ROW, MIX_ROW, VEC_ROWS = 12, 28, 40, 56, 64
SHARD_ROWS = 16


def vector_row(at):
    for begin, row, width in (
        (3 * D + H * CQ * CK, MIX_ROW, 4), (3 * D, THETA_ROW, CQ * CK), (2 * D, FFN_ROW, 128), (D, HEAD_ROW, DH), (0, 0, 128)
    ):
        if at >= begin:
            return row + (at - begin) // width


def vector_rows(own_vec, shards):
    return [min(vector_row(shard * own_vec), VEC_ROWS - SHARD_ROWS) // 8 * 8 for shard in range(shards)]


def rows_of_vector(flat):
    conv_end = 3 * D + H * CQ * CK
    return jnp.concatenate(
        [
            flat[:D].reshape(-1, 128),
            jnp.pad(flat[D : 2 * D].reshape(H, DH), ((0, 0), (0, 128 - DH))),
            flat[2 * D : 3 * D].reshape(-1, 128),
            jnp.pad(flat[3 * D : conv_end].reshape(H, CQ * CK), ((0, 0), (0, 128 - CQ * CK))),
            jnp.pad(flat[conv_end : conv_end + 2 * H].reshape(CHIPS, 4), ((0, 0), (0, 124))),
        ],
        axis=0,
    )


def source_at(mask):
    return ((other_bit("g", mask & 4) * 2 + other_bit("a", mask & 2)) * 2 + other_bit("b", mask & 1)) * 2 + lax.axis_index("c")


def front_body(
    first_rows, length_ref, vec_ref, x_ref, w_query_ref, w_key_ref, w_value_ref, cot_ref,
    w_out_ref, w_gate_ref, w_up_ref, w_down_ref, dy_ref, len_ref, mix_ref, gains_ref, toep_ref, gain_ref, strips_ref, hmid_ref,
    xn_out, qkv_out, s_out, p_out, o_out, wq_out, wo_out, hn_all_ref, w_in_ref, w_dn_ref, dy_all_ref,
    xn_ref, qkv_ref, s_ref, p_ref, o_ref, wq_ref, wo_ref, heads_ref, leave_sems,
    blocks_ref, own_len_ref, vecs_ref, full_ref, x_all_ref, pad_ref, out_heads, hn_ref, passing, vec_send, vec_recv, len_send, len_recv, local_sems, q_send, q_recv, q_core_send, q_core_recv,
    o_send, o_recv, o_side_send, o_side_recv, o_core_send, o_core_recv, d_send, d_recv,
    w_send, w_recv, u_send, u_recv, core_send, core_recv, head_send, head_recv, *hops,
):
    seqs, rows, _ = x_all_ref.shape
    g, a, b, c, y = (lax.axis_index(axis) for axis in ALL)
    me = chip_index()
    mine = source_at(0)
    shard = {mask: source_at(mask) for mask in range(8)}
    low, high = pl.ds(0, BLK), pl.ds(BLK, BLK)
    order = (4, 6, 5, 7, 2, 1, 3)

    def columns(chip):
        return pl.ds(pl.multiple_of(chip * BLK, BLK), BLK)

    def block_to(mask):
        return (y * 2 + other_bit("a", mask & 2)) * 2 + other_bit("b", mask & 1)

    local = [
        pltpu.make_async_copy(w_out_ref, wo_ref.at[mine], local_sems.at[1]),
        pltpu.make_async_copy(w_gate_ref.at[:, columns(me)], w_in_ref.at[mine, :, low], local_sems.at[2]),
        pltpu.make_async_copy(w_up_ref.at[:, columns(me)], w_in_ref.at[mine, :, high], local_sems.at[3]),
    ]
    down_local = pltpu.make_async_copy(w_down_ref, w_dn_ref.at[c], local_sems.at[4])
    own_len_ref[...] = jnp.full(own_len_ref.shape, length_ref[0].astype(f32), f32)
    own_small = [
        pltpu.make_async_copy(vec_ref, vecs_ref.at[mine], local_sems.at[5]),
        pltpu.make_async_copy(own_len_ref, len_ref.at[me], local_sems.at[6]),
    ]
    for copy in local + own_small:
        copy.start()

    @pl.when(g == y)
    def _():
        down_local.start()

    greet_all()
    leaving = []

    def leave(src, dst):
        copy = pltpu.make_async_copy(src, dst, leave_sems.at[len(leaving)])
        copy.start()
        leaving.append(copy)

    sent, relayed = {}, []
    first = Gather(x_ref, x_all_ref, *hops[:7])
    side = SideGather(dy_ref, dy_all_ref, *hops[7:14])
    gather = Gather(hn_ref, hn_all_ref, *hops[14:])

    def push_vec(step, carry):
        to = lax.rem(mine + step, 16)
        pltpu.make_async_remote_copy(
            src_ref=vec_ref, dst_ref=vecs_ref.at[mine], send_sem=vec_send, recv_sem=vec_recv,
            device_id={
                "g": lax.div(to, 8), "a": lax.rem(lax.div(to, 4), 2), "b": lax.rem(lax.div(to, 2), 2), "c": lax.rem(to, 2)
            },
        ).start()
        return carry

    lax.fori_loop(1, 16, push_vec, 0)
    lengths_sent = [
        push(own_len_ref, len_ref.at[me], len_send.at[mask], len_recv.at[mask], chip_at(mask)) for mask in range(1, 8)
    ]

    first.start()
    for chip in range(CHIPS):
        cols = slice(chip * 2 * DH, (chip + 1) * 2 * DH)
        blocks_ref[chip] = jnp.concatenate([w_query_ref[:, cols], w_key_ref[:, cols], w_value_ref[:, cols]], axis=1)
    wq_ref[mine] = blocks_ref[me]
    valid = lax.broadcasted_iota(jnp.int32, cot_ref.shape, 0) < length_ref[0]
    dy_ref[...] = jnp.where(valid, cot_ref[...].astype(f32), 0.0).astype(bf16)

    for mask in order:
        sent[mask] = push(blocks_ref.at[block_to(mask)], wq_ref.at[mine], q_send.at[mask], q_recv.at[mask], group_at(mask))

    def relay_qkv(mask):
        sent[mask].wait_recv()
        block = wq_ref.at[shard[mask]]
        relayed.append(push(block, block, q_core_send.at[mask], q_core_recv.at[mask], across("c")))

    half = pl.ds(pl.multiple_of(y * 48, 16), 48)
    lines, o_side, o_core = {}, {}, []

    def start_lines():
        for mask in (2, 4, 6):
            lines[mask] = push(w_out_ref.at[half], wo_ref.at[mine, half], o_send.at[mask], o_recv.at[mask], group_at(mask))
        lines[1] = push(w_out_ref.at[half], wo_ref.at[mine, half], o_send.at[1], o_recv.at[1], across("b"))
        o_core.append(push(w_out_ref, wo_ref.at[mine], o_core_send.at[0], o_core_recv.at[0], across("c")))

    def to_side(mask):
        lines[mask].wait_recv()
        piece = wo_ref.at[shard[mask], half]
        o_side[mask] = push(piece, piece, o_side_send.at[mask], o_side_recv.at[mask], across("y"))
        if mask in (2, 4, 6):
            lines[mask + 1] = push(piece, piece, o_send.at[mask + 1], o_recv.at[mask + 1], across("b"))

    def out_to_core(masks):
        for mask in masks:
            o_side[mask].wait_recv()
            block = wo_ref.at[shard[mask]]
            o_core.append(push(block, block, o_core_send.at[mask], o_core_recv.at[mask], across("c")))

    count = w_down_ref.shape[0] // 2
    upper, lower = pl.ds(0, count), pl.ds(count, count)

    def down_copy(src, dst, at, axis):
        return pltpu.make_async_remote_copy(
            src_ref=src, dst_ref=dst, send_sem=d_send.at[at], recv_sem=d_recv.at[at], device_id=across(axis)
        )

    def down_direct():
        return down_copy(w_down_ref.at[upper], w_dn_ref.at[c, upper], 0, "g")

    def down_around():
        return down_copy(w_down_ref.at[lower], passing, 1, "g")

    def down_over():
        return down_copy(passing, w_dn_ref.at[c, lower], 2, "y")

    def down_to_core():
        return down_copy(w_dn_ref.at[c], w_dn_ref.at[c], 3, "c")

    def down_start():
        @pl.when(g == y)
        def _():
            down_direct().start()

        @pl.when(g != y)
        def _():
            down_around().start()

    def down_pass():
        @pl.when(g == y)
        def _():
            down_around().wait_recv()
            down_over().start()

    def down_last():
        @pl.when(g == y)
        def _():
            down_local.wait()
            down_to_core().start()
            down_direct().wait_send()
            down_over().wait_send()

        @pl.when(g != y)
        def _():
            down_direct().wait_recv()
            down_over().wait_recv()
            down_to_core().start()
            down_around().wait_send()

    gate, up = {}, {}

    def send_columns(masks):
        for mask in masks:
            to = columns(block_to(mask))
            gate[mask] = push(w_gate_ref.at[:, to], w_in_ref.at[mine, :, low], w_send.at[mask], w_recv.at[mask], group_at(mask))
            up[mask] = push(w_up_ref.at[:, to], w_in_ref.at[mine, :, high], u_send.at[mask], u_recv.at[mask], group_at(mask))

    def relay(mask):
        gate[mask].wait_recv()
        up[mask].wait_recv()
        block = w_in_ref.at[shard[mask]]
        relayed.append(push(block, block, core_send.at[mask], core_recv.at[mask], across("c")))

    side.start()
    relayed.append(push(wq_ref.at[mine], wq_ref.at[mine], q_core_send.at[0], q_core_recv.at[0], across("c")))
    first.onward()
    start_lines()

    for copy in own_small:
        copy.wait()
    others = vecs_ref.at[pl.ds(0, 15)]
    pltpu.make_async_copy(others, others, vec_recv).wait()
    full_ref[...] = jnp.zeros_like(full_ref)
    for at, row in enumerate(first_rows):
        full_ref[row : row + SHARD_ROWS, :] += vecs_ref[at]
    gains_ref[...] = jnp.zeros_like(gains_ref)
    for row in range(D // 128):
        gains_ref[0:1, row * 128 : (row + 1) * 128] = full_ref[row : row + 1, :]
        gains_ref[1:2, row * 128 : (row + 1) * 128] = full_ref[FFN_ROW + row : FFN_ROW + row + 1, :]
    mix_ref[...] = jnp.zeros_like(mix_ref)
    mix_row = full_ref[pl.ds(MIX_ROW + me, 1), :]
    for at in range(4):
        mix_ref[at : at + 1, :] = jnp.broadcast_to(mix_row[:, at : at + 1], (1, 128))
    query_at = lax.broadcasted_iota(jnp.int32, (rows, rows), 0)
    key_at = lax.broadcasted_iota(jnp.int32, (rows, rows), 1)
    key_float = key_at.astype(f32)
    tap_at = query_at - key_at + CK // 2
    for head in range(2):
        gain_ref[:, head * HP : (head + 1) * HP] = full_ref[pl.ds(HEAD_ROW + 2 * me + head, 1), :]
        theta = full_ref[pl.ds(THETA_ROW + 2 * me + head, 1), :]
        for lag in range(CQ):
            band_values = jnp.zeros((rows, rows), f32)
            for tap in range(CK):
                at = lag * CK + tap
                band_values = jnp.where(tap_at == tap, theta[:, at : at + 1], band_values)
            toep_ref[head, lag * rows : (lag + 1) * rows, :] = band_values.astype(bf16)

    side.onward()
    first.last()
    side.last()
    down_start()
    for mask in order:
        relay_qkv(mask)
    send_columns((2, 1, 3, 4, 6, 5, 7))
    first.finish()
    for copy in relayed + lengths_sent:
        copy.wait_recv()
    qkv_relayed = relayed[:]
    del relayed[:]

    pad_ref[0:8, :] = jnp.zeros((8, rows), f32)
    blank = jnp.zeros((rows, HP - DH), bf16)
    batch = 4

    def project(at, carry):
        values = x_all_ref[pl.ds(at * batch, batch)].astype(f32).reshape(batch * rows, D)
        normed = (values * rms(values) * gains_ref[0:1, :]).astype(bf16)
        xn_ref[pl.ds(at * batch, batch)] = normed.reshape(batch, rows, D)
        made = dot(normed, wq_ref[...].reshape(D, 6 * DH)).astype(bf16)
        for seq in range(batch):
            for piece in range(6):
                qkv_ref[at * batch + seq, :, piece * HP : (piece + 1) * HP] = jnp.concatenate(
                    [made[seq * rows : (seq + 1) * rows, piece * DH : (piece + 1) * DH], blank], axis=1
                )
        return carry

    project(0, 0)
    for mask in (2, 4, 6, 1):
        to_side(mask)
    project(1, 0)
    leave(xn_ref, xn_out)
    leave(qkv_ref, qkv_out)
    leave(wq_ref, wq_out)
    for copy in local:
        copy.wait()
    relayed.append(push(w_in_ref.at[mine], w_in_ref.at[mine], core_send.at[0], core_recv.at[0], across("c")))

    def head_copy(seq):
        return pltpu.make_async_remote_copy(
            src_ref=out_heads.at[seq], dst_ref=heads_ref.at[me], send_sem=head_send.at[seq], recv_sem=head_recv.at[me],
            device_id={"y": lax.div(seq, 4), "a": lax.rem(lax.div(seq, 2), 2), "b": lax.rem(seq, 2)},
        )

    def attend(step, carry):
        seq = lax.rem(me + step, seqs)
        keep = (key_at <= query_at) & (key_float < len_ref[seq, 0:1, :])
        weights, made = [], []
        for head in range(2):
            query = qkv_ref[seq, :, head * HP : (head + 1) * HP]
            key = qkv_ref[seq, :, (2 + head) * HP : (3 + head) * HP]
            scores = jnp.where(keep, dot_nt(query, key) * (1.0 / math.sqrt(DH)), 0.0)
            s_ref[seq, head] = scores.astype(bf16)
            wide = shifted_down(pad_ref, scores)
            near = wide.astype(bf16)
            rest = (wide - near.astype(f32)).astype(bf16)
            conv = dot(near, toep_ref[head]) + dot(rest, toep_ref[head])
            logits = jnp.where(keep, conv, -1e30)
            weight = jnp.exp(logits - jnp.max(logits, axis=-1, keepdims=True))
            weight = weight / jnp.sum(weight, axis=-1, keepdims=True)
            p_ref[seq, head] = weight
            weights.append(weight)
        for head in range(2):
            mixed = mix_ref[2 * head : 2 * head + 1, :] * weights[0] + mix_ref[2 * head + 1 : 2 * head + 2, :] * weights[1]
            value = qkv_ref[seq, :, (4 + head) * HP : (5 + head) * HP]
            out = dot(mixed.astype(bf16), value)
            o_ref[seq, :, head * HP : (head + 1) * HP] = out
            scale = lax.rsqrt(jnp.sum(out * out, axis=-1, keepdims=True) * (1.0 / DH) + eps_norm)
            made.append((out * scale * gain_ref[:, head * HP : (head + 1) * HP])[:, :DH])
        out_heads[seq] = jnp.concatenate(made, axis=1).astype(bf16)

        @pl.when(step > 0)
        def _():
            head_copy(seq).start()

        return carry

    lax.fori_loop(0, 3, attend, 0)
    for mask in (3, 5, 7):
        to_side(mask)
    down_pass()
    lax.fori_loop(3, 6, attend, 0)
    out_to_core((2, 4, 6))
    lax.fori_loop(6, seqs, attend, 0)
    out_to_core((1, 3, 5, 7))
    heads_ref[me] = out_heads[me]
    leave(s_ref, s_out)
    leave(p_ref, p_out)
    leave(o_ref, o_out)
    for copy in o_core:
        copy.wait_recv()
    leave(wo_ref, wo_out)

    def head_arrived(step, carry):
        source = lax.rem(me + step, seqs)
        pltpu.make_async_copy(out_heads.at[source], heads_ref.at[source], head_recv.at[source]).wait()
        return carry

    lax.fori_loop(1, seqs, head_arrived, 0)

    def project_out(at, carry):
        cols = pl.ds(pl.multiple_of(at * BLK, BLK), BLK)
        total = x_ref[:, cols].astype(f32)
        for chip in range(CHIPS):
            weight = wo_ref[2 * chip : 2 * chip + 2, :, cols].reshape(2 * DH, BLK)
            total += dot(heads_ref[chip], weight)
        hmid_ref[:, cols] = total
        return carry

    lax.fori_loop(0, ROW_TILES, project_out, 0)
    hmid = hmid_ref[...]
    hn_ref[...] = (hmid * rms(hmid) * gains_ref[1:2, :]).astype(bf16)
    gather.start()
    width = BLK // (2 * CHIPS)
    for chip in range(CHIPS):
        pieces = []
        for at in range(2 * ROW_TILES):
            begin = at * (BLK // 2) + chip * width
            source, begin = begin // (2 * DH), begin % (2 * DH)
            pieces.append(heads_ref[source, :, begin : begin + width])
        strips_ref[chip] = jnp.concatenate(pieces, axis=1)
    for mask in (4, 6):
        relay(mask)
    gather.onward()
    for mask in (5, 7, 2):
        relay(mask)
    gather.last()
    for mask in (1, 3):
        relay(mask)
    down_last()
    down_to_core().wait()
    side.finish()
    gather.finish()
    for copy in relayed:
        copy.wait_recv()
    for copy in leaving:
        copy.wait()

    def head_left(step, carry):
        head_copy(lax.rem(me + step, seqs)).wait_send()
        return carry

    lax.fori_loop(1, seqs, head_left, 0)
    first.drain()
    side.drain()
    gather.drain()
    for copies in (sent, lines, o_side, gate, up):
        for copy in copies.values():
            copy.wait_send()
    pltpu.make_async_copy(others, others, vec_send).wait()
    for copy in qkv_relayed + relayed + o_core + lengths_sent:
        copy.wait_send()


def run_front(first_rows, length, vec, x, w_query, w_key, w_value, cotangent, w_out, w_gate, w_up, w_down):
    rows = x.shape[0]
    dma = pltpu.SemaphoreType.DMA
    small = [
        (x.shape, bf16), ((CHIPS, 8, 128), f32), ((8, 128), f32), ((8, D), f32), ((2, CQ * rows, rows), bf16), ((1, 2 * HP), f32),
        ((CHIPS, rows, 2 * DH), bf16), ((rows, D), f32),
    ]
    large = [
        ((CHIPS, rows, D), bf16), ((CHIPS, rows, 6 * HP), bf16), ((CHIPS, 2, rows, rows), bf16), ((CHIPS, 2, rows, rows), f32),
        ((CHIPS, rows, 2 * HP), f32), ((16, w_query.shape[0], 6 * DH), bf16), ((16,) + w_out.shape, bf16),
    ]
    gathered = [
        ((CHIPS, rows, D), bf16), ((16, w_gate.shape[0], 2 * BLK), bf16), ((2,) + w_down.shape, bf16), ((CHIPS, rows, D), bf16),
    ]
    return pl.pallas_call(
        functools.partial(front_body, first_rows),
        in_specs=[SMEM] + [VMEM] * 6 + [ANYS] * 4,
        out_specs=[VMEM] * len(small) + [ANYS] * (len(large) + len(gathered)),
        out_shape=[jax.ShapeDtypeStruct(*shape) for shape in small + large + gathered],
        scratch_shapes=[pltpu.VMEM(*shape) for shape in large] + [
            pltpu.VMEM((CHIPS, rows, 2 * DH), bf16), dma((len(large),)),
            pltpu.VMEM((CHIPS, w_query.shape[0], 6 * DH), bf16), pltpu.VMEM((8, 128), f32), pltpu.VMEM((16,) + vec.shape, f32), pltpu.VMEM((VEC_ROWS, 128), f32), pltpu.VMEM((CHIPS, rows, D), bf16), pltpu.VMEM((rows + 8, rows), f32), pltpu.VMEM((CHIPS, rows, 2 * DH), bf16),
            pltpu.VMEM((rows, D), bf16), pltpu.VMEM((w_down.shape[0] // 2, D), bf16), dma, dma, dma((8,)), dma((8,)), dma((7,)),
        ] + [dma((8,))] * 10 + [dma((4,))] * 2 + [dma((8,))] * 8 + hop_sems() + side_sems() + hop_sems(),
        name="front",
        compiler_params=pltpu.CompilerParams(collective_id=2, has_side_effects=True, vmem_limit_bytes=56 * 2**20),
    )(length, vec, x, w_query, w_key, w_value, cotangent, w_out, w_gate, w_up, w_down)


def middle_body(
    len_ref, mix_ref, hn_ref, dy_ref, xn_ref, w_in_hbm, w_dn_hbm, wq_hbm, dy_own_ref, hmid_ref, gains_ref, wo_hbm,
    qkv_hbm, toep_ref, gain_ref, s_hbm, p_hbm, o_hbm, strips_ref,
    inner_ref, dhmid_ref, dxn_ref, gain_ffn_grad_ref, theta_ref, mixer_ref, gain_grad_ref, tiles_ref,
    w_in_ref, w_dn_ref, wq_ref, wo_ref, qkv_ref, s_ref, p_ref, o_ref, enter_sems,
    theta_sums, pad_ref, first_ref, second_ref, dboth_ref, parts_ref, dattn_ref, grads_ref, sent_ref, strips_in, gin_ref, gd_ref,
    half_in, half_d, near_in, near_d, dqkv_ref, gq_ref, go_ref, core_q, core_o, in_q, in_o,
    near3, in23, in33, local_sems, load_sems, strip_send, strip_recv, head_send, head_recv,
    core_send, core_recv, near_send, near_recv, gu_send, gu_recv, q_send, q_recv, *rest,
):
    scatter_args, scatter3_sems, side = rest[:11], rest[11:17], rest[17:]
    seqs, rows, _ = hn_ref.shape
    g, a, b, c, y = (lax.axis_index(axis) for axis in ALL)
    me = chip_index()
    pairs = [(1 - y) * 2 + 1 - a, (1 - y) * 2 + a, y * 2 + 1 - a, y * 2 + a]
    loads = []
    for at, pair in enumerate(pairs):
        two = pl.ds(pair * 2, 2)
        loads.append(
            [
                pltpu.make_async_copy(hn_ref.at[two], first_ref.at[two], load_sems.at[at]),
                pltpu.make_async_copy(dy_ref.at[two], second_ref.at[two], load_sems.at[4 + at]),
            ]
        )
    enter = [
        pltpu.make_async_copy(src, dst, enter_sems.at[at])
        for at, (src, dst) in enumerate(
            (
                (w_in_hbm, w_in_ref), (w_dn_hbm, w_dn_ref), (wo_hbm, wo_ref), (qkv_hbm, qkv_ref), (s_hbm, s_ref),
                (p_hbm, p_ref), (o_hbm, o_ref), (wq_hbm, wq_ref),
            )
        )
    ]
    enter[0].start()
    for copies in loads:
        for copy in copies:
            copy.start()
    for copy in enter[1:]:
        copy.start()
    strip_local = pltpu.make_async_copy(strips_ref.at[me], strips_in.at[me], local_sems.at[0])
    strip_local.start()
    greet_all()
    chips = (7, 6, 5, 3, 4, 2, 1)
    to_chip = {mask: flipped(me, [axis for axis in BITS if mask & BITS[axis]]) for mask in chips}
    strips_sent = [
        push(strips_ref.at[to_chip[mask]], strips_in.at[me], strip_send.at[mask], strip_recv.at[mask], chip_at(mask))
        for mask in chips
    ]

    def hidden(pair):
        two = pl.ds(pair * 2, 2)
        both = dot(first_ref[two].reshape(2 * rows, D), w_in_ref[...])
        gate, up = both[:, :BLK], both[:, BLK:]
        dinner = dot_nt(second_ref[two].reshape(2 * rows, D), w_dn_ref[...])
        sig = jax.nn.sigmoid(gate)
        silu = gate * sig
        inner_ref[two] = (silu * up).astype(bf16).reshape(2, rows, BLK)
        dgate = (dinner * up * (sig * (1.0 + gate * (1.0 - sig)))).astype(bf16)
        dup = (dinner * silu).astype(bf16)
        dboth_ref[two, :, 0:BLK] = dgate.reshape(2, rows, BLK)
        dboth_ref[two, :, BLK:] = dup.reshape(2, rows, BLK)
        back = dot_nt(dgate, w_in_ref[:, 0:BLK]) + dot_nt(dup, w_in_ref[:, BLK:])
        parts_ref[two] = back.astype(bf16).reshape(2, rows, D)

    def wait_load(at):
        for copy in loads[at]:
            copy.wait()

    wait_load(0)
    enter[0].wait()
    enter[1].wait()
    hidden(pairs[0])
    scatter = Scatter(parts_ref, *scatter_args)
    scatter.start()
    wait_load(1)
    wait_load(2)

    def two_more(step, carry):
        hidden((1 - y) * 2 + a + step * ((2 * y - 1) * 2 + 1 - a - a))
        return carry

    lax.fori_loop(0, 2, two_more, 0)
    scatter.onward()
    wait_load(3)
    hidden(pairs[3])

    def down_grad(col, carry):
        cols = pl.ds(pl.multiple_of(col * BLK, BLK), BLK)
        made = dot_tn(inner_ref[...].reshape(seqs * rows, BLK), second_ref[:, :, cols].reshape(seqs * rows, BLK))
        gd_ref[:, :, :, :, cols] = made.astype(bf16).reshape(2, CHIPS, 2, BLK // 32, BLK)
        return carry

    lax.fori_loop(0, ROW_TILES, down_grad, 0)
    to_core = [push(gd_ref.at[1 - c], half_d, core_send.at[0], core_recv.at[0], across("c"))]

    def in_grad(row, carry):
        values = first_ref[:, :, pl.ds(pl.multiple_of(row * BLK, BLK), BLK)].reshape(seqs * rows, BLK)
        for which in range(2):
            cols = slice(which * BLK, (which + 1) * BLK)
            made = dot_tn(values, dboth_ref[:, :, cols].reshape(seqs * rows, BLK))
            gin_ref[row, :, :, :, :, cols] = made.astype(bf16).reshape(2, CHIPS, 2, BLK // 32, BLK)
        return carry

    def in_to_core(row):
        to_core.append(push(gin_ref.at[row, 1 - c], half_in.at[row], core_send.at[1 + row], core_recv.at[1 + row], across("c")))

    in_grad(0, 0)
    in_to_core(0)
    to_core[0].wait_recv()

    def core_down(chip, carry):
        half_d[chip] = (half_d[chip].astype(f32) + gd_ref[c, chip].astype(f32)).astype(bf16)
        return carry

    lax.fori_loop(0, CHIPS, core_down, 0)
    to_near = [push(half_d.at[:, 1 - g], near_d, near_send.at[0], near_recv.at[0], across("g"))]
    scatter.last()
    lax.fori_loop(1, ROW_TILES, in_grad, 0)
    in_to_core(1)
    in_to_core(2)
    xn_load = pltpu.make_async_copy(xn_ref, first_ref, load_sems.at[8])
    xn_load.start()

    def core_rows(row):
        to_core[1 + row].wait_recv()

        def core_chip(chip, carry):
            half_in[row, chip] = (half_in[row, chip].astype(f32) + gin_ref[row, c, chip].astype(f32)).astype(bf16)
            return carry

        lax.fori_loop(0, CHIPS, core_chip, 0)
        to_near.append(push(half_in.at[row, :, 1 - g], near_in.at[row], near_send.at[1 + row], near_recv.at[1 + row], across("g")))

    core_rows(0)
    core_rows(1)
    core_rows(2)
    half = rows // 2
    gain_sum = jnp.zeros((1, D), f32)
    for part in range(2):
        here = pl.ds(part * half, half)
        grad = scatter.finish(part)
        values = hmid_ref[here]
        scale = rms(values)
        unit = values * scale
        inside = grad * gains_ref[1:2, :]
        gain_sum += jnp.sum(grad * unit, axis=0, keepdims=True)
        dhmid = scale * (inside - unit * jnp.mean(inside * unit, axis=-1, keepdims=True)) + dy_own_ref[here].astype(f32)
        dhmid_ref[here] = dhmid
        dattn_ref[here] = dhmid.astype(bf16)
    gain_ffn_grad_ref[...] = gain_sum

    for copy in enter[2:]:
        copy.wait()

    def grad_copy(to):
        return pltpu.make_async_remote_copy(
            src_ref=sent_ref.at[to], dst_ref=grads_ref.at[me], send_sem=head_send.at[to], recv_sem=head_recv.at[me],
            device_id={"y": lax.div(to, 4), "a": lax.rem(lax.div(to, 2), 2), "b": lax.rem(to, 2)},
        )

    def send_grad(step, carry):
        to = lax.rem(me + step, seqs)
        sent_ref[to] = dot_nt(dattn_ref[...], wo_ref[to]).astype(bf16)

        @pl.when(step > 0)
        def _():
            grad_copy(to).start()

        return carry

    lax.fori_loop(0, seqs, send_grad, 0)
    grads_ref[me] = sent_ref[me]
    gather = SideGather(dattn_ref, second_ref, *side)
    gather.start()

    pad_ref[rows : rows + 8, :] = jnp.zeros((8, rows), f32)
    theta_sums[...] = jnp.zeros_like(theta_sums)
    mixer_ref[...] = jnp.zeros_like(mixer_ref)
    gain_grad_ref[...] = jnp.zeros_like(gain_grad_ref)
    query_at = lax.broadcasted_iota(jnp.int32, (rows, rows), 0)
    key_at = lax.broadcasted_iota(jnp.int32, (rows, rows), 1)
    key_float = key_at.astype(f32)
    blank = jnp.zeros((rows, HP - DH), f32)

    def grad_arrived(step, carry):
        source = lax.rem(me + step, seqs)
        pltpu.make_async_copy(sent_ref.at[source], grads_ref.at[source], head_recv.at[source]).wait()
        return carry

    lax.fori_loop(1, seqs, grad_arrived, 0)

    def one(seq, carry):
        keep = (key_at <= query_at) & (key_float < len_ref[seq, 0:1, :])
        weights = [p_ref[seq, 0], p_ref[seq, 1]]
        grad_mixed, made = [], [None] * 6
        grads = grads_ref[seq].astype(f32)
        for head in range(2):
            cols = slice(head * HP, (head + 1) * HP)
            out = o_ref[seq, :, cols]
            grad = jnp.concatenate([grads[:, head * DH : (head + 1) * DH], blank], axis=1)
            scale = lax.rsqrt(jnp.sum(out * out, axis=-1, keepdims=True) * (1.0 / DH) + eps_norm)
            unit = out * scale
            gain_grad_ref[:, cols] += jnp.sum(grad * unit, axis=0, keepdims=True)
            inner = grad * gain_ref[:, cols]
            grad_out = scale * (inner - unit * (jnp.sum(inner * unit, axis=-1, keepdims=True) * (1.0 / DH)))
            grad_out = grad_out.astype(bf16)
            value = qkv_ref[seq, :, (4 + head) * HP : (5 + head) * HP]
            mixed = (
                mix_ref[2 * head : 2 * head + 1, :] * weights[0] + mix_ref[2 * head + 1 : 2 * head + 2, :] * weights[1]
            ).astype(bf16)
            made[4 + head] = dot_tn(mixed, grad_out)
            back = dot_nt(grad_out, value)
            grad_mixed.append(back)
            for source in range(2):
                mixer_ref[2 * head + source : 2 * head + source + 1, :] += jnp.sum(
                    back * weights[source], axis=0, keepdims=True
                )
        for head in range(2):
            grad_weight = mix_ref[head : head + 1, :] * grad_mixed[0] + mix_ref[2 + head : 3 + head, :] * grad_mixed[1]
            weight = weights[head]
            grad_conv = weight * (grad_weight - jnp.sum(weight * grad_weight, axis=-1, keepdims=True))
            wide = shifted_up(pad_ref, grad_conv).astype(bf16)
            theta_sums[head] += dot_tn(s_ref[seq, head], wide)
            grad_scores = jnp.zeros((rows, rows), f32)
            for lag in range(CQ):
                grad_scores += dot_nt(
                    wide[:, lag * rows : (lag + 1) * rows], toep_ref[head, lag * rows : (lag + 1) * rows, :]
                )
            grad_scores = jnp.where(keep, grad_scores * (1.0 / math.sqrt(DH)), 0.0).astype(bf16)
            query = qkv_ref[seq, :, head * HP : (head + 1) * HP]
            key = qkv_ref[seq, :, (2 + head) * HP : (3 + head) * HP]
            made[head] = dot(grad_scores, key)
            made[2 + head] = dot_tn(grad_scores, query)
        dqkv_ref[seq] = jnp.concatenate([part[:, :DH] for part in made], axis=1).astype(bf16)
        return carry

    lax.fori_loop(0, 4, one, 0)
    gather.onward()
    lax.fori_loop(4, seqs, one, 0)
    scatter.drain()
    tiles_sent = []

    tap_at = query_at - key_at + CK // 2

    def taps(at, carry):
        lag = lax.rem(at, CQ)
        values = theta_sums[lax.div(at, CQ), :, pl.ds(pl.multiple_of(lag * rows, rows), rows)]
        for tap in range(CK):
            theta_ref[pl.ds(at * CK + tap, 1), :] = jnp.sum(
                jnp.where(tap_at == tap, values, 0.0), axis=0, keepdims=True
            )
        return carry

    xn_load.wait()
    all_rows = seqs * rows

    def qkv_grad(row, carry):
        cols = pl.ds(pl.multiple_of(row * BLK, BLK), BLK)
        made = dot_tn(first_ref[:, :, cols].reshape(all_rows, BLK), dqkv_ref[...].reshape(all_rows, 6 * DH))
        gq_ref[row] = made.astype(bf16).reshape(2, CHIPS, 2, BLK // 32, 6 * DH)
        return carry

    lax.fori_loop(0, ROW_TILES, qkv_grad, 0)
    to_core.append(push(gq_ref.at[:, 1 - c], core_q, core_send.at[4], core_recv.at[4], across("c")))

    def input_part(at, carry):
        two = pl.ds(at * 2, 2)
        made = dot_nt(dqkv_ref[two].reshape(2 * rows, 6 * DH), wq_ref[...])
        parts_ref[two] = made.astype(bf16).reshape(2, rows, D)
        return carry

    lax.fori_loop(0, seqs // 2, input_part, 0)
    scatter3 = Scatter(parts_ref, near3, in23, in33, *scatter_args[3:5], *scatter3_sems)
    scatter3.start()
    lax.fori_loop(0, 2 * CQ, taps, 0)
    to_core[4].wait_recv()

    def core_chip_q(chip, carry):
        for row in range(ROW_TILES):
            core_q[row, chip] = (core_q[row, chip].astype(f32) + gq_ref[row, c, chip].astype(f32)).astype(bf16)
        return carry

    lax.fori_loop(0, CHIPS, core_chip_q, 0)
    slot = g * CHIPS + me
    order = (15, 14, 13, 11, 12, 10, 9, 8, 7, 6, 5, 3, 4, 2, 1)
    for mask in order:
        to = flipped(me, [axis for axis in BITS if mask & BITS[axis]])
        tiles_sent.append(
            push(core_q.at[:, to, other_bit("g", mask & 8)], in_q.at[slot], q_send.at[mask], q_recv.at[mask], wide_at(mask))
        )
    in_q[slot] = core_q[:, me, g]
    gather.last()
    to_near[0].wait_recv()

    def near_down(chip, carry):
        half_d[chip, g] = (half_d[chip, g].astype(f32) + near_d[chip].astype(f32)).astype(bf16)
        return carry

    lax.fori_loop(0, CHIPS, near_down, 0)
    base = 4 * ROW_TILES**2

    def spread(ref, cols, tile, which):
        for mask in chips:
            at = which * CHIPS + mask
            tiles_sent.append(
                push(ref.at[to_chip[mask], g, :, cols], tiles_ref.at[tile], gu_send.at[at], gu_recv.at[at], chip_at(mask))
            )
        tiles_ref[tile] = ref[me, g, :, cols]

    for col in range(ROW_TILES):
        spread(half_d, pl.ds(col * BLK, BLK), base + 2 * ROW_TILES * FF_TILES + me * ROW_TILES + col, 6 + col)
    scatter3.onward()
    gather.finish()
    strip_local.wait()
    for copy in strips_sent:
        copy.wait_recv()

    def out_grad(col, carry):
        cols = pl.ds(pl.multiple_of(col * BLK, BLK), BLK)
        made = dot_tn(strips_in[...].reshape(all_rows, 2 * DH), second_ref[:, :, cols].reshape(all_rows, BLK))
        go_ref[:, :, :, :, cols] = made.astype(bf16).reshape(ROW_TILES, 2, 2, BLK // 32, BLK)
        return carry

    lax.fori_loop(0, ROW_TILES, out_grad, 0)
    to_core.append(push(go_ref.at[:, 1 - c], core_o, core_send.at[5], core_recv.at[5], across("c")))

    def near_rows(row):
        to_near[1 + row].wait_recv()

        def near_chip(chip, carry):
            half_in[row, chip, g] = (half_in[row, chip, g].astype(f32) + near_in[row, chip].astype(f32)).astype(bf16)
            return carry

        lax.fori_loop(0, CHIPS, near_chip, 0)
        for which in range(2):
            spread(
                half_in.at[row], pl.ds(which * BLK, BLK), base + (which * ROW_TILES + row) * FF_TILES + me, 2 * row + which
            )

    near_rows(0)
    to_core[5].wait_recv()
    core_o[...] = (core_o[...].astype(f32) + go_ref[:, c].astype(f32)).astype(bf16)
    to_near.append(push(core_o.at[:, 1 - g], in_o, near_send.at[4], near_recv.at[4], across("g")))
    scatter3.last()
    near_rows(1)
    near_rows(2)
    dxn_ref[0:half] = scatter3.finish(0)
    dxn_ref[half:] = scatter3.finish(1)

    def three_tiles(at, values):
        for col in range(ROW_TILES):
            tiles_ref[at + col] = values[:, col * BLK : (col + 1) * BLK].astype(bf16)

    to_near[4].wait_recv()
    for row in range(ROW_TILES):
        three_tiles(3 * ROW_TILES**2 + row * ROW_TILES, in_o[row].astype(f32) + core_o[row, g].astype(f32))
    for copy in tiles_sent:
        copy.wait_recv()
    for row in range(ROW_TILES):
        sums = [in_q[chip, row].astype(f32) + in_q[CHIPS + chip, row].astype(f32) for chip in range(CHIPS)]
        for which in range(3):
            three_tiles(
                which * ROW_TILES**2 + row * ROW_TILES,
                jnp.concatenate([part[:, which * 2 * DH : (which + 1) * 2 * DH] for part in sums], axis=1),
            )
    tiles_ref[tiles_ref.shape[0] - 1] = jnp.zeros(tiles_ref.shape[1:], bf16)

    def grad_left(step, carry):
        grad_copy(lax.rem(me + step, seqs)).wait_send()
        return carry

    lax.fori_loop(1, seqs, grad_left, 0)
    gather.drain()
    scatter3.drain()
    for copy in strips_sent + to_core + to_near + tiles_sent:
        copy.wait_send()


def chip_at(mask):
    return {axis: 1 - lax.axis_index(axis) for axis in BITS if mask & BITS[axis]}


def wide_at(mask):
    at = chip_at(mask & 7)
    if mask & 8:
        at["g"] = 1 - lax.axis_index("g")
    return at


def run_middle(
    lengths, mix, hn, dy, xn, w_in, w_dn, w_qkv, dy_own, hmid, gain_ffn, w_o, qkv, toep, gain, scores, weights, outs, strips
):
    seqs, rows, _ = hn.shape
    dma = pltpu.SemaphoreType.DMA
    part = BLK // 32
    tiles = 4 * ROW_TILES**2 + 3 * ROW_TILES * FF_TILES
    shapes = [
        ((seqs, rows, BLK), bf16), ((rows, D), f32), ((rows, D), f32), ((1, D), f32), ((2 * CQ * CK, rows), f32),
        ((8, rows), f32), ((1, 2 * HP), f32), ((tiles + 1, part, BLK), bf16),
    ]

    def low(*dims):
        return pltpu.VMEM(dims, bf16)

    every, heads = low(CHIPS, rows, D), low(CHIPS, rows, 2 * DH)
    return pl.pallas_call(
        middle_body,
        in_specs=[VMEM] * 2 + [ANYS] * 6 + [VMEM] * 3 + [ANYS] * 2 + [VMEM] * 2 + [ANYS] * 3 + [VMEM],
        out_specs=[VMEM] * len(shapes),
        out_shape=[jax.ShapeDtypeStruct(*shape) for shape in shapes],
        scratch_shapes=[pltpu.VMEM(a.shape, a.dtype) for a in (w_in, w_dn, w_qkv, w_o, qkv, scores, weights, outs)] + [
            dma((8,)),
            pltpu.VMEM((2, rows, CQ * rows), f32), pltpu.VMEM((rows + 8, rows), f32), every, every, low(seqs, rows, 2 * BLK), every, low(rows, D), heads, heads, heads,
            low(ROW_TILES, 2, CHIPS, 2, part, 2 * BLK), low(2, CHIPS, 2, part, D),
            low(ROW_TILES, CHIPS, 2, part, 2 * BLK), low(CHIPS, 2, part, D),
            low(ROW_TILES, CHIPS, part, 2 * BLK), low(CHIPS, part, D),
            low(seqs, rows, 6 * DH), low(ROW_TILES, 2, CHIPS, 2, part, 6 * DH), low(ROW_TILES, 2, 2, part, D),
            low(ROW_TILES, CHIPS, 2, part, 6 * DH), low(ROW_TILES, 2, part, D),
            low(2 * CHIPS, ROW_TILES, part, 6 * DH), low(ROW_TILES, part, D),
            low(3, rows, D), low(rows, D), low(3, rows, D), dma((1,)), dma((9,)),
        ] + [dma((8,))] * 4 + [dma((6,))] * 2 + [dma((5,))] * 2 + [dma((9 * CHIPS,))] * 2 + [dma((16,))] * 2
        + scatter_scratch(rows, D) + [dma((3,))] * 2 + [dma((3, 2))] * 4 + side_sems(),
        name="middle",
        compiler_params=pltpu.CompilerParams(collective_id=3, has_side_effects=True, vmem_limit_bytes=63 * 2**20),
    )(
        lengths, mix, hn, dy, xn, w_in, w_dn, w_qkv, dy_own, hmid, gain_ffn, w_o,
        qkv, toep, gain, scores, weights, outs, strips,
    )


def to_slots_body(
    pick_ref, tiles_ref, vec_ref, inner_hbm, w_dn_hbm, hmid_hbm, out_ref, vecs_ref, layer_ref,
    inner_ref, w_dn_ref, hmid_ref, enter_sems, slots_ref, parts_ref, local_sems, send, recv, vec_send, vec_recv, *scatter_args,
):
    devices = lax.axis_size(ALL)
    own_slots, side = out_ref.shape[:2]
    part = slots_ref.shape[1]
    enter = [
        pltpu.make_async_copy(src, dst, enter_sems.at[at])
        for at, (src, dst) in enumerate(((inner_hbm, inner_ref), (w_dn_hbm, w_dn_ref), (hmid_hbm, hmid_ref)))
    ]
    for copy in enter:
        copy.start()

    def fill(at, carry):
        slots_ref[at] = tiles_ref[pick_ref[at]]
        return carry

    lax.fori_loop(0, slots_ref.shape[0], fill, 0)
    me = device_index()
    place = (lax.axis_index("c") * CHIPS + chip_index()) * 2 + lax.axis_index("g")
    rows = pl.ds(pl.multiple_of(place * part, part), part)
    local = [pltpu.make_async_copy(vec_ref.at[me], vecs_ref.at[me], local_sems.at[0])]
    for slot in range(own_slots):
        local.append(
            pltpu.make_async_copy(
                slots_ref.at[me * own_slots + slot], out_ref.at[slot, rows], local_sems.at[1 + slot]
            )
        )
    for copy in local:
        copy.start()
    greet_all()

    def push_all(step, carry):
        to = lax.rem(me + step, devices)
        pltpu.make_async_remote_copy(
            src_ref=vec_ref.at[to], dst_ref=vecs_ref.at[me], send_sem=vec_send, recv_sem=vec_recv, device_id=device_at(to)
        ).start()
        pltpu.make_async_remote_copy(
            src_ref=slots_ref.at[pl.ds(to * own_slots, own_slots)], dst_ref=out_ref.at[:, rows],
            send_sem=send, recv_sem=recv, device_id=device_at(to),
        ).start()
        return carry

    lax.fori_loop(devices // 4, devices, push_all, 0)
    lax.fori_loop(1, devices // 4, push_all, 0)

    seqs, length = inner_ref.shape[:2]
    for copy in enter:
        copy.wait()

    def outputs(at, carry):
        two = pl.ds(at * 2, 2)
        made = dot(inner_ref[two].reshape(2 * length, BLK), w_dn_ref[...])
        parts_ref[two] = made.astype(bf16).reshape(2, length, D)
        return carry

    lax.fori_loop(0, seqs // 2, outputs, 0)
    scatter = SideScatter(parts_ref, *scatter_args)
    scatter.start()
    scatter.onward()
    scatter.last()
    layer_ref[...] = (hmid_ref[...] + scatter.finish()).astype(bf16)
    scatter.drain()
    others = vecs_ref.at[pl.ds(0, devices - 1)]
    pltpu.make_async_copy(others, others, vec_recv).wait()
    pltpu.make_async_copy(others, others, vec_send).wait()
    others = out_ref.at[:, pl.ds(0, side - part)]
    pltpu.make_async_copy(others, others, recv).wait()
    pltpu.make_async_copy(others, others, send).wait()
    for copy in local:
        copy.wait()


def to_slots(pick, tiles, vecs, inner, w_dn, hmid, own_slots):
    rows = hmid.shape[0]
    dma = pltpu.SemaphoreType.DMA
    return pl.pallas_call(
        to_slots_body,
        in_specs=[SMEM, VMEM] + [ANYS] * 4,
        out_specs=[ANYS] * 2 + [VMEM],
        out_shape=[
            jax.ShapeDtypeStruct((own_slots, BLK, BLK), bf16), jax.ShapeDtypeStruct(vecs.shape, vecs.dtype),
            jax.ShapeDtypeStruct(hmid.shape, bf16),
        ],
        scratch_shapes=[pltpu.VMEM(a.shape, a.dtype) for a in (inner, w_dn, hmid)] + [
            dma((3,)), pltpu.VMEM((pick.shape[0],) + tiles.shape[1:], bf16), pltpu.VMEM((CHIPS, rows, D), bf16), dma((1 + own_slots,)),
        ] + [dma] * 4 + side_scatter_scratch(rows, D),
        name="to_slots",
        compiler_params=pltpu.CompilerParams(collective_id=6, has_side_effects=True, vmem_limit_bytes=60 * 2**20),
    )(pick, tiles, vecs, inner, w_dn, hmid)


def update_body(grad_ref, left_ref, right_ref, master_ref, first_ref, second_ref, first_out, second_out, master_out, copy_out):
    left, right = left_ref[0].astype(bf16), right_ref[0].astype(bf16)
    rotated = dot(dot_tn(left, grad_ref[0]).astype(bf16), right)
    first = beta_first * first_ref[0] + (1.0 - beta_first) * rotated
    second = beta_second * second_ref[0] + (1.0 - beta_second) * rotated * rotated
    first_out[0] = first
    second_out[0] = second
    direction = (first / (jnp.sqrt(second) + eps_adam)).astype(bf16)
    turned = dot_nt(dot(left, direction).astype(bf16), right)
    master = master_ref[0]
    master = master - rate_block * (turned + decay_block * master)
    master_out[0] = master
    copy_out[0] = master.astype(bf16)


def update(grad, left, right, master, first, second):
    spec = pl.BlockSpec((1, BLK, BLK), lambda slot: (slot, 0, 0))
    return pl.pallas_call(
        update_body,
        grid=(grad.shape[0],),
        in_specs=[spec] * 6,
        out_specs=[spec] * 4,
        out_shape=[jax.ShapeDtypeStruct(grad.shape, kind) for kind in (f32, f32, f32, bf16)],
        name="update",
        compiler_params=pltpu.CompilerParams(vmem_limit_bytes=60 * 2**20),
        cost_estimate=pl.CostEstimate(flops=43 * 10**8, bytes_accessed=36 * 2**20, transcendentals=10**6),
    )(grad, left, right, master, first, second)


def body_fast(
    layer_input, lengths, cotangent, w_query, w_key, w_value, w_out, w_gate, w_up, w_down, vec_copy, owners,
    basis_left, basis_right, block_master, block_first, block_second, vec_master, vec_first, vec_second,
):
    chip = chip_index()
    seq_len = layer_input.shape[0]
    own_vec = vec_copy.shape[0]
    devices, fs_size, reps = lax.axis_size(ALL), lax.axis_size(FS), lax.axis_size("y")

    fs_index = ((lax.axis_index("g") * 2 + lax.axis_index("a")) * 2 + lax.axis_index("b")) * 2 + lax.axis_index("c")
    first_rows = vector_rows(own_vec, fs_size)
    flat = lax.dynamic_update_slice_in_dim(jnp.zeros((fs_size * own_vec,), f32), vec_copy.astype(f32), fs_index * own_vec, 0)
    first = sum(
        (first_rows[at] - first_rows[at - 1]) * (fs_index >= at).astype(jnp.int32)
        for at in range(1, fs_size) if first_rows[at] != first_rows[at - 1]
    )
    vec = lax.dynamic_slice_in_dim(rows_of_vector(flat), first, SHARD_ROWS, 0)

    (
        dy, group_lengths, mix, gains, toep, gain_pair, strips, hmid, xn, qkv, scores, weights, outs, w_qkv, w_out_all,
        hn_rows, w_in, w_dn, dy_rows,
    ) = run_front(
        first_rows, lengths, vec, layer_input, w_query, w_key, w_value, cotangent, w_out, w_gate, w_up, w_down
    )
    gain_attn = gains[0]
    w_qkv = w_qkv.reshape(D, 6 * DH)
    w_in, w_dn = w_in.reshape(D, 2 * BLK), w_dn.reshape(BLK, D)
    input_float = layer_input.astype(f32)
    input_scale = rms(input_float)

    own_slots = basis_left.shape[0]
    matches = jnp.arange(own_slots * devices)[:, None] == owners[None, :]
    tile_count = owners.shape[0]
    pick = jnp.min(jnp.where(matches, jnp.arange(tile_count, dtype=jnp.int32)[None, :], tile_count), axis=1)
    inner, dhmid, dxn, grad_gain_ffn, theta_sums, mixer_sums, gain_sums, tiles = run_middle(
        group_lengths, mix, hn_rows, dy_rows, xn, w_in, w_dn, w_qkv, dy, hmid, gains,
        w_out_all.reshape(CHIPS, 2 * DH, D), qkv, toep, gain_pair, scores, weights, outs, strips,
    )
    dinput, grad_gain_attn = norm_backward(input_float, input_scale, gain_attn, dxn)
    input_grad = dinput + dhmid

    grad_theta = jnp.sum(theta_sums, axis=1)
    grad_mixer = jnp.sum(mixer_sums[:4], axis=1)
    vector_grad = jnp.concatenate(
        [
            grad_gain_attn,
            lax.dynamic_update_slice_in_dim(
                jnp.zeros((D,), f32), gain_sums.reshape(2, HP)[:, :DH].reshape(-1), chip * 2 * DH, 0
            ),
            grad_gain_ffn.reshape(-1),
            lax.dynamic_update_slice_in_dim(
                jnp.zeros((H * CQ * CK,), f32), grad_theta.reshape(-1), chip * 2 * CQ * CK, 0
            ),
            lax.dynamic_update_slice_in_dim(jnp.zeros((2 * H,), f32), grad_mixer, chip * 4, 0),
        ]
    )
    pieces = jnp.pad(vector_grad.reshape(fs_size, 1, own_vec), ((0, 0), (0, 0), (0, 1024 - own_vec)))
    pieces = jnp.broadcast_to(pieces, (fs_size, reps, 1024)).reshape(devices, 8, 128)

    own_grad, pieces, layer_output = to_slots(
        pick, tiles, pieces, inner, w_dn, hmid, own_slots
    )
    vector_total = jnp.sum(pieces, axis=0).reshape(1024)[:own_vec]
    first_new, second_new, master_new, copy_new = update(
        own_grad, basis_left, basis_right, block_master, block_first, block_second
    )
    vec_first_new = beta_first * vec_first + (1.0 - beta_first) * vector_total
    vec_second_new = beta_second * vec_second + (1.0 - beta_second) * vector_total * vector_total
    vec_master_new = vec_master - rate_vector * vec_first_new / (jnp.sqrt(vec_second_new) + eps_adam)
    return (
        layer_output, input_grad, first_new, second_new, master_new, copy_new,
        vec_first_new, vec_second_new, vec_master_new, vec_master_new.astype(bf16),
    )


def solution(mesh):
    fsdp, rep = mesh.shape["fsdp"], mesh.shape["rep"]
    fine = Mesh(mesh.devices.reshape(fsdp // 8, 2, 2, 2, rep), ALL)
    rows, both = P(ALL, None), P(ALL, None, None)
    weight, vec = P(FS, None), P(FS)
    return jax.shard_map(
        body_fast if (fsdp, rep) == (16, 2) else body_any,
        mesh=fine,
        in_specs=(rows, P(ALL), rows) + (weight,) * 7 + (vec, P()) + (both,) * 5 + (vec,) * 3,
        out_specs=(rows, rows) + (both,) * 4 + (vec,) * 4,
        check_vma=False,
    )
```

```python
import functools
import math

import jax
import jax.numpy as jnp
import numpy as np
from jax import lax
from jax.experimental import pallas as pl
from jax.experimental.pallas import tpu as pltpu
from jax.sharding import Mesh
from jax.sharding import PartitionSpec as P

H = 16
DH = 96
HP = 128
D = H * DH
FF = 4096
CQ = 6
CK = 11
BLK = 512
CHIPS = 8
ROW_TILES = D // BLK
FF_TILES = FF // BLK

eps_norm = 1e-05
eps_adam = 1e-08
rate_block = 0.02
rate_vector = 0.3
decay_block = 0.1
beta_first = 0.5
beta_second = 0.5

FS = ("g", "a", "b", "c")
CHIP = ("y", "a", "b")
ALL = ("g", "a", "b", "c", "y")
bf16 = jnp.bfloat16
f32 = jnp.float32


def dot(left, right):
    return jnp.dot(left, right, preferred_element_type=f32)


def dot_nt(left, right):
    return lax.dot_general(left, right, (((1,), (1,)), ((), ())), preferred_element_type=f32)


def dot_tn(left, right):
    return lax.dot_general(left, right, (((0,), (0,)), ((), ())), preferred_element_type=f32)


def rms(values):
    return lax.rsqrt(jnp.mean(values * values, axis=-1, keepdims=True) + eps_norm)


def norm_backward(values, scale, gain, grad):
    unit = values * scale
    inner = grad * gain
    grad_values = scale * (inner - unit * jnp.mean(inner * unit, axis=-1, keepdims=True))
    return grad_values, jnp.sum(grad * unit, axis=0)


def shifted_down(pad_ref, values):
    rows = values.shape[0]
    pad_ref[8 : 8 + rows, :] = values
    return jnp.concatenate(
        [values] + [pad_ref[8 - lag : 8 - lag + rows, :] for lag in range(1, CQ)], axis=1
    )


def shifted_up(pad_ref, values):
    rows = values.shape[0]
    pad_ref[0:rows, :] = values
    return jnp.concatenate(
        [values] + [pad_ref[lag : lag + rows, :] for lag in range(1, CQ)], axis=1
    )


def attention_forward(len_ref, mix_ref, qkv_ref, toep_ref, gain_ref, heads_ref, s_ref, p_ref, o_ref, pad_ref):
    rows = qkv_ref.shape[1]
    length = len_ref[pl.program_id(0)]
    query_at = lax.broadcasted_iota(jnp.int32, (rows, rows), 0)
    key_at = lax.broadcasted_iota(jnp.int32, (rows, rows), 1)
    keep = (key_at <= query_at) & (key_at < length)
    pad_ref[0:8, :] = jnp.zeros((8, rows), f32)
    weights = []
    for head in range(2):
        query = qkv_ref[0, :, head * HP : (head + 1) * HP]
        key = qkv_ref[0, :, (2 + head) * HP : (3 + head) * HP]
        scores = jnp.where(keep, dot_nt(query, key) * (1.0 / math.sqrt(DH)), 0.0)
        s_ref[0, head] = scores.astype(bf16)
        wide = shifted_down(pad_ref, scores)
        high = wide.astype(bf16)
        low = (wide - high.astype(f32)).astype(bf16)
        conv = dot(high, toep_ref[head]) + dot(low, toep_ref[head])
        logits = jnp.where(keep, conv, -1e30)
        weight = jnp.exp(logits - jnp.max(logits, axis=-1, keepdims=True))
        weight = weight / jnp.sum(weight, axis=-1, keepdims=True)
        p_ref[0, head] = weight
        weights.append(weight)
    for head in range(2):
        mixed = mix_ref[2 * head] * weights[0] + mix_ref[2 * head + 1] * weights[1]
        value = qkv_ref[0, :, (4 + head) * HP : (5 + head) * HP]
        out = dot(mixed.astype(bf16), value)
        o_ref[0, :, head * HP : (head + 1) * HP] = out
        scale = lax.rsqrt(jnp.sum(out * out, axis=-1, keepdims=True) * (1.0 / DH) + eps_norm)
        heads_ref[0, :, head * HP : (head + 1) * HP] = (
            out * scale * gain_ref[:, head * HP : (head + 1) * HP]
        ).astype(bf16)


def attention_backward(
    len_ref, mix_ref, qkv_ref, toep_ref, gain_ref, s_ref, p_ref, o_ref, grad_ref,
    dqkv_ref, theta_ref, mixer_ref, gain_grad_ref, pad_ref,
):
    rows = qkv_ref.shape[1]
    length = len_ref[pl.program_id(0)]
    query_at = lax.broadcasted_iota(jnp.int32, (rows, rows), 0)
    key_at = lax.broadcasted_iota(jnp.int32, (rows, rows), 1)
    keep = (key_at <= query_at) & (key_at < length)
    pad_ref[rows : rows + 8, :] = jnp.zeros((8, rows), f32)

    @pl.when(pl.program_id(0) == 0)
    def _():
        theta_ref[...] = jnp.zeros_like(theta_ref)
        mixer_ref[...] = jnp.zeros_like(mixer_ref)
        gain_grad_ref[...] = jnp.zeros_like(gain_grad_ref)

    weights = [p_ref[0, 0], p_ref[0, 1]]
    grad_mixed = []
    for head in range(2):
        cols = slice(head * HP, (head + 1) * HP)
        out = o_ref[0, :, cols]
        grad = grad_ref[0, :, cols].astype(f32)
        scale = lax.rsqrt(jnp.sum(out * out, axis=-1, keepdims=True) * (1.0 / DH) + eps_norm)
        unit = out * scale
        gain_grad_ref[:, cols] += jnp.sum(grad * unit, axis=0, keepdims=True)
        inner = grad * gain_ref[:, cols]
        grad_out = scale * (inner - unit * (jnp.sum(inner * unit, axis=-1, keepdims=True) * (1.0 / DH)))
        grad_out = grad_out.astype(bf16)
        value = qkv_ref[0, :, (4 + head) * HP : (5 + head) * HP]
        mixed = (mix_ref[2 * head] * weights[0] + mix_ref[2 * head + 1] * weights[1]).astype(bf16)
        dqkv_ref[0, :, (4 + head) * HP : (5 + head) * HP] = dot_tn(mixed, grad_out).astype(bf16)
        back = dot_nt(grad_out, value)
        grad_mixed.append(back)
        for source in range(2):
            mixer_ref[2 * head + source : 2 * head + source + 1, :] += jnp.sum(
                back * weights[source], axis=0, keepdims=True
            )
    for head in range(2):
        grad_weight = mix_ref[head] * grad_mixed[0] + mix_ref[2 + head] * grad_mixed[1]
        weight = weights[head]
        grad_conv = weight * (grad_weight - jnp.sum(weight * grad_weight, axis=-1, keepdims=True))
        wide = shifted_up(pad_ref, grad_conv).astype(bf16)
        theta_ref[head] += dot_tn(s_ref[0, head], wide)
        grad_scores = jnp.zeros((rows, rows), f32)
        for lag in range(CQ):
            grad_scores += dot_nt(
                wide[:, lag * rows : (lag + 1) * rows], toep_ref[head, lag * rows : (lag + 1) * rows, :]
            )
        grad_scores = jnp.where(keep, grad_scores * (1.0 / math.sqrt(DH)), 0.0).astype(bf16)
        query = qkv_ref[0, :, head * HP : (head + 1) * HP]
        key = qkv_ref[0, :, (2 + head) * HP : (3 + head) * HP]
        dqkv_ref[0, :, head * HP : (head + 1) * HP] = dot(grad_scores, key).astype(bf16)
        dqkv_ref[0, :, (2 + head) * HP : (3 + head) * HP] = dot_tn(grad_scores, query).astype(bf16)


SMEM = pl.BlockSpec(memory_space=pltpu.SMEM)


def seq_spec(*dims):
    return pl.BlockSpec((1,) + dims, lambda s: (s,) + (0,) * len(dims))


def whole_spec(*dims):
    return pl.BlockSpec(dims, lambda s: (0,) * len(dims))


def run_forward(lengths, mix, qkv, toep, gain):
    seqs, rows, _ = qkv.shape
    return pl.pallas_call(
        attention_forward,
        grid=(seqs,),
        in_specs=[SMEM, SMEM, seq_spec(rows, 6 * HP), whole_spec(2, CQ * rows, rows), whole_spec(1, 2 * HP)],
        out_specs=[seq_spec(rows, 2 * HP), seq_spec(2, rows, rows), seq_spec(2, rows, rows), seq_spec(rows, 2 * HP)],
        out_shape=[
            jax.ShapeDtypeStruct((seqs, rows, 2 * HP), bf16),
            jax.ShapeDtypeStruct((seqs, 2, rows, rows), bf16),
            jax.ShapeDtypeStruct((seqs, 2, rows, rows), f32),
            jax.ShapeDtypeStruct((seqs, rows, 2 * HP), f32),
        ],
        scratch_shapes=[pltpu.VMEM((rows + 8, rows), f32)],
        name="attention_forward",
        compiler_params=pltpu.CompilerParams(vmem_limit_bytes=24 * 2**20),
        cost_estimate=pl.CostEstimate(flops=2 * 10**9, bytes_accessed=8 * 2**20, transcendentals=10**5),
    )(lengths, mix, qkv, toep, gain)


def run_backward(lengths, mix, qkv, toep, gain, scores, weights, outs, grads):
    seqs, rows, _ = qkv.shape
    return pl.pallas_call(
        attention_backward,
        grid=(seqs,),
        in_specs=[
            SMEM, SMEM, seq_spec(rows, 6 * HP), whole_spec(2, CQ * rows, rows), whole_spec(1, 2 * HP),
            seq_spec(2, rows, rows), seq_spec(2, rows, rows), seq_spec(rows, 2 * HP), seq_spec(rows, 2 * HP),
        ],
        out_specs=[seq_spec(rows, 6 * HP), whole_spec(2, rows, CQ * rows), whole_spec(8, rows), whole_spec(1, 2 * HP)],
        out_shape=[
            jax.ShapeDtypeStruct((seqs, rows, 6 * HP), bf16),
            jax.ShapeDtypeStruct((2, rows, CQ * rows), f32),
            jax.ShapeDtypeStruct((8, rows), f32),
            jax.ShapeDtypeStruct((1, 2 * HP), f32),
        ],
        scratch_shapes=[pltpu.VMEM((rows + 8, rows), f32)],
        name="attention_backward",
        compiler_params=pltpu.CompilerParams(vmem_limit_bytes=24 * 2**20),
        cost_estimate=pl.CostEstimate(flops=4 * 10**9, bytes_accessed=12 * 2**20, transcendentals=10**5),
    )(lengths, mix, qkv, toep, gain, scores, weights, outs, grads)


BITS = {"y": 4, "a": 2, "b": 1}
HOPS = (("y", "b", "a"), ("a", "y", "b"), ("b", "a", "y"))
THIRDS = ((0, 48), (48, 48), (96, 32))
ANYS = pl.BlockSpec(memory_space=pl.ANY)


def chip_index():
    return (lax.axis_index("y") * 2 + lax.axis_index("a")) * 2 + lax.axis_index("b")


def flipped(chip, axes):
    for axis in axes:
        chip = chip + BITS[axis] * (1 - 2 * lax.axis_index(axis))
    return chip


def across(axis):
    return {axis: 1 - lax.axis_index(axis)}


def device_index():
    index = lax.axis_index("g")
    for axis in ("a", "b", "c", "y"):
        index = index * lax.axis_size(axis) + lax.axis_index(axis)
    return index


def device_at(index):
    at = {}
    for axis in ("y", "c", "b", "a", "g"):
        at[axis] = lax.rem(index, lax.axis_size(axis))
        index = lax.div(index, lax.axis_size(axis))
    return at


def greet_all():
    devices = lax.axis_size(ALL)
    me = device_index()
    barrier = pltpu.get_barrier_semaphore()

    def greet(step, carry):
        pl.semaphore_signal(barrier, inc=1, device_id=device_at(lax.rem(me + step, devices)))
        return carry

    lax.fori_loop(1, devices, greet, 0)
    pl.semaphore_wait(barrier, devices - 1)


def greet_neighbours():
    barrier = pltpu.get_barrier_semaphore()
    for axis in BITS:
        pl.semaphore_signal(barrier, inc=1, device_id=across(axis))
    pl.semaphore_wait(barrier, 3)


def remote(src, dst, send, recv, axis):
    return pltpu.make_async_remote_copy(src_ref=src, dst_ref=dst, send_sem=send, recv_sem=recv, device_id=across(axis))


def gather_body(x_ref, out_ref, *sems):
    greet_neighbours()
    gather_hops(x_ref, out_ref, *sems)


def gather_first_body(x_ref, vec_ref, out_ref, vecs_ref, vec_send, vec_recv, vec_local, *sems):
    devices = lax.axis_size(ALL)
    me = device_index()
    local = pltpu.make_async_copy(vec_ref, vecs_ref.at[me], vec_local)
    local.start()
    greet_all()

    def push(step, carry):
        pltpu.make_async_remote_copy(
            src_ref=vec_ref, dst_ref=vecs_ref.at[me], send_sem=vec_send, recv_sem=vec_recv,
            device_id=device_at(lax.rem(me + step, devices)),
        ).start()
        return carry

    lax.fori_loop(1, devices, push, 0)
    gather_hops(x_ref, out_ref, *sems)
    others = vecs_ref.at[pl.ds(0, devices - 1)]
    pltpu.make_async_copy(others, others, vec_recv).wait()
    pltpu.make_async_copy(others, others, vec_send).wait()
    local.wait()


def gather_hops(x_ref, out_ref, local_sem, send1, recv1, send2, recv2, send3, recv3):
    me = chip_index()
    rows = x_ref.shape[0]
    half = rows // 2
    local = pltpu.make_async_copy(x_ref, out_ref.at[me], local_sem)
    local.start()
    first = []
    for part in range(2):
        here = pl.ds(part * half, half)
        for at, (axis, _, _) in enumerate(HOPS):
            copy = remote(x_ref.at[here], out_ref.at[me, here], send1.at[at, part], recv1.at[at, part], axis)
            copy.start()
            first.append(copy)
    second = []
    for part in range(2):
        here = pl.ds(part * half, half)
        for at, (axis, onward, _) in enumerate(HOPS):
            first[part * 3 + at].wait_recv()
            block = out_ref.at[flipped(me, (axis,)), here]
            copy = remote(block, block, send2.at[at, part], recv2.at[at, part], onward)
            copy.start()
            second.append(copy)
    third = []
    for at, (axis, onward, last) in enumerate(HOPS):
        begin, count = THIRDS[at]
        block = flipped(me, (axis, onward))
        for part in range(2):
            if part * half < begin + count and begin < (part + 1) * half:
                second[part * 3 + at].wait_recv()
        piece = out_ref.at[block, pl.ds(begin, count)]
        copy = remote(piece, piece, send3.at[at], recv3.at[at], last)
        copy.start()
        third.append(copy)
    for at in range(3):
        begin, count = THIRDS[at]
        for part in range(2):
            if not (part * half < begin + count and begin < (part + 1) * half):
                second[part * 3 + at].wait_recv()
    for copy in third:
        copy.wait_recv()
    for copy in first + second + third:
        copy.wait_send()
    local.wait()


def hop_sems():
    dma = pltpu.SemaphoreType.DMA
    return [dma] + [dma((3, 2))] * 4 + [dma((3,))] * 2


def gather_first(rows, vec, collective_id):
    count, width = rows.shape
    return pl.pallas_call(
        gather_first_body,
        in_specs=[ANYS, ANYS],
        out_specs=[ANYS, ANYS],
        out_shape=[
            jax.ShapeDtypeStruct((CHIPS, count, width), rows.dtype),
            jax.ShapeDtypeStruct((lax.axis_size(ALL),) + vec.shape, vec.dtype),
        ],
        scratch_shapes=[pltpu.SemaphoreType.DMA] * 3 + hop_sems(),
        name="gather_first",
        compiler_params=pltpu.CompilerParams(collective_id=collective_id, has_side_effects=True),
    )(rows, vec)


def gather_chips(rows, collective_id):
    count, width = rows.shape
    return pl.pallas_call(
        gather_body,
        in_specs=[ANYS],
        out_specs=ANYS,
        out_shape=jax.ShapeDtypeStruct((CHIPS, count, width), rows.dtype),
        scratch_shapes=hop_sems(),
        name="gather_chips",
        compiler_params=pltpu.CompilerParams(collective_id=collective_id, has_side_effects=True),
    )(rows)


def scatter_body(
    parts_ref, out_ref, near_ref, in2_ref, in3_ref, acc2_ref, acc3_ref, send1, recv1, send2, recv2, send3, recv3
):
    me = chip_index()
    greet_neighbours()
    opposite = flipped(me, ("y", "a", "b"))
    first = []
    for at, (axis, onward, last) in enumerate(HOPS):
        begin, count = THIRDS[at]
        copy = remote(parts_ref.at[opposite, pl.ds(begin, count)], in2_ref.at[pl.ds(begin, count)], send1.at[at], recv1.at[at], last)
        copy.start()
        first.append(copy)
    second = []
    rows = parts_ref.shape[1]
    half = rows // 2
    for part in range(2):
        here = pl.ds(part * half, half)
        for at, (axis, onward, last) in enumerate(HOPS):
            dest = flipped(me, (axis, onward))
            begin, count = THIRDS[at]
            if part == 0:
                first[at].wait_recv()
                acc2_ref[at] = parts_ref[dest]
                piece = pl.ds(begin, count)
                acc2_ref[at, piece] = (parts_ref[dest, piece].astype(f32) + in2_ref[piece].astype(f32)).astype(bf16)
            copy = remote(acc2_ref.at[at, here], in3_ref.at[at, here], send2.at[at, part], recv2.at[at, part], onward)
            copy.start()
            second.append(copy)
    third = []
    for part in range(2):
        here = pl.ds(part * half, half)
        for at, (axis, onward, last) in enumerate(HOPS):
            dest = flipped(me, (axis,))
            second[part * 3 + at].wait_recv()
            acc3_ref[at, here] = (parts_ref[dest, here].astype(f32) + in3_ref[at, here].astype(f32)).astype(bf16)
            copy = remote(acc3_ref.at[at, here], near_ref.at[at, here], send3.at[at, part], recv3.at[at, part], axis)
            copy.start()
            third.append(copy)
    for part in range(2):
        here = pl.ds(part * half, half)
        for at in range(3):
            third[part * 3 + at].wait_recv()
        out_ref[here] = (
            (parts_ref[me, here].astype(f32) + near_ref[0, here].astype(f32))
            + (near_ref[1, here].astype(f32) + near_ref[2, here].astype(f32))
        )
    for copy in first + second + third:
        copy.wait_send()


def scatter_chips(parts, collective_id):
    _, rows, width = parts.shape
    vmem = pl.BlockSpec(memory_space=pltpu.VMEM)
    dma = pltpu.SemaphoreType.DMA
    return pl.pallas_call(
        scatter_body,
        in_specs=[vmem],
        out_specs=vmem,
        out_shape=jax.ShapeDtypeStruct((rows, width), f32),
        scratch_shapes=[pltpu.VMEM((3, rows, width), bf16), pltpu.VMEM((rows, width), bf16)] + [pltpu.VMEM((3, rows, width), bf16)] * 3
        + [dma((3,))] * 2 + [dma((3, 2))] * 4,
        name="scatter_chips",
        compiler_params=pltpu.CompilerParams(collective_id=collective_id, has_side_effects=True, vmem_limit_bytes=32*2**20),
    )(parts)


def gather_slow(rows):
    return lax.all_to_all(
        jnp.broadcast_to(rows[None], (CHIPS,) + rows.shape), CHIP, split_axis=0, concat_axis=0, tiled=True
    )


def exchange_chips(parts):
    return lax.all_to_all(parts, CHIP, split_axis=0, concat_axis=0, tiled=True)


def scatter_slow(parts):
    return jnp.sum(exchange_chips(parts.astype(bf16)).astype(f32), axis=0)


def swap(values, axis):
    return lax.ppermute(values, axis, [(0, 1), (1, 0)])


def both_cores(own, axis):
    other = swap(own, "c")
    first = lax.axis_index("c") == 0
    return jnp.stack([jnp.where(first, own, other), jnp.where(first, other, own)], axis=axis)


def half_for_core(values, axis):
    core = lax.axis_index("c")
    own = lax.dynamic_index_in_dim(values, core, axis, keepdims=False)
    sent = lax.dynamic_index_in_dim(values, 1 - core, axis, keepdims=False)
    return own + swap(sent.astype(bf16), "c").astype(f32)


def sum_groups(tiles):
    groups = lax.axis_size("g")
    if groups != 2:
        return lax.psum_scatter(tiles.astype(f32), "g", scatter_dimension=1, tiled=True).astype(bf16)
    part = tiles.shape[1] // 2
    group = lax.axis_index("g")
    own = lax.dynamic_slice_in_dim(tiles, group * part, part, 1)
    sent = lax.dynamic_slice_in_dim(tiles, (1 - group) * part, part, 1)
    return (own.astype(f32) + swap(sent, "g").astype(f32)).astype(bf16)


def spread_columns(weight, width):
    rows = weight.shape[0]
    blocks = weight.reshape(rows, 2, CHIPS // 2, width)
    mine = lax.dynamic_index_in_dim(blocks, lax.axis_index("y"), 1, keepdims=False)
    return jnp.transpose(mine, (1, 0, 2))


def to_columns(blocks):
    groups = lax.axis_size("g")
    sent = jnp.broadcast_to(blocks[None], (groups,) + blocks.shape).reshape((-1,) + blocks.shape[1:])
    got = lax.all_to_all(sent, ("g", "a", "b"), split_axis=0, concat_axis=0, tiled=True)
    return both_cores(got, 1).reshape(-1, blocks.shape[-1])


def down_rows(w_down, chip):
    if lax.axis_size("g") == 2:
        other = swap(w_down, "g")
        mine = jnp.where(lax.axis_index("g") == lax.axis_index("y"), w_down, other)
        return both_cores(mine, 0).reshape(BLK, D)
    return lax.dynamic_slice_in_dim(lax.all_gather(w_down, FS, axis=0, tiled=True), chip * BLK, BLK, 0)


def band():
    tap = np.arange(CK)[:, None, None]
    source = np.arange(128)[None, :, None]
    target = np.arange(128)[None, None, :]
    return source - target + CK // 2 == tap


def body_any(
    layer_input, lengths, cotangent, w_query, w_key, w_value, w_out, w_gate, w_up, w_down, vec_copy, owners,
    basis_left, basis_right, block_master, block_first, block_second, vec_master, vec_first, vec_second,
):
    chip = (lax.axis_index("y") * 2 + lax.axis_index("a")) * 2 + lax.axis_index("b")
    fs_index = ((lax.axis_index("g") * 2 + lax.axis_index("a")) * 2 + lax.axis_index("b")) * 2 + lax.axis_index("c")
    seq_len = layer_input.shape[0]
    length = lengths[0]
    reps = lax.axis_size("y")
    fs_size = lax.axis_size(FS)

    own_vec = vec_copy.shape[0]
    small = jnp.concatenate(
        [vec_copy.astype(f32), jnp.zeros((1023 - own_vec,), f32), length.astype(f32).reshape(1)]
    ).reshape(8, 128)
    x_all, small_all = gather_first(layer_input, small, 1)
    small_all = small_all.reshape(fs_size, reps, 1024)
    vector = small_all[:, 0, :own_vec].reshape(-1)
    group_lengths = small_all[:, :, 1023].reshape(-1, 2, 2, 2, reps)
    group_lengths = lax.dynamic_index_in_dim(group_lengths, lax.axis_index("g"), 0, keepdims=False)
    group_lengths = lax.dynamic_index_in_dim(group_lengths, lax.axis_index("c"), 2, keepdims=False)
    group_lengths = jnp.transpose(group_lengths, (2, 0, 1)).reshape(CHIPS).astype(jnp.int32)
    gain_attn, gain_head, gain_ffn = vector[:D], vector[D : 2 * D], vector[2 * D : 3 * D]
    conv_end = 3 * D + H * CQ * CK
    theta = lax.dynamic_slice_in_dim(vector[3 * D : conv_end].reshape(H, CQ, CK), chip * 2, 2, 0)
    mixer = lax.dynamic_slice_in_dim(vector[conv_end : conv_end + 2 * H].reshape(H, 2), chip * 2, 2, 0)
    mix = mixer.reshape(4)
    gain_pair = jnp.pad(
        lax.dynamic_slice_in_dim(gain_head.reshape(H, DH), chip * 2, 2, 0), ((0, 0), (0, HP - DH))
    ).reshape(1, 2 * HP)
    toep = jnp.zeros((2, CQ, seq_len, seq_len), f32)
    offset = (
        jnp.arange(seq_len, dtype=jnp.int32)[:, None] - jnp.arange(seq_len, dtype=jnp.int32)[None, :] + CK // 2
    )
    for tap in range(CK):
        toep = jnp.where(offset[None, None] == tap, theta[:, :, tap][:, :, None, None], toep)
    toep = toep.astype(bf16).reshape(2, CQ * seq_len, seq_len)

    qkv_rows = to_columns(
        jnp.concatenate([spread_columns(w, 2 * DH) for w in (w_query, w_key, w_value)], axis=2)
    )
    w_qkv = jnp.pad(qkv_rows.reshape(D, 6, DH), ((0, 0), (0, 0), (0, HP - DH))).reshape(D, 6 * HP)
    w_in = to_columns(jnp.concatenate([spread_columns(w, BLK) for w in (w_gate, w_up)], axis=2))
    w_dn = down_rows(w_down, chip)
    w_o = lax.all_gather(w_out, FS, axis=0, tiled=True)

    input_float = layer_input.astype(f32)
    input_scale = rms(input_float)
    x_rows = x_all.reshape(CHIPS * seq_len, D).astype(f32)
    xn_rows = (x_rows * rms(x_rows) * gain_attn).astype(bf16)
    qkv = dot(xn_rows, w_qkv).astype(bf16).reshape(CHIPS, seq_len, 6 * HP)
    heads_pad, scores, weights, outs = run_forward(group_lengths, mix, qkv, toep, gain_pair)
    heads_sent = heads_pad.reshape(CHIPS, seq_len, 2, HP)[..., :DH].reshape(CHIPS, seq_len, 2 * DH)
    heads = jnp.transpose(exchange_chips(heads_sent), (1, 0, 2)).reshape(seq_len, D)
    hmid = input_float + dot(heads, w_o)
    hmid_scale = rms(hmid)
    hn_rows = gather_chips((hmid * hmid_scale * gain_ffn).astype(bf16), 2).reshape(CHIPS * seq_len, D)
    both = dot(hn_rows, w_in)
    gate, up = both[:, :BLK], both[:, BLK:]
    sig = jax.nn.sigmoid(gate)
    silu = gate * sig
    inner = (silu * up).astype(bf16)
    ffn = scatter_slow(dot(inner, w_dn).reshape(CHIPS, seq_len, D))
    layer_output = (hmid + ffn).astype(bf16)

    valid = (jnp.arange(seq_len) < length).astype(f32)
    dy = cotangent.astype(f32) * valid[:, None]
    dy_rows = gather_slow(dy.astype(bf16)).reshape(CHIPS * seq_len, D)
    dinner = dot_nt(dy_rows, w_dn)
    dgate = (dinner * up * (sig * (1.0 + gate * (1.0 - sig)))).astype(bf16)
    dup = (dinner * silu).astype(bf16)
    dboth = jnp.concatenate([dgate, dup], axis=1)
    dhn = scatter_chips(dot_nt(dboth, w_in).astype(bf16).reshape(CHIPS, seq_len, D), 3)
    dhmid, grad_gain_ffn = norm_backward(hmid, hmid_scale, gain_ffn, dhn)
    dhmid = dhmid + dy
    dattn = dhmid.astype(bf16)
    dheads = dot_nt(dattn, w_o).astype(bf16).reshape(seq_len, CHIPS, 2 * DH)
    dheads = exchange_chips(jnp.transpose(dheads, (1, 0, 2)))
    dheads = jnp.pad(dheads.reshape(CHIPS, seq_len, 2, DH), ((0, 0), (0, 0), (0, 0), (0, HP - DH)))
    dqkv, theta_sums, mixer_sums, gain_sums = run_backward(
        group_lengths, mix, qkv, toep, gain_pair, scores, weights, outs, dheads.reshape(CHIPS, seq_len, 2 * HP)
    )
    dqkv_rows = dqkv.reshape(CHIPS * seq_len, 6 * HP)
    dxn = scatter_slow(dot_nt(dqkv_rows, w_qkv).reshape(CHIPS, seq_len, D))
    dinput, grad_gain_attn = norm_backward(input_float, input_scale, gain_attn, dxn)
    input_grad = dinput + dhmid

    taps = jnp.asarray(band())
    theta_sums = theta_sums.reshape(2, seq_len, CQ, seq_len)
    grad_theta = jnp.stack(
        [jnp.sum(jnp.where(taps[tap][None, :, None, :], theta_sums, 0.0), axis=(1, 3)) for tap in range(CK)], axis=2
    )
    grad_mixer = jnp.sum(mixer_sums[:4], axis=1)
    vector_grad = jnp.concatenate(
        [
            grad_gain_attn,
            lax.dynamic_update_slice_in_dim(
                jnp.zeros((D,), f32), gain_sums.reshape(2, HP)[:, :DH].reshape(-1), chip * 2 * DH, 0
            ),
            grad_gain_ffn,
            lax.dynamic_update_slice_in_dim(
                jnp.zeros((H * CQ * CK,), f32), grad_theta.reshape(-1), chip * 2 * CQ * CK, 0
            ),
            lax.dynamic_update_slice_in_dim(jnp.zeros((2 * H,), f32), grad_mixer, chip * 4, 0),
        ]
    )
    pieces = jnp.pad(vector_grad.reshape(fs_size, 1, own_vec), ((0, 0), (0, 0), (0, 512 - own_vec)))
    pieces = jnp.broadcast_to(pieces, (fs_size, reps, 512)).reshape(-1, 4, 128)
    vector_total = jnp.sum(
        lax.all_to_all(pieces, ALL, split_axis=0, concat_axis=0, tiled=True), axis=0
    ).reshape(512)[:own_vec]

    strip = BLK // (2 * CHIPS)
    grad_in = dot_tn(hn_rows, dboth).reshape(ROW_TILES, 2, CHIPS, strip, 2, BLK)
    grad_down = dot_tn(inner, dy_rows).reshape(2, CHIPS, strip, ROW_TILES, BLK)
    grad_in = jnp.transpose(half_for_core(grad_in, 1), (1, 3, 0, 2, 4)).reshape(CHIPS, 2 * ROW_TILES, strip, BLK)
    grad_down = jnp.transpose(half_for_core(grad_down, 0), (0, 2, 1, 3))
    ffn_tiles = exchange_chips(jnp.concatenate([grad_in, grad_down], axis=1).astype(bf16))
    gate_tiles = jnp.transpose(ffn_tiles[:, : 2 * ROW_TILES], (1, 0, 2, 3)).reshape(-1, strip, BLK)
    down_tiles = ffn_tiles[:, 2 * ROW_TILES :].reshape(-1, strip, BLK)
    grad_qkv = dot_tn(xn_rows, dqkv_rows).reshape(ROW_TILES, 2, CHIPS, strip, 6, HP)[..., :DH]
    grad_qkv = jnp.transpose(half_for_core(grad_qkv, 1), (1, 0, 2, 3, 4))
    grad_qkv = exchange_chips(grad_qkv.astype(bf16).reshape(CHIPS, ROW_TILES, strip, 6 * DH))
    grad_qkv = jnp.transpose(
        grad_qkv.reshape(CHIPS, ROW_TILES, strip, 3, 2 * DH), (3, 1, 2, 0, 4)
    ).reshape(3, ROW_TILES, strip, ROW_TILES, BLK)
    qkv_tiles = jnp.transpose(grad_qkv, (0, 1, 3, 2, 4)).reshape(-1, strip, BLK)
    heads_strips = jnp.transpose(heads.reshape(seq_len, 2 * ROW_TILES, CHIPS, strip), (2, 0, 1, 3))
    heads_strips = exchange_chips(heads_strips.reshape(CHIPS, seq_len, 2 * ROW_TILES * strip))
    dattn_rows = gather_slow(dattn).reshape(CHIPS * seq_len, D)
    grad_out = dot_tn(heads_strips.reshape(CHIPS * seq_len, -1), dattn_rows)
    grad_out = half_for_core(grad_out.reshape(ROW_TILES, 2, strip, ROW_TILES, BLK), 1)
    out_tiles = jnp.transpose(grad_out.astype(bf16), (0, 2, 1, 3)).reshape(-1, strip, BLK)

    groups = lax.axis_size("g")
    part = strip // groups
    own_slots = basis_left.shape[0]
    devices = groups * 2 * CHIPS
    slot_total = own_slots * devices
    sums = jnp.concatenate(
        [sum_groups(jnp.concatenate([qkv_tiles, out_tiles], axis=0)), sum_groups(jnp.concatenate([gate_tiles, down_tiles], axis=0))],
        axis=0,
    )
    matches = (jnp.arange(slot_total)[:, None] == owners[None, :]).astype(bf16)
    slots = dot(matches, sums.reshape(sums.shape[0], -1)).astype(bf16)
    slots = lax.all_to_all(
        slots.reshape(devices, own_slots, part, BLK), ALL, split_axis=0, concat_axis=0, tiled=True
    )
    slots = slots.reshape(groups, 2, 2, 2, 2, own_slots, part, BLK)
    own_grad = jnp.transpose(slots, (5, 3, 4, 1, 2, 0, 6, 7)).reshape(own_slots, BLK, BLK)

    left_low, right_low = basis_left.astype(bf16), basis_right.astype(bf16)
    rotated = jnp.einsum("sia,sij->saj", left_low, own_grad, preferred_element_type=f32)
    rotated = jnp.einsum("saj,sjb->sab", rotated.astype(bf16), right_low, preferred_element_type=f32)
    first_new = beta_first * block_first + (1.0 - beta_first) * rotated
    second_new = beta_second * block_second + (1.0 - beta_second) * rotated * rotated
    direction = (first_new / (jnp.sqrt(second_new) + eps_adam)).astype(bf16)
    turned = jnp.einsum("sia,sab->sib", left_low, direction, preferred_element_type=f32)
    turned = jnp.einsum("sib,sjb->sij", turned.astype(bf16), right_low, preferred_element_type=f32)
    master_new = block_master - rate_block * (turned + decay_block * block_master)
    vec_first_new = beta_first * vec_first + (1.0 - beta_first) * vector_total
    vec_second_new = beta_second * vec_second + (1.0 - beta_second) * vector_total * vector_total
    vec_master_new = vec_master - rate_vector * vec_first_new / (jnp.sqrt(vec_second_new) + eps_adam)
    return (
        layer_output, input_grad, first_new, second_new, master_new, master_new.astype(bf16),
        vec_first_new, vec_second_new, vec_master_new, vec_master_new.astype(bf16),
    )


def group_at(mask):
    return {axis: 1 - lax.axis_index(axis) for axis, bit in (("g", 4), ("a", 2), ("b", 1)) if mask & bit}


def other_bit(axis, changed):
    at = lax.axis_index(axis)
    return 1 - at if changed else at


def push(src, dst, send, recv, device):
    copy = pltpu.make_async_remote_copy(src_ref=src, dst_ref=dst, send_sem=send, recv_sem=recv, device_id=device)
    copy.start()
    return copy


class Gather:
    def __init__(self, x_ref, out_ref, local_sem, send1, recv1, send2, recv2, send3, recv3):
        self.x, self.out, self.local_sem = x_ref, out_ref, local_sem
        self.sems = ((send1, recv1), (send2, recv2), (send3, recv3))
        self.me = chip_index()
        self.half = x_ref.shape[0] // 2
        self.sent, self.second = [], []

    def here(self, part):
        return pl.ds(part * self.half, self.half)

    def start(self):
        self.local = pltpu.make_async_copy(self.x, self.out.at[self.me], self.local_sem)
        self.local.start()
        send, recv = self.sems[0]
        for part in range(2):
            for at, (axis, _, _) in enumerate(HOPS):
                self.sent.append(
                    push(
                        self.x.at[self.here(part)], self.out.at[self.me, self.here(part)],
                        send.at[at, part], recv.at[at, part], across(axis),
                    )
                )

    def onward(self):
        send, recv = self.sems[1]
        for part in range(2):
            for at, (axis, onward, _) in enumerate(HOPS):
                self.sent[part * 3 + at].wait_recv()
                block = self.out.at[flipped(self.me, (axis,)), self.here(part)]
                self.second.append(push(block, block, send.at[at, part], recv.at[at, part], across(onward)))

    def last(self):
        send, recv = self.sems[2]
        self.third = []
        for copy in self.second:
            copy.wait_recv()
        for at, (axis, onward, last) in enumerate(HOPS):
            begin, count = THIRDS[at]
            piece = self.out.at[flipped(self.me, (axis, onward)), pl.ds(begin, count)]
            self.third.append(push(piece, piece, send.at[at], recv.at[at], across(last)))

    def finish(self):
        for copy in self.third:
            copy.wait_recv()
        self.local.wait()

    def drain(self):
        for copy in self.sent + self.second + self.third:
            copy.wait_send()


class SideGather:
    def __init__(self, x_ref, out_ref, local_sem, send1, recv1, send2, recv2, send3, recv3):
        self.x, self.out, self.local_sem = x_ref, out_ref, local_sem
        self.sems = ((send1, recv1), (send2, recv2), (send3, recv3))
        self.me = chip_index()
        half = x_ref.shape[0] // 2
        self.low, self.high = pl.ds(0, half), pl.ds(half, half)

    def start(self):
        self.local = pltpu.make_async_copy(self.x, self.out.at[self.me], self.local_sem)
        self.local.start()
        send, recv = self.sems[0]
        self.first = [
            push(self.x, self.out.at[self.me], send.at[at], recv.at[at], across(axis)) for at, axis in enumerate("aby")
        ]

    def onward(self):
        send, recv = self.sems[1]
        blocks = [self.out.at[flipped(self.me, (axis,))] for axis in "aby"]
        self.first[0].wait_recv()
        self.second = [
            push(blocks[0], blocks[0], send.at[0], recv.at[0], across("b")),
            push(blocks[0], blocks[0], send.at[1], recv.at[1], across("y")),
        ]
        self.first[1].wait_recv()
        piece = blocks[1].at[self.high]
        self.second.append(push(piece, piece, send.at[2], recv.at[2], across("y")))
        self.first[2].wait_recv()
        piece = blocks[2].at[self.low]
        self.second.append(push(piece, piece, send.at[3], recv.at[3], across("b")))

    def last(self):
        send, recv = self.sems[2]
        self.second[0].wait_recv()
        piece = self.out.at[flipped(self.me, ("a", "b")), self.high]
        self.third = [push(piece, piece, send.at[0], recv.at[0], across("y"))]
        self.second[1].wait_recv()
        piece = self.out.at[flipped(self.me, ("a", "y")), self.low]
        self.third.append(push(piece, piece, send.at[1], recv.at[1], across("b")))

    def finish(self):
        for copy in self.second[2:] + self.third:
            copy.wait_recv()
        self.local.wait()

    def drain(self):
        for copy in self.first + self.second + self.third:
            copy.wait_send()


def side_sems():
    dma = pltpu.SemaphoreType.DMA
    return [dma] + [dma((3,))] * 2 + [dma((4,))] * 2 + [dma((2,))] * 2


class Scatter:
    def __init__(self, parts, near, in2, in3, acc2, acc3, send1, recv1, send2, recv2, send3, recv3):
        self.parts, self.near, self.in2, self.in3, self.acc2, self.acc3 = parts, near, in2, in3, acc2, acc3
        self.sems = ((send1, recv1), (send2, recv2), (send3, recv3))
        self.me = chip_index()
        self.half = parts.shape[1] // 2

    def here(self, part):
        return pl.ds(part * self.half, self.half)

    def start(self):
        send, recv = self.sems[0]
        opposite = flipped(self.me, ("y", "a", "b"))
        self.first = []
        for at, (_, _, last) in enumerate(HOPS):
            rows = pl.ds(*THIRDS[at])
            self.first.append(push(self.parts.at[opposite, rows], self.in2.at[rows], send.at[at], recv.at[at], across(last)))

    def onward(self):
        send, recv = self.sems[1]
        self.second = []
        for part in range(2):
            for at, (axis, onward, _) in enumerate(HOPS):
                dest = flipped(self.me, (axis, onward))
                if part == 0:
                    self.first[at].wait_recv()
                    rows = pl.ds(*THIRDS[at])
                    self.acc2[at] = self.parts[dest]
                    self.acc2[at, rows] = (
                        self.parts[dest, rows].astype(f32) + self.in2[rows].astype(f32)
                    ).astype(bf16)
                here = self.here(part)
                self.second.append(
                    push(self.acc2.at[at, here], self.in3.at[at, here], send.at[at, part], recv.at[at, part], across(onward))
                )

    def last(self):
        send, recv = self.sems[2]
        self.third = []
        for part in range(2):
            here = self.here(part)
            for at, (axis, _, _) in enumerate(HOPS):
                dest = flipped(self.me, (axis,))
                self.second[part * 3 + at].wait_recv()
                self.acc3[at, here] = (
                    self.parts[dest, here].astype(f32) + self.in3[at, here].astype(f32)
                ).astype(bf16)
                self.third.append(
                    push(self.acc3.at[at, here], self.near.at[at, here], send.at[at, part], recv.at[at, part], across(axis))
                )

    def finish(self, part):
        here = self.here(part)
        for at in range(3):
            self.third[part * 3 + at].wait_recv()
        return (self.parts[self.me, here].astype(f32) + self.near[0, here].astype(f32)) + (
            self.near[1, here].astype(f32) + self.near[2, here].astype(f32)
        )

    def drain(self):
        for copy in self.first + self.second + self.third:
            copy.wait_send()


class SideScatter:
    def __init__(self, parts, near, in1, in2, acc2, acc3, send1, recv1, send2, recv2, send3, recv3):
        self.parts, self.near, self.in1, self.in2, self.acc2, self.acc3 = parts, near, in1, in2, acc2, acc3
        self.sems = ((send1, recv1), (send2, recv2), (send3, recv3))
        self.me = chip_index()
        half = parts.shape[1] // 2
        self.low, self.high = pl.ds(0, half), pl.ds(half, half)

    def start(self):
        send, recv = self.sems[0]
        far, side = flipped(self.me, ("a", "b", "y")), flipped(self.me, ("b", "y"))
        self.first = [
            push(self.parts.at[block, rows], self.in1.at[at], send.at[at], recv.at[at], across(axis))
            for at, (block, rows, axis) in enumerate(
                ((far, self.high, "y"), (far, self.low, "b"), (side, self.low, "b"), (side, self.high, "y"))
            )
        ]

    def add(self, at, axes, rows, acc):
        self.first[at].wait_recv()
        block = flipped(self.me, axes)
        acc[...] = self.parts[block]
        acc[rows] = (self.parts[block, rows].astype(f32) + self.in1[at].astype(f32)).astype(bf16)
        return acc

    def onward(self):
        send, recv = self.sems[1]
        third_send, third_recv = self.sems[2]
        self.second = [
            push(self.add(0, ("a", "b"), self.high, self.acc2.at[0]), self.in2.at[0], send.at[0], recv.at[0], across("b")),
            push(self.add(1, ("a", "y"), self.low, self.acc2.at[1]), self.in2.at[1], send.at[1], recv.at[1], across("y")),
        ]
        self.third = [
            push(self.add(at, (axis,), rows, self.acc3.at[to]), self.near.at[to], third_send.at[to], third_recv.at[to], across(axis))
            for at, axis, rows, to in ((3, "b", self.high, 1), (2, "y", self.low, 2))
        ]

    def last(self):
        send, recv = self.sems[2]
        for copy in self.second:
            copy.wait_recv()
        self.acc3[0] = (
            self.parts[flipped(self.me, ("a",))].astype(f32) + (self.in2[0].astype(f32) + self.in2[1].astype(f32))
        ).astype(bf16)
        self.third.append(push(self.acc3.at[0], self.near.at[0], send.at[0], recv.at[0], across("a")))

    def finish(self):
        for copy in self.third:
            copy.wait_recv()
        return (self.parts[self.me].astype(f32) + self.near[0].astype(f32)) + (
            self.near[1].astype(f32) + self.near[2].astype(f32)
        )

    def drain(self):
        for copy in self.first + self.second + self.third:
            copy.wait_send()


def side_scatter_scratch(rows, width):
    dma = pltpu.SemaphoreType.DMA
    return [
        pltpu.VMEM(dims + (width,), bf16) for dims in ((3, rows), (4, rows // 2), (2, rows), (2, rows), (3, rows))
    ] + [dma((4,))] * 2 + [dma((2,))] * 2 + [dma((3,))] * 2


def scatter_scratch(rows, width):
    dma = pltpu.SemaphoreType.DMA
    three = pltpu.VMEM((3, rows, width), bf16)
    return [three, pltpu.VMEM((rows, width), bf16), three, three, three] + [dma((3,))] * 2 + [dma((3, 2))] * 4


VMEM = pl.BlockSpec(memory_space=pltpu.VMEM)


HEAD_ROW, FFN_ROW, THETA_ROW, MIX_ROW, VEC_ROWS = 12, 28, 40, 56, 64
SHARD_ROWS = 16


def vector_row(at):
    for begin, row, width in (
        (3 * D + H * CQ * CK, MIX_ROW, 4), (3 * D, THETA_ROW, CQ * CK), (2 * D, FFN_ROW, 128), (D, HEAD_ROW, DH), (0, 0, 128)
    ):
        if at >= begin:
            return row + (at - begin) // width


def vector_rows(own_vec, shards):
    return [min(vector_row(shard * own_vec), VEC_ROWS - SHARD_ROWS) // 8 * 8 for shard in range(shards)]


def rows_of_vector(flat):
    conv_end = 3 * D + H * CQ * CK
    return jnp.concatenate(
        [
            flat[:D].reshape(-1, 128),
            jnp.pad(flat[D : 2 * D].reshape(H, DH), ((0, 0), (0, 128 - DH))),
            flat[2 * D : 3 * D].reshape(-1, 128),
            jnp.pad(flat[3 * D : conv_end].reshape(H, CQ * CK), ((0, 0), (0, 128 - CQ * CK))),
            jnp.pad(flat[conv_end : conv_end + 2 * H].reshape(CHIPS, 4), ((0, 0), (0, 124))),
        ],
        axis=0,
    )


def source_at(mask):
    return ((other_bit("g", mask & 4) * 2 + other_bit("a", mask & 2)) * 2 + other_bit("b", mask & 1)) * 2 + lax.axis_index("c")


def front_body(
    first_rows, length_ref, vec_ref, x_ref, w_query_ref, w_key_ref, w_value_ref, cot_ref,
    w_out_ref, w_gate_ref, w_up_ref, w_down_ref, dy_ref, len_ref, mix_ref, gains_ref, toep_ref, gain_ref, strips_ref, hmid_ref,
    xn_out, qkv_out, s_out, p_out, o_out, wq_out, wo_out, hn_all_ref, w_in_ref, w_dn_ref, dy_all_ref,
    xn_ref, qkv_ref, s_ref, p_ref, o_ref, wq_ref, wo_ref, heads_ref, leave_sems,
    blocks_ref, own_len_ref, vecs_ref, full_ref, x_all_ref, pad_ref, out_heads, hn_ref, passing, vec_send, vec_recv, len_send, len_recv, local_sems, q_send, q_recv, q_core_send, q_core_recv,
    o_send, o_recv, o_side_send, o_side_recv, o_core_send, o_core_recv, d_send, d_recv,
    w_send, w_recv, u_send, u_recv, core_send, core_recv, head_send, head_recv, *hops,
):
    seqs, rows, _ = x_all_ref.shape
    g, a, b, c, y = (lax.axis_index(axis) for axis in ALL)
    me = chip_index()
    mine = source_at(0)
    shard = {mask: source_at(mask) for mask in range(8)}
    low, high = pl.ds(0, BLK), pl.ds(BLK, BLK)
    order = (4, 6, 5, 7, 2, 1, 3)

    def columns(chip):
        return pl.ds(pl.multiple_of(chip * BLK, BLK), BLK)

    def block_to(mask):
        return (y * 2 + other_bit("a", mask & 2)) * 2 + other_bit("b", mask & 1)

    local = [
        pltpu.make_async_copy(w_out_ref, wo_ref.at[mine], local_sems.at[1]),
        pltpu.make_async_copy(w_gate_ref.at[:, columns(me)], w_in_ref.at[mine, :, low], local_sems.at[2]),
        pltpu.make_async_copy(w_up_ref.at[:, columns(me)], w_in_ref.at[mine, :, high], local_sems.at[3]),
    ]
    down_local = pltpu.make_async_copy(w_down_ref, w_dn_ref.at[c], local_sems.at[4])
    own_len_ref[...] = jnp.full(own_len_ref.shape, length_ref[0].astype(f32), f32)
    own_small = [
        pltpu.make_async_copy(vec_ref, vecs_ref.at[mine], local_sems.at[5]),
        pltpu.make_async_copy(own_len_ref, len_ref.at[me], local_sems.at[6]),
    ]
    for copy in local + own_small:
        copy.start()

    @pl.when(g == y)
    def _():
        down_local.start()

    greet_all()
    leaving = []

    def leave(src, dst):
        copy = pltpu.make_async_copy(src, dst, leave_sems.at[len(leaving)])
        copy.start()
        leaving.append(copy)

    sent, relayed = {}, []
    first = Gather(x_ref, x_all_ref, *hops[:7])
    side = SideGather(dy_ref, dy_all_ref, *hops[7:14])
    gather = Gather(hn_ref, hn_all_ref, *hops[14:])

    def push_vec(step, carry):
        to = lax.rem(mine + step, 16)
        pltpu.make_async_remote_copy(
            src_ref=vec_ref, dst_ref=vecs_ref.at[mine], send_sem=vec_send, recv_sem=vec_recv,
            device_id={
                "g": lax.div(to, 8), "a": lax.rem(lax.div(to, 4), 2), "b": lax.rem(lax.div(to, 2), 2), "c": lax.rem(to, 2)
            },
        ).start()
        return carry

    lax.fori_loop(1, 16, push_vec, 0)
    lengths_sent = [
        push(own_len_ref, len_ref.at[me], len_send.at[mask], len_recv.at[mask], chip_at(mask)) for mask in range(1, 8)
    ]

    first.start()
    for chip in range(CHIPS):
        cols = slice(chip * 2 * DH, (chip + 1) * 2 * DH)
        blocks_ref[chip] = jnp.concatenate([w_query_ref[:, cols], w_key_ref[:, cols], w_value_ref[:, cols]], axis=1)
    wq_ref[mine] = blocks_ref[me]
    valid = lax.broadcasted_iota(jnp.int32, cot_ref.shape, 0) < length_ref[0]
    dy_ref[...] = jnp.where(valid, cot_ref[...].astype(f32), 0.0).astype(bf16)

    for mask in order:
        sent[mask] = push(blocks_ref.at[block_to(mask)], wq_ref.at[mine], q_send.at[mask], q_recv.at[mask], group_at(mask))

    def relay_qkv(mask):
        sent[mask].wait_recv()
        block = wq_ref.at[shard[mask]]
        relayed.append(push(block, block, q_core_send.at[mask], q_core_recv.at[mask], across("c")))

    half = pl.ds(pl.multiple_of(y * 48, 16), 48)
    lines, o_side, o_core = {}, {}, []

    def start_lines():
        for mask in (2, 4, 6):
            lines[mask] = push(w_out_ref.at[half], wo_ref.at[mine, half], o_send.at[mask], o_recv.at[mask], group_at(mask))
        lines[1] = push(w_out_ref.at[half], wo_ref.at[mine, half], o_send.at[1], o_recv.at[1], across("b"))
        o_core.append(push(w_out_ref, wo_ref.at[mine], o_core_send.at[0], o_core_recv.at[0], across("c")))

    def to_side(mask):
        lines[mask].wait_recv()
        piece = wo_ref.at[shard[mask], half]
        o_side[mask] = push(piece, piece, o_side_send.at[mask], o_side_recv.at[mask], across("y"))
        if mask in (2, 4, 6):
            lines[mask + 1] = push(piece, piece, o_send.at[mask + 1], o_recv.at[mask + 1], across("b"))

    def out_to_core(masks):
        for mask in masks:
            o_side[mask].wait_recv()
            block = wo_ref.at[shard[mask]]
            o_core.append(push(block, block, o_core_send.at[mask], o_core_recv.at[mask], across("c")))

    count = w_down_ref.shape[0] // 2
    upper, lower = pl.ds(0, count), pl.ds(count, count)

    def down_copy(src, dst, at, axis):
        return pltpu.make_async_remote_copy(
            src_ref=src, dst_ref=dst, send_sem=d_send.at[at], recv_sem=d_recv.at[at], device_id=across(axis)
        )

    def down_direct():
        return down_copy(w_down_ref.at[upper], w_dn_ref.at[c, upper], 0, "g")

    def down_around():
        return down_copy(w_down_ref.at[lower], passing, 1, "g")

    def down_over():
        return down_copy(passing, w_dn_ref.at[c, lower], 2, "y")

    def down_to_core():
        return down_copy(w_dn_ref.at[c], w_dn_ref.at[c], 3, "c")

    def down_start():
        @pl.when(g == y)
        def _():
            down_direct().start()

        @pl.when(g != y)
        def _():
            down_around().start()

    def down_pass():
        @pl.when(g == y)
        def _():
            down_around().wait_recv()
            down_over().start()

    def down_last():
        @pl.when(g == y)
        def _():
            down_local.wait()
            down_to_core().start()
            down_direct().wait_send()
            down_over().wait_send()

        @pl.when(g != y)
        def _():
            down_direct().wait_recv()
            down_over().wait_recv()
            down_to_core().start()
            down_around().wait_send()

    gate, up = {}, {}

    def send_columns(masks):
        for mask in masks:
            to = columns(block_to(mask))
            gate[mask] = push(w_gate_ref.at[:, to], w_in_ref.at[mine, :, low], w_send.at[mask], w_recv.at[mask], group_at(mask))
            up[mask] = push(w_up_ref.at[:, to], w_in_ref.at[mine, :, high], u_send.at[mask], u_recv.at[mask], group_at(mask))

    def relay(mask):
        gate[mask].wait_recv()
        up[mask].wait_recv()
        block = w_in_ref.at[shard[mask]]
        relayed.append(push(block, block, core_send.at[mask], core_recv.at[mask], across("c")))

    side.start()
    relayed.append(push(wq_ref.at[mine], wq_ref.at[mine], q_core_send.at[0], q_core_recv.at[0], across("c")))
    first.onward()
    start_lines()

    for copy in own_small:
        copy.wait()
    others = vecs_ref.at[pl.ds(0, 15)]
    pltpu.make_async_copy(others, others, vec_recv).wait()
    full_ref[...] = jnp.zeros_like(full_ref)
    for at, row in enumerate(first_rows):
        full_ref[row : row + SHARD_ROWS, :] += vecs_ref[at]
    gains_ref[...] = jnp.zeros_like(gains_ref)
    for row in range(D // 128):
        gains_ref[0:1, row * 128 : (row + 1) * 128] = full_ref[row : row + 1, :]
        gains_ref[1:2, row * 128 : (row + 1) * 128] = full_ref[FFN_ROW + row : FFN_ROW + row + 1, :]
    mix_ref[...] = jnp.zeros_like(mix_ref)
    mix_row = full_ref[pl.ds(MIX_ROW + me, 1), :]
    for at in range(4):
        mix_ref[at : at + 1, :] = jnp.broadcast_to(mix_row[:, at : at + 1], (1, 128))
    query_at = lax.broadcasted_iota(jnp.int32, (rows, rows), 0)
    key_at = lax.broadcasted_iota(jnp.int32, (rows, rows), 1)
    key_float = key_at.astype(f32)
    tap_at = query_at - key_at + CK // 2
    for head in range(2):
        gain_ref[:, head * HP : (head + 1) * HP] = full_ref[pl.ds(HEAD_ROW + 2 * me + head, 1), :]
        theta = full_ref[pl.ds(THETA_ROW + 2 * me + head, 1), :]
        for lag in range(CQ):
            band_values = jnp.zeros((rows, rows), f32)
            for tap in range(CK):
                at = lag * CK + tap
                band_values = jnp.where(tap_at == tap, theta[:, at : at + 1], band_values)
            toep_ref[head, lag * rows : (lag + 1) * rows, :] = band_values.astype(bf16)

    side.onward()
    first.last()
    side.last()
    down_start()
    for mask in order:
        relay_qkv(mask)
    send_columns((2, 1, 3, 4, 6, 5, 7))
    first.finish()
    for copy in relayed + lengths_sent:
        copy.wait_recv()
    qkv_relayed = relayed[:]
    del relayed[:]

    pad_ref[0:8, :] = jnp.zeros((8, rows), f32)
    blank = jnp.zeros((rows, HP - DH), bf16)
    batch = 4

    def project(at, carry):
        values = x_all_ref[pl.ds(at * batch, batch)].astype(f32).reshape(batch * rows, D)
        normed = (values * rms(values) * gains_ref[0:1, :]).astype(bf16)
        xn_ref[pl.ds(at * batch, batch)] = normed.reshape(batch, rows, D)
        made = dot(normed, wq_ref[...].reshape(D, 6 * DH)).astype(bf16)
        for seq in range(batch):
            for piece in range(6):
                qkv_ref[at * batch + seq, :, piece * HP : (piece + 1) * HP] = jnp.concatenate(
                    [made[seq * rows : (seq + 1) * rows, piece * DH : (piece + 1) * DH], blank], axis=1
                )
        return carry

    project(0, 0)
    for mask in (2, 4, 6, 1):
        to_side(mask)
    project(1, 0)
    leave(xn_ref, xn_out)
    leave(qkv_ref, qkv_out)
    leave(wq_ref, wq_out)
    for copy in local:
        copy.wait()
    relayed.append(push(w_in_ref.at[mine], w_in_ref.at[mine], core_send.at[0], core_recv.at[0], across("c")))

    def head_copy(seq):
        return pltpu.make_async_remote_copy(
            src_ref=out_heads.at[seq], dst_ref=heads_ref.at[me], send_sem=head_send.at[seq], recv_sem=head_recv.at[me],
            device_id={"y": lax.div(seq, 4), "a": lax.rem(lax.div(seq, 2), 2), "b": lax.rem(seq, 2)},
        )

    def attend(step, carry):
        seq = lax.rem(me + step, seqs)
        keep = (key_at <= query_at) & (key_float < len_ref[seq, 0:1, :])
        weights, made = [], []
        for head in range(2):
            query = qkv_ref[seq, :, head * HP : (head + 1) * HP]
            key = qkv_ref[seq, :, (2 + head) * HP : (3 + head) * HP]
            scores = jnp.where(keep, dot_nt(query, key) * (1.0 / math.sqrt(DH)), 0.0)
            s_ref[seq, head] = scores.astype(bf16)
            wide = shifted_down(pad_ref, scores)
            near = wide.astype(bf16)
            rest = (wide - near.astype(f32)).astype(bf16)
            conv = dot(near, toep_ref[head]) + dot(rest, toep_ref[head])
            logits = jnp.where(keep, conv, -1e30)
            weight = jnp.exp(logits - jnp.max(logits, axis=-1, keepdims=True))
            weight = weight / jnp.sum(weight, axis=-1, keepdims=True)
            p_ref[seq, head] = weight
            weights.append(weight)
        for head in range(2):
            mixed = mix_ref[2 * head : 2 * head + 1, :] * weights[0] + mix_ref[2 * head + 1 : 2 * head + 2, :] * weights[1]
            value = qkv_ref[seq, :, (4 + head) * HP : (5 + head) * HP]
            out = dot(mixed.astype(bf16), value)
            o_ref[seq, :, head * HP : (head + 1) * HP] = out
            scale = lax.rsqrt(jnp.sum(out * out, axis=-1, keepdims=True) * (1.0 / DH) + eps_norm)
            made.append((out * scale * gain_ref[:, head * HP : (head + 1) * HP])[:, :DH])
        out_heads[seq] = jnp.concatenate(made, axis=1).astype(bf16)

        @pl.when(step > 0)
        def _():
            head_copy(seq).start()

        return carry

    lax.fori_loop(0, 3, attend, 0)
    for mask in (3, 5, 7):
        to_side(mask)
    down_pass()
    lax.fori_loop(3, 6, attend, 0)
    out_to_core((2, 4, 6))
    lax.fori_loop(6, seqs, attend, 0)
    out_to_core((1, 3, 5, 7))
    heads_ref[me] = out_heads[me]
    leave(s_ref, s_out)
    leave(p_ref, p_out)
    leave(o_ref, o_out)
    for copy in o_core:
        copy.wait_recv()
    leave(wo_ref, wo_out)

    def head_arrived(step, carry):
        source = lax.rem(me + step, seqs)
        pltpu.make_async_copy(out_heads.at[source], heads_ref.at[source], head_recv.at[source]).wait()
        return carry

    lax.fori_loop(1, seqs, head_arrived, 0)

    def project_out(at, carry):
        cols = pl.ds(pl.multiple_of(at * BLK, BLK), BLK)
        total = x_ref[:, cols].astype(f32)
        for chip in range(CHIPS):
            weight = wo_ref[2 * chip : 2 * chip + 2, :, cols].reshape(2 * DH, BLK)
            total += dot(heads_ref[chip], weight)
        hmid_ref[:, cols] = total
        return carry

    lax.fori_loop(0, ROW_TILES, project_out, 0)
    hmid = hmid_ref[...]
    hn_ref[...] = (hmid * rms(hmid) * gains_ref[1:2, :]).astype(bf16)
    gather.start()
    width = BLK // (2 * CHIPS)
    for chip in range(CHIPS):
        pieces = []
        for at in range(2 * ROW_TILES):
            begin = at * (BLK // 2) + chip * width
            source, begin = begin // (2 * DH), begin % (2 * DH)
            pieces.append(heads_ref[source, :, begin : begin + width])
        strips_ref[chip] = jnp.concatenate(pieces, axis=1)
    for mask in (4, 6):
        relay(mask)
    gather.onward()
    for mask in (5, 7, 2):
        relay(mask)
    gather.last()
    for mask in (1, 3):
        relay(mask)
    down_last()
    down_to_core().wait()
    side.finish()
    gather.finish()
    for copy in relayed:
        copy.wait_recv()
    for copy in leaving:
        copy.wait()

    def head_left(step, carry):
        head_copy(lax.rem(me + step, seqs)).wait_send()
        return carry

    lax.fori_loop(1, seqs, head_left, 0)
    first.drain()
    side.drain()
    gather.drain()
    for copies in (sent, lines, o_side, gate, up):
        for copy in copies.values():
            copy.wait_send()
    pltpu.make_async_copy(others, others, vec_send).wait()
    for copy in qkv_relayed + relayed + o_core + lengths_sent:
        copy.wait_send()


def run_front(first_rows, length, vec, x, w_query, w_key, w_value, cotangent, w_out, w_gate, w_up, w_down):
    rows = x.shape[0]
    dma = pltpu.SemaphoreType.DMA
    small = [
        (x.shape, bf16), ((CHIPS, 8, 128), f32), ((8, 128), f32), ((8, D), f32), ((2, CQ * rows, rows), bf16), ((1, 2 * HP), f32),
        ((CHIPS, rows, 2 * DH), bf16), ((rows, D), f32),
    ]
    large = [
        ((CHIPS, rows, D), bf16), ((CHIPS, rows, 6 * HP), bf16), ((CHIPS, 2, rows, rows), bf16), ((CHIPS, 2, rows, rows), f32),
        ((CHIPS, rows, 2 * HP), f32), ((16, w_query.shape[0], 6 * DH), bf16), ((16,) + w_out.shape, bf16),
    ]
    gathered = [
        ((CHIPS, rows, D), bf16), ((16, w_gate.shape[0], 2 * BLK), bf16), ((2,) + w_down.shape, bf16), ((CHIPS, rows, D), bf16),
    ]
    return pl.pallas_call(
        functools.partial(front_body, first_rows),
        in_specs=[SMEM] + [VMEM] * 6 + [ANYS] * 4,
        out_specs=[VMEM] * len(small) + [ANYS] * (len(large) + len(gathered)),
        out_shape=[jax.ShapeDtypeStruct(*shape) for shape in small + large + gathered],
        scratch_shapes=[pltpu.VMEM(*shape) for shape in large] + [
            pltpu.VMEM((CHIPS, rows, 2 * DH), bf16), dma((len(large),)),
            pltpu.VMEM((CHIPS, w_query.shape[0], 6 * DH), bf16), pltpu.VMEM((8, 128), f32), pltpu.VMEM((16,) + vec.shape, f32), pltpu.VMEM((VEC_ROWS, 128), f32), pltpu.VMEM((CHIPS, rows, D), bf16), pltpu.VMEM((rows + 8, rows), f32), pltpu.VMEM((CHIPS, rows, 2 * DH), bf16),
            pltpu.VMEM((rows, D), bf16), pltpu.VMEM((w_down.shape[0] // 2, D), bf16), dma, dma, dma((8,)), dma((8,)), dma((7,)),
        ] + [dma((8,))] * 10 + [dma((4,))] * 2 + [dma((8,))] * 8 + hop_sems() + side_sems() + hop_sems(),
        name="front",
        compiler_params=pltpu.CompilerParams(collective_id=2, has_side_effects=True, vmem_limit_bytes=56 * 2**20),
    )(length, vec, x, w_query, w_key, w_value, cotangent, w_out, w_gate, w_up, w_down)


def middle_body(
    len_ref, mix_ref, hn_ref, dy_ref, xn_ref, w_in_hbm, w_dn_hbm, wq_hbm, dy_own_ref, hmid_ref, gains_ref, wo_hbm,
    qkv_hbm, toep_ref, gain_ref, s_hbm, p_hbm, o_hbm, strips_ref,
    inner_ref, dhmid_ref, dxn_ref, gain_ffn_grad_ref, theta_ref, gain_grad_ref, tiles_ref,
    w_in_ref, w_dn_ref, wq_ref, wo_ref, qkv_ref, s_ref, p_ref, o_ref, enter_sems,
    theta_sums, pad_ref, first_ref, second_ref, dboth_ref, parts_ref, dattn_ref, grads_ref, sent_ref, strips_in, gin_ref, gd_ref,
    half_in, half_d, near_in, near_d, dqkv_ref, gq_ref, go_ref, core_q, core_o, in_q, in_o,
    near3, in23, in33, local_sems, load_sems, strip_send, strip_recv, head_send, head_recv,
    core_send, core_recv, near_send, near_recv, gu_send, gu_recv, q_send, q_recv, *rest,
):
    scatter_args, scatter3_sems, side = rest[:11], rest[11:17], rest[17:]
    seqs, rows, _ = hn_ref.shape
    g, a, b, c, y = (lax.axis_index(axis) for axis in ALL)
    me = chip_index()
    pairs = [(1 - y) * 2 + 1 - a, (1 - y) * 2 + a, y * 2 + 1 - a, y * 2 + a]
    loads = []
    for at, pair in enumerate(pairs):
        two = pl.ds(pair * 2, 2)
        loads.append(
            [
                pltpu.make_async_copy(hn_ref.at[two], first_ref.at[two], load_sems.at[at]),
                pltpu.make_async_copy(dy_ref.at[two], second_ref.at[two], load_sems.at[4 + at]),
            ]
        )
    enter = [
        pltpu.make_async_copy(src, dst, enter_sems.at[at])
        for at, (src, dst) in enumerate(
            (
                (w_in_hbm, w_in_ref), (w_dn_hbm, w_dn_ref), (wo_hbm, wo_ref), (qkv_hbm, qkv_ref), (s_hbm, s_ref),
                (p_hbm, p_ref), (o_hbm, o_ref), (wq_hbm, wq_ref),
            )
        )
    ]
    enter[0].start()
    for copies in loads:
        for copy in copies:
            copy.start()
    for copy in enter[1:]:
        copy.start()
    strip_local = pltpu.make_async_copy(strips_ref.at[me], strips_in.at[me], local_sems.at[0])
    strip_local.start()
    greet_all()
    chips = (7, 6, 5, 3, 4, 2, 1)
    to_chip = {mask: flipped(me, [axis for axis in BITS if mask & BITS[axis]]) for mask in chips}
    strips_sent = [
        push(strips_ref.at[to_chip[mask]], strips_in.at[me], strip_send.at[mask], strip_recv.at[mask], chip_at(mask))
        for mask in chips
    ]

    def hidden(pair):
        two = pl.ds(pair * 2, 2)
        both = dot(first_ref[two].reshape(2 * rows, D), w_in_ref[...])
        gate, up = both[:, :BLK], both[:, BLK:]
        dinner = dot_nt(second_ref[two].reshape(2 * rows, D), w_dn_ref[...])
        sig = jax.nn.sigmoid(gate)
        silu = gate * sig
        inner_ref[two] = (silu * up).astype(bf16).reshape(2, rows, BLK)
        dgate = (dinner * up * (sig * (1.0 + gate * (1.0 - sig)))).astype(bf16)
        dup = (dinner * silu).astype(bf16)
        dboth_ref[two, :, 0:BLK] = dgate.reshape(2, rows, BLK)
        dboth_ref[two, :, BLK:] = dup.reshape(2, rows, BLK)
        back = dot_nt(dgate, w_in_ref[:, 0:BLK]) + dot_nt(dup, w_in_ref[:, BLK:])
        parts_ref[two] = back.astype(bf16).reshape(2, rows, D)

    def wait_load(at):
        for copy in loads[at]:
            copy.wait()

    wait_load(0)
    enter[0].wait()
    enter[1].wait()
    hidden(pairs[0])
    scatter = Scatter(parts_ref, *scatter_args)
    scatter.start()
    wait_load(1)
    wait_load(2)

    def two_more(step, carry):
        hidden((1 - y) * 2 + a + step * ((2 * y - 1) * 2 + 1 - a - a))
        return carry

    lax.fori_loop(0, 2, two_more, 0)
    scatter.onward()
    wait_load(3)
    hidden(pairs[3])

    def down_grad(col, carry):
        cols = pl.ds(pl.multiple_of(col * BLK, BLK), BLK)
        made = dot_tn(inner_ref[...].reshape(seqs * rows, BLK), second_ref[:, :, cols].reshape(seqs * rows, BLK))
        gd_ref[:, :, :, :, cols] = made.astype(bf16).reshape(2, CHIPS, 2, BLK // 32, BLK)
        return carry

    lax.fori_loop(0, ROW_TILES, down_grad, 0)
    to_core = [push(gd_ref.at[1 - c], half_d, core_send.at[0], core_recv.at[0], across("c"))]

    def in_grad(row, carry):
        values = first_ref[:, :, pl.ds(pl.multiple_of(row * BLK, BLK), BLK)].reshape(seqs * rows, BLK)
        for which in range(2):
            cols = slice(which * BLK, (which + 1) * BLK)
            made = dot_tn(values, dboth_ref[:, :, cols].reshape(seqs * rows, BLK))
            gin_ref[row, :, :, :, :, cols] = made.astype(bf16).reshape(2, CHIPS, 2, BLK // 32, BLK)
        return carry

    def in_to_core(row):
        to_core.append(push(gin_ref.at[row, 1 - c], half_in.at[row], core_send.at[1 + row], core_recv.at[1 + row], across("c")))

    in_grad(0, 0)
    in_to_core(0)
    to_core[0].wait_recv()

    def core_down(chip, carry):
        half_d[chip] = (half_d[chip].astype(f32) + gd_ref[c, chip].astype(f32)).astype(bf16)
        return carry

    lax.fori_loop(0, CHIPS, core_down, 0)
    to_near = [push(half_d.at[:, 1 - g], near_d, near_send.at[0], near_recv.at[0], across("g"))]
    scatter.last()
    lax.fori_loop(1, ROW_TILES, in_grad, 0)
    in_to_core(1)
    in_to_core(2)
    xn_load = pltpu.make_async_copy(xn_ref, first_ref, load_sems.at[8])
    xn_load.start()

    def core_rows(row):
        to_core[1 + row].wait_recv()

        def core_chip(chip, carry):
            half_in[row, chip] = (half_in[row, chip].astype(f32) + gin_ref[row, c, chip].astype(f32)).astype(bf16)
            return carry

        lax.fori_loop(0, CHIPS, core_chip, 0)
        to_near.append(push(half_in.at[row, :, 1 - g], near_in.at[row], near_send.at[1 + row], near_recv.at[1 + row], across("g")))

    core_rows(0)
    core_rows(1)
    core_rows(2)
    half = rows // 2
    gain_sum = jnp.zeros((1, D), f32)
    for part in range(2):
        here = pl.ds(part * half, half)
        grad = scatter.finish(part)
        values = hmid_ref[here]
        scale = rms(values)
        unit = values * scale
        inside = grad * gains_ref[1:2, :]
        gain_sum += jnp.sum(grad * unit, axis=0, keepdims=True)
        dhmid = scale * (inside - unit * jnp.mean(inside * unit, axis=-1, keepdims=True)) + dy_own_ref[here].astype(f32)
        dhmid_ref[here] = dhmid
        dattn_ref[here] = dhmid.astype(bf16)
    gain_ffn_grad_ref[...] = gain_sum

    for copy in enter[2:]:
        copy.wait()

    def grad_copy(to):
        return pltpu.make_async_remote_copy(
            src_ref=sent_ref.at[to], dst_ref=grads_ref.at[me], send_sem=head_send.at[to], recv_sem=head_recv.at[me],
            device_id={"y": lax.div(to, 4), "a": lax.rem(lax.div(to, 2), 2), "b": lax.rem(to, 2)},
        )

    def send_grad(step, carry):
        to = lax.rem(me + step, seqs)
        sent_ref[to] = dot_nt(dattn_ref[...], wo_ref[to]).astype(bf16)

        @pl.when(step > 0)
        def _():
            grad_copy(to).start()

        return carry

    lax.fori_loop(0, seqs, send_grad, 0)
    grads_ref[me] = sent_ref[me]
    gather = SideGather(dattn_ref, second_ref, *side)
    gather.start()

    pad_ref[rows : rows + 8, :] = jnp.zeros((8, rows), f32)
    theta_sums[...] = jnp.zeros_like(theta_sums)
    taps_end = 2 * CQ * CK
    mixer_ref = theta_ref.at[pl.ds(taps_end + 4, 8)]
    theta_ref[taps_end:, :] = jnp.zeros((theta_ref.shape[0] - taps_end, rows), f32)
    gain_grad_ref[...] = jnp.zeros_like(gain_grad_ref)
    query_at = lax.broadcasted_iota(jnp.int32, (rows, rows), 0)
    key_at = lax.broadcasted_iota(jnp.int32, (rows, rows), 1)
    key_float = key_at.astype(f32)
    blank = jnp.zeros((rows, HP - DH), f32)

    def grad_arrived(step, carry):
        source = lax.rem(me + step, seqs)
        pltpu.make_async_copy(sent_ref.at[source], grads_ref.at[source], head_recv.at[source]).wait()
        return carry

    lax.fori_loop(1, seqs, grad_arrived, 0)

    def one(seq, carry):
        keep = (key_at <= query_at) & (key_float < len_ref[seq, 0:1, :])
        weights = [p_ref[seq, 0], p_ref[seq, 1]]
        grad_mixed, made = [], [None] * 6
        grads = grads_ref[seq].astype(f32)
        for head in range(2):
            cols = slice(head * HP, (head + 1) * HP)
            out = o_ref[seq, :, cols]
            grad = jnp.concatenate([grads[:, head * DH : (head + 1) * DH], blank], axis=1)
            scale = lax.rsqrt(jnp.sum(out * out, axis=-1, keepdims=True) * (1.0 / DH) + eps_norm)
            unit = out * scale
            gain_grad_ref[:, cols] += jnp.sum(grad * unit, axis=0, keepdims=True)
            inner = grad * gain_ref[:, cols]
            grad_out = scale * (inner - unit * (jnp.sum(inner * unit, axis=-1, keepdims=True) * (1.0 / DH)))
            grad_out = grad_out.astype(bf16)
            value = qkv_ref[seq, :, (4 + head) * HP : (5 + head) * HP]
            mixed = (
                mix_ref[2 * head : 2 * head + 1, :] * weights[0] + mix_ref[2 * head + 1 : 2 * head + 2, :] * weights[1]
            ).astype(bf16)
            made[4 + head] = dot_tn(mixed, grad_out)
            back = dot_nt(grad_out, value)
            grad_mixed.append(back)
            for source in range(2):
                mixer_ref[2 * head + source : 2 * head + source + 1, :] += jnp.sum(
                    back * weights[source], axis=0, keepdims=True
                )
        for head in range(2):
            grad_weight = mix_ref[head : head + 1, :] * grad_mixed[0] + mix_ref[2 + head : 3 + head, :] * grad_mixed[1]
            weight = weights[head]
            grad_conv = weight * (grad_weight - jnp.sum(weight * grad_weight, axis=-1, keepdims=True))
            wide = shifted_up(pad_ref, grad_conv).astype(bf16)
            theta_sums[head] += dot_tn(s_ref[seq, head], wide)
            grad_scores = jnp.zeros((rows, rows), f32)
            for lag in range(CQ):
                grad_scores += dot_nt(
                    wide[:, lag * rows : (lag + 1) * rows], toep_ref[head, lag * rows : (lag + 1) * rows, :]
                )
            grad_scores = jnp.where(keep, grad_scores * (1.0 / math.sqrt(DH)), 0.0).astype(bf16)
            query = qkv_ref[seq, :, head * HP : (head + 1) * HP]
            key = qkv_ref[seq, :, (2 + head) * HP : (3 + head) * HP]
            made[head] = dot(grad_scores, key)
            made[2 + head] = dot_tn(grad_scores, query)
        dqkv_ref[seq] = jnp.concatenate([part[:, :DH] for part in made], axis=1).astype(bf16)
        return carry

    lax.fori_loop(0, 4, one, 0)
    gather.onward()
    lax.fori_loop(4, seqs, one, 0)
    scatter.drain()
    tiles_sent = []

    tap_at = query_at - key_at + CK // 2

    def taps(at, carry):
        lag = lax.rem(at, CQ)
        values = theta_sums[lax.div(at, CQ), :, pl.ds(pl.multiple_of(lag * rows, rows), rows)]
        for tap in range(CK):
            theta_ref[pl.ds(at * CK + tap, 1), :] = jnp.sum(
                jnp.where(tap_at == tap, values, 0.0), axis=0, keepdims=True
            )
        return carry

    xn_load.wait()
    all_rows = seqs * rows

    def qkv_grad(row, carry):
        cols = pl.ds(pl.multiple_of(row * BLK, BLK), BLK)
        made = dot_tn(first_ref[:, :, cols].reshape(all_rows, BLK), dqkv_ref[...].reshape(all_rows, 6 * DH))
        gq_ref[row] = made.astype(bf16).reshape(2, CHIPS, 2, BLK // 32, 6 * DH)
        return carry

    lax.fori_loop(0, ROW_TILES, qkv_grad, 0)
    to_core.append(push(gq_ref.at[:, 1 - c], core_q, core_send.at[4], core_recv.at[4], across("c")))

    def input_part(at, carry):
        two = pl.ds(at * 2, 2)
        made = dot_nt(dqkv_ref[two].reshape(2 * rows, 6 * DH), wq_ref[...])
        parts_ref[two] = made.astype(bf16).reshape(2, rows, D)
        return carry

    lax.fori_loop(0, seqs // 2, input_part, 0)
    scatter3 = Scatter(parts_ref, near3, in23, in33, *scatter_args[3:5], *scatter3_sems)
    scatter3.start()
    lax.fori_loop(0, 2 * CQ, taps, 0)
    to_core[4].wait_recv()

    def core_chip_q(chip, carry):
        for row in range(ROW_TILES):
            core_q[row, chip] = (core_q[row, chip].astype(f32) + gq_ref[row, c, chip].astype(f32)).astype(bf16)
        return carry

    lax.fori_loop(0, CHIPS, core_chip_q, 0)
    slot = g * CHIPS + me
    order = (15, 14, 13, 11, 12, 10, 9, 8, 7, 6, 5, 3, 4, 2, 1)
    for mask in order:
        to = flipped(me, [axis for axis in BITS if mask & BITS[axis]])
        tiles_sent.append(
            push(core_q.at[:, to, other_bit("g", mask & 8)], in_q.at[slot], q_send.at[mask], q_recv.at[mask], wide_at(mask))
        )
    in_q[slot] = core_q[:, me, g]
    gather.last()
    to_near[0].wait_recv()

    def near_down(chip, carry):
        half_d[chip, g] = (half_d[chip, g].astype(f32) + near_d[chip].astype(f32)).astype(bf16)
        return carry

    lax.fori_loop(0, CHIPS, near_down, 0)
    base = 4 * ROW_TILES**2

    def spread(ref, cols, tile, which):
        for mask in chips:
            at = which * CHIPS + mask
            tiles_sent.append(
                push(ref.at[to_chip[mask], g, :, cols], tiles_ref.at[tile], gu_send.at[at], gu_recv.at[at], chip_at(mask))
            )
        tiles_ref[tile] = ref[me, g, :, cols]

    for col in range(ROW_TILES):
        spread(half_d, pl.ds(col * BLK, BLK), base + 2 * ROW_TILES * FF_TILES + me * ROW_TILES + col, 6 + col)
    scatter3.onward()
    gather.finish()
    strip_local.wait()
    for copy in strips_sent:
        copy.wait_recv()

    def out_grad(col, carry):
        cols = pl.ds(pl.multiple_of(col * BLK, BLK), BLK)
        made = dot_tn(strips_in[...].reshape(all_rows, 2 * DH), second_ref[:, :, cols].reshape(all_rows, BLK))
        go_ref[:, :, :, :, cols] = made.astype(bf16).reshape(ROW_TILES, 2, 2, BLK // 32, BLK)
        return carry

    lax.fori_loop(0, ROW_TILES, out_grad, 0)
    to_core.append(push(go_ref.at[:, 1 - c], core_o, core_send.at[5], core_recv.at[5], across("c")))

    def near_rows(row):
        to_near[1 + row].wait_recv()

        def near_chip(chip, carry):
            half_in[row, chip, g] = (half_in[row, chip, g].astype(f32) + near_in[row, chip].astype(f32)).astype(bf16)
            return carry

        lax.fori_loop(0, CHIPS, near_chip, 0)
        for which in range(2):
            spread(
                half_in.at[row], pl.ds(which * BLK, BLK), base + (which * ROW_TILES + row) * FF_TILES + me, 2 * row + which
            )

    near_rows(0)
    to_core[5].wait_recv()
    core_o[...] = (core_o[...].astype(f32) + go_ref[:, c].astype(f32)).astype(bf16)
    to_near.append(push(core_o.at[:, 1 - g], in_o, near_send.at[4], near_recv.at[4], across("g")))
    scatter3.last()
    near_rows(1)
    near_rows(2)
    dxn_ref[0:half] = scatter3.finish(0)
    dxn_ref[half:] = scatter3.finish(1)

    def three_tiles(at, values):
        for col in range(ROW_TILES):
            tiles_ref[at + col] = values[:, col * BLK : (col + 1) * BLK].astype(bf16)

    to_near[4].wait_recv()
    for row in range(ROW_TILES):
        three_tiles(3 * ROW_TILES**2 + row * ROW_TILES, in_o[row].astype(f32) + core_o[row, g].astype(f32))
    for copy in tiles_sent:
        copy.wait_recv()
    for row in range(ROW_TILES):
        sums = [in_q[chip, row].astype(f32) + in_q[CHIPS + chip, row].astype(f32) for chip in range(CHIPS)]
        for which in range(3):
            three_tiles(
                which * ROW_TILES**2 + row * ROW_TILES,
                jnp.concatenate([part[:, which * 2 * DH : (which + 1) * 2 * DH] for part in sums], axis=1),
            )
    tiles_ref[tiles_ref.shape[0] - 1] = jnp.zeros(tiles_ref.shape[1:], bf16)

    def grad_left(step, carry):
        grad_copy(lax.rem(me + step, seqs)).wait_send()
        return carry

    lax.fori_loop(1, seqs, grad_left, 0)
    gather.drain()
    scatter3.drain()
    for copy in strips_sent + to_core + to_near + tiles_sent:
        copy.wait_send()


def chip_at(mask):
    return {axis: 1 - lax.axis_index(axis) for axis in BITS if mask & BITS[axis]}


def wide_at(mask):
    at = chip_at(mask & 7)
    if mask & 8:
        at["g"] = 1 - lax.axis_index("g")
    return at


def run_middle(
    lengths, mix, hn, dy, xn, w_in, w_dn, w_qkv, dy_own, hmid, gain_ffn, w_o, qkv, toep, gain, scores, weights, outs, strips
):
    seqs, rows, _ = hn.shape
    dma = pltpu.SemaphoreType.DMA
    part = BLK // 32
    tiles = 4 * ROW_TILES**2 + 3 * ROW_TILES * FF_TILES
    shapes = [
        ((seqs, rows, BLK), bf16), ((rows, D), f32), ((rows, D), f32), ((1, D), f32), ((2 * CQ * CK + 12, rows), f32),
        ((1, 2 * HP), f32), ((tiles + 1, part, BLK), bf16),
    ]

    def low(*dims):
        return pltpu.VMEM(dims, bf16)

    every, heads = low(CHIPS, rows, D), low(CHIPS, rows, 2 * DH)
    return pl.pallas_call(
        middle_body,
        in_specs=[VMEM] * 2 + [ANYS] * 6 + [VMEM] * 3 + [ANYS] * 2 + [VMEM] * 2 + [ANYS] * 3 + [VMEM],
        out_specs=[VMEM] * len(shapes),
        out_shape=[jax.ShapeDtypeStruct(*shape) for shape in shapes],
        scratch_shapes=[pltpu.VMEM(a.shape, a.dtype) for a in (w_in, w_dn, w_qkv, w_o, qkv, scores, weights, outs)] + [
            dma((8,)),
            pltpu.VMEM((2, rows, CQ * rows), f32), pltpu.VMEM((rows + 8, rows), f32), every, every, low(seqs, rows, 2 * BLK), every, low(rows, D), heads, heads, heads,
            low(ROW_TILES, 2, CHIPS, 2, part, 2 * BLK), low(2, CHIPS, 2, part, D),
            low(ROW_TILES, CHIPS, 2, part, 2 * BLK), low(CHIPS, 2, part, D),
            low(ROW_TILES, CHIPS, part, 2 * BLK), low(CHIPS, part, D),
            low(seqs, rows, 6 * DH), low(ROW_TILES, 2, CHIPS, 2, part, 6 * DH), low(ROW_TILES, 2, 2, part, D),
            low(ROW_TILES, CHIPS, 2, part, 6 * DH), low(ROW_TILES, 2, part, D),
            low(2 * CHIPS, ROW_TILES, part, 6 * DH), low(ROW_TILES, part, D),
            low(3, rows, D), low(rows, D), low(3, rows, D), dma((1,)), dma((9,)),
        ] + [dma((8,))] * 4 + [dma((6,))] * 2 + [dma((5,))] * 2 + [dma((9 * CHIPS,))] * 2 + [dma((16,))] * 2
        + scatter_scratch(rows, D) + [dma((3,))] * 2 + [dma((3, 2))] * 4 + side_sems(),
        name="middle",
        compiler_params=pltpu.CompilerParams(collective_id=3, has_side_effects=True, vmem_limit_bytes=63 * 2**20),
    )(
        lengths, mix, hn, dy, xn, w_in, w_dn, w_qkv, dy_own, hmid, gain_ffn, w_o,
        qkv, toep, gain, scores, weights, outs, strips,
    )


def to_slots_body(
    pick_ref, tiles_ref, vec_ref, inner_hbm, w_dn_hbm, hmid_hbm, out_ref, vecs_ref, layer_ref,
    inner_ref, w_dn_ref, hmid_ref, enter_sems, slots_ref, parts_ref, local_sems, send, recv, vec_send, vec_recv, *scatter_args,
):
    devices = lax.axis_size(ALL)
    own_slots, side = out_ref.shape[:2]
    part = slots_ref.shape[1]
    enter = [
        pltpu.make_async_copy(src, dst, enter_sems.at[at])
        for at, (src, dst) in enumerate(((inner_hbm, inner_ref), (w_dn_hbm, w_dn_ref), (hmid_hbm, hmid_ref)))
    ]
    for copy in enter:
        copy.start()

    def fill(at, carry):
        slots_ref[at] = tiles_ref[pick_ref[at]]
        return carry

    lax.fori_loop(0, slots_ref.shape[0], fill, 0)
    me = device_index()
    place = (lax.axis_index("c") * CHIPS + chip_index()) * 2 + lax.axis_index("g")
    rows = pl.ds(pl.multiple_of(place * part, part), part)
    local = [pltpu.make_async_copy(vec_ref.at[me], vecs_ref.at[me], local_sems.at[0])]
    for slot in range(own_slots):
        local.append(
            pltpu.make_async_copy(
                slots_ref.at[me * own_slots + slot], out_ref.at[slot, rows], local_sems.at[1 + slot]
            )
        )
    for copy in local:
        copy.start()
    greet_all()

    def push_all(step, carry):
        to = lax.rem(me + step, devices)
        pltpu.make_async_remote_copy(
            src_ref=vec_ref.at[to], dst_ref=vecs_ref.at[me], send_sem=vec_send, recv_sem=vec_recv, device_id=device_at(to)
        ).start()
        pltpu.make_async_remote_copy(
            src_ref=slots_ref.at[pl.ds(to * own_slots, own_slots)], dst_ref=out_ref.at[:, rows],
            send_sem=send, recv_sem=recv, device_id=device_at(to),
        ).start()
        return carry

    lax.fori_loop(devices // 4, devices, push_all, 0)
    lax.fori_loop(1, devices // 4, push_all, 0)

    seqs, length = inner_ref.shape[:2]
    for copy in enter:
        copy.wait()

    def outputs(at, carry):
        two = pl.ds(at * 2, 2)
        made = dot(inner_ref[two].reshape(2 * length, BLK), w_dn_ref[...])
        parts_ref[two] = made.astype(bf16).reshape(2, length, D)
        return carry

    lax.fori_loop(0, seqs // 2, outputs, 0)
    scatter = SideScatter(parts_ref, *scatter_args)
    scatter.start()
    scatter.onward()
    scatter.last()
    layer_ref[...] = (hmid_ref[...] + scatter.finish()).astype(bf16)
    scatter.drain()
    others = vecs_ref.at[pl.ds(0, devices - 1)]
    pltpu.make_async_copy(others, others, vec_recv).wait()
    pltpu.make_async_copy(others, others, vec_send).wait()
    others = out_ref.at[:, pl.ds(0, side - part)]
    pltpu.make_async_copy(others, others, recv).wait()
    pltpu.make_async_copy(others, others, send).wait()
    for copy in local:
        copy.wait()


def to_slots(pick, tiles, vecs, inner, w_dn, hmid, own_slots):
    rows = hmid.shape[0]
    dma = pltpu.SemaphoreType.DMA
    return pl.pallas_call(
        to_slots_body,
        in_specs=[SMEM, VMEM] + [ANYS] * 4,
        out_specs=[ANYS] * 2 + [VMEM],
        out_shape=[
            jax.ShapeDtypeStruct((own_slots, BLK, BLK), bf16), jax.ShapeDtypeStruct(vecs.shape, vecs.dtype),
            jax.ShapeDtypeStruct(hmid.shape, bf16),
        ],
        scratch_shapes=[pltpu.VMEM(a.shape, a.dtype) for a in (inner, w_dn, hmid)] + [
            dma((3,)), pltpu.VMEM((pick.shape[0],) + tiles.shape[1:], bf16), pltpu.VMEM((CHIPS, rows, D), bf16), dma((1 + own_slots,)),
        ] + [dma] * 4 + side_scatter_scratch(rows, D),
        name="to_slots",
        compiler_params=pltpu.CompilerParams(collective_id=6, has_side_effects=True, vmem_limit_bytes=60 * 2**20),
    )(pick, tiles, vecs, inner, w_dn, hmid)


def update_body(grad_ref, left_ref, right_ref, master_ref, first_ref, second_ref, first_out, second_out, master_out, copy_out):
    left, right = left_ref[0].astype(bf16), right_ref[0].astype(bf16)
    rotated = dot(dot_tn(left, grad_ref[0]).astype(bf16), right)
    first = beta_first * first_ref[0] + (1.0 - beta_first) * rotated
    second = beta_second * second_ref[0] + (1.0 - beta_second) * rotated * rotated
    first_out[0] = first
    second_out[0] = second
    direction = (first / (jnp.sqrt(second) + eps_adam)).astype(bf16)
    turned = dot_nt(dot(left, direction).astype(bf16), right)
    master = master_ref[0]
    master = master - rate_block * (turned + decay_block * master)
    master_out[0] = master
    copy_out[0] = master.astype(bf16)


def update(grad, left, right, master, first, second):
    spec = pl.BlockSpec((1, BLK, BLK), lambda slot: (slot, 0, 0))
    return pl.pallas_call(
        update_body,
        grid=(grad.shape[0],),
        in_specs=[spec] * 6,
        out_specs=[spec] * 4,
        out_shape=[jax.ShapeDtypeStruct(grad.shape, kind) for kind in (f32, f32, f32, bf16)],
        name="update",
        compiler_params=pltpu.CompilerParams(vmem_limit_bytes=60 * 2**20),
        cost_estimate=pl.CostEstimate(flops=43 * 10**8, bytes_accessed=36 * 2**20, transcendentals=10**6),
    )(grad, left, right, master, first, second)


def body_fast(
    layer_input, lengths, cotangent, w_query, w_key, w_value, w_out, w_gate, w_up, w_down, vec_copy, owners,
    basis_left, basis_right, block_master, block_first, block_second, vec_master, vec_first, vec_second,
):
    chip = chip_index()
    seq_len = layer_input.shape[0]
    own_vec = vec_copy.shape[0]
    devices, fs_size, reps = lax.axis_size(ALL), lax.axis_size(FS), lax.axis_size("y")

    fs_index = ((lax.axis_index("g") * 2 + lax.axis_index("a")) * 2 + lax.axis_index("b")) * 2 + lax.axis_index("c")
    first_rows = vector_rows(own_vec, fs_size)
    flat = lax.dynamic_update_slice_in_dim(jnp.zeros((fs_size * own_vec,), f32), vec_copy.astype(f32), fs_index * own_vec, 0)
    first = sum(
        (first_rows[at] - first_rows[at - 1]) * (fs_index >= at).astype(jnp.int32)
        for at in range(1, fs_size) if first_rows[at] != first_rows[at - 1]
    )
    vec = lax.dynamic_slice_in_dim(rows_of_vector(flat), first, SHARD_ROWS, 0)

    (
        dy, group_lengths, mix, gains, toep, gain_pair, strips, hmid, xn, qkv, scores, weights, outs, w_qkv, w_out_all,
        hn_rows, w_in, w_dn, dy_rows,
    ) = run_front(
        first_rows, lengths, vec, layer_input, w_query, w_key, w_value, cotangent, w_out, w_gate, w_up, w_down
    )
    gain_attn = gains[0]
    w_qkv = w_qkv.reshape(D, 6 * DH)
    w_in, w_dn = w_in.reshape(D, 2 * BLK), w_dn.reshape(BLK, D)
    input_float = layer_input.astype(f32)
    input_scale = rms(input_float)

    own_slots = basis_left.shape[0]
    matches = jnp.arange(own_slots * devices)[:, None] == owners[None, :]
    tile_count = owners.shape[0]
    pick = jnp.min(jnp.where(matches, jnp.arange(tile_count, dtype=jnp.int32)[None, :], tile_count), axis=1)
    inner, dhmid, dxn, grad_gain_ffn, theta_sums, gain_sums, tiles = run_middle(
        group_lengths, mix, hn_rows, dy_rows, xn, w_in, w_dn, w_qkv, dy, hmid, gains,
        w_out_all.reshape(CHIPS, 2 * DH, D), qkv, toep, gain_pair, scores, weights, outs, strips,
    )
    dinput, grad_gain_attn = norm_backward(input_float, input_scale, gain_attn, dxn)
    input_grad = dinput + dhmid

    tap_sums = jnp.sum(theta_sums, axis=1)
    grad_theta = tap_sums[: 2 * CQ * CK]
    grad_mixer = tap_sums[2 * CQ * CK + 4 : 2 * CQ * CK + 8]
    vector_grad = jnp.concatenate(
        [
            grad_gain_attn,
            lax.dynamic_update_slice_in_dim(
                jnp.zeros((D,), f32), gain_sums.reshape(2, HP)[:, :DH].reshape(-1), chip * 2 * DH, 0
            ),
            grad_gain_ffn.reshape(-1),
            lax.dynamic_update_slice_in_dim(
                jnp.zeros((H * CQ * CK,), f32), grad_theta.reshape(-1), chip * 2 * CQ * CK, 0
            ),
            lax.dynamic_update_slice_in_dim(jnp.zeros((2 * H,), f32), grad_mixer, chip * 4, 0),
        ]
    )
    pieces = jnp.pad(vector_grad.reshape(fs_size, 1, own_vec), ((0, 0), (0, 0), (0, 1024 - own_vec)))
    pieces = jnp.broadcast_to(pieces, (fs_size, reps, 1024)).reshape(devices, 8, 128)

    own_grad, pieces, layer_output = to_slots(
        pick, tiles, pieces, inner, w_dn, hmid, own_slots
    )
    vector_total = jnp.sum(pieces, axis=0).reshape(1024)[:own_vec]
    first_new, second_new, master_new, copy_new = update(
        own_grad, basis_left, basis_right, block_master, block_first, block_second
    )
    vec_first_new = beta_first * vec_first + (1.0 - beta_first) * vector_total
    vec_second_new = beta_second * vec_second + (1.0 - beta_second) * vector_total * vector_total
    vec_master_new = vec_master - rate_vector * vec_first_new / (jnp.sqrt(vec_second_new) + eps_adam)
    return (
        layer_output, input_grad, first_new, second_new, master_new, copy_new,
        vec_first_new, vec_second_new, vec_master_new, vec_master_new.astype(bf16),
    )


def solution(mesh):
    fsdp, rep = mesh.shape["fsdp"], mesh.shape["rep"]
    fine = Mesh(mesh.devices.reshape(fsdp // 8, 2, 2, 2, rep), ALL)
    rows, both = P(ALL, None), P(ALL, None, None)
    weight, vec = P(FS, None), P(FS)
    return jax.shard_map(
        body_fast if (fsdp, rep) == (16, 2) else body_any,
        mesh=fine,
        in_specs=(rows, P(ALL), rows) + (weight,) * 7 + (vec, P()) + (both,) * 5 + (vec,) * 3,
        out_specs=(rows, rows) + (both,) * 4 + (vec,) * 4,
        check_vma=False,
    )
```
